32 devices in a mesh: dp: 8 (over z, x), group: 4 (over y, core).
Axes of the slice: x: 2, y: 2, z: 4, core: 2. Of those that a mesh axis runs over, the one named last changes fastest.
Arguments:
- tokens: bfloat16 [512, 144, 384], P('dp', 'group'), may hold values from -6 to 6
- keep_mask: int32 [512, 144], P(('dp', 'group')), may hold values from 0 to 1, as said below
- cotangent: bfloat16 [512, 144, 384], P('dp', 'group'), may hold values from -12 to 12
- qkv_weight: float32 [384, 1152], P('dp', 'group'), may hold values from -0.3125 to 0.3125
- proj_weight: float32 [384, 384], P('dp', 'group'), may hold values from -1.75 to 1.75
- up_weight: float32 [384, 1536], P('dp', 'group'), may hold values from -0.3125 to 0.3125
- down_weight: float32 [1536, 384], P('dp', 'group'), may hold values from -0.15625 to 0.15625
- vectors: float32 [12, 384], replicated, may hold values from -0.9 to 1.45
- qkv_rows: float32 [384], P('dp'), may hold values from 20643.84 to 81100.8
- qkv_cols: float32 [1152], P('group'), may hold values from 20643.84 to 81100.8
- proj_rows: float32 [384], P('dp'), may hold values from 2949.12 to 11059.2
- proj_cols: float32 [384], P('group'), may hold values from 2949.12 to 11059.2
- up_rows: float32 [384], P('dp'), may hold values from 23592.96 to 95846.4
- up_cols: float32 [1536], P('group'), may hold values from 23592.96 to 95846.4
- down_rows: float32 [1536], P('dp'), may hold values from 22118.4 to 88473.6
- down_cols: float32 [384], P('group'), may hold values from 22118.4 to 88473.6
- vector_moment: float32 [12, 384], replicated, may hold values from 28016.64 to 110592
Outputs:
- block_output: bfloat16 [512, 144, 384], P('dp', 'group')
- input_grad: bfloat16 [512, 144, 384], P('dp', 'group')
- qkv_grad: float32 [384, 1152], P('dp', 'group')
- qkv_rows_new: float32 [384], P('dp')
- qkv_cols_new: float32 [1152], P('group')
- qkv_new: float32 [384, 1152], P('dp', 'group')
- proj_grad: float32 [384, 384], P('dp', 'group')
- proj_rows_new: float32 [384], P('dp')
- proj_cols_new: float32 [384], P('group')
- proj_new: float32 [384, 384], P('dp', 'group')
- up_grad: float32 [384, 1536], P('dp', 'group')
- up_rows_new: float32 [384], P('dp')
- up_cols_new: float32 [1536], P('group')
- up_new: float32 [384, 1536], P('dp', 'group')
- down_grad: float32 [1536, 384], P('dp', 'group')
- down_rows_new: float32 [1536], P('dp')
- down_cols_new: float32 [384], P('group')
- down_new: float32 [1536, 384], P('dp', 'group')
- vector_grad: float32 [12, 384], replicated
- vector_moment_new: float32 [12, 384], replicated
- vector_new: float32 [12, 384], replicated
The draws below stay inside these ranges and needn't reach their ends.
Inputs may be any that keep to these rules, and one draw needn't show every extreme that they name: `keep_mask`: each image keeps its slot 0 and at least half of its 144 slots.
All inputs are finite; a program needn't handle non-finite values.
Results may differ from the reference program's by a relative error of at most 0.012.
Values may be sent and summed in bfloat16 or wider, within the bound.
No kernel may reach another device: no remote copies, remote signals or barrier semaphores. Data moves between devices by JAX's collectives and lax.ppermute only.
A program may use at most 192 MiB of HBM per device.

```python
import math
import jax
import jax.numpy as jnp
from jax import lax

HEAD_DIM = 64
D = 384
FF = 1536
LEN = 144
IMG_DEV = 16
STEP_NUMBER = 10
IMAGES = 512


def draw_keep_mask(key, part):
    key = jax.random.fold_in(key, 11)
    count_key, order_key = jax.random.split(key)
    counts = jax.random.randint(count_key, (IMAGES, 1), LEN // 2, LEN + 1)
    random_bits = jax.random.randint(order_key, (IMAGES, LEN), 0, 1 << 20)
    positions = jnp.arange(LEN, dtype=jnp.int32)[None, :]
    scores = jnp.where(positions == 0, -1, random_bits * LEN + positions)
    order_rank = jnp.argsort(jnp.argsort(scores, axis=1), axis=1)
    return (order_rank < counts).astype(jnp.int32)


def draw_cotangent(key, part):
    key = jax.random.fold_in(key, 12)
    position = jnp.arange(IMAGES, dtype=jnp.float32) / max(IMAGES - 1, 1)
    rising = 1.0 + 2.0 * position
    noise_base = jax.random.truncated_normal(key, -4.0, 4.0, (IMAGES, LEN, D), jnp.float32)
    return (noise_base * rising[:, None, None]).astype(jnp.bfloat16)


def draw_vectors(key, part):
    key = jax.random.fold_in(key, 13)
    noise_base = jax.random.truncated_normal(key, -3.0, 3.0, (12, D), jnp.float32)
    row_index = jnp.arange(12, dtype=jnp.int32)[:, None]
    gain_rows = (row_index == 0) | (row_index == 5)
    return jnp.where(gain_rows, 1.0 + 0.15 * noise_base, 0.3 * noise_base)


def steps_of(stream_key, extent, pieces, least, top_value):
    level, own = 1.0, jax.random.fold_in(stream_key, 6)
    for dim, parts in pieces:
        draws = jnp.exp(jax.random.uniform(jax.random.fold_in(own, dim), (parts,), jnp.float32, least / len(pieces), top_value / len(pieces)))
        level = level * jnp.repeat(draws, extent[dim] // parts).reshape([-1 if axis == dim else 1 for axis in range(len(extent))])
    return level


def normal_values(key, shape, deviation, most, shards=(), kind=jnp.bfloat16):
    result = deviation * jax.random.normal(key, shape, jnp.float32)
    if shards:
        result = result * steps_of(key, shape, shards, -0.22, 0.18)
    return jnp.clip(result, -most, most).astype(kind)


def setup_inputs(seed: int = 0) -> dict:
    splits = jax.random.split(jax.random.key(seed), 18)
    return {
        "tokens": normal_values(splits[0], (IMAGES, LEN, D), 1.0, 6.0, ((0, 8), (1, 4))),
        "keep_mask": draw_keep_mask(jax.random.fold_in(splits[17], 71), 0),
        "cotangent": draw_cotangent(jax.random.fold_in(splits[17], 71), 0),
        "qkv_weight": normal_values(splits[3], (D, 3 * D), D ** -0.5, 0.3125, ((0, 8), (1, 4)), jnp.float32),
        "proj_weight": normal_values(splits[4], (D, D), (D // 32) ** -0.5, 1.75, ((0, 8), (1, 4)), jnp.float32),
        "up_weight": normal_values(splits[5], (D, FF), D ** -0.5, 0.3125, ((0, 8), (1, 4)), jnp.float32),
        "down_weight": normal_values(splits[6], (FF, D), FF ** -0.5, 0.15625, ((0, 8), (1, 4)), jnp.float32),
        "vectors": draw_vectors(jax.random.fold_in(splits[17], 71), 0),
        "qkv_rows": jnp.clip(jnp.exp(math.log(81100.8) - 1.3682758246537599 * jax.random.uniform(splits[8], (D,), jnp.float32) ** steps_of(splits[8], (D,), ((0, 8),), -0.2, 0.2)), 20643.84, 81100.8),
        "qkv_cols": jnp.clip(jnp.exp(math.log(81100.8) - 1.3682758246537599 * jax.random.uniform(splits[9], (3 * D,), jnp.float32) ** steps_of(splits[9], (3 * D,), ((0, 4),), -0.2, 0.2)), 20643.84, 81100.8),
        "proj_rows": jnp.clip(jnp.exp(math.log(11059.2) - 1.3217558 * jax.random.uniform(splits[10], (D,), jnp.float32) ** steps_of(splits[10], (D,), ((0, 8),), -0.2, 0.2)), 2949.12, 11059.2),
        "proj_cols": jnp.clip(jnp.exp(math.log(11059.2) - 1.3217558 * jax.random.uniform(splits[11], (D,), jnp.float32) ** steps_of(splits[11], (D,), ((0, 4),), -0.2, 0.2)), 2949.12, 11059.2),
        "up_rows": jnp.clip(jnp.exp(math.log(95846.4) - 1.4017985 * jax.random.uniform(splits[12], (D,), jnp.float32) ** steps_of(splits[12], (D,), ((0, 8),), -0.2, 0.2)), 23592.96, 95846.4),
        "up_cols": jnp.clip(jnp.exp(math.log(95846.4) - 1.4017985 * jax.random.uniform(splits[13], (FF,), jnp.float32) ** steps_of(splits[13], (FF,), ((0, 4),), -0.2, 0.2)), 23592.96, 95846.4),
        "down_rows": jnp.clip(jnp.exp(math.log(88473.6) - 1.3862944 * jax.random.uniform(splits[14], (FF,), jnp.float32) ** steps_of(splits[14], (FF,), ((0, 8),), -0.2, 0.2)), 22118.4, 88473.6),
        "down_cols": jnp.clip(jnp.exp(math.log(88473.6) - 1.3862944 * jax.random.uniform(splits[15], (D,), jnp.float32) ** steps_of(splits[15], (D,), ((0, 4),), -0.2, 0.2)), 22118.4, 88473.6),
        "vector_moment": jnp.clip(jnp.exp(jax.random.uniform(splits[16], (12, D), jnp.float32, math.log(28016.64), math.log(110592.0))), 28016.64, 110592.0),
    }


step_rate = 0.3
norm_epsilon = 1e-06
tiny_square = 1e-30

@jax.custom_vjp
def low(v):
    return lax.optimization_barrier(v.astype(jnp.bfloat16)).astype(jnp.float32)

@jax.custom_vjp
def low_back(v):
    return v

def low_keep(v):
    return (low(v), None)

def low_pass(kept, grad):
    return (grad,)

def back_keep(v):
    return (v, None)

def back_low(kept, grad):
    return (low(grad),)
low.defvjp(low_keep, low_pass)
low_back.defvjp(back_keep, back_low)

def layer_norm(values, gain, shift):
    center = lax.optimization_barrier(jnp.mean(values, axis=-1, keepdims=True))
    centered = values - center
    spread = lax.optimization_barrier(jnp.mean(centered * centered, axis=-1, keepdims=True))
    return centered * lax.rsqrt(spread + norm_epsilon) * gain + shift

def matmul(left, right):
    return jnp.einsum('bli,ij->blj', left, right, precision=lax.Precision.HIGHEST)

def forward(inputs, allowed, w_qkv, w_proj, w_up, w_down, vecs):
    images = inputs.shape[0]
    length = inputs.shape[1]
    model_width = inputs.shape[2]
    head_count = model_width // HEAD_DIM
    normed = low(layer_norm(inputs, vecs[0], vecs[1]))
    projected = matmul(normed, low(w_qkv))
    queries = low_back(low(projected[..., :model_width] + vecs[2]))
    keys = low_back(low(projected[..., model_width:2 * model_width]))
    values = low_back(low(projected[..., 2 * model_width:] + vecs[3]))
    queries = queries.reshape(images, length, head_count, HEAD_DIM)
    keys = keys.reshape(images, length, head_count, HEAD_DIM)
    values = values.reshape(images, length, head_count, HEAD_DIM)
    scores = jnp.einsum('bqhd,bkhd->bhqk', queries, keys, precision=lax.Precision.HIGHEST) * HEAD_DIM ** (-0.5)
    scores = low_back(scores)
    masked = jnp.where(allowed[:, None], scores, -1e+30)
    highest = lax.optimization_barrier(jnp.max(masked, axis=-1, keepdims=True))
    weights = jnp.where(allowed[:, None], jnp.exp(masked - highest), 0.0)
    probs = weights / lax.optimization_barrier(jnp.sum(weights, axis=-1, keepdims=True))
    attended = jnp.einsum('bhqk,bkhd->bqhd', low(probs), values, precision=lax.Precision.HIGHEST)
    attended = low_back(low(attended.reshape(images, length, model_width)))
    branch = low_back(matmul(attended, low(w_proj)) + vecs[4])
    middle = inputs + branch
    normed_two = low(layer_norm(middle, vecs[5], vecs[6]))
    hidden_pre = low_back(matmul(normed_two, low(w_up)) + vecs[7:11].reshape(-1))
    active = low(jax.nn.gelu(hidden_pre, approximate=False))
    down_out = low_back(matmul(active, low(w_down)) + vecs[11])
    return middle + down_out

def factored(gradient, weight, rows_old, cols_old):
    decay_rate = 1.0 - STEP_NUMBER ** (-0.8)
    square = gradient * gradient + tiny_square
    rows_new = decay_rate * rows_old + (1.0 - decay_rate) * lax.optimization_barrier(jnp.mean(square, axis=1))
    cols_new = decay_rate * cols_old + (1.0 - decay_rate) * lax.optimization_barrier(jnp.mean(square, axis=0))
    second = rows_new[:, None] * cols_new[None, :] / jnp.mean(rows_new)
    spread = jnp.sqrt(jnp.mean(weight * weight))
    return (rows_new, cols_new, weight - step_rate * spread * gradient * lax.rsqrt(second))

def reference(tokens, keep_mask, cotangent, qkv_weight, proj_weight, up_weight, down_weight, vectors, qkv_rows, qkv_cols, proj_rows, proj_cols, up_rows, up_cols, down_rows, down_cols, vector_moment):
    group_images = 4 * IMG_DEV
    block_count = IMAGES // group_images
    stacked = (tokens.reshape(block_count, group_images, LEN, D), keep_mask.reshape(block_count, group_images, LEN), cotangent.reshape(block_count, group_images, LEN, D))
    positions = jnp.arange(LEN, dtype=jnp.int32)
    diagonal = positions[:, None] == positions[None, :]
    zero_grads = (jnp.zeros_like(qkv_weight), jnp.zeros_like(proj_weight), jnp.zeros_like(up_weight), jnp.zeros_like(down_weight), jnp.zeros_like(vectors))

    def advance(totals, carried):
        inputs, keep_flags, upstream = carried
        allowed = (keep_flags[:, None, :] > 0) | diagonal[None]

        def apply(values, w_qkv, w_proj, w_up, w_down, vecs):
            return forward(values, allowed, w_qkv, w_proj, w_up, w_down, vecs)
        output, pull = jax.vjp(apply, inputs.astype(jnp.float32), qkv_weight, proj_weight, up_weight, down_weight, vectors)
        gradients = pull(upstream.astype(jnp.float32))
        totals = tuple((total + part for total, part in zip(totals, gradients[1:])))
        return (totals, (output.astype(jnp.bfloat16), gradients[0].astype(jnp.bfloat16)))
    totals, results = lax.scan(advance, zero_grads, stacked)
    block_output = results[0].reshape(IMAGES, LEN, D)
    input_grad = results[1].reshape(IMAGES, LEN, D)
    qkv_grad, proj_grad, up_grad, down_grad, vector_grad = totals
    qkv_rows_new, qkv_cols_new, qkv_new = factored(qkv_grad, qkv_weight, qkv_rows, qkv_cols)
    proj_rows_new, proj_cols_new, proj_new = factored(proj_grad, proj_weight, proj_rows, proj_cols)
    up_rows_new, up_cols_new, up_new = factored(up_grad, up_weight, up_rows, up_cols)
    down_rows_new, down_cols_new, down_new = factored(down_grad, down_weight, down_rows, down_cols)
    decay_rate = 1.0 - STEP_NUMBER ** (-0.8)
    vector_moment_new = decay_rate * vector_moment + (1.0 - decay_rate) * (vector_grad * vector_grad + tiny_square)
    row_spread = jnp.sqrt(lax.optimization_barrier(jnp.mean(vectors * vectors, axis=1, keepdims=True)))
    vector_new = vectors - step_rate * row_spread * vector_grad * lax.rsqrt(vector_moment_new)
    return (block_output, input_grad, qkv_grad, qkv_rows_new, qkv_cols_new, qkv_new, proj_grad, proj_rows_new, proj_cols_new, proj_new, up_grad, up_rows_new, up_cols_new, up_new, down_grad, down_rows_new, down_cols_new, down_new, vector_grad, vector_moment_new, vector_new)
```

```python
import jax
import jax.numpy as jnp
from jax import lax
from jax.sharding import PartitionSpec as P

HEAD_DIM = 64
STEP_NUMBER = 10


step_rate = 0.3
norm_epsilon = 1e-06
tiny_square = 1e-30


def for_sending(array):

    def short(part):
        return part.astype(jnp.bfloat16) if part.dtype == jnp.float32 else part

    return jax.tree.map(short, array)


def layer_norm(values, gain, shift):
    center = jnp.mean(values, axis=-1, keepdims=True)
    centered = values - center
    spread = jnp.mean(centered * centered, axis=-1, keepdims=True)
    return centered * lax.rsqrt(spread + norm_epsilon) * gain + shift


def exact_gelu(values):
    return jax.nn.gelu(values, approximate=False)


def product(left, right):
    return jnp.einsum("bli,ij->blj", left, right, preferred_element_type=jnp.float32)


def back_product(left, right):
    return jnp.einsum("blj,ij->bli", left, right, preferred_element_type=jnp.float32)


def outer_sum(left, right):
    return jnp.einsum("bli,blj->ij", left, right, preferred_element_type=jnp.float32)


def axis_bits(name):
    count = lax.axis_size(name)
    return [(name, 1 << place) for place in range(count.bit_length() - 1)]


def swap_partner(array, step):
    name, bit = step
    count = lax.axis_size(name)
    return lax.ppermute(array, name, [(rank, rank ^ bit) for rank in range(count)])


def upper_side(step):
    name, bit = step
    return (lax.axis_index(name) & bit) != 0


def gather_blocks(array, steps):
    for step in steps:
        arrived = swap_partner(array, step)
        upper = upper_side(step)
        array = jnp.stack([jnp.where(upper, arrived, array), jnp.where(upper, array, arrived)])
    return array


def scatter_sum(array, steps):
    for step in steps:
        upper = upper_side(step)
        leaving = jnp.where(upper, array[0], array[1]).astype(jnp.bfloat16)
        arrived = swap_partner(leaving, step)
        array = jnp.where(upper, array[1], array[0]).astype(jnp.float32) + arrived.astype(jnp.float32)
    return array


def sum_everywhere(array, steps):
    for step in steps:
        array = array + swap_partner(array, step)
    return array


def sum_parts(parts, steps):
    flat = [part.reshape(-1) for part in parts]
    total = sum_everywhere(jnp.concatenate(flat), steps)
    result, start = [], 0
    for part in parts:
        result.append(total[start : start + part.size].reshape(part.shape))
        start += part.size
    return result


def block_order(steps):
    order = []
    for name in ("dp", "group"):
        bits = sorted((step for step in steps if step[0] == name), key=lambda step: -step[1])
        order.append([steps.index(step) for step in bits])
    return order


def blocks_to_whole(blocks, steps):
    count = len(steps)
    rows, cols = blocks.shape[count:]
    dp_axes, group_axes = block_order(steps)
    dp_axes = [count - 1 - axis for axis in dp_axes]
    group_axes = [count - 1 - axis for axis in group_axes]
    whole = blocks.transpose(dp_axes + [count] + group_axes + [count + 1])
    return whole.reshape(rows << len(dp_axes), cols << len(group_axes))


def whole_to_blocks(whole, steps):
    dp_axes, group_axes = block_order(steps)
    rows = whole.shape[0] >> len(dp_axes)
    cols = whole.shape[1] >> len(group_axes)
    split = whole.reshape([2] * len(dp_axes) + [rows] + [2] * len(group_axes) + [cols])
    places = dp_axes + [len(steps)] + group_axes + [len(steps) + 1]
    return split.transpose([places.index(axis) for axis in range(len(places))])


def body(
    tokens,
    keep_mask,
    cotangent,
    qkv_weight,
    proj_weight,
    up_weight,
    down_weight,
    vectors,
    qkv_rows,
    qkv_cols,
    proj_rows,
    proj_cols,
    up_rows,
    up_cols,
    down_rows,
    down_cols,
    vector_moment,
):
    masters = (qkv_weight, proj_weight, up_weight, down_weight)
    lowered = tuple((master.astype(jnp.bfloat16) for master in masters))
    dp_bits, group_bits = axis_bits("dp"), axis_bits("group")
    gather_steps = dp_bits[1:] + group_bits[1:] + dp_bits[:1] + group_bits[:1]
    scatter_steps = gather_steps[::-1]
    w_qkv, w_proj, w_up, w_down = tuple(
        blocks_to_whole(gather_blocks(part, gather_steps), gather_steps) for part in lowered
    )
    spread = lax.axis_size("group")

    def slots_in(array):
        held, slots, width = array.shape
        parts = array.transpose(1, 0, 2).reshape(slots, spread, held // spread, width)
        parts = lax.all_to_all(
            parts.transpose(1, 0, 2, 3), "group", split_axis=0, concat_axis=0, tiled=True
        )
        return parts.reshape(spread * slots, held // spread, width).transpose(1, 0, 2)

    def slots_out(array):
        held, slots, width = array.shape
        parts = array.transpose(1, 0, 2).reshape(spread, slots // spread, held, width)
        parts = lax.all_to_all(parts, "group", split_axis=0, concat_axis=0, tiled=True)
        parts = parts.transpose(1, 0, 2, 3).reshape(slots // spread, spread * held, width)
        return parts.transpose(1, 0, 2)

    inputs, upstream = slots_in(tokens), slots_in(cotangent)
    images = inputs.shape[0]
    length = inputs.shape[1]
    model_width = inputs.shape[2]
    head_count = model_width // HEAD_DIM
    score_scale = HEAD_DIM ** (-0.5)
    positions = jnp.arange(length, dtype=jnp.int32)
    allowed = (keep_mask[:, None, :] > 0) | (positions[:, None] == positions[None, :])[None]
    x_full = inputs.astype(jnp.float32)
    normed, norm_pull = jax.vjp(layer_norm, x_full, vectors[0], vectors[1])
    normed_low = normed.astype(jnp.bfloat16)
    projected = product(normed_low, w_qkv)
    queries = (projected[..., :model_width] + vectors[2]).astype(jnp.bfloat16)
    keys = projected[..., model_width : 2 * model_width].astype(jnp.bfloat16)
    values = (projected[..., 2 * model_width :] + vectors[3]).astype(jnp.bfloat16)
    queries = queries.reshape(images, length, head_count, HEAD_DIM)
    keys = keys.reshape(images, length, head_count, HEAD_DIM)
    values = values.reshape(images, length, head_count, HEAD_DIM)
    scores = (
        jnp.einsum("bqhd,bkhd->bhqk", queries, keys, preferred_element_type=jnp.float32)
        * score_scale
    )
    masked = jnp.where(allowed[:, None], scores, -1e30)
    highest = jnp.max(masked, axis=-1, keepdims=True)
    weights = jnp.where(allowed[:, None], jnp.exp(masked - highest), 0.0)
    probs = weights / jnp.sum(weights, axis=-1, keepdims=True)
    probs_low = probs.astype(jnp.bfloat16)
    attended = jnp.einsum("bhqk,bkhd->bqhd", probs_low, values, preferred_element_type=jnp.float32)
    attended = attended.reshape(images, length, model_width).astype(jnp.bfloat16)
    middle = x_full + product(attended, w_proj) + vectors[4]
    normed_two, norm_two_pull = jax.vjp(layer_norm, middle, vectors[5], vectors[6])
    normed_two_low = normed_two.astype(jnp.bfloat16)
    hidden_pre = product(normed_two_low, w_up) + vectors[7:11].reshape(-1)
    active, gelu_pull = jax.vjp(exact_gelu, hidden_pre)
    active_low = active.astype(jnp.bfloat16)
    output = middle + product(active_low, w_down) + vectors[11]
    grad_out = upstream.astype(jnp.float32)
    down_grad = outer_sum(active_low, upstream)
    bias_down = jnp.sum(grad_out, axis=(0, 1))
    d_active = back_product(upstream, w_down)
    d_hidden = gelu_pull(d_active)[0].astype(jnp.bfloat16)
    up_grad = outer_sum(normed_two_low, d_hidden)
    bias_up = jnp.sum(d_hidden.astype(jnp.float32), axis=(0, 1))
    d_normed_two = back_product(d_hidden, w_up)
    d_middle_norm, gain_two_grad, shift_two_grad = norm_two_pull(d_normed_two)
    d_middle = grad_out + d_middle_norm
    d_branch = d_middle.astype(jnp.bfloat16)
    proj_grad = outer_sum(attended, d_branch)
    bias_proj = jnp.sum(d_branch.astype(jnp.float32), axis=(0, 1))
    d_attended = back_product(d_branch, w_proj).astype(jnp.bfloat16)
    d_attended = d_attended.reshape(images, length, head_count, HEAD_DIM)
    d_values = jnp.einsum(
        "bhqk,bqhd->bkhd", probs_low, d_attended, preferred_element_type=jnp.float32
    ).astype(jnp.bfloat16)
    d_probs = jnp.einsum("bqhd,bkhd->bhqk", d_attended, values, preferred_element_type=jnp.float32)
    d_scores = (probs * (d_probs - jnp.sum(d_probs * probs, axis=-1, keepdims=True))).astype(
        jnp.bfloat16
    )
    d_queries = (
        jnp.einsum("bhqk,bkhd->bqhd", d_scores, keys, preferred_element_type=jnp.float32)
        * score_scale
    ).astype(jnp.bfloat16)
    d_keys = (
        jnp.einsum("bhqk,bqhd->bkhd", d_scores, queries, preferred_element_type=jnp.float32)
        * score_scale
    ).astype(jnp.bfloat16)
    d_projected = jnp.concatenate(
        [
            d_queries.reshape(images, length, model_width),
            d_keys.reshape(images, length, model_width),
            d_values.reshape(images, length, model_width),
        ],
        axis=-1,
    )
    qkv_grad = outer_sum(normed_low, d_projected)
    bias_query = jnp.sum(d_queries.astype(jnp.float32), axis=(0, 1)).reshape(-1)
    bias_value = jnp.sum(d_values.astype(jnp.float32), axis=(0, 1)).reshape(-1)
    d_normed = back_product(d_projected, w_qkv)
    d_input_norm, gain_one_grad, shift_one_grad = norm_pull(d_normed)
    d_input = d_middle + d_input_norm
    block_output, input_grad = (
        slots_out(output.astype(jnp.bfloat16)),
        slots_out(d_input.astype(jnp.bfloat16)),
    )
    local_vectors = jnp.concatenate(
        [
            gain_one_grad[None],
            shift_one_grad[None],
            bias_query[None],
            bias_value[None],
            bias_proj[None],
            gain_two_grad[None],
            shift_two_grad[None],
            bias_up.reshape(4, model_width),
            bias_down[None],
        ],
        axis=0,
    )
    vector_grad = sum_everywhere(local_vectors, group_bits + dp_bits)
    local_grads = (qkv_grad, proj_grad, up_grad, down_grad)
    owned = tuple(
        scatter_sum(whole_to_blocks(part, scatter_steps), scatter_steps) for part in local_grads
    )
    decay_rate = 1.0 - STEP_NUMBER ** (-0.8)
    squares = tuple((gradient * gradient + tiny_square for gradient in owned))
    row_parts = tuple((jnp.sum(square, axis=1) for square in squares)) + tuple(
        (jnp.sum(master * master, axis=1) for master in masters)
    )
    row_sums = sum_parts(row_parts, group_bits)
    rows_old = (qkv_rows, proj_rows, up_rows, down_rows)
    cols_old = (qkv_cols, proj_cols, up_cols, down_cols)
    total_cols = tuple((gradient.shape[1] * lax.axis_size("group") for gradient in owned))
    total_rows = tuple((gradient.shape[0] * lax.axis_size("dp") for gradient in owned))
    rows_new = tuple(
        (
            decay_rate * rows_old[which] + (1.0 - decay_rate) * row_sums[which] / total_cols[which]
            for which in range(4)
        )
    )
    col_parts = (
        tuple((jnp.sum(square, axis=0) for square in squares))
        + tuple((jnp.sum(row_stat) for row_stat in rows_new))
        + tuple((jnp.sum(row_sums[4 + which]) for which in range(4)))
    )
    col_sums = sum_parts(col_parts, dp_bits)
    results = []
    for which in range(4):
        cols_new = (
            decay_rate * cols_old[which] + (1.0 - decay_rate) * col_sums[which] / total_rows[which]
        )
        mean_rows = col_sums[4 + which] / total_rows[which]
        spread = jnp.sqrt(col_sums[8 + which] / (total_rows[which] * total_cols[which]))
        second = rows_new[which][:, None] * cols_new[None, :] / mean_rows
        updated = masters[which] - step_rate * spread * owned[which] * lax.rsqrt(second)
        results.append((owned[which], rows_new[which], cols_new, updated))
    vector_moment_new = decay_rate * vector_moment + (1.0 - decay_rate) * (
        vector_grad * vector_grad + tiny_square
    )
    row_spread = jnp.sqrt(jnp.mean(vectors * vectors, axis=1, keepdims=True))
    vector_new = vectors - step_rate * row_spread * vector_grad * lax.rsqrt(vector_moment_new)
    return (
        block_output,
        input_grad,
        results[0][0],
        results[0][1],
        results[0][2],
        results[0][3],
        results[1][0],
        results[1][1],
        results[1][2],
        results[1][3],
        results[2][0],
        results[2][1],
        results[2][2],
        results[2][3],
        results[3][0],
        results[3][1],
        results[3][2],
        results[3][3],
        vector_grad,
        vector_moment_new,
        vector_new,
    )


def solution(mesh):
    in_specs = (
        P("dp", "group", None),
        P(("dp", "group"), None),
        P("dp", "group", None),
        P("dp", "group"),
        P("dp", "group"),
        P("dp", "group"),
        P("dp", "group"),
        P(),
        P("dp"),
        P("group"),
        P("dp"),
        P("group"),
        P("dp"),
        P("group"),
        P("dp"),
        P("group"),
        P(),
    )
    out_specs = (
        P("dp", "group", None),
        P("dp", "group", None),
        P("dp", "group"),
        P("dp"),
        P("group"),
        P("dp", "group"),
        P("dp", "group"),
        P("dp"),
        P("group"),
        P("dp", "group"),
        P("dp", "group"),
        P("dp"),
        P("group"),
        P("dp", "group"),
        P("dp", "group"),
        P("dp"),
        P("group"),
        P("dp", "group"),
        P(),
        P(),
        P(),
    )
    return jax.shard_map(body, mesh=mesh, in_specs=in_specs, out_specs=out_specs, check_vma=False)
```

```python
import functools
import math

import jax
import jax.numpy as jnp
from jax import lax
from jax.experimental import pallas as pl
from jax.experimental.pallas import tpu as pltpu
from jax.sharding import PartitionSpec as P

HEAD_DIM = 64
STEP_NUMBER = 10


step_rate = 0.3
norm_epsilon = 1e-06
tiny_square = 1e-30
LOG2_E = 1.4426950408889634


def axis_bits(name):
    count = lax.axis_size(name)
    return [(name, 1 << place) for place in range(count.bit_length() - 1)]


def swap_partner(array, step):
    name, bit = step
    count = lax.axis_size(name)
    return lax.ppermute(array, name, [(rank, rank ^ bit) for rank in range(count)])


def upper_side(step):
    name, bit = step
    return (lax.axis_index(name) & bit) != 0


def gather_blocks(array, steps):
    for step in steps:
        arrived = swap_partner(array, step)
        upper = upper_side(step)
        array = jnp.stack([jnp.where(upper, arrived, array), jnp.where(upper, array, arrived)])
    return array


def scatter_sum(array, steps):
    for step in steps:
        upper = upper_side(step)
        leaving = jnp.where(upper, array[0], array[1]).astype(jnp.bfloat16)
        arrived = swap_partner(leaving, step)
        array = jnp.where(upper, array[1], array[0]).astype(jnp.float32) + arrived.astype(jnp.float32)
    return array


def sum_everywhere(array, steps):
    for step in steps:
        array = array + swap_partner(array, step)
    return array


def sum_parts(parts, steps):
    flat = [part.reshape(-1) for part in parts]
    total = sum_everywhere(jnp.concatenate(flat), steps)
    result, start = [], 0
    for part in parts:
        result.append(total[start : start + part.size].reshape(part.shape))
        start += part.size
    return result


def block_order(steps):
    order = []
    for name in ("dp", "group"):
        bits = sorted((step for step in steps if step[0] == name), key=lambda step: -step[1])
        order.append([steps.index(step) for step in bits])
    return order


def blocks_to_whole(blocks, steps):
    count = len(steps)
    rows, cols = blocks.shape[count:]
    dp_axes, group_axes = block_order(steps)
    dp_axes = [count - 1 - axis for axis in dp_axes]
    group_axes = [count - 1 - axis for axis in group_axes]
    whole = blocks.transpose(dp_axes + [count] + group_axes + [count + 1])
    return whole.reshape(rows << len(dp_axes), cols << len(group_axes))


def whole_to_blocks(whole, steps):
    dp_axes, group_axes = block_order(steps)
    rows = whole.shape[0] >> len(dp_axes)
    cols = whole.shape[1] >> len(group_axes)
    split = whole.reshape([2] * len(dp_axes) + [rows] + [2] * len(group_axes) + [cols])
    places = dp_axes + [len(steps)] + group_axes + [len(steps) + 1]
    return split.transpose([places.index(axis) for axis in range(len(places))])


PER_STEP = 4
FF_CHUNK = 256
vmem_bytes = 60 * 1024 * 1024


def dot(left, right, left_axis=1, right_axis=0):
    return lax.dot_general(
        left, right, (((left_axis,), (right_axis,)), ((), ())), preferred_element_type=jnp.float32
    )


def normal_form(values):
    center = jnp.mean(values, axis=-1, keepdims=True)
    centered = values - center
    spread = jnp.mean(centered * centered, axis=-1, keepdims=True)
    scale = lax.rsqrt(spread + norm_epsilon)
    return centered * scale, scale


def norm_back(grad, unit, scale, gain):
    weighted = grad * gain
    along = jnp.mean(weighted * unit, axis=-1, keepdims=True)
    level = jnp.mean(weighted, axis=-1, keepdims=True)
    return scale * (weighted - level - unit * along)


def column_sum(values):
    return jnp.sum(values, axis=0, keepdims=True)


def pair_mask(length):
    return lax.broadcasted_iota(jnp.int32, (length, 2 * HEAD_DIM), 1) < HEAD_DIM


def stack_heads(pair, first):
    none = jnp.zeros_like(pair)
    return jnp.concatenate([jnp.where(first, pair, none), jnp.where(first, none, pair)], axis=0)


def join_heads(rows, first):
    length = rows.shape[0] // 2
    return jnp.where(first, rows[:length], rows[length:])


def gelu_and_slope(pre):
    bell = jnp.exp2(pre * pre * (-0.5 * LOG2_E))
    inverse = 1.0 / (1.0 + (0.3275911 * 0.5**0.5) * jnp.abs(pre))
    poly = inverse * (
        0.5 * 0.254829592
        + inverse
        * (
            0.5 * -0.284496736
            + inverse
            * (0.5 * 1.421413741 + inverse * (0.5 * -1.453152027 + inverse * (0.5 * 1.061405429)))
        )
    )
    tail = poly * bell
    below = jnp.where(pre >= 0, 1.0 - tail, tail)
    return pre * below, below + pre * bell * 0.3989422804014327


def widen(source_ref, wide_ref, images):
    tiles, total, lanes = wide_ref.shape
    rows_at_once = 8 * images

    @pl.loop(0, total // rows_at_once)
    def _(part):
        rows = pl.ds(pl.multiple_of(part * rows_at_once, rows_at_once), rows_at_once)
        for tile in range(tiles):
            cols = slice(tile * lanes, (tile + 1) * lanes)
            wide_ref[tile, rows, :] = source_ref[rows, cols].astype(jnp.float32)


def narrow(wide_ref, target_ref, images):
    tiles, total, lanes = wide_ref.shape
    rows_at_once = 8 * images

    @pl.loop(0, total // rows_at_once)
    def _(part):
        rows = pl.ds(pl.multiple_of(part * rows_at_once, rows_at_once), rows_at_once)
        for tile in range(tiles):
            cols = slice(tile * lanes, (tile + 1) * lanes)
            target_ref[rows, cols] = wide_ref[tile, rows, :].astype(target_ref.dtype)


def take_image(wide_ref, image, images):
    tiles, total, _ = wide_ref.shape
    rows = pl.ds(image, total // images, images)
    return jnp.concatenate([wide_ref[tile, rows, :] for tile in range(tiles)], axis=1)


def put_image(wide_ref, image, images, values):
    tiles, total, lanes = wide_ref.shape
    rows = pl.ds(image, total // images, images)
    for tile in range(tiles):
        wide_ref[tile, rows, :] = values[:, tile * lanes : (tile + 1) * lanes]


def attention_kernel(
    images, tokens_ref, bias_ref, w_qkv_ref, w_proj_ref, vectors_ref,
    x_ref, qkv_ref, probs_ref, attended_ref, middle_ref, wide_ref, normed_ref,
):
    step = pl.program_id(0)
    length = tokens_ref.shape[0] // images
    width = tokens_ref.shape[1]
    per_step = bias_ref.shape[0]

    @pl.when(step == 0)
    def _():
        widen(tokens_ref, wide_ref, images)

    for image in range(per_step):
        rows = slice(image * length, (image + 1) * length)
        x = take_image(wide_ref, step * per_step + image, images)
        x_ref[rows, :] = x.astype(jnp.bfloat16)
        unit, _ = normal_form(x)
        normed_ref[rows, :] = (unit * vectors_ref[0:1] + vectors_ref[1:2]).astype(jnp.bfloat16)
    for part in range(3):
        cols = slice(part * width, (part + 1) * width)
        projected = dot(normed_ref[...], w_qkv_ref[:, cols])
        if part != 1:
            row = 2 if part == 0 else 3
            projected = projected + vectors_ref[row : row + 1]
        qkv_ref[:, cols] = projected.astype(jnp.bfloat16)

    @pl.loop(0, per_step)
    def _(image):
        rows = pl.ds(pl.multiple_of(image * length, length), length)
        first = pair_mask(length)
        place = lax.broadcasted_iota(jnp.int32, (length, 2 * length), 0)
        asker = lax.broadcasted_iota(jnp.int32, (length, 2 * length), 1)
        asker = jnp.where(asker >= length, asker - length, asker)
        bias = jnp.where(place == asker, 0.0, bias_ref[image])
        for pair in range(width // (2 * HEAD_DIM)):
            low = pair * 2 * HEAD_DIM
            queries = stack_heads(qkv_ref[rows, low : low + 2 * HEAD_DIM], first)
            keys = qkv_ref[rows, width + low : width + low + 2 * HEAD_DIM]
            values = qkv_ref[rows, 2 * width + low : 2 * width + low + 2 * HEAD_DIM]
            scores = dot(keys, queries, 1, 1) * (HEAD_DIM**-0.5 * LOG2_E) + bias
            weights = jnp.exp2(scores - jnp.max(scores, axis=0, keepdims=True))
            probs = weights * (1.0 / jnp.sum(weights, axis=0, keepdims=True))
            probs = probs.astype(jnp.bfloat16)
            probs_ref[image, pair] = probs
            attended = join_heads(dot(probs, values, 0, 0), first)
            attended_ref[rows, low : low + 2 * HEAD_DIM] = attended.astype(jnp.bfloat16)

    middle_ref[...] = (
        x_ref[...].astype(jnp.float32)
        + dot(attended_ref[...], w_proj_ref[...])
        + vectors_ref[4:5]
    )


def feed_forward_kernel(
    images, middle_ref, cotangent_ref, attended_ref, w_up_ref, w_down_ref, w_proj_ref, vectors_ref, bias_up_ref,
    output_ref, d_middle_ref, d_attended_ref, up_grad_ref, down_grad_ref, proj_grad_ref, vector_sums_ref, up_sums_ref,
    wide_ref, normed_ref, normed_t_ref, dy_ref, dy_t_ref, unit_ref, scale_ref, ahead_ref, back_ref,
    up_total_ref, down_total_ref, proj_total_ref,
):
    step = pl.program_id(0)
    length = cotangent_ref.shape[0] // images
    width = middle_ref.shape[1]
    hidden = w_up_ref.shape[1]
    per_step = middle_ref.shape[0] // length

    @pl.when(step == 0)
    def _():
        widen(cotangent_ref, wide_ref, images)
        for total in (up_total_ref, down_total_ref, proj_total_ref, vector_sums_ref, up_sums_ref):
            total[...] = jnp.zeros_like(total)

    for image in range(per_step):
        rows = slice(image * length, (image + 1) * length)
        dy = take_image(wide_ref, step * per_step + image, images)
        dy_ref[rows, :] = dy.astype(jnp.bfloat16)
        vector_sums_ref[3:4] += column_sum(dy)
        unit, scale = normal_form(middle_ref[rows, :])
        unit_ref[rows, :] = unit
        scale_ref[rows, :] = jnp.broadcast_to(scale, (length, scale_ref.shape[1]))
        normed_ref[rows, :] = (unit * vectors_ref[5:6] + vectors_ref[6:7]).astype(jnp.bfloat16)
    normed_t_ref[...] = normed_ref[...].T
    dy_t_ref[...] = dy_ref[...].T
    ahead_ref[...] = jnp.zeros_like(ahead_ref)
    back_ref[...] = jnp.zeros_like(back_ref)

    @pl.loop(0, hidden // FF_CHUNK)
    def _(chunk):
        cols = pl.ds(pl.multiple_of(chunk * FF_CHUNK, FF_CHUNK), FF_CHUNK)
        w_up = w_up_ref[:, cols]
        w_down = w_down_ref[cols, :]
        active, slope = gelu_and_slope(dot(normed_ref[...], w_up) + bias_up_ref[:, cols])
        active = active.astype(jnp.bfloat16)
        d_hidden = dot(dy_ref[...], w_down, 1, 1) * slope
        d_hidden = d_hidden.astype(jnp.bfloat16)
        ahead_ref[...] += dot(active, w_down)
        back_ref[...] += dot(d_hidden, w_up, 1, 1)
        down_total_ref[:, cols] += dot(dy_t_ref[...], active)
        up_total_ref[:, cols] += dot(normed_t_ref[...], d_hidden)
        up_sums_ref[:, cols] += column_sum(d_hidden.astype(jnp.float32))

    for image in range(per_step):
        rows = slice(image * length, (image + 1) * length)
        output = middle_ref[rows, :] + ahead_ref[rows, :] + vectors_ref[11:12]
        put_image(wide_ref, step * per_step + image, images, output)
        unit = unit_ref[rows, :]
        grad = back_ref[rows, :]
        vector_sums_ref[1:2] += column_sum(grad * unit)
        vector_sums_ref[2:3] += column_sum(grad)
        d_middle = dy_ref[rows, :].astype(jnp.float32) + norm_back(
            grad, unit, scale_ref[rows, 0:1], vectors_ref[5:6]
        )
        d_middle_ref[rows, :] = d_middle
        d_branch = d_middle.astype(jnp.bfloat16)
        dy_ref[rows, :] = d_branch
        vector_sums_ref[0:1] += column_sum(d_branch.astype(jnp.float32))
    proj_total_ref[...] += dot(attended_ref[...], dy_ref[...], 0, 0)
    d_attended_ref[...] = dot(dy_ref[...], w_proj_ref[...], 1, 1).astype(jnp.bfloat16)

    @pl.when(step == pl.num_programs(0) - 1)
    def _():
        narrow(wide_ref, output_ref, images)
        up_grad_ref[...] = up_total_ref[...].astype(jnp.bfloat16)
        down_grad_ref[...] = down_total_ref[...].T.astype(jnp.bfloat16)
        proj_grad_ref[...] = proj_total_ref[...].astype(jnp.bfloat16)


def attention_back_kernel(
    images, x_ref, qkv_ref, probs_ref, d_attended_ref, d_middle_ref, w_qkv_ref, vectors_ref,
    input_grad_ref, qkv_grad_ref, vector_sums_ref, wide_ref, normed_ref, d_projected_ref, back_ref, qkv_total_ref,
):
    step = pl.program_id(0)
    width = x_ref.shape[1]
    length = probs_ref.shape[2]
    per_step = probs_ref.shape[0]

    @pl.when(step == 0)
    def _():
        qkv_total_ref[...] = jnp.zeros_like(qkv_total_ref)
        vector_sums_ref[...] = jnp.zeros_like(vector_sums_ref)

    @pl.loop(0, per_step)
    def _(image):
        rows = pl.ds(pl.multiple_of(image * length, length), length)
        first = pair_mask(length)
        for pair in range(width // (2 * HEAD_DIM)):
            low = pair * 2 * HEAD_DIM
            cols = [slice(part * width + low, part * width + low + 2 * HEAD_DIM) for part in range(3)]
            queries = stack_heads(qkv_ref[rows, cols[0]], first)
            keys = qkv_ref[rows, cols[1]]
            values = qkv_ref[rows, cols[2]]
            probs = probs_ref[image, pair]
            d_attended = stack_heads(d_attended_ref[rows, cols[0]], first)
            d_projected_ref[rows, cols[2]] = dot(probs, d_attended).astype(jnp.bfloat16)
            d_probs = dot(values, d_attended, 1, 1)
            probs = probs.astype(jnp.float32)
            along = jnp.sum(d_probs * probs, axis=0, keepdims=True)
            d_scores = (probs * (d_probs - along)).astype(jnp.bfloat16)
            scale = HEAD_DIM**-0.5
            d_queries = join_heads(dot(d_scores, keys, 0, 0), first) * scale
            d_projected_ref[rows, cols[0]] = d_queries.astype(jnp.bfloat16)
            d_projected_ref[rows, cols[1]] = (dot(d_scores, queries) * scale).astype(jnp.bfloat16)

    vector_sums_ref[2:3] += column_sum(d_projected_ref[:, :width].astype(jnp.float32))
    vector_sums_ref[3:4] += column_sum(d_projected_ref[:, 2 * width :].astype(jnp.float32))
    back_ref[...] = dot(d_projected_ref[...], w_qkv_ref[...], 1, 1)
    for image in range(per_step):
        rows = slice(image * length, (image + 1) * length)
        unit, scale = normal_form(x_ref[rows, :].astype(jnp.float32))
        normed_ref[rows, :] = (unit * vectors_ref[0:1] + vectors_ref[1:2]).astype(jnp.bfloat16)
        grad = back_ref[rows, :]
        vector_sums_ref[0:1] += column_sum(grad * unit)
        vector_sums_ref[1:2] += column_sum(grad)
        d_input = d_middle_ref[rows, :] + norm_back(grad, unit, scale, vectors_ref[0:1])
        put_image(wide_ref, step * per_step + image, images, d_input)
    qkv_total_ref[...] += dot(normed_ref[...], d_projected_ref[...], 0, 0)

    @pl.when(step == pl.num_programs(0) - 1)
    def _():
        narrow(wide_ref, input_grad_ref, images)
        qkv_grad_ref[...] = qkv_total_ref[...].astype(jnp.bfloat16)


def whole_block(shape):
    return pl.BlockSpec(shape, lambda step: (0,) * len(shape))


def step_block(shape):
    return pl.BlockSpec(shape, lambda step: (step,) + (0,) * (len(shape) - 1))


def scratch(*shape, dtype=jnp.float32):
    return pltpu.VMEM(shape, dtype)


def call_kernel(kernel, images, steps, ins, outs, scratches, operands, flops, transcendentals=0):
    in_specs = [
        whole_block(op.shape) if block is None else step_block(block)
        for op, block in zip(operands, ins)
    ]
    out_specs = [
        whole_block(shape) if block is None else step_block(block) for shape, dtype, block in outs
    ]
    moved = sum(op.size * op.dtype.itemsize for op in operands) + sum(
        math.prod(shape) * jnp.dtype(dtype).itemsize for shape, dtype, block in outs
    )
    return pl.pallas_call(
        functools.partial(kernel, images),
        grid=(steps,),
        in_specs=in_specs,
        out_specs=out_specs,
        out_shape=[jax.ShapeDtypeStruct(shape, dtype) for shape, dtype, block in outs],
        scratch_shapes=scratches,
        compiler_params=pltpu.CompilerParams(vmem_limit_bytes=vmem_bytes),
        cost_estimate=pl.CostEstimate(
            flops=flops, bytes_accessed=moved, transcendentals=transcendentals
        ),
    )(*operands)


def attention_forward(tokens, bias, w_qkv, w_proj, vectors):
    images, length, _ = bias.shape
    total, width = tokens.shape
    pairs = width // (2 * HEAD_DIM)
    rows = PER_STEP * length
    low, high = jnp.bfloat16, jnp.float32
    outs = [
        ((total, width), low, (rows, width)),
        ((total, 3 * width), low, (rows, 3 * width)),
        ((images, pairs, length, 2 * length), low, (PER_STEP, pairs, length, 2 * length)),
        ((total, width), low, (rows, width)),
        ((total, width), high, (rows, width)),
    ]
    return call_kernel(
        attention_kernel, images, images // PER_STEP,
        [None, (PER_STEP, length, 1), None, None, None], outs,
        [scratch(width // 128, total, 128), scratch(rows, width, dtype=low)],
        (tokens, bias, w_qkv, w_proj, vectors),
        2 * total * width * 4 * width + 8 * total * length * width,
    )


def feed_forward(images, middle, cotangent, attended, w_up, w_down, w_proj, vectors):
    total, width = middle.shape
    hidden = w_up.shape[1]
    rows = total // images * PER_STEP
    low, high = jnp.bfloat16, jnp.float32
    block = (rows, width)
    outs = [
        ((total, width), low, None),
        ((total, width), high, block),
        ((total, width), low, block),
        ((width, hidden), low, None),
        ((hidden, width), low, None),
        ((width, width), low, None),
        ((8, width), high, None),
        ((1, hidden), high, None),
    ]
    scratches = [
        scratch(width // 128, total, 128),
        scratch(rows, width, dtype=low),
        scratch(width, rows, dtype=low),
        scratch(rows, width, dtype=low),
        scratch(width, rows, dtype=low),
        scratch(rows, width),
        scratch(rows, 128),
        scratch(rows, width),
        scratch(rows, width),
        scratch(width, hidden),
        scratch(width, hidden),
        scratch(width, width),
    ]
    return call_kernel(
        feed_forward_kernel, images, images // PER_STEP,
        [block, None, block, None, None, None, None, None], outs, scratches,
        (middle, cotangent, attended, w_up, w_down, w_proj, vectors, vectors[7:11].reshape(1, hidden)),
        12 * total * width * hidden + 4 * total * width * width, total * hidden,
    )


def attention_back(x, qkv, probs, d_attended, d_middle, w_qkv, vectors):
    images, pairs, length, _ = probs.shape
    total, width = x.shape
    rows = PER_STEP * length
    low, high = jnp.bfloat16, jnp.float32
    block = (rows, width)
    outs = [
        ((total, width), low, None),
        ((width, 3 * width), low, None),
        ((8, width), high, None),
    ]
    scratches = [
        scratch(width // 128, total, 128),
        scratch(rows, width, dtype=low),
        scratch(rows, 3 * width, dtype=low),
        scratch(rows, width),
        scratch(width, 3 * width),
    ]
    return call_kernel(
        attention_back_kernel, images, images // PER_STEP,
        [block, (rows, 3 * width), (PER_STEP, pairs, length, 2 * length), block, block, None, None],
        outs, scratches, (x, qkv, probs, d_attended, d_middle, w_qkv, vectors),
        4 * total * width * 3 * width + 16 * total * length * width,
    )


def body(
    tokens,
    keep_mask,
    cotangent,
    qkv_weight,
    proj_weight,
    up_weight,
    down_weight,
    vectors,
    qkv_rows,
    qkv_cols,
    proj_rows,
    proj_cols,
    up_rows,
    up_cols,
    down_rows,
    down_cols,
    vector_moment,
):
    masters = (qkv_weight, proj_weight, up_weight, down_weight)
    lowered = tuple((master.astype(jnp.bfloat16) for master in masters))
    dp_bits, group_bits = axis_bits("dp"), axis_bits("group")
    gather_steps = dp_bits[1:] + group_bits[1:] + dp_bits[:1] + group_bits[:1]
    scatter_steps = gather_steps[::-1]
    w_qkv, w_proj, w_up, w_down = tuple(
        blocks_to_whole(gather_blocks(part, gather_steps), gather_steps) for part in lowered
    )
    spread = lax.axis_size("group")

    def slots_in(array):
        held, slots, width = array.shape
        parts = array.transpose(1, 0, 2).reshape(slots, spread, held // spread, width)
        parts = lax.all_to_all(
            parts.transpose(1, 0, 2, 3), "group", split_axis=0, concat_axis=0, tiled=True
        )
        return parts.reshape(spread * slots * (held // spread), width)

    def slots_out(array):
        held, slots, width = tokens.shape
        parts = array.reshape(spread, slots, held // spread, width)
        parts = lax.all_to_all(parts, "group", split_axis=0, concat_axis=0, tiled=True)
        return parts.transpose(1, 0, 2, 3).reshape(slots, held, width).transpose(1, 0, 2)

    images = keep_mask.shape[0]
    bias = jnp.where(keep_mask > 0, 0.0, -1e30)[:, :, None]
    x, qkv, probs, attended, middle = attention_forward(
        slots_in(tokens), bias, w_qkv, w_proj, vectors
    )
    output, d_middle, d_attended, up_grad, down_grad, proj_grad, ff_sums, up_sums = feed_forward(
        images, middle, slots_in(cotangent), attended, w_up, w_down, w_proj, vectors
    )
    block_output = slots_out(output)
    d_input, qkv_grad, att_sums = attention_back(
        x, qkv, probs, d_attended, d_middle, w_qkv, vectors
    )
    input_grad = slots_out(d_input)
    local_vectors = jnp.concatenate(
        [att_sums[:4], ff_sums[:3], up_sums.reshape(4, -1), ff_sums[3:4]], axis=0
    )
    vector_grad = sum_everywhere(local_vectors, group_bits + dp_bits)
    local_grads = (qkv_grad, proj_grad, up_grad, down_grad)
    owned = tuple(
        scatter_sum(whole_to_blocks(part, scatter_steps), scatter_steps) for part in local_grads
    )
    decay_rate = 1.0 - STEP_NUMBER ** (-0.8)
    squares = tuple((gradient * gradient + tiny_square for gradient in owned))
    row_parts = tuple((jnp.sum(square, axis=1) for square in squares)) + tuple(
        (jnp.sum(master * master, axis=1) for master in masters)
    )
    row_sums = sum_parts(row_parts, group_bits)
    rows_old = (qkv_rows, proj_rows, up_rows, down_rows)
    cols_old = (qkv_cols, proj_cols, up_cols, down_cols)
    total_cols = tuple((gradient.shape[1] * lax.axis_size("group") for gradient in owned))
    total_rows = tuple((gradient.shape[0] * lax.axis_size("dp") for gradient in owned))
    rows_new = tuple(
        (
            decay_rate * rows_old[which] + (1.0 - decay_rate) * row_sums[which] / total_cols[which]
            for which in range(4)
        )
    )
    col_parts = (
        tuple((jnp.sum(square, axis=0) for square in squares))
        + tuple((jnp.sum(row_stat) for row_stat in rows_new))
        + tuple((jnp.sum(row_sums[4 + which]) for which in range(4)))
    )
    col_sums = sum_parts(col_parts, dp_bits)
    results = []
    for which in range(4):
        cols_new = (
            decay_rate * cols_old[which] + (1.0 - decay_rate) * col_sums[which] / total_rows[which]
        )
        mean_rows = col_sums[4 + which] / total_rows[which]
        spread = jnp.sqrt(col_sums[8 + which] / (total_rows[which] * total_cols[which]))
        second = rows_new[which][:, None] * cols_new[None, :] / mean_rows
        updated = masters[which] - step_rate * spread * owned[which] * lax.rsqrt(second)
        results.append((owned[which], rows_new[which], cols_new, updated))
    vector_moment_new = decay_rate * vector_moment + (1.0 - decay_rate) * (
        vector_grad * vector_grad + tiny_square
    )
    row_spread = jnp.sqrt(jnp.mean(vectors * vectors, axis=1, keepdims=True))
    vector_new = vectors - step_rate * row_spread * vector_grad * lax.rsqrt(vector_moment_new)
    return (
        block_output,
        input_grad,
        results[0][0],
        results[0][1],
        results[0][2],
        results[0][3],
        results[1][0],
        results[1][1],
        results[1][2],
        results[1][3],
        results[2][0],
        results[2][1],
        results[2][2],
        results[2][3],
        results[3][0],
        results[3][1],
        results[3][2],
        results[3][3],
        vector_grad,
        vector_moment_new,
        vector_new,
    )


def solution(mesh):
    in_specs = (
        P("dp", "group", None),
        P(("dp", "group"), None),
        P("dp", "group", None),
        P("dp", "group"),
        P("dp", "group"),
        P("dp", "group"),
        P("dp", "group"),
        P(),
        P("dp"),
        P("group"),
        P("dp"),
        P("group"),
        P("dp"),
        P("group"),
        P("dp"),
        P("group"),
        P(),
    )
    out_specs = (
        P("dp", "group", None),
        P("dp", "group", None),
        P("dp", "group"),
        P("dp"),
        P("group"),
        P("dp", "group"),
        P("dp", "group"),
        P("dp"),
        P("group"),
        P("dp", "group"),
        P("dp", "group"),
        P("dp"),
        P("group"),
        P("dp", "group"),
        P("dp", "group"),
        P("dp"),
        P("group"),
        P("dp", "group"),
        P(),
        P(),
        P(),
    )
    return jax.shard_map(body, mesh=mesh, in_specs=in_specs, out_specs=out_specs, check_vma=False)
```

```python
import functools
import math

import jax
import jax.numpy as jnp
from jax import lax
from jax.experimental import pallas as pl
from jax.experimental.pallas import tpu as pltpu
from jax.sharding import PartitionSpec as P

HEAD_DIM = 64
STEP_NUMBER = 10


step_rate = 0.3
norm_epsilon = 1e-06
tiny_square = 1e-30
decay_rate = 1.0 - STEP_NUMBER ** (-0.8)
LOG2_E = 1.4426950408889634


def axis_bits(name):
    count = lax.axis_size(name)
    return [(name, 1 << place) for place in range(count.bit_length() - 1)]


def swap_partner(array, step):
    name, bit = step
    count = lax.axis_size(name)
    return lax.ppermute(array, name, [(rank, rank ^ bit) for rank in range(count)])


def upper_side(step):
    name, bit = step
    return (lax.axis_index(name) & bit) != 0


def gather_blocks(array, steps):
    for step in steps:
        arrived = swap_partner(array, step)
        upper = upper_side(step)
        array = jnp.stack([jnp.where(upper, arrived, array), jnp.where(upper, array, arrived)])
    return array


def scatter_sum(array, steps):
    for step in steps:
        upper = upper_side(step)
        leaving = jnp.where(upper, array[0], array[1]).astype(jnp.bfloat16)
        arrived = swap_partner(leaving, step)
        array = jnp.where(upper, array[1], array[0]).astype(jnp.float32) + arrived.astype(jnp.float32)
    return array


def sum_everywhere(array, steps):
    for step in steps:
        array = array + swap_partner(array, step)
    return array


def sum_parts(parts, steps):
    flat = [part.reshape(-1) for part in parts]
    total = sum_everywhere(jnp.concatenate(flat), steps)
    result, start = [], 0
    for part in parts:
        result.append(total[start : start + part.size].reshape(part.shape))
        start += part.size
    return result


def block_order(steps):
    order = []
    for name in ("dp", "group"):
        bits = sorted((step for step in steps if step[0] == name), key=lambda step: -step[1])
        order.append([steps.index(step) for step in bits])
    return order


def blocks_to_whole(blocks, steps):
    count = len(steps)
    rows, cols = blocks.shape[count:]
    dp_axes, group_axes = block_order(steps)
    dp_axes = [count - 1 - axis for axis in dp_axes]
    group_axes = [count - 1 - axis for axis in group_axes]
    whole = blocks.transpose(dp_axes + [count] + group_axes + [count + 1])
    return whole.reshape(rows << len(dp_axes), cols << len(group_axes))


def whole_to_blocks(whole, steps):
    dp_axes, group_axes = block_order(steps)
    rows = whole.shape[0] >> len(dp_axes)
    cols = whole.shape[1] >> len(group_axes)
    split = whole.reshape([2] * len(dp_axes) + [rows] + [2] * len(group_axes) + [cols])
    places = dp_axes + [len(steps)] + group_axes + [len(steps) + 1]
    return split.transpose([places.index(axis) for axis in range(len(places))])


PER_STEP = 4
FF_CHUNK = 256
vmem_bytes = 60 * 1024 * 1024


def dot(left, right, left_axis=1, right_axis=0):
    return lax.dot_general(
        left, right, (((left_axis,), (right_axis,)), ((), ())), preferred_element_type=jnp.float32
    )


def normal_form(values):
    center = jnp.mean(values, axis=-1, keepdims=True)
    centered = values - center
    spread = jnp.mean(centered * centered, axis=-1, keepdims=True)
    scale = lax.rsqrt(spread + norm_epsilon)
    return centered * scale, scale


def norm_back(grad, unit, scale, gain):
    weighted = grad * gain
    along = jnp.mean(weighted * unit, axis=-1, keepdims=True)
    level = jnp.mean(weighted, axis=-1, keepdims=True)
    return scale * (weighted - level - unit * along)


def column_sum(values):
    return jnp.sum(values, axis=0, keepdims=True)


def pair_mask(length):
    return lax.broadcasted_iota(jnp.int32, (length, 2 * HEAD_DIM), 1) < HEAD_DIM


def stack_heads(pair, first):
    none = jnp.zeros_like(pair)
    return jnp.concatenate([jnp.where(first, pair, none), jnp.where(first, none, pair)], axis=0)


def join_heads(rows, first):
    length = rows.shape[0] // 2
    return jnp.where(first, rows[:length], rows[length:])


def gelu_and_slope(pre):
    bell = jnp.exp2(pre * pre * (-0.5 * LOG2_E))
    inverse = 1.0 / (1.0 + (0.3275911 * 0.5**0.5) * jnp.abs(pre))
    poly = inverse * (
        0.5 * 0.254829592
        + inverse
        * (
            0.5 * -0.284496736
            + inverse
            * (0.5 * 1.421413741 + inverse * (0.5 * -1.453152027 + inverse * (0.5 * 1.061405429)))
        )
    )
    tail = poly * bell
    below = jnp.where(pre >= 0, 1.0 - tail, tail)
    return pre * below, below + pre * bell * 0.3989422804014327


def widen(source_ref, wide_ref, images):
    tiles, total, lanes = wide_ref.shape
    rows_at_once = 8 * images

    @pl.loop(0, total // rows_at_once)
    def _(part):
        rows = pl.ds(pl.multiple_of(part * rows_at_once, rows_at_once), rows_at_once)
        for tile in range(tiles):
            cols = slice(tile * lanes, (tile + 1) * lanes)
            wide_ref[tile, rows, :] = source_ref[rows, cols].astype(jnp.float32)


def narrow(wide_ref, target_ref, images):
    tiles, total, lanes = wide_ref.shape
    rows_at_once = 8 * images

    @pl.loop(0, total // rows_at_once)
    def _(part):
        rows = pl.ds(pl.multiple_of(part * rows_at_once, rows_at_once), rows_at_once)
        for tile in range(tiles):
            cols = slice(tile * lanes, (tile + 1) * lanes)
            target_ref[rows, cols] = wide_ref[tile, rows, :].astype(target_ref.dtype)


def take_image(wide_ref, image, images):
    tiles, total, _ = wide_ref.shape
    rows = pl.ds(image, total // images, images)
    return jnp.concatenate([wide_ref[tile, rows, :] for tile in range(tiles)], axis=1)


def put_image(wide_ref, image, images, values):
    tiles, total, lanes = wide_ref.shape
    rows = pl.ds(image, total // images, images)
    for tile in range(tiles):
        wide_ref[tile, rows, :] = values[:, tile * lanes : (tile + 1) * lanes]


def attention_kernel(images, tokens_ref, *refs):
    wide_ref = refs[-2]

    @pl.when(pl.program_id(0) == 0)
    def _():
        widen(tokens_ref, wide_ref, images)

    attention_steps(images, *refs)


def attention_steps(
    images, bias_ref, w_qkv_ref, w_proj_ref, vectors_ref,
    x_ref, qkv_ref, probs_ref, attended_ref, middle_ref, wide_ref, normed_ref,
):
    step = pl.program_id(0)
    length = bias_ref.shape[1]
    width = x_ref.shape[1]
    per_step = bias_ref.shape[0]

    for image in range(per_step):
        rows = slice(image * length, (image + 1) * length)
        x = take_image(wide_ref, step * per_step + image, images)
        x_ref[rows, :] = x.astype(jnp.bfloat16)
        unit, _ = normal_form(x)
        normed_ref[rows, :] = (unit * vectors_ref[0:1] + vectors_ref[1:2]).astype(jnp.bfloat16)
    for part in range(3):
        cols = slice(part * width, (part + 1) * width)
        projected = dot(normed_ref[...], w_qkv_ref[:, cols])
        if part != 1:
            row = 2 if part == 0 else 3
            projected = projected + vectors_ref[row : row + 1]
        qkv_ref[:, cols] = projected.astype(jnp.bfloat16)

    @pl.loop(0, per_step)
    def _(image):
        rows = pl.ds(pl.multiple_of(image * length, length), length)
        first = pair_mask(length)
        place = lax.broadcasted_iota(jnp.int32, (length, 2 * length), 0)
        asker = lax.broadcasted_iota(jnp.int32, (length, 2 * length), 1)
        asker = jnp.where(asker >= length, asker - length, asker)
        bias = jnp.where(place == asker, 0.0, bias_ref[image])
        for pair in range(width // (2 * HEAD_DIM)):
            low = pair * 2 * HEAD_DIM
            queries = stack_heads(qkv_ref[rows, low : low + 2 * HEAD_DIM], first)
            keys = qkv_ref[rows, width + low : width + low + 2 * HEAD_DIM]
            values = qkv_ref[rows, 2 * width + low : 2 * width + low + 2 * HEAD_DIM]
            scores = dot(keys, queries, 1, 1) * (HEAD_DIM**-0.5 * LOG2_E) + bias
            weights = jnp.exp2(scores - jnp.max(scores, axis=0, keepdims=True))
            probs = weights * (1.0 / jnp.sum(weights, axis=0, keepdims=True))
            probs = probs.astype(jnp.bfloat16)
            probs_ref[image, pair] = probs
            attended = join_heads(dot(probs, values, 0, 0), first)
            attended_ref[rows, low : low + 2 * HEAD_DIM] = attended.astype(jnp.bfloat16)

    middle_ref[...] = (
        x_ref[...].astype(jnp.float32)
        + dot(attended_ref[...], w_proj_ref[...])
        + vectors_ref[4:5]
    )


def feed_forward_kernel(
    images, middle_ref, cotangent_ref, attended_ref, w_up_ref, w_down_ref, w_proj_ref, vectors_ref, bias_up_ref,
    output_ref, d_middle_ref, d_attended_ref, up_grad_ref, down_grad_ref, proj_grad_ref, vector_sums_ref, up_sums_ref,
    wide_ref, *scratches,
):
    up_total_ref, down_total_ref, proj_total_ref = scratches[-3:]

    @pl.when(pl.program_id(0) == 0)
    def _():
        widen(cotangent_ref, wide_ref, images)

    feed_forward_steps(
        images, middle_ref, attended_ref, w_up_ref, w_down_ref, w_proj_ref, vectors_ref, bias_up_ref,
        d_middle_ref, d_attended_ref, vector_sums_ref, up_sums_ref, wide_ref, *scratches,
    )

    @pl.when(pl.program_id(0) == pl.num_programs(0) - 1)
    def _():
        narrow(wide_ref, output_ref, images)
        up_grad_ref[...] = up_total_ref[...].astype(jnp.bfloat16)
        down_grad_ref[...] = down_total_ref[...].T.astype(jnp.bfloat16)
        proj_grad_ref[...] = proj_total_ref[...].astype(jnp.bfloat16)


def feed_forward_steps(
    images, middle_ref, attended_ref, w_up_ref, w_down_ref, w_proj_ref, vectors_ref, bias_up_ref,
    d_middle_ref, d_attended_ref, vector_sums_ref, up_sums_ref,
    wide_ref, normed_ref, normed_t_ref, dy_ref, dy_t_ref, unit_ref, scale_ref, ahead_ref, back_ref,
    up_total_ref, down_total_ref, proj_total_ref,
):
    step = pl.program_id(0)
    length = wide_ref.shape[1] // images
    hidden = w_up_ref.shape[1]
    per_step = middle_ref.shape[0] // length

    @pl.when(step == 0)
    def _():
        for total in (up_total_ref, down_total_ref, proj_total_ref, vector_sums_ref, up_sums_ref):
            total[...] = jnp.zeros_like(total)

    for image in range(per_step):
        rows = slice(image * length, (image + 1) * length)
        dy = take_image(wide_ref, step * per_step + image, images)
        dy_ref[rows, :] = dy.astype(jnp.bfloat16)
        vector_sums_ref[3:4] += column_sum(dy)
        unit, scale = normal_form(middle_ref[rows, :])
        unit_ref[rows, :] = unit
        scale_ref[rows, :] = jnp.broadcast_to(scale, (length, scale_ref.shape[1]))
        normed_ref[rows, :] = (unit * vectors_ref[5:6] + vectors_ref[6:7]).astype(jnp.bfloat16)
    normed_t_ref[...] = normed_ref[...].T
    dy_t_ref[...] = dy_ref[...].T
    ahead_ref[...] = jnp.zeros_like(ahead_ref)
    back_ref[...] = jnp.zeros_like(back_ref)

    @pl.loop(0, hidden // FF_CHUNK)
    def _(chunk):
        cols = pl.ds(pl.multiple_of(chunk * FF_CHUNK, FF_CHUNK), FF_CHUNK)
        w_up = w_up_ref[:, cols]
        w_down = w_down_ref[cols, :]
        active, slope = gelu_and_slope(dot(normed_ref[...], w_up) + bias_up_ref[:, cols])
        active = active.astype(jnp.bfloat16)
        d_hidden = dot(dy_ref[...], w_down, 1, 1) * slope
        d_hidden = d_hidden.astype(jnp.bfloat16)
        ahead_ref[...] += dot(active, w_down)
        back_ref[...] += dot(d_hidden, w_up, 1, 1)
        down_total_ref[:, cols] += dot(dy_t_ref[...], active)
        up_total_ref[:, cols] += dot(normed_t_ref[...], d_hidden)
        up_sums_ref[:, cols] += column_sum(d_hidden.astype(jnp.float32))

    for image in range(per_step):
        rows = slice(image * length, (image + 1) * length)
        output = middle_ref[rows, :] + ahead_ref[rows, :] + vectors_ref[11:12]
        put_image(wide_ref, step * per_step + image, images, output)
        unit = unit_ref[rows, :]
        grad = back_ref[rows, :]
        vector_sums_ref[1:2] += column_sum(grad * unit)
        vector_sums_ref[2:3] += column_sum(grad)
        d_middle = dy_ref[rows, :].astype(jnp.float32) + norm_back(
            grad, unit, scale_ref[rows, 0:1], vectors_ref[5:6]
        )
        d_middle_ref[rows, :] = d_middle
        d_branch = d_middle.astype(jnp.bfloat16)
        dy_ref[rows, :] = d_branch
        vector_sums_ref[0:1] += column_sum(d_branch.astype(jnp.float32))
    proj_total_ref[...] += dot(attended_ref[...], dy_ref[...], 0, 0)
    d_attended_ref[...] = dot(dy_ref[...], w_proj_ref[...], 1, 1).astype(jnp.bfloat16)


def attention_back_kernel(
    images, x_ref, qkv_ref, probs_ref, d_attended_ref, d_middle_ref, w_qkv_ref, vectors_ref,
    input_grad_ref, qkv_grad_ref, vector_sums_ref, wide_ref, *scratches,
):
    attention_back_steps(
        images, x_ref, qkv_ref, probs_ref, d_attended_ref, d_middle_ref, w_qkv_ref, vectors_ref,
        vector_sums_ref, wide_ref, *scratches,
    )

    @pl.when(pl.program_id(0) == pl.num_programs(0) - 1)
    def _():
        narrow(wide_ref, input_grad_ref, images)
        qkv_grad_ref[...] = scratches[-1][...].astype(jnp.bfloat16)


def attention_back_steps(
    images, x_ref, qkv_ref, probs_ref, d_attended_ref, d_middle_ref, w_qkv_ref, vectors_ref,
    vector_sums_ref, wide_ref, normed_ref, d_projected_ref, back_ref, qkv_total_ref,
):
    step = pl.program_id(0)
    width = x_ref.shape[1]
    length = probs_ref.shape[2]
    per_step = probs_ref.shape[0]

    @pl.when(step == 0)
    def _():
        qkv_total_ref[...] = jnp.zeros_like(qkv_total_ref)
        vector_sums_ref[...] = jnp.zeros_like(vector_sums_ref)

    @pl.loop(0, per_step)
    def _(image):
        rows = pl.ds(pl.multiple_of(image * length, length), length)
        first = pair_mask(length)
        for pair in range(width // (2 * HEAD_DIM)):
            low = pair * 2 * HEAD_DIM
            cols = [slice(part * width + low, part * width + low + 2 * HEAD_DIM) for part in range(3)]
            queries = stack_heads(qkv_ref[rows, cols[0]], first)
            keys = qkv_ref[rows, cols[1]]
            values = qkv_ref[rows, cols[2]]
            probs = probs_ref[image, pair]
            d_attended = stack_heads(d_attended_ref[rows, cols[0]], first)
            d_projected_ref[rows, cols[2]] = dot(probs, d_attended).astype(jnp.bfloat16)
            d_probs = dot(values, d_attended, 1, 1)
            probs = probs.astype(jnp.float32)
            along = jnp.sum(d_probs * probs, axis=0, keepdims=True)
            d_scores = (probs * (d_probs - along)).astype(jnp.bfloat16)
            scale = HEAD_DIM**-0.5
            d_queries = join_heads(dot(d_scores, keys, 0, 0), first) * scale
            d_projected_ref[rows, cols[0]] = d_queries.astype(jnp.bfloat16)
            d_projected_ref[rows, cols[1]] = (dot(d_scores, queries) * scale).astype(jnp.bfloat16)

    vector_sums_ref[2:3] += column_sum(d_projected_ref[:, :width].astype(jnp.float32))
    vector_sums_ref[3:4] += column_sum(d_projected_ref[:, 2 * width :].astype(jnp.float32))
    back_ref[...] = dot(d_projected_ref[...], w_qkv_ref[...], 1, 1)
    for image in range(per_step):
        rows = slice(image * length, (image + 1) * length)
        unit, scale = normal_form(x_ref[rows, :].astype(jnp.float32))
        normed_ref[rows, :] = (unit * vectors_ref[0:1] + vectors_ref[1:2]).astype(jnp.bfloat16)
        grad = back_ref[rows, :]
        vector_sums_ref[0:1] += column_sum(grad * unit)
        vector_sums_ref[1:2] += column_sum(grad)
        d_input = d_middle_ref[rows, :] + norm_back(grad, unit, scale, vectors_ref[0:1])
        put_image(wide_ref, step * per_step + image, images, d_input)
    qkv_total_ref[...] += dot(normed_ref[...], d_projected_ref[...], 0, 0)


def whole_block(shape):
    return pl.BlockSpec(shape, lambda step: (0,) * len(shape))


def step_block(shape):
    return pl.BlockSpec(shape, lambda step: (step,) + (0,) * (len(shape) - 1))


def scratch(*shape, dtype=jnp.float32):
    return pltpu.VMEM(shape, dtype)


def call_kernel(kernel, statics, steps, ins, outs, scratches, operands, flops, transcendentals=0):
    in_specs = [
        pl.BlockSpec(memory_space=pltpu.SMEM)
        if block == "place"
        else whole_block(op.shape) if block is None else step_block(block)
        for op, block in zip(operands, ins)
    ]
    out_specs = [
        whole_block(shape) if block is None else step_block(block) for shape, dtype, block in outs
    ]
    moved = sum(op.size * op.dtype.itemsize for op in operands) + sum(
        math.prod(shape) * jnp.dtype(dtype).itemsize for shape, dtype, block in outs
    )
    return pl.pallas_call(
        functools.partial(kernel, *statics),
        grid=(steps,),
        in_specs=in_specs,
        out_specs=out_specs,
        out_shape=[jax.ShapeDtypeStruct(shape, dtype) for shape, dtype, block in outs],
        scratch_shapes=scratches,
        compiler_params=pltpu.CompilerParams(vmem_limit_bytes=vmem_bytes),
        cost_estimate=pl.CostEstimate(
            flops=flops, bytes_accessed=moved, transcendentals=transcendentals
        ),
    )(*operands)


def attention_forward(tokens, bias, w_qkv, w_proj, vectors):
    images, length, _ = bias.shape
    total, width = tokens.shape
    pairs = width // (2 * HEAD_DIM)
    rows = PER_STEP * length
    low, high = jnp.bfloat16, jnp.float32
    outs = [
        ((total, width), low, (rows, width)),
        ((total, 3 * width), low, (rows, 3 * width)),
        ((images, pairs, length, 2 * length), low, (PER_STEP, pairs, length, 2 * length)),
        ((total, width), low, (rows, width)),
        ((total, width), high, (rows, width)),
    ]
    return call_kernel(
        attention_kernel, (images,), images // PER_STEP,
        [None, (PER_STEP, length, 1), None, None, None], outs,
        [scratch(width // 128, total, 128), scratch(rows, width, dtype=low)],
        (tokens, bias, w_qkv, w_proj, vectors),
        2 * total * width * 4 * width + 8 * total * length * width,
    )


def feed_forward(images, middle, cotangent, attended, w_up, w_down, w_proj, vectors):
    total, width = middle.shape
    hidden = w_up.shape[1]
    rows = total // images * PER_STEP
    low, high = jnp.bfloat16, jnp.float32
    block = (rows, width)
    outs = [
        ((total, width), low, None),
        ((total, width), high, block),
        ((total, width), low, block),
        ((width, hidden), low, None),
        ((hidden, width), low, None),
        ((width, width), low, None),
        ((8, width), high, None),
        ((1, hidden), high, None),
    ]
    scratches = [
        scratch(width // 128, total, 128),
        scratch(rows, width, dtype=low),
        scratch(width, rows, dtype=low),
        scratch(rows, width, dtype=low),
        scratch(width, rows, dtype=low),
        scratch(rows, width),
        scratch(rows, 128),
        scratch(rows, width),
        scratch(rows, width),
        scratch(width, hidden),
        scratch(width, hidden),
        scratch(width, width),
    ]
    return call_kernel(
        feed_forward_kernel, (images,), images // PER_STEP,
        [block, None, block, None, None, None, None, None], outs, scratches,
        (middle, cotangent, attended, w_up, w_down, w_proj, vectors, vectors[7:11].reshape(1, hidden)),
        12 * total * width * hidden + 4 * total * width * width, total * hidden,
    )


def attention_back(x, qkv, probs, d_attended, d_middle, w_qkv, vectors):
    images, pairs, length, _ = probs.shape
    total, width = x.shape
    rows = PER_STEP * length
    low, high = jnp.bfloat16, jnp.float32
    block = (rows, width)
    outs = [
        ((total, width), low, None),
        ((width, 3 * width), low, None),
        ((8, width), high, None),
    ]
    scratches = [
        scratch(width // 128, total, 128),
        scratch(rows, width, dtype=low),
        scratch(rows, 3 * width, dtype=low),
        scratch(rows, width),
        scratch(width, 3 * width),
    ]
    return call_kernel(
        attention_back_kernel, (images,), images // PER_STEP,
        [block, (rows, 3 * width), (PER_STEP, pairs, length, 2 * length), block, block, None, None],
        outs, scratches, (x, qkv, probs, d_attended, d_middle, w_qkv, vectors),
        4 * total * width * 3 * width + 16 * total * length * width,
    )

def linear_place():
    return lax.axis_index("dp") * lax.axis_size("group") + lax.axis_index("group")


def permute(array, mask):
    count = lax.axis_size("dp") * lax.axis_size("group")
    return lax.ppermute(array, ("dp", "group"), [(rank, rank ^ mask) for rank in range(count)])


def direct_masks(bits):
    masks = [0]
    for bit in bits:
        masks = masks + [mask | bit for mask in masks]
    return masks[1:]


def gather_packed(block, rounds):
    held = block[None]
    for bits in rounds[:-1]:
        held = jnp.concatenate([held] + [permute(held, mask) for mask in direct_masks(bits)])
    return held, permute(held, rounds[-1][0])


def scatter_packed(held, leaving, rounds):
    held = held.astype(jnp.float32) + permute(leaving, rounds[0][0]).astype(jnp.float32)
    for bits in rounds[1:]:
        masks = direct_masks(bits)
        size = held.shape[0] // (len(masks) + 1)
        parts = [
            permute(held[size * (at + 1) : size * (at + 2)].astype(jnp.bfloat16), mask)
            for at, mask in enumerate(masks)
        ]
        if bits is rounds[-1]:
            return [held[0]] + [part[0] for part in parts]
        held = held[:size]
        for part in parts:
            held = held + part.astype(jnp.float32)


def sum_direct(array, rounds):
    for bits in rounds:
        terms = [array] + [permute(array, mask) for mask in direct_masks(bits)]
        while len(terms) > 1:
            terms = [left + right for left, right in zip(terms[::2], terms[1::2])]
        array = terms[0]
    return array


def packed_place(mask, spread, count):
    return ((mask >> 1) & (spread - 1)) * (count // (2 * spread)) + (mask >> (spread.bit_length()))


def unpack(place_ref, own_ref, arrived_ref, put, dp_size, spread):
    place = place_ref[0]
    odd = (place & 1) == 1
    for row in range(dp_size):
        for col in range(spread):
            at = packed_place((row * spread + col) ^ place, spread, dp_size * spread)
            own = own_ref[at]
            other = arrived_ref[at]
            put(row, col, jnp.where(odd == (col % 2 == 1), own, other))


def pack(place_ref, take, keep_ref, leave_ref, dp_size, spread):
    place = place_ref[0]
    odd = (place & 1) == 1
    for row in range(dp_size):
        for col in range(0, spread, 2):
            at = packed_place((row * spread + col) ^ place, spread, dp_size * spread)
            even_block, odd_block = take(row, col), take(row, col + 1)
            keep_ref[at] = jnp.where(odd, odd_block, even_block)
            leave_ref[at] = jnp.where(odd, even_block, odd_block)


def lane_slice(ref, rows, start, count):
    return ref[rows, start : start + count]


def widen_pieces(place_ref, piece_refs, wide_ref, spread):
    tiles, _, lanes = wide_ref.shape
    rows_of_piece = piece_refs[0].shape[0]
    step = 64
    group = place_ref[0] & (spread - 1)
    for relative, piece_ref in enumerate(piece_refs):
        base = (group ^ relative) * rows_of_piece

        @pl.loop(0, rows_of_piece // step)
        def _(part):
            source = pl.ds(pl.multiple_of(part * step, step), step)
            target = pl.ds(pl.multiple_of(base + part * step, step), step)
            for tile in range(tiles):
                cols = slice(tile * lanes, (tile + 1) * lanes)
                wide_ref[tile, target, :] = piece_ref[source, cols].astype(jnp.float32)


def narrow_pieces(place_ref, wide_ref, piece_refs, spread):
    tiles, _, lanes = wide_ref.shape
    rows_of_piece = piece_refs[0].shape[0]
    step = 64
    group = place_ref[0] & (spread - 1)
    for relative, piece_ref in enumerate(piece_refs):
        base = (group ^ relative) * rows_of_piece

        @pl.loop(0, rows_of_piece // step)
        def _(part):
            target = pl.ds(pl.multiple_of(part * step, step), step)
            source = pl.ds(pl.multiple_of(base + part * step, step), step)
            for tile in range(tiles):
                cols = slice(tile * lanes, (tile + 1) * lanes)
                piece_ref[target, cols] = wide_ref[tile, source, :].astype(jnp.bfloat16)


def general_body(
    tokens,
    keep_mask,
    cotangent,
    qkv_weight,
    proj_weight,
    up_weight,
    down_weight,
    vectors,
    qkv_rows,
    qkv_cols,
    proj_rows,
    proj_cols,
    up_rows,
    up_cols,
    down_rows,
    down_cols,
    vector_moment,
):
    masters = (qkv_weight, proj_weight, up_weight, down_weight)
    lowered = tuple((master.astype(jnp.bfloat16) for master in masters))
    dp_bits, group_bits = axis_bits("dp"), axis_bits("group")
    gather_steps = dp_bits[1:] + group_bits[1:] + dp_bits[:1] + group_bits[:1]
    scatter_steps = gather_steps[::-1]
    w_qkv, w_proj, w_up, w_down = tuple(
        blocks_to_whole(gather_blocks(part, gather_steps), gather_steps) for part in lowered
    )
    spread = lax.axis_size("group")

    def slots_in(array):
        held, slots, width = array.shape
        parts = array.transpose(1, 0, 2).reshape(slots, spread, held // spread, width)
        parts = lax.all_to_all(
            parts.transpose(1, 0, 2, 3), "group", split_axis=0, concat_axis=0, tiled=True
        )
        return parts.reshape(spread * slots * (held // spread), width)

    def slots_out(array):
        held, slots, width = tokens.shape
        parts = array.reshape(spread, slots, held // spread, width)
        parts = lax.all_to_all(parts, "group", split_axis=0, concat_axis=0, tiled=True)
        return parts.transpose(1, 0, 2, 3).reshape(slots, held, width).transpose(1, 0, 2)

    images = keep_mask.shape[0]
    bias = jnp.where(keep_mask > 0, 0.0, -1e30)[:, :, None]
    x, qkv, probs, attended, middle = attention_forward(
        slots_in(tokens), bias, w_qkv, w_proj, vectors
    )
    output, d_middle, d_attended, up_grad, down_grad, proj_grad, ff_sums, up_sums = feed_forward(
        images, middle, slots_in(cotangent), attended, w_up, w_down, w_proj, vectors
    )
    block_output = slots_out(output)
    d_input, qkv_grad, att_sums = attention_back(
        x, qkv, probs, d_attended, d_middle, w_qkv, vectors
    )
    input_grad = slots_out(d_input)
    local_vectors = jnp.concatenate(
        [att_sums[:4], ff_sums[:3], up_sums.reshape(4, -1), ff_sums[3:4]], axis=0
    )
    vector_grad = sum_everywhere(local_vectors, group_bits + dp_bits)
    local_grads = (qkv_grad, proj_grad, up_grad, down_grad)
    owned = tuple(
        scatter_sum(whole_to_blocks(part, scatter_steps), scatter_steps) for part in local_grads
    )
    squares = tuple((gradient * gradient + tiny_square for gradient in owned))
    row_parts = tuple((jnp.sum(square, axis=1) for square in squares)) + tuple(
        (jnp.sum(master * master, axis=1) for master in masters)
    )
    row_sums = sum_parts(row_parts, group_bits)
    rows_old = (qkv_rows, proj_rows, up_rows, down_rows)
    cols_old = (qkv_cols, proj_cols, up_cols, down_cols)
    total_cols = tuple((gradient.shape[1] * lax.axis_size("group") for gradient in owned))
    total_rows = tuple((gradient.shape[0] * lax.axis_size("dp") for gradient in owned))
    rows_new = tuple(
        (
            decay_rate * rows_old[which] + (1.0 - decay_rate) * row_sums[which] / total_cols[which]
            for which in range(4)
        )
    )
    col_parts = (
        tuple((jnp.sum(square, axis=0) for square in squares))
        + tuple((jnp.sum(row_stat) for row_stat in rows_new))
        + tuple((jnp.sum(row_sums[4 + which]) for which in range(4)))
    )
    col_sums = sum_parts(col_parts, dp_bits)
    results = []
    for which in range(4):
        cols_new = (
            decay_rate * cols_old[which] + (1.0 - decay_rate) * col_sums[which] / total_rows[which]
        )
        mean_rows = col_sums[4 + which] / total_rows[which]
        spread = jnp.sqrt(col_sums[8 + which] / (total_rows[which] * total_cols[which]))
        second = rows_new[which][:, None] * cols_new[None, :] / mean_rows
        updated = masters[which] - step_rate * spread * owned[which] * lax.rsqrt(second)
        results.append((owned[which], rows_new[which], cols_new, updated))
    vector_moment_new = decay_rate * vector_moment + (1.0 - decay_rate) * (
        vector_grad * vector_grad + tiny_square
    )
    row_spread = jnp.sqrt(jnp.mean(vectors * vectors, axis=1, keepdims=True))
    vector_new = vectors - step_rate * row_spread * vector_grad * lax.rsqrt(vector_moment_new)
    return (
        block_output,
        input_grad,
        results[0][0],
        results[0][1],
        results[0][2],
        results[0][3],
        results[1][0],
        results[1][1],
        results[1][2],
        results[1][3],
        results[2][0],
        results[2][1],
        results[2][2],
        results[2][3],
        results[3][0],
        results[3][1],
        results[3][2],
        results[3][3],
        vector_grad,
        vector_moment_new,
        vector_new,
    )


def attention_packed_kernel(
    images, dp_size, spread, place_ref, *refs
):
    pieces, refs = refs[:spread], refs[spread:]
    (
        bias_ref, own_ref, arrived_ref, vectors_ref,
        x_ref, qkv_ref, probs_ref, attended_ref, middle_ref, w_qkv_ref, w_proj_ref, wide_ref, normed_ref,
    ) = refs
    rows = own_ref.shape[1]
    qkv_cols, proj_cols = w_qkv_ref.shape[1] // spread, w_proj_ref.shape[1] // spread

    @pl.when(pl.program_id(0) == 0)
    def _():
        widen_pieces(place_ref, pieces, wide_ref, spread)

        def put(row, col, block):
            down = slice(row * rows, (row + 1) * rows)
            w_qkv_ref[down, col * qkv_cols : (col + 1) * qkv_cols] = block[:, :qkv_cols]
            w_proj_ref[down, col * proj_cols : (col + 1) * proj_cols] = block[:, qkv_cols:]

        unpack(place_ref, own_ref, arrived_ref, put, dp_size, spread)

    attention_steps(
        images, bias_ref, w_qkv_ref, w_proj_ref, vectors_ref,
        x_ref, qkv_ref, probs_ref, attended_ref, middle_ref, wide_ref, normed_ref,
    )


def feed_forward_packed_kernel(images, dp_size, spread, place_ref, *refs):
    pieces, refs = refs[:spread], refs[spread:]
    middle_ref, attended_ref, own_ref, arrived_ref, w_proj_ref, vectors_ref, bias_up_ref = refs[:7]
    outputs, refs = refs[7 : 7 + spread], refs[7 + spread :]
    d_middle_ref, d_attended_ref, keep_ref, leave_ref, vector_sums_ref, up_sums_ref = refs[:6]
    w_up_ref, w_down_ref, down_low_ref, wide_ref = refs[6:10]
    scratches = refs[10:]
    up_total_ref, down_total_ref, proj_total_ref = scratches[-3:]
    rows = own_ref.shape[1]
    up_cols = w_up_ref.shape[1] // spread
    out_cols = w_down_ref.shape[1] // spread
    folds = w_down_ref.shape[0] // w_up_ref.shape[0]

    @pl.when(pl.program_id(0) == 0)
    def _():
        widen_pieces(place_ref, pieces, wide_ref, spread)

        def put(row, col, block):
            w_up_ref[row * rows : (row + 1) * rows, col * up_cols : (col + 1) * up_cols] = block[:, :up_cols]
            for fold in range(folds):
                down = (row * folds + fold) * rows
                start = up_cols + fold * out_cols
                w_down_ref[down : down + rows, col * out_cols : (col + 1) * out_cols] = block[
                    :, start : start + out_cols
                ]

        unpack(place_ref, own_ref, arrived_ref, put, dp_size, spread)

    feed_forward_steps(
        images, middle_ref, attended_ref, w_up_ref, w_down_ref, w_proj_ref, vectors_ref, bias_up_ref,
        d_middle_ref, d_attended_ref, vector_sums_ref, up_sums_ref, wide_ref, *scratches,
    )

    @pl.when(pl.program_id(0) == pl.num_programs(0) - 1)
    def _():
        narrow_pieces(place_ref, wide_ref, outputs, spread)
        down_low_ref[...] = down_total_ref[...].T.astype(jnp.bfloat16)

        def take(row, col):
            across = slice(row * rows, (row + 1) * rows)
            cols = slice(col * out_cols, (col + 1) * out_cols)
            parts = [up_total_ref[across, col * up_cols : (col + 1) * up_cols].astype(jnp.bfloat16)]
            for fold in range(folds):
                down = (row * folds + fold) * rows
                parts.append(down_low_ref[down : down + rows, cols])
            parts.append(proj_total_ref[across, cols].astype(jnp.bfloat16))
            return jnp.concatenate(parts, axis=1)

        pack(place_ref, take, keep_ref, leave_ref, dp_size, spread)


def attention_back_packed_kernel(
    images, dp_size, spread, place_ref, x_ref, qkv_ref, probs_ref, d_attended_ref, d_middle_ref, w_qkv_ref,
    vectors_ref, *refs,
):
    pieces, refs = refs[:spread], refs[spread:]
    keep_ref, leave_ref, vector_sums_ref, wide_ref = refs[:4]
    scratches = refs[4:]
    total_ref = scratches[-1]
    attention_back_steps(
        images, x_ref, qkv_ref, probs_ref, d_attended_ref, d_middle_ref, w_qkv_ref, vectors_ref,
        vector_sums_ref, wide_ref, *scratches,
    )

    @pl.when(pl.program_id(0) == pl.num_programs(0) - 1)
    def _():
        narrow_pieces(place_ref, wide_ref, pieces, spread)
        rows, cols = keep_ref.shape[1:]

        def take(row, col):
            block = total_ref[row * rows : (row + 1) * rows, col * cols : (col + 1) * cols]
            return block.astype(jnp.bfloat16)

        pack(place_ref, take, keep_ref, leave_ref, dp_size, spread)


def settle_kernel(spread, place_ref, *refs):
    pieces, output_ref = refs[:spread], refs[spread]
    group = place_ref[0] & (spread - 1)
    held = pieces[0].shape[1]
    for relative, piece_ref in enumerate(pieces):
        start = pl.multiple_of((group ^ relative) * held, held)
        output_ref[:, pl.ds(start, held), :] = piece_ref[...]


def lane_table(rows, columns):
    lane = lax.broadcasted_iota(jnp.int32, (rows, 128), 1)
    table = jnp.zeros((rows, 128), jnp.float32)
    for at, column in enumerate(columns):
        table = jnp.where(lane == at, column, table)
    return table


def added(parts):
    while len(parts) > 1:
        parts = [sum(parts[at : at + 2][1:], parts[at]) for at in range(0, len(parts), 2)]
    return parts[0]


def row_sum(values):
    return jnp.sum(values, axis=1, keepdims=True)


def gradient_kernel(count, *refs):
    qkv_parts, ff_parts, refs = refs[:count], refs[count : 2 * count], refs[2 * count :]
    masters, refs = refs[:4], refs[4:]
    grads, (row_ref, col_ref) = refs[:4], refs[4:]
    qkv = added([part[...].astype(jnp.float32) for part in qkv_parts])
    rest = added([part[...].astype(jnp.float32) for part in ff_parts])
    rows, up_cols = grads[2].shape
    out_cols = grads[1].shape[1]
    folds = grads[3].shape[0] // rows
    up = rest[:, :up_cols]
    downs = [rest[:, up_cols + fold * out_cols :][:, :out_cols] for fold in range(folds)]
    proj = rest[:, up_cols + folds * out_cols :]
    grads[0][...] = qkv
    grads[1][...] = proj
    grads[2][...] = up
    for fold in range(folds):
        grads[3][fold * rows : (fold + 1) * rows, :] = downs[fold]
    squares = [part * part + tiny_square for part in (qkv, proj, up, *downs)]
    weights = [master[...] for master in masters[:3]]
    weights += [masters[3][fold * rows : (fold + 1) * rows, :] for fold in range(folds)]
    columns = [row_sum(square) for square in squares] + [row_sum(part * part) for part in weights]
    row_ref[...] = lane_table(rows, columns)
    col_ref[...] = jnp.zeros_like(col_ref)
    for at, square in enumerate((*squares[:3], added(squares[3:]))):
        col_ref[at : at + 1, : square.shape[1]] = column_sum(square)


def row_kernel(widths, rows_old_ref, col_ref, *refs):
    parts, (rows_ref, message_ref) = refs[:-2], refs[-2:]
    sums = added([part[...] for part in parts])
    lane = lax.broadcasted_iota(jnp.int32, sums.shape, 1)
    share = jnp.ones_like(sums)
    for at, size in enumerate(widths):
        share = jnp.where(lane == at, (1.0 - decay_rate) / size, share)
    rows = jnp.where(lane < len(widths), decay_rate, 0.0) * rows_old_ref[...] + share * sums
    rows_ref[...] = rows
    message_ref[...] = col_ref[...]
    message_ref[4:5, :128] = column_sum(rows)


def update_kernel(count, heights, widths, *refs):
    messages, refs = refs[:count], refs[count:]
    rows_ref, vector_parts, refs = refs[0], refs[1:5], refs[5:]
    vectors_ref, moment_ref, refs = refs[0], refs[1], refs[2:]
    grads, masters, cols_old, refs = refs[:4], refs[4:8], refs[8:12], refs[12:]
    news, cols_new, refs = refs[:4], refs[4:8], refs[8:]
    row_out_ref, vector_grad_ref, moment_new_ref, vector_new_ref = refs
    total = added([message[...] for message in messages])
    rows_new = rows_ref[...]
    height = rows_new.shape[0]
    row_out_ref[...] = rows_new.T
    folds = grads[3].shape[0] // height
    lanes = [[0], [1], [2], list(range(3, 3 + folds))]
    for which in range(4):
        entries = heights[which] * widths[which]
        cols = cols_old[which].shape[1]
        new = decay_rate * cols_old[which][...] + (1.0 - decay_rate) / heights[which] * total[
            which : which + 1, :cols
        ]
        cols_new[which][...] = new
        mean_rows = sum(total[4:5, lane : lane + 1] for lane in lanes[which]) / heights[which]
        squares = sum(total[4:5, 3 + folds + lane : 4 + folds + lane] for lane in lanes[which])
        rate = step_rate * jnp.sqrt(squares / entries)
        across = new / mean_rows
        for fold, lane in enumerate(lanes[which]):
            part = slice(fold * height, (fold + 1) * height)
            second = rows_new[:, lane : lane + 1] * across
            news[which][part, :] = masters[which][part, :] - rate * grads[which][part, :] * lax.rsqrt(second)
    gradient = added([part[...] for part in vector_parts])
    vector_grad_ref[...] = gradient
    moment = decay_rate * moment_ref[...] + (1.0 - decay_rate) * (gradient * gradient + tiny_square)
    moment_new_ref[...] = moment
    vectors = vectors_ref[...]
    spread = jnp.sqrt(jnp.mean(vectors * vectors, axis=1, keepdims=True))
    vector_new_ref[...] = vectors - step_rate * spread * gradient * lax.rsqrt(moment)


def packed_body(
    tokens, keep_mask, cotangent, qkv_weight, proj_weight, up_weight, down_weight, vectors,
    qkv_rows, qkv_cols, proj_rows, proj_cols, up_rows, up_cols, down_rows, down_cols, vector_moment,
):
    spread, dp_size = lax.axis_size("group"), lax.axis_size("dp")
    low, high = jnp.bfloat16, jnp.float32
    place = linear_place().astype(jnp.int32).reshape(1)
    group = lax.axis_index("group")
    held, slots, width = tokens.shape
    images, length = keep_mask.shape
    hidden = up_weight.shape[1] * spread
    total = images * length
    rows = qkv_weight.shape[0]
    folds = down_weight.shape[0] // rows
    core_bits = (1,)
    near_bits = tuple(1 << at for at in range(1, spread.bit_length()))
    far_bits = tuple(spread << at for at in range(1, dp_size.bit_length() - 1))
    half = spread * dp_size // 2

    def pieces_out(array):
        by_slot = array.transpose(1, 0, 2)
        parts = [
            lax.dynamic_slice_in_dim(by_slot, (group ^ relative) * images, images, axis=1)
            for relative in range(spread)
        ]
        return exchange([part.reshape(slots * images, width) for part in parts])

    def exchange(parts):
        return [parts[0]] + [permute(part, relative) for relative, part in enumerate(parts) if relative]

    def settle(parts):
        parts = [part.reshape(slots, images, width) for part in parts]
        block = slots // 4
        whole = pl.pallas_call(
            functools.partial(settle_kernel, spread),
            grid=(4,),
            in_specs=[pl.BlockSpec(memory_space=pltpu.SMEM)] + [step_block((block, images, width))] * spread,
            out_specs=step_block((block, held, width)),
            out_shape=jax.ShapeDtypeStruct((slots, held, width), low),
            compiler_params=pltpu.CompilerParams(vmem_limit_bytes=vmem_bytes),
        )(place, *parts)
        return whole.transpose(1, 0, 2)

    fold_cols = [down_weight[fold * rows : (fold + 1) * rows] for fold in range(folds)]
    first_pack = jnp.concatenate([qkv_weight, proj_weight], axis=1).astype(low)
    second_pack = jnp.concatenate([up_weight] + fold_cols, axis=1).astype(low)
    first_own, first_arrived = gather_packed(first_pack, [far_bits, near_bits, core_bits])
    token_parts = pieces_out(tokens)
    cotangent_parts = pieces_out(cotangent)
    second_own, second_arrived = gather_packed(
        second_pack, [far_bits] + [(bit,) for bit in near_bits] + [core_bits]
    )
    bias = jnp.where(keep_mask > 0, 0.0, -1e30)[:, :, None]

    step_rows = PER_STEP * length
    block = (step_rows, width)
    pairs = width // (2 * HEAD_DIM)
    steps = images // PER_STEP
    statics = (images, dp_size, spread)
    wide = scratch(width // 128, total, 128)
    probs_block = (PER_STEP, pairs, length, 2 * length)
    x, qkv, probs, attended, middle, w_qkv, w_proj = call_kernel(
        attention_packed_kernel, statics, steps,
        ["place"] + [None] * spread + [(PER_STEP, length, 1), None, None, None],
        [
            ((total, width), low, block),
            ((total, 3 * width), low, (step_rows, 3 * width)),
            ((images, *probs_block[1:]), low, probs_block),
            ((total, width), low, block),
            ((total, width), high, block),
            ((width, 3 * width), low, None),
            ((width, width), low, None),
        ],
        [wide, scratch(step_rows, width, dtype=low)],
        (place, *token_parts, bias, first_own, first_arrived, vectors),
        2 * total * width * 4 * width + 8 * total * length * width,
    )
    piece = ((slots * images, width), low, None)
    pack_cols = up_weight.shape[1] + (folds + 1) * proj_weight.shape[1]
    results = call_kernel(
        feed_forward_packed_kernel, statics, steps,
        ["place"] + [None] * spread + [block, block] + [None] * 5,
        [piece] * spread
        + [
            ((total, width), high, block),
            ((total, width), low, block),
            ((half, rows, pack_cols), low, None),
            ((half, rows, pack_cols), low, None),
            ((8, width), high, None),
            ((1, hidden), high, None),
        ],
        [
            scratch(width, hidden, dtype=low),
            scratch(hidden, width, dtype=low),
            scratch(hidden, width, dtype=low),
            wide,
            scratch(step_rows, width, dtype=low),
            scratch(width, step_rows, dtype=low),
            scratch(step_rows, width, dtype=low),
            scratch(width, step_rows, dtype=low),
            scratch(step_rows, width),
            scratch(step_rows, 128),
            scratch(step_rows, width),
            scratch(step_rows, width),
            scratch(width, hidden),
            scratch(width, hidden),
            scratch(width, width),
        ],
        (
            place, *cotangent_parts, middle, attended, second_own, second_arrived, w_proj, vectors,
            vectors[7:11].reshape(1, hidden),
        ),
        12 * total * width * hidden + 4 * total * width * width, total * hidden,
    )
    output_parts = exchange(results[:spread])
    d_middle, d_attended, ff_keep, ff_leave, ff_sums, up_sums = results[spread:]
    results = call_kernel(
        attention_back_packed_kernel, statics, steps,
        ["place", block, (step_rows, 3 * width), probs_block, block, block, None, None],
        [piece] * spread
        + [
            ((half, rows, qkv_weight.shape[1]), low, None),
            ((half, rows, qkv_weight.shape[1]), low, None),
            ((8, width), high, None),
        ],
        [
            wide,
            scratch(step_rows, width, dtype=low),
            scratch(step_rows, 3 * width, dtype=low),
            scratch(step_rows, width),
            scratch(width, 3 * width),
        ],
        (place, x, qkv, probs, d_attended, d_middle, w_qkv, vectors),
        4 * total * width * 3 * width + 16 * total * length * width,
    )
    input_parts = exchange(results[:spread])
    qkv_keep, qkv_leave, att_sums = results[spread:]
    ff_parts = scatter_packed(
        ff_keep, ff_leave, [core_bits] + [(bit,) for bit in near_bits[::-1]] + [far_bits]
    )
    qkv_parts = scatter_packed(qkv_keep, qkv_leave, [core_bits, near_bits, far_bits])
    local_vectors = jnp.concatenate(
        [att_sums[:4], ff_sums[:3], up_sums.reshape(hidden // width, width), ff_sums[3:4]], axis=0
    )
    vector_sums = sum_direct(local_vectors, [core_bits, near_bits])
    vector_parts = [vector_sums] + [permute(vector_sums, mask) for mask in direct_masks(far_bits)]

    masters = (qkv_weight, proj_weight, up_weight, down_weight)
    rows_old = [qkv_rows, proj_rows, up_rows] + list(down_rows.reshape(folds, rows))
    rows_old = jnp.pad(jnp.stack(rows_old, axis=1), ((0, 0), (0, 128 - len(rows_old))))
    heights = [master.shape[0] * dp_size for master in masters]
    widths = [master.shape[1] * spread for master in masters]
    cols = max(384, max(master.shape[1] for master in masters))
    small = functools.partial(
        pl.pallas_call, compiler_params=pltpu.CompilerParams(vmem_limit_bytes=vmem_bytes)
    )
    *grads, row_part, col_part = small(
        functools.partial(gradient_kernel, len(qkv_parts)),
        out_shape=[jax.ShapeDtypeStruct(master.shape, high) for master in masters]
        + [jax.ShapeDtypeStruct((rows, 128), high), jax.ShapeDtypeStruct((8, cols), high)],
    )(*qkv_parts, *ff_parts, *masters)
    row_parts = [row_part] + [permute(row_part, mask) for mask in range(1, spread)]
    rows_new, message = small(
        functools.partial(row_kernel, widths[:3] + widths[3:] * folds),
        out_shape=[jax.ShapeDtypeStruct((rows, 128), high), jax.ShapeDtypeStruct((8, cols), high)],
    )(rows_old, col_part, *row_parts)
    messages = [message] + [permute(message, spread * mask) for mask in range(1, dp_size)]
    cols_old = [part.reshape(1, -1) for part in (qkv_cols, proj_cols, up_cols, down_cols)]
    results = small(
        functools.partial(update_kernel, len(messages), heights, widths),
        out_shape=[jax.ShapeDtypeStruct(master.shape, high) for master in masters]
        + [jax.ShapeDtypeStruct(part.shape, high) for part in cols_old]
        + [jax.ShapeDtypeStruct((128, rows), high)]
        + [jax.ShapeDtypeStruct(vectors.shape, high)] * 3,
    )(*messages, rows_new, *vector_parts, vectors, vector_moment, *grads, *masters, *cols_old)
    news, cols_new = results[:4], [part.reshape(-1) for part in results[4:8]]
    row_table, vector_grad, vector_moment_new, vector_new = results[8:]
    rows_out = [row_table[0], row_table[1], row_table[2], row_table[3 : 3 + folds].reshape(-1)]
    factored = []
    for which in range(4):
        factored += [grads[which], rows_out[which], cols_new[which], news[which]]
    return (settle(output_parts), settle(input_parts), *factored, vector_grad, vector_moment_new, vector_new)


def body(*arrays):
    spread, dp_size = lax.axis_size("group"), lax.axis_size("dp")
    rows, images = arrays[3].shape[0], arrays[1].shape[0]
    slots = arrays[0].shape[1]
    powers = all(size & (size - 1) == 0 for size in (spread, dp_size))
    fits = powers and spread > 1 and dp_size > 2
    fits = fits and rows % 16 == 0 and images % 16 == 0 and slots % 4 == 0
    return packed_body(*arrays) if fits else general_body(*arrays)


def solution(mesh):
    in_specs = (
        P("dp", "group", None),
        P(("dp", "group"), None),
        P("dp", "group", None),
        P("dp", "group"),
        P("dp", "group"),
        P("dp", "group"),
        P("dp", "group"),
        P(),
        P("dp"),
        P("group"),
        P("dp"),
        P("group"),
        P("dp"),
        P("group"),
        P("dp"),
        P("group"),
        P(),
    )
    out_specs = (
        P("dp", "group", None),
        P("dp", "group", None),
        P("dp", "group"),
        P("dp"),
        P("group"),
        P("dp", "group"),
        P("dp", "group"),
        P("dp"),
        P("group"),
        P("dp", "group"),
        P("dp", "group"),
        P("dp"),
        P("group"),
        P("dp", "group"),
        P("dp", "group"),
        P("dp"),
        P("group"),
        P("dp", "group"),
        P(),
        P(),
        P(),
    )
    return jax.shard_map(body, mesh=mesh, in_specs=in_specs, out_specs=out_specs, check_vma=False)
```

```python
import functools
import math

import jax
import jax.numpy as jnp
from jax import lax
from jax.experimental import pallas as pl
from jax.experimental.pallas import tpu as pltpu
from jax.sharding import PartitionSpec as P

HEAD_DIM = 64
STEP_NUMBER = 10


step_rate = 0.3
norm_epsilon = 1e-06
tiny_square = 1e-30
decay_rate = 1.0 - STEP_NUMBER ** (-0.8)
LOG2_E = 1.4426950408889634


def axis_bits(name):
    count = lax.axis_size(name)
    return [(name, 1 << place) for place in range(count.bit_length() - 1)]


def swap_partner(array, step):
    name, bit = step
    count = lax.axis_size(name)
    return lax.ppermute(array, name, [(rank, rank ^ bit) for rank in range(count)])


def upper_side(step):
    name, bit = step
    return (lax.axis_index(name) & bit) != 0


def gather_blocks(array, steps):
    for step in steps:
        arrived = swap_partner(array, step)
        upper = upper_side(step)
        array = jnp.stack([jnp.where(upper, arrived, array), jnp.where(upper, array, arrived)])
    return array


def scatter_sum(array, steps):
    for step in steps:
        upper = upper_side(step)
        leaving = jnp.where(upper, array[0], array[1]).astype(jnp.bfloat16)
        arrived = swap_partner(leaving, step)
        array = jnp.where(upper, array[1], array[0]).astype(jnp.float32) + arrived.astype(jnp.float32)
    return array


def sum_everywhere(array, steps):
    for step in steps:
        array = array + swap_partner(array, step)
    return array


def sum_parts(parts, steps):
    flat = [part.reshape(-1) for part in parts]
    total = sum_everywhere(jnp.concatenate(flat), steps)
    result, start = [], 0
    for part in parts:
        result.append(total[start : start + part.size].reshape(part.shape))
        start += part.size
    return result


def block_order(steps):
    order = []
    for name in ("dp", "group"):
        bits = sorted((step for step in steps if step[0] == name), key=lambda step: -step[1])
        order.append([steps.index(step) for step in bits])
    return order


def blocks_to_whole(blocks, steps):
    count = len(steps)
    rows, cols = blocks.shape[count:]
    dp_axes, group_axes = block_order(steps)
    dp_axes = [count - 1 - axis for axis in dp_axes]
    group_axes = [count - 1 - axis for axis in group_axes]
    whole = blocks.transpose(dp_axes + [count] + group_axes + [count + 1])
    return whole.reshape(rows << len(dp_axes), cols << len(group_axes))


def whole_to_blocks(whole, steps):
    dp_axes, group_axes = block_order(steps)
    rows = whole.shape[0] >> len(dp_axes)
    cols = whole.shape[1] >> len(group_axes)
    split = whole.reshape([2] * len(dp_axes) + [rows] + [2] * len(group_axes) + [cols])
    places = dp_axes + [len(steps)] + group_axes + [len(steps) + 1]
    return split.transpose([places.index(axis) for axis in range(len(places))])


PER_STEP = 4
FF_CHUNK = 256
vmem_bytes = 60 * 1024 * 1024


def dot(left, right, left_axis=1, right_axis=0):
    return lax.dot_general(
        left, right, (((left_axis,), (right_axis,)), ((), ())), preferred_element_type=jnp.float32
    )


def normal_form(values):
    center = jnp.mean(values, axis=-1, keepdims=True)
    centered = values - center
    spread = jnp.mean(centered * centered, axis=-1, keepdims=True)
    scale = lax.rsqrt(spread + norm_epsilon)
    return centered * scale, scale


def norm_back(grad, unit, scale, gain):
    weighted = grad * gain
    along = jnp.mean(weighted * unit, axis=-1, keepdims=True)
    level = jnp.mean(weighted, axis=-1, keepdims=True)
    return scale * (weighted - level - unit * along)


def column_sum(values):
    return jnp.sum(values, axis=0, keepdims=True)


def pair_mask(length):
    return lax.broadcasted_iota(jnp.int32, (length, 2 * HEAD_DIM), 1) < HEAD_DIM


def stack_heads(pair, first):
    none = jnp.zeros_like(pair)
    return jnp.concatenate([jnp.where(first, pair, none), jnp.where(first, none, pair)], axis=0)


def join_heads(rows, first):
    length = rows.shape[0] // 2
    return jnp.where(first, rows[:length], rows[length:])


def gelu_and_slope(pre):
    bell = jnp.exp2(pre * pre * (-0.5 * LOG2_E))
    inverse = 1.0 / (1.0 + (0.3275911 * 0.5**0.5) * jnp.abs(pre))
    poly = inverse * (
        0.5 * 0.254829592
        + inverse
        * (
            0.5 * -0.284496736
            + inverse
            * (0.5 * 1.421413741 + inverse * (0.5 * -1.453152027 + inverse * (0.5 * 1.061405429)))
        )
    )
    tail = poly * bell
    below = jnp.where(pre >= 0, 1.0 - tail, tail)
    return pre * below, below + pre * bell * 0.3989422804014327


def widen(source_ref, wide_ref, images):
    tiles, total, lanes = wide_ref.shape
    rows_at_once = 8 * images

    @pl.loop(0, total // rows_at_once)
    def _(part):
        rows = pl.ds(pl.multiple_of(part * rows_at_once, rows_at_once), rows_at_once)
        for tile in range(tiles):
            cols = slice(tile * lanes, (tile + 1) * lanes)
            wide_ref[tile, rows, :] = source_ref[rows, cols].astype(jnp.float32)


def narrow(wide_ref, target_ref, images):
    tiles, total, lanes = wide_ref.shape
    rows_at_once = 8 * images

    @pl.loop(0, total // rows_at_once)
    def _(part):
        rows = pl.ds(pl.multiple_of(part * rows_at_once, rows_at_once), rows_at_once)
        for tile in range(tiles):
            cols = slice(tile * lanes, (tile + 1) * lanes)
            target_ref[rows, cols] = wide_ref[tile, rows, :].astype(target_ref.dtype)


def take_image(wide_ref, image, images):
    tiles, total, _ = wide_ref.shape
    rows = pl.ds(image, total // images, images)
    return jnp.concatenate([wide_ref[tile, rows, :] for tile in range(tiles)], axis=1)


def put_image(wide_ref, image, images, values):
    tiles, total, lanes = wide_ref.shape
    rows = pl.ds(image, total // images, images)
    for tile in range(tiles):
        wide_ref[tile, rows, :] = values[:, tile * lanes : (tile + 1) * lanes]


def attention_kernel(images, tokens_ref, *refs):
    wide_ref = refs[-2]

    @pl.when(pl.program_id(0) == 0)
    def _():
        widen(tokens_ref, wide_ref, images)

    attention_steps(images, *refs)


def attention_steps(
    images, bias_ref, w_qkv_ref, w_proj_ref, vectors_ref,
    x_ref, qkv_ref, probs_ref, attended_ref, middle_ref, wide_ref, normed_ref,
):
    step = pl.program_id(0)
    length = bias_ref.shape[1]
    width = x_ref.shape[1]
    per_step = bias_ref.shape[0]

    for image in range(per_step):
        rows = slice(image * length, (image + 1) * length)
        x = take_image(wide_ref, step * per_step + image, images)
        x_ref[rows, :] = x.astype(jnp.bfloat16)
        unit, _ = normal_form(x)
        normed_ref[rows, :] = (unit * vectors_ref[0:1] + vectors_ref[1:2]).astype(jnp.bfloat16)
    for part in range(3):
        cols = slice(part * width, (part + 1) * width)
        projected = dot(normed_ref[...], w_qkv_ref[:, cols])
        if part != 1:
            row = 2 if part == 0 else 3
            projected = projected + vectors_ref[row : row + 1]
        qkv_ref[:, cols] = projected.astype(jnp.bfloat16)

    @pl.loop(0, per_step)
    def _(image):
        rows = pl.ds(pl.multiple_of(image * length, length), length)
        first = pair_mask(length)
        place = lax.broadcasted_iota(jnp.int32, (length, 2 * length), 0)
        asker = lax.broadcasted_iota(jnp.int32, (length, 2 * length), 1)
        asker = jnp.where(asker >= length, asker - length, asker)
        bias = jnp.where(place == asker, 0.0, bias_ref[image])
        for pair in range(width // (2 * HEAD_DIM)):
            low = pair * 2 * HEAD_DIM
            queries = stack_heads(qkv_ref[rows, low : low + 2 * HEAD_DIM], first)
            keys = qkv_ref[rows, width + low : width + low + 2 * HEAD_DIM]
            values = qkv_ref[rows, 2 * width + low : 2 * width + low + 2 * HEAD_DIM]
            scores = dot(keys, queries, 1, 1) * (HEAD_DIM**-0.5 * LOG2_E) + bias
            weights = jnp.exp2(scores - jnp.max(scores, axis=0, keepdims=True))
            probs = weights * (1.0 / jnp.sum(weights, axis=0, keepdims=True))
            probs = probs.astype(jnp.bfloat16)
            probs_ref[image, pair] = probs
            attended = join_heads(dot(probs, values, 0, 0), first)
            attended_ref[rows, low : low + 2 * HEAD_DIM] = attended.astype(jnp.bfloat16)

    middle_ref[...] = (
        x_ref[...].astype(jnp.float32)
        + dot(attended_ref[...], w_proj_ref[...])
        + vectors_ref[4:5]
    )


def feed_forward_kernel(
    images, middle_ref, cotangent_ref, attended_ref, w_up_ref, w_down_ref, w_proj_ref, vectors_ref, bias_up_ref,
    output_ref, d_middle_ref, d_attended_ref, up_grad_ref, down_grad_ref, proj_grad_ref, vector_sums_ref, up_sums_ref,
    wide_ref, *scratches,
):
    up_total_ref, down_total_ref, proj_total_ref = scratches[-3:]

    @pl.when(pl.program_id(0) == 0)
    def _():
        widen(cotangent_ref, wide_ref, images)

    feed_forward_steps(
        images, middle_ref, attended_ref, w_up_ref, w_down_ref, w_proj_ref, vectors_ref, bias_up_ref,
        d_middle_ref, d_attended_ref, vector_sums_ref, up_sums_ref, wide_ref, *scratches,
    )

    @pl.when(pl.program_id(0) == pl.num_programs(0) - 1)
    def _():
        narrow(wide_ref, output_ref, images)
        up_grad_ref[...] = up_total_ref[...].astype(jnp.bfloat16)
        down_grad_ref[...] = down_total_ref[...].T.astype(jnp.bfloat16)
        proj_grad_ref[...] = proj_total_ref[...].astype(jnp.bfloat16)


def feed_forward_steps(
    images, middle_ref, attended_ref, w_up_ref, w_down_ref, w_proj_ref, vectors_ref, bias_up_ref,
    d_middle_ref, d_attended_ref, vector_sums_ref, up_sums_ref,
    wide_ref, normed_ref, normed_t_ref, dy_ref, dy_t_ref, unit_ref, scale_ref, ahead_ref, back_ref,
    up_total_ref, down_total_ref, proj_total_ref,
):
    step = pl.program_id(0)
    length = wide_ref.shape[1] // images
    hidden = w_up_ref.shape[1]
    per_step = middle_ref.shape[0] // length

    @pl.when(step == 0)
    def _():
        for total in (up_total_ref, down_total_ref, proj_total_ref, vector_sums_ref, up_sums_ref):
            total[...] = jnp.zeros_like(total)

    for image in range(per_step):
        rows = slice(image * length, (image + 1) * length)
        dy = take_image(wide_ref, step * per_step + image, images)
        dy_ref[rows, :] = dy.astype(jnp.bfloat16)
        vector_sums_ref[3:4] += column_sum(dy)
        unit, scale = normal_form(middle_ref[rows, :])
        unit_ref[rows, :] = unit
        scale_ref[rows, :] = jnp.broadcast_to(scale, (length, scale_ref.shape[1]))
        normed_ref[rows, :] = (unit * vectors_ref[5:6] + vectors_ref[6:7]).astype(jnp.bfloat16)
    normed_t_ref[...] = normed_ref[...].T
    dy_t_ref[...] = dy_ref[...].T
    ahead_ref[...] = jnp.zeros_like(ahead_ref)
    back_ref[...] = jnp.zeros_like(back_ref)

    @pl.loop(0, hidden // FF_CHUNK)
    def _(chunk):
        cols = pl.ds(pl.multiple_of(chunk * FF_CHUNK, FF_CHUNK), FF_CHUNK)
        w_up = w_up_ref[:, cols]
        w_down = w_down_ref[cols, :]
        active, slope = gelu_and_slope(dot(normed_ref[...], w_up) + bias_up_ref[:, cols])
        active = active.astype(jnp.bfloat16)
        d_hidden = dot(dy_ref[...], w_down, 1, 1) * slope
        d_hidden = d_hidden.astype(jnp.bfloat16)
        ahead_ref[...] += dot(active, w_down)
        back_ref[...] += dot(d_hidden, w_up, 1, 1)
        down_total_ref[:, cols] += dot(dy_t_ref[...], active)
        up_total_ref[:, cols] += dot(normed_t_ref[...], d_hidden)
        up_sums_ref[:, cols] += column_sum(d_hidden.astype(jnp.float32))

    for image in range(per_step):
        rows = slice(image * length, (image + 1) * length)
        output = middle_ref[rows, :] + ahead_ref[rows, :] + vectors_ref[11:12]
        put_image(wide_ref, step * per_step + image, images, output)
        unit = unit_ref[rows, :]
        grad = back_ref[rows, :]
        vector_sums_ref[1:2] += column_sum(grad * unit)
        vector_sums_ref[2:3] += column_sum(grad)
        d_middle = dy_ref[rows, :].astype(jnp.float32) + norm_back(
            grad, unit, scale_ref[rows, 0:1], vectors_ref[5:6]
        )
        d_middle_ref[rows, :] = d_middle
        d_branch = d_middle.astype(jnp.bfloat16)
        dy_ref[rows, :] = d_branch
        vector_sums_ref[0:1] += column_sum(d_branch.astype(jnp.float32))
    proj_total_ref[...] += dot(attended_ref[...], dy_ref[...], 0, 0)
    d_attended_ref[...] = dot(dy_ref[...], w_proj_ref[...], 1, 1).astype(jnp.bfloat16)


def attention_back_kernel(
    images, x_ref, qkv_ref, probs_ref, d_attended_ref, d_middle_ref, w_qkv_ref, vectors_ref,
    input_grad_ref, qkv_grad_ref, vector_sums_ref, wide_ref, *scratches,
):
    attention_back_steps(
        images, x_ref, qkv_ref, probs_ref, d_attended_ref, d_middle_ref, w_qkv_ref, vectors_ref,
        vector_sums_ref, wide_ref, *scratches,
    )

    @pl.when(pl.program_id(0) == pl.num_programs(0) - 1)
    def _():
        narrow(wide_ref, input_grad_ref, images)
        qkv_grad_ref[...] = scratches[-1][...].astype(jnp.bfloat16)


def attention_back_steps(
    images, x_ref, qkv_ref, probs_ref, d_attended_ref, d_middle_ref, w_qkv_ref, vectors_ref,
    vector_sums_ref, wide_ref, normed_ref, d_projected_ref, back_ref, qkv_total_ref,
):
    step = pl.program_id(0)
    width = x_ref.shape[1]
    length = probs_ref.shape[2]
    per_step = probs_ref.shape[0]

    @pl.when(step == 0)
    def _():
        qkv_total_ref[...] = jnp.zeros_like(qkv_total_ref)
        vector_sums_ref[...] = jnp.zeros_like(vector_sums_ref)

    @pl.loop(0, per_step)
    def _(image):
        rows = pl.ds(pl.multiple_of(image * length, length), length)
        first = pair_mask(length)
        for pair in range(width // (2 * HEAD_DIM)):
            low = pair * 2 * HEAD_DIM
            cols = [slice(part * width + low, part * width + low + 2 * HEAD_DIM) for part in range(3)]
            queries = stack_heads(qkv_ref[rows, cols[0]], first)
            keys = qkv_ref[rows, cols[1]]
            values = qkv_ref[rows, cols[2]]
            probs = probs_ref[image, pair]
            d_attended = stack_heads(d_attended_ref[rows, cols[0]], first)
            d_projected_ref[rows, cols[2]] = dot(probs, d_attended).astype(jnp.bfloat16)
            d_probs = dot(values, d_attended, 1, 1)
            probs = probs.astype(jnp.float32)
            along = jnp.sum(d_probs * probs, axis=0, keepdims=True)
            d_scores = (probs * (d_probs - along)).astype(jnp.bfloat16)
            scale = HEAD_DIM**-0.5
            d_queries = join_heads(dot(d_scores, keys, 0, 0), first) * scale
            d_projected_ref[rows, cols[0]] = d_queries.astype(jnp.bfloat16)
            d_projected_ref[rows, cols[1]] = (dot(d_scores, queries) * scale).astype(jnp.bfloat16)

    vector_sums_ref[2:3] += column_sum(d_projected_ref[:, :width].astype(jnp.float32))
    vector_sums_ref[3:4] += column_sum(d_projected_ref[:, 2 * width :].astype(jnp.float32))
    back_ref[...] = dot(d_projected_ref[...], w_qkv_ref[...], 1, 1)
    for image in range(per_step):
        rows = slice(image * length, (image + 1) * length)
        unit, scale = normal_form(x_ref[rows, :].astype(jnp.float32))
        normed_ref[rows, :] = (unit * vectors_ref[0:1] + vectors_ref[1:2]).astype(jnp.bfloat16)
        grad = back_ref[rows, :]
        vector_sums_ref[0:1] += column_sum(grad * unit)
        vector_sums_ref[1:2] += column_sum(grad)
        d_input = d_middle_ref[rows, :] + norm_back(grad, unit, scale, vectors_ref[0:1])
        put_image(wide_ref, step * per_step + image, images, d_input)
    qkv_total_ref[...] += dot(normed_ref[...], d_projected_ref[...], 0, 0)


def whole_block(shape):
    return pl.BlockSpec(shape, lambda step: (0,) * len(shape))


def step_block(shape):
    return pl.BlockSpec(shape, lambda step: (step,) + (0,) * (len(shape) - 1))


def scratch(*shape, dtype=jnp.float32):
    return pltpu.VMEM(shape, dtype)


def call_kernel(kernel, statics, steps, ins, outs, scratches, operands, flops, transcendentals=0):
    in_specs = [
        pl.BlockSpec(memory_space=pltpu.SMEM)
        if block == "place"
        else pl.BlockSpec(memory_space=pl.ANY)
        if block == "await"
        else whole_block(op.shape) if block is None else step_block(block)
        for op, block in zip(operands, ins)
    ]
    out_specs = [
        whole_block(shape) if block is None else step_block(block) for shape, dtype, block in outs
    ]
    moved = sum(op.size * op.dtype.itemsize for op in operands) + sum(
        math.prod(shape) * jnp.dtype(dtype).itemsize for shape, dtype, block in outs
    )
    return pl.pallas_call(
        functools.partial(kernel, *statics),
        grid=(steps,),
        in_specs=in_specs,
        out_specs=out_specs,
        out_shape=[jax.ShapeDtypeStruct(shape, dtype) for shape, dtype, block in outs],
        scratch_shapes=scratches,
        compiler_params=pltpu.CompilerParams(vmem_limit_bytes=vmem_bytes),
        cost_estimate=pl.CostEstimate(
            flops=flops, bytes_accessed=moved, transcendentals=transcendentals
        ),
    )(*operands)


def attention_forward(tokens, bias, w_qkv, w_proj, vectors):
    images, length, _ = bias.shape
    total, width = tokens.shape
    pairs = width // (2 * HEAD_DIM)
    rows = PER_STEP * length
    low, high = jnp.bfloat16, jnp.float32
    outs = [
        ((total, width), low, (rows, width)),
        ((total, 3 * width), low, (rows, 3 * width)),
        ((images, pairs, length, 2 * length), low, (PER_STEP, pairs, length, 2 * length)),
        ((total, width), low, (rows, width)),
        ((total, width), high, (rows, width)),
    ]
    return call_kernel(
        attention_kernel, (images,), images // PER_STEP,
        [None, (PER_STEP, length, 1), None, None, None], outs,
        [scratch(width // 128, total, 128), scratch(rows, width, dtype=low)],
        (tokens, bias, w_qkv, w_proj, vectors),
        2 * total * width * 4 * width + 8 * total * length * width,
    )


def feed_forward(images, middle, cotangent, attended, w_up, w_down, w_proj, vectors):
    total, width = middle.shape
    hidden = w_up.shape[1]
    rows = total // images * PER_STEP
    low, high = jnp.bfloat16, jnp.float32
    block = (rows, width)
    outs = [
        ((total, width), low, None),
        ((total, width), high, block),
        ((total, width), low, block),
        ((width, hidden), low, None),
        ((hidden, width), low, None),
        ((width, width), low, None),
        ((8, width), high, None),
        ((1, hidden), high, None),
    ]
    scratches = [
        scratch(width // 128, total, 128),
        scratch(rows, width, dtype=low),
        scratch(width, rows, dtype=low),
        scratch(rows, width, dtype=low),
        scratch(width, rows, dtype=low),
        scratch(rows, width),
        scratch(rows, 128),
        scratch(rows, width),
        scratch(rows, width),
        scratch(width, hidden),
        scratch(width, hidden),
        scratch(width, width),
    ]
    return call_kernel(
        feed_forward_kernel, (images,), images // PER_STEP,
        [block, None, block, None, None, None, None, None], outs, scratches,
        (middle, cotangent, attended, w_up, w_down, w_proj, vectors, vectors[7:11].reshape(1, hidden)),
        12 * total * width * hidden + 4 * total * width * width, total * hidden,
    )


def attention_back(x, qkv, probs, d_attended, d_middle, w_qkv, vectors):
    images, pairs, length, _ = probs.shape
    total, width = x.shape
    rows = PER_STEP * length
    low, high = jnp.bfloat16, jnp.float32
    block = (rows, width)
    outs = [
        ((total, width), low, None),
        ((width, 3 * width), low, None),
        ((8, width), high, None),
    ]
    scratches = [
        scratch(width // 128, total, 128),
        scratch(rows, width, dtype=low),
        scratch(rows, 3 * width, dtype=low),
        scratch(rows, width),
        scratch(width, 3 * width),
    ]
    return call_kernel(
        attention_back_kernel, (images,), images // PER_STEP,
        [block, (rows, 3 * width), (PER_STEP, pairs, length, 2 * length), block, block, None, None],
        outs, scratches, (x, qkv, probs, d_attended, d_middle, w_qkv, vectors),
        4 * total * width * 3 * width + 16 * total * length * width,
    )

def linear_place():
    return lax.axis_index("dp") * lax.axis_size("group") + lax.axis_index("group")


def permute(array, mask):
    count = lax.axis_size("dp") * lax.axis_size("group")
    return lax.ppermute(array, ("dp", "group"), [(rank, rank ^ mask) for rank in range(count)])


def direct_masks(bits):
    masks = [0]
    for bit in bits:
        masks = masks + [mask | bit for mask in masks]
    return masks[1:]


def scatter_step(held, bits):
    masks = direct_masks(bits)
    size = held.shape[0] // (len(masks) + 1)
    parts = [
        permute(held[size * (at + 1) : size * (at + 2)].astype(jnp.bfloat16), mask)
        for at, mask in enumerate(masks)
    ]
    return held[:size], parts


def add_wide(first, *rest):
    total = first.astype(jnp.float32)
    for part in rest:
        total = total + part.astype(jnp.float32)
    return total


def packed_place(mask, spread, count):
    return ((mask >> 1) & (spread - 1)) * (count // (2 * spread)) + (mask >> (spread.bit_length()))


def unpack(blocks_ref, put, dp_size, spread):
    for row in range(dp_size):
        for col in range(spread):
            put(row, col, blocks_ref[row * spread + col])


def pack(place_ref, take, keep_ref, leave_ref, dp_size, spread):
    place = place_ref[0]
    odd = (place & 1) == 1
    for row in range(dp_size):
        for col in range(0, spread, 2):
            at = packed_place((row * spread + col) ^ place, spread, dp_size * spread)
            even_block, odd_block = take(row, col), take(row, col + 1)
            keep_ref[at] = jnp.where(odd, odd_block, even_block)
            leave_ref[at] = jnp.where(odd, even_block, odd_block)


def widen_pieces(place_ref, piece_refs, wide_ref, spread):
    tiles, _, lanes = wide_ref.shape
    rows_of_piece = piece_refs[0].shape[0]
    step = 64
    group = place_ref[0] & (spread - 1)
    for relative, piece_ref in enumerate(piece_refs):
        base = (group ^ relative) * rows_of_piece

        @pl.loop(0, rows_of_piece // step)
        def _(part):
            source = pl.ds(pl.multiple_of(part * step, step), step)
            target = pl.ds(pl.multiple_of(base + part * step, step), step)
            for tile in range(tiles):
                cols = slice(tile * lanes, (tile + 1) * lanes)
                wide_ref[tile, target, :] = piece_ref[source, cols].astype(jnp.float32)


def narrow_pieces(place_ref, wide_ref, piece_refs, spread):
    tiles, _, lanes = wide_ref.shape
    rows_of_piece = piece_refs[0].shape[0]
    step = 64
    group = place_ref[0] & (spread - 1)
    for relative, piece_ref in enumerate(piece_refs):
        base = (group ^ relative) * rows_of_piece

        @pl.loop(0, rows_of_piece // step)
        def _(part):
            target = pl.ds(pl.multiple_of(part * step, step), step)
            source = pl.ds(pl.multiple_of(base + part * step, step), step)
            for tile in range(tiles):
                cols = slice(tile * lanes, (tile + 1) * lanes)
                piece_ref[target, cols] = wide_ref[tile, source, :].astype(jnp.bfloat16)


def general_body(
    tokens,
    keep_mask,
    cotangent,
    qkv_weight,
    proj_weight,
    up_weight,
    down_weight,
    vectors,
    qkv_rows,
    qkv_cols,
    proj_rows,
    proj_cols,
    up_rows,
    up_cols,
    down_rows,
    down_cols,
    vector_moment,
):
    masters = (qkv_weight, proj_weight, up_weight, down_weight)
    lowered = tuple((master.astype(jnp.bfloat16) for master in masters))
    dp_bits, group_bits = axis_bits("dp"), axis_bits("group")
    gather_steps = dp_bits[1:] + group_bits[1:] + dp_bits[:1] + group_bits[:1]
    scatter_steps = gather_steps[::-1]
    w_qkv, w_proj, w_up, w_down = tuple(
        blocks_to_whole(gather_blocks(part, gather_steps), gather_steps) for part in lowered
    )
    spread = lax.axis_size("group")

    def slots_in(array):
        held, slots, width = array.shape
        parts = array.transpose(1, 0, 2).reshape(slots, spread, held // spread, width)
        parts = lax.all_to_all(
            parts.transpose(1, 0, 2, 3), "group", split_axis=0, concat_axis=0, tiled=True
        )
        return parts.reshape(spread * slots * (held // spread), width)

    def slots_out(array):
        held, slots, width = tokens.shape
        parts = array.reshape(spread, slots, held // spread, width)
        parts = lax.all_to_all(parts, "group", split_axis=0, concat_axis=0, tiled=True)
        return parts.transpose(1, 0, 2, 3).reshape(slots, held, width).transpose(1, 0, 2)

    images = keep_mask.shape[0]
    bias = jnp.where(keep_mask > 0, 0.0, -1e30)[:, :, None]
    x, qkv, probs, attended, middle = attention_forward(
        slots_in(tokens), bias, w_qkv, w_proj, vectors
    )
    output, d_middle, d_attended, up_grad, down_grad, proj_grad, ff_sums, up_sums = feed_forward(
        images, middle, slots_in(cotangent), attended, w_up, w_down, w_proj, vectors
    )
    block_output = slots_out(output)
    d_input, qkv_grad, att_sums = attention_back(
        x, qkv, probs, d_attended, d_middle, w_qkv, vectors
    )
    input_grad = slots_out(d_input)
    local_vectors = jnp.concatenate(
        [att_sums[:4], ff_sums[:3], up_sums.reshape(4, -1), ff_sums[3:4]], axis=0
    )
    vector_grad = sum_everywhere(local_vectors, group_bits + dp_bits)
    local_grads = (qkv_grad, proj_grad, up_grad, down_grad)
    owned = tuple(
        scatter_sum(whole_to_blocks(part, scatter_steps), scatter_steps) for part in local_grads
    )
    squares = tuple((gradient * gradient + tiny_square for gradient in owned))
    row_parts = tuple((jnp.sum(square, axis=1) for square in squares)) + tuple(
        (jnp.sum(master * master, axis=1) for master in masters)
    )
    row_sums = sum_parts(row_parts, group_bits)
    rows_old = (qkv_rows, proj_rows, up_rows, down_rows)
    cols_old = (qkv_cols, proj_cols, up_cols, down_cols)
    total_cols = tuple((gradient.shape[1] * lax.axis_size("group") for gradient in owned))
    total_rows = tuple((gradient.shape[0] * lax.axis_size("dp") for gradient in owned))
    rows_new = tuple(
        (
            decay_rate * rows_old[which] + (1.0 - decay_rate) * row_sums[which] / total_cols[which]
            for which in range(4)
        )
    )
    col_parts = (
        tuple((jnp.sum(square, axis=0) for square in squares))
        + tuple((jnp.sum(row_stat) for row_stat in rows_new))
        + tuple((jnp.sum(row_sums[4 + which]) for which in range(4)))
    )
    col_sums = sum_parts(col_parts, dp_bits)
    results = []
    for which in range(4):
        cols_new = (
            decay_rate * cols_old[which] + (1.0 - decay_rate) * col_sums[which] / total_rows[which]
        )
        mean_rows = col_sums[4 + which] / total_rows[which]
        spread = jnp.sqrt(col_sums[8 + which] / (total_rows[which] * total_cols[which]))
        second = rows_new[which][:, None] * cols_new[None, :] / mean_rows
        updated = masters[which] - step_rate * spread * owned[which] * lax.rsqrt(second)
        results.append((owned[which], rows_new[which], cols_new, updated))
    vector_moment_new = decay_rate * vector_moment + (1.0 - decay_rate) * (
        vector_grad * vector_grad + tiny_square
    )
    row_spread = jnp.sqrt(jnp.mean(vectors * vectors, axis=1, keepdims=True))
    vector_new = vectors - step_rate * row_spread * vector_grad * lax.rsqrt(vector_moment_new)
    return (
        block_output,
        input_grad,
        results[0][0],
        results[0][1],
        results[0][2],
        results[0][3],
        results[1][0],
        results[1][1],
        results[1][2],
        results[1][3],
        results[2][0],
        results[2][1],
        results[2][2],
        results[2][3],
        results[3][0],
        results[3][1],
        results[3][2],
        results[3][3],
        vector_grad,
        vector_moment_new,
        vector_new,
    )


def attention_packed_kernel(
    images, dp_size, spread, place_ref, *refs
):
    pieces, refs = refs[:spread], refs[spread:]
    (
        bias_ref, blocks_ref, vectors_ref,
        x_ref, qkv_ref, probs_ref, attended_ref, middle_ref, w_qkv_ref, w_proj_ref, wide_ref, normed_ref,
    ) = refs
    rows = blocks_ref.shape[1]
    qkv_cols, proj_cols = w_qkv_ref.shape[1] // spread, w_proj_ref.shape[1] // spread

    @pl.when(pl.program_id(0) == 0)
    def _():
        widen_pieces(place_ref, pieces, wide_ref, spread)

        def put(row, col, block):
            down = slice(row * rows, (row + 1) * rows)
            w_qkv_ref[down, col * qkv_cols : (col + 1) * qkv_cols] = block[:, :qkv_cols]
            w_proj_ref[down, col * proj_cols : (col + 1) * proj_cols] = block[:, qkv_cols:]

        unpack(blocks_ref, put, dp_size, spread)

    attention_steps(
        images, bias_ref, w_qkv_ref, w_proj_ref, vectors_ref,
        x_ref, qkv_ref, probs_ref, attended_ref, middle_ref, wide_ref, normed_ref,
    )


def feed_forward_packed_kernel(images, dp_size, spread, place_ref, *refs):
    pieces, refs = refs[:spread], refs[spread:]
    middle_ref, attended_ref, blocks_ref, w_proj_ref, vectors_ref, bias_up_ref = refs[:6]
    outputs, refs = refs[6 : 6 + spread], refs[6 + spread :]
    d_middle_ref, d_attended_ref, keep_ref, leave_ref, vector_sums_ref, up_sums_ref = refs[:6]
    w_up_ref, w_down_ref, down_low_ref, wide_ref = refs[6:10]
    scratches = refs[10:]
    up_total_ref, down_total_ref, proj_total_ref = scratches[-3:]
    rows = blocks_ref.shape[1]
    up_cols = w_up_ref.shape[1] // spread
    out_cols = w_down_ref.shape[1] // spread
    folds = w_down_ref.shape[0] // w_up_ref.shape[0]

    @pl.when(pl.program_id(0) == 0)
    def _():
        widen_pieces(place_ref, pieces, wide_ref, spread)

        def put(row, col, block):
            w_up_ref[row * rows : (row + 1) * rows, col * up_cols : (col + 1) * up_cols] = block[:, :up_cols]
            for fold in range(folds):
                down = (row * folds + fold) * rows
                start = up_cols + fold * out_cols
                w_down_ref[down : down + rows, col * out_cols : (col + 1) * out_cols] = block[
                    :, start : start + out_cols
                ]

        unpack(blocks_ref, put, dp_size, spread)

    feed_forward_steps(
        images, middle_ref, attended_ref, w_up_ref, w_down_ref, w_proj_ref, vectors_ref, bias_up_ref,
        d_middle_ref, d_attended_ref, vector_sums_ref, up_sums_ref, wide_ref, *scratches,
    )

    @pl.when(pl.program_id(0) == pl.num_programs(0) - 1)
    def _():
        narrow_pieces(place_ref, wide_ref, outputs, spread)
        down_low_ref[...] = down_total_ref[...].T.astype(jnp.bfloat16)

        def take(row, col):
            across = slice(row * rows, (row + 1) * rows)
            cols = slice(col * out_cols, (col + 1) * out_cols)
            parts = [up_total_ref[across, col * up_cols : (col + 1) * up_cols].astype(jnp.bfloat16)]
            for fold in range(folds):
                down = (row * folds + fold) * rows
                parts.append(down_low_ref[down : down + rows, cols])
            parts.append(proj_total_ref[across, cols].astype(jnp.bfloat16))
            return jnp.concatenate(parts, axis=1)

        pack(place_ref, take, keep_ref, leave_ref, dp_size, spread)


def attention_back_packed_kernel(
    images, dp_size, spread, place_ref, x_ref, qkv_ref, probs_ref, d_attended_ref, d_middle_ref, w_qkv_ref,
    vectors_ref, _, *refs,
):
    pieces, refs = refs[:spread], refs[spread:]
    keep_ref, leave_ref, vector_sums_ref, wide_ref = refs[:4]
    scratches = refs[4:]
    total_ref = scratches[-1]
    attention_back_steps(
        images, x_ref, qkv_ref, probs_ref, d_attended_ref, d_middle_ref, w_qkv_ref, vectors_ref,
        vector_sums_ref, wide_ref, *scratches,
    )

    @pl.when(pl.program_id(0) == pl.num_programs(0) - 1)
    def _():
        narrow_pieces(place_ref, wide_ref, pieces, spread)
        rows, cols = keep_ref.shape[1:]

        def take(row, col):
            block = total_ref[row * rows : (row + 1) * rows, col * cols : (col + 1) * cols]
            return block.astype(jnp.bfloat16)

        pack(place_ref, take, keep_ref, leave_ref, dp_size, spread)


def settle_kernel(spread, place_ref, *refs):
    pieces, output_ref = refs[:spread], refs[spread]
    group = place_ref[0] & (spread - 1)
    held = pieces[0].shape[1]
    for relative, piece_ref in enumerate(pieces):
        start = pl.multiple_of((group ^ relative) * held, held)
        output_ref[:, pl.ds(start, held), :] = piece_ref[...]


def lane_table(rows, columns):
    lane = lax.broadcasted_iota(jnp.int32, (rows, 128), 1)
    table = jnp.zeros((rows, 128), jnp.float32)
    for at, column in enumerate(columns):
        table = jnp.where(lane == at, column, table)
    return table


def added(parts):
    while len(parts) > 1:
        parts = [sum(parts[at : at + 2][1:], parts[at]) for at in range(0, len(parts), 2)]
    return parts[0]


def row_sum(values):
    return jnp.sum(values, axis=1, keepdims=True)


def add_kernel(count, keep_ref, arrived_ref, *refs):
    parts = refs[-count:]
    size = parts[0].shape[0]
    for at, part_ref in enumerate(parts):
        rows = slice(at * size, (at + 1) * size)
        total = keep_ref[rows].astype(jnp.float32) + arrived_ref[rows].astype(jnp.float32)
        part_ref[...] = total.astype(part_ref.dtype)


def gradient_kernel(count, *refs):
    block_parts, sums, refs = refs[:count], refs[count : count + 3], refs[count + 3 :]
    masters, refs = refs[:4], refs[4:]
    grads, (message_ref, col_ref) = refs[:4], refs[4:]
    blocks = added([part[0].astype(jnp.float32) for part in block_parts])
    rows, up_cols = grads[2].shape
    qkv_cols, out_cols = grads[0].shape[1], grads[1].shape[1]
    folds = grads[3].shape[0] // rows
    up = blocks[:, :up_cols]
    downs = [blocks[:, up_cols + fold * out_cols :][:, :out_cols] for fold in range(folds)]
    start = up_cols + folds * out_cols
    proj = blocks[:, start : start + out_cols]
    qkv = blocks[:, start + out_cols :]
    grads[0][...] = qkv
    grads[1][...] = proj
    grads[2][...] = up
    for fold in range(folds):
        grads[3][fold * rows : (fold + 1) * rows, :] = downs[fold]
    squares = [part * part + tiny_square for part in (qkv, proj, up, *downs)]
    weights = [master[...] for master in masters[:3]]
    weights += [masters[3][fold * rows : (fold + 1) * rows, :] for fold in range(folds)]
    columns = [row_sum(square) for square in squares] + [row_sum(part * part) for part in weights]
    width = message_ref.shape[1]
    message_ref[...] = jnp.zeros_like(message_ref)
    message_ref[:rows, :128] = lane_table(rows, columns)
    put_vectors(message_ref, rows, sums, width)
    col_ref[...] = jnp.zeros_like(col_ref)
    for at, square in enumerate((*squares[:3], added(squares[3:]))):
        col_ref[at : at + 1, : square.shape[1]] = column_sum(square)


def put_vectors(message_ref, base, sums, width):
    att_ref, ff_ref, up_ref = sums
    message_ref[base : base + 4, :] = att_ref[:4]
    message_ref[base + 4 : base + 7, :] = ff_ref[:3]
    count = up_ref.shape[1] // width
    for at in range(count):
        message_ref[base + 7 + at : base + 8 + at, :] = up_ref[:, at * width : (at + 1) * width]
    message_ref[base + 7 + count : base + 8 + count, :] = ff_ref[3:4]


def row_kernel(widths, qkv_old_ref, proj_old_ref, up_old_ref, down_old_ref, col_ref, *refs):
    parts, (rows_ref, message_ref) = refs[:-2], refs[-2:]
    sums = added([part[...] for part in parts])
    height = rows_ref.shape[0]
    table = sums[:height, :128]
    folds = down_old_ref.shape[0]
    old = jnp.concatenate(
        [
            qkv_old_ref[...],
            proj_old_ref[...],
            up_old_ref[...],
            down_old_ref[...],
            jnp.zeros((128 - 3 - folds, height), jnp.float32),
        ],
        axis=0,
    ).T
    lane = lax.broadcasted_iota(jnp.int32, table.shape, 1)
    share = jnp.ones_like(table)
    for at, size in enumerate(widths):
        share = jnp.where(lane == at, (1.0 - decay_rate) / size, share)
    rows = decay_rate * old + share * table
    rows_ref[...] = rows
    message_ref[:8, :] = col_ref[...]
    message_ref[4:5, :128] = column_sum(rows)
    message_ref[8:, :] = sums[height:]


def update_kernel(count, heights, widths, *refs):
    messages, refs = refs[:count], refs[count:]
    rows_ref, vectors_ref, moment_ref, refs = refs[0], refs[1], refs[2], refs[3:]
    grads, masters, cols_old, refs = refs[:4], refs[4:8], refs[8:12], refs[12:]
    news, cols_new, refs = refs[:4], refs[4:8], refs[8:]
    row_out_ref, vector_grad_ref, moment_new_ref, vector_new_ref = refs
    total = added([message[...] for message in messages])
    rows_new = rows_ref[...]
    height = rows_new.shape[0]
    row_out_ref[...] = rows_new.T[: row_out_ref.shape[0]]
    folds = grads[3].shape[0] // height
    lanes = [[0], [1], [2], list(range(3, 3 + folds))]
    for which in range(4):
        entries = heights[which] * widths[which]
        cols = cols_old[which].shape[1]
        new = decay_rate * cols_old[which][...] + (1.0 - decay_rate) / heights[which] * total[
            which : which + 1, :cols
        ]
        cols_new[which][...] = new
        mean_rows = sum(total[4:5, lane : lane + 1] for lane in lanes[which]) / heights[which]
        squares = sum(total[4:5, 3 + folds + lane : 4 + folds + lane] for lane in lanes[which])
        rate = step_rate * jnp.sqrt(squares / entries)
        across = new / mean_rows
        for fold, lane in enumerate(lanes[which]):
            part = slice(fold * height, (fold + 1) * height)
            second = rows_new[:, lane : lane + 1] * across
            news[which][part, :] = masters[which][part, :] - rate * grads[which][part, :] * lax.rsqrt(second)
    vectors = vectors_ref[...]
    gradient = total[8 : 8 + vectors.shape[0]]
    vector_grad_ref[...] = gradient
    moment = decay_rate * moment_ref[...] + (1.0 - decay_rate) * (gradient * gradient + tiny_square)
    moment_new_ref[...] = moment
    spread = jnp.sqrt(jnp.mean(vectors * vectors, axis=1, keepdims=True))
    vector_new_ref[...] = vectors - step_rate * spread * gradient * lax.rsqrt(moment)


def packed_body(
    tokens, keep_mask, cotangent, qkv_weight, proj_weight, up_weight, down_weight, vectors,
    qkv_rows, qkv_cols, proj_rows, proj_cols, up_rows, up_cols, down_rows, down_cols, vector_moment,
):
    spread, dp_size = lax.axis_size("group"), lax.axis_size("dp")
    low, high = jnp.bfloat16, jnp.float32
    place = linear_place().astype(jnp.int32).reshape(1)
    group = lax.axis_index("group")
    held, slots, width = tokens.shape
    images, length = keep_mask.shape
    hidden = up_weight.shape[1] * spread
    total = images * length
    rows = qkv_weight.shape[0]
    folds = down_weight.shape[0] // rows
    core_bits = (1,)
    near_bits = tuple(1 << at for at in range(1, spread.bit_length()))
    far_bits = tuple(spread << at for at in range(1, dp_size.bit_length() - 1))
    half = spread * dp_size // 2

    def pieces_out(array):
        by_slot = array.transpose(1, 0, 2)
        parts = [
            lax.dynamic_slice_in_dim(by_slot, (group ^ relative) * images, images, axis=1)
            for relative in range(spread)
        ]
        return exchange([part.reshape(slots * images, width) for part in parts])

    def exchange(parts):
        return [parts[0]] + [permute(part, relative) for relative, part in enumerate(parts) if relative]

    def settle(parts):
        parts = [part.reshape(slots, images, width) for part in parts]
        block = slots // 4
        whole = pl.pallas_call(
            functools.partial(settle_kernel, spread),
            grid=(4,),
            in_specs=[pl.BlockSpec(memory_space=pltpu.SMEM)] + [step_block((block, images, width))] * spread,
            out_specs=step_block((block, held, width)),
            out_shape=jax.ShapeDtypeStruct((slots, held, width), low),
            compiler_params=pltpu.CompilerParams(vmem_limit_bytes=vmem_bytes),
        )(place, *parts)
        return whole.transpose(1, 0, 2)

    fold_cols = [down_weight[fold * rows : (fold + 1) * rows] for fold in range(folds)]
    first_pack = jnp.concatenate([qkv_weight, proj_weight], axis=1).astype(low)
    second_pack = jnp.concatenate([up_weight] + fold_cols, axis=1).astype(low)
    first_blocks = lax.all_gather(first_pack, ("dp", "group"), axis=0)
    token_parts = pieces_out(tokens)
    cotangent_parts = pieces_out(cotangent)
    second_blocks = lax.all_gather(second_pack, ("dp", "group"), axis=0)
    bias = jnp.where(keep_mask > 0, 0.0, -1e30)[:, :, None]

    step_rows = PER_STEP * length
    block = (step_rows, width)
    pairs = width // (2 * HEAD_DIM)
    steps = images // PER_STEP
    statics = (images, dp_size, spread)
    wide = scratch(width // 128, total, 128)
    probs_block = (PER_STEP, pairs, length, 2 * length)
    x, qkv, probs, attended, middle, w_qkv, w_proj = call_kernel(
        attention_packed_kernel, statics, steps,
        ["place"] + [None] * spread + [(PER_STEP, length, 1), None, None],
        [
            ((total, width), low, block),
            ((total, 3 * width), low, (step_rows, 3 * width)),
            ((images, *probs_block[1:]), low, probs_block),
            ((total, width), low, block),
            ((total, width), high, block),
            ((width, 3 * width), low, None),
            ((width, width), low, None),
        ],
        [wide, scratch(step_rows, width, dtype=low)],
        (place, *token_parts, bias, first_blocks, vectors),
        2 * total * width * 4 * width + 8 * total * length * width,
    )
    piece = ((slots * images, width), low, None)
    pack_cols = up_weight.shape[1] + (folds + 1) * proj_weight.shape[1]
    results = call_kernel(
        feed_forward_packed_kernel, statics, steps,
        ["place"] + [None] * spread + [block, block] + [None] * 4,
        [piece] * spread
        + [
            ((total, width), high, block),
            ((total, width), low, block),
            ((half, rows, pack_cols), low, None),
            ((half, rows, pack_cols), low, None),
            ((8, width), high, None),
            ((1, hidden), high, None),
        ],
        [
            scratch(width, hidden, dtype=low),
            scratch(hidden, width, dtype=low),
            scratch(hidden, width, dtype=low),
            wide,
            scratch(step_rows, width, dtype=low),
            scratch(width, step_rows, dtype=low),
            scratch(step_rows, width, dtype=low),
            scratch(width, step_rows, dtype=low),
            scratch(step_rows, width),
            scratch(step_rows, 128),
            scratch(step_rows, width),
            scratch(step_rows, width),
            scratch(width, hidden),
            scratch(width, hidden),
            scratch(width, width),
        ],
        (
            place, *cotangent_parts, middle, attended, second_blocks, w_proj, vectors,
            vectors[7:11].reshape(1, hidden),
        ),
        12 * total * width * hidden + 4 * total * width * width, total * hidden,
    )
    output_parts = exchange(results[:spread])
    d_middle, d_attended, ff_keep, ff_leave, ff_sums, up_sums = results[spread:]
    small = functools.partial(
        pl.pallas_call, compiler_params=pltpu.CompilerParams(vmem_limit_bytes=vmem_bytes)
    )
    in_vmem, anywhere = pl.BlockSpec(memory_space=pltpu.VMEM), pl.BlockSpec(memory_space=pl.ANY)

    def add_parts(count, keep, arrived, awaited):
        part = (keep.shape[0] // count, *keep.shape[1:])
        return small(
            functools.partial(add_kernel, count),
            in_specs=[in_vmem] * 2 + [anywhere] * len(awaited),
            out_specs=[in_vmem] * count,
            out_shape=[jax.ShapeDtypeStruct(part, high)]
            + [jax.ShapeDtypeStruct(part, low)] * (count - 1),
        )(keep, arrived, *awaited)

    ff_held, ff_leave = add_parts(2, ff_keep, permute(ff_leave, core_bits[0]), [])
    ff_arrived = permute(ff_leave, near_bits[-1])
    results = call_kernel(
        attention_back_packed_kernel, statics, steps,
        ["place", block, (step_rows, 3 * width), probs_block, block, block, None, None, "await"],
        [piece] * spread
        + [
            ((half, rows, qkv_weight.shape[1]), low, None),
            ((half, rows, qkv_weight.shape[1]), low, None),
            ((8, width), high, None),
        ],
        [
            wide,
            scratch(step_rows, width, dtype=low),
            scratch(step_rows, 3 * width, dtype=low),
            scratch(step_rows, width),
            scratch(width, 3 * width),
        ],
        (place, x, qkv, probs, d_attended, d_middle, w_qkv, vectors, ff_held),
        4 * total * width * 3 * width + 16 * total * length * width,
    )
    qkv_keep, qkv_leave, att_sums = results[spread:]
    qkv_arrived = permute(qkv_leave, core_bits[0])
    input_parts = exchange(results[:spread])
    qkv_held, *leaving = add_parts(4, qkv_keep, qkv_arrived, output_parts[1:])
    near_masks = direct_masks(near_bits)
    qkv_parts = [permute(part, mask) for part, mask in zip(leaving, near_masks)]
    ff_held, ff_leave = add_parts(2, ff_held, ff_arrived, [])
    ff_held = add_wide(ff_held, permute(ff_leave, near_bits[0]))
    qkv_held = add_wide(qkv_held, *qkv_parts)
    blocks, block_parts = scatter_step(jnp.concatenate([ff_held, qkv_held], axis=2), far_bits)
    block_parts = [blocks] + block_parts

    masters = (qkv_weight, proj_weight, up_weight, down_weight)
    heights = [master.shape[0] * dp_size for master in masters]
    widths = [master.shape[1] * spread for master in masters]
    message_rows = vectors.shape[0] + 4
    *grads, message, col_part = small(
        functools.partial(gradient_kernel, len(block_parts)),
        out_shape=[jax.ShapeDtypeStruct(master.shape, high) for master in masters]
        + [jax.ShapeDtypeStruct((rows + message_rows, width), high), jax.ShapeDtypeStruct((8, width), high)],
    )(*block_parts, att_sums, ff_sums, up_sums, *masters)
    messages = [message] + [permute(message, mask) for mask in range(1, spread)]
    rows_old = [part.reshape(-1, rows) for part in (qkv_rows, proj_rows, up_rows, down_rows)]
    rows_new, message = small(
        functools.partial(row_kernel, widths[:3] + widths[3:] * folds),
        out_shape=[
            jax.ShapeDtypeStruct((rows, 128), high),
            jax.ShapeDtypeStruct((8 + message_rows, width), high),
        ],
    )(*rows_old, col_part, *messages)
    message = message + permute(message, near_bits[-1])
    messages = [message] + [permute(message, mask) for mask in direct_masks(far_bits)]
    cols_old = [part.reshape(1, -1) for part in (qkv_cols, proj_cols, up_cols, down_cols)]
    results = small(
        functools.partial(update_kernel, len(messages), heights, widths),
        out_shape=[jax.ShapeDtypeStruct(master.shape, high) for master in masters]
        + [jax.ShapeDtypeStruct(part.shape, high) for part in cols_old]
        + [jax.ShapeDtypeStruct((8, rows), high)]
        + [jax.ShapeDtypeStruct(vectors.shape, high)] * 3,
    )(*messages, rows_new, vectors, vector_moment, *grads, *masters, *cols_old)
    news, cols_new = results[:4], [part.reshape(-1) for part in results[4:8]]
    row_table, vector_grad, vector_moment_new, vector_new = results[8:]
    rows_out = [row_table[0], row_table[1], row_table[2], row_table[3 : 3 + folds].reshape(-1)]
    factored = []
    for which in range(4):
        factored += [grads[which], rows_out[which], cols_new[which], news[which]]
    return (settle(output_parts), settle(input_parts), *factored, vector_grad, vector_moment_new, vector_new)


def body(*arrays):
    spread, dp_size = lax.axis_size("group"), lax.axis_size("dp")
    rows, images = arrays[3].shape[0], arrays[1].shape[0]
    slots, width = arrays[0].shape[1:]
    folds = arrays[6].shape[0] // rows
    powers = all(size & (size - 1) == 0 for size in (spread, dp_size))
    fits = powers and spread == 4 and dp_size > 2
    fits = fits and arrays[5].shape[1] <= width and folds <= 5
    fits = fits and rows % 16 == 0 and images % 16 == 0 and slots % 4 == 0
    return packed_body(*arrays) if fits else general_body(*arrays)


def solution(mesh):
    in_specs = (
        P("dp", "group", None),
        P(("dp", "group"), None),
        P("dp", "group", None),
        P("dp", "group"),
        P("dp", "group"),
        P("dp", "group"),
        P("dp", "group"),
        P(),
        P("dp"),
        P("group"),
        P("dp"),
        P("group"),
        P("dp"),
        P("group"),
        P("dp"),
        P("group"),
        P(),
    )
    out_specs = (
        P("dp", "group", None),
        P("dp", "group", None),
        P("dp", "group"),
        P("dp"),
        P("group"),
        P("dp", "group"),
        P("dp", "group"),
        P("dp"),
        P("group"),
        P("dp", "group"),
        P("dp", "group"),
        P("dp"),
        P("group"),
        P("dp", "group"),
        P("dp", "group"),
        P("dp"),
        P("group"),
        P("dp", "group"),
        P(),
        P(),
        P(),
    )
    return jax.shard_map(body, mesh=mesh, in_specs=in_specs, out_specs=out_specs, check_vma=False)
```

```python
import functools
import math

import jax
import jax.numpy as jnp
from jax import lax
from jax.experimental import pallas as pl
from jax.experimental.pallas import tpu as pltpu
from jax.sharding import PartitionSpec as P

HEAD_DIM = 64
STEP_NUMBER = 10


step_rate = 0.3
norm_epsilon = 1e-06
tiny_square = 1e-30
decay_rate = 1.0 - STEP_NUMBER ** (-0.8)
LOG2_E = 1.4426950408889634


def axis_bits(name):
    count = lax.axis_size(name)
    return [(name, 1 << place) for place in range(count.bit_length() - 1)]


def swap_partner(array, step):
    name, bit = step
    count = lax.axis_size(name)
    return lax.ppermute(array, name, [(rank, rank ^ bit) for rank in range(count)])


def upper_side(step):
    name, bit = step
    return (lax.axis_index(name) & bit) != 0


def gather_blocks(array, steps):
    for step in steps:
        arrived = swap_partner(array, step)
        upper = upper_side(step)
        array = jnp.stack([jnp.where(upper, arrived, array), jnp.where(upper, array, arrived)])
    return array


def scatter_sum(array, steps):
    for step in steps:
        upper = upper_side(step)
        leaving = jnp.where(upper, array[0], array[1]).astype(jnp.bfloat16)
        arrived = swap_partner(leaving, step)
        array = jnp.where(upper, array[1], array[0]).astype(jnp.float32) + arrived.astype(jnp.float32)
    return array


def sum_everywhere(array, steps):
    for step in steps:
        array = array + swap_partner(array, step)
    return array


def sum_parts(parts, steps):
    flat = [part.reshape(-1) for part in parts]
    total = sum_everywhere(jnp.concatenate(flat), steps)
    result, start = [], 0
    for part in parts:
        result.append(total[start : start + part.size].reshape(part.shape))
        start += part.size
    return result


def block_order(steps):
    order = []
    for name in ("dp", "group"):
        bits = sorted((step for step in steps if step[0] == name), key=lambda step: -step[1])
        order.append([steps.index(step) for step in bits])
    return order


def blocks_to_whole(blocks, steps):
    count = len(steps)
    rows, cols = blocks.shape[count:]
    dp_axes, group_axes = block_order(steps)
    dp_axes = [count - 1 - axis for axis in dp_axes]
    group_axes = [count - 1 - axis for axis in group_axes]
    whole = blocks.transpose(dp_axes + [count] + group_axes + [count + 1])
    return whole.reshape(rows << len(dp_axes), cols << len(group_axes))


def whole_to_blocks(whole, steps):
    dp_axes, group_axes = block_order(steps)
    rows = whole.shape[0] >> len(dp_axes)
    cols = whole.shape[1] >> len(group_axes)
    split = whole.reshape([2] * len(dp_axes) + [rows] + [2] * len(group_axes) + [cols])
    places = dp_axes + [len(steps)] + group_axes + [len(steps) + 1]
    return split.transpose([places.index(axis) for axis in range(len(places))])


PER_STEP = 4
FF_CHUNK = 256
vmem_bytes = 60 * 1024 * 1024


def dot(left, right, left_axis=1, right_axis=0):
    return lax.dot_general(
        left, right, (((left_axis,), (right_axis,)), ((), ())), preferred_element_type=jnp.float32
    )


def normal_form(values):
    center = jnp.mean(values, axis=-1, keepdims=True)
    centered = values - center
    spread = jnp.mean(centered * centered, axis=-1, keepdims=True)
    scale = lax.rsqrt(spread + norm_epsilon)
    return centered * scale, scale


def norm_back(grad, unit, scale, gain):
    weighted = grad * gain
    along = jnp.mean(weighted * unit, axis=-1, keepdims=True)
    level = jnp.mean(weighted, axis=-1, keepdims=True)
    return scale * (weighted - level - unit * along)


def column_sum(values):
    return jnp.sum(values, axis=0, keepdims=True)


def pair_mask(length):
    return lax.broadcasted_iota(jnp.int32, (length, 2 * HEAD_DIM), 1) < HEAD_DIM


def stack_heads(pair, first):
    none = jnp.zeros_like(pair)
    return jnp.concatenate([jnp.where(first, pair, none), jnp.where(first, none, pair)], axis=0)


def join_heads(rows, first):
    length = rows.shape[0] // 2
    return jnp.where(first, rows[:length], rows[length:])


def gelu_and_slope(pre):
    bell = jnp.exp2(pre * pre * (-0.5 * LOG2_E))
    inverse = 1.0 / (1.0 + (0.3275911 * 0.5**0.5) * jnp.abs(pre))
    poly = inverse * (
        0.5 * 0.254829592
        + inverse
        * (
            0.5 * -0.284496736
            + inverse
            * (0.5 * 1.421413741 + inverse * (0.5 * -1.453152027 + inverse * (0.5 * 1.061405429)))
        )
    )
    tail = poly * bell
    below = jnp.where(pre >= 0, 1.0 - tail, tail)
    return pre * below, below + pre * bell * 0.3989422804014327


def widen(source_ref, wide_ref, images):
    tiles, total, lanes = wide_ref.shape
    rows_at_once = 8 * images

    @pl.loop(0, total // rows_at_once)
    def _(part):
        rows = pl.ds(pl.multiple_of(part * rows_at_once, rows_at_once), rows_at_once)
        for tile in range(tiles):
            cols = slice(tile * lanes, (tile + 1) * lanes)
            wide_ref[tile, rows, :] = source_ref[rows, cols].astype(jnp.float32)


def narrow(wide_ref, target_ref, images):
    tiles, total, lanes = wide_ref.shape
    rows_at_once = 8 * images

    @pl.loop(0, total // rows_at_once)
    def _(part):
        rows = pl.ds(pl.multiple_of(part * rows_at_once, rows_at_once), rows_at_once)
        for tile in range(tiles):
            cols = slice(tile * lanes, (tile + 1) * lanes)
            target_ref[rows, cols] = wide_ref[tile, rows, :].astype(target_ref.dtype)


def take_image(wide_ref, image, images):
    tiles, total, _ = wide_ref.shape
    rows = pl.ds(image, total // images, images)
    return jnp.concatenate([wide_ref[tile, rows, :] for tile in range(tiles)], axis=1)


def put_image(wide_ref, image, images, values):
    tiles, total, lanes = wide_ref.shape
    rows = pl.ds(image, total // images, images)
    for tile in range(tiles):
        wide_ref[tile, rows, :] = values[:, tile * lanes : (tile + 1) * lanes]


def attention_kernel(images, tokens_ref, bias_ref, *refs):
    wide_ref = refs[-2]

    @pl.when(pl.program_id(0) == 0)
    def _():
        widen(tokens_ref, wide_ref, images)

    attention_steps(images, lambda image: bias_ref[image], *refs)


def attention_steps(
    images, bias_column, w_qkv_ref, w_proj_ref, vectors_ref,
    x_ref, qkv_ref, probs_ref, attended_ref, middle_ref, wide_ref, normed_ref,
):
    step = pl.program_id(0)
    length = wide_ref.shape[1] // images
    width = x_ref.shape[1]
    per_step = x_ref.shape[0] // length

    for image in range(per_step):
        rows = slice(image * length, (image + 1) * length)
        x = take_image(wide_ref, step * per_step + image, images)
        x_ref[rows, :] = x.astype(jnp.bfloat16)
        unit, _ = normal_form(x)
        normed_ref[rows, :] = (unit * vectors_ref[0:1] + vectors_ref[1:2]).astype(jnp.bfloat16)
    for part in range(3):
        cols = slice(part * width, (part + 1) * width)
        projected = dot(normed_ref[...], w_qkv_ref[:, cols])
        if part != 1:
            row = 2 if part == 0 else 3
            projected = projected + vectors_ref[row : row + 1]
        qkv_ref[:, cols] = projected.astype(jnp.bfloat16)

    @pl.loop(0, per_step)
    def _(image):
        rows = pl.ds(pl.multiple_of(image * length, length), length)
        first = pair_mask(length)
        place = lax.broadcasted_iota(jnp.int32, (length, 2 * length), 0)
        asker = lax.broadcasted_iota(jnp.int32, (length, 2 * length), 1)
        asker = jnp.where(asker >= length, asker - length, asker)
        bias = jnp.where(place == asker, 0.0, bias_column(image))
        for pair in range(width // (2 * HEAD_DIM)):
            low = pair * 2 * HEAD_DIM
            queries = stack_heads(qkv_ref[rows, low : low + 2 * HEAD_DIM], first)
            keys = qkv_ref[rows, width + low : width + low + 2 * HEAD_DIM]
            values = qkv_ref[rows, 2 * width + low : 2 * width + low + 2 * HEAD_DIM]
            scores = dot(keys, queries, 1, 1) * (HEAD_DIM**-0.5 * LOG2_E) + bias
            weights = jnp.exp2(scores - jnp.max(scores, axis=0, keepdims=True))
            probs = weights * (1.0 / jnp.sum(weights, axis=0, keepdims=True))
            probs = probs.astype(jnp.bfloat16)
            probs_ref[image, pair] = probs
            attended = join_heads(dot(probs, values, 0, 0), first)
            attended_ref[rows, low : low + 2 * HEAD_DIM] = attended.astype(jnp.bfloat16)

    middle_ref[...] = (
        x_ref[...].astype(jnp.float32)
        + dot(attended_ref[...], w_proj_ref[...])
        + vectors_ref[4:5]
    )


def feed_forward_kernel(
    images, middle_ref, cotangent_ref, attended_ref, w_up_ref, w_down_ref, w_proj_ref, vectors_ref, bias_up_ref,
    output_ref, d_middle_ref, d_attended_ref, up_grad_ref, down_grad_ref, proj_grad_ref, vector_sums_ref, up_sums_ref,
    wide_ref, *scratches,
):
    up_total_ref, down_total_ref, proj_total_ref = scratches[-3:]

    @pl.when(pl.program_id(0) == 0)
    def _():
        widen(cotangent_ref, wide_ref, images)

    feed_forward_steps(
        images, middle_ref, attended_ref, w_up_ref, w_down_ref, w_proj_ref, vectors_ref, bias_up_ref,
        d_middle_ref, d_attended_ref, vector_sums_ref, up_sums_ref, wide_ref, *scratches,
    )

    @pl.when(pl.program_id(0) == pl.num_programs(0) - 1)
    def _():
        narrow(wide_ref, output_ref, images)
        up_grad_ref[...] = up_total_ref[...].astype(jnp.bfloat16)
        down_grad_ref[...] = down_total_ref[...].T.astype(jnp.bfloat16)
        proj_grad_ref[...] = proj_total_ref[...].astype(jnp.bfloat16)


def feed_forward_steps(
    images, middle_ref, attended_ref, w_up_ref, w_down_ref, w_proj_ref, vectors_ref, bias_up_ref,
    d_middle_ref, d_attended_ref, vector_sums_ref, up_sums_ref,
    wide_ref, normed_ref, normed_t_ref, dy_ref, dy_t_ref, unit_ref, scale_ref, ahead_ref, back_ref,
    up_total_ref, down_total_ref, proj_total_ref,
):
    step = pl.program_id(0)
    length = wide_ref.shape[1] // images
    hidden = w_up_ref.shape[1]
    per_step = middle_ref.shape[0] // length

    @pl.when(step == 0)
    def _():
        for total in (up_total_ref, down_total_ref, proj_total_ref, vector_sums_ref, up_sums_ref):
            total[...] = jnp.zeros_like(total)

    for image in range(per_step):
        rows = slice(image * length, (image + 1) * length)
        dy = take_image(wide_ref, step * per_step + image, images)
        dy_ref[rows, :] = dy.astype(jnp.bfloat16)
        vector_sums_ref[3:4] += column_sum(dy)
        unit, scale = normal_form(middle_ref[rows, :])
        unit_ref[rows, :] = unit
        scale_ref[rows, :] = jnp.broadcast_to(scale, (length, scale_ref.shape[1]))
        normed_ref[rows, :] = (unit * vectors_ref[5:6] + vectors_ref[6:7]).astype(jnp.bfloat16)
    normed_t_ref[...] = normed_ref[...].T
    dy_t_ref[...] = dy_ref[...].T
    ahead_ref[...] = jnp.zeros_like(ahead_ref)
    back_ref[...] = jnp.zeros_like(back_ref)

    @pl.loop(0, hidden // FF_CHUNK)
    def _(chunk):
        cols = pl.ds(pl.multiple_of(chunk * FF_CHUNK, FF_CHUNK), FF_CHUNK)
        w_up = w_up_ref[:, cols]
        w_down = w_down_ref[cols, :]
        active, slope = gelu_and_slope(dot(normed_ref[...], w_up) + bias_up_ref[:, cols])
        active = active.astype(jnp.bfloat16)
        d_hidden = dot(dy_ref[...], w_down, 1, 1) * slope
        d_hidden = d_hidden.astype(jnp.bfloat16)
        ahead_ref[...] += dot(active, w_down)
        back_ref[...] += dot(d_hidden, w_up, 1, 1)
        down_total_ref[:, cols] += dot(dy_t_ref[...], active)
        up_total_ref[:, cols] += dot(normed_t_ref[...], d_hidden)
        up_sums_ref[:, cols] += column_sum(d_hidden.astype(jnp.float32))

    for image in range(per_step):
        rows = slice(image * length, (image + 1) * length)
        output = middle_ref[rows, :] + ahead_ref[rows, :] + vectors_ref[11:12]
        put_image(wide_ref, step * per_step + image, images, output)
        unit = unit_ref[rows, :]
        grad = back_ref[rows, :]
        vector_sums_ref[1:2] += column_sum(grad * unit)
        vector_sums_ref[2:3] += column_sum(grad)
        d_middle = dy_ref[rows, :].astype(jnp.float32) + norm_back(
            grad, unit, scale_ref[rows, 0:1], vectors_ref[5:6]
        )
        d_middle_ref[rows, :] = d_middle
        d_branch = d_middle.astype(jnp.bfloat16)
        dy_ref[rows, :] = d_branch
        vector_sums_ref[0:1] += column_sum(d_branch.astype(jnp.float32))
    proj_total_ref[...] += dot(attended_ref[...], dy_ref[...], 0, 0)
    d_attended_ref[...] = dot(dy_ref[...], w_proj_ref[...], 1, 1).astype(jnp.bfloat16)


def attention_back_kernel(
    images, x_ref, qkv_ref, probs_ref, d_attended_ref, d_middle_ref, w_qkv_ref, vectors_ref,
    input_grad_ref, qkv_grad_ref, vector_sums_ref, wide_ref, *scratches,
):
    attention_back_steps(
        images, x_ref, qkv_ref, probs_ref, d_attended_ref, d_middle_ref, w_qkv_ref, vectors_ref,
        vector_sums_ref, wide_ref, *scratches,
    )

    @pl.when(pl.program_id(0) == pl.num_programs(0) - 1)
    def _():
        narrow(wide_ref, input_grad_ref, images)
        qkv_grad_ref[...] = scratches[-1][...].astype(jnp.bfloat16)


def attention_back_steps(
    images, x_ref, qkv_ref, probs_ref, d_attended_ref, d_middle_ref, w_qkv_ref, vectors_ref,
    vector_sums_ref, wide_ref, normed_ref, d_projected_ref, back_ref, qkv_total_ref,
):
    step = pl.program_id(0)
    width = x_ref.shape[1]
    length = probs_ref.shape[2]
    per_step = probs_ref.shape[0]

    @pl.when(step == 0)
    def _():
        qkv_total_ref[...] = jnp.zeros_like(qkv_total_ref)
        vector_sums_ref[...] = jnp.zeros_like(vector_sums_ref)

    @pl.loop(0, per_step)
    def _(image):
        rows = pl.ds(pl.multiple_of(image * length, length), length)
        first = pair_mask(length)
        for pair in range(width // (2 * HEAD_DIM)):
            low = pair * 2 * HEAD_DIM
            cols = [slice(part * width + low, part * width + low + 2 * HEAD_DIM) for part in range(3)]
            queries = stack_heads(qkv_ref[rows, cols[0]], first)
            keys = qkv_ref[rows, cols[1]]
            values = qkv_ref[rows, cols[2]]
            probs = probs_ref[image, pair]
            d_attended = stack_heads(d_attended_ref[rows, cols[0]], first)
            d_projected_ref[rows, cols[2]] = dot(probs, d_attended).astype(jnp.bfloat16)
            d_probs = dot(values, d_attended, 1, 1)
            probs = probs.astype(jnp.float32)
            along = jnp.sum(d_probs * probs, axis=0, keepdims=True)
            d_scores = (probs * (d_probs - along)).astype(jnp.bfloat16)
            scale = HEAD_DIM**-0.5
            d_queries = join_heads(dot(d_scores, keys, 0, 0), first) * scale
            d_projected_ref[rows, cols[0]] = d_queries.astype(jnp.bfloat16)
            d_projected_ref[rows, cols[1]] = (dot(d_scores, queries) * scale).astype(jnp.bfloat16)

    vector_sums_ref[2:3] += column_sum(d_projected_ref[:, :width].astype(jnp.float32))
    vector_sums_ref[3:4] += column_sum(d_projected_ref[:, 2 * width :].astype(jnp.float32))
    back_ref[...] = dot(d_projected_ref[...], w_qkv_ref[...], 1, 1)
    for image in range(per_step):
        rows = slice(image * length, (image + 1) * length)
        unit, scale = normal_form(x_ref[rows, :].astype(jnp.float32))
        normed_ref[rows, :] = (unit * vectors_ref[0:1] + vectors_ref[1:2]).astype(jnp.bfloat16)
        grad = back_ref[rows, :]
        vector_sums_ref[0:1] += column_sum(grad * unit)
        vector_sums_ref[1:2] += column_sum(grad)
        d_input = d_middle_ref[rows, :] + norm_back(grad, unit, scale, vectors_ref[0:1])
        put_image(wide_ref, step * per_step + image, images, d_input)
    qkv_total_ref[...] += dot(normed_ref[...], d_projected_ref[...], 0, 0)


def whole_block(shape):
    return pl.BlockSpec(shape, lambda step: (0,) * len(shape))


def step_block(shape):
    return pl.BlockSpec(shape, lambda step: (step,) + (0,) * (len(shape) - 1))


def scratch(*shape, dtype=jnp.float32):
    return pltpu.VMEM(shape, dtype)


def call_kernel(kernel, statics, steps, ins, outs, scratches, operands, flops, transcendentals=0):
    in_specs = [
        pl.BlockSpec(memory_space=pltpu.SMEM)
        if block == "place"
        else pl.BlockSpec(memory_space=pl.ANY)
        if block == "await"
        else whole_block(op.shape) if block is None else step_block(block)
        for op, block in zip(operands, ins)
    ]
    out_specs = [
        whole_block(shape) if block is None else step_block(block) for shape, dtype, block in outs
    ]
    moved = sum(op.size * op.dtype.itemsize for op in operands) + sum(
        math.prod(shape) * jnp.dtype(dtype).itemsize for shape, dtype, block in outs
    )
    return pl.pallas_call(
        functools.partial(kernel, *statics),
        grid=(steps,),
        in_specs=in_specs,
        out_specs=out_specs,
        out_shape=[jax.ShapeDtypeStruct(shape, dtype) for shape, dtype, block in outs],
        scratch_shapes=scratches,
        compiler_params=pltpu.CompilerParams(vmem_limit_bytes=vmem_bytes),
        cost_estimate=pl.CostEstimate(
            flops=flops, bytes_accessed=moved, transcendentals=transcendentals
        ),
    )(*operands)


def attention_forward(tokens, bias, w_qkv, w_proj, vectors):
    images, length, _ = bias.shape
    total, width = tokens.shape
    pairs = width // (2 * HEAD_DIM)
    rows = PER_STEP * length
    low, high = jnp.bfloat16, jnp.float32
    outs = [
        ((total, width), low, (rows, width)),
        ((total, 3 * width), low, (rows, 3 * width)),
        ((images, pairs, length, 2 * length), low, (PER_STEP, pairs, length, 2 * length)),
        ((total, width), low, (rows, width)),
        ((total, width), high, (rows, width)),
    ]
    return call_kernel(
        attention_kernel, (images,), images // PER_STEP,
        [None, (PER_STEP, length, 1), None, None, None], outs,
        [scratch(width // 128, total, 128), scratch(rows, width, dtype=low)],
        (tokens, bias, w_qkv, w_proj, vectors),
        2 * total * width * 4 * width + 8 * total * length * width,
    )


def feed_forward(images, middle, cotangent, attended, w_up, w_down, w_proj, vectors):
    total, width = middle.shape
    hidden = w_up.shape[1]
    rows = total // images * PER_STEP
    low, high = jnp.bfloat16, jnp.float32
    block = (rows, width)
    outs = [
        ((total, width), low, None),
        ((total, width), high, block),
        ((total, width), low, block),
        ((width, hidden), low, None),
        ((hidden, width), low, None),
        ((width, width), low, None),
        ((8, width), high, None),
        ((1, hidden), high, None),
    ]
    scratches = [
        scratch(width // 128, total, 128),
        scratch(rows, width, dtype=low),
        scratch(width, rows, dtype=low),
        scratch(rows, width, dtype=low),
        scratch(width, rows, dtype=low),
        scratch(rows, width),
        scratch(rows, 128),
        scratch(rows, width),
        scratch(rows, width),
        scratch(width, hidden),
        scratch(width, hidden),
        scratch(width, width),
    ]
    return call_kernel(
        feed_forward_kernel, (images,), images // PER_STEP,
        [block, None, block, None, None, None, None, None], outs, scratches,
        (middle, cotangent, attended, w_up, w_down, w_proj, vectors, vectors[7:11].reshape(1, hidden)),
        12 * total * width * hidden + 4 * total * width * width, total * hidden,
    )


def attention_back(x, qkv, probs, d_attended, d_middle, w_qkv, vectors):
    images, pairs, length, _ = probs.shape
    total, width = x.shape
    rows = PER_STEP * length
    low, high = jnp.bfloat16, jnp.float32
    block = (rows, width)
    outs = [
        ((total, width), low, None),
        ((width, 3 * width), low, None),
        ((8, width), high, None),
    ]
    scratches = [
        scratch(width // 128, total, 128),
        scratch(rows, width, dtype=low),
        scratch(rows, 3 * width, dtype=low),
        scratch(rows, width),
        scratch(width, 3 * width),
    ]
    return call_kernel(
        attention_back_kernel, (images,), images // PER_STEP,
        [block, (rows, 3 * width), (PER_STEP, pairs, length, 2 * length), block, block, None, None],
        outs, scratches, (x, qkv, probs, d_attended, d_middle, w_qkv, vectors),
        4 * total * width * 3 * width + 16 * total * length * width,
    )

def linear_place():
    return lax.axis_index("dp") * lax.axis_size("group") + lax.axis_index("group")


def permute(array, mask):
    count = lax.axis_size("dp") * lax.axis_size("group")
    return lax.ppermute(array, ("dp", "group"), [(rank, rank ^ mask) for rank in range(count)])


def direct_masks(bits):
    masks = [0]
    for bit in bits:
        masks = masks + [mask | bit for mask in masks]
    return masks[1:]


def scatter_step(held, bits):
    masks = direct_masks(bits)
    size = held.shape[0] // (len(masks) + 1)
    parts = [
        permute(held[size * (at + 1) : size * (at + 2)].astype(jnp.bfloat16), mask)
        for at, mask in enumerate(masks)
    ]
    return held[:size], parts


def add_wide(first, *rest):
    total = first.astype(jnp.float32)
    for part in rest:
        total = total + part.astype(jnp.float32)
    return total


def packed_place(mask, spread, count):
    return ((mask >> 1) & (spread - 1)) * (count // (2 * spread)) + (mask >> (spread.bit_length()))


def gather_packed(block, first_bits, later_rounds):
    held = [block[None]]
    held = held + [permute(held[0], mask) for mask in direct_masks(first_bits)]
    held = [jnp.concatenate(held)]
    for bits in later_rounds:
        held = held + [permute(part, mask) for mask in direct_masks(bits) for part in held]
    return held


def unpack(place_ref, block_refs, packed_ref, put, dp_size, spread):
    place = place_ref[0]
    size = block_refs[0].shape[0]
    for at, block_ref in enumerate(block_refs):
        packed_ref[at * size : (at + 1) * size] = block_ref[...]
    count = dp_size * spread
    for row in range(dp_size):
        for col in range(spread):
            mask = (row * spread + col) ^ place
            at = packed_place(mask, spread, count) + (mask & 1) * (count // 2)
            put(row, col, packed_ref[at])


def pack(place_ref, take, keep_ref, leave_ref, dp_size, spread):
    place = place_ref[0]
    odd = (place & 1) == 1
    for row in range(dp_size):
        for col in range(0, spread, 2):
            at = packed_place((row * spread + col) ^ place, spread, dp_size * spread)
            even_block, odd_block = take(row, col), take(row, col + 1)
            keep_ref[at] = jnp.where(odd, odd_block, even_block)
            leave_ref[at] = jnp.where(odd, even_block, odd_block)


def narrow_pieces(place_ref, wide_ref, piece_refs, spread):
    tiles, _, lanes = wide_ref.shape
    rows_of_piece = piece_refs[0].shape[0]
    step = 64
    group = place_ref[0] & (spread - 1)
    for relative, piece_ref in enumerate(piece_refs):
        base = (group ^ relative) * rows_of_piece

        @pl.loop(0, rows_of_piece // step)
        def _(part):
            target = pl.ds(pl.multiple_of(part * step, step), step)
            source = pl.ds(pl.multiple_of(base + part * step, step), step)
            for tile in range(tiles):
                cols = slice(tile * lanes, (tile + 1) * lanes)
                piece_ref[target, cols] = wide_ref[tile, source, :].astype(jnp.bfloat16)


def general_body(
    tokens,
    keep_mask,
    cotangent,
    qkv_weight,
    proj_weight,
    up_weight,
    down_weight,
    vectors,
    qkv_rows,
    qkv_cols,
    proj_rows,
    proj_cols,
    up_rows,
    up_cols,
    down_rows,
    down_cols,
    vector_moment,
):
    masters = (qkv_weight, proj_weight, up_weight, down_weight)
    lowered = tuple((master.astype(jnp.bfloat16) for master in masters))
    dp_bits, group_bits = axis_bits("dp"), axis_bits("group")
    gather_steps = dp_bits[1:] + group_bits[1:] + dp_bits[:1] + group_bits[:1]
    scatter_steps = gather_steps[::-1]
    w_qkv, w_proj, w_up, w_down = tuple(
        blocks_to_whole(gather_blocks(part, gather_steps), gather_steps) for part in lowered
    )
    spread = lax.axis_size("group")

    def slots_in(array):
        held, slots, width = array.shape
        parts = array.transpose(1, 0, 2).reshape(slots, spread, held // spread, width)
        parts = lax.all_to_all(
            parts.transpose(1, 0, 2, 3), "group", split_axis=0, concat_axis=0, tiled=True
        )
        return parts.reshape(spread * slots * (held // spread), width)

    def slots_out(array):
        held, slots, width = tokens.shape
        parts = array.reshape(spread, slots, held // spread, width)
        parts = lax.all_to_all(parts, "group", split_axis=0, concat_axis=0, tiled=True)
        return parts.transpose(1, 0, 2, 3).reshape(slots, held, width).transpose(1, 0, 2)

    images = keep_mask.shape[0]
    bias = jnp.where(keep_mask > 0, 0.0, -1e30)[:, :, None]
    x, qkv, probs, attended, middle = attention_forward(
        slots_in(tokens), bias, w_qkv, w_proj, vectors
    )
    output, d_middle, d_attended, up_grad, down_grad, proj_grad, ff_sums, up_sums = feed_forward(
        images, middle, slots_in(cotangent), attended, w_up, w_down, w_proj, vectors
    )
    block_output = slots_out(output)
    d_input, qkv_grad, att_sums = attention_back(
        x, qkv, probs, d_attended, d_middle, w_qkv, vectors
    )
    input_grad = slots_out(d_input)
    local_vectors = jnp.concatenate(
        [att_sums[:4], ff_sums[:3], up_sums.reshape(4, -1), ff_sums[3:4]], axis=0
    )
    vector_grad = sum_everywhere(local_vectors, group_bits + dp_bits)
    local_grads = (qkv_grad, proj_grad, up_grad, down_grad)
    owned = tuple(
        scatter_sum(whole_to_blocks(part, scatter_steps), scatter_steps) for part in local_grads
    )
    squares = tuple((gradient * gradient + tiny_square for gradient in owned))
    row_parts = tuple((jnp.sum(square, axis=1) for square in squares)) + tuple(
        (jnp.sum(master * master, axis=1) for master in masters)
    )
    row_sums = sum_parts(row_parts, group_bits)
    rows_old = (qkv_rows, proj_rows, up_rows, down_rows)
    cols_old = (qkv_cols, proj_cols, up_cols, down_cols)
    total_cols = tuple((gradient.shape[1] * lax.axis_size("group") for gradient in owned))
    total_rows = tuple((gradient.shape[0] * lax.axis_size("dp") for gradient in owned))
    rows_new = tuple(
        (
            decay_rate * rows_old[which] + (1.0 - decay_rate) * row_sums[which] / total_cols[which]
            for which in range(4)
        )
    )
    col_parts = (
        tuple((jnp.sum(square, axis=0) for square in squares))
        + tuple((jnp.sum(row_stat) for row_stat in rows_new))
        + tuple((jnp.sum(row_sums[4 + which]) for which in range(4)))
    )
    col_sums = sum_parts(col_parts, dp_bits)
    results = []
    for which in range(4):
        cols_new = (
            decay_rate * cols_old[which] + (1.0 - decay_rate) * col_sums[which] / total_rows[which]
        )
        mean_rows = col_sums[4 + which] / total_rows[which]
        spread = jnp.sqrt(col_sums[8 + which] / (total_rows[which] * total_cols[which]))
        second = rows_new[which][:, None] * cols_new[None, :] / mean_rows
        updated = masters[which] - step_rate * spread * owned[which] * lax.rsqrt(second)
        results.append((owned[which], rows_new[which], cols_new, updated))
    vector_moment_new = decay_rate * vector_moment + (1.0 - decay_rate) * (
        vector_grad * vector_grad + tiny_square
    )
    row_spread = jnp.sqrt(jnp.mean(vectors * vectors, axis=1, keepdims=True))
    vector_new = vectors - step_rate * row_spread * vector_grad * lax.rsqrt(vector_moment_new)
    return (
        block_output,
        input_grad,
        results[0][0],
        results[0][1],
        results[0][2],
        results[0][3],
        results[1][0],
        results[1][1],
        results[1][2],
        results[1][3],
        results[2][0],
        results[2][1],
        results[2][2],
        results[2][3],
        results[3][0],
        results[3][1],
        results[3][2],
        results[3][3],
        vector_grad,
        vector_moment_new,
        vector_new,
    )


def attention_packed_kernel(
    images, dp_size, spread, place_ref, tokens_ref, *refs
):
    blocks, refs = refs[: 2 * spread], refs[2 * spread :]
    (
        keep_ref, vectors_ref,
        x_ref, qkv_ref, probs_ref, attended_ref, middle_ref, w_qkv_ref, w_proj_ref,
        packed_ref, bias_ref, wide_ref, normed_ref,
    ) = refs
    rows = packed_ref.shape[1]
    qkv_cols, proj_cols = w_qkv_ref.shape[1] // spread, w_proj_ref.shape[1] // spread

    @pl.when(pl.program_id(0) == 0)
    def _():
        widen(tokens_ref, wide_ref, images)
        bias_ref[...] = jnp.where(keep_ref[...] > 0, 0.0, -1e30).T

        def put(row, col, block):
            down = slice(row * rows, (row + 1) * rows)
            w_qkv_ref[down, col * qkv_cols : (col + 1) * qkv_cols] = block[:, :qkv_cols]
            w_proj_ref[down, col * proj_cols : (col + 1) * proj_cols] = block[:, qkv_cols:]

        unpack(place_ref, blocks, packed_ref, put, dp_size, spread)

    def bias_column(image):
        here = pl.program_id(0) * probs_ref.shape[0] + image
        lane = lax.broadcasted_iota(jnp.int32, bias_ref.shape, 1)
        return row_sum(jnp.where(lane == here, bias_ref[...], 0.0))

    attention_steps(
        images, bias_column, w_qkv_ref, w_proj_ref, vectors_ref,
        x_ref, qkv_ref, probs_ref, attended_ref, middle_ref, wide_ref, normed_ref,
    )


def feed_forward_packed_kernel(images, dp_size, spread, place_ref, *refs):
    cotangent_ref, blocks, refs = refs[0], refs[1 : 1 + 2 * spread], refs[1 + 2 * spread :]
    middle_ref, attended_ref, w_proj_ref, vectors_ref = refs[:4]
    outputs, refs = refs[4 : 4 + spread], refs[4 + spread :]
    d_middle_ref, d_attended_ref, keep_ref, leave_ref, vector_sums_ref, up_sums_ref = refs[:6]
    w_up_ref, w_down_ref, down_low_ref, packed_ref, bias_up_ref, wide_ref = refs[6:12]
    scratches = refs[12:]
    width = w_up_ref.shape[0]
    up_total_ref, down_total_ref, proj_total_ref = scratches[-3:]
    rows = packed_ref.shape[1]
    up_cols = w_up_ref.shape[1] // spread
    out_cols = w_down_ref.shape[1] // spread
    folds = w_down_ref.shape[0] // w_up_ref.shape[0]

    @pl.when(pl.program_id(0) == 0)
    def _():
        widen(cotangent_ref, wide_ref, images)
        for fold in range(bias_up_ref.shape[1] // width):
            bias_up_ref[:, fold * width : (fold + 1) * width] = vectors_ref[7 + fold : 8 + fold]

        def put(row, col, block):
            w_up_ref[row * rows : (row + 1) * rows, col * up_cols : (col + 1) * up_cols] = block[:, :up_cols]
            for fold in range(folds):
                down = (row * folds + fold) * rows
                start = up_cols + fold * out_cols
                w_down_ref[down : down + rows, col * out_cols : (col + 1) * out_cols] = block[
                    :, start : start + out_cols
                ]

        unpack(place_ref, blocks, packed_ref, put, dp_size, spread)

    feed_forward_steps(
        images, middle_ref, attended_ref, w_up_ref, w_down_ref, w_proj_ref, vectors_ref, bias_up_ref,
        d_middle_ref, d_attended_ref, vector_sums_ref, up_sums_ref, wide_ref, *scratches,
    )

    @pl.when(pl.program_id(0) == pl.num_programs(0) - 1)
    def _():
        narrow_pieces(place_ref, wide_ref, outputs, spread)
        down_low_ref[...] = down_total_ref[...].T.astype(jnp.bfloat16)

        def take(row, col):
            across = slice(row * rows, (row + 1) * rows)
            cols = slice(col * out_cols, (col + 1) * out_cols)
            parts = [up_total_ref[across, col * up_cols : (col + 1) * up_cols].astype(jnp.bfloat16)]
            for fold in range(folds):
                down = (row * folds + fold) * rows
                parts.append(down_low_ref[down : down + rows, cols])
            parts.append(proj_total_ref[across, cols].astype(jnp.bfloat16))
            return jnp.concatenate(parts, axis=1)

        pack(place_ref, take, keep_ref, leave_ref, dp_size, spread)


def attention_back_packed_kernel(
    images, dp_size, spread, place_ref, x_ref, qkv_ref, probs_ref, d_attended_ref, d_middle_ref, w_qkv_ref,
    vectors_ref, _, *refs,
):
    pieces, refs = refs[:spread], refs[spread:]
    keep_ref, leave_ref, vector_sums_ref, wide_ref = refs[:4]
    scratches = refs[4:]
    total_ref = scratches[-1]
    attention_back_steps(
        images, x_ref, qkv_ref, probs_ref, d_attended_ref, d_middle_ref, w_qkv_ref, vectors_ref,
        vector_sums_ref, wide_ref, *scratches,
    )

    @pl.when(pl.program_id(0) == pl.num_programs(0) - 1)
    def _():
        narrow_pieces(place_ref, wide_ref, pieces, spread)
        rows, cols = keep_ref.shape[1:]

        def take(row, col):
            block = total_ref[row * rows : (row + 1) * rows, col * cols : (col + 1) * cols]
            return block.astype(jnp.bfloat16)

        pack(place_ref, take, keep_ref, leave_ref, dp_size, spread)


def cut_copies(spread, array_ref, parts_ref, done):
    count = parts_ref.shape[2]
    return [
        pltpu.make_async_copy(
            array_ref.at[:, member * count : (member + 1) * count, :], parts_ref.at[member], done.at[member]
        )
        for member in range(spread)
    ]


def cut_kernel(spread, array_ref, parts_ref, done):
    copies = cut_copies(spread, array_ref, parts_ref, done)
    for copy in copies:
        copy.start()
    for copy in copies:
        copy.wait()


def front_kernel(spread, array_ref, qkv_ref, proj_ref, up_ref, down_ref, parts_ref, first_ref, second_ref, done):
    copies = cut_copies(spread, array_ref, parts_ref, done)
    for copy in copies:
        copy.start()
    rows, start = first_ref.shape[0], qkv_ref.shape[1]
    first_ref[:, :start] = qkv_ref[...].astype(jnp.bfloat16)
    first_ref[:, start:] = proj_ref[...].astype(jnp.bfloat16)
    start, count = up_ref.shape[1], down_ref.shape[1]
    second_ref[:, :start] = up_ref[...].astype(jnp.bfloat16)
    for fold in range(down_ref.shape[0] // rows):
        at = start + fold * count
        second_ref[:, at : at + count] = down_ref[fold * rows : (fold + 1) * rows, :].astype(jnp.bfloat16)
    for copy in copies:
        copy.wait()


def settle_kernel(spread, place_ref, *refs):
    pieces, output_ref, done = refs[:spread], refs[spread], refs[spread + 1]
    group = place_ref[0] & (spread - 1)
    count = pieces[0].shape[1]
    copies = []
    for relative, piece_ref in enumerate(pieces):
        start = pl.multiple_of((group ^ relative) * count, count)
        copies.append(
            pltpu.make_async_copy(piece_ref, output_ref.at[:, pl.ds(start, count), :], done.at[relative])
        )
    for copy in copies:
        copy.start()
    for copy in copies:
        copy.wait()


def lane_table(rows, columns):
    lane = lax.broadcasted_iota(jnp.int32, (rows, 128), 1)
    table = jnp.zeros((rows, 128), jnp.float32)
    for at, column in enumerate(columns):
        table = jnp.where(lane == at, column, table)
    return table


def added(parts):
    while len(parts) > 1:
        parts = [sum(parts[at : at + 2][1:], parts[at]) for at in range(0, len(parts), 2)]
    return parts[0]


def row_sum(values):
    return jnp.sum(values, axis=1, keepdims=True)


def add_kernel(count, keep_ref, arrived_ref, *refs):
    parts = refs[-count:]
    size = parts[0].shape[0]
    for at, part_ref in enumerate(parts):
        rows = slice(at * size, (at + 1) * size)
        total = keep_ref[rows].astype(jnp.float32) + arrived_ref[rows].astype(jnp.float32)
        part_ref[...] = total.astype(part_ref.dtype)


def gradient_kernel(count, *refs):
    block_parts, sums, refs = refs[:count], refs[count : count + 3], refs[count + 3 :]
    masters, refs = refs[:4], refs[4:]
    grads, (message_ref, col_ref) = refs[:4], refs[4:]
    blocks = added([part[0].astype(jnp.float32) for part in block_parts])
    rows, up_cols = grads[2].shape
    qkv_cols, out_cols = grads[0].shape[1], grads[1].shape[1]
    folds = grads[3].shape[0] // rows
    up = blocks[:, :up_cols]
    downs = [blocks[:, up_cols + fold * out_cols :][:, :out_cols] for fold in range(folds)]
    start = up_cols + folds * out_cols
    proj = blocks[:, start : start + out_cols]
    qkv = blocks[:, start + out_cols :]
    grads[0][...] = qkv
    grads[1][...] = proj
    grads[2][...] = up
    for fold in range(folds):
        grads[3][fold * rows : (fold + 1) * rows, :] = downs[fold]
    squares = [part * part + tiny_square for part in (qkv, proj, up, *downs)]
    weights = [master[...] for master in masters[:3]]
    weights += [masters[3][fold * rows : (fold + 1) * rows, :] for fold in range(folds)]
    columns = [row_sum(square) for square in squares] + [row_sum(part * part) for part in weights]
    message_ref[...] = jnp.zeros_like(message_ref)
    message_ref[:16, :rows] = lane_table(rows, columns).T[:16]
    put_vectors(message_ref, sums)
    col_ref[...] = jnp.zeros_like(col_ref)
    for at, square in enumerate((*squares[:3], added(squares[3:]))):
        col_ref[at : at + 1, : square.shape[1]] = column_sum(square)


def put_vectors(message_ref, sums):
    att_ref, ff_ref, up_ref = sums
    width = att_ref.shape[1]
    count = up_ref.shape[1] // width
    step = 8 + count
    for tile in range(width // 128):
        base = 16 + tile * step
        cols = slice(tile * 128, (tile + 1) * 128)
        message_ref[base : base + 4, :] = att_ref[:4, cols]
        message_ref[base + 4 : base + 7, :] = ff_ref[:3, cols]
        for at in range(count):
            start = at * width + tile * 128
            message_ref[base + 7 + at : base + 8 + at, :] = up_ref[:, start : start + 128]
        message_ref[base + 7 + count : base + 8 + count, :] = ff_ref[3:4, cols]


def row_kernel(widths, qkv_old_ref, proj_old_ref, up_old_ref, down_old_ref, col_ref, *refs):
    parts, (rows_ref, message_ref) = refs[:-2], refs[-2:]
    sums = added([part[...] for part in parts])
    height = rows_ref.shape[0]
    folds = down_old_ref.shape[0] // height
    down_old = down_old_ref[...].reshape(1, folds * height)
    table = jnp.concatenate([sums[:16, :height], jnp.zeros((112, height), jnp.float32)], axis=0).T
    old = jnp.concatenate(
        [
            qkv_old_ref[...].reshape(1, height),
            proj_old_ref[...].reshape(1, height),
            up_old_ref[...].reshape(1, height),
            *[down_old[:, fold * height : (fold + 1) * height] for fold in range(folds)],
            jnp.zeros((128 - 3 - folds, height), jnp.float32),
        ],
        axis=0,
    ).T
    lane = lax.broadcasted_iota(jnp.int32, table.shape, 1)
    share = jnp.ones_like(table)
    for at, size in enumerate(widths):
        share = jnp.where(lane == at, (1.0 - decay_rate) / size, share)
    rows = decay_rate * old + share * table
    rows_ref[...] = rows
    message_ref[:8, :] = col_ref[...]
    message_ref[4:5, :128] = column_sum(rows)
    tiles = message_ref.shape[1] // 128
    step = (sums.shape[0] - 16) // tiles // 4 * 4
    message_ref[8:, :] = jnp.zeros((message_ref.shape[0] - 8, tiles * 128), jnp.float32)
    for tile in range(tiles):
        base = 16 + tile * step
        message_ref[8 : 8 + step, tile * 128 : (tile + 1) * 128] = sums[base : base + step]


def update_kernel(count, heights, widths, *refs):
    messages, refs = refs[:count], refs[count:]
    rows_ref, vectors_ref, moment_ref, refs = refs[0], refs[1], refs[2], refs[3:]
    grads, masters, cols_old, refs = refs[:4], refs[4:8], refs[8:12], refs[12:]
    news, cols_new, refs = refs[:4], refs[4:8], refs[8:]
    rows_out, (vector_grad_ref, moment_new_ref, vector_new_ref) = refs[:4], refs[4:]
    total = added([message[...] for message in messages])
    rows_new = rows_ref[...]
    height = rows_new.shape[0]
    folds = grads[3].shape[0] // height
    across_rows = rows_new.T
    for which in range(3):
        rows_out[which][...] = across_rows[which]
    rows_out[3][...] = jnp.concatenate([across_rows[3 + fold : 4 + fold] for fold in range(folds)], axis=1)[0]
    lanes = [[0], [1], [2], list(range(3, 3 + folds))]
    for which in range(4):
        entries = heights[which] * widths[which]
        cols = cols_old[which].shape[0]
        new = decay_rate * cols_old[which][...].reshape(1, cols) + (1.0 - decay_rate) / heights[which] * total[
            which : which + 1, :cols
        ]
        cols_new[which][...] = new[0]
        mean_rows = sum(total[4:5, lane : lane + 1] for lane in lanes[which]) / heights[which]
        squares = sum(total[4:5, 3 + folds + lane : 4 + folds + lane] for lane in lanes[which])
        rate = step_rate * jnp.sqrt(squares / entries)
        across = new / mean_rows
        for fold, lane in enumerate(lanes[which]):
            part = slice(fold * height, (fold + 1) * height)
            second = rows_new[:, lane : lane + 1] * across
            news[which][part, :] = masters[which][part, :] - rate * grads[which][part, :] * lax.rsqrt(second)
    vectors = vectors_ref[...]
    gradient = total[8 : 8 + vectors.shape[0]]
    vector_grad_ref[...] = gradient
    moment = decay_rate * moment_ref[...] + (1.0 - decay_rate) * (gradient * gradient + tiny_square)
    moment_new_ref[...] = moment
    spread = jnp.sqrt(jnp.mean(vectors * vectors, axis=1, keepdims=True))
    vector_new_ref[...] = vectors - step_rate * spread * gradient * lax.rsqrt(moment)


def packed_body(
    tokens, keep_mask, cotangent, qkv_weight, proj_weight, up_weight, down_weight, vectors,
    qkv_rows, qkv_cols, proj_rows, proj_cols, up_rows, up_cols, down_rows, down_cols, vector_moment,
):
    spread, dp_size = lax.axis_size("group"), lax.axis_size("dp")
    low, high = jnp.bfloat16, jnp.float32
    place = linear_place().astype(jnp.int32).reshape(1)
    group = lax.axis_index("group")
    held, slots, width = tokens.shape
    images, length = keep_mask.shape
    hidden = up_weight.shape[1] * spread
    total = images * length
    rows = qkv_weight.shape[0]
    folds = down_weight.shape[0] // rows
    core_bits = (1,)
    near_bits = tuple(1 << at for at in range(1, spread.bit_length()))
    far_bits = tuple(spread << at for at in range(1, dp_size.bit_length() - 1))
    half = spread * dp_size // 2

    anywhere = pl.BlockSpec(memory_space=pl.ANY)
    in_smem = pl.BlockSpec(memory_space=pltpu.SMEM)

    parted = jax.ShapeDtypeStruct((spread, slots, images, width), low)

    def to_images(parts):
        arrived = lax.all_to_all(parts, "group", split_axis=0, concat_axis=0, tiled=True)
        return arrived.reshape(total, width)

    def exchange(parts):
        return [parts[0]] + [permute(part, relative) for relative, part in enumerate(parts) if relative]

    def settle(parts):
        parts = [part.reshape(slots, images, width) for part in parts]
        whole = pl.pallas_call(
            functools.partial(settle_kernel, spread),
            in_specs=[in_smem] + [anywhere] * spread,
            out_specs=anywhere,
            out_shape=jax.ShapeDtypeStruct((slots, held, width), low),
            scratch_shapes=[pltpu.SemaphoreType.DMA((spread,))],
        )(place, *parts)
        return whole.transpose(1, 0, 2)

    in_vmem = pl.BlockSpec(memory_space=pltpu.VMEM)
    small = functools.partial(
        pl.pallas_call, compiler_params=pltpu.CompilerParams(vmem_limit_bytes=vmem_bytes)
    )
    masters = (qkv_weight, proj_weight, up_weight, down_weight)
    first_cols = qkv_weight.shape[1] + proj_weight.shape[1]
    second_cols = up_weight.shape[1] + folds * down_weight.shape[1]
    token_cut, first_pack, second_pack = small(
        functools.partial(front_kernel, spread),
        in_specs=[anywhere] + [in_vmem] * 4,
        out_specs=[anywhere, in_vmem, in_vmem],
        out_shape=[
            parted,
            jax.ShapeDtypeStruct((rows, first_cols), low),
            jax.ShapeDtypeStruct((rows, second_cols), low),
        ],
        scratch_shapes=[pltpu.SemaphoreType.DMA((spread,))],
    )(tokens.transpose(1, 0, 2), *masters)
    inputs = to_images(token_cut)
    first_blocks = gather_packed(first_pack, far_bits, [near_bits, core_bits])
    cotangent_cut = small(
        functools.partial(cut_kernel, spread),
        in_specs=[anywhere],
        out_specs=anywhere,
        out_shape=parted,
        scratch_shapes=[pltpu.SemaphoreType.DMA((spread,))],
    )(cotangent.transpose(1, 0, 2))
    upstream = to_images(cotangent_cut)
    second_blocks = gather_packed(
        second_pack, far_bits, [(bit,) for bit in near_bits] + [core_bits]
    )
    step_rows = PER_STEP * length
    block = (step_rows, width)
    pairs = width // (2 * HEAD_DIM)
    steps = images // PER_STEP
    statics = (images, dp_size, spread)
    wide = scratch(width // 128, total, 128)
    probs_block = (PER_STEP, pairs, length, 2 * length)
    x, qkv, probs, attended, middle, w_qkv, w_proj = call_kernel(
        attention_packed_kernel, statics, steps,
        ["place"] + [None] * (2 * spread + 3),
        [
            ((total, width), low, block),
            ((total, 3 * width), low, (step_rows, 3 * width)),
            ((images, *probs_block[1:]), low, probs_block),
            ((total, width), low, block),
            ((total, width), high, block),
            ((width, 3 * width), low, None),
            ((width, width), low, None),
        ],
        [
            scratch(dp_size * spread, *first_pack.shape, dtype=low),
            scratch(length, images),
            wide,
            scratch(step_rows, width, dtype=low),
        ],
        (place, inputs, *first_blocks, keep_mask, vectors),
        2 * total * width * 4 * width + 8 * total * length * width,
    )
    piece = ((slots * images, width), low, None)
    pack_cols = up_weight.shape[1] + (folds + 1) * proj_weight.shape[1]
    results = call_kernel(
        feed_forward_packed_kernel, statics, steps,
        ["place"] + [None] * (2 * spread + 1) + [block, block] + [None] * 2,
        [piece] * spread
        + [
            ((total, width), high, block),
            ((total, width), low, block),
            ((half, rows, pack_cols), low, None),
            ((half, rows, pack_cols), low, None),
            ((8, width), high, None),
            ((1, hidden), high, None),
        ],
        [
            scratch(width, hidden, dtype=low),
            scratch(hidden, width, dtype=low),
            scratch(hidden, width, dtype=low),
            scratch(dp_size * spread, *second_pack.shape, dtype=low),
            scratch(1, hidden),
            wide,
            scratch(step_rows, width, dtype=low),
            scratch(width, step_rows, dtype=low),
            scratch(step_rows, width, dtype=low),
            scratch(width, step_rows, dtype=low),
            scratch(step_rows, width),
            scratch(step_rows, 128),
            scratch(step_rows, width),
            scratch(step_rows, width),
            scratch(width, hidden),
            scratch(width, hidden),
            scratch(width, width),
        ],
        (
            place, upstream, *second_blocks, middle, attended, w_proj, vectors,
        ),
        12 * total * width * hidden + 4 * total * width * width, total * hidden,
    )
    output_parts = exchange(results[:spread])
    d_middle, d_attended, ff_keep, ff_leave, ff_sums, up_sums = results[spread:]

    def add_parts(count, keep, arrived, awaited):
        part = (keep.shape[0] // count, *keep.shape[1:])
        return small(
            functools.partial(add_kernel, count),
            in_specs=[in_vmem] * 2 + [anywhere] * len(awaited),
            out_specs=[in_vmem] * count,
            out_shape=[jax.ShapeDtypeStruct(part, high)]
            + [jax.ShapeDtypeStruct(part, low)] * (count - 1),
        )(keep, arrived, *awaited)

    ff_first = permute(ff_leave, core_bits[0])
    ff_count = half // 2
    ff_next = add_wide(ff_keep[ff_count:], ff_first[ff_count:]).astype(low)
    ff_arrived = permute(ff_next, near_bits[-1])
    results = call_kernel(
        attention_back_packed_kernel, statics, steps,
        ["place", block, (step_rows, 3 * width), probs_block, block, block, None, None, "await"],
        [piece] * spread
        + [
            ((half, rows, qkv_weight.shape[1]), low, None),
            ((half, rows, qkv_weight.shape[1]), low, None),
            ((8, width), high, None),
        ],
        [
            wide,
            scratch(step_rows, width, dtype=low),
            scratch(step_rows, 3 * width, dtype=low),
            scratch(step_rows, width),
            scratch(width, 3 * width),
        ],
        (place, x, qkv, probs, d_attended, d_middle, w_qkv, vectors, ff_next),
        4 * total * width * 3 * width + 16 * total * length * width,
    )
    qkv_keep, qkv_leave, att_sums = results[spread:]
    qkv_arrived = permute(qkv_leave, core_bits[0])
    input_parts = exchange(results[:spread])
    qkv_held, *leaving = add_parts(4, qkv_keep, qkv_arrived, output_parts[1:])
    qkv_parts = [permute(part, mask) for part, mask in zip(leaving, direct_masks(near_bits))]
    ff_held = add_wide(ff_keep[:ff_count], ff_first[:ff_count], ff_arrived)
    ff_held, ff_parts = scatter_step(ff_held, near_bits[:-1])
    ff_held = add_wide(ff_held, *ff_parts)
    qkv_held = add_wide(qkv_held, *qkv_parts)
    blocks, block_parts = scatter_step(jnp.concatenate([ff_held, qkv_held], axis=2), far_bits)
    block_parts = [blocks] + block_parts

    heights = [master.shape[0] * dp_size for master in masters]
    widths = [master.shape[1] * spread for master in masters]
    message_rows = -(-(16 + width // 128 * vectors.shape[0]) // 8) * 8
    *grads, message, col_part = small(
        functools.partial(gradient_kernel, len(block_parts)),
        out_shape=[jax.ShapeDtypeStruct(master.shape, high) for master in masters]
        + [jax.ShapeDtypeStruct((message_rows, 128), high), jax.ShapeDtypeStruct((8, width), high)],
    )(*block_parts, att_sums, ff_sums, up_sums, *masters)
    messages = [message] + [permute(message, mask) for mask in range(1, spread)]
    rows_old = [qkv_rows, proj_rows, up_rows, down_rows]
    rows_new, message = small(
        functools.partial(row_kernel, widths[:3] + widths[3:] * folds),
        out_shape=[
            jax.ShapeDtypeStruct((rows, 128), high),
            jax.ShapeDtypeStruct((24, width), high),
        ],
    )(*rows_old, col_part, *messages)
    message = message + permute(message, near_bits[-1])
    messages = [message] + [permute(message, mask) for mask in direct_masks(far_bits)]
    cols_old = [qkv_cols, proj_cols, up_cols, down_cols]
    results = small(
        functools.partial(update_kernel, len(messages), heights, widths),
        out_shape=[jax.ShapeDtypeStruct(master.shape, high) for master in masters]
        + [jax.ShapeDtypeStruct(part.shape, high) for part in cols_old]
        + [jax.ShapeDtypeStruct(part.shape, high) for part in (qkv_rows, proj_rows, up_rows, down_rows)]
        + [jax.ShapeDtypeStruct(vectors.shape, high)] * 3,
    )(*messages, rows_new, vectors, vector_moment, *grads, *masters, *cols_old)
    news, cols_new, rows_out = results[:4], results[4:8], results[8:12]
    vector_grad, vector_moment_new, vector_new = results[12:]
    factored = []
    for which in range(4):
        factored += [grads[which], rows_out[which], cols_new[which], news[which]]
    return (settle(output_parts), settle(input_parts), *factored, vector_grad, vector_moment_new, vector_new)


def body(*arrays):
    spread, dp_size = lax.axis_size("group"), lax.axis_size("dp")
    rows, images = arrays[3].shape[0], arrays[1].shape[0]
    slots, width = arrays[0].shape[1:]
    folds = arrays[6].shape[0] // rows
    powers = all(size & (size - 1) == 0 for size in (spread, dp_size))
    fits = powers and spread == 4 and dp_size > 2
    fits = fits and arrays[5].shape[1] <= width and folds <= 5
    fits = fits and rows % 16 == 0 and images % 16 == 0 and slots % 4 == 0
    return packed_body(*arrays) if fits else general_body(*arrays)


def solution(mesh):
    in_specs = (
        P("dp", "group", None),
        P(("dp", "group"), None),
        P("dp", "group", None),
        P("dp", "group"),
        P("dp", "group"),
        P("dp", "group"),
        P("dp", "group"),
        P(),
        P("dp"),
        P("group"),
        P("dp"),
        P("group"),
        P("dp"),
        P("group"),
        P("dp"),
        P("group"),
        P(),
    )
    out_specs = (
        P("dp", "group", None),
        P("dp", "group", None),
        P("dp", "group"),
        P("dp"),
        P("group"),
        P("dp", "group"),
        P("dp", "group"),
        P("dp"),
        P("group"),
        P("dp", "group"),
        P("dp", "group"),
        P("dp"),
        P("group"),
        P("dp", "group"),
        P("dp", "group"),
        P("dp"),
        P("group"),
        P("dp", "group"),
        P(),
        P(),
        P(),
    )
    return jax.shard_map(body, mesh=mesh, in_specs=in_specs, out_specs=out_specs, check_vma=False)
```

```python
import functools
import math

import jax
import jax.numpy as jnp
from jax import lax
from jax.experimental import pallas as pl
from jax.experimental.pallas import tpu as pltpu
from jax.sharding import PartitionSpec as P

HEAD_DIM = 64
STEP_NUMBER = 10


step_rate = 0.3
norm_epsilon = 1e-06
tiny_square = 1e-30
decay_rate = 1.0 - STEP_NUMBER ** (-0.8)
LOG2_E = 1.4426950408889634


def axis_bits(name):
    count = lax.axis_size(name)
    return [(name, 1 << place) for place in range(count.bit_length() - 1)]


def swap_partner(array, step):
    name, bit = step
    count = lax.axis_size(name)
    return lax.ppermute(array, name, [(rank, rank ^ bit) for rank in range(count)])


def upper_side(step):
    name, bit = step
    return (lax.axis_index(name) & bit) != 0


def gather_blocks(array, steps):
    for step in steps:
        arrived = swap_partner(array, step)
        upper = upper_side(step)
        array = jnp.stack([jnp.where(upper, arrived, array), jnp.where(upper, array, arrived)])
    return array


def scatter_sum(array, steps):
    for step in steps:
        upper = upper_side(step)
        leaving = jnp.where(upper, array[0], array[1]).astype(jnp.bfloat16)
        arrived = swap_partner(leaving, step)
        array = jnp.where(upper, array[1], array[0]).astype(jnp.float32) + arrived.astype(jnp.float32)
    return array


def sum_everywhere(array, steps):
    for step in steps:
        array = array + swap_partner(array, step)
    return array


def sum_parts(parts, steps):
    flat = [part.reshape(-1) for part in parts]
    total = sum_everywhere(jnp.concatenate(flat), steps)
    result, start = [], 0
    for part in parts:
        result.append(total[start : start + part.size].reshape(part.shape))
        start += part.size
    return result


def block_order(steps):
    order = []
    for name in ("dp", "group"):
        bits = sorted((step for step in steps if step[0] == name), key=lambda step: -step[1])
        order.append([steps.index(step) for step in bits])
    return order


def blocks_to_whole(blocks, steps):
    count = len(steps)
    rows, cols = blocks.shape[count:]
    dp_axes, group_axes = block_order(steps)
    dp_axes = [count - 1 - axis for axis in dp_axes]
    group_axes = [count - 1 - axis for axis in group_axes]
    whole = blocks.transpose(dp_axes + [count] + group_axes + [count + 1])
    return whole.reshape(rows << len(dp_axes), cols << len(group_axes))


def whole_to_blocks(whole, steps):
    dp_axes, group_axes = block_order(steps)
    rows = whole.shape[0] >> len(dp_axes)
    cols = whole.shape[1] >> len(group_axes)
    split = whole.reshape([2] * len(dp_axes) + [rows] + [2] * len(group_axes) + [cols])
    places = dp_axes + [len(steps)] + group_axes + [len(steps) + 1]
    return split.transpose([places.index(axis) for axis in range(len(places))])


PER_STEP = 4
FF_CHUNK = 256
vmem_bytes = 60 * 1024 * 1024


def dot(left, right, left_axis=1, right_axis=0):
    return lax.dot_general(
        left, right, (((left_axis,), (right_axis,)), ((), ())), preferred_element_type=jnp.float32
    )


def normal_form(values):
    center = jnp.mean(values, axis=-1, keepdims=True)
    centered = values - center
    spread = jnp.mean(centered * centered, axis=-1, keepdims=True)
    scale = lax.rsqrt(spread + norm_epsilon)
    return centered * scale, scale


def norm_back(grad, unit, scale, gain):
    weighted = grad * gain
    along = jnp.mean(weighted * unit, axis=-1, keepdims=True)
    level = jnp.mean(weighted, axis=-1, keepdims=True)
    return scale * (weighted - level - unit * along)


def column_sum(values):
    return jnp.sum(values, axis=0, keepdims=True)


def pair_mask(length):
    return lax.broadcasted_iota(jnp.int32, (length, 2 * HEAD_DIM), 1) < HEAD_DIM


def stack_heads(pair, first):
    none = jnp.zeros_like(pair)
    return jnp.concatenate([jnp.where(first, pair, none), jnp.where(first, none, pair)], axis=0)


def join_heads(rows, first):
    length = rows.shape[0] // 2
    return jnp.where(first, rows[:length], rows[length:])


def gelu_and_slope(pre):
    bell = jnp.exp2(pre * pre * (-0.5 * LOG2_E))
    inverse = 1.0 / (1.0 + (0.3275911 * 0.5**0.5) * jnp.abs(pre))
    poly = inverse * (
        0.5 * 0.254829592
        + inverse
        * (
            0.5 * -0.284496736
            + inverse
            * (0.5 * 1.421413741 + inverse * (0.5 * -1.453152027 + inverse * (0.5 * 1.061405429)))
        )
    )
    tail = poly * bell
    below = jnp.where(pre >= 0, 1.0 - tail, tail)
    return pre * below, below + pre * bell * 0.3989422804014327


def widen(source_ref, wide_ref, images):
    tiles, total, lanes = wide_ref.shape
    rows_at_once = 8 * images

    @pl.loop(0, total // rows_at_once)
    def _(part):
        rows = pl.ds(pl.multiple_of(part * rows_at_once, rows_at_once), rows_at_once)
        for tile in range(tiles):
            cols = slice(tile * lanes, (tile + 1) * lanes)
            wide_ref[tile, rows, :] = source_ref[rows, cols].astype(jnp.float32)


def narrow(wide_ref, target_ref, images):
    tiles, total, lanes = wide_ref.shape
    rows_at_once = 8 * images

    @pl.loop(0, total // rows_at_once)
    def _(part):
        rows = pl.ds(pl.multiple_of(part * rows_at_once, rows_at_once), rows_at_once)
        for tile in range(tiles):
            cols = slice(tile * lanes, (tile + 1) * lanes)
            target_ref[rows, cols] = wide_ref[tile, rows, :].astype(target_ref.dtype)


def take_image(wide_ref, image, images):
    tiles, total, _ = wide_ref.shape
    rows = pl.ds(image, total // images, images)
    return jnp.concatenate([wide_ref[tile, rows, :] for tile in range(tiles)], axis=1)


def put_image(wide_ref, image, images, values):
    tiles, total, lanes = wide_ref.shape
    rows = pl.ds(image, total // images, images)
    for tile in range(tiles):
        wide_ref[tile, rows, :] = values[:, tile * lanes : (tile + 1) * lanes]


def attention_kernel(
    images, tokens_ref, bias_ref, w_qkv_ref, w_proj_ref, vectors_ref,
    x_ref, qkv_ref, probs_ref, attended_ref, middle_ref, wide_ref, normed_ref,
):
    @pl.when(pl.program_id(0) == 0)
    def _():
        widen(tokens_ref, wide_ref, images)
        to_image_rows(wide_ref, x_ref, images)

    attention_steps(
        x_ref, lambda image: bias_ref[image], w_qkv_ref, w_proj_ref, vectors_ref,
        qkv_ref, probs_ref, attended_ref, middle_ref, normed_ref,
    )


def to_image_rows(wide_ref, x_ref, images):
    length = wide_ref.shape[1] // images

    @pl.loop(0, images)
    def _(image):
        rows = pl.ds(pl.multiple_of(image * length, length), length)
        x_ref[rows, :] = take_image(wide_ref, image, images).astype(jnp.bfloat16)


def attention_steps(
    x_ref, bias_column, w_qkv_ref, w_proj_ref, vectors_ref,
    qkv_ref, probs_ref, attended_ref, middle_ref, normed_ref,
):
    per_step, _, length, _ = probs_ref.shape
    step_rows, width = middle_ref.shape
    base = 0 if x_ref.shape[0] == step_rows else pl.program_id(0) * step_rows

    for image in range(per_step):
        rows = slice(image * length, (image + 1) * length)
        x = x_ref[pl.ds(pl.multiple_of(base + image * length, length), length), :].astype(jnp.float32)
        unit, _ = normal_form(x)
        normed_ref[rows, :] = (unit * vectors_ref[0:1] + vectors_ref[1:2]).astype(jnp.bfloat16)
    for part in range(3):
        cols = slice(part * width, (part + 1) * width)
        projected = dot(normed_ref[...], w_qkv_ref[:, cols])
        if part != 1:
            row = 2 if part == 0 else 3
            projected = projected + vectors_ref[row : row + 1]
        qkv_ref[:, cols] = projected.astype(jnp.bfloat16)

    @pl.loop(0, per_step)
    def _(image):
        rows = pl.ds(pl.multiple_of(image * length, length), length)
        first = pair_mask(length)
        place = lax.broadcasted_iota(jnp.int32, (length, 2 * length), 0)
        asker = lax.broadcasted_iota(jnp.int32, (length, 2 * length), 1)
        asker = jnp.where(asker >= length, asker - length, asker)
        bias = jnp.where(place == asker, 0.0, bias_column(image))
        for pair in range(width // (2 * HEAD_DIM)):
            low = pair * 2 * HEAD_DIM
            queries = stack_heads(qkv_ref[rows, low : low + 2 * HEAD_DIM], first)
            keys = qkv_ref[rows, width + low : width + low + 2 * HEAD_DIM]
            values = qkv_ref[rows, 2 * width + low : 2 * width + low + 2 * HEAD_DIM]
            scores = dot(keys, queries, 1, 1) * (HEAD_DIM**-0.5 * LOG2_E) + bias
            weights = jnp.exp2(scores - jnp.max(scores, axis=0, keepdims=True))
            probs = weights * (1.0 / jnp.sum(weights, axis=0, keepdims=True))
            probs = probs.astype(jnp.bfloat16)
            probs_ref[image, pair] = probs
            attended = join_heads(dot(probs, values, 0, 0), first)
            attended_ref[rows, low : low + 2 * HEAD_DIM] = attended.astype(jnp.bfloat16)

    middle_ref[...] = (
        x_ref[pl.ds(pl.multiple_of(base, length), step_rows), :].astype(jnp.float32)
        + dot(attended_ref[...], w_proj_ref[...])
        + vectors_ref[4:5]
    )


def feed_forward_kernel(
    images, middle_ref, cotangent_ref, attended_ref, w_up_ref, w_down_ref, w_proj_ref, vectors_ref, bias_up_ref,
    output_ref, d_middle_ref, d_attended_ref, up_grad_ref, down_grad_ref, proj_grad_ref, vector_sums_ref, up_sums_ref,
    wide_ref, *scratches,
):
    up_total_ref, down_total_ref, proj_total_ref = scratches[-3:]

    @pl.when(pl.program_id(0) == 0)
    def _():
        widen(cotangent_ref, wide_ref, images)

    feed_forward_steps(
        images, middle_ref, attended_ref, w_up_ref, w_down_ref, w_proj_ref, vectors_ref, bias_up_ref,
        d_middle_ref, d_attended_ref, vector_sums_ref, up_sums_ref, wide_ref, *scratches,
    )

    @pl.when(pl.program_id(0) == pl.num_programs(0) - 1)
    def _():
        narrow(wide_ref, output_ref, images)
        up_grad_ref[...] = up_total_ref[...].astype(jnp.bfloat16)
        down_grad_ref[...] = down_total_ref[...].T.astype(jnp.bfloat16)
        proj_grad_ref[...] = proj_total_ref[...].astype(jnp.bfloat16)


def feed_forward_steps(
    images, middle_ref, attended_ref, w_up_ref, w_down_ref, w_proj_ref, vectors_ref, bias_up_ref,
    d_middle_ref, d_attended_ref, vector_sums_ref, up_sums_ref,
    wide_ref, normed_ref, normed_t_ref, dy_ref, dy_t_ref, unit_ref, scale_ref, ahead_ref, back_ref,
    up_total_ref, down_total_ref, proj_total_ref,
):
    step = pl.program_id(0)
    length = wide_ref.shape[1] // images
    hidden = w_up_ref.shape[1]
    per_step = middle_ref.shape[0] // length

    @pl.when(step == 0)
    def _():
        for total in (up_total_ref, down_total_ref, proj_total_ref, vector_sums_ref, up_sums_ref):
            total[...] = jnp.zeros_like(total)

    for image in range(per_step):
        rows = slice(image * length, (image + 1) * length)
        dy = take_image(wide_ref, step * per_step + image, images)
        dy_ref[rows, :] = dy.astype(jnp.bfloat16)
        vector_sums_ref[3:4] += column_sum(dy)
        unit, scale = normal_form(middle_ref[rows, :])
        unit_ref[rows, :] = unit
        scale_ref[rows, :] = jnp.broadcast_to(scale, (length, scale_ref.shape[1]))
        normed_ref[rows, :] = (unit * vectors_ref[5:6] + vectors_ref[6:7]).astype(jnp.bfloat16)
    normed_t_ref[...] = normed_ref[...].T
    dy_t_ref[...] = dy_ref[...].T
    ahead_ref[...] = jnp.zeros_like(ahead_ref)
    back_ref[...] = jnp.zeros_like(back_ref)

    @pl.loop(0, hidden // FF_CHUNK)
    def _(chunk):
        cols = pl.ds(pl.multiple_of(chunk * FF_CHUNK, FF_CHUNK), FF_CHUNK)
        w_up = w_up_ref[:, cols]
        w_down = w_down_ref[cols, :]
        active, slope = gelu_and_slope(dot(normed_ref[...], w_up) + bias_up_ref[:, cols])
        active = active.astype(jnp.bfloat16)
        d_hidden = dot(dy_ref[...], w_down, 1, 1) * slope
        d_hidden = d_hidden.astype(jnp.bfloat16)
        ahead_ref[...] += dot(active, w_down)
        back_ref[...] += dot(d_hidden, w_up, 1, 1)
        down_total_ref[:, cols] += dot(dy_t_ref[...], active)
        up_total_ref[:, cols] += dot(normed_t_ref[...], d_hidden)
        up_sums_ref[:, cols] += column_sum(d_hidden.astype(jnp.float32))

    for image in range(per_step):
        rows = slice(image * length, (image + 1) * length)
        output = middle_ref[rows, :] + ahead_ref[rows, :] + vectors_ref[11:12]
        put_image(wide_ref, step * per_step + image, images, output)
        unit = unit_ref[rows, :]
        grad = back_ref[rows, :]
        vector_sums_ref[1:2] += column_sum(grad * unit)
        vector_sums_ref[2:3] += column_sum(grad)
        d_middle = dy_ref[rows, :].astype(jnp.float32) + norm_back(
            grad, unit, scale_ref[rows, 0:1], vectors_ref[5:6]
        )
        d_middle_ref[rows, :] = d_middle
        d_branch = d_middle.astype(jnp.bfloat16)
        dy_ref[rows, :] = d_branch
        vector_sums_ref[0:1] += column_sum(d_branch.astype(jnp.float32))
    proj_total_ref[...] += dot(attended_ref[...], dy_ref[...], 0, 0)
    d_attended_ref[...] = dot(dy_ref[...], w_proj_ref[...], 1, 1).astype(jnp.bfloat16)


def attention_back_kernel(
    images, x_ref, qkv_ref, probs_ref, d_attended_ref, d_middle_ref, w_qkv_ref, vectors_ref,
    input_grad_ref, qkv_grad_ref, vector_sums_ref, wide_ref, *scratches,
):
    @pl.when(pl.program_id(0) == 0)
    def _():
        scratches[-1][...] = jnp.zeros_like(scratches[-1])
        vector_sums_ref[...] = jnp.zeros_like(vector_sums_ref)

    attention_back_steps(
        images, x_ref, qkv_ref, probs_ref, d_attended_ref, d_middle_ref, w_qkv_ref, vectors_ref,
        vector_sums_ref, wide_ref, *scratches,
    )

    @pl.when(pl.program_id(0) == pl.num_programs(0) - 1)
    def _():
        narrow(wide_ref, input_grad_ref, images)
        qkv_grad_ref[...] = scratches[-1][...].astype(jnp.bfloat16)


def attention_back_steps(
    images, x_ref, qkv_ref, probs_ref, d_attended_ref, d_middle_ref, w_qkv_ref, vectors_ref,
    vector_sums_ref, wide_ref, normed_ref, d_projected_ref, back_ref, qkv_total_ref,
):
    step = pl.program_id(0)
    width = x_ref.shape[1]
    length = probs_ref.shape[2]
    per_step = probs_ref.shape[0]

    @pl.loop(0, per_step)
    def _(image):
        rows = pl.ds(pl.multiple_of(image * length, length), length)
        first = pair_mask(length)
        for pair in range(width // (2 * HEAD_DIM)):
            low = pair * 2 * HEAD_DIM
            cols = [slice(part * width + low, part * width + low + 2 * HEAD_DIM) for part in range(3)]
            queries = stack_heads(qkv_ref[rows, cols[0]], first)
            keys = qkv_ref[rows, cols[1]]
            values = qkv_ref[rows, cols[2]]
            probs = probs_ref[image, pair]
            d_attended = stack_heads(d_attended_ref[rows, cols[0]], first)
            d_projected_ref[rows, cols[2]] = dot(probs, d_attended).astype(jnp.bfloat16)
            d_probs = dot(values, d_attended, 1, 1)
            probs = probs.astype(jnp.float32)
            along = jnp.sum(d_probs * probs, axis=0, keepdims=True)
            d_scores = (probs * (d_probs - along)).astype(jnp.bfloat16)
            scale = HEAD_DIM**-0.5
            d_queries = join_heads(dot(d_scores, keys, 0, 0), first) * scale
            d_projected_ref[rows, cols[0]] = d_queries.astype(jnp.bfloat16)
            d_projected_ref[rows, cols[1]] = (dot(d_scores, queries) * scale).astype(jnp.bfloat16)

    vector_sums_ref[2:3] += column_sum(d_projected_ref[:, :width].astype(jnp.float32))
    vector_sums_ref[3:4] += column_sum(d_projected_ref[:, 2 * width :].astype(jnp.float32))
    back_ref[...] = dot(d_projected_ref[...], w_qkv_ref[...], 1, 1)
    for image in range(per_step):
        rows = slice(image * length, (image + 1) * length)
        unit, scale = normal_form(x_ref[rows, :].astype(jnp.float32))
        normed_ref[rows, :] = (unit * vectors_ref[0:1] + vectors_ref[1:2]).astype(jnp.bfloat16)
        grad = back_ref[rows, :]
        vector_sums_ref[0:1] += column_sum(grad * unit)
        vector_sums_ref[1:2] += column_sum(grad)
        d_input = d_middle_ref[rows, :] + norm_back(grad, unit, scale, vectors_ref[0:1])
        put_image(wide_ref, step * per_step + image, images, d_input)
    qkv_total_ref[...] += dot(normed_ref[...], d_projected_ref[...], 0, 0)


def whole_block(shape):
    return pl.BlockSpec(shape, lambda step: (0,) * len(shape))


def step_block(shape, first=0):
    return pl.BlockSpec(shape, lambda step: (first + step,) + (0,) * (len(shape) - 1))


def scratch(*shape, dtype=jnp.float32):
    return pltpu.VMEM(shape, dtype)


def call_kernel(kernel, statics, steps, ins, outs, scratches, operands, flops, transcendentals=0, first_step=0, aliases={}):
    in_specs = [
        pl.BlockSpec(memory_space=pltpu.SMEM)
        if block == "place"
        else pl.BlockSpec(memory_space=pl.ANY)
        if block == "await"
        else whole_block(op.shape) if block is None else step_block(block, first_step)
        for op, block in zip(operands, ins)
    ]
    out_specs = [
        whole_block(shape) if block is None else step_block(block, first_step) for shape, dtype, block in outs
    ]
    moved = sum(op.size * op.dtype.itemsize for op in operands) + sum(
        math.prod(shape) * jnp.dtype(dtype).itemsize for shape, dtype, block in outs
    )
    return pl.pallas_call(
        functools.partial(kernel, *statics),
        grid=(steps,),
        in_specs=in_specs,
        out_specs=out_specs,
        out_shape=[jax.ShapeDtypeStruct(shape, dtype) for shape, dtype, block in outs],
        scratch_shapes=scratches,
        input_output_aliases=aliases,
        compiler_params=pltpu.CompilerParams(vmem_limit_bytes=vmem_bytes),
        cost_estimate=pl.CostEstimate(
            flops=flops * 8, bytes_accessed=moved, transcendentals=transcendentals
        ),
    )(*operands)


def attention_forward(tokens, bias, w_qkv, w_proj, vectors):
    images, length, _ = bias.shape
    total, width = tokens.shape
    pairs = width // (2 * HEAD_DIM)
    rows = PER_STEP * length
    low, high = jnp.bfloat16, jnp.float32
    outs = [
        ((total, width), low, None),
        ((total, 3 * width), low, (rows, 3 * width)),
        ((images, pairs, length, 2 * length), low, (PER_STEP, pairs, length, 2 * length)),
        ((total, width), low, (rows, width)),
        ((total, width), high, (rows, width)),
    ]
    return call_kernel(
        attention_kernel, (images,), images // PER_STEP,
        [None, (PER_STEP, length, 1), None, None, None], outs,
        [scratch(width // 128, total, 128), scratch(rows, width, dtype=low)],
        (tokens, bias, w_qkv, w_proj, vectors),
        2 * total * width * 4 * width + 8 * total * length * width,
    )


def feed_forward(images, middle, cotangent, attended, w_up, w_down, w_proj, vectors):
    total, width = middle.shape
    hidden = w_up.shape[1]
    rows = total // images * PER_STEP
    low, high = jnp.bfloat16, jnp.float32
    block = (rows, width)
    outs = [
        ((total, width), low, None),
        ((total, width), high, block),
        ((total, width), low, block),
        ((width, hidden), low, None),
        ((hidden, width), low, None),
        ((width, width), low, None),
        ((8, width), high, None),
        ((1, hidden), high, None),
    ]
    scratches = [
        scratch(width // 128, total, 128),
        scratch(rows, width, dtype=low),
        scratch(width, rows, dtype=low),
        scratch(rows, width, dtype=low),
        scratch(width, rows, dtype=low),
        scratch(rows, width),
        scratch(rows, 128),
        scratch(rows, width),
        scratch(rows, width),
        scratch(width, hidden),
        scratch(width, hidden),
        scratch(width, width),
    ]
    return call_kernel(
        feed_forward_kernel, (images,), images // PER_STEP,
        [block, None, block, None, None, None, None, None], outs, scratches,
        (middle, cotangent, attended, w_up, w_down, w_proj, vectors, vectors[7:11].reshape(1, hidden)),
        12 * total * width * hidden + 4 * total * width * width, total * hidden,
    )


def attention_back(x, qkv, probs, d_attended, d_middle, w_qkv, vectors):
    images, pairs, length, _ = probs.shape
    total, width = x.shape
    rows = PER_STEP * length
    low, high = jnp.bfloat16, jnp.float32
    block = (rows, width)
    outs = [
        ((total, width), low, None),
        ((width, 3 * width), low, None),
        ((8, width), high, None),
    ]
    scratches = [
        scratch(width // 128, total, 128),
        scratch(rows, width, dtype=low),
        scratch(rows, 3 * width, dtype=low),
        scratch(rows, width),
        scratch(width, 3 * width),
    ]
    return call_kernel(
        attention_back_kernel, (images,), images // PER_STEP,
        [block, (rows, 3 * width), (PER_STEP, pairs, length, 2 * length), block, block, None, None],
        outs, scratches, (x, qkv, probs, d_attended, d_middle, w_qkv, vectors),
        4 * total * width * 3 * width + 16 * total * length * width,
    )

def linear_place():
    return lax.axis_index("dp") * lax.axis_size("group") + lax.axis_index("group")


def permute(array, mask):
    count = lax.axis_size("dp") * lax.axis_size("group")
    return lax.ppermute(array, ("dp", "group"), [(rank, rank ^ mask) for rank in range(count)])


def direct_masks(bits):
    masks = [0]
    for bit in bits:
        masks = masks + [mask | bit for mask in masks]
    return masks[1:]


def scatter_step(held, bits):
    masks = direct_masks(bits)
    size = held.shape[0] // (len(masks) + 1)
    parts = [
        permute(held[size * (at + 1) : size * (at + 2)].astype(jnp.bfloat16), mask)
        for at, mask in enumerate(masks)
    ]
    return held[:size], parts


def add_wide(first, *rest):
    total = first.astype(jnp.float32)
    for part in rest:
        total = total + part.astype(jnp.float32)
    return total


def packed_place(mask, spread, count):
    return ((mask >> 1) & (spread - 1)) * (count // (2 * spread)) + (mask >> (spread.bit_length()))


def gather_step(held, bits):
    return held + [permute(part, mask) for mask in direct_masks(bits) for part in held]


def unpack(place_ref, block_refs, packed_ref, put, dp_size, spread):
    place = place_ref[0]
    size = block_refs[0].shape[0]
    for at, block_ref in enumerate(block_refs):
        packed_ref[at * size : (at + 1) * size] = block_ref[...]
    count = dp_size * spread
    for row in range(dp_size):
        for col in range(spread):
            mask = (row * spread + col) ^ place
            at = packed_place(mask, spread, count) + (mask & 1) * (count // 2)
            put(row, col, packed_ref[at])


def pack(place_ref, take, keep_ref, leave_ref, dp_size, spread):
    place = place_ref[0]
    odd = (place & 1) == 1
    for row in range(dp_size):
        for col in range(0, spread, 2):
            at = packed_place((row * spread + col) ^ place, spread, dp_size * spread)
            even_block, odd_block = take(row, col), take(row, col + 1)
            keep_ref[at] = jnp.where(odd, odd_block, even_block)
            leave_ref[at] = jnp.where(odd, even_block, odd_block)


def narrow_pieces(place_ref, wide_ref, piece_refs, spread):
    tiles, _, lanes = wide_ref.shape
    rows_of_piece = piece_refs[0].shape[0]
    step = 64
    group = place_ref[0] & (spread - 1)
    for relative, piece_ref in enumerate(piece_refs):
        base = (group ^ relative) * rows_of_piece

        @pl.loop(0, rows_of_piece // step)
        def _(part):
            target = pl.ds(pl.multiple_of(part * step, step), step)
            source = pl.ds(pl.multiple_of(base + part * step, step), step)
            for tile in range(tiles):
                cols = slice(tile * lanes, (tile + 1) * lanes)
                piece_ref[target, cols] = wide_ref[tile, source, :].astype(jnp.bfloat16)


def general_body(
    tokens,
    keep_mask,
    cotangent,
    qkv_weight,
    proj_weight,
    up_weight,
    down_weight,
    vectors,
    qkv_rows,
    qkv_cols,
    proj_rows,
    proj_cols,
    up_rows,
    up_cols,
    down_rows,
    down_cols,
    vector_moment,
):
    masters = (qkv_weight, proj_weight, up_weight, down_weight)
    lowered = tuple((master.astype(jnp.bfloat16) for master in masters))
    dp_bits, group_bits = axis_bits("dp"), axis_bits("group")
    gather_steps = dp_bits[1:] + group_bits[1:] + dp_bits[:1] + group_bits[:1]
    scatter_steps = gather_steps[::-1]
    w_qkv, w_proj, w_up, w_down = tuple(
        blocks_to_whole(gather_blocks(part, gather_steps), gather_steps) for part in lowered
    )
    spread = lax.axis_size("group")

    def slots_in(array):
        held, slots, width = array.shape
        parts = array.transpose(1, 0, 2).reshape(slots, spread, held // spread, width)
        parts = lax.all_to_all(
            parts.transpose(1, 0, 2, 3), "group", split_axis=0, concat_axis=0, tiled=True
        )
        return parts.reshape(spread * slots * (held // spread), width)

    def slots_out(array):
        held, slots, width = tokens.shape
        parts = array.reshape(spread, slots, held // spread, width)
        parts = lax.all_to_all(parts, "group", split_axis=0, concat_axis=0, tiled=True)
        return parts.transpose(1, 0, 2, 3).reshape(slots, held, width).transpose(1, 0, 2)

    images = keep_mask.shape[0]
    bias = jnp.where(keep_mask > 0, 0.0, -1e30)[:, :, None]
    x, qkv, probs, attended, middle = attention_forward(
        slots_in(tokens), bias, w_qkv, w_proj, vectors
    )
    output, d_middle, d_attended, up_grad, down_grad, proj_grad, ff_sums, up_sums = feed_forward(
        images, middle, slots_in(cotangent), attended, w_up, w_down, w_proj, vectors
    )
    block_output = slots_out(output)
    d_input, qkv_grad, att_sums = attention_back(
        x, qkv, probs, d_attended, d_middle, w_qkv, vectors
    )
    input_grad = slots_out(d_input)
    local_vectors = jnp.concatenate(
        [att_sums[:4], ff_sums[:3], up_sums.reshape(4, -1), ff_sums[3:4]], axis=0
    )
    vector_grad = sum_everywhere(local_vectors, group_bits + dp_bits)
    local_grads = (qkv_grad, proj_grad, up_grad, down_grad)
    owned = tuple(
        scatter_sum(whole_to_blocks(part, scatter_steps), scatter_steps) for part in local_grads
    )
    squares = tuple((gradient * gradient + tiny_square for gradient in owned))
    row_parts = tuple((jnp.sum(square, axis=1) for square in squares)) + tuple(
        (jnp.sum(master * master, axis=1) for master in masters)
    )
    row_sums = sum_parts(row_parts, group_bits)
    rows_old = (qkv_rows, proj_rows, up_rows, down_rows)
    cols_old = (qkv_cols, proj_cols, up_cols, down_cols)
    total_cols = tuple((gradient.shape[1] * lax.axis_size("group") for gradient in owned))
    total_rows = tuple((gradient.shape[0] * lax.axis_size("dp") for gradient in owned))
    rows_new = tuple(
        (
            decay_rate * rows_old[which] + (1.0 - decay_rate) * row_sums[which] / total_cols[which]
            for which in range(4)
        )
    )
    col_parts = (
        tuple((jnp.sum(square, axis=0) for square in squares))
        + tuple((jnp.sum(row_stat) for row_stat in rows_new))
        + tuple((jnp.sum(row_sums[4 + which]) for which in range(4)))
    )
    col_sums = sum_parts(col_parts, dp_bits)
    results = []
    for which in range(4):
        cols_new = (
            decay_rate * cols_old[which] + (1.0 - decay_rate) * col_sums[which] / total_rows[which]
        )
        mean_rows = col_sums[4 + which] / total_rows[which]
        spread = jnp.sqrt(col_sums[8 + which] / (total_rows[which] * total_cols[which]))
        second = rows_new[which][:, None] * cols_new[None, :] / mean_rows
        updated = masters[which] - step_rate * spread * owned[which] * lax.rsqrt(second)
        results.append((owned[which], rows_new[which], cols_new, updated))
    vector_moment_new = decay_rate * vector_moment + (1.0 - decay_rate) * (
        vector_grad * vector_grad + tiny_square
    )
    row_spread = jnp.sqrt(jnp.mean(vectors * vectors, axis=1, keepdims=True))
    vector_new = vectors - step_rate * row_spread * vector_grad * lax.rsqrt(vector_moment_new)
    return (
        block_output,
        input_grad,
        results[0][0],
        results[0][1],
        results[0][2],
        results[0][3],
        results[1][0],
        results[1][1],
        results[1][2],
        results[1][3],
        results[2][0],
        results[2][1],
        results[2][2],
        results[2][3],
        results[3][0],
        results[3][1],
        results[3][2],
        results[3][3],
        vector_grad,
        vector_moment_new,
        vector_new,
    )


def first_attention_kernel(images, dp_size, spread, place_ref, tokens_ref, *refs):
    blocks, refs = refs[: 2 * spread], refs[2 * spread :]
    far, refs = refs[: dp_size // 2], refs[dp_size // 2 :]
    keep_ref, vectors_ref, *outs, x_ref, w_qkv_ref, w_proj_ref, joined_ref = refs[:-4]
    packed_ref, wide_ref, bias_ref, normed_ref = refs[-4:]
    rows = packed_ref.shape[1]
    qkv_cols, proj_cols = w_qkv_ref.shape[1] // spread, w_proj_ref.shape[1] // spread

    @pl.when(pl.program_id(0) == 0)
    def _():
        widen(tokens_ref, wide_ref, images)
        to_image_rows(wide_ref, x_ref, images)

        def put(row, col, block):
            down = slice(row * rows, (row + 1) * rows)
            w_qkv_ref[down, col * qkv_cols : (col + 1) * qkv_cols] = block[:, :qkv_cols]
            w_proj_ref[down, col * proj_cols : (col + 1) * proj_cols] = block[:, qkv_cols:]

        unpack(place_ref, blocks, packed_ref, put, dp_size, spread)
        for at, far_ref in enumerate(far):
            joined_ref[at] = far_ref[0]

    attention_part(0, x_ref, keep_ref, w_qkv_ref, w_proj_ref, vectors_ref, *outs, bias_ref, normed_ref)


def next_attention_kernel(start, x_ref, keep_ref, w_qkv_ref, w_proj_ref, vectors_ref, *refs):
    attention_part(start, x_ref, keep_ref, w_qkv_ref, w_proj_ref, vectors_ref, *refs[-6:])


def attention_part(
    start, x_ref, keep_ref, w_qkv_ref, w_proj_ref, vectors_ref,
    qkv_ref, probs_ref, attended_ref, middle_ref, bias_ref, normed_ref,
):
    @pl.when(pl.program_id(0) == 0)
    def _():
        bias_ref[...] = jnp.where(keep_ref[...] > 0, 0.0, -1e30).T

    def bias_column(image):
        here = start + pl.program_id(0) * probs_ref.shape[0] + image
        lane = lax.broadcasted_iota(jnp.int32, bias_ref.shape, 1)
        return row_sum(jnp.where(lane == here, bias_ref[...], 0.0))

    attention_steps(
        x_ref, bias_column, w_qkv_ref, w_proj_ref, vectors_ref,
        qkv_ref, probs_ref, attended_ref, middle_ref, normed_ref,
    )


def feed_forward_packed_kernel(images, dp_size, spread, place_ref, *refs):
    cotangent_ref, blocks, refs = refs[0], refs[1 : 1 + 2 * spread], refs[1 + 2 * spread :]
    middle_ref, attended_ref, w_proj_ref, vectors_ref, output_ref = refs[:5]
    refs = refs[5:]
    d_middle_ref, d_attended_ref, keep_ref, leave_ref, vector_sums_ref, up_sums_ref = refs[:6]
    w_up_ref, w_down_ref, down_low_ref, packed_ref, bias_up_ref, wide_ref = refs[6:12]
    scratches = refs[12:]
    width = w_up_ref.shape[0]
    up_total_ref, down_total_ref, proj_total_ref = scratches[-3:]
    rows = packed_ref.shape[1]
    up_cols = w_up_ref.shape[1] // spread
    out_cols = w_down_ref.shape[1] // spread
    folds = w_down_ref.shape[0] // w_up_ref.shape[0]

    @pl.when(pl.program_id(0) == 0)
    def _():
        widen(cotangent_ref, wide_ref, images)
        for fold in range(bias_up_ref.shape[1] // width):
            bias_up_ref[:, fold * width : (fold + 1) * width] = vectors_ref[7 + fold : 8 + fold]

        def put(row, col, block):
            w_up_ref[row * rows : (row + 1) * rows, col * up_cols : (col + 1) * up_cols] = block[:, :up_cols]
            for fold in range(folds):
                down = (row * folds + fold) * rows
                start = up_cols + fold * out_cols
                w_down_ref[down : down + rows, col * out_cols : (col + 1) * out_cols] = block[
                    :, start : start + out_cols
                ]

        unpack(place_ref, blocks, packed_ref, put, dp_size, spread)

    feed_forward_steps(
        images, middle_ref, attended_ref, w_up_ref, w_down_ref, w_proj_ref, vectors_ref, bias_up_ref,
        d_middle_ref, d_attended_ref, vector_sums_ref, up_sums_ref, wide_ref, *scratches,
    )

    @pl.when(pl.program_id(0) == pl.num_programs(0) - 1)
    def _():
        narrow(wide_ref, output_ref, images)
        down_low_ref[...] = down_total_ref[...].T.astype(jnp.bfloat16)

        def take(row, col):
            across = slice(row * rows, (row + 1) * rows)
            cols = slice(col * out_cols, (col + 1) * out_cols)
            parts = [up_total_ref[across, col * up_cols : (col + 1) * up_cols].astype(jnp.bfloat16)]
            for fold in range(folds):
                down = (row * folds + fold) * rows
                parts.append(down_low_ref[down : down + rows, cols])
            parts.append(proj_total_ref[across, cols].astype(jnp.bfloat16))
            return jnp.concatenate(parts, axis=1)

        pack(place_ref, take, keep_ref, leave_ref, dp_size, spread)


def attention_back_packed_kernel(
    images, dp_size, spread, place_ref, x_ref, qkv_ref, probs_ref, d_attended_ref, d_middle_ref, w_qkv_ref,
    vectors_ref, *refs,
):
    refs = refs[spread - 1 :]
    pieces, (keep_ref, leave_ref, vector_sums_ref, wide_ref, *scratches) = refs[:spread], refs[spread:]
    total_ref = scratches[-1]

    @pl.when(pl.program_id(0) == 0)
    def _():
        total_ref[...] = jnp.zeros_like(total_ref)
        vector_sums_ref[...] = jnp.zeros_like(vector_sums_ref)

    attention_back_steps(
        images, x_ref, qkv_ref, probs_ref, d_attended_ref, d_middle_ref, w_qkv_ref, vectors_ref,
        vector_sums_ref, wide_ref, *scratches,
    )

    @pl.when(pl.program_id(0) == pl.num_programs(0) - 1)
    def _():
        narrow_pieces(place_ref, wide_ref, pieces, spread)
        rows, cols = keep_ref.shape[1:]

        def take(row, col):
            block = total_ref[row * rows : (row + 1) * rows, col * cols : (col + 1) * cols]
            return block.astype(jnp.bfloat16)

        pack(place_ref, take, keep_ref, leave_ref, dp_size, spread)


def cut(array_ref, parts_ref):
    count = parts_ref.shape[2]
    for member in range(parts_ref.shape[0]):
        parts_ref[member] = array_ref[:, member * count : (member + 1) * count, :]


def front_kernel(array_ref, qkv_ref, proj_ref, parts_ref, pack_ref):
    start = qkv_ref.shape[1]
    pack_ref[:, :start] = qkv_ref[...].astype(jnp.bfloat16)
    pack_ref[:, start:] = proj_ref[...].astype(jnp.bfloat16)
    cut(array_ref, parts_ref)


def second_front_kernel(array_ref, up_ref, down_ref, _, parts_ref, pack_ref):
    rows, start, count = pack_ref.shape[0], up_ref.shape[1], down_ref.shape[1]
    pack_ref[:, :start] = up_ref[...].astype(jnp.bfloat16)
    for fold in range(down_ref.shape[0] // rows):
        at = start + fold * count
        pack_ref[:, at : at + count] = down_ref[fold * rows : (fold + 1) * rows, :].astype(jnp.bfloat16)
    cut(array_ref, parts_ref)


def settle_whole_kernel(parts_ref, output_ref):
    count = parts_ref.shape[2]
    for member in range(parts_ref.shape[0]):
        output_ref[:, member * count : (member + 1) * count, :] = parts_ref[member]


def settle_kernel(spread, place_ref, *refs):
    lists, output_ref = refs[:-1], refs[-1]
    group = place_ref[0] & (spread - 1)
    count = lists[0].shape[1]
    share = len(lists) // spread * count
    for at, piece_ref in enumerate(lists):
        relative, part = at % spread, at // spread
        start = pl.multiple_of((group ^ relative) * share + part * count, count)
        output_ref[:, pl.ds(start, count), :] = piece_ref[...]


def lane_table(rows, columns):
    lane = lax.broadcasted_iota(jnp.int32, (rows, 128), 1)
    table = jnp.zeros((rows, 128), jnp.float32)
    for at, column in enumerate(columns):
        table = jnp.where(lane == at, column, table)
    return table


def added(parts):
    while len(parts) > 1:
        parts = [sum(parts[at : at + 2][1:], parts[at]) for at in range(0, len(parts), 2)]
    return parts[0]


def row_sum(values):
    return jnp.sum(values, axis=1, keepdims=True)


def add_kernel(count, keep_ref, arrived_ref, *refs):
    parts = refs[-count:]
    size = parts[0].shape[0]
    for at, part_ref in enumerate(parts):
        rows = slice(at * size, (at + 1) * size)
        total = keep_ref[rows].astype(jnp.float32) + arrived_ref[rows].astype(jnp.float32)
        part_ref[...] = total.astype(part_ref.dtype)


def gradient_kernel(count, *refs):
    block_parts, sums, refs = refs[:count], refs[count : count + 3], refs[count + 3 :]
    masters, refs = refs[:4], refs[4:]
    grads, (message_ref, col_ref) = refs[:4], refs[4:]
    blocks = added([part[0].astype(jnp.float32) for part in block_parts])
    rows, up_cols = grads[2].shape
    qkv_cols, out_cols = grads[0].shape[1], grads[1].shape[1]
    folds = grads[3].shape[0] // rows
    up = blocks[:, :up_cols]
    downs = [blocks[:, up_cols + fold * out_cols :][:, :out_cols] for fold in range(folds)]
    start = up_cols + folds * out_cols
    proj = blocks[:, start : start + out_cols]
    qkv = blocks[:, start + out_cols :]
    grads[0][...] = qkv
    grads[1][...] = proj
    grads[2][...] = up
    for fold in range(folds):
        grads[3][fold * rows : (fold + 1) * rows, :] = downs[fold]
    squares = [part * part + tiny_square for part in (qkv, proj, up, *downs)]
    weights = [master[...] for master in masters[:3]]
    weights += [masters[3][fold * rows : (fold + 1) * rows, :] for fold in range(folds)]
    columns = [row_sum(square) for square in squares] + [row_sum(part * part) for part in weights]
    message_ref[...] = jnp.zeros_like(message_ref)
    message_ref[:16, :rows] = lane_table(rows, columns).T[:16]
    put_vectors(message_ref, sums)
    col_ref[...] = jnp.zeros_like(col_ref)
    for at, square in enumerate((*squares[:3], added(squares[3:]))):
        col_ref[at : at + 1, : square.shape[1]] = column_sum(square)


def put_vectors(message_ref, sums):
    att_ref, ff_ref, up_ref = sums
    width = att_ref.shape[1]
    count = up_ref.shape[1] // width
    step = 8 + count
    for tile in range(width // 128):
        base = 16 + tile * step
        cols = slice(tile * 128, (tile + 1) * 128)
        message_ref[base : base + 4, :] = att_ref[:4, cols]
        message_ref[base + 4 : base + 7, :] = ff_ref[:3, cols]
        for at in range(count):
            start = at * width + tile * 128
            message_ref[base + 7 + at : base + 8 + at, :] = up_ref[:, start : start + 128]
        message_ref[base + 7 + count : base + 8 + count, :] = ff_ref[3:4, cols]


def row_kernel(widths, qkv_old_ref, proj_old_ref, up_old_ref, down_old_ref, col_ref, *refs):
    parts, (rows_ref, message_ref) = refs[:-2], refs[-2:]
    sums = added([part[...] for part in parts])
    height = rows_ref.shape[0]
    folds = down_old_ref.shape[0] // height
    down_old = down_old_ref[...].reshape(1, folds * height)
    table = jnp.concatenate([sums[:16, :height], jnp.zeros((112, height), jnp.float32)], axis=0).T
    old = jnp.concatenate(
        [
            qkv_old_ref[...].reshape(1, height),
            proj_old_ref[...].reshape(1, height),
            up_old_ref[...].reshape(1, height),
            *[down_old[:, fold * height : (fold + 1) * height] for fold in range(folds)],
            jnp.zeros((128 - 3 - folds, height), jnp.float32),
        ],
        axis=0,
    ).T
    lane = lax.broadcasted_iota(jnp.int32, table.shape, 1)
    share = jnp.ones_like(table)
    for at, size in enumerate(widths):
        share = jnp.where(lane == at, (1.0 - decay_rate) / size, share)
    rows = decay_rate * old + share * table
    rows_ref[...] = rows
    message_ref[:8, :] = col_ref[...]
    message_ref[4:5, :128] = column_sum(rows)
    tiles = message_ref.shape[1] // 128
    step = (sums.shape[0] - 16) // tiles // 4 * 4
    message_ref[8:, :] = jnp.zeros((message_ref.shape[0] - 8, tiles * 128), jnp.float32)
    for tile in range(tiles):
        base = 16 + tile * step
        message_ref[8 : 8 + step, tile * 128 : (tile + 1) * 128] = sums[base : base + step]


def update_kernel(count, heights, widths, *refs):
    messages, refs = refs[:count], refs[count:]
    rows_ref, vectors_ref, moment_ref, refs = refs[0], refs[1], refs[2], refs[3:]
    grads, masters, cols_old, refs = refs[:4], refs[4:8], refs[8:12], refs[12:]
    news, cols_new, refs = refs[:4], refs[4:8], refs[8:]
    rows_out, (vector_grad_ref, moment_new_ref, vector_new_ref) = refs[:4], refs[4:]
    total = added([message[...] for message in messages])
    rows_new = rows_ref[...]
    height = rows_new.shape[0]
    folds = grads[3].shape[0] // height
    across_rows = rows_new.T
    for which in range(3):
        rows_out[which][...] = across_rows[which]
    rows_out[3][...] = jnp.concatenate([across_rows[3 + fold : 4 + fold] for fold in range(folds)], axis=1)[0]
    lanes = [[0], [1], [2], list(range(3, 3 + folds))]
    for which in range(4):
        entries = heights[which] * widths[which]
        cols = cols_old[which].shape[0]
        new = decay_rate * cols_old[which][...].reshape(1, cols) + (1.0 - decay_rate) / heights[which] * total[
            which : which + 1, :cols
        ]
        cols_new[which][...] = new[0]
        mean_rows = sum(total[4:5, lane : lane + 1] for lane in lanes[which]) / heights[which]
        squares = sum(total[4:5, 3 + folds + lane : 4 + folds + lane] for lane in lanes[which])
        rate = step_rate * jnp.sqrt(squares / entries)
        across = new / mean_rows
        for fold, lane in enumerate(lanes[which]):
            part = slice(fold * height, (fold + 1) * height)
            second = rows_new[:, lane : lane + 1] * across
            news[which][part, :] = masters[which][part, :] - rate * grads[which][part, :] * lax.rsqrt(second)
    vectors = vectors_ref[...]
    gradient = total[8 : 8 + vectors.shape[0]]
    vector_grad_ref[...] = gradient
    moment = decay_rate * moment_ref[...] + (1.0 - decay_rate) * (gradient * gradient + tiny_square)
    moment_new_ref[...] = moment
    spread = jnp.sqrt(jnp.mean(vectors * vectors, axis=1, keepdims=True))
    vector_new_ref[...] = vectors - step_rate * spread * gradient * lax.rsqrt(moment)


def packed_body(
    tokens, keep_mask, cotangent, qkv_weight, proj_weight, up_weight, down_weight, vectors,
    qkv_rows, qkv_cols, proj_rows, proj_cols, up_rows, up_cols, down_rows, down_cols, vector_moment,
):
    spread, dp_size = lax.axis_size("group"), lax.axis_size("dp")
    low, high = jnp.bfloat16, jnp.float32
    place = linear_place().astype(jnp.int32).reshape(1)
    group = lax.axis_index("group")
    held, slots, width = tokens.shape
    images, length = keep_mask.shape
    hidden = up_weight.shape[1] * spread
    total = images * length
    rows = qkv_weight.shape[0]
    folds = down_weight.shape[0] // rows
    core_bits = (1,)
    near_bits = tuple(1 << at for at in range(1, spread.bit_length()))
    far_bits = tuple(spread << at for at in range(1, dp_size.bit_length() - 1))
    half = spread * dp_size // 2

    anywhere = pl.BlockSpec(memory_space=pl.ANY)
    in_smem = pl.BlockSpec(memory_space=pltpu.SMEM)

    in_vmem = pl.BlockSpec(memory_space=pltpu.VMEM)
    small = functools.partial(
        pl.pallas_call, compiler_params=pltpu.CompilerParams(vmem_limit_bytes=vmem_bytes)
    )
    masters = (qkv_weight, proj_weight, up_weight, down_weight)
    parted = jax.ShapeDtypeStruct((spread, slots, images, width), low)

    def to_group(parts):
        return lax.all_to_all(parts, "group", split_axis=0, concat_axis=0, tiled=True)

    def to_images(parts):
        return to_group(parts).reshape(total, width)

    def exchange(parts):
        return [parts[0]] + [permute(part, relative) for relative, part in enumerate(parts) if relative]

    def settle_whole(parts):
        whole = small(settle_whole_kernel, out_shape=jax.ShapeDtypeStruct((slots, held, width), low))(parts)
        return whole.transpose(1, 0, 2)

    def settle(parts):
        parts = [part.reshape(slots, -1, width) for part in parts]
        whole = small(
            functools.partial(settle_kernel, spread),
            in_specs=[in_smem] + [in_vmem] * len(parts),
            out_specs=in_vmem,
            out_shape=jax.ShapeDtypeStruct((slots, held, width), low),
        )(place, *parts)
        return whole.transpose(1, 0, 2)

    token_cut, first_pack = small(
        front_kernel,
        out_shape=[
            parted,
            jax.ShapeDtypeStruct((rows, qkv_weight.shape[1] + proj_weight.shape[1]), low),
        ],
    )(tokens.transpose(1, 0, 2), qkv_weight, proj_weight)
    inputs = to_images(token_cut)
    first_blocks = jnp.concatenate(gather_step([first_pack[None]], far_bits))
    cotangent_cut, second_pack = small(
        second_front_kernel,
        in_specs=[in_vmem] * 3 + [anywhere],
        out_shape=[
            parted,
            jax.ShapeDtypeStruct((rows, up_weight.shape[1] + folds * down_weight.shape[1]), low),
        ],
    )(cotangent.transpose(1, 0, 2), up_weight, down_weight, first_blocks)
    upstream = to_images(cotangent_cut)
    first_blocks = gather_step(gather_step([first_blocks], near_bits), core_bits)
    second_far = gather_step([second_pack[None]], far_bits)

    step_rows = PER_STEP * length
    block = (step_rows, width)
    pairs = width // (2 * HEAD_DIM)
    steps = images // PER_STEP
    statics = (images, dp_size, spread)
    wide = scratch(width // 128, total, 128)
    probs_block = (PER_STEP, pairs, length, 2 * length)
    attention_outs = [
        ((total, 3 * width), low, (step_rows, 3 * width)),
        ((images, *probs_block[1:]), low, probs_block),
        ((total, width), low, block),
        ((total, width), high, block),
    ]
    attention_flops = (2 * total * width * 4 * width + 8 * total * length * width) // steps
    attention_scratches = [scratch(length, images), scratch(step_rows, width, dtype=low)]
    *attention, x, w_qkv, w_proj, second_joined = call_kernel(
        first_attention_kernel, statics, 1,
        ["place"] + [None] * (2 * spread + 3 + len(second_far)),
        attention_outs
        + [
            ((total, width), low, None),
            ((width, 3 * width), low, None),
            ((width, width), low, None),
            ((len(second_far), *second_pack.shape), low, None),
        ],
        [scratch(dp_size * spread, *first_pack.shape, dtype=low), wide] + attention_scratches,
        (place, inputs, *first_blocks, *second_far, keep_mask, vectors),
        attention_flops,
    )
    for first_step, count in ((1, steps - 2), (steps - 1, 1)):
        attention = call_kernel(
            next_attention_kernel, (first_step * PER_STEP,), count,
            [block] + [None] * 4 + ["await"] * len(attention),
            attention_outs, attention_scratches,
            (x, keep_mask, w_qkv, w_proj, vectors, *attention),
            attention_flops * count, first_step=first_step,
            aliases={5 + at: at for at in range(len(attention))},
        )
    qkv, probs, attended, middle = attention
    second_blocks = gather_step(gather_step([second_joined], near_bits), core_bits)
    piece = ((slots * images, width), low, None)
    pack_cols = up_weight.shape[1] + (folds + 1) * proj_weight.shape[1]
    results = call_kernel(
        feed_forward_packed_kernel, statics, steps,
        ["place"] + [None] * (2 * spread + 1) + [block, block] + [None] * 2,
        [
            ((total, width), low, None),
            ((total, width), high, block),
            ((total, width), low, block),
            ((half, rows, pack_cols), low, None),
            ((half, rows, pack_cols), low, None),
            ((8, width), high, None),
            ((1, hidden), high, None),
        ],
        [
            scratch(width, hidden, dtype=low),
            scratch(hidden, width, dtype=low),
            scratch(hidden, width, dtype=low),
            scratch(dp_size * spread, *second_pack.shape, dtype=low),
            scratch(1, hidden),
            wide,
            scratch(step_rows, width, dtype=low),
            scratch(width, step_rows, dtype=low),
            scratch(step_rows, width, dtype=low),
            scratch(width, step_rows, dtype=low),
            scratch(step_rows, width),
            scratch(step_rows, 128),
            scratch(step_rows, width),
            scratch(step_rows, width),
            scratch(width, hidden),
            scratch(width, hidden),
            scratch(width, width),
        ],
        (
            place, upstream, *second_blocks, middle, attended, w_proj, vectors,
        ),
        12 * total * width * hidden + 4 * total * width * width, total * hidden,
    )
    output, d_middle, d_attended, ff_keep, ff_leave, ff_sums, up_sums = results
    output = to_group(output.reshape(parted.shape))

    def add_parts(count, keep, arrived, awaited):
        part = (keep.shape[0] // count, *keep.shape[1:])
        return small(
            functools.partial(add_kernel, count),
            in_specs=[in_vmem] * 2 + [anywhere] * len(awaited),
            out_specs=[in_vmem] * count,
            out_shape=[jax.ShapeDtypeStruct(part, high)]
            + [jax.ShapeDtypeStruct(part, low)] * (count - 1),
        )(keep, arrived, *awaited)

    ff_first = permute(ff_leave, core_bits[0])
    ff_quarter = half // 4
    ff_parts = [
        add_wide(ff_keep[at : at + ff_quarter], ff_first[at : at + ff_quarter]).astype(low)
        for at in range(ff_quarter, half, ff_quarter)
    ]
    near_masks = direct_masks(near_bits)
    ff_near = [permute(part, mask) for part, mask in zip(ff_parts, near_masks)]
    results = call_kernel(
        attention_back_packed_kernel, statics, steps,
        ["place", block, (step_rows, 3 * width), probs_block, block, block, None, None] + ["await"] * len(ff_parts),
        [piece] * spread
        + [
            ((half, rows, qkv_weight.shape[1]), low, None),
            ((half, rows, qkv_weight.shape[1]), low, None),
            ((8, width), high, None),
        ],
        [
            wide,
            scratch(step_rows, width, dtype=low),
            scratch(step_rows, 3 * width, dtype=low),
            scratch(step_rows, width),
            scratch(width, 3 * width),
        ],
        (place, x, qkv, probs, d_attended, d_middle, w_qkv, vectors, *ff_parts),
        4 * total * width * 3 * width + 16 * total * length * width,
    )
    qkv_keep, qkv_leave, att_sums = results[spread:]
    qkv_arrived = permute(qkv_leave, core_bits[0])
    input_parts = exchange(results[:spread])
    qkv_held, *leaving = add_parts(4, qkv_keep, qkv_arrived, ff_near + [output])
    qkv_parts = [permute(part, mask) for part, mask in zip(leaving, near_masks)]
    ff_held = add_wide(ff_keep[:ff_quarter], ff_first[:ff_quarter], *ff_near)
    qkv_held = add_wide(qkv_held, *qkv_parts)
    blocks, block_parts = scatter_step(jnp.concatenate([ff_held, qkv_held], axis=2), far_bits)
    block_parts = [blocks] + block_parts

    heights = [master.shape[0] * dp_size for master in masters]
    widths = [master.shape[1] * spread for master in masters]
    message_rows = -(-(16 + width // 128 * vectors.shape[0]) // 8) * 8
    *grads, message, col_part = small(
        functools.partial(gradient_kernel, len(block_parts)),
        out_shape=[jax.ShapeDtypeStruct(master.shape, high) for master in masters]
        + [jax.ShapeDtypeStruct((message_rows, 128), high), jax.ShapeDtypeStruct((8, width), high)],
    )(*block_parts, att_sums, ff_sums, up_sums, *masters)
    messages = [message] + [permute(message, mask) for mask in range(1, spread)]
    rows_old = [qkv_rows, proj_rows, up_rows, down_rows]
    rows_new, message = small(
        functools.partial(row_kernel, widths[:3] + widths[3:] * folds),
        out_shape=[
            jax.ShapeDtypeStruct((rows, 128), high),
            jax.ShapeDtypeStruct((24, width), high),
        ],
    )(*rows_old, col_part, *messages)
    message = message + permute(message, near_bits[-1])
    messages = [message] + [permute(message, mask) for mask in direct_masks(far_bits)]
    cols_old = [qkv_cols, proj_cols, up_cols, down_cols]
    results = small(
        functools.partial(update_kernel, len(messages), heights, widths),
        out_shape=[jax.ShapeDtypeStruct(master.shape, high) for master in masters]
        + [jax.ShapeDtypeStruct(part.shape, high) for part in cols_old]
        + [jax.ShapeDtypeStruct(part.shape, high) for part in (qkv_rows, proj_rows, up_rows, down_rows)]
        + [jax.ShapeDtypeStruct(vectors.shape, high)] * 3,
    )(*messages, rows_new, vectors, vector_moment, *grads, *masters, *cols_old)
    news, cols_new, rows_out = results[:4], results[4:8], results[8:12]
    vector_grad, vector_moment_new, vector_new = results[12:]
    factored = []
    for which in range(4):
        factored += [grads[which], rows_out[which], cols_new[which], news[which]]
    return (settle_whole(output), settle(input_parts), *factored, vector_grad, vector_moment_new, vector_new)


def body(*arrays):
    spread, dp_size = lax.axis_size("group"), lax.axis_size("dp")
    rows, images = arrays[3].shape[0], arrays[1].shape[0]
    slots, width = arrays[0].shape[1:]
    folds = arrays[6].shape[0] // rows
    powers = all(size & (size - 1) == 0 for size in (spread, dp_size))
    fits = powers and spread == 4 and dp_size > 2
    fits = fits and arrays[5].shape[1] <= width and folds <= 5
    fits = fits and rows % 16 == 0 and images % PER_STEP == 0 and images > 2 * PER_STEP and images % 16 == 0 and slots % 4 == 0
    return packed_body(*arrays) if fits else general_body(*arrays)


def solution(mesh):
    in_specs = (
        P("dp", "group", None),
        P(("dp", "group"), None),
        P("dp", "group", None),
        P("dp", "group"),
        P("dp", "group"),
        P("dp", "group"),
        P("dp", "group"),
        P(),
        P("dp"),
        P("group"),
        P("dp"),
        P("group"),
        P("dp"),
        P("group"),
        P("dp"),
        P("group"),
        P(),
    )
    out_specs = (
        P("dp", "group", None),
        P("dp", "group", None),
        P("dp", "group"),
        P("dp"),
        P("group"),
        P("dp", "group"),
        P("dp", "group"),
        P("dp"),
        P("group"),
        P("dp", "group"),
        P("dp", "group"),
        P("dp"),
        P("group"),
        P("dp", "group"),
        P("dp", "group"),
        P("dp"),
        P("group"),
        P("dp", "group"),
        P(),
        P(),
        P(),
    )
    return jax.shard_map(body, mesh=mesh, in_specs=in_specs, out_specs=out_specs, check_vma=False)
```

```python
import functools
import math

import jax
import jax.numpy as jnp
from jax import lax
from jax.experimental import pallas as pl
from jax.experimental.pallas import tpu as pltpu
from jax.sharding import PartitionSpec as P

HEAD_DIM = 64
STEP_NUMBER = 10


step_rate = 0.3
norm_epsilon = 1e-06
tiny_square = 1e-30
decay_rate = 1.0 - STEP_NUMBER ** (-0.8)
LOG2_E = 1.4426950408889634


def axis_bits(name):
    count = lax.axis_size(name)
    return [(name, 1 << place) for place in range(count.bit_length() - 1)]


def swap_partner(array, step):
    name, bit = step
    count = lax.axis_size(name)
    return lax.ppermute(array, name, [(rank, rank ^ bit) for rank in range(count)])


def upper_side(step):
    name, bit = step
    return (lax.axis_index(name) & bit) != 0


def gather_blocks(array, steps):
    for step in steps:
        arrived = swap_partner(array, step)
        upper = upper_side(step)
        array = jnp.stack([jnp.where(upper, arrived, array), jnp.where(upper, array, arrived)])
    return array


def scatter_sum(array, steps):
    for step in steps:
        upper = upper_side(step)
        leaving = jnp.where(upper, array[0], array[1]).astype(jnp.bfloat16)
        arrived = swap_partner(leaving, step)
        array = jnp.where(upper, array[1], array[0]).astype(jnp.float32) + arrived.astype(jnp.float32)
    return array


def sum_everywhere(array, steps):
    for step in steps:
        array = array + swap_partner(array, step)
    return array


def sum_parts(parts, steps):
    flat = [part.reshape(-1) for part in parts]
    total = sum_everywhere(jnp.concatenate(flat), steps)
    result, start = [], 0
    for part in parts:
        result.append(total[start : start + part.size].reshape(part.shape))
        start += part.size
    return result


def block_order(steps):
    order = []
    for name in ("dp", "group"):
        bits = sorted((step for step in steps if step[0] == name), key=lambda step: -step[1])
        order.append([steps.index(step) for step in bits])
    return order


def blocks_to_whole(blocks, steps):
    count = len(steps)
    rows, cols = blocks.shape[count:]
    dp_axes, group_axes = block_order(steps)
    dp_axes = [count - 1 - axis for axis in dp_axes]
    group_axes = [count - 1 - axis for axis in group_axes]
    whole = blocks.transpose(dp_axes + [count] + group_axes + [count + 1])
    return whole.reshape(rows << len(dp_axes), cols << len(group_axes))


def whole_to_blocks(whole, steps):
    dp_axes, group_axes = block_order(steps)
    rows = whole.shape[0] >> len(dp_axes)
    cols = whole.shape[1] >> len(group_axes)
    split = whole.reshape([2] * len(dp_axes) + [rows] + [2] * len(group_axes) + [cols])
    places = dp_axes + [len(steps)] + group_axes + [len(steps) + 1]
    return split.transpose([places.index(axis) for axis in range(len(places))])


PER_STEP = 4
FF_CHUNK = 256
vmem_bytes = 60 * 1024 * 1024


def dot(left, right, left_axis=1, right_axis=0):
    return lax.dot_general(
        left, right, (((left_axis,), (right_axis,)), ((), ())), preferred_element_type=jnp.float32
    )


def normal_form(values):
    center = jnp.mean(values, axis=-1, keepdims=True)
    centered = values - center
    spread = jnp.mean(centered * centered, axis=-1, keepdims=True)
    scale = lax.rsqrt(spread + norm_epsilon)
    return centered * scale, scale


def norm_back(grad, unit, scale, gain):
    weighted = grad * gain
    along = jnp.mean(weighted * unit, axis=-1, keepdims=True)
    level = jnp.mean(weighted, axis=-1, keepdims=True)
    return scale * (weighted - level - unit * along)


def column_sum(values):
    return jnp.sum(values, axis=0, keepdims=True)


def pair_mask(length):
    return lax.broadcasted_iota(jnp.int32, (length, 2 * HEAD_DIM), 1) < HEAD_DIM


def stack_heads(pair, first):
    none = jnp.zeros_like(pair)
    return jnp.concatenate([jnp.where(first, pair, none), jnp.where(first, none, pair)], axis=0)


def join_heads(rows, first):
    length = rows.shape[0] // 2
    return jnp.where(first, rows[:length], rows[length:])


def gelu_and_slope(pre):
    bell = jnp.exp2(pre * pre * (-0.5 * LOG2_E))
    inverse = 1.0 / (1.0 + (0.3275911 * 0.5**0.5) * jnp.abs(pre))
    poly = inverse * (
        0.5 * 0.254829592
        + inverse
        * (
            0.5 * -0.284496736
            + inverse
            * (0.5 * 1.421413741 + inverse * (0.5 * -1.453152027 + inverse * (0.5 * 1.061405429)))
        )
    )
    tail = poly * bell
    below = jnp.where(pre >= 0, 1.0 - tail, tail)
    return pre * below, below + pre * bell * 0.3989422804014327


def widen(source_ref, wide_ref, images):
    tiles, total, lanes = wide_ref.shape
    rows_at_once = 8 * images

    @pl.loop(0, total // rows_at_once)
    def _(part):
        rows = pl.ds(pl.multiple_of(part * rows_at_once, rows_at_once), rows_at_once)
        for tile in range(tiles):
            cols = slice(tile * lanes, (tile + 1) * lanes)
            wide_ref[tile, rows, :] = source_ref[rows, cols].astype(jnp.float32)


def narrow(wide_ref, target_ref, images):
    tiles, total, lanes = wide_ref.shape
    rows_at_once = 8 * images

    @pl.loop(0, total // rows_at_once)
    def _(part):
        rows = pl.ds(pl.multiple_of(part * rows_at_once, rows_at_once), rows_at_once)
        for tile in range(tiles):
            cols = slice(tile * lanes, (tile + 1) * lanes)
            target_ref[rows, cols] = wide_ref[tile, rows, :].astype(target_ref.dtype)


def take_image(wide_ref, image, images):
    tiles, total, _ = wide_ref.shape
    rows = pl.ds(image, total // images, images)
    return jnp.concatenate([wide_ref[tile, rows, :] for tile in range(tiles)], axis=1)


def put_image(wide_ref, image, images, values):
    tiles, total, lanes = wide_ref.shape
    rows = pl.ds(image, total // images, images)
    for tile in range(tiles):
        wide_ref[tile, rows, :] = values[:, tile * lanes : (tile + 1) * lanes]


def attention_kernel(
    images, tokens_ref, bias_ref, w_qkv_ref, w_proj_ref, vectors_ref,
    x_ref, qkv_ref, probs_ref, attended_ref, middle_ref, wide_ref, normed_ref,
):
    @pl.when(pl.program_id(0) == 0)
    def _():
        widen(tokens_ref, wide_ref, images)
        to_image_rows(wide_ref, x_ref, images)

    attention_steps(
        x_ref, lambda image: bias_ref[image], w_qkv_ref, w_proj_ref, vectors_ref,
        qkv_ref, probs_ref, attended_ref, middle_ref, normed_ref,
    )


def to_image_rows(wide_ref, x_ref, images):
    length = wide_ref.shape[1] // images

    @pl.loop(0, images)
    def _(image):
        rows = pl.ds(pl.multiple_of(image * length, length), length)
        x_ref[rows, :] = take_image(wide_ref, image, images).astype(jnp.bfloat16)


def attention_steps(
    x_ref, bias_column, w_qkv_ref, w_proj_ref, vectors_ref,
    qkv_ref, probs_ref, attended_ref, middle_ref, normed_ref,
):
    per_step, _, length, _ = probs_ref.shape
    step_rows, width = middle_ref.shape
    base = 0 if x_ref.shape[0] == step_rows else pl.program_id(0) * step_rows

    for image in range(per_step):
        rows = slice(image * length, (image + 1) * length)
        x = x_ref[pl.ds(pl.multiple_of(base + image * length, length), length), :].astype(jnp.float32)
        unit, _ = normal_form(x)
        normed_ref[rows, :] = (unit * vectors_ref[0:1] + vectors_ref[1:2]).astype(jnp.bfloat16)
    for part in range(3):
        cols = slice(part * width, (part + 1) * width)
        projected = dot(normed_ref[...], w_qkv_ref[:, cols])
        if part != 1:
            row = 2 if part == 0 else 3
            projected = projected + vectors_ref[row : row + 1]
        qkv_ref[:, cols] = projected.astype(jnp.bfloat16)

    @pl.loop(0, per_step)
    def _(image):
        rows = pl.ds(pl.multiple_of(image * length, length), length)
        first = pair_mask(length)
        place = lax.broadcasted_iota(jnp.int32, (length, 2 * length), 0)
        asker = lax.broadcasted_iota(jnp.int32, (length, 2 * length), 1)
        asker = jnp.where(asker >= length, asker - length, asker)
        bias = jnp.where(place == asker, 0.0, bias_column(image))
        for pair in range(width // (2 * HEAD_DIM)):
            low = pair * 2 * HEAD_DIM
            queries = stack_heads(qkv_ref[rows, low : low + 2 * HEAD_DIM], first)
            keys = qkv_ref[rows, width + low : width + low + 2 * HEAD_DIM]
            values = qkv_ref[rows, 2 * width + low : 2 * width + low + 2 * HEAD_DIM]
            scores = dot(keys, queries, 1, 1) * (HEAD_DIM**-0.5 * LOG2_E) + bias
            weights = jnp.exp2(scores - jnp.max(scores, axis=0, keepdims=True))
            probs = weights * (1.0 / jnp.sum(weights, axis=0, keepdims=True))
            probs = probs.astype(jnp.bfloat16)
            probs_ref[image, pair] = probs
            attended = join_heads(dot(probs, values, 0, 0), first)
            attended_ref[rows, low : low + 2 * HEAD_DIM] = attended.astype(jnp.bfloat16)

    middle_ref[...] = (
        x_ref[pl.ds(pl.multiple_of(base, length), step_rows), :].astype(jnp.float32)
        + dot(attended_ref[...], w_proj_ref[...])
        + vectors_ref[4:5]
    )


def feed_forward_kernel(
    images, middle_ref, cotangent_ref, attended_ref, w_up_ref, w_down_ref, w_proj_ref, vectors_ref, bias_up_ref,
    output_ref, d_middle_ref, d_attended_ref, up_grad_ref, down_grad_ref, proj_grad_ref, vector_sums_ref, up_sums_ref,
    wide_ref, *scratches,
):
    up_total_ref, down_total_ref, proj_total_ref = scratches[-3:]

    @pl.when(pl.program_id(0) == 0)
    def _():
        widen(cotangent_ref, wide_ref, images)

    feed_forward_steps(
        images, middle_ref, attended_ref, w_up_ref, w_down_ref, w_proj_ref, vectors_ref, bias_up_ref,
        d_middle_ref, d_attended_ref, vector_sums_ref, up_sums_ref, wide_ref, *scratches,
    )

    @pl.when(pl.program_id(0) == pl.num_programs(0) - 1)
    def _():
        narrow(wide_ref, output_ref, images)
        up_grad_ref[...] = up_total_ref[...].astype(jnp.bfloat16)
        down_grad_ref[...] = down_total_ref[...].T.astype(jnp.bfloat16)
        proj_grad_ref[...] = proj_total_ref[...].astype(jnp.bfloat16)


def feed_forward_steps(
    images, middle_ref, attended_ref, w_up_ref, w_down_ref, w_proj_ref, vectors_ref, bias_up_ref,
    d_middle_ref, d_attended_ref, vector_sums_ref, up_sums_ref,
    wide_ref, normed_ref, normed_t_ref, dy_ref, dy_t_ref, unit_ref, scale_ref, ahead_ref, back_ref,
    up_total_ref, down_total_ref, proj_total_ref,
):
    step = pl.program_id(0)
    length = wide_ref.shape[1] // images
    hidden = w_up_ref.shape[1]
    per_step = middle_ref.shape[0] // length

    @pl.when(step == 0)
    def _():
        for total in (up_total_ref, down_total_ref, proj_total_ref, vector_sums_ref, up_sums_ref):
            total[...] = jnp.zeros_like(total)

    for image in range(per_step):
        rows = slice(image * length, (image + 1) * length)
        dy = take_image(wide_ref, step * per_step + image, images)
        dy_ref[rows, :] = dy.astype(jnp.bfloat16)
        vector_sums_ref[3:4] += column_sum(dy)
        unit, scale = normal_form(middle_ref[rows, :])
        unit_ref[rows, :] = unit
        scale_ref[rows, :] = jnp.broadcast_to(scale, (length, scale_ref.shape[1]))
        normed_ref[rows, :] = (unit * vectors_ref[5:6] + vectors_ref[6:7]).astype(jnp.bfloat16)
    normed_t_ref[...] = normed_ref[...].T
    dy_t_ref[...] = dy_ref[...].T
    ahead_ref[...] = jnp.zeros_like(ahead_ref)
    back_ref[...] = jnp.zeros_like(back_ref)

    @pl.loop(0, hidden // FF_CHUNK)
    def _(chunk):
        cols = pl.ds(pl.multiple_of(chunk * FF_CHUNK, FF_CHUNK), FF_CHUNK)
        w_up = w_up_ref[:, cols]
        w_down = w_down_ref[cols, :]
        active, slope = gelu_and_slope(dot(normed_ref[...], w_up) + bias_up_ref[:, cols])
        active = active.astype(jnp.bfloat16)
        d_hidden = dot(dy_ref[...], w_down, 1, 1) * slope
        d_hidden = d_hidden.astype(jnp.bfloat16)
        ahead_ref[...] += dot(active, w_down)
        back_ref[...] += dot(d_hidden, w_up, 1, 1)
        down_total_ref[:, cols] += dot(dy_t_ref[...], active)
        up_total_ref[:, cols] += dot(normed_t_ref[...], d_hidden)
        up_sums_ref[:, cols] += column_sum(d_hidden.astype(jnp.float32))

    for image in range(per_step):
        rows = slice(image * length, (image + 1) * length)
        output = middle_ref[rows, :] + ahead_ref[rows, :] + vectors_ref[11:12]
        put_image(wide_ref, step * per_step + image, images, output)
        unit = unit_ref[rows, :]
        grad = back_ref[rows, :]
        vector_sums_ref[1:2] += column_sum(grad * unit)
        vector_sums_ref[2:3] += column_sum(grad)
        d_middle = dy_ref[rows, :].astype(jnp.float32) + norm_back(
            grad, unit, scale_ref[rows, 0:1], vectors_ref[5:6]
        )
        d_middle_ref[rows, :] = d_middle
        d_branch = d_middle.astype(jnp.bfloat16)
        dy_ref[rows, :] = d_branch
        vector_sums_ref[0:1] += column_sum(d_branch.astype(jnp.float32))
    proj_total_ref[...] += dot(attended_ref[...], dy_ref[...], 0, 0)
    d_attended_ref[...] = dot(dy_ref[...], w_proj_ref[...], 1, 1).astype(jnp.bfloat16)


def attention_back_kernel(
    images, x_ref, qkv_ref, probs_ref, d_attended_ref, d_middle_ref, w_qkv_ref, vectors_ref,
    input_grad_ref, qkv_grad_ref, vector_sums_ref, wide_ref, *scratches,
):
    @pl.when(pl.program_id(0) == 0)
    def _():
        scratches[-1][...] = jnp.zeros_like(scratches[-1])
        vector_sums_ref[...] = jnp.zeros_like(vector_sums_ref)

    def put(image, rows, values):
        put_image(wide_ref, image, images, values)

    attention_back_steps(
        put, x_ref, qkv_ref, probs_ref, d_attended_ref, d_middle_ref, w_qkv_ref, vectors_ref,
        vector_sums_ref, *scratches,
    )

    @pl.when(pl.program_id(0) == pl.num_programs(0) - 1)
    def _():
        narrow(wide_ref, input_grad_ref, images)
        qkv_grad_ref[...] = scratches[-1][...].astype(jnp.bfloat16)


def attention_back_steps(
    put, x_ref, qkv_ref, probs_ref, d_attended_ref, d_middle_ref, w_qkv_ref, vectors_ref,
    vector_sums_ref, normed_ref, d_projected_ref, back_ref, qkv_total_ref,
):
    step = pl.program_id(0)
    width = x_ref.shape[1]
    length = probs_ref.shape[2]
    per_step = probs_ref.shape[0]

    @pl.loop(0, per_step)
    def _(image):
        rows = pl.ds(pl.multiple_of(image * length, length), length)
        first = pair_mask(length)
        for pair in range(width // (2 * HEAD_DIM)):
            low = pair * 2 * HEAD_DIM
            cols = [slice(part * width + low, part * width + low + 2 * HEAD_DIM) for part in range(3)]
            queries = stack_heads(qkv_ref[rows, cols[0]], first)
            keys = qkv_ref[rows, cols[1]]
            values = qkv_ref[rows, cols[2]]
            probs = probs_ref[image, pair]
            d_attended = stack_heads(d_attended_ref[rows, cols[0]], first)
            d_projected_ref[rows, cols[2]] = dot(probs, d_attended).astype(jnp.bfloat16)
            d_probs = dot(values, d_attended, 1, 1)
            probs = probs.astype(jnp.float32)
            along = jnp.sum(d_probs * probs, axis=0, keepdims=True)
            d_scores = (probs * (d_probs - along)).astype(jnp.bfloat16)
            scale = HEAD_DIM**-0.5
            d_queries = join_heads(dot(d_scores, keys, 0, 0), first) * scale
            d_projected_ref[rows, cols[0]] = d_queries.astype(jnp.bfloat16)
            d_projected_ref[rows, cols[1]] = (dot(d_scores, queries) * scale).astype(jnp.bfloat16)

    vector_sums_ref[2:3] += column_sum(d_projected_ref[:, :width].astype(jnp.float32))
    vector_sums_ref[3:4] += column_sum(d_projected_ref[:, 2 * width :].astype(jnp.float32))
    back_ref[...] = dot(d_projected_ref[...], w_qkv_ref[...], 1, 1)
    for image in range(per_step):
        rows = slice(image * length, (image + 1) * length)
        unit, scale = normal_form(x_ref[rows, :].astype(jnp.float32))
        normed_ref[rows, :] = (unit * vectors_ref[0:1] + vectors_ref[1:2]).astype(jnp.bfloat16)
        grad = back_ref[rows, :]
        vector_sums_ref[0:1] += column_sum(grad * unit)
        vector_sums_ref[1:2] += column_sum(grad)
        d_input = d_middle_ref[rows, :] + norm_back(grad, unit, scale, vectors_ref[0:1])
        put(step * per_step + image, rows, d_input)
    qkv_total_ref[...] += dot(normed_ref[...], d_projected_ref[...], 0, 0)


def whole_block(shape):
    return pl.BlockSpec(shape, lambda step: (0,) * len(shape))


def step_block(shape, first=0):
    return pl.BlockSpec(shape, lambda step: (first + step,) + (0,) * (len(shape) - 1))


def scratch(*shape, dtype=jnp.float32):
    return pltpu.VMEM(shape, dtype)


def call_kernel(kernel, statics, steps, ins, outs, scratches, operands, flops, transcendentals=0, first_step=0, aliases={}):
    in_specs = [
        pl.BlockSpec(memory_space=pltpu.SMEM)
        if block == "place"
        else pl.BlockSpec(memory_space=pl.ANY)
        if block == "await"
        else whole_block(op.shape) if block is None else step_block(block, first_step)
        for op, block in zip(operands, ins)
    ]
    out_specs = [
        whole_block(shape) if block is None else step_block(block, first_step) for shape, dtype, block in outs
    ]
    moved = sum(op.size * op.dtype.itemsize for op in operands) + sum(
        math.prod(shape) * jnp.dtype(dtype).itemsize for shape, dtype, block in outs
    )
    return pl.pallas_call(
        functools.partial(kernel, *statics),
        grid=(steps,),
        in_specs=in_specs,
        out_specs=out_specs,
        out_shape=[jax.ShapeDtypeStruct(shape, dtype) for shape, dtype, block in outs],
        scratch_shapes=scratches,
        input_output_aliases=aliases,
        compiler_params=pltpu.CompilerParams(vmem_limit_bytes=vmem_bytes),
        cost_estimate=pl.CostEstimate(
            flops=flops * 8, bytes_accessed=moved, transcendentals=transcendentals
        ),
    )(*operands)


def attention_forward(tokens, bias, w_qkv, w_proj, vectors):
    images, length, _ = bias.shape
    total, width = tokens.shape
    pairs = width // (2 * HEAD_DIM)
    rows = PER_STEP * length
    low, high = jnp.bfloat16, jnp.float32
    outs = [
        ((total, width), low, None),
        ((total, 3 * width), low, (rows, 3 * width)),
        ((images, pairs, length, 2 * length), low, (PER_STEP, pairs, length, 2 * length)),
        ((total, width), low, (rows, width)),
        ((total, width), high, (rows, width)),
    ]
    return call_kernel(
        attention_kernel, (images,), images // PER_STEP,
        [None, (PER_STEP, length, 1), None, None, None], outs,
        [scratch(width // 128, total, 128), scratch(rows, width, dtype=low)],
        (tokens, bias, w_qkv, w_proj, vectors),
        2 * total * width * 4 * width + 8 * total * length * width,
    )


def feed_forward(images, middle, cotangent, attended, w_up, w_down, w_proj, vectors):
    total, width = middle.shape
    hidden = w_up.shape[1]
    rows = total // images * PER_STEP
    low, high = jnp.bfloat16, jnp.float32
    block = (rows, width)
    outs = [
        ((total, width), low, None),
        ((total, width), high, block),
        ((total, width), low, block),
        ((width, hidden), low, None),
        ((hidden, width), low, None),
        ((width, width), low, None),
        ((8, width), high, None),
        ((1, hidden), high, None),
    ]
    scratches = [
        scratch(width // 128, total, 128),
        scratch(rows, width, dtype=low),
        scratch(width, rows, dtype=low),
        scratch(rows, width, dtype=low),
        scratch(width, rows, dtype=low),
        scratch(rows, width),
        scratch(rows, 128),
        scratch(rows, width),
        scratch(rows, width),
        scratch(width, hidden),
        scratch(width, hidden),
        scratch(width, width),
    ]
    return call_kernel(
        feed_forward_kernel, (images,), images // PER_STEP,
        [block, None, block, None, None, None, None, None], outs, scratches,
        (middle, cotangent, attended, w_up, w_down, w_proj, vectors, vectors[7:11].reshape(1, hidden)),
        12 * total * width * hidden + 4 * total * width * width, total * hidden,
    )


def attention_back(x, qkv, probs, d_attended, d_middle, w_qkv, vectors):
    images, pairs, length, _ = probs.shape
    total, width = x.shape
    rows = PER_STEP * length
    low, high = jnp.bfloat16, jnp.float32
    block = (rows, width)
    outs = [
        ((total, width), low, None),
        ((width, 3 * width), low, None),
        ((8, width), high, None),
    ]
    scratches = [
        scratch(width // 128, total, 128),
        scratch(rows, width, dtype=low),
        scratch(rows, 3 * width, dtype=low),
        scratch(rows, width),
        scratch(width, 3 * width),
    ]
    return call_kernel(
        attention_back_kernel, (images,), images // PER_STEP,
        [block, (rows, 3 * width), (PER_STEP, pairs, length, 2 * length), block, block, None, None],
        outs, scratches, (x, qkv, probs, d_attended, d_middle, w_qkv, vectors),
        4 * total * width * 3 * width + 16 * total * length * width,
    )

def linear_place():
    return lax.axis_index("dp") * lax.axis_size("group") + lax.axis_index("group")


def permute(array, mask):
    count = lax.axis_size("dp") * lax.axis_size("group")
    return lax.ppermute(array, ("dp", "group"), [(rank, rank ^ mask) for rank in range(count)])


def direct_masks(bits):
    masks = [0]
    for bit in bits:
        masks = masks + [mask | bit for mask in masks]
    return masks[1:]


def scatter_step(held, bits):
    masks = direct_masks(bits)
    size = held.shape[0] // (len(masks) + 1)
    parts = [
        permute(held[size * (at + 1) : size * (at + 2)].astype(jnp.bfloat16), mask)
        for at, mask in enumerate(masks)
    ]
    return held[:size], parts


def add_wide(first, *rest):
    total = first.astype(jnp.float32)
    for part in rest:
        total = total + part.astype(jnp.float32)
    return total


def packed_place(mask, spread, count):
    return ((mask >> 1) & (spread - 1)) * (count // (2 * spread)) + (mask >> (spread.bit_length()))


def scatter_step(held, bits):
    masks = direct_masks(bits)
    size = held.shape[0] // (len(masks) + 1)
    parts = [
        permute(held[size * (at + 1) : size * (at + 2)].astype(jnp.bfloat16), mask)
        for at, mask in enumerate(masks)
    ]
    return held[:size], parts


def add_wide(first, *rest):
    total = first.astype(jnp.float32)
    for part in rest:
        total = total + part.astype(jnp.float32)
    return total


def packed_place(mask, spread, count):
    return ((mask >> 1) & (spread - 1)) * (count // (2 * spread)) + (mask >> (spread.bit_length()))


def gather_step(held, bits):
    return held + [permute(part, mask) for mask in direct_masks(bits) for part in held]


def gathered_place(mask, count):
    return (mask & 1) * (count // 2) + ((mask >> 2) & 1) * (count // 4) + (mask >> 3) * 2 + ((mask >> 1) & 1)


def unpack(place_ref, block_refs, packed_ref, put, dp_size, spread):
    place = place_ref[0]
    size = block_refs[0].shape[0]
    for at, block_ref in enumerate(block_refs):
        packed_ref[at * size : (at + 1) * size] = block_ref[...]
    count = dp_size * spread
    for row in range(dp_size):
        for col in range(spread):
            put(row, col, packed_ref[gathered_place((row * spread + col) ^ place, count)])


def pack(place_ref, take, keep_ref, leave_ref, dp_size, spread):
    place = place_ref[0]
    odd = (place & 1) == 1
    for row in range(dp_size):
        for col in range(0, spread, 2):
            at = packed_place((row * spread + col) ^ place, spread, dp_size * spread)
            even_block, odd_block = take(row, col), take(row, col + 1)
            keep_ref[at] = jnp.where(odd, odd_block, even_block)
            leave_ref[at] = jnp.where(odd, even_block, odd_block)


def narrow_pieces(place_ref, wide_ref, piece_refs, spread):
    tiles, _, lanes = wide_ref.shape
    rows_of_piece = piece_refs[0].shape[0]
    step = 64
    group = place_ref[0] & (spread - 1)
    for relative, piece_ref in enumerate(piece_refs):
        base = (group ^ relative) * rows_of_piece

        @pl.loop(0, rows_of_piece // step)
        def _(part):
            target = pl.ds(pl.multiple_of(part * step, step), step)
            source = pl.ds(pl.multiple_of(base + part * step, step), step)
            for tile in range(tiles):
                cols = slice(tile * lanes, (tile + 1) * lanes)
                piece_ref[target, cols] = wide_ref[tile, source, :].astype(jnp.bfloat16)


def general_body(
    tokens,
    keep_mask,
    cotangent,
    qkv_weight,
    proj_weight,
    up_weight,
    down_weight,
    vectors,
    qkv_rows,
    qkv_cols,
    proj_rows,
    proj_cols,
    up_rows,
    up_cols,
    down_rows,
    down_cols,
    vector_moment,
):
    masters = (qkv_weight, proj_weight, up_weight, down_weight)
    lowered = tuple((master.astype(jnp.bfloat16) for master in masters))
    dp_bits, group_bits = axis_bits("dp"), axis_bits("group")
    gather_steps = dp_bits[1:] + group_bits[1:] + dp_bits[:1] + group_bits[:1]
    scatter_steps = gather_steps[::-1]
    w_qkv, w_proj, w_up, w_down = tuple(
        blocks_to_whole(gather_blocks(part, gather_steps), gather_steps) for part in lowered
    )
    spread = lax.axis_size("group")

    def slots_in(array):
        held, slots, width = array.shape
        parts = array.transpose(1, 0, 2).reshape(slots, spread, held // spread, width)
        parts = lax.all_to_all(
            parts.transpose(1, 0, 2, 3), "group", split_axis=0, concat_axis=0, tiled=True
        )
        return parts.reshape(spread * slots * (held // spread), width)

    def slots_out(array):
        held, slots, width = tokens.shape
        parts = array.reshape(spread, slots, held // spread, width)
        parts = lax.all_to_all(parts, "group", split_axis=0, concat_axis=0, tiled=True)
        return parts.transpose(1, 0, 2, 3).reshape(slots, held, width).transpose(1, 0, 2)

    images = keep_mask.shape[0]
    bias = jnp.where(keep_mask > 0, 0.0, -1e30)[:, :, None]
    x, qkv, probs, attended, middle = attention_forward(
        slots_in(tokens), bias, w_qkv, w_proj, vectors
    )
    output, d_middle, d_attended, up_grad, down_grad, proj_grad, ff_sums, up_sums = feed_forward(
        images, middle, slots_in(cotangent), attended, w_up, w_down, w_proj, vectors
    )
    block_output = slots_out(output)
    d_input, qkv_grad, att_sums = attention_back(
        x, qkv, probs, d_attended, d_middle, w_qkv, vectors
    )
    input_grad = slots_out(d_input)
    local_vectors = jnp.concatenate(
        [att_sums[:4], ff_sums[:3], up_sums.reshape(4, -1), ff_sums[3:4]], axis=0
    )
    vector_grad = sum_everywhere(local_vectors, group_bits + dp_bits)
    local_grads = (qkv_grad, proj_grad, up_grad, down_grad)
    owned = tuple(
        scatter_sum(whole_to_blocks(part, scatter_steps), scatter_steps) for part in local_grads
    )
    squares = tuple((gradient * gradient + tiny_square for gradient in owned))
    row_parts = tuple((jnp.sum(square, axis=1) for square in squares)) + tuple(
        (jnp.sum(master * master, axis=1) for master in masters)
    )
    row_sums = sum_parts(row_parts, group_bits)
    rows_old = (qkv_rows, proj_rows, up_rows, down_rows)
    cols_old = (qkv_cols, proj_cols, up_cols, down_cols)
    total_cols = tuple((gradient.shape[1] * lax.axis_size("group") for gradient in owned))
    total_rows = tuple((gradient.shape[0] * lax.axis_size("dp") for gradient in owned))
    rows_new = tuple(
        (
            decay_rate * rows_old[which] + (1.0 - decay_rate) * row_sums[which] / total_cols[which]
            for which in range(4)
        )
    )
    col_parts = (
        tuple((jnp.sum(square, axis=0) for square in squares))
        + tuple((jnp.sum(row_stat) for row_stat in rows_new))
        + tuple((jnp.sum(row_sums[4 + which]) for which in range(4)))
    )
    col_sums = sum_parts(col_parts, dp_bits)
    results = []
    for which in range(4):
        cols_new = (
            decay_rate * cols_old[which] + (1.0 - decay_rate) * col_sums[which] / total_rows[which]
        )
        mean_rows = col_sums[4 + which] / total_rows[which]
        spread = jnp.sqrt(col_sums[8 + which] / (total_rows[which] * total_cols[which]))
        second = rows_new[which][:, None] * cols_new[None, :] / mean_rows
        updated = masters[which] - step_rate * spread * owned[which] * lax.rsqrt(second)
        results.append((owned[which], rows_new[which], cols_new, updated))
    vector_moment_new = decay_rate * vector_moment + (1.0 - decay_rate) * (
        vector_grad * vector_grad + tiny_square
    )
    row_spread = jnp.sqrt(jnp.mean(vectors * vectors, axis=1, keepdims=True))
    vector_new = vectors - step_rate * row_spread * vector_grad * lax.rsqrt(vector_moment_new)
    return (
        block_output,
        input_grad,
        results[0][0],
        results[0][1],
        results[0][2],
        results[0][3],
        results[1][0],
        results[1][1],
        results[1][2],
        results[1][3],
        results[2][0],
        results[2][1],
        results[2][2],
        results[2][3],
        results[3][0],
        results[3][1],
        results[3][2],
        results[3][3],
        vector_grad,
        vector_moment_new,
        vector_new,
    )


def first_attention_kernel(images, dp_size, spread, place_ref, tokens_ref, *refs):
    blocks, refs = refs[:4], refs[4:]
    keep_ref, vectors_ref, *outs, x_ref, w_qkv_ref, w_proj_ref = refs[:-4]
    packed_ref, wide_ref, bias_ref, normed_ref = refs[-4:]
    rows = packed_ref.shape[1]
    qkv_cols, proj_cols = w_qkv_ref.shape[1] // spread, w_proj_ref.shape[1] // spread

    @pl.when(pl.program_id(0) == 0)
    def _():
        widen(tokens_ref, wide_ref, images)
        to_image_rows(wide_ref, x_ref, images)

        def put(row, col, block):
            down = slice(row * rows, (row + 1) * rows)
            w_qkv_ref[down, col * qkv_cols : (col + 1) * qkv_cols] = block[:, :qkv_cols]
            w_proj_ref[down, col * proj_cols : (col + 1) * proj_cols] = block[:, qkv_cols:]

        unpack(place_ref, blocks, packed_ref, put, dp_size, spread)

    attention_part(0, x_ref, keep_ref, w_qkv_ref, w_proj_ref, vectors_ref, *outs, bias_ref, normed_ref)


def next_attention_kernel(start, x_ref, keep_ref, w_qkv_ref, w_proj_ref, vectors_ref, *refs):
    attention_part(start, x_ref, keep_ref, w_qkv_ref, w_proj_ref, vectors_ref, *refs[-6:])


def attention_part(
    start, x_ref, keep_ref, w_qkv_ref, w_proj_ref, vectors_ref,
    qkv_ref, probs_ref, attended_ref, middle_ref, bias_ref, normed_ref,
):
    @pl.when(pl.program_id(0) == 0)
    def _():
        bias_ref[...] = jnp.where(keep_ref[...] > 0, 0.0, -1e30).T

    def bias_column(image):
        here = start + pl.program_id(0) * probs_ref.shape[0] + image
        lane = lax.broadcasted_iota(jnp.int32, bias_ref.shape, 1)
        return row_sum(jnp.where(lane == here, bias_ref[...], 0.0))

    attention_steps(
        x_ref, bias_column, w_qkv_ref, w_proj_ref, vectors_ref,
        qkv_ref, probs_ref, attended_ref, middle_ref, normed_ref,
    )


def feed_forward_packed_kernel(images, dp_size, spread, place_ref, *refs):
    cotangent_ref, blocks, refs = refs[0], refs[1:5], refs[5:]
    middle_ref, attended_ref, w_proj_ref, vectors_ref, output_ref = refs[:5]
    refs = refs[5:]
    d_middle_ref, d_attended_ref, keep_ref, leave_ref, vector_sums_ref, up_sums_ref = refs[:6]
    w_up_ref, w_down_ref, down_low_ref, packed_ref, bias_up_ref, wide_ref = refs[6:12]
    scratches = refs[12:]
    width = w_up_ref.shape[0]
    up_total_ref, down_total_ref, proj_total_ref = scratches[-3:]
    rows = packed_ref.shape[1]
    up_cols = w_up_ref.shape[1] // spread
    out_cols = w_down_ref.shape[1] // spread
    folds = w_down_ref.shape[0] // w_up_ref.shape[0]

    @pl.when(pl.program_id(0) == 0)
    def _():
        widen(cotangent_ref, wide_ref, images)
        for fold in range(bias_up_ref.shape[1] // width):
            bias_up_ref[:, fold * width : (fold + 1) * width] = vectors_ref[7 + fold : 8 + fold]

        def put(row, col, block):
            w_up_ref[row * rows : (row + 1) * rows, col * up_cols : (col + 1) * up_cols] = block[:, :up_cols]
            for fold in range(folds):
                down = (row * folds + fold) * rows
                start = up_cols + fold * out_cols
                w_down_ref[down : down + rows, col * out_cols : (col + 1) * out_cols] = block[
                    :, start : start + out_cols
                ]

        unpack(place_ref, blocks, packed_ref, put, dp_size, spread)

    feed_forward_steps(
        images, middle_ref, attended_ref, w_up_ref, w_down_ref, w_proj_ref, vectors_ref, bias_up_ref,
        d_middle_ref, d_attended_ref, vector_sums_ref, up_sums_ref, wide_ref, *scratches,
    )

    @pl.when(pl.program_id(0) == pl.num_programs(0) - 1)
    def _():
        narrow(wide_ref, output_ref, images)
        down_low_ref[...] = down_total_ref[...].T.astype(jnp.bfloat16)

        def take(row, col):
            across = slice(row * rows, (row + 1) * rows)
            cols = slice(col * out_cols, (col + 1) * out_cols)
            parts = [up_total_ref[across, col * up_cols : (col + 1) * up_cols].astype(jnp.bfloat16)]
            for fold in range(folds):
                down = (row * folds + fold) * rows
                parts.append(down_low_ref[down : down + rows, cols])
            parts.append(proj_total_ref[across, cols].astype(jnp.bfloat16))
            return jnp.concatenate(parts, axis=1)

        pack(place_ref, take, keep_ref, leave_ref, dp_size, spread)


def first_back_kernel(
    x_ref, qkv_ref, probs_ref, d_attended_ref, d_middle_ref, w_qkv_ref, vectors_ref, *refs
):
    d_input_ref, total_ref, vector_sums_ref, *scratches = refs[-6:]

    @pl.when(pl.program_id(0) == 0)
    def _():
        total_ref[...] = jnp.zeros_like(total_ref)
        vector_sums_ref[...] = jnp.zeros_like(vector_sums_ref)

    def put(image, rows, values):
        d_input_ref[rows, :] = values.astype(jnp.bfloat16)

    attention_back_steps(
        put, x_ref, qkv_ref, probs_ref, d_attended_ref, d_middle_ref, w_qkv_ref, vectors_ref,
        vector_sums_ref, *scratches, total_ref,
    )


def last_back_kernel(
    images, dp_size, spread, first, place_ref, x_ref, qkv_ref, probs_ref, d_attended_ref, d_middle_ref, w_qkv_ref,
    vectors_ref, d_input_ref, before_ref, sums_before_ref, *refs,
):
    refs = refs[-(spread + 8) :]
    pieces, (keep_ref, leave_ref, vector_sums_ref, wide_ref, *scratches) = refs[:spread], refs[spread:]
    total_ref = scratches[-1]
    length = d_input_ref.shape[0] // images

    @pl.when(pl.program_id(0) == 0)
    def _():
        total_ref[...] = before_ref[...]
        vector_sums_ref[...] = sums_before_ref[...]

        @pl.loop(0, first)
        def _(image):
            rows = pl.ds(pl.multiple_of(image * length, length), length)
            put_image(wide_ref, image, images, d_input_ref[rows, :].astype(jnp.float32))

    def put(image, rows, values):
        put_image(wide_ref, first + image, images, values)

    attention_back_steps(
        put, x_ref, qkv_ref, probs_ref, d_attended_ref, d_middle_ref, w_qkv_ref, vectors_ref,
        vector_sums_ref, *scratches,
    )

    @pl.when(pl.program_id(0) == pl.num_programs(0) - 1)
    def _():
        narrow_pieces(place_ref, wide_ref, pieces, spread)
        rows, cols = keep_ref.shape[1:]

        def take(row, col):
            block = total_ref[row * rows : (row + 1) * rows, col * cols : (col + 1) * cols]
            return block.astype(jnp.bfloat16)

        pack(place_ref, take, keep_ref, leave_ref, dp_size, spread)


def cut(array_ref, parts_ref):
    count = parts_ref.shape[2]
    for member in range(parts_ref.shape[0]):
        parts_ref[member] = array_ref[:, member * count : (member + 1) * count, :]


def pack_kernel(qkv_ref, proj_ref, up_ref, down_ref, pack_ref):
    rows, start = pack_ref.shape[0], 0
    parts = [qkv_ref[...], proj_ref[...], up_ref[...]]
    parts += [down_ref[fold * rows : (fold + 1) * rows, :] for fold in range(down_ref.shape[0] // rows)]
    for part in parts:
        pack_ref[:, start : start + part.shape[1]] = part.astype(jnp.bfloat16)
        start += part.shape[1]


def token_kernel(array_ref, own_ref, arrived_ref, parts_ref, pair_ref):
    cols = pair_ref.shape[2]
    pair_ref[0] = own_ref[:, :cols]
    pair_ref[1] = arrived_ref[:, :cols]
    cut(array_ref, parts_ref)


def cotangent_kernel(array_ref, own_ref, arrived_ref, _, parts_ref, pair_ref):
    start = own_ref.shape[1] - pair_ref.shape[2]
    pair_ref[0] = own_ref[:, start:]
    pair_ref[1] = arrived_ref[:, start:]
    cut(array_ref, parts_ref)


def join_kernel(count, *refs):
    parts, joined_ref = refs[:count], refs[-1]
    size = parts[0].shape[0]
    for at, part_ref in enumerate(parts):
        joined_ref[at * size : (at + 1) * size] = part_ref[...]


def settle_whole_kernel(parts_ref, output_ref):
    count = parts_ref.shape[2]
    for member in range(parts_ref.shape[0]):
        output_ref[:, member * count : (member + 1) * count, :] = parts_ref[member]


def settle_kernel(spread, place_ref, *refs):
    lists, output_ref = refs[:-1], refs[-1]
    group = place_ref[0] & (spread - 1)
    count = lists[0].shape[1]
    share = len(lists) // spread * count
    for at, piece_ref in enumerate(lists):
        relative, part = at % spread, at // spread
        start = pl.multiple_of((group ^ relative) * share + part * count, count)
        output_ref[:, pl.ds(start, count), :] = piece_ref[...]


def lane_table(rows, columns):
    lane = lax.broadcasted_iota(jnp.int32, (rows, 128), 1)
    table = jnp.zeros((rows, 128), jnp.float32)
    for at, column in enumerate(columns):
        table = jnp.where(lane == at, column, table)
    return table


def added(parts):
    while len(parts) > 1:
        parts = [sum(parts[at : at + 2][1:], parts[at]) for at in range(0, len(parts), 2)]
    return parts[0]


def row_sum(values):
    return jnp.sum(values, axis=1, keepdims=True)


def gradient_kernel(count, *refs):
    block_parts, sums, refs = refs[:count], refs[count : count + 3], refs[count + 3 :]
    masters, rows_old, refs = refs[:4], refs[4:8], refs[8:]
    grads, (row_ref, message_ref) = refs[:4], refs[4:]
    blocks = added([part[0].astype(jnp.float32) for part in block_parts])
    rows, up_cols = grads[2].shape
    qkv_cols, out_cols = grads[0].shape[1], grads[1].shape[1]
    folds = grads[3].shape[0] // rows
    up = blocks[:, :up_cols]
    downs = [blocks[:, up_cols + fold * out_cols :][:, :out_cols] for fold in range(folds)]
    start = up_cols + folds * out_cols
    proj = blocks[:, start : start + out_cols]
    qkv = blocks[:, start + out_cols :]
    grads[0][...] = qkv
    grads[1][...] = proj
    grads[2][...] = up
    for fold in range(folds):
        grads[3][fold * rows : (fold + 1) * rows, :] = downs[fold]
    squares = [part * part + tiny_square for part in (qkv, proj, up, *downs)]
    row_ref[...] = lane_table(rows, [row_sum(square) for square in squares]).T[: row_ref.shape[0], :]
    width = message_ref.shape[1]
    message_ref[...] = jnp.zeros_like(message_ref)
    for at, square in enumerate((*squares[:3], added(squares[3:]))):
        message_ref[at : at + 1, : square.shape[1]] = column_sum(square)
    scalars = [column_sum(row_sum(master[...] * master[...])) for master in masters]
    scalars += [row_sum(part[...].reshape(1, part.shape[0])) for part in rows_old]
    message_ref[4:5, :128] = lane_table(1, scalars)
    att_ref, ff_ref, up_ref = sums
    count = up_ref.shape[1] // width
    message_ref[8:12, :] = att_ref[:4]
    message_ref[12:15, :] = ff_ref[:3]
    for at in range(count):
        message_ref[15 + at : 16 + at, :] = up_ref[:, at * width : (at + 1) * width]
    message_ref[15 + count : 16 + count, :] = ff_ref[3:4]


def column_kernel(row_ref, *refs):
    parts, (cols_ref, message_ref) = refs[:-2], refs[-2:]
    total = added([part[...] for part in parts])
    cols_ref[...] = total[:8]
    width = total.shape[1]
    rows = row_ref.shape[1]
    message_ref[...] = jnp.zeros_like(message_ref)
    message_ref[:8, :rows] = row_ref[...]
    columns = [row_sum(total[which : which + 1]) for which in range(4)]
    squares = [total[4:5, which : which + 1] for which in range(4)]
    message_ref[8:9, :] = lane_table(1, columns + squares)
    for tile in range(width // 128):
        message_ref[16 * (tile + 1) : 16 * (tile + 2), :] = total[8:, tile * 128 : (tile + 1) * 128]


def update_kernel(count, heights, widths, *refs):
    messages, refs = refs[:count], refs[count:]
    cols_ref, vectors_ref, moment_ref, refs = refs[0], refs[1], refs[2], refs[3:]
    grads, masters, rows_old, cols_old, refs = refs[:4], refs[4:8], refs[8:12], refs[12:16], refs[16:]
    news, cols_new, rows_out, refs = refs[:4], refs[4:8], refs[8:12], refs[12:]
    vector_grad_ref, moment_new_ref, vector_new_ref = refs
    sums = added([message[...] for message in messages])
    height = grads[0].shape[0]
    folds = grads[3].shape[0] // height
    lanes = [[0], [1], [2], list(range(3, 3 + folds))]
    share = 1.0 - decay_rate
    for which in range(4):
        entries = heights[which] * widths[which]
        cols = cols_old[which].shape[0]
        new = decay_rate * cols_old[which][...].reshape(1, cols) + share / heights[which] * cols_ref[
            which : which + 1, :cols
        ]
        cols_new[which][...] = new[0]
        old_total = cols_ref[4:5, 4 + which : 5 + which]
        mean_rows = (decay_rate * old_total + share / widths[which] * sums[8:9, which : which + 1]) / heights[which]
        rate = step_rate * jnp.sqrt(sums[8:9, 4 + which : 5 + which] / entries)
        across = new / mean_rows
        old = rows_old[which][...].reshape(1, len(lanes[which]) * height)
        row_sums = jnp.concatenate([sums[lane : lane + 1, :height] for lane in lanes[which]], axis=1)
        row = decay_rate * old + share / widths[which] * row_sums
        rows_out[which][...] = row[0]
        for fold in range(len(lanes[which])):
            part = slice(fold * height, (fold + 1) * height)
            column = jnp.broadcast_to(row[:, part], (8, height)).T[:, :1]
            news[which][part, :] = masters[which][part, :] - rate * grads[which][part, :] * lax.rsqrt(column * across)
    vectors = vectors_ref[...]
    count = vectors.shape[0]
    gradient = jnp.concatenate(
        [sums[16 * (tile + 1) : 16 * (tile + 1) + count] for tile in range(vectors.shape[1] // 128)], axis=1
    )
    vector_grad_ref[...] = gradient
    moment = decay_rate * moment_ref[...] + share * (gradient * gradient + tiny_square)
    moment_new_ref[...] = moment
    spread = jnp.sqrt(jnp.mean(vectors * vectors, axis=1, keepdims=True))
    vector_new_ref[...] = vectors - step_rate * spread * gradient * lax.rsqrt(moment)


def packed_body(
    tokens, keep_mask, cotangent, qkv_weight, proj_weight, up_weight, down_weight, vectors,
    qkv_rows, qkv_cols, proj_rows, proj_cols, up_rows, up_cols, down_rows, down_cols, vector_moment,
):
    spread, dp_size = lax.axis_size("group"), lax.axis_size("dp")
    low, high = jnp.bfloat16, jnp.float32
    place = linear_place().astype(jnp.int32).reshape(1)
    group = lax.axis_index("group")
    held, slots, width = tokens.shape
    images, length = keep_mask.shape
    hidden = up_weight.shape[1] * spread
    total = images * length
    rows = qkv_weight.shape[0]
    folds = down_weight.shape[0] // rows
    core_bits = (1,)
    near_bits = tuple(1 << at for at in range(1, spread.bit_length()))
    far_bits = tuple(spread << at for at in range(1, dp_size.bit_length() - 1))
    half = spread * dp_size // 2

    anywhere = pl.BlockSpec(memory_space=pl.ANY)
    in_smem = pl.BlockSpec(memory_space=pltpu.SMEM)

    in_vmem = pl.BlockSpec(memory_space=pltpu.VMEM)
    small = functools.partial(
        pl.pallas_call, compiler_params=pltpu.CompilerParams(vmem_limit_bytes=vmem_bytes)
    )
    masters = (qkv_weight, proj_weight, up_weight, down_weight)
    parted = jax.ShapeDtypeStruct((spread, slots, images, width), low)

    def to_group(parts):
        return lax.all_to_all(parts, "group", split_axis=0, concat_axis=0, tiled=True)

    def to_images(parts):
        return to_group(parts).reshape(total, width)

    def exchange(parts):
        return [parts[0]] + [permute(part, relative) for relative, part in enumerate(parts) if relative]

    def settle_whole(parts):
        whole = small(settle_whole_kernel, out_shape=jax.ShapeDtypeStruct((slots, held, width), low))(parts)
        return whole.transpose(1, 0, 2)

    def settle(parts):
        parts = [part.reshape(slots, -1, width) for part in parts]
        whole = small(
            functools.partial(settle_kernel, spread),
            in_specs=[in_smem] + [in_vmem] * len(parts),
            out_specs=in_vmem,
            out_shape=jax.ShapeDtypeStruct((slots, held, width), low),
        )(place, *parts)
        return whole.transpose(1, 0, 2)

    first_cols = qkv_weight.shape[1] + proj_weight.shape[1]
    second_cols = up_weight.shape[1] + folds * down_weight.shape[1]
    pack_own = small(pack_kernel, out_shape=jax.ShapeDtypeStruct((rows, first_cols + second_cols), low))(*masters)
    across_y, across_x = near_bits
    pack_arrived = permute(pack_own, across_y)
    token_cut, first_pair = small(
        token_kernel,
        out_shape=[parted, jax.ShapeDtypeStruct((2, rows, first_cols), low)],
    )(tokens.transpose(1, 0, 2), pack_own, pack_arrived)
    inputs = to_images(token_cut)

    def gather_far(pair):
        return [pair] + [permute(pair, mask) for mask in direct_masks(far_bits)]

    def join(parts, awaited=()):
        count = len(parts) * parts[0].shape[0]
        return small(
            functools.partial(join_kernel, len(parts)),
            in_specs=[in_vmem] * len(parts) + [anywhere] * len(awaited),
            out_shape=jax.ShapeDtypeStruct((count, *parts[0].shape[1:]), low),
        )(*parts, *awaited)

    def gather_rest(held):
        arrived = permute(held, across_x)
        return [held, arrived, permute(held, core_bits[0]), permute(arrived, core_bits[0])]

    first_far = join(gather_far(first_pair))
    cotangent_cut, second_pair = small(
        cotangent_kernel,
        in_specs=[in_vmem] * 3 + [anywhere],
        out_shape=[parted, jax.ShapeDtypeStruct((2, rows, second_cols), low)],
    )(cotangent.transpose(1, 0, 2), pack_own, pack_arrived, first_far)
    upstream = to_images(cotangent_cut)
    first_blocks = gather_rest(first_far)
    second_far = gather_far(second_pair)

    step_rows = PER_STEP * length
    block = (step_rows, width)
    pairs = width // (2 * HEAD_DIM)
    steps = images // PER_STEP
    statics = (images, dp_size, spread)
    wide = scratch(width // 128, total, 128)
    probs_block = (PER_STEP, pairs, length, 2 * length)
    attention_outs = [
        ((total, 3 * width), low, (step_rows, 3 * width)),
        ((images, *probs_block[1:]), low, probs_block),
        ((total, width), low, block),
        ((total, width), high, block),
    ]
    attention_flops = (2 * total * width * 4 * width + 8 * total * length * width) // steps
    attention_scratches = [scratch(length, images), scratch(step_rows, width, dtype=low)]
    *attention, x, w_qkv, w_proj = call_kernel(
        first_attention_kernel, statics, 1,
        ["place"] + [None] * 7,
        attention_outs
        + [
            ((total, width), low, None),
            ((width, 3 * width), low, None),
            ((width, width), low, None),
        ],
        [scratch(dp_size * spread, rows, first_cols, dtype=low), wide] + attention_scratches,
        (place, inputs, *first_blocks, keep_mask, vectors),
        attention_flops,
    )
    second_blocks = gather_rest(join(second_far, attention[:1]))
    for first_step, count in ((1, steps - 2), (steps - 1, 1)):
        attention = call_kernel(
            next_attention_kernel, (first_step * PER_STEP,), count,
            [block] + [None] * 4 + ["await"] * len(attention),
            attention_outs, attention_scratches,
            (x, keep_mask, w_qkv, w_proj, vectors, *attention),
            attention_flops * count, first_step=first_step,
            aliases={5 + at: at for at in range(len(attention))},
        )
    qkv, probs, attended, middle = attention
    piece = ((slots * images, width), low, None)
    pack_cols = up_weight.shape[1] + (folds + 1) * proj_weight.shape[1]
    results = call_kernel(
        feed_forward_packed_kernel, statics, steps,
        ["place"] + [None] * 5 + [block, block] + [None] * 2,
        [
            ((total, width), low, None),
            ((total, width), high, block),
            ((total, width), low, block),
            ((half, rows, pack_cols), low, None),
            ((half, rows, pack_cols), low, None),
            ((8, width), high, None),
            ((1, hidden), high, None),
        ],
        [
            scratch(width, hidden, dtype=low),
            scratch(hidden, width, dtype=low),
            scratch(hidden, width, dtype=low),
            scratch(dp_size * spread, rows, second_cols, dtype=low),
            scratch(1, hidden),
            wide,
            scratch(step_rows, width, dtype=low),
            scratch(width, step_rows, dtype=low),
            scratch(step_rows, width, dtype=low),
            scratch(width, step_rows, dtype=low),
            scratch(step_rows, width),
            scratch(step_rows, 128),
            scratch(step_rows, width),
            scratch(step_rows, width),
            scratch(width, hidden),
            scratch(width, hidden),
            scratch(width, width),
        ],
        (
            place, upstream, *second_blocks, middle, attended, w_proj, vectors,
        ),
        12 * total * width * hidden + 4 * total * width * width, total * hidden,
    )
    output, d_middle, d_attended, ff_keep, ff_leave, ff_sums, up_sums = results
    output = to_group(output.reshape(parted.shape))
    ff_first = permute(ff_leave, core_bits[0])
    ff_quarter = half // 4
    ff_parts = [
        add_wide(ff_keep[at : at + ff_quarter], ff_first[at : at + ff_quarter]).astype(low)
        for at in range(ff_quarter, half, ff_quarter)
    ]
    near_masks = direct_masks(near_bits)
    ff_near = [permute(part, mask) for part, mask in zip(ff_parts, near_masks)]
    back_ins = [block, (step_rows, 3 * width), probs_block, block, block, None, None]
    back_scratches = [
        scratch(step_rows, width, dtype=low),
        scratch(step_rows, 3 * width, dtype=low),
        scratch(step_rows, width),
    ]
    back_flops = (4 * total * width * 3 * width + 16 * total * length * width) // steps
    back_operands = (x, qkv, probs, d_attended, d_middle, w_qkv, vectors)
    d_input, qkv_total, att_sums = call_kernel(
        first_back_kernel, (), steps - 1, back_ins + ["await"] * len(ff_parts),
        [((total, width), low, block), ((width, 3 * width), high, None), ((8, width), high, None)],
        back_scratches, (*back_operands, *ff_parts), back_flops * (steps - 1),
    )
    qkv_pack = ((half, rows, qkv_weight.shape[1]), low, None)
    results = call_kernel(
        last_back_kernel, (*statics, (steps - 1) * PER_STEP), 1,
        ["place"] + back_ins + [None] * 3 + ["await"] * (len(ff_near) + 1),
        [piece] * spread + [qkv_pack, qkv_pack, ((8, width), high, None)],
        [wide] + back_scratches + [scratch(width, 3 * width)],
        (place, *back_operands, d_input, qkv_total, att_sums, *ff_near, output),
        back_flops, first_step=steps - 1,
    )
    qkv_keep, qkv_leave, att_sums = results[spread:]
    qkv_held = add_wide(qkv_keep, permute(qkv_leave, core_bits[0]))
    input_parts = exchange(results[:spread])
    qkv_held, qkv_parts = scatter_step(qkv_held, near_bits)
    ff_held = add_wide(ff_keep[:ff_quarter], ff_first[:ff_quarter], *ff_near)
    qkv_held = add_wide(qkv_held, *qkv_parts)
    blocks, block_parts = scatter_step(jnp.concatenate([ff_held, qkv_held], axis=2), far_bits)
    block_parts = [blocks] + block_parts

    heights = [master.shape[0] * dp_size for master in masters]
    widths = [master.shape[1] * spread for master in masters]
    rows_old, cols_old = [qkv_rows, proj_rows, up_rows, down_rows], [qkv_cols, proj_cols, up_cols, down_cols]

    def like(*arrays):
        return [jax.ShapeDtypeStruct(array.shape, high) for array in arrays]

    *grads, row_sums, message = small(
        functools.partial(gradient_kernel, len(block_parts)),
        out_shape=like(*masters) + [jax.ShapeDtypeStruct((8, rows), high), jax.ShapeDtypeStruct((24, width), high)],
    )(*block_parts, att_sums, ff_sums, up_sums, *masters, *rows_old)
    message = message + permute(message, across_x)
    messages = [message] + [permute(message, mask) for mask in direct_masks(far_bits)]
    col_sums, message = small(
        column_kernel,
        out_shape=[
            jax.ShapeDtypeStruct((8, width), high),
            jax.ShapeDtypeStruct((16 + width // 8, 128), high),
        ],
    )(row_sums, *messages)
    messages = [message] + [permute(message, mask) for mask in range(1, spread)]
    results = small(
        functools.partial(update_kernel, len(messages), heights, widths),
        out_shape=like(*masters, *cols_old, *rows_old, vectors, vectors, vectors),
    )(*messages, col_sums, vectors, vector_moment, *grads, *masters, *rows_old, *cols_old)
    news, cols_new, rows_out = results[:4], results[4:8], results[8:12]
    vector_grad, vector_moment_new, vector_new = results[12:]
    factored = []
    for which in range(4):
        factored += [grads[which], rows_out[which], cols_new[which], news[which]]
    return (settle_whole(output), settle(input_parts), *factored, vector_grad, vector_moment_new, vector_new)


def body(*arrays):
    spread, dp_size = lax.axis_size("group"), lax.axis_size("dp")
    rows, images = arrays[3].shape[0], arrays[1].shape[0]
    slots, width = arrays[0].shape[1:]
    folds = arrays[6].shape[0] // rows
    powers = all(size & (size - 1) == 0 for size in (spread, dp_size))
    fits = powers and spread == 4 and dp_size > 2
    fits = fits and arrays[5].shape[1] <= width and folds <= 5
    fits = fits and rows % 16 == 0 and images % PER_STEP == 0 and images > 2 * PER_STEP and images % 16 == 0 and slots % 4 == 0
    return packed_body(*arrays) if fits else general_body(*arrays)


def solution(mesh):
    in_specs = (
        P("dp", "group", None),
        P(("dp", "group"), None),
        P("dp", "group", None),
        P("dp", "group"),
        P("dp", "group"),
        P("dp", "group"),
        P("dp", "group"),
        P(),
        P("dp"),
        P("group"),
        P("dp"),
        P("group"),
        P("dp"),
        P("group"),
        P("dp"),
        P("group"),
        P(),
    )
    out_specs = (
        P("dp", "group", None),
        P("dp", "group", None),
        P("dp", "group"),
        P("dp"),
        P("group"),
        P("dp", "group"),
        P("dp", "group"),
        P("dp"),
        P("group"),
        P("dp", "group"),
        P("dp", "group"),
        P("dp"),
        P("group"),
        P("dp", "group"),
        P("dp", "group"),
        P("dp"),
        P("group"),
        P("dp", "group"),
        P(),
        P(),
        P(),
    )
    return jax.shard_map(body, mesh=mesh, in_specs=in_specs, out_specs=out_specs, check_vma=False)
```

```python
import functools
import math

import jax
import jax.numpy as jnp
from jax import lax
from jax.experimental import pallas as pl
from jax.experimental.pallas import tpu as pltpu
from jax.sharding import PartitionSpec as P

HEAD_DIM = 64
STEP_NUMBER = 10


step_rate = 0.3
norm_epsilon = 1e-06
tiny_square = 1e-30
decay_rate = 1.0 - STEP_NUMBER ** (-0.8)
LOG2_E = 1.4426950408889634


def axis_bits(name):
    count = lax.axis_size(name)
    return [(name, 1 << place) for place in range(count.bit_length() - 1)]


def swap_partner(array, step):
    name, bit = step
    count = lax.axis_size(name)
    return lax.ppermute(array, name, [(rank, rank ^ bit) for rank in range(count)])


def upper_side(step):
    name, bit = step
    return (lax.axis_index(name) & bit) != 0


def gather_blocks(array, steps):
    for step in steps:
        arrived = swap_partner(array, step)
        upper = upper_side(step)
        array = jnp.stack([jnp.where(upper, arrived, array), jnp.where(upper, array, arrived)])
    return array


def scatter_sum(array, steps):
    for step in steps:
        upper = upper_side(step)
        leaving = jnp.where(upper, array[0], array[1]).astype(jnp.bfloat16)
        arrived = swap_partner(leaving, step)
        array = jnp.where(upper, array[1], array[0]).astype(jnp.float32) + arrived.astype(jnp.float32)
    return array


def sum_everywhere(array, steps):
    for step in steps:
        array = array + swap_partner(array, step)
    return array


def sum_parts(parts, steps):
    flat = [part.reshape(-1) for part in parts]
    total = sum_everywhere(jnp.concatenate(flat), steps)
    result, start = [], 0
    for part in parts:
        result.append(total[start : start + part.size].reshape(part.shape))
        start += part.size
    return result


def block_order(steps):
    order = []
    for name in ("dp", "group"):
        bits = sorted((step for step in steps if step[0] == name), key=lambda step: -step[1])
        order.append([steps.index(step) for step in bits])
    return order


def blocks_to_whole(blocks, steps):
    count = len(steps)
    rows, cols = blocks.shape[count:]
    dp_axes, group_axes = block_order(steps)
    dp_axes = [count - 1 - axis for axis in dp_axes]
    group_axes = [count - 1 - axis for axis in group_axes]
    whole = blocks.transpose(dp_axes + [count] + group_axes + [count + 1])
    return whole.reshape(rows << len(dp_axes), cols << len(group_axes))


def whole_to_blocks(whole, steps):
    dp_axes, group_axes = block_order(steps)
    rows = whole.shape[0] >> len(dp_axes)
    cols = whole.shape[1] >> len(group_axes)
    split = whole.reshape([2] * len(dp_axes) + [rows] + [2] * len(group_axes) + [cols])
    places = dp_axes + [len(steps)] + group_axes + [len(steps) + 1]
    return split.transpose([places.index(axis) for axis in range(len(places))])


PER_STEP = 4
FF_CHUNK = 256
vmem_bytes = 60 * 1024 * 1024


def dot(left, right, left_axis=1, right_axis=0):
    return lax.dot_general(
        left, right, (((left_axis,), (right_axis,)), ((), ())), preferred_element_type=jnp.float32
    )


def normal_form(values):
    center = jnp.mean(values, axis=-1, keepdims=True)
    centered = values - center
    spread = jnp.mean(centered * centered, axis=-1, keepdims=True)
    scale = lax.rsqrt(spread + norm_epsilon)
    return centered * scale, scale


def norm_back(grad, unit, scale, gain):
    weighted = grad * gain
    along = jnp.mean(weighted * unit, axis=-1, keepdims=True)
    level = jnp.mean(weighted, axis=-1, keepdims=True)
    return scale * (weighted - level - unit * along)


def column_sum(values):
    return jnp.sum(values, axis=0, keepdims=True)


def pair_mask(length):
    return lax.broadcasted_iota(jnp.int32, (length, 2 * HEAD_DIM), 1) < HEAD_DIM


def stack_heads(pair, first):
    none = jnp.zeros_like(pair)
    return jnp.concatenate([jnp.where(first, pair, none), jnp.where(first, none, pair)], axis=0)


def join_heads(rows, first):
    length = rows.shape[0] // 2
    return jnp.where(first, rows[:length], rows[length:])


def gelu_and_slope(pre):
    bell = jnp.exp2(pre * pre * (-0.5 * LOG2_E))
    inverse = 1.0 / (1.0 + (0.3275911 * 0.5**0.5) * jnp.abs(pre))
    poly = inverse * (
        0.5 * 0.254829592
        + inverse
        * (
            0.5 * -0.284496736
            + inverse
            * (0.5 * 1.421413741 + inverse * (0.5 * -1.453152027 + inverse * (0.5 * 1.061405429)))
        )
    )
    tail = poly * bell
    below = jnp.where(pre >= 0, 1.0 - tail, tail)
    return pre * below, below + pre * bell * 0.3989422804014327


def widen(source_ref, wide_ref, images):
    tiles, total, lanes = wide_ref.shape
    rows_at_once = 8 * images

    @pl.loop(0, total // rows_at_once)
    def _(part):
        rows = pl.ds(pl.multiple_of(part * rows_at_once, rows_at_once), rows_at_once)
        for tile in range(tiles):
            cols = slice(tile * lanes, (tile + 1) * lanes)
            wide_ref[tile, rows, :] = source_ref[rows, cols].astype(jnp.float32)


def narrow(wide_ref, target_ref, images):
    tiles, total, lanes = wide_ref.shape
    rows_at_once = 8 * images

    @pl.loop(0, total // rows_at_once)
    def _(part):
        rows = pl.ds(pl.multiple_of(part * rows_at_once, rows_at_once), rows_at_once)
        for tile in range(tiles):
            cols = slice(tile * lanes, (tile + 1) * lanes)
            target_ref[rows, cols] = wide_ref[tile, rows, :].astype(target_ref.dtype)


def take_image(wide_ref, image, images):
    tiles, total, _ = wide_ref.shape
    rows = pl.ds(image, total // images, images)
    return jnp.concatenate([wide_ref[tile, rows, :] for tile in range(tiles)], axis=1)


def put_image(wide_ref, image, images, values):
    tiles, total, lanes = wide_ref.shape
    rows = pl.ds(image, total // images, images)
    for tile in range(tiles):
        wide_ref[tile, rows, :] = values[:, tile * lanes : (tile + 1) * lanes]


def attention_kernel(
    images, tokens_ref, bias_ref, w_qkv_ref, w_proj_ref, vectors_ref,
    x_ref, qkv_ref, probs_ref, attended_ref, middle_ref, wide_ref, normed_ref,
):
    @pl.when(pl.program_id(0) == 0)
    def _():
        widen(tokens_ref, wide_ref, images)
        to_image_rows(wide_ref, x_ref, images)

    attention_steps(
        x_ref, lambda image: bias_ref[image], w_qkv_ref, w_proj_ref, vectors_ref,
        qkv_ref, probs_ref, attended_ref, middle_ref, normed_ref,
    )


def to_image_rows(wide_ref, x_ref, images):
    length = wide_ref.shape[1] // images

    @pl.loop(0, images)
    def _(image):
        rows = pl.ds(pl.multiple_of(image * length, length), length)
        x_ref[rows, :] = take_image(wide_ref, image, images).astype(jnp.bfloat16)


def attention_steps(
    x_ref, bias_column, w_qkv_ref, w_proj_ref, vectors_ref,
    qkv_ref, probs_ref, attended_ref, middle_ref, normed_ref,
):
    per_step, _, length, _ = probs_ref.shape
    step_rows, width = middle_ref.shape
    base = 0 if x_ref.shape[0] == step_rows else pl.program_id(0) * step_rows

    for image in range(per_step):
        rows = slice(image * length, (image + 1) * length)
        x = x_ref[pl.ds(pl.multiple_of(base + image * length, length), length), :].astype(jnp.float32)
        unit, _ = normal_form(x)
        normed_ref[rows, :] = (unit * vectors_ref[0:1] + vectors_ref[1:2]).astype(jnp.bfloat16)
    for part in range(3):
        cols = slice(part * width, (part + 1) * width)
        projected = dot(normed_ref[...], w_qkv_ref[:, cols])
        if part != 1:
            row = 2 if part == 0 else 3
            projected = projected + vectors_ref[row : row + 1]
        qkv_ref[:, cols] = projected.astype(jnp.bfloat16)

    for image in range(per_step):
        rows = slice(image * length, (image + 1) * length)
        first = pair_mask(length)
        place = lax.broadcasted_iota(jnp.int32, (length, 2 * length), 0)
        asker = lax.broadcasted_iota(jnp.int32, (length, 2 * length), 1)
        asker = jnp.where(asker >= length, asker - length, asker)
        bias = jnp.where(place == asker, 0.0, bias_column(image))
        for pair in range(width // (2 * HEAD_DIM)):
            low = pair * 2 * HEAD_DIM
            queries = stack_heads(qkv_ref[rows, low : low + 2 * HEAD_DIM], first)
            keys = qkv_ref[rows, width + low : width + low + 2 * HEAD_DIM]
            values = qkv_ref[rows, 2 * width + low : 2 * width + low + 2 * HEAD_DIM]
            scores = dot(keys, queries, 1, 1) * (HEAD_DIM**-0.5 * LOG2_E) + bias
            weights = jnp.exp2(scores - jnp.max(scores, axis=0, keepdims=True))
            probs = weights * (1.0 / jnp.sum(weights, axis=0, keepdims=True))
            probs = probs.astype(jnp.bfloat16)
            probs_ref[image, pair] = probs
            attended = join_heads(dot(probs, values, 0, 0), first)
            attended_ref[rows, low : low + 2 * HEAD_DIM] = attended.astype(jnp.bfloat16)

    middle_ref[...] = (
        x_ref[pl.ds(pl.multiple_of(base, length), step_rows), :].astype(jnp.float32)
        + dot(attended_ref[...], w_proj_ref[...])
        + vectors_ref[4:5]
    )


def feed_forward_kernel(
    images, middle_ref, cotangent_ref, attended_ref, w_up_ref, w_down_ref, w_proj_ref, vectors_ref, bias_up_ref,
    output_ref, d_middle_ref, d_attended_ref, up_grad_ref, down_grad_ref, proj_grad_ref, vector_sums_ref, up_sums_ref,
    wide_ref, *scratches,
):
    up_total_ref, down_total_ref, proj_total_ref = scratches[-3:]

    @pl.when(pl.program_id(0) == 0)
    def _():
        widen(cotangent_ref, wide_ref, images)

    feed_forward_steps(
        images, middle_ref, attended_ref, w_up_ref, w_down_ref, w_proj_ref, vectors_ref, bias_up_ref,
        d_middle_ref, d_attended_ref, vector_sums_ref, up_sums_ref, wide_ref, *scratches,
    )

    @pl.when(pl.program_id(0) == pl.num_programs(0) - 1)
    def _():
        narrow(wide_ref, output_ref, images)
        up_grad_ref[...] = up_total_ref[...].astype(jnp.bfloat16)
        down_grad_ref[...] = down_total_ref[...].T.astype(jnp.bfloat16)
        proj_grad_ref[...] = proj_total_ref[...].astype(jnp.bfloat16)


def feed_forward_steps(
    images, middle_ref, attended_ref, w_up_ref, w_down_ref, w_proj_ref, vectors_ref, bias_up_ref,
    d_middle_ref, d_attended_ref, vector_sums_ref, up_sums_ref,
    wide_ref, normed_ref, normed_t_ref, dy_ref, dy_t_ref, unit_ref, scale_ref, ahead_ref, back_ref,
    up_total_ref, down_total_ref, proj_total_ref,
):
    step = pl.program_id(0)
    length = wide_ref.shape[1] // images
    hidden = w_up_ref.shape[1]
    per_step = middle_ref.shape[0] // length

    @pl.when(step == 0)
    def _():
        for total in (up_total_ref, down_total_ref, proj_total_ref, vector_sums_ref, up_sums_ref):
            total[...] = jnp.zeros_like(total)

    for image in range(per_step):
        rows = slice(image * length, (image + 1) * length)
        dy = take_image(wide_ref, step * per_step + image, images)
        dy_ref[rows, :] = dy.astype(jnp.bfloat16)
        vector_sums_ref[3:4] += column_sum(dy)
        unit, scale = normal_form(middle_ref[rows, :])
        unit_ref[rows, :] = unit
        scale_ref[rows, :] = jnp.broadcast_to(scale, (length, scale_ref.shape[1]))
        normed_ref[rows, :] = (unit * vectors_ref[5:6] + vectors_ref[6:7]).astype(jnp.bfloat16)
    normed_t_ref[...] = normed_ref[...].T
    dy_t_ref[...] = dy_ref[...].T
    ahead_ref[...] = jnp.zeros_like(ahead_ref)
    back_ref[...] = jnp.zeros_like(back_ref)

    for chunk in range(hidden // FF_CHUNK):
        cols = slice(chunk * FF_CHUNK, (chunk + 1) * FF_CHUNK)
        w_up = w_up_ref[:, cols]
        w_down = w_down_ref[cols, :]
        active, slope = gelu_and_slope(dot(normed_ref[...], w_up) + bias_up_ref[:, cols])
        active = active.astype(jnp.bfloat16)
        d_hidden = dot(dy_ref[...], w_down, 1, 1) * slope
        d_hidden = d_hidden.astype(jnp.bfloat16)
        ahead_ref[...] += dot(active, w_down)
        back_ref[...] += dot(d_hidden, w_up, 1, 1)
        down_total_ref[:, cols] += dot(dy_t_ref[...], active)
        up_total_ref[:, cols] += dot(normed_t_ref[...], d_hidden)
        up_sums_ref[:, cols] += column_sum(d_hidden.astype(jnp.float32))

    for image in range(per_step):
        rows = slice(image * length, (image + 1) * length)
        output = middle_ref[rows, :] + ahead_ref[rows, :] + vectors_ref[11:12]
        put_image(wide_ref, step * per_step + image, images, output)
        unit = unit_ref[rows, :]
        grad = back_ref[rows, :]
        vector_sums_ref[1:2] += column_sum(grad * unit)
        vector_sums_ref[2:3] += column_sum(grad)
        d_middle = dy_ref[rows, :].astype(jnp.float32) + norm_back(
            grad, unit, scale_ref[rows, 0:1], vectors_ref[5:6]
        )
        d_middle_ref[rows, :] = d_middle
        d_branch = d_middle.astype(jnp.bfloat16)
        dy_ref[rows, :] = d_branch
        vector_sums_ref[0:1] += column_sum(d_branch.astype(jnp.float32))
    proj_total_ref[...] += dot(attended_ref[...], dy_ref[...], 0, 0)
    d_attended_ref[...] = dot(dy_ref[...], w_proj_ref[...], 1, 1).astype(jnp.bfloat16)


def attention_back_kernel(
    images, x_ref, qkv_ref, probs_ref, d_attended_ref, d_middle_ref, w_qkv_ref, vectors_ref,
    input_grad_ref, qkv_grad_ref, vector_sums_ref, wide_ref, *scratches,
):
    @pl.when(pl.program_id(0) == 0)
    def _():
        scratches[-1][...] = jnp.zeros_like(scratches[-1])
        vector_sums_ref[...] = jnp.zeros_like(vector_sums_ref)

    def put(image, rows, values):
        put_image(wide_ref, image, images, values)

    attention_back_steps(
        put, x_ref, qkv_ref, probs_ref, d_attended_ref, d_middle_ref, w_qkv_ref, vectors_ref,
        vector_sums_ref, *scratches,
    )

    @pl.when(pl.program_id(0) == pl.num_programs(0) - 1)
    def _():
        narrow(wide_ref, input_grad_ref, images)
        qkv_grad_ref[...] = scratches[-1][...].astype(jnp.bfloat16)


def attention_back_steps(
    put, x_ref, qkv_ref, probs_ref, d_attended_ref, d_middle_ref, w_qkv_ref, vectors_ref,
    vector_sums_ref, normed_ref, d_projected_ref, back_ref, qkv_total_ref,
):
    step = pl.program_id(0)
    width = x_ref.shape[1]
    length = probs_ref.shape[2]
    per_step = probs_ref.shape[0]

    for image in range(per_step):
        rows = slice(image * length, (image + 1) * length)
        first = pair_mask(length)
        for pair in range(width // (2 * HEAD_DIM)):
            low = pair * 2 * HEAD_DIM
            cols = [slice(part * width + low, part * width + low + 2 * HEAD_DIM) for part in range(3)]
            queries = stack_heads(qkv_ref[rows, cols[0]], first)
            keys = qkv_ref[rows, cols[1]]
            values = qkv_ref[rows, cols[2]]
            probs = probs_ref[image, pair]
            d_attended = stack_heads(d_attended_ref[rows, cols[0]], first)
            d_projected_ref[rows, cols[2]] = dot(probs, d_attended).astype(jnp.bfloat16)
            d_probs = dot(values, d_attended, 1, 1)
            probs = probs.astype(jnp.float32)
            along = jnp.sum(d_probs * probs, axis=0, keepdims=True)
            d_scores = (probs * (d_probs - along)).astype(jnp.bfloat16)
            scale = HEAD_DIM**-0.5
            d_queries = join_heads(dot(d_scores, keys, 0, 0), first) * scale
            d_projected_ref[rows, cols[0]] = d_queries.astype(jnp.bfloat16)
            d_projected_ref[rows, cols[1]] = (dot(d_scores, queries) * scale).astype(jnp.bfloat16)

    vector_sums_ref[2:3] += column_sum(d_projected_ref[:, :width].astype(jnp.float32))
    vector_sums_ref[3:4] += column_sum(d_projected_ref[:, 2 * width :].astype(jnp.float32))
    back_ref[...] = dot(d_projected_ref[...], w_qkv_ref[...], 1, 1)
    for image in range(per_step):
        rows = slice(image * length, (image + 1) * length)
        unit, scale = normal_form(x_ref[rows, :].astype(jnp.float32))
        normed_ref[rows, :] = (unit * vectors_ref[0:1] + vectors_ref[1:2]).astype(jnp.bfloat16)
        grad = back_ref[rows, :]
        vector_sums_ref[0:1] += column_sum(grad * unit)
        vector_sums_ref[1:2] += column_sum(grad)
        d_input = d_middle_ref[rows, :] + norm_back(grad, unit, scale, vectors_ref[0:1])
        put(step * per_step + image, rows, d_input)
    qkv_total_ref[...] += dot(normed_ref[...], d_projected_ref[...], 0, 0)


def whole_block(shape):
    return pl.BlockSpec(shape, lambda step: (0,) * len(shape))


def step_block(shape, first=0):
    return pl.BlockSpec(shape, lambda step: (first + step,) + (0,) * (len(shape) - 1))


def scratch(*shape, dtype=jnp.float32):
    return pltpu.VMEM(shape, dtype)


def call_kernel(kernel, statics, steps, ins, outs, scratches, operands, flops, transcendentals=0, first_step=0, aliases={}):
    in_specs = [
        pl.BlockSpec(memory_space=pltpu.SMEM)
        if block == "place"
        else pl.BlockSpec(memory_space=pl.ANY)
        if block == "await"
        else whole_block(op.shape) if block is None else step_block(block, first_step)
        for op, block in zip(operands, ins)
    ]
    out_specs = [
        whole_block(shape) if block is None else step_block(block, first_step) for shape, dtype, block in outs
    ]
    moved = sum(op.size * op.dtype.itemsize for op in operands) + sum(
        math.prod(shape) * jnp.dtype(dtype).itemsize for shape, dtype, block in outs
    )
    return pl.pallas_call(
        functools.partial(kernel, *statics),
        grid=(steps,),
        in_specs=in_specs,
        out_specs=out_specs,
        out_shape=[jax.ShapeDtypeStruct(shape, dtype) for shape, dtype, block in outs],
        scratch_shapes=scratches,
        input_output_aliases=aliases,
        compiler_params=pltpu.CompilerParams(vmem_limit_bytes=vmem_bytes),
        cost_estimate=pl.CostEstimate(
            flops=flops * 8, bytes_accessed=moved, transcendentals=transcendentals
        ),
    )(*operands)


def attention_forward(tokens, bias, w_qkv, w_proj, vectors):
    images, length, _ = bias.shape
    total, width = tokens.shape
    pairs = width // (2 * HEAD_DIM)
    rows = PER_STEP * length
    low, high = jnp.bfloat16, jnp.float32
    outs = [
        ((total, width), low, None),
        ((total, 3 * width), low, (rows, 3 * width)),
        ((images, pairs, length, 2 * length), low, (PER_STEP, pairs, length, 2 * length)),
        ((total, width), low, (rows, width)),
        ((total, width), high, (rows, width)),
    ]
    return call_kernel(
        attention_kernel, (images,), images // PER_STEP,
        [None, (PER_STEP, length, 1), None, None, None], outs,
        [scratch(width // 128, total, 128), scratch(rows, width, dtype=low)],
        (tokens, bias, w_qkv, w_proj, vectors),
        2 * total * width * 4 * width + 8 * total * length * width,
    )


def feed_forward(images, middle, cotangent, attended, w_up, w_down, w_proj, vectors):
    total, width = middle.shape
    hidden = w_up.shape[1]
    rows = total // images * PER_STEP
    low, high = jnp.bfloat16, jnp.float32
    block = (rows, width)
    outs = [
        ((total, width), low, None),
        ((total, width), high, block),
        ((total, width), low, block),
        ((width, hidden), low, None),
        ((hidden, width), low, None),
        ((width, width), low, None),
        ((8, width), high, None),
        ((1, hidden), high, None),
    ]
    scratches = [
        scratch(width // 128, total, 128),
        scratch(rows, width, dtype=low),
        scratch(width, rows, dtype=low),
        scratch(rows, width, dtype=low),
        scratch(width, rows, dtype=low),
        scratch(rows, width),
        scratch(rows, 128),
        scratch(rows, width),
        scratch(rows, width),
        scratch(width, hidden),
        scratch(width, hidden),
        scratch(width, width),
    ]
    return call_kernel(
        feed_forward_kernel, (images,), images // PER_STEP,
        [block, None, block, None, None, None, None, None], outs, scratches,
        (middle, cotangent, attended, w_up, w_down, w_proj, vectors, vectors[7:11].reshape(1, hidden)),
        12 * total * width * hidden + 4 * total * width * width, total * hidden,
    )


def attention_back(x, qkv, probs, d_attended, d_middle, w_qkv, vectors):
    images, pairs, length, _ = probs.shape
    total, width = x.shape
    rows = PER_STEP * length
    low, high = jnp.bfloat16, jnp.float32
    block = (rows, width)
    outs = [
        ((total, width), low, None),
        ((width, 3 * width), low, None),
        ((8, width), high, None),
    ]
    scratches = [
        scratch(width // 128, total, 128),
        scratch(rows, width, dtype=low),
        scratch(rows, 3 * width, dtype=low),
        scratch(rows, width),
        scratch(width, 3 * width),
    ]
    return call_kernel(
        attention_back_kernel, (images,), images // PER_STEP,
        [block, (rows, 3 * width), (PER_STEP, pairs, length, 2 * length), block, block, None, None],
        outs, scratches, (x, qkv, probs, d_attended, d_middle, w_qkv, vectors),
        4 * total * width * 3 * width + 16 * total * length * width,
    )

def linear_place():
    return lax.axis_index("dp") * lax.axis_size("group") + lax.axis_index("group")


def permute(array, mask):
    count = lax.axis_size("dp") * lax.axis_size("group")
    return lax.ppermute(array, ("dp", "group"), [(rank, rank ^ mask) for rank in range(count)])


def direct_masks(bits):
    masks = [0]
    for bit in bits:
        masks = masks + [mask | bit for mask in masks]
    return masks[1:]


def scatter_step(held, bits):
    masks = direct_masks(bits)
    size = held.shape[0] // (len(masks) + 1)
    parts = [
        permute(held[size * (at + 1) : size * (at + 2)].astype(jnp.bfloat16), mask)
        for at, mask in enumerate(masks)
    ]
    return held[:size], parts


def add_wide(first, *rest):
    total = first.astype(jnp.float32)
    for part in rest:
        total = total + part.astype(jnp.float32)
    return total


def packed_place(mask, spread, count):
    return ((mask >> 1) & (spread - 1)) * (count // (2 * spread)) + (mask >> (spread.bit_length()))


def scatter_step(held, bits):
    masks = direct_masks(bits)
    size = held.shape[0] // (len(masks) + 1)
    parts = [
        permute(held[size * (at + 1) : size * (at + 2)].astype(jnp.bfloat16), mask)
        for at, mask in enumerate(masks)
    ]
    return held[:size], parts


def add_wide(first, *rest):
    total = first.astype(jnp.float32)
    for part in rest:
        total = total + part.astype(jnp.float32)
    return total


def packed_place(mask, spread, count):
    return ((mask >> 1) & (spread - 1)) * (count // (2 * spread)) + (mask >> (spread.bit_length()))


def gather_step(held, bits):
    return held + [permute(part, mask) for mask in direct_masks(bits) for part in held]


def gathered_place(mask, count):
    return (mask & 1) * (count // 2) + ((mask >> 2) & 1) * (count // 4) + (mask >> 3) * 2 + ((mask >> 1) & 1)


def unpack(place_ref, block_refs, packed_ref, put, dp_size, spread):
    place = place_ref[0]
    size = block_refs[0].shape[0]
    for at, block_ref in enumerate(block_refs):
        packed_ref[at * size : (at + 1) * size] = block_ref[...]
    count = dp_size * spread
    for row in range(dp_size):
        for col in range(spread):
            put(row, col, packed_ref[gathered_place((row * spread + col) ^ place, count)])


def pack(place_ref, take, keep_ref, leave_ref, dp_size, spread):
    place = place_ref[0]
    odd = (place & 1) == 1
    for row in range(dp_size):
        for col in range(0, spread, 2):
            at = packed_place((row * spread + col) ^ place, spread, dp_size * spread)
            even_block, odd_block = take(row, col), take(row, col + 1)
            keep_ref[at] = jnp.where(odd, odd_block, even_block)
            leave_ref[at] = jnp.where(odd, even_block, odd_block)


def narrow_pieces(place_ref, wide_ref, piece_refs, spread):
    tiles, _, lanes = wide_ref.shape
    rows_of_piece = piece_refs[0].shape[0]
    step = 64
    group = place_ref[0] & (spread - 1)
    for relative, piece_ref in enumerate(piece_refs):
        base = (group ^ relative) * rows_of_piece

        @pl.loop(0, rows_of_piece // step)
        def _(part):
            target = pl.ds(pl.multiple_of(part * step, step), step)
            source = pl.ds(pl.multiple_of(base + part * step, step), step)
            for tile in range(tiles):
                cols = slice(tile * lanes, (tile + 1) * lanes)
                piece_ref[target, cols] = wide_ref[tile, source, :].astype(jnp.bfloat16)


def general_body(
    tokens,
    keep_mask,
    cotangent,
    qkv_weight,
    proj_weight,
    up_weight,
    down_weight,
    vectors,
    qkv_rows,
    qkv_cols,
    proj_rows,
    proj_cols,
    up_rows,
    up_cols,
    down_rows,
    down_cols,
    vector_moment,
):
    masters = (qkv_weight, proj_weight, up_weight, down_weight)
    lowered = tuple((master.astype(jnp.bfloat16) for master in masters))
    dp_bits, group_bits = axis_bits("dp"), axis_bits("group")
    gather_steps = dp_bits[1:] + group_bits[1:] + dp_bits[:1] + group_bits[:1]
    scatter_steps = gather_steps[::-1]
    w_qkv, w_proj, w_up, w_down = tuple(
        blocks_to_whole(gather_blocks(part, gather_steps), gather_steps) for part in lowered
    )
    spread = lax.axis_size("group")

    def slots_in(array):
        held, slots, width = array.shape
        parts = array.transpose(1, 0, 2).reshape(slots, spread, held // spread, width)
        parts = lax.all_to_all(
            parts.transpose(1, 0, 2, 3), "group", split_axis=0, concat_axis=0, tiled=True
        )
        return parts.reshape(spread * slots * (held // spread), width)

    def slots_out(array):
        held, slots, width = tokens.shape
        parts = array.reshape(spread, slots, held // spread, width)
        parts = lax.all_to_all(parts, "group", split_axis=0, concat_axis=0, tiled=True)
        return parts.transpose(1, 0, 2, 3).reshape(slots, held, width).transpose(1, 0, 2)

    images = keep_mask.shape[0]
    bias = jnp.where(keep_mask > 0, 0.0, -1e30)[:, :, None]
    x, qkv, probs, attended, middle = attention_forward(
        slots_in(tokens), bias, w_qkv, w_proj, vectors
    )
    output, d_middle, d_attended, up_grad, down_grad, proj_grad, ff_sums, up_sums = feed_forward(
        images, middle, slots_in(cotangent), attended, w_up, w_down, w_proj, vectors
    )
    block_output = slots_out(output)
    d_input, qkv_grad, att_sums = attention_back(
        x, qkv, probs, d_attended, d_middle, w_qkv, vectors
    )
    input_grad = slots_out(d_input)
    local_vectors = jnp.concatenate(
        [att_sums[:4], ff_sums[:3], up_sums.reshape(4, -1), ff_sums[3:4]], axis=0
    )
    vector_grad = sum_everywhere(local_vectors, group_bits + dp_bits)
    local_grads = (qkv_grad, proj_grad, up_grad, down_grad)
    owned = tuple(
        scatter_sum(whole_to_blocks(part, scatter_steps), scatter_steps) for part in local_grads
    )
    squares = tuple((gradient * gradient + tiny_square for gradient in owned))
    row_parts = tuple((jnp.sum(square, axis=1) for square in squares)) + tuple(
        (jnp.sum(master * master, axis=1) for master in masters)
    )
    row_sums = sum_parts(row_parts, group_bits)
    rows_old = (qkv_rows, proj_rows, up_rows, down_rows)
    cols_old = (qkv_cols, proj_cols, up_cols, down_cols)
    total_cols = tuple((gradient.shape[1] * lax.axis_size("group") for gradient in owned))
    total_rows = tuple((gradient.shape[0] * lax.axis_size("dp") for gradient in owned))
    rows_new = tuple(
        (
            decay_rate * rows_old[which] + (1.0 - decay_rate) * row_sums[which] / total_cols[which]
            for which in range(4)
        )
    )
    col_parts = (
        tuple((jnp.sum(square, axis=0) for square in squares))
        + tuple((jnp.sum(row_stat) for row_stat in rows_new))
        + tuple((jnp.sum(row_sums[4 + which]) for which in range(4)))
    )
    col_sums = sum_parts(col_parts, dp_bits)
    results = []
    for which in range(4):
        cols_new = (
            decay_rate * cols_old[which] + (1.0 - decay_rate) * col_sums[which] / total_rows[which]
        )
        mean_rows = col_sums[4 + which] / total_rows[which]
        spread = jnp.sqrt(col_sums[8 + which] / (total_rows[which] * total_cols[which]))
        second = rows_new[which][:, None] * cols_new[None, :] / mean_rows
        updated = masters[which] - step_rate * spread * owned[which] * lax.rsqrt(second)
        results.append((owned[which], rows_new[which], cols_new, updated))
    vector_moment_new = decay_rate * vector_moment + (1.0 - decay_rate) * (
        vector_grad * vector_grad + tiny_square
    )
    row_spread = jnp.sqrt(jnp.mean(vectors * vectors, axis=1, keepdims=True))
    vector_new = vectors - step_rate * row_spread * vector_grad * lax.rsqrt(vector_moment_new)
    return (
        block_output,
        input_grad,
        results[0][0],
        results[0][1],
        results[0][2],
        results[0][3],
        results[1][0],
        results[1][1],
        results[1][2],
        results[1][3],
        results[2][0],
        results[2][1],
        results[2][2],
        results[2][3],
        results[3][0],
        results[3][1],
        results[3][2],
        results[3][3],
        vector_grad,
        vector_moment_new,
        vector_new,
    )


def first_attention_kernel(images, dp_size, spread, place_ref, tokens_ref, *refs):
    blocks, far, refs = refs[:4], refs[4 : 4 + dp_size // 2], refs[4 + dp_size // 2 :]
    keep_ref, vectors_ref, *outs, x_ref, w_qkv_ref, w_proj_ref, joined_ref = refs[:-4]
    packed_ref, wide_ref, bias_ref, normed_ref = refs[-4:]
    rows = packed_ref.shape[1]
    qkv_cols, proj_cols = w_qkv_ref.shape[1] // spread, w_proj_ref.shape[1] // spread

    @pl.when(pl.program_id(0) == 0)
    def _():
        widen(tokens_ref, wide_ref, images)
        to_image_rows(wide_ref, x_ref, images)

        def put(row, col, block):
            down = slice(row * rows, (row + 1) * rows)
            w_qkv_ref[down, col * qkv_cols : (col + 1) * qkv_cols] = block[:, :qkv_cols]
            w_proj_ref[down, col * proj_cols : (col + 1) * proj_cols] = block[:, qkv_cols:]

        unpack(place_ref, blocks, packed_ref, put, dp_size, spread)
        for at, far_ref in enumerate(far):
            joined_ref[2 * at : 2 * at + 2] = far_ref[...]

    attention_part(0, x_ref, keep_ref, w_qkv_ref, w_proj_ref, vectors_ref, *outs, bias_ref, normed_ref)


def next_attention_kernel(start, x_ref, keep_ref, w_qkv_ref, w_proj_ref, vectors_ref, *refs):
    attention_part(start, x_ref, keep_ref, w_qkv_ref, w_proj_ref, vectors_ref, *refs[-6:])


def attention_part(
    start, x_ref, keep_ref, w_qkv_ref, w_proj_ref, vectors_ref,
    qkv_ref, probs_ref, attended_ref, middle_ref, bias_ref, normed_ref,
):
    @pl.when(pl.program_id(0) == 0)
    def _():
        bias_ref[...] = jnp.where(keep_ref[...] > 0, 0.0, -1e30).T

    def bias_column(image):
        here = start + pl.program_id(0) * probs_ref.shape[0] + image
        lane = lax.broadcasted_iota(jnp.int32, bias_ref.shape, 1)
        return row_sum(jnp.where(lane == here, bias_ref[...], 0.0))

    attention_steps(
        x_ref, bias_column, w_qkv_ref, w_proj_ref, vectors_ref,
        qkv_ref, probs_ref, attended_ref, middle_ref, normed_ref,
    )


def feed_forward_packed_kernel(images, dp_size, spread, place_ref, *refs):
    cotangent_ref, blocks, refs = refs[0], refs[1:5], refs[5:]
    middle_ref, attended_ref, w_proj_ref, vectors_ref = refs[:4]
    outputs, refs = refs[4 : 4 + spread], refs[4 + spread :]
    d_middle_ref, d_attended_ref, keep_ref, leave_ref, proj_total_ref, vector_sums_ref, up_sums_ref = refs[:7]
    w_up_ref, w_down_ref, down_low_ref, packed_ref, bias_up_ref, wide_ref = refs[7:13]
    scratches = refs[13:]
    width = w_up_ref.shape[0]
    up_total_ref, down_total_ref = scratches[-2:]
    rows = packed_ref.shape[1]
    up_cols = w_up_ref.shape[1] // spread
    out_cols = w_down_ref.shape[1] // spread
    folds = w_down_ref.shape[0] // w_up_ref.shape[0]

    @pl.when(pl.program_id(0) == 0)
    def _():
        widen(cotangent_ref, wide_ref, images)
        for fold in range(bias_up_ref.shape[1] // width):
            bias_up_ref[:, fold * width : (fold + 1) * width] = vectors_ref[7 + fold : 8 + fold]

        def put(row, col, block):
            w_up_ref[row * rows : (row + 1) * rows, col * up_cols : (col + 1) * up_cols] = block[:, :up_cols]
            for fold in range(folds):
                down = (row * folds + fold) * rows
                start = up_cols + fold * out_cols
                w_down_ref[down : down + rows, col * out_cols : (col + 1) * out_cols] = block[
                    :, start : start + out_cols
                ]

        unpack(place_ref, blocks, packed_ref, put, dp_size, spread)

    feed_forward_steps(
        images, middle_ref, attended_ref, w_up_ref, w_down_ref, w_proj_ref, vectors_ref, bias_up_ref,
        d_middle_ref, d_attended_ref, vector_sums_ref, up_sums_ref, wide_ref, *scratches, proj_total_ref,
    )

    @pl.when(pl.program_id(0) == pl.num_programs(0) - 1)
    def _():
        narrow_pieces(place_ref, wide_ref, outputs, spread)
        down_low_ref[...] = down_total_ref[...].T.astype(jnp.bfloat16)

        def take(row, col):
            across = slice(row * rows, (row + 1) * rows)
            cols = slice(col * out_cols, (col + 1) * out_cols)
            parts = [up_total_ref[across, col * up_cols : (col + 1) * up_cols].astype(jnp.bfloat16)]
            for fold in range(folds):
                down = (row * folds + fold) * rows
                parts.append(down_low_ref[down : down + rows, cols])
            return jnp.concatenate(parts, axis=1)

        pack(place_ref, take, keep_ref, leave_ref, dp_size, spread)


def attention_back_packed_kernel(
    images, dp_size, spread, place_ref, x_ref, qkv_ref, probs_ref, d_attended_ref, d_middle_ref, w_qkv_ref,
    vectors_ref, proj_total_ref, _, *refs,
):
    pieces, (keep_ref, leave_ref, vector_sums_ref, wide_ref, *scratches) = refs[:spread], refs[spread:]
    total_ref = scratches[-1]

    @pl.when(pl.program_id(0) == 0)
    def _():
        total_ref[...] = jnp.zeros_like(total_ref)
        vector_sums_ref[...] = jnp.zeros_like(vector_sums_ref)

    def put(image, rows, values):
        put_image(wide_ref, image, images, values)

    attention_back_steps(
        put, x_ref, qkv_ref, probs_ref, d_attended_ref, d_middle_ref, w_qkv_ref, vectors_ref,
        vector_sums_ref, *scratches,
    )

    @pl.when(pl.program_id(0) == pl.num_programs(0) - 1)
    def _():
        narrow_pieces(place_ref, wide_ref, pieces, spread)
        rows = keep_ref.shape[1]
        qkv_cols, proj_cols = total_ref.shape[1] // spread, proj_total_ref.shape[1] // spread

        def take(row, col):
            down = slice(row * rows, (row + 1) * rows)
            parts = [
                total_ref[down, col * qkv_cols : (col + 1) * qkv_cols],
                proj_total_ref[down, col * proj_cols : (col + 1) * proj_cols],
            ]
            return jnp.concatenate(parts, axis=1).astype(jnp.bfloat16)

        pack(place_ref, take, keep_ref, leave_ref, dp_size, spread)


def cut(array_ref, parts_ref):
    count = parts_ref.shape[2]
    for member in range(parts_ref.shape[0]):
        parts_ref[member] = array_ref[:, member * count : (member + 1) * count, :]


def pack_kernel(qkv_ref, proj_ref, up_ref, down_ref, pack_ref):
    rows, start = pack_ref.shape[0], 0
    parts = [qkv_ref[...], proj_ref[...], up_ref[...]]
    parts += [down_ref[fold * rows : (fold + 1) * rows, :] for fold in range(down_ref.shape[0] // rows)]
    for part in parts:
        pack_ref[:, start : start + part.shape[1]] = part.astype(jnp.bfloat16)
        start += part.shape[1]


def token_kernel(array_ref, own_ref, arrived_ref, parts_ref, pair_ref):
    cols = pair_ref.shape[2]
    pair_ref[0] = own_ref[:, :cols]
    pair_ref[1] = arrived_ref[:, :cols]
    cut(array_ref, parts_ref)


def cotangent_kernel(array_ref, own_ref, arrived_ref, parts_ref, pair_ref):
    start = own_ref.shape[1] - pair_ref.shape[2]
    pair_ref[0] = own_ref[:, start:]
    pair_ref[1] = arrived_ref[:, start:]
    cut(array_ref, parts_ref)


def join_kernel(*refs):
    size = refs[0].shape[0]
    for at, part_ref in enumerate(refs[:-1]):
        refs[-1][at * size : (at + 1) * size] = part_ref[...]


def settle_kernel(spread, place_ref, *refs):
    lists, output_ref = refs[:-1], refs[-1]
    group = place_ref[0] & (spread - 1)
    count = lists[0].shape[1]
    share = len(lists) // spread * count
    for at, piece_ref in enumerate(lists):
        relative, part = at % spread, at // spread
        start = pl.multiple_of((group ^ relative) * share + part * count, count)
        output_ref[:, pl.ds(start, count), :] = piece_ref[...]


def lane_table(rows, columns):
    lane = lax.broadcasted_iota(jnp.int32, (rows, 128), 1)
    table = jnp.zeros((rows, 128), jnp.float32)
    for at, column in enumerate(columns):
        table = jnp.where(lane == at, column, table)
    return table


def added(parts):
    while len(parts) > 1:
        parts = [sum(parts[at : at + 2][1:], parts[at]) for at in range(0, len(parts), 2)]
    return parts[0]


def row_sum(values):
    return jnp.sum(values, axis=1, keepdims=True)


def after_kernel(*refs):
    pass


def add_kernel(count, keep_ref, arrived_ref, *refs):
    parts = refs[-count:]
    size = parts[0].shape[0]
    for at, part_ref in enumerate(parts):
        rows = slice(at * size, (at + 1) * size)
        total = keep_ref[rows].astype(jnp.float32) + arrived_ref[rows].astype(jnp.float32)
        part_ref[...] = total.astype(part_ref.dtype)


def gradient_kernel(count, *refs):
    block_parts, sums, refs = refs[:count], refs[count : count + 3], refs[count + 3 :]
    masters, rows_old, refs = refs[:4], refs[4:8], refs[8:]
    grads, (row_ref, message_ref) = refs[:4], refs[4:]
    blocks = added([part[0].astype(jnp.float32) for part in block_parts])
    rows, up_cols = grads[2].shape
    qkv_cols, out_cols = grads[0].shape[1], grads[1].shape[1]
    folds = grads[3].shape[0] // rows
    up = blocks[:, :up_cols]
    downs = [blocks[:, up_cols + fold * out_cols :][:, :out_cols] for fold in range(folds)]
    start = up_cols + folds * out_cols
    qkv = blocks[:, start : start + qkv_cols]
    proj = blocks[:, start + qkv_cols :]
    grads[0][...] = qkv
    grads[1][...] = proj
    grads[2][...] = up
    for fold in range(folds):
        grads[3][fold * rows : (fold + 1) * rows, :] = downs[fold]
    squares = [part * part + tiny_square for part in (qkv, proj, up, *downs)]
    row_ref[...] = lane_table(rows, [row_sum(square) for square in squares]).T[: row_ref.shape[0], :]
    width = message_ref.shape[1]
    message_ref[...] = jnp.zeros_like(message_ref)
    for at, square in enumerate((*squares[:3], added(squares[3:]))):
        message_ref[at : at + 1, : square.shape[1]] = column_sum(square)
    scalars = [column_sum(row_sum(master[...] * master[...])) for master in masters]
    scalars += [row_sum(part[...].reshape(1, part.shape[0])) for part in rows_old]
    message_ref[4:5, :128] = lane_table(1, scalars)
    att_ref, ff_ref, up_ref = sums
    count = up_ref.shape[1] // width
    message_ref[8:12, :] = att_ref[:4]
    message_ref[12:15, :] = ff_ref[:3]
    for at in range(count):
        message_ref[15 + at : 16 + at, :] = up_ref[:, at * width : (at + 1) * width]
    message_ref[15 + count : 16 + count, :] = ff_ref[3:4]


def column_kernel(row_ref, *refs):
    parts, (cols_ref, message_ref) = refs[:-2], refs[-2:]
    total = added([part[...] for part in parts])
    cols_ref[...] = total[:8]
    width = total.shape[1]
    rows = row_ref.shape[1]
    message_ref[...] = jnp.zeros_like(message_ref)
    message_ref[:8, :rows] = row_ref[...]
    columns = [row_sum(total[which : which + 1]) for which in range(4)]
    squares = [total[4:5, which : which + 1] for which in range(4)]
    message_ref[8:9, :] = lane_table(1, columns + squares)
    for tile in range(width // 128):
        message_ref[16 * (tile + 1) : 16 * (tile + 2), :] = total[8:, tile * 128 : (tile + 1) * 128]


def update_kernel(count, heights, widths, *refs):
    messages, refs = refs[:count], refs[count:]
    cols_ref, vectors_ref, moment_ref, refs = refs[0], refs[1], refs[2], refs[3:]
    grads, masters, rows_old, cols_old, refs = refs[:4], refs[4:8], refs[8:12], refs[12:16], refs[16:]
    news, cols_new, rows_out, refs = refs[:4], refs[4:8], refs[8:12], refs[12:]
    vector_grad_ref, moment_new_ref, vector_new_ref = refs
    sums = added([message[...] for message in messages])
    height = grads[0].shape[0]
    folds = grads[3].shape[0] // height
    lanes = [[0], [1], [2], list(range(3, 3 + folds))]
    share = 1.0 - decay_rate
    for which in range(4):
        entries = heights[which] * widths[which]
        cols = cols_old[which].shape[0]
        new = decay_rate * cols_old[which][...].reshape(1, cols) + share / heights[which] * cols_ref[
            which : which + 1, :cols
        ]
        cols_new[which][...] = new[0]
        old_total = cols_ref[4:5, 4 + which : 5 + which]
        mean_rows = (decay_rate * old_total + share / widths[which] * sums[8:9, which : which + 1]) / heights[which]
        rate = step_rate * jnp.sqrt(sums[8:9, 4 + which : 5 + which] / entries)
        across = new / mean_rows
        old = rows_old[which][...].reshape(1, len(lanes[which]) * height)
        row_sums = jnp.concatenate([sums[lane : lane + 1, :height] for lane in lanes[which]], axis=1)
        row = decay_rate * old + share / widths[which] * row_sums
        rows_out[which][...] = row[0]
        for fold in range(len(lanes[which])):
            part = slice(fold * height, (fold + 1) * height)
            column = jnp.broadcast_to(row[:, part], (8, height)).T[:, :1]
            news[which][part, :] = masters[which][part, :] - rate * grads[which][part, :] * lax.rsqrt(column * across)
    vectors = vectors_ref[...]
    count = vectors.shape[0]
    gradient = jnp.concatenate(
        [sums[16 * (tile + 1) : 16 * (tile + 1) + count] for tile in range(vectors.shape[1] // 128)], axis=1
    )
    vector_grad_ref[...] = gradient
    moment = decay_rate * moment_ref[...] + share * (gradient * gradient + tiny_square)
    moment_new_ref[...] = moment
    spread = jnp.sqrt(jnp.mean(vectors * vectors, axis=1, keepdims=True))
    vector_new_ref[...] = vectors - step_rate * spread * gradient * lax.rsqrt(moment)


def packed_body(
    tokens, keep_mask, cotangent, qkv_weight, proj_weight, up_weight, down_weight, vectors,
    qkv_rows, qkv_cols, proj_rows, proj_cols, up_rows, up_cols, down_rows, down_cols, vector_moment,
):
    spread, dp_size = lax.axis_size("group"), lax.axis_size("dp")
    low, high = jnp.bfloat16, jnp.float32
    place = linear_place().astype(jnp.int32).reshape(1)
    group = lax.axis_index("group")
    held, slots, width = tokens.shape
    images, length = keep_mask.shape
    hidden = up_weight.shape[1] * spread
    total = images * length
    rows = qkv_weight.shape[0]
    folds = down_weight.shape[0] // rows
    core_bits = (1,)
    near_bits = tuple(1 << at for at in range(1, spread.bit_length()))
    far_bits = tuple(spread << at for at in range(1, dp_size.bit_length() - 1))
    half = spread * dp_size // 2

    anywhere = pl.BlockSpec(memory_space=pl.ANY)
    in_smem = pl.BlockSpec(memory_space=pltpu.SMEM)

    in_vmem = pl.BlockSpec(memory_space=pltpu.VMEM)
    small = functools.partial(
        pl.pallas_call, compiler_params=pltpu.CompilerParams(vmem_limit_bytes=vmem_bytes)
    )
    masters = (qkv_weight, proj_weight, up_weight, down_weight)
    parted = jax.ShapeDtypeStruct((spread, slots, images, width), low)

    def to_group(parts):
        return lax.all_to_all(parts, "group", split_axis=0, concat_axis=0, tiled=True)

    def to_images(parts):
        return to_group(parts).reshape(total, width)

    def exchange(parts):
        return [parts[0]] + [permute(part, relative) for relative, part in enumerate(parts) if relative]

    def settle(parts):
        parts = [part.reshape(slots, -1, width) for part in parts]
        whole = small(
            functools.partial(settle_kernel, spread),
            in_specs=[in_smem] + [in_vmem] * len(parts),
            out_specs=in_vmem,
            out_shape=jax.ShapeDtypeStruct((slots, held, width), low),
        )(place, *parts)
        return whole.transpose(1, 0, 2)

    first_cols = qkv_weight.shape[1] + proj_weight.shape[1]
    second_cols = up_weight.shape[1] + folds * down_weight.shape[1]
    pack_own = small(pack_kernel, out_shape=jax.ShapeDtypeStruct((rows, first_cols + second_cols), low))(*masters)
    across_y, across_x = near_bits
    pack_arrived = permute(pack_own, across_y)
    token_cut, first_pair = small(
        token_kernel,
        out_shape=[parted, jax.ShapeDtypeStruct((2, rows, first_cols), low)],
    )(tokens.transpose(1, 0, 2), pack_own, pack_arrived)
    inputs = to_images(token_cut)

    def gather_far(pair):
        return [pair] + [permute(pair, mask) for mask in direct_masks(far_bits)]

    def join(parts):
        count = len(parts) * parts[0].shape[0]
        return small(join_kernel, out_shape=jax.ShapeDtypeStruct((count, *parts[0].shape[1:]), low))(*parts)

    def gather_rest(held):
        arrived = permute(held, across_x)
        return [held, arrived, permute(held, core_bits[0]), permute(arrived, core_bits[0])]

    first_far = join(gather_far(first_pair))
    cotangent_cut, second_pair = small(
        cotangent_kernel,
        out_shape=[parted, jax.ShapeDtypeStruct((2, rows, second_cols), low)],
    )(cotangent.transpose(1, 0, 2), pack_own, pack_arrived)
    upstream = to_images(cotangent_cut)
    first_blocks = gather_rest(first_far)
    second_far = gather_far(second_pair)

    step_rows = PER_STEP * length
    block = (step_rows, width)
    pairs = width // (2 * HEAD_DIM)
    steps = images // PER_STEP
    statics = (images, dp_size, spread)
    wide = scratch(width // 128, total, 128)
    probs_block = (PER_STEP, pairs, length, 2 * length)
    attention_outs = [
        ((total, 3 * width), low, (step_rows, 3 * width)),
        ((images, *probs_block[1:]), low, probs_block),
        ((total, width), low, block),
        ((total, width), high, block),
    ]
    attention_flops = (2 * total * width * 4 * width + 8 * total * length * width) // steps
    attention_scratches = [scratch(length, images), scratch(step_rows, width, dtype=low)]
    *attention, x, w_qkv, w_proj, second_joined = call_kernel(
        first_attention_kernel, statics, 1,
        ["place"] + [None] * (7 + len(second_far)),
        attention_outs
        + [
            ((total, width), low, None),
            ((width, 3 * width), low, None),
            ((width, width), low, None),
            ((dp_size, rows, second_cols), low, None),
        ],
        [scratch(dp_size * spread, rows, first_cols, dtype=low), wide] + attention_scratches,
        (place, inputs, *first_blocks, *second_far, keep_mask, vectors),
        attention_flops,
    )
    second_blocks = gather_rest(second_joined)
    for first_step, count in ((1, steps - 2), (steps - 1, 1)):
        attention = call_kernel(
            next_attention_kernel, (first_step * PER_STEP,), count,
            [block] + [None] * 4 + ["await"] * len(attention),
            attention_outs, attention_scratches,
            (x, keep_mask, w_qkv, w_proj, vectors, *attention),
            attention_flops * count, first_step=first_step,
            aliases={5 + at: at for at in range(len(attention))},
        )
    qkv, probs, attended, middle = attention
    piece = ((slots * images, width), low, None)
    results = call_kernel(
        feed_forward_packed_kernel, statics, steps,
        ["place"] + [None] * 5 + [block, block] + [None] * 2,
        [piece] * spread
        + [
            ((total, width), high, block),
            ((total, width), low, block),
            ((half, rows, second_cols), low, None),
            ((half, rows, second_cols), low, None),
            ((width, width), high, None),
            ((8, width), high, None),
            ((1, hidden), high, None),
        ],
        [
            scratch(width, hidden, dtype=low),
            scratch(hidden, width, dtype=low),
            scratch(hidden, width, dtype=low),
            scratch(dp_size * spread, rows, second_cols, dtype=low),
            scratch(1, hidden),
            wide,
            scratch(step_rows, width, dtype=low),
            scratch(width, step_rows, dtype=low),
            scratch(step_rows, width, dtype=low),
            scratch(width, step_rows, dtype=low),
            scratch(step_rows, width),
            scratch(step_rows, 128),
            scratch(step_rows, width),
            scratch(step_rows, width),
            scratch(width, hidden),
            scratch(width, hidden),
        ],
        (
            place, upstream, *second_blocks, middle, attended, w_proj, vectors,
        ),
        12 * total * width * hidden + 4 * total * width * width, total * hidden,
    )
    d_middle, d_attended, ff_keep, ff_leave, proj_total, ff_sums, up_sums = results[spread:]

    def after(array, awaited):
        return small(
            after_kernel,
            in_specs=[anywhere] * (1 + len(awaited)),
            out_specs=anywhere,
            out_shape=jax.ShapeDtypeStruct(array.shape, array.dtype),
            input_output_aliases={0: 0},
        )(array, *awaited)

    def add_parts(count, keep, arrived, awaited):
        part = (keep.shape[0] // count, *keep.shape[1:])
        return small(
            functools.partial(add_kernel, count),
            in_specs=[in_vmem] * 2 + [anywhere] * len(awaited),
            out_specs=[in_vmem] * count,
            out_shape=[jax.ShapeDtypeStruct(part, high)]
            + [jax.ShapeDtypeStruct(part, low)] * (count - 1),
        )(keep, arrived, *awaited)

    ff_first = permute(ff_leave, core_bits[0])
    ff_count = half // 2
    ff_next = add_wide(ff_keep[ff_count:], ff_first[ff_count:]).astype(low)
    ff_arrived = permute(ff_next, across_x)
    output_parts = exchange(results[:spread])
    pack_half = ((half, rows, first_cols), low, None)
    results = call_kernel(
        attention_back_packed_kernel, statics, steps,
        ["place", block, (step_rows, 3 * width), probs_block, block, block, None, None, None, "await"],
        [piece] * spread + [pack_half, pack_half, ((8, width), high, None)],
        [
            wide,
            scratch(step_rows, width, dtype=low),
            scratch(step_rows, 3 * width, dtype=low),
            scratch(step_rows, width),
            scratch(width, 3 * width),
        ],
        (place, x, qkv, probs, d_attended, d_middle, w_qkv, vectors, proj_total, ff_next),
        4 * total * width * 3 * width + 16 * total * length * width,
    )
    qkv_keep, qkv_leave, att_sums = results[spread:]
    qkv_arrived = permute(after(qkv_leave, output_parts[1:]), core_bits[0])
    input_parts = exchange(results[:spread])
    ff_quarter = half // 4
    ff_last = add_wide(
        ff_keep[ff_quarter:ff_count], ff_first[ff_quarter:ff_count], ff_arrived[ff_quarter:]
    ).astype(low)
    ff_last_arrived = permute(ff_last, across_y)
    qkv_held, *leaving = add_parts(4, qkv_keep, qkv_arrived, [ff_last])
    qkv_parts = [permute(part, mask) for part, mask in zip(leaving, direct_masks(near_bits))]
    ff_held = add_wide(
        ff_keep[:ff_quarter], ff_first[:ff_quarter], ff_arrived[:ff_quarter], ff_last_arrived
    )
    qkv_held = add_wide(qkv_held, *qkv_parts)
    blocks, block_parts = scatter_step(jnp.concatenate([ff_held, qkv_held], axis=2), far_bits)
    block_parts = [blocks] + block_parts

    heights = [master.shape[0] * dp_size for master in masters]
    widths = [master.shape[1] * spread for master in masters]
    rows_old, cols_old = [qkv_rows, proj_rows, up_rows, down_rows], [qkv_cols, proj_cols, up_cols, down_cols]

    def like(*arrays):
        return [jax.ShapeDtypeStruct(array.shape, high) for array in arrays]

    *grads, row_sums, message = small(
        functools.partial(gradient_kernel, len(block_parts)),
        out_shape=like(*masters) + [jax.ShapeDtypeStruct((8, rows), high), jax.ShapeDtypeStruct((24, width), high)],
    )(*block_parts, att_sums, ff_sums, up_sums, *masters, *rows_old)
    message = message + permute(message, across_x)
    messages = [message] + [permute(message, mask) for mask in direct_masks(far_bits)]
    col_sums, message = small(
        column_kernel,
        out_shape=[
            jax.ShapeDtypeStruct((8, width), high),
            jax.ShapeDtypeStruct((16 + width // 8, 128), high),
        ],
    )(row_sums, *messages)
    messages = [message] + [permute(message, mask) for mask in range(1, spread)]
    results = small(
        functools.partial(update_kernel, len(messages), heights, widths),
        out_shape=like(*masters, *cols_old, *rows_old, vectors, vectors, vectors),
    )(*messages, col_sums, vectors, vector_moment, *grads, *masters, *rows_old, *cols_old)
    news, cols_new, rows_out = results[:4], results[4:8], results[8:12]
    vector_grad, vector_moment_new, vector_new = results[12:]
    factored = []
    for which in range(4):
        factored += [grads[which], rows_out[which], cols_new[which], news[which]]
    return (settle(output_parts), settle(input_parts), *factored, vector_grad, vector_moment_new, vector_new)


def body(*arrays):
    spread, dp_size = lax.axis_size("group"), lax.axis_size("dp")
    rows, images = arrays[3].shape[0], arrays[1].shape[0]
    slots, width = arrays[0].shape[1:]
    folds = arrays[6].shape[0] // rows
    powers = all(size & (size - 1) == 0 for size in (spread, dp_size))
    fits = powers and spread == 4 and dp_size > 2
    fits = fits and arrays[5].shape[1] <= width and folds <= 5
    fits = fits and rows % 16 == 0 and images % PER_STEP == 0 and images > 2 * PER_STEP and images % 16 == 0 and slots % 4 == 0
    return packed_body(*arrays) if fits else general_body(*arrays)


def solution(mesh):
    in_specs = (
        P("dp", "group", None),
        P(("dp", "group"), None),
        P("dp", "group", None),
        P("dp", "group"),
        P("dp", "group"),
        P("dp", "group"),
        P("dp", "group"),
        P(),
        P("dp"),
        P("group"),
        P("dp"),
        P("group"),
        P("dp"),
        P("group"),
        P("dp"),
        P("group"),
        P(),
    )
    out_specs = (
        P("dp", "group", None),
        P("dp", "group", None),
        P("dp", "group"),
        P("dp"),
        P("group"),
        P("dp", "group"),
        P("dp", "group"),
        P("dp"),
        P("group"),
        P("dp", "group"),
        P("dp", "group"),
        P("dp"),
        P("group"),
        P("dp", "group"),
        P("dp", "group"),
        P("dp"),
        P("group"),
        P("dp", "group"),
        P(),
        P(),
        P(),
    )
    return jax.shard_map(body, mesh=mesh, in_specs=in_specs, out_specs=out_specs, check_vma=False)
```

```python
import functools
import math

import jax
import jax.numpy as jnp
from jax import lax
from jax.experimental import pallas as pl
from jax.experimental.pallas import tpu as pltpu
from jax.sharding import PartitionSpec as P

HEAD_DIM = 64
STEP_NUMBER = 10


step_rate = 0.3
norm_epsilon = 1e-06
tiny_square = 1e-30
decay_rate = 1.0 - STEP_NUMBER ** (-0.8)
LOG2_E = 1.4426950408889634


def axis_bits(name):
    count = lax.axis_size(name)
    return [(name, 1 << place) for place in range(count.bit_length() - 1)]


def swap_partner(array, step):
    name, bit = step
    count = lax.axis_size(name)
    return lax.ppermute(array, name, [(rank, rank ^ bit) for rank in range(count)])


def upper_side(step):
    name, bit = step
    return (lax.axis_index(name) & bit) != 0


def gather_blocks(array, steps):
    for step in steps:
        arrived = swap_partner(array, step)
        upper = upper_side(step)
        array = jnp.stack([jnp.where(upper, arrived, array), jnp.where(upper, array, arrived)])
    return array


def scatter_sum(array, steps):
    for step in steps:
        upper = upper_side(step)
        leaving = jnp.where(upper, array[0], array[1]).astype(jnp.bfloat16)
        arrived = swap_partner(leaving, step)
        array = jnp.where(upper, array[1], array[0]).astype(jnp.float32) + arrived.astype(jnp.float32)
    return array


def sum_everywhere(array, steps):
    for step in steps:
        array = array + swap_partner(array, step)
    return array


def sum_parts(parts, steps):
    flat = [part.reshape(-1) for part in parts]
    total = sum_everywhere(jnp.concatenate(flat), steps)
    result, start = [], 0
    for part in parts:
        result.append(total[start : start + part.size].reshape(part.shape))
        start += part.size
    return result


def block_order(steps):
    order = []
    for name in ("dp", "group"):
        bits = sorted((step for step in steps if step[0] == name), key=lambda step: -step[1])
        order.append([steps.index(step) for step in bits])
    return order


def blocks_to_whole(blocks, steps):
    count = len(steps)
    rows, cols = blocks.shape[count:]
    dp_axes, group_axes = block_order(steps)
    dp_axes = [count - 1 - axis for axis in dp_axes]
    group_axes = [count - 1 - axis for axis in group_axes]
    whole = blocks.transpose(dp_axes + [count] + group_axes + [count + 1])
    return whole.reshape(rows << len(dp_axes), cols << len(group_axes))


def whole_to_blocks(whole, steps):
    dp_axes, group_axes = block_order(steps)
    rows = whole.shape[0] >> len(dp_axes)
    cols = whole.shape[1] >> len(group_axes)
    split = whole.reshape([2] * len(dp_axes) + [rows] + [2] * len(group_axes) + [cols])
    places = dp_axes + [len(steps)] + group_axes + [len(steps) + 1]
    return split.transpose([places.index(axis) for axis in range(len(places))])


PER_STEP = 4
FF_CHUNK = 256
vmem_bytes = 60 * 1024 * 1024


def dot(left, right, left_axis=1, right_axis=0):
    return lax.dot_general(
        left, right, (((left_axis,), (right_axis,)), ((), ())), preferred_element_type=jnp.float32
    )


def normal_form(values):
    center = jnp.mean(values, axis=-1, keepdims=True)
    centered = values - center
    spread = jnp.mean(centered * centered, axis=-1, keepdims=True)
    scale = lax.rsqrt(spread + norm_epsilon)
    return centered * scale, scale


def norm_back(grad, unit, scale, gain):
    weighted = grad * gain
    along = jnp.mean(weighted * unit, axis=-1, keepdims=True)
    level = jnp.mean(weighted, axis=-1, keepdims=True)
    return scale * (weighted - level - unit * along)


def column_sum(values):
    return jnp.sum(values, axis=0, keepdims=True)


def pair_mask(length):
    return lax.broadcasted_iota(jnp.int32, (length, 2 * HEAD_DIM), 1) < HEAD_DIM


def stack_heads(pair, first):
    none = jnp.zeros_like(pair)
    return jnp.concatenate([jnp.where(first, pair, none), jnp.where(first, none, pair)], axis=0)


def join_heads(rows, first):
    length = rows.shape[0] // 2
    return jnp.where(first, rows[:length], rows[length:])


def gelu_and_slope(pre):
    bell = jnp.exp2(pre * pre * (-0.5 * LOG2_E))
    base = 1.0 + (0.3275911 * 0.5**0.5) * jnp.abs(pre)
    inverse = pl.reciprocal(base, approx=True)
    inverse = inverse * (2.0 - base * inverse)
    poly = inverse * (
        0.5 * 0.254829592
        + inverse
        * (
            0.5 * -0.284496736
            + inverse
            * (0.5 * 1.421413741 + inverse * (0.5 * -1.453152027 + inverse * (0.5 * 1.061405429)))
        )
    )
    tail = poly * bell
    below = jnp.where(pre >= 0, 1.0 - tail, tail)
    return pre * below, below + pre * bell * 0.3989422804014327


def widen(source_ref, wide_ref, images):
    tiles, total, lanes = wide_ref.shape
    rows_at_once = 8 * images

    @pl.loop(0, total // rows_at_once)
    def _(part):
        rows = pl.ds(pl.multiple_of(part * rows_at_once, rows_at_once), rows_at_once)
        for tile in range(tiles):
            cols = slice(tile * lanes, (tile + 1) * lanes)
            wide_ref[tile, rows, :] = source_ref[rows, cols].astype(jnp.float32)


def narrow(wide_ref, target_ref, images):
    tiles, total, lanes = wide_ref.shape
    rows_at_once = 8 * images

    @pl.loop(0, total // rows_at_once)
    def _(part):
        rows = pl.ds(pl.multiple_of(part * rows_at_once, rows_at_once), rows_at_once)
        for tile in range(tiles):
            cols = slice(tile * lanes, (tile + 1) * lanes)
            target_ref[rows, cols] = wide_ref[tile, rows, :].astype(target_ref.dtype)


def take_image(wide_ref, image, images):
    tiles, total, _ = wide_ref.shape
    rows = pl.ds(image, total // images, images)
    return jnp.concatenate([wide_ref[tile, rows, :] for tile in range(tiles)], axis=1)


def put_image(wide_ref, image, images, values):
    tiles, total, lanes = wide_ref.shape
    rows = pl.ds(image, total // images, images)
    for tile in range(tiles):
        wide_ref[tile, rows, :] = values[:, tile * lanes : (tile + 1) * lanes]


def attention_kernel(
    images, tokens_ref, bias_ref, w_qkv_ref, w_proj_ref, vectors_ref,
    x_ref, qkv_ref, probs_ref, attended_ref, middle_ref, wide_ref, normed_ref,
):
    @pl.when(pl.program_id(0) == 0)
    def _():
        widen(tokens_ref, wide_ref, images)
        to_image_rows(wide_ref, x_ref, images)

    attention_steps(
        x_ref, lambda image: bias_ref[image], w_qkv_ref, w_proj_ref, vectors_ref,
        qkv_ref, probs_ref, attended_ref, middle_ref, normed_ref,
    )


def to_image_rows(wide_ref, x_ref, images):
    length = wide_ref.shape[1] // images

    @pl.loop(0, images)
    def _(image):
        rows = pl.ds(pl.multiple_of(image * length, length), length)
        x_ref[rows, :] = take_image(wide_ref, image, images).astype(jnp.bfloat16)


def attention_steps(
    x_ref, bias_column, w_qkv_ref, w_proj_ref, vectors_ref,
    qkv_ref, probs_ref, attended_ref, middle_ref, normed_ref,
):
    per_step, _, length, _ = probs_ref.shape
    step_rows, width = middle_ref.shape
    base = 0 if x_ref.shape[0] == step_rows else pl.program_id(0) * step_rows

    for image in range(per_step):
        rows = slice(image * length, (image + 1) * length)
        x = x_ref[pl.ds(pl.multiple_of(base + image * length, length), length), :].astype(jnp.float32)
        unit, _ = normal_form(x)
        normed_ref[rows, :] = (unit * vectors_ref[0:1] + vectors_ref[1:2]).astype(jnp.bfloat16)
    for part in range(3):
        cols = slice(part * width, (part + 1) * width)
        projected = dot(normed_ref[...], w_qkv_ref[:, cols])
        if part != 1:
            row = 2 if part == 0 else 3
            projected = projected + vectors_ref[row : row + 1]
        qkv_ref[:, cols] = projected.astype(jnp.bfloat16)

    for image in range(per_step):
        rows = slice(image * length, (image + 1) * length)
        first = pair_mask(length)
        place = lax.broadcasted_iota(jnp.int32, (length, 2 * length), 0)
        asker = lax.broadcasted_iota(jnp.int32, (length, 2 * length), 1)
        asker = jnp.where(asker >= length, asker - length, asker)
        bias = jnp.where(place == asker, 0.0, bias_column(image))
        for pair in range(width // (2 * HEAD_DIM)):
            low = pair * 2 * HEAD_DIM
            queries = stack_heads(qkv_ref[rows, low : low + 2 * HEAD_DIM], first)
            keys = qkv_ref[rows, width + low : width + low + 2 * HEAD_DIM]
            values = qkv_ref[rows, 2 * width + low : 2 * width + low + 2 * HEAD_DIM]
            scores = dot(keys, queries, 1, 1) * (HEAD_DIM**-0.5 * LOG2_E) + bias
            weights = jnp.exp2(scores - jnp.max(scores, axis=0, keepdims=True))
            probs = weights * (1.0 / jnp.sum(weights, axis=0, keepdims=True))
            probs = probs.astype(jnp.bfloat16)
            probs_ref[image, pair] = probs
            attended = join_heads(dot(probs, values, 0, 0), first)
            attended_ref[rows, low : low + 2 * HEAD_DIM] = attended.astype(jnp.bfloat16)

    middle_ref[...] = (
        x_ref[pl.ds(pl.multiple_of(base, length), step_rows), :].astype(jnp.float32)
        + dot(attended_ref[...], w_proj_ref[...])
        + vectors_ref[4:5]
    )


def feed_forward_kernel(
    images, middle_ref, cotangent_ref, attended_ref, w_up_ref, w_down_ref, w_proj_ref, vectors_ref, bias_up_ref,
    output_ref, d_middle_ref, d_attended_ref, up_grad_ref, down_grad_ref, proj_grad_ref, vector_sums_ref, up_sums_ref,
    wide_ref, *scratches,
):
    up_total_ref, down_total_ref, proj_total_ref = scratches[-3:]

    @pl.when(pl.program_id(0) == 0)
    def _():
        widen(cotangent_ref, wide_ref, images)

    feed_forward_steps(
        images, middle_ref, attended_ref, w_up_ref, w_down_ref, w_proj_ref, vectors_ref, bias_up_ref,
        d_middle_ref, d_attended_ref, vector_sums_ref, up_sums_ref, wide_ref, *scratches,
    )

    @pl.when(pl.program_id(0) == pl.num_programs(0) - 1)
    def _():
        narrow(wide_ref, output_ref, images)
        up_grad_ref[...] = up_total_ref[...].astype(jnp.bfloat16)
        down_grad_ref[...] = down_total_ref[...].T.astype(jnp.bfloat16)
        proj_grad_ref[...] = proj_total_ref[...].astype(jnp.bfloat16)


def feed_forward_steps(
    images, middle_ref, attended_ref, w_up_ref, w_down_ref, w_proj_ref, vectors_ref, bias_up_ref,
    d_middle_ref, d_attended_ref, vector_sums_ref, up_sums_ref,
    wide_ref, normed_ref, normed_t_ref, dy_ref, dy_t_ref, unit_ref, scale_ref, ahead_ref, back_ref,
    up_total_ref, down_total_ref, proj_total_ref,
):
    step = pl.program_id(0)
    length = wide_ref.shape[1] // images
    hidden = w_up_ref.shape[1]
    per_step = middle_ref.shape[0] // length

    @pl.when(step == 0)
    def _():
        for total in (up_total_ref, down_total_ref, proj_total_ref, vector_sums_ref, up_sums_ref):
            total[...] = jnp.zeros_like(total)

    for image in range(per_step):
        rows = slice(image * length, (image + 1) * length)
        dy = take_image(wide_ref, step * per_step + image, images)
        dy_ref[rows, :] = dy.astype(jnp.bfloat16)
        vector_sums_ref[3:4] += column_sum(dy)
        unit, scale = normal_form(middle_ref[rows, :])
        unit_ref[rows, :] = unit
        scale_ref[rows, :] = jnp.broadcast_to(scale, (length, scale_ref.shape[1]))
        normed_ref[rows, :] = (unit * vectors_ref[5:6] + vectors_ref[6:7]).astype(jnp.bfloat16)
    normed_t_ref[...] = normed_ref[...].T
    dy_t_ref[...] = dy_ref[...].T
    chunks = hidden // FF_CHUNK

    def cols_of(chunk):
        return slice(chunk * FF_CHUNK, (chunk + 1) * FF_CHUNK)

    def into(chunk):
        cols = cols_of(chunk)
        pre = dot(normed_ref[...], w_up_ref[:, cols])
        return pre + bias_up_ref[:, cols], dot(dy_ref[...], w_down_ref[cols, :], 1, 1)

    def across(pre, d_active):
        active, slope = gelu_and_slope(pre)
        return active.astype(jnp.bfloat16), (d_active * slope).astype(jnp.bfloat16)

    def out_of(chunk, active, d_hidden):
        cols = cols_of(chunk)
        ahead, back = dot(active, w_down_ref[cols, :]), dot(d_hidden, w_up_ref[:, cols], 1, 1)
        if chunk == 0:
            ahead_ref[...] = ahead
            back_ref[...] = back
        else:
            ahead_ref[...] += ahead
            back_ref[...] += back
        down_total_ref[:, cols] += dot(dy_t_ref[...], active)
        up_total_ref[:, cols] += dot(normed_t_ref[...], d_hidden)
        up_sums_ref[:, cols] += column_sum(d_hidden.astype(jnp.float32))

    entered, crossed = into(0), None
    for chunk in range(chunks + 1):
        next_entered = into(chunk + 1) if chunk + 1 < chunks else None
        next_crossed = across(*entered) if chunk < chunks else None
        if crossed is not None:
            out_of(chunk - 1, *crossed)
        entered, crossed = next_entered, next_crossed

    for image in range(per_step):
        rows = slice(image * length, (image + 1) * length)
        output = middle_ref[rows, :] + ahead_ref[rows, :] + vectors_ref[11:12]
        put_image(wide_ref, step * per_step + image, images, output)
        unit = unit_ref[rows, :]
        grad = back_ref[rows, :]
        vector_sums_ref[1:2] += column_sum(grad * unit)
        vector_sums_ref[2:3] += column_sum(grad)
        d_middle = dy_ref[rows, :].astype(jnp.float32) + norm_back(
            grad, unit, scale_ref[rows, 0:1], vectors_ref[5:6]
        )
        d_middle_ref[rows, :] = d_middle
        d_branch = d_middle.astype(jnp.bfloat16)
        dy_ref[rows, :] = d_branch
        vector_sums_ref[0:1] += column_sum(d_branch.astype(jnp.float32))
    proj_total_ref[...] += dot(attended_ref[...], dy_ref[...], 0, 0)
    d_attended_ref[...] = dot(dy_ref[...], w_proj_ref[...], 1, 1).astype(jnp.bfloat16)


def attention_back_kernel(
    images, x_ref, qkv_ref, probs_ref, d_attended_ref, d_middle_ref, w_qkv_ref, vectors_ref,
    input_grad_ref, qkv_grad_ref, vector_sums_ref, wide_ref, normed_ref, d_projected_ref, back_ref, qkv_total_ref,
):
    @pl.when(pl.program_id(0) == 0)
    def _():
        qkv_total_ref[...] = jnp.zeros_like(qkv_total_ref)
        vector_sums_ref[...] = jnp.zeros_like(vector_sums_ref)

    def put(image, rows, values):
        put_image(wide_ref, image, images, values)

    attention_back_steps(
        x_ref, qkv_ref, probs_ref, d_attended_ref, vectors_ref, vector_sums_ref, normed_ref, d_projected_ref, qkv_total_ref
    )
    input_back_steps(
        put, probs_ref.shape[2], x_ref, d_projected_ref, d_middle_ref, w_qkv_ref, vectors_ref, vector_sums_ref, back_ref
    )

    @pl.when(pl.program_id(0) == pl.num_programs(0) - 1)
    def _():
        narrow(wide_ref, input_grad_ref, images)
        qkv_grad_ref[...] = qkv_total_ref[...].astype(jnp.bfloat16)


def attention_back_steps(
    x_ref, qkv_ref, probs_ref, d_attended_ref, vectors_ref, vector_sums_ref, normed_ref, d_projected_ref, qkv_total_ref
):
    width = x_ref.shape[1]
    length = probs_ref.shape[2]
    per_step = probs_ref.shape[0]

    for image in range(per_step):
        rows = slice(image * length, (image + 1) * length)
        first = pair_mask(length)
        for pair in range(width // (2 * HEAD_DIM)):
            low = pair * 2 * HEAD_DIM
            cols = [slice(part * width + low, part * width + low + 2 * HEAD_DIM) for part in range(3)]
            queries = stack_heads(qkv_ref[rows, cols[0]], first)
            keys = qkv_ref[rows, cols[1]]
            values = qkv_ref[rows, cols[2]]
            probs = probs_ref[image, pair]
            d_attended = stack_heads(d_attended_ref[rows, cols[0]], first)
            d_projected_ref[rows, cols[2]] = dot(probs, d_attended).astype(jnp.bfloat16)
            d_probs = dot(values, d_attended, 1, 1)
            probs = probs.astype(jnp.float32)
            along = jnp.sum(d_probs * probs, axis=0, keepdims=True)
            d_scores = (probs * (d_probs - along)).astype(jnp.bfloat16)
            scale = HEAD_DIM**-0.5
            d_queries = join_heads(dot(d_scores, keys, 0, 0), first) * scale
            d_projected_ref[rows, cols[0]] = d_queries.astype(jnp.bfloat16)
            d_projected_ref[rows, cols[1]] = (dot(d_scores, queries) * scale).astype(jnp.bfloat16)

    vector_sums_ref[2:3] += column_sum(d_projected_ref[:, :width].astype(jnp.float32))
    vector_sums_ref[3:4] += column_sum(d_projected_ref[:, 2 * width :].astype(jnp.float32))
    for image in range(per_step):
        rows = slice(image * length, (image + 1) * length)
        unit, _ = normal_form(x_ref[rows, :].astype(jnp.float32))
        normed_ref[rows, :] = (unit * vectors_ref[0:1] + vectors_ref[1:2]).astype(jnp.bfloat16)
    qkv_total_ref[...] += dot(normed_ref[...], d_projected_ref[...], 0, 0)


def input_back_steps(
    put, length, x_ref, d_projected_ref, d_middle_ref, w_qkv_ref, vectors_ref, vector_sums_ref, back_ref
):
    step = pl.program_id(0)
    per_step = x_ref.shape[0] // length
    back_ref[...] = dot(d_projected_ref[...], w_qkv_ref[...], 1, 1)
    for image in range(per_step):
        rows = slice(image * length, (image + 1) * length)
        unit, scale = normal_form(x_ref[rows, :].astype(jnp.float32))
        grad = back_ref[rows, :]
        vector_sums_ref[0:1] += column_sum(grad * unit)
        vector_sums_ref[1:2] += column_sum(grad)
        d_input = d_middle_ref[rows, :] + norm_back(grad, unit, scale, vectors_ref[0:1])
        put(step * per_step + image, rows, d_input)


def whole_block(shape):
    return pl.BlockSpec(shape, lambda step: (0,) * len(shape))


def step_block(shape, first=0):
    return pl.BlockSpec(shape, lambda step: (first + step,) + (0,) * (len(shape) - 1))


def scratch(*shape, dtype=jnp.float32):
    return pltpu.VMEM(shape, dtype)


def call_kernel(kernel, statics, steps, ins, outs, scratches, operands, flops, transcendentals=0, first_step=0, aliases={}):
    in_specs = [
        pl.BlockSpec(memory_space=pltpu.SMEM)
        if block == "place"
        else pl.BlockSpec(memory_space=pl.ANY)
        if block == "await"
        else whole_block(op.shape) if block is None else step_block(block, first_step)
        for op, block in zip(operands, ins)
    ]
    out_specs = [
        whole_block(shape) if block is None else step_block(block, first_step) for shape, dtype, block in outs
    ]
    moved = sum(op.size * op.dtype.itemsize for op in operands) + sum(
        math.prod(shape) * jnp.dtype(dtype).itemsize for shape, dtype, block in outs
    )
    return pl.pallas_call(
        functools.partial(kernel, *statics),
        grid=(steps,),
        in_specs=in_specs,
        out_specs=out_specs,
        out_shape=[jax.ShapeDtypeStruct(shape, dtype) for shape, dtype, block in outs],
        scratch_shapes=scratches,
        input_output_aliases=aliases,
        compiler_params=pltpu.CompilerParams(vmem_limit_bytes=vmem_bytes),
        cost_estimate=pl.CostEstimate(
            flops=flops * 8, bytes_accessed=moved, transcendentals=transcendentals
        ),
    )(*operands)


def attention_forward(tokens, bias, w_qkv, w_proj, vectors):
    images, length, _ = bias.shape
    total, width = tokens.shape
    pairs = width // (2 * HEAD_DIM)
    rows = PER_STEP * length
    low, high = jnp.bfloat16, jnp.float32
    outs = [
        ((total, width), low, None),
        ((total, 3 * width), low, (rows, 3 * width)),
        ((images, pairs, length, 2 * length), low, (PER_STEP, pairs, length, 2 * length)),
        ((total, width), low, (rows, width)),
        ((total, width), high, (rows, width)),
    ]
    return call_kernel(
        attention_kernel, (images,), images // PER_STEP,
        [None, (PER_STEP, length, 1), None, None, None], outs,
        [scratch(width // 128, total, 128), scratch(rows, width, dtype=low)],
        (tokens, bias, w_qkv, w_proj, vectors),
        2 * total * width * 4 * width + 8 * total * length * width,
    )


def feed_forward(images, middle, cotangent, attended, w_up, w_down, w_proj, vectors):
    total, width = middle.shape
    hidden = w_up.shape[1]
    rows = total // images * PER_STEP
    low, high = jnp.bfloat16, jnp.float32
    block = (rows, width)
    outs = [
        ((total, width), low, None),
        ((total, width), high, block),
        ((total, width), low, block),
        ((width, hidden), low, None),
        ((hidden, width), low, None),
        ((width, width), low, None),
        ((8, width), high, None),
        ((1, hidden), high, None),
    ]
    scratches = [
        scratch(width // 128, total, 128),
        scratch(rows, width, dtype=low),
        scratch(width, rows, dtype=low),
        scratch(rows, width, dtype=low),
        scratch(width, rows, dtype=low),
        scratch(rows, width),
        scratch(rows, 128),
        scratch(rows, width),
        scratch(rows, width),
        scratch(width, hidden),
        scratch(width, hidden),
        scratch(width, width),
    ]
    return call_kernel(
        feed_forward_kernel, (images,), images // PER_STEP,
        [block, None, block, None, None, None, None, None], outs, scratches,
        (middle, cotangent, attended, w_up, w_down, w_proj, vectors, vectors[7:11].reshape(1, hidden)),
        12 * total * width * hidden + 4 * total * width * width, total * hidden,
    )


def attention_back(x, qkv, probs, d_attended, d_middle, w_qkv, vectors):
    images, pairs, length, _ = probs.shape
    total, width = x.shape
    rows = PER_STEP * length
    low, high = jnp.bfloat16, jnp.float32
    block = (rows, width)
    outs = [
        ((total, width), low, None),
        ((width, 3 * width), low, None),
        ((8, width), high, None),
    ]
    scratches = [
        scratch(width // 128, total, 128),
        scratch(rows, width, dtype=low),
        scratch(rows, 3 * width, dtype=low),
        scratch(rows, width),
        scratch(width, 3 * width),
    ]
    return call_kernel(
        attention_back_kernel, (images,), images // PER_STEP,
        [block, (rows, 3 * width), (PER_STEP, pairs, length, 2 * length), block, block, None, None],
        outs, scratches, (x, qkv, probs, d_attended, d_middle, w_qkv, vectors),
        4 * total * width * 3 * width + 16 * total * length * width,
    )

def linear_place():
    return lax.axis_index("dp") * lax.axis_size("group") + lax.axis_index("group")


def permute(array, mask):
    count = lax.axis_size("dp") * lax.axis_size("group")
    return lax.ppermute(array, ("dp", "group"), [(rank, rank ^ mask) for rank in range(count)])


def direct_masks(bits):
    masks = [0]
    for bit in bits:
        masks = masks + [mask | bit for mask in masks]
    return masks[1:]


def scatter_step(held, bits):
    masks = direct_masks(bits)
    size = held.shape[0] // (len(masks) + 1)
    parts = [
        permute(held[size * (at + 1) : size * (at + 2)].astype(jnp.bfloat16), mask)
        for at, mask in enumerate(masks)
    ]
    return held[:size], parts


def add_wide(first, *rest):
    total = first.astype(jnp.float32)
    for part in rest:
        total = total + part.astype(jnp.float32)
    return total


def packed_place(mask, spread, count):
    return ((mask >> 1) & (spread - 1)) * (count // (2 * spread)) + (mask >> (spread.bit_length()))


def scatter_step(held, bits):
    masks = direct_masks(bits)
    size = held.shape[0] // (len(masks) + 1)
    parts = [
        permute(held[size * (at + 1) : size * (at + 2)].astype(jnp.bfloat16), mask)
        for at, mask in enumerate(masks)
    ]
    return held[:size], parts


def add_wide(first, *rest):
    total = first.astype(jnp.float32)
    for part in rest:
        total = total + part.astype(jnp.float32)
    return total


def packed_place(mask, spread, count):
    return ((mask >> 1) & (spread - 1)) * (count // (2 * spread)) + (mask >> (spread.bit_length()))


def gather_step(held, bits):
    return held + [permute(part, mask) for mask in direct_masks(bits) for part in held]


def gathered_place(mask, count):
    return (mask & 1) * (count // 2) + ((mask >> 2) & 1) * (count // 4) + (mask >> 3) * 2 + ((mask >> 1) & 1)


def unpack(place_ref, block_refs, packed_ref, put, dp_size, spread):
    place = place_ref[0]
    size = block_refs[0].shape[0]
    for at, block_ref in enumerate(block_refs):
        packed_ref[at * size : (at + 1) * size] = block_ref[...]
    count = dp_size * spread
    for row in range(dp_size):
        for col in range(spread):
            put(row, col, packed_ref[gathered_place((row * spread + col) ^ place, count)])


def pack(place_ref, take, keep_ref, leave_ref, dp_size, spread):
    place = place_ref[0]
    odd = (place & 1) == 1
    for row in range(dp_size):
        for col in range(0, spread, 2):
            at = packed_place((row * spread + col) ^ place, spread, dp_size * spread)
            even_block, odd_block = take(row, col), take(row, col + 1)
            keep_ref[at] = jnp.where(odd, odd_block, even_block)
            leave_ref[at] = jnp.where(odd, even_block, odd_block)


def narrow_pieces(place_ref, wide_ref, piece_refs, spread):
    tiles, _, lanes = wide_ref.shape
    rows_of_piece = piece_refs[0].shape[0]
    step = 64
    group = place_ref[0] & (spread - 1)
    for relative, piece_ref in enumerate(piece_refs):
        base = (group ^ relative) * rows_of_piece

        @pl.loop(0, rows_of_piece // step)
        def _(part):
            target = pl.ds(pl.multiple_of(part * step, step), step)
            source = pl.ds(pl.multiple_of(base + part * step, step), step)
            for tile in range(tiles):
                cols = slice(tile * lanes, (tile + 1) * lanes)
                piece_ref[target, cols] = wide_ref[tile, source, :].astype(jnp.bfloat16)


def general_body(
    tokens,
    keep_mask,
    cotangent,
    qkv_weight,
    proj_weight,
    up_weight,
    down_weight,
    vectors,
    qkv_rows,
    qkv_cols,
    proj_rows,
    proj_cols,
    up_rows,
    up_cols,
    down_rows,
    down_cols,
    vector_moment,
):
    masters = (qkv_weight, proj_weight, up_weight, down_weight)
    lowered = tuple((master.astype(jnp.bfloat16) for master in masters))
    dp_bits, group_bits = axis_bits("dp"), axis_bits("group")
    gather_steps = dp_bits[1:] + group_bits[1:] + dp_bits[:1] + group_bits[:1]
    scatter_steps = gather_steps[::-1]
    w_qkv, w_proj, w_up, w_down = tuple(
        blocks_to_whole(gather_blocks(part, gather_steps), gather_steps) for part in lowered
    )
    spread = lax.axis_size("group")

    def slots_in(array):
        held, slots, width = array.shape
        parts = array.transpose(1, 0, 2).reshape(slots, spread, held // spread, width)
        parts = lax.all_to_all(
            parts.transpose(1, 0, 2, 3), "group", split_axis=0, concat_axis=0, tiled=True
        )
        return parts.reshape(spread * slots * (held // spread), width)

    def slots_out(array):
        held, slots, width = tokens.shape
        parts = array.reshape(spread, slots, held // spread, width)
        parts = lax.all_to_all(parts, "group", split_axis=0, concat_axis=0, tiled=True)
        return parts.transpose(1, 0, 2, 3).reshape(slots, held, width).transpose(1, 0, 2)

    images = keep_mask.shape[0]
    bias = jnp.where(keep_mask > 0, 0.0, -1e30)[:, :, None]
    x, qkv, probs, attended, middle = attention_forward(
        slots_in(tokens), bias, w_qkv, w_proj, vectors
    )
    output, d_middle, d_attended, up_grad, down_grad, proj_grad, ff_sums, up_sums = feed_forward(
        images, middle, slots_in(cotangent), attended, w_up, w_down, w_proj, vectors
    )
    block_output = slots_out(output)
    d_input, qkv_grad, att_sums = attention_back(
        x, qkv, probs, d_attended, d_middle, w_qkv, vectors
    )
    input_grad = slots_out(d_input)
    local_vectors = jnp.concatenate(
        [att_sums[:4], ff_sums[:3], up_sums.reshape(4, -1), ff_sums[3:4]], axis=0
    )
    vector_grad = sum_everywhere(local_vectors, group_bits + dp_bits)
    local_grads = (qkv_grad, proj_grad, up_grad, down_grad)
    owned = tuple(
        scatter_sum(whole_to_blocks(part, scatter_steps), scatter_steps) for part in local_grads
    )
    squares = tuple((gradient * gradient + tiny_square for gradient in owned))
    row_parts = tuple((jnp.sum(square, axis=1) for square in squares)) + tuple(
        (jnp.sum(master * master, axis=1) for master in masters)
    )
    row_sums = sum_parts(row_parts, group_bits)
    rows_old = (qkv_rows, proj_rows, up_rows, down_rows)
    cols_old = (qkv_cols, proj_cols, up_cols, down_cols)
    total_cols = tuple((gradient.shape[1] * lax.axis_size("group") for gradient in owned))
    total_rows = tuple((gradient.shape[0] * lax.axis_size("dp") for gradient in owned))
    rows_new = tuple(
        (
            decay_rate * rows_old[which] + (1.0 - decay_rate) * row_sums[which] / total_cols[which]
            for which in range(4)
        )
    )
    col_parts = (
        tuple((jnp.sum(square, axis=0) for square in squares))
        + tuple((jnp.sum(row_stat) for row_stat in rows_new))
        + tuple((jnp.sum(row_sums[4 + which]) for which in range(4)))
    )
    col_sums = sum_parts(col_parts, dp_bits)
    results = []
    for which in range(4):
        cols_new = (
            decay_rate * cols_old[which] + (1.0 - decay_rate) * col_sums[which] / total_rows[which]
        )
        mean_rows = col_sums[4 + which] / total_rows[which]
        spread = jnp.sqrt(col_sums[8 + which] / (total_rows[which] * total_cols[which]))
        second = rows_new[which][:, None] * cols_new[None, :] / mean_rows
        updated = masters[which] - step_rate * spread * owned[which] * lax.rsqrt(second)
        results.append((owned[which], rows_new[which], cols_new, updated))
    vector_moment_new = decay_rate * vector_moment + (1.0 - decay_rate) * (
        vector_grad * vector_grad + tiny_square
    )
    row_spread = jnp.sqrt(jnp.mean(vectors * vectors, axis=1, keepdims=True))
    vector_new = vectors - step_rate * row_spread * vector_grad * lax.rsqrt(vector_moment_new)
    return (
        block_output,
        input_grad,
        results[0][0],
        results[0][1],
        results[0][2],
        results[0][3],
        results[1][0],
        results[1][1],
        results[1][2],
        results[1][3],
        results[2][0],
        results[2][1],
        results[2][2],
        results[2][3],
        results[3][0],
        results[3][1],
        results[3][2],
        results[3][3],
        vector_grad,
        vector_moment_new,
        vector_new,
    )


def first_attention_kernel(images, dp_size, spread, place_ref, tokens_ref, *refs):
    blocks, refs = refs[:4], refs[4:]
    keep_ref, vectors_ref, *outs, x_ref, w_qkv_ref, w_proj_ref = refs[:-4]
    packed_ref, wide_ref, bias_ref, normed_ref = refs[-4:]
    rows = packed_ref.shape[1]
    qkv_cols, proj_cols = w_qkv_ref.shape[1] // spread, w_proj_ref.shape[1] // spread

    @pl.when(pl.program_id(0) == 0)
    def _():
        widen(tokens_ref, wide_ref, images)
        to_image_rows(wide_ref, x_ref, images)

        def put(row, col, block):
            down = slice(row * rows, (row + 1) * rows)
            w_qkv_ref[down, col * qkv_cols : (col + 1) * qkv_cols] = block[:, :qkv_cols]
            w_proj_ref[down, col * proj_cols : (col + 1) * proj_cols] = block[:, qkv_cols:]

        unpack(place_ref, blocks, packed_ref, put, dp_size, spread)

    attention_part(0, x_ref, keep_ref, w_qkv_ref, w_proj_ref, vectors_ref, *outs, bias_ref, normed_ref)


def next_attention_kernel(start, x_ref, keep_ref, w_qkv_ref, w_proj_ref, vectors_ref, *refs):
    attention_part(start, x_ref, keep_ref, w_qkv_ref, w_proj_ref, vectors_ref, *refs[-6:])


def attention_part(
    start, x_ref, keep_ref, w_qkv_ref, w_proj_ref, vectors_ref,
    qkv_ref, probs_ref, attended_ref, middle_ref, bias_ref, normed_ref,
):
    @pl.when(pl.program_id(0) == 0)
    def _():
        bias_ref[...] = jnp.where(keep_ref[...] > 0, 0.0, -1e30).T

    def bias_column(image):
        here = start + pl.program_id(0) * probs_ref.shape[0] + image
        lane = lax.broadcasted_iota(jnp.int32, bias_ref.shape, 1)
        return row_sum(jnp.where(lane == here, bias_ref[...], 0.0))

    attention_steps(
        x_ref, bias_column, w_qkv_ref, w_proj_ref, vectors_ref,
        qkv_ref, probs_ref, attended_ref, middle_ref, normed_ref,
    )


def feed_forward_packed_kernel(images, dp_size, spread, place_ref, *refs):
    cotangent_ref, blocks, refs = refs[0], refs[1:5], refs[5:]
    middle_ref, attended_ref, w_proj_ref, vectors_ref = refs[:4]
    outputs, refs = refs[4 : 4 + spread], refs[4 + spread :]
    d_middle_ref, d_attended_ref, keep_ref, leave_ref, proj_total_ref, vector_sums_ref, up_sums_ref = refs[:7]
    w_up_ref, w_down_ref, down_low_ref, packed_ref, bias_up_ref, wide_ref = refs[7:13]
    scratches = refs[13:]
    width = w_up_ref.shape[0]
    up_total_ref, down_total_ref = scratches[-2:]
    rows = packed_ref.shape[1]
    up_cols = w_up_ref.shape[1] // spread
    out_cols = w_down_ref.shape[1] // spread
    folds = w_down_ref.shape[0] // w_up_ref.shape[0]

    @pl.when(pl.program_id(0) == 0)
    def _():
        widen(cotangent_ref, wide_ref, images)
        for fold in range(bias_up_ref.shape[1] // width):
            bias_up_ref[:, fold * width : (fold + 1) * width] = vectors_ref[7 + fold : 8 + fold]

        def put(row, col, block):
            w_up_ref[row * rows : (row + 1) * rows, col * up_cols : (col + 1) * up_cols] = block[:, :up_cols]
            for fold in range(folds):
                down = (row * folds + fold) * rows
                start = up_cols + fold * out_cols
                w_down_ref[down : down + rows, col * out_cols : (col + 1) * out_cols] = block[
                    :, start : start + out_cols
                ]

        unpack(place_ref, blocks, packed_ref, put, dp_size, spread)

    feed_forward_steps(
        images, middle_ref, attended_ref, w_up_ref, w_down_ref, w_proj_ref, vectors_ref, bias_up_ref,
        d_middle_ref, d_attended_ref, vector_sums_ref, up_sums_ref, wide_ref, *scratches, proj_total_ref,
    )

    @pl.when(pl.program_id(0) == pl.num_programs(0) - 1)
    def _():
        narrow_pieces(place_ref, wide_ref, outputs, spread)
        down_low_ref[...] = down_total_ref[...].T.astype(jnp.bfloat16)

        def take(row, col):
            across = slice(row * rows, (row + 1) * rows)
            cols = slice(col * out_cols, (col + 1) * out_cols)
            parts = [up_total_ref[across, col * up_cols : (col + 1) * up_cols].astype(jnp.bfloat16)]
            for fold in range(folds):
                down = (row * folds + fold) * rows
                parts.append(down_low_ref[down : down + rows, cols])
            return jnp.concatenate(parts, axis=1)

        pack(place_ref, take, keep_ref, leave_ref, dp_size, spread)


def attention_back_packed_kernel(
    dp_size, spread, place_ref, x_ref, qkv_ref, probs_ref, d_attended_ref, vectors_ref, proj_total_ref, _,
    d_projected_ref, keep_ref, leave_ref, vector_sums_ref, normed_ref, total_ref,
):
    @pl.when(pl.program_id(0) == 0)
    def _():
        total_ref[...] = jnp.zeros_like(total_ref)
        vector_sums_ref[...] = jnp.zeros_like(vector_sums_ref)

    attention_back_steps(
        x_ref, qkv_ref, probs_ref, d_attended_ref, vectors_ref, vector_sums_ref, normed_ref, d_projected_ref, total_ref
    )

    @pl.when(pl.program_id(0) == pl.num_programs(0) - 1)
    def _():
        rows = keep_ref.shape[1]
        qkv_cols, proj_cols = total_ref.shape[1] // spread, proj_total_ref.shape[1] // spread

        def take(row, col):
            down = slice(row * rows, (row + 1) * rows)
            parts = [
                total_ref[down, col * qkv_cols : (col + 1) * qkv_cols],
                proj_total_ref[down, col * proj_cols : (col + 1) * proj_cols],
            ]
            return jnp.concatenate(parts, axis=1).astype(jnp.bfloat16)

        pack(place_ref, take, keep_ref, leave_ref, dp_size, spread)


def first_input_kernel(
    length, x_ref, d_projected_ref, d_middle_ref, w_qkv_ref, vectors_ref, before_ref,
    d_input_ref, vector_sums_ref, back_ref,
):
    @pl.when(pl.program_id(0) == 0)
    def _():
        vector_sums_ref[...] = before_ref[...]

    def put(image, rows, values):
        d_input_ref[rows, :] = values.astype(jnp.bfloat16)

    input_back_steps(
        put, length, x_ref, d_projected_ref, d_middle_ref, w_qkv_ref, vectors_ref, vector_sums_ref, back_ref
    )


def last_input_kernel(
    images, spread, length, first, place_ref, x_ref, d_projected_ref, d_middle_ref, w_qkv_ref, vectors_ref, before_ref,
    d_input_ref, *refs,
):
    pieces, (vector_sums_ref, wide_ref, back_ref) = refs[:spread], refs[spread:]

    @pl.when(pl.program_id(0) == 0)
    def _():
        vector_sums_ref[...] = before_ref[...]
        for image in range(first):
            rows = slice(image * length, (image + 1) * length)
            put_image(wide_ref, image, images, d_input_ref[rows, :].astype(jnp.float32))

    def put(image, rows, values):
        put_image(wide_ref, first + image, images, values)

    input_back_steps(
        put, length, x_ref, d_projected_ref, d_middle_ref, w_qkv_ref, vectors_ref, vector_sums_ref, back_ref
    )

    @pl.when(pl.program_id(0) == pl.num_programs(0) - 1)
    def _():
        narrow_pieces(place_ref, wide_ref, pieces, spread)


def cut(array_ref, parts_ref):
    count = parts_ref.shape[2]
    for member in range(parts_ref.shape[0]):
        parts_ref[member] = array_ref[:, member * count : (member + 1) * count, :]


def pack_kernel(qkv_ref, proj_ref, up_ref, down_ref, pack_ref):
    rows, start = pack_ref.shape[0], 0
    parts = [qkv_ref[...], proj_ref[...], up_ref[...]]
    parts += [down_ref[fold * rows : (fold + 1) * rows, :] for fold in range(down_ref.shape[0] // rows)]
    for part in parts:
        pack_ref[:, start : start + part.shape[1]] = part.astype(jnp.bfloat16)
        start += part.shape[1]


def token_kernel(array_ref, own_ref, arrived_ref, _, parts_ref, first_ref, second_ref):
    start = first_ref.shape[2]
    for at, pack_ref in enumerate((own_ref, arrived_ref)):
        first_ref[at] = pack_ref[:, :start]
        second_ref[at] = pack_ref[:, start:]
    cut(array_ref, parts_ref)


def join_kernel(count, *refs):
    size = refs[0].shape[0]
    for at, part_ref in enumerate(refs[:count]):
        refs[-1][at * size : (at + 1) * size] = part_ref[...]


def settle_kernel(spread, place_ref, *refs):
    lists, output_ref = refs[:-1], refs[-1]
    group = place_ref[0] & (spread - 1)
    count = lists[0].shape[1]
    share = len(lists) // spread * count
    for at, piece_ref in enumerate(lists):
        relative, part = at % spread, at // spread
        start = pl.multiple_of((group ^ relative) * share + part * count, count)
        output_ref[:, pl.ds(start, count), :] = piece_ref[...]


def lane_table(rows, columns):
    lane = lax.broadcasted_iota(jnp.int32, (rows, 128), 1)
    table = jnp.zeros((rows, 128), jnp.float32)
    for at, column in enumerate(columns):
        table = jnp.where(lane == at, column, table)
    return table


def added(parts):
    while len(parts) > 1:
        parts = [sum(parts[at : at + 2][1:], parts[at]) for at in range(0, len(parts), 2)]
    return parts[0]


def row_sum(values):
    return jnp.sum(values, axis=1, keepdims=True)


def after_kernel(*refs):
    pass


def add_kernel(count, keep_ref, arrived_ref, *refs):
    parts = refs[-count:]
    size = parts[0].shape[0]
    for at, part_ref in enumerate(parts):
        rows = slice(at * size, (at + 1) * size)
        total = keep_ref[rows].astype(jnp.float32) + arrived_ref[rows].astype(jnp.float32)
        part_ref[...] = total.astype(part_ref.dtype)


def gradient_kernel(count, *refs):
    block_parts, sums, refs = refs[:count], refs[count : count + 3], refs[count + 3 :]
    masters, rows_old, refs = refs[:4], refs[4:8], refs[9:]
    grads, (row_ref, message_ref) = refs[:4], refs[4:]
    blocks = added([part[0].astype(jnp.float32) for part in block_parts])
    rows, up_cols = grads[2].shape
    qkv_cols, out_cols = grads[0].shape[1], grads[1].shape[1]
    folds = grads[3].shape[0] // rows
    up = blocks[:, :up_cols]
    downs = [blocks[:, up_cols + fold * out_cols :][:, :out_cols] for fold in range(folds)]
    start = up_cols + folds * out_cols
    qkv = blocks[:, start : start + qkv_cols]
    proj = blocks[:, start + qkv_cols :]
    grads[0][...] = qkv
    grads[1][...] = proj
    grads[2][...] = up
    for fold in range(folds):
        grads[3][fold * rows : (fold + 1) * rows, :] = downs[fold]
    squares = [part * part + tiny_square for part in (qkv, proj, up, *downs)]
    row_ref[...] = lane_table(rows, [row_sum(square) for square in squares]).T[: row_ref.shape[0], :]
    width = message_ref.shape[1]
    message_ref[...] = jnp.zeros_like(message_ref)
    for at, square in enumerate((*squares[:3], added(squares[3:]))):
        message_ref[at : at + 1, : square.shape[1]] = column_sum(square)
    scalars = [column_sum(row_sum(master[...] * master[...])) for master in masters]
    scalars += [row_sum(part[...].reshape(1, part.shape[0])) for part in rows_old]
    message_ref[4:5, :128] = lane_table(1, scalars)
    att_ref, ff_ref, up_ref = sums
    count = up_ref.shape[1] // width
    message_ref[8:12, :] = att_ref[:4]
    message_ref[12:15, :] = ff_ref[:3]
    for at in range(count):
        message_ref[15 + at : 16 + at, :] = up_ref[:, at * width : (at + 1) * width]
    message_ref[15 + count : 16 + count, :] = ff_ref[3:4]


def column_kernel(row_ref, *refs):
    parts, (cols_ref, message_ref) = refs[:-2], refs[-2:]
    total = added([part[...] for part in parts])
    cols_ref[...] = total[:8]
    width = total.shape[1]
    rows = row_ref.shape[1]
    message_ref[...] = jnp.zeros_like(message_ref)
    message_ref[:8, :rows] = row_ref[...]
    columns = [row_sum(total[which : which + 1]) for which in range(4)]
    squares = [total[4:5, which : which + 1] for which in range(4)]
    message_ref[8:9, :] = lane_table(1, columns + squares)
    for tile in range(width // 128):
        message_ref[16 * (tile + 1) : 16 * (tile + 2), :] = total[8:, tile * 128 : (tile + 1) * 128]


def update_kernel(count, heights, widths, *refs):
    messages, refs = refs[:count], refs[count:]
    cols_ref, vectors_ref, moment_ref, refs = refs[0], refs[1], refs[2], refs[3:]
    grads, masters, rows_old, cols_old, refs = refs[:4], refs[4:8], refs[8:12], refs[12:16], refs[16:]
    news, cols_new, rows_out, refs = refs[:4], refs[4:8], refs[8:12], refs[12:]
    vector_grad_ref, moment_new_ref, vector_new_ref = refs
    sums = added([message[...] for message in messages])
    height = grads[0].shape[0]
    folds = grads[3].shape[0] // height
    lanes = [[0], [1], [2], list(range(3, 3 + folds))]
    share = 1.0 - decay_rate
    for which in range(4):
        entries = heights[which] * widths[which]
        cols = cols_old[which].shape[0]
        new = decay_rate * cols_old[which][...].reshape(1, cols) + share / heights[which] * cols_ref[
            which : which + 1, :cols
        ]
        cols_new[which][...] = new[0]
        old_total = cols_ref[4:5, 4 + which : 5 + which]
        mean_rows = (decay_rate * old_total + share / widths[which] * sums[8:9, which : which + 1]) / heights[which]
        rate = step_rate * jnp.sqrt(sums[8:9, 4 + which : 5 + which] / entries)
        across = new / mean_rows
        old = rows_old[which][...].reshape(1, len(lanes[which]) * height)
        row_sums = jnp.concatenate([sums[lane : lane + 1, :height] for lane in lanes[which]], axis=1)
        row = decay_rate * old + share / widths[which] * row_sums
        rows_out[which][...] = row[0]
        for fold in range(len(lanes[which])):
            part = slice(fold * height, (fold + 1) * height)
            column = jnp.broadcast_to(row[:, part], (8, height)).T[:, :1]
            news[which][part, :] = masters[which][part, :] - rate * grads[which][part, :] * lax.rsqrt(column * across)
    vectors = vectors_ref[...]
    count = vectors.shape[0]
    gradient = jnp.concatenate(
        [sums[16 * (tile + 1) : 16 * (tile + 1) + count] for tile in range(vectors.shape[1] // 128)], axis=1
    )
    vector_grad_ref[...] = gradient
    moment = decay_rate * moment_ref[...] + share * (gradient * gradient + tiny_square)
    moment_new_ref[...] = moment
    spread = jnp.sqrt(jnp.mean(vectors * vectors, axis=1, keepdims=True))
    vector_new_ref[...] = vectors - step_rate * spread * gradient * lax.rsqrt(moment)


def packed_body(
    tokens, keep_mask, cotangent, qkv_weight, proj_weight, up_weight, down_weight, vectors,
    qkv_rows, qkv_cols, proj_rows, proj_cols, up_rows, up_cols, down_rows, down_cols, vector_moment,
):
    spread, dp_size = lax.axis_size("group"), lax.axis_size("dp")
    low, high = jnp.bfloat16, jnp.float32
    place = linear_place().astype(jnp.int32).reshape(1)
    group = lax.axis_index("group")
    held, slots, width = tokens.shape
    images, length = keep_mask.shape
    hidden = up_weight.shape[1] * spread
    total = images * length
    rows = qkv_weight.shape[0]
    folds = down_weight.shape[0] // rows
    core_bits = (1,)
    near_bits = tuple(1 << at for at in range(1, spread.bit_length()))
    far_bits = tuple(spread << at for at in range(1, dp_size.bit_length() - 1))
    half = spread * dp_size // 2

    anywhere = pl.BlockSpec(memory_space=pl.ANY)
    in_smem = pl.BlockSpec(memory_space=pltpu.SMEM)

    in_vmem = pl.BlockSpec(memory_space=pltpu.VMEM)
    small = functools.partial(
        pl.pallas_call, compiler_params=pltpu.CompilerParams(vmem_limit_bytes=vmem_bytes)
    )
    masters = (qkv_weight, proj_weight, up_weight, down_weight)
    parted = jax.ShapeDtypeStruct((spread, slots, images, width), low)

    def to_group(parts):
        return lax.all_to_all(parts, "group", split_axis=0, concat_axis=0, tiled=True)

    def to_images(parts):
        return to_group(parts).reshape(total, width)

    def exchange(parts):
        return [parts[0]] + [permute(part, relative) for relative, part in enumerate(parts) if relative]

    def settle(parts):
        parts = [part.reshape(slots, -1, width) for part in parts]
        whole = small(
            functools.partial(settle_kernel, spread),
            in_specs=[in_smem] + [in_vmem] * len(parts),
            out_specs=in_vmem,
            out_shape=jax.ShapeDtypeStruct((slots, held, width), low),
        )(place, *parts)
        return whole.transpose(1, 0, 2)

    first_cols = qkv_weight.shape[1] + proj_weight.shape[1]
    second_cols = up_weight.shape[1] + folds * down_weight.shape[1]
    pack_own = small(pack_kernel, out_shape=jax.ShapeDtypeStruct((rows, first_cols + second_cols), low))(*masters)
    across_y, across_x = near_bits
    pack_arrived = permute(pack_own, across_y)
    cotangent_cut = small(cut, out_shape=parted)(cotangent.transpose(1, 0, 2))
    token_cut, first_pair, second_pair = small(
        token_kernel,
        in_specs=[in_vmem] * 3 + [anywhere],
        out_shape=[
            parted,
            jax.ShapeDtypeStruct((2, rows, first_cols), low),
            jax.ShapeDtypeStruct((2, rows, second_cols), low),
        ],
    )(tokens.transpose(1, 0, 2), pack_own, pack_arrived, cotangent_cut)
    inputs = to_images(token_cut)

    def gather_far(pair):
        return [pair] + [permute(pair, mask) for mask in direct_masks(far_bits)]

    def join(parts, awaited=()):
        count = len(parts) * parts[0].shape[0]
        return small(
            functools.partial(join_kernel, len(parts)),
            in_specs=[in_vmem] * len(parts) + [anywhere] * len(awaited),
            out_shape=jax.ShapeDtypeStruct((count, *parts[0].shape[1:]), low),
        )(*parts, *awaited)

    def gather_rest(held):
        arrived = permute(held, across_x)
        return [held, arrived, permute(held, core_bits[0]), permute(arrived, core_bits[0])]

    first_far = join(gather_far(first_pair))
    upstream = to_images(cotangent_cut)
    first_blocks = gather_rest(first_far)
    second_far = gather_far(second_pair)

    step_rows = PER_STEP * length
    block = (step_rows, width)
    pairs = width // (2 * HEAD_DIM)
    steps = images // PER_STEP
    statics = (images, dp_size, spread)
    wide = scratch(width // 128, total, 128)
    probs_block = (PER_STEP, pairs, length, 2 * length)
    attention_outs = [
        ((total, 3 * width), low, (step_rows, 3 * width)),
        ((images, *probs_block[1:]), low, probs_block),
        ((total, width), low, block),
        ((total, width), high, block),
    ]
    attention_flops = (2 * total * width * 4 * width + 8 * total * length * width) // steps
    attention_scratches = [scratch(length, images), scratch(step_rows, width, dtype=low)]
    *attention, x, w_qkv, w_proj = call_kernel(
        first_attention_kernel, statics, 1,
        ["place"] + [None] * 7,
        attention_outs
        + [
            ((total, width), low, None),
            ((width, 3 * width), low, None),
            ((width, width), low, None),
        ],
        [scratch(dp_size * spread, rows, first_cols, dtype=low), wide] + attention_scratches,
        (place, inputs, *first_blocks, keep_mask, vectors),
        attention_flops,
    )
    second_blocks = gather_rest(join(second_far, attention[:1]))
    for first_step, count in ((1, steps - 2), (steps - 1, 1)):
        attention = call_kernel(
            next_attention_kernel, (first_step * PER_STEP,), count,
            [block] + [None] * 4 + ["await"] * len(attention),
            attention_outs, attention_scratches,
            (x, keep_mask, w_qkv, w_proj, vectors, *attention),
            attention_flops * count, first_step=first_step,
            aliases={5 + at: at for at in range(len(attention))},
        )
    qkv, probs, attended, middle = attention
    piece = ((slots * images, width), low, None)
    results = call_kernel(
        feed_forward_packed_kernel, statics, steps,
        ["place"] + [None] * 5 + [block, block] + [None] * 2,
        [piece] * spread
        + [
            ((total, width), high, block),
            ((total, width), low, block),
            ((half, rows, second_cols), low, None),
            ((half, rows, second_cols), low, None),
            ((width, width), high, None),
            ((8, width), high, None),
            ((1, hidden), high, None),
        ],
        [
            scratch(width, hidden, dtype=low),
            scratch(hidden, width, dtype=low),
            scratch(hidden, width, dtype=low),
            scratch(dp_size * spread, rows, second_cols, dtype=low),
            scratch(1, hidden),
            wide,
            scratch(step_rows, width, dtype=low),
            scratch(width, step_rows, dtype=low),
            scratch(step_rows, width, dtype=low),
            scratch(width, step_rows, dtype=low),
            scratch(step_rows, width),
            scratch(step_rows, 128),
            scratch(step_rows, width),
            scratch(step_rows, width),
            scratch(width, hidden),
            scratch(width, hidden),
        ],
        (
            place, upstream, *second_blocks, middle, attended, w_proj, vectors,
        ),
        12 * total * width * hidden + 4 * total * width * width, total * hidden,
    )
    d_middle, d_attended, ff_keep, ff_leave, proj_total, ff_sums, up_sums = results[spread:]

    def after(array, awaited):
        return small(
            after_kernel,
            in_specs=[anywhere] * (1 + len(awaited)),
            out_specs=anywhere,
            out_shape=jax.ShapeDtypeStruct(array.shape, array.dtype),
            input_output_aliases={0: 0},
        )(array, *awaited)

    def add_parts(count, keep, arrived, awaited):
        part = (keep.shape[0] // count, *keep.shape[1:])
        return small(
            functools.partial(add_kernel, count),
            in_specs=[in_vmem] * 2 + [anywhere] * len(awaited),
            out_specs=[in_vmem] * count,
            out_shape=[jax.ShapeDtypeStruct(part, high)]
            + [jax.ShapeDtypeStruct(part, low)] * (count - 1),
        )(keep, arrived, *awaited)

    ff_first = permute(ff_leave, core_bits[0])
    ff_count = half // 2
    ff_next = add_wide(ff_keep[ff_count:], ff_first[ff_count:]).astype(low)
    ff_arrived = permute(ff_next, across_x)
    output_parts = exchange(results[:spread])
    pack_half = ((half, rows, first_cols), low, None)
    wide_rows = (step_rows, 3 * width)
    d_projected, qkv_keep, qkv_leave, att_sums = call_kernel(
        attention_back_packed_kernel, (dp_size, spread), steps,
        ["place", block, wide_rows, probs_block, block, None, None, "await"],
        [((total, 3 * width), low, wide_rows), pack_half, pack_half, ((8, width), high, None)],
        [scratch(step_rows, width, dtype=low), scratch(width, 3 * width)],
        (place, x, qkv, probs, d_attended, vectors, proj_total, ff_next),
        2 * total * width * 3 * width + 16 * total * length * width,
    )
    qkv_arrived = permute(after(qkv_leave, output_parts[1:]), core_bits[0])
    input_flops = total * width * 3 * width
    d_input, att_sums = call_kernel(
        first_input_kernel, (length,), steps // 2,
        [block, wide_rows, block, None, None, None],
        [((total, width), low, block), ((8, width), high, None)],
        [scratch(step_rows, width)],
        (x, d_projected, d_middle, w_qkv, vectors, att_sums), input_flops,
    )
    results = call_kernel(
        last_input_kernel, (images, spread, length, images // 2), steps // 2,
        ["place", block, wide_rows, block, None, None, None, None],
        [piece] * spread + [((8, width), high, None)],
        [wide, scratch(step_rows, width)],
        (place, x, d_projected, d_middle, w_qkv, vectors, att_sums, d_input), input_flops,
        first_step=steps // 2,
    )
    att_sums = results[spread]
    input_parts = exchange(results[:spread])
    ff_quarter = half // 4
    ff_last = add_wide(
        ff_keep[ff_quarter:ff_count], ff_first[ff_quarter:ff_count], ff_arrived[ff_quarter:]
    ).astype(low)
    ff_last_arrived = permute(ff_last, across_y)
    qkv_held, *leaving = add_parts(4, qkv_keep, qkv_arrived, [ff_last])
    qkv_parts = [permute(part, mask) for part, mask in zip(leaving, direct_masks(near_bits))]
    ff_held = add_wide(
        ff_keep[:ff_quarter], ff_first[:ff_quarter], ff_arrived[:ff_quarter], ff_last_arrived
    )
    qkv_held = add_wide(qkv_held, *qkv_parts)
    blocks, block_parts = scatter_step(jnp.concatenate([ff_held, qkv_held], axis=2), far_bits)
    block_parts = [blocks] + block_parts

    heights = [master.shape[0] * dp_size for master in masters]
    widths = [master.shape[1] * spread for master in masters]
    rows_old, cols_old = [qkv_rows, proj_rows, up_rows, down_rows], [qkv_cols, proj_cols, up_cols, down_cols]

    def like(*arrays):
        return [jax.ShapeDtypeStruct(array.shape, high) for array in arrays]

    block_output = settle(output_parts)
    operands = (*block_parts, att_sums, ff_sums, up_sums, *masters, *rows_old)
    *grads, row_sums, message = small(
        functools.partial(gradient_kernel, len(block_parts)),
        in_specs=[in_vmem] * len(operands) + [anywhere],
        out_shape=like(*masters) + [jax.ShapeDtypeStruct((8, rows), high), jax.ShapeDtypeStruct((24, width), high)],
    )(*operands, block_output)
    message = added([message] + [permute(message, mask) for mask in direct_masks((across_x, far_bits[0]))])
    for bit in far_bits[1:-1]:
        message = message + permute(message, bit)
    messages = [message, permute(message, far_bits[-1])]
    col_sums, message = small(
        column_kernel,
        out_shape=[
            jax.ShapeDtypeStruct((8, width), high),
            jax.ShapeDtypeStruct((16 + width // 8, 128), high),
        ],
    )(row_sums, *messages)
    messages = [message] + [permute(message, mask) for mask in range(1, spread)]
    results = small(
        functools.partial(update_kernel, len(messages), heights, widths),
        out_shape=like(*masters, *cols_old, *rows_old, vectors, vectors, vectors),
    )(*messages, col_sums, vectors, vector_moment, *grads, *masters, *rows_old, *cols_old)
    news, cols_new, rows_out = results[:4], results[4:8], results[8:12]
    vector_grad, vector_moment_new, vector_new = results[12:]
    factored = []
    for which in range(4):
        factored += [grads[which], rows_out[which], cols_new[which], news[which]]
    return (block_output, settle(input_parts), *factored, vector_grad, vector_moment_new, vector_new)


def body(*arrays):
    spread, dp_size = lax.axis_size("group"), lax.axis_size("dp")
    rows, images = arrays[3].shape[0], arrays[1].shape[0]
    slots, width = arrays[0].shape[1:]
    folds = arrays[6].shape[0] // rows
    powers = all(size & (size - 1) == 0 for size in (spread, dp_size))
    fits = powers and spread == 4 and dp_size > 2
    fits = fits and arrays[5].shape[1] <= width and folds <= 5
    fits = fits and rows % 16 == 0 and images % PER_STEP == 0 and images > 2 * PER_STEP and images % 16 == 0 and slots % 4 == 0
    return packed_body(*arrays) if fits else general_body(*arrays)


def solution(mesh):
    in_specs = (
        P("dp", "group", None),
        P(("dp", "group"), None),
        P("dp", "group", None),
        P("dp", "group"),
        P("dp", "group"),
        P("dp", "group"),
        P("dp", "group"),
        P(),
        P("dp"),
        P("group"),
        P("dp"),
        P("group"),
        P("dp"),
        P("group"),
        P("dp"),
        P("group"),
        P(),
    )
    out_specs = (
        P("dp", "group", None),
        P("dp", "group", None),
        P("dp", "group"),
        P("dp"),
        P("group"),
        P("dp", "group"),
        P("dp", "group"),
        P("dp"),
        P("group"),
        P("dp", "group"),
        P("dp", "group"),
        P("dp"),
        P("group"),
        P("dp", "group"),
        P("dp", "group"),
        P("dp"),
        P("group"),
        P("dp", "group"),
        P(),
        P(),
        P(),
    )
    return jax.shard_map(body, mesh=mesh, in_specs=in_specs, out_specs=out_specs, check_vma=False)
```

```python
import functools
import math

import jax
import jax.numpy as jnp
from jax import lax
from jax.experimental import pallas as pl
from jax.experimental.pallas import tpu as pltpu
from jax.sharding import PartitionSpec as P

HEAD_DIM = 64
STEP_NUMBER = 10


step_rate = 0.3
norm_epsilon = 1e-06
tiny_square = 1e-30
decay_rate = 1.0 - STEP_NUMBER ** (-0.8)
LOG2_E = 1.4426950408889634


def axis_bits(name):
    count = lax.axis_size(name)
    return [(name, 1 << place) for place in range(count.bit_length() - 1)]


def swap_partner(array, step):
    name, bit = step
    count = lax.axis_size(name)
    return lax.ppermute(array, name, [(rank, rank ^ bit) for rank in range(count)])


def upper_side(step):
    name, bit = step
    return (lax.axis_index(name) & bit) != 0


def gather_blocks(array, steps):
    for step in steps:
        arrived = swap_partner(array, step)
        upper = upper_side(step)
        array = jnp.stack([jnp.where(upper, arrived, array), jnp.where(upper, array, arrived)])
    return array


def scatter_sum(array, steps):
    for step in steps:
        upper = upper_side(step)
        leaving = jnp.where(upper, array[0], array[1]).astype(jnp.bfloat16)
        arrived = swap_partner(leaving, step)
        array = jnp.where(upper, array[1], array[0]).astype(jnp.float32) + arrived.astype(jnp.float32)
    return array


def sum_everywhere(array, steps):
    for step in steps:
        array = array + swap_partner(array, step)
    return array


def sum_parts(parts, steps):
    flat = [part.reshape(-1) for part in parts]
    total = sum_everywhere(jnp.concatenate(flat), steps)
    result, start = [], 0
    for part in parts:
        result.append(total[start : start + part.size].reshape(part.shape))
        start += part.size
    return result


def block_order(steps):
    order = []
    for name in ("dp", "group"):
        bits = sorted((step for step in steps if step[0] == name), key=lambda step: -step[1])
        order.append([steps.index(step) for step in bits])
    return order


def blocks_to_whole(blocks, steps):
    count = len(steps)
    rows, cols = blocks.shape[count:]
    dp_axes, group_axes = block_order(steps)
    dp_axes = [count - 1 - axis for axis in dp_axes]
    group_axes = [count - 1 - axis for axis in group_axes]
    whole = blocks.transpose(dp_axes + [count] + group_axes + [count + 1])
    return whole.reshape(rows << len(dp_axes), cols << len(group_axes))


def whole_to_blocks(whole, steps):
    dp_axes, group_axes = block_order(steps)
    rows = whole.shape[0] >> len(dp_axes)
    cols = whole.shape[1] >> len(group_axes)
    split = whole.reshape([2] * len(dp_axes) + [rows] + [2] * len(group_axes) + [cols])
    places = dp_axes + [len(steps)] + group_axes + [len(steps) + 1]
    return split.transpose([places.index(axis) for axis in range(len(places))])


PER_STEP = 4
FF_CHUNK = 256
vmem_bytes = 60 * 1024 * 1024


def dot(left, right, left_axis=1, right_axis=0):
    return lax.dot_general(
        left, right, (((left_axis,), (right_axis,)), ((), ())), preferred_element_type=jnp.float32
    )


def normal_form(values):
    center = jnp.mean(values, axis=-1, keepdims=True)
    centered = values - center
    spread = jnp.mean(centered * centered, axis=-1, keepdims=True)
    scale = lax.rsqrt(spread + norm_epsilon)
    return centered * scale, scale


def norm_back(grad, unit, scale, gain):
    weighted = grad * gain
    along = jnp.mean(weighted * unit, axis=-1, keepdims=True)
    level = jnp.mean(weighted, axis=-1, keepdims=True)
    return scale * (weighted - level - unit * along)


def column_sum(values):
    return jnp.sum(values, axis=0, keepdims=True)


def pair_mask(length):
    return lax.broadcasted_iota(jnp.int32, (length, 2 * HEAD_DIM), 1) < HEAD_DIM


def stack_heads(pair, first):
    none = jnp.zeros_like(pair)
    return jnp.concatenate([jnp.where(first, pair, none), jnp.where(first, none, pair)], axis=0)


def join_heads(rows, first):
    length = rows.shape[0] // 2
    return jnp.where(first, rows[:length], rows[length:])


def gelu_and_slope(pre):
    bell = jnp.exp2(pre * pre * (-0.5 * LOG2_E))
    base = 1.0 + (0.3275911 * 0.5**0.5) * jnp.abs(pre)
    inverse = pl.reciprocal(base, approx=True)
    inverse = inverse * (2.0 - base * inverse)
    poly = inverse * (
        0.5 * 0.254829592
        + inverse
        * (
            0.5 * -0.284496736
            + inverse
            * (0.5 * 1.421413741 + inverse * (0.5 * -1.453152027 + inverse * (0.5 * 1.061405429)))
        )
    )
    tail = poly * bell
    below = jnp.where(pre >= 0, 1.0 - tail, tail)
    return pre * below, below + pre * bell * 0.3989422804014327


def widen(source_ref, wide_ref, images):
    tiles, total, lanes = wide_ref.shape
    rows_at_once = 8 * images

    @pl.loop(0, total // rows_at_once)
    def _(part):
        rows = pl.ds(pl.multiple_of(part * rows_at_once, rows_at_once), rows_at_once)
        for tile in range(tiles):
            cols = slice(tile * lanes, (tile + 1) * lanes)
            wide_ref[tile, rows, :] = source_ref[rows, cols].astype(jnp.float32)


def narrow(wide_ref, target_ref, images):
    tiles, total, lanes = wide_ref.shape
    rows_at_once = 8 * images

    @pl.loop(0, total // rows_at_once)
    def _(part):
        rows = pl.ds(pl.multiple_of(part * rows_at_once, rows_at_once), rows_at_once)
        for tile in range(tiles):
            cols = slice(tile * lanes, (tile + 1) * lanes)
            target_ref[rows, cols] = wide_ref[tile, rows, :].astype(target_ref.dtype)


def take_image(wide_ref, image, images):
    tiles, total, _ = wide_ref.shape
    rows = pl.ds(image, total // images, images)
    return jnp.concatenate([wide_ref[tile, rows, :] for tile in range(tiles)], axis=1)


def put_image(wide_ref, image, images, values):
    tiles, total, lanes = wide_ref.shape
    rows = pl.ds(image, total // images, images)
    for tile in range(tiles):
        wide_ref[tile, rows, :] = values[:, tile * lanes : (tile + 1) * lanes]


def attention_kernel(
    images, tokens_ref, bias_ref, w_qkv_ref, w_proj_ref, vectors_ref,
    x_ref, qkv_ref, probs_ref, attended_ref, middle_ref, wide_ref, normed_ref,
):
    @pl.when(pl.program_id(0) == 0)
    def _():
        widen(tokens_ref, wide_ref, images)
        to_image_rows(wide_ref, x_ref, images)

    attention_steps(
        x_ref, lambda image: bias_ref[image], w_qkv_ref, w_proj_ref, vectors_ref,
        qkv_ref, probs_ref, attended_ref, middle_ref, normed_ref,
    )


def to_image_rows(wide_ref, x_ref, images):
    length = wide_ref.shape[1] // images

    @pl.loop(0, images)
    def _(image):
        rows = pl.ds(pl.multiple_of(image * length, length), length)
        x_ref[rows, :] = take_image(wide_ref, image, images).astype(jnp.bfloat16)


def attention_steps(
    x_ref, bias_column, w_qkv_ref, w_proj_ref, vectors_ref,
    qkv_ref, probs_ref, attended_ref, middle_ref, normed_ref,
):
    per_step, _, length, _ = probs_ref.shape
    step_rows, width = middle_ref.shape
    base = 0 if x_ref.shape[0] == step_rows else pl.program_id(0) * step_rows

    for image in range(per_step):
        rows = slice(image * length, (image + 1) * length)
        x = x_ref[pl.ds(pl.multiple_of(base + image * length, length), length), :].astype(jnp.float32)
        unit, _ = normal_form(x)
        normed_ref[rows, :] = (unit * vectors_ref[0:1] + vectors_ref[1:2]).astype(jnp.bfloat16)
    for part in range(3):
        cols = slice(part * width, (part + 1) * width)
        projected = dot(normed_ref[...], w_qkv_ref[:, cols])
        if part != 1:
            row = 2 if part == 0 else 3
            projected = projected + vectors_ref[row : row + 1]
        qkv_ref[:, cols] = projected.astype(jnp.bfloat16)

    pairs = width // (2 * HEAD_DIM)
    first = pair_mask(length)
    place = lax.broadcasted_iota(jnp.int32, (length, 2 * length), 0)
    asker = lax.broadcasted_iota(jnp.int32, (length, 2 * length), 1)
    own = place == jnp.where(asker >= length, asker - length, asker)

    def scores_of(image):
        rows = slice(image * length, (image + 1) * length)
        result = []
        for pair in range(pairs):
            low = pair * 2 * HEAD_DIM
            queries = stack_heads(qkv_ref[rows, low : low + 2 * HEAD_DIM], first)
            result.append(dot(qkv_ref[rows, width + low : width + low + 2 * HEAD_DIM], queries, 1, 1))
        return result

    next_scores = scores_of(0)
    for image in range(per_step):
        rows = slice(image * length, (image + 1) * length)
        all_scores = next_scores
        if image + 1 < per_step:
            next_scores = scores_of(image + 1)
        bias = jnp.where(own, 0.0, bias_column(image))
        for pair in range(pairs):
            scores = all_scores[pair] * (HEAD_DIM**-0.5 * LOG2_E) + bias
            weights = jnp.exp2(scores - jnp.max(scores, axis=0, keepdims=True))
            probs = weights * (1.0 / jnp.sum(weights, axis=0, keepdims=True))
            probs_ref[image, pair] = probs.astype(jnp.bfloat16)
        for pair in range(pairs):
            low = pair * 2 * HEAD_DIM
            values = qkv_ref[rows, 2 * width + low : 2 * width + low + 2 * HEAD_DIM]
            attended = join_heads(dot(probs_ref[image, pair], values, 0, 0), first)
            attended_ref[rows, low : low + 2 * HEAD_DIM] = attended.astype(jnp.bfloat16)

    middle_ref[...] = (
        x_ref[pl.ds(pl.multiple_of(base, length), step_rows), :].astype(jnp.float32)
        + dot(attended_ref[...], w_proj_ref[...])
        + vectors_ref[4:5]
    )


def feed_forward_kernel(
    images, middle_ref, cotangent_ref, attended_ref, w_up_ref, w_down_ref, w_proj_ref, vectors_ref, bias_up_ref,
    output_ref, d_middle_ref, d_attended_ref, up_grad_ref, down_grad_ref, proj_grad_ref, vector_sums_ref, up_sums_ref,
    wide_ref, *scratches,
):
    up_total_ref, down_total_ref, proj_total_ref = scratches[-3:]

    @pl.when(pl.program_id(0) == 0)
    def _():
        widen(cotangent_ref, wide_ref, images)

    feed_forward_steps(
        images, middle_ref, attended_ref, w_up_ref, w_down_ref, w_proj_ref, vectors_ref, bias_up_ref,
        d_middle_ref, d_attended_ref, vector_sums_ref, up_sums_ref, wide_ref, *scratches,
    )

    @pl.when(pl.program_id(0) == pl.num_programs(0) - 1)
    def _():
        narrow(wide_ref, output_ref, images)
        up_grad_ref[...] = up_total_ref[...].astype(jnp.bfloat16)
        down_grad_ref[...] = down_total_ref[...].T.astype(jnp.bfloat16)
        proj_grad_ref[...] = proj_total_ref[...].astype(jnp.bfloat16)


def feed_forward_steps(
    images, middle_ref, attended_ref, w_up_ref, w_down_ref, w_proj_ref, vectors_ref, bias_up_ref,
    d_middle_ref, d_attended_ref, vector_sums_ref, up_sums_ref,
    wide_ref, normed_ref, normed_t_ref, dy_ref, dy_t_ref, unit_ref, scale_ref, ahead_ref, back_ref,
    up_t_ref, down_t_ref, up_total_ref, down_total_ref, proj_total_ref,
):
    step = pl.program_id(0)
    length = wide_ref.shape[1] // images
    hidden = w_up_ref.shape[1]
    per_step = middle_ref.shape[0] // length

    @pl.when(step == 0)
    def _():
        for total in (up_total_ref, down_total_ref, proj_total_ref, vector_sums_ref, up_sums_ref):
            total[...] = jnp.zeros_like(total)
        up_t_ref[...] = w_up_ref[...].T
        down_t_ref[...] = w_down_ref[...].T

    for image in range(per_step):
        rows = slice(image * length, (image + 1) * length)
        dy = take_image(wide_ref, step * per_step + image, images)
        dy_ref[rows, :] = dy.astype(jnp.bfloat16)
        vector_sums_ref[3:4] += column_sum(dy)
        unit, scale = normal_form(middle_ref[rows, :])
        unit_ref[rows, :] = unit
        scale_ref[rows, :] = jnp.broadcast_to(scale, (length, scale_ref.shape[1]))
        normed_ref[rows, :] = (unit * vectors_ref[5:6] + vectors_ref[6:7]).astype(jnp.bfloat16)
    normed_t_ref[...] = normed_ref[...].T
    dy_t_ref[...] = dy_ref[...].T
    chunks = hidden // FF_CHUNK

    def cols_of(chunk):
        return slice(chunk * FF_CHUNK, (chunk + 1) * FF_CHUNK)

    def into(chunk):
        cols = cols_of(chunk)
        pre = dot(normed_ref[...], w_up_ref[:, cols])
        return pre + bias_up_ref[:, cols], dot(dy_ref[...], down_t_ref[:, cols])

    def across(pre, d_active):
        active, slope = gelu_and_slope(pre)
        return active.astype(jnp.bfloat16), (d_active * slope).astype(jnp.bfloat16)

    def out_of(chunk, active, d_hidden):
        cols = cols_of(chunk)
        ahead, back = dot(active, w_down_ref[cols, :]), dot(d_hidden, up_t_ref[cols, :])
        if chunk == 0:
            ahead_ref[...] = ahead
            back_ref[...] = back
        else:
            ahead_ref[...] += ahead
            back_ref[...] += back
        down_total_ref[:, cols] += dot(dy_t_ref[...], active)
        up_total_ref[:, cols] += dot(normed_t_ref[...], d_hidden)
        up_sums_ref[:, cols] += column_sum(d_hidden.astype(jnp.float32))

    entered, crossed = into(0), None
    for chunk in range(chunks + 1):
        next_entered = into(chunk + 1) if chunk + 1 < chunks else None
        next_crossed = across(*entered) if chunk < chunks else None
        if crossed is not None:
            out_of(chunk - 1, *crossed)
        entered, crossed = next_entered, next_crossed

    for image in range(per_step):
        rows = slice(image * length, (image + 1) * length)
        output = middle_ref[rows, :] + ahead_ref[rows, :] + vectors_ref[11:12]
        put_image(wide_ref, step * per_step + image, images, output)
        unit = unit_ref[rows, :]
        grad = back_ref[rows, :]
        vector_sums_ref[1:2] += column_sum(grad * unit)
        vector_sums_ref[2:3] += column_sum(grad)
        d_middle = dy_ref[rows, :].astype(jnp.float32) + norm_back(
            grad, unit, scale_ref[rows, 0:1], vectors_ref[5:6]
        )
        d_middle_ref[rows, :] = d_middle
        d_branch = d_middle.astype(jnp.bfloat16)
        dy_ref[rows, :] = d_branch
        vector_sums_ref[0:1] += column_sum(d_branch.astype(jnp.float32))
    proj_total_ref[...] += dot(attended_ref[...], dy_ref[...], 0, 0)
    d_attended_ref[...] = dot(dy_ref[...], w_proj_ref[...], 1, 1).astype(jnp.bfloat16)


def attention_back_kernel(
    images, x_ref, qkv_ref, probs_ref, d_attended_ref, d_middle_ref, w_qkv_ref, vectors_ref,
    input_grad_ref, qkv_grad_ref, vector_sums_ref, wide_ref, normed_ref, d_projected_ref, back_ref, qkv_total_ref,
):
    @pl.when(pl.program_id(0) == 0)
    def _():
        qkv_total_ref[...] = jnp.zeros_like(qkv_total_ref)
        vector_sums_ref[...] = jnp.zeros_like(vector_sums_ref)

    def put(image, rows, values):
        put_image(wide_ref, image, images, values)

    attention_back_steps(
        x_ref, qkv_ref, probs_ref, d_attended_ref, vectors_ref, vector_sums_ref, normed_ref, d_projected_ref, qkv_total_ref
    )
    input_back_steps(
        put, probs_ref.shape[2], x_ref, d_projected_ref, d_middle_ref, w_qkv_ref, vectors_ref, vector_sums_ref, back_ref
    )

    @pl.when(pl.program_id(0) == pl.num_programs(0) - 1)
    def _():
        narrow(wide_ref, input_grad_ref, images)
        qkv_grad_ref[...] = qkv_total_ref[...].astype(jnp.bfloat16)


def attention_back_steps(
    x_ref, qkv_ref, probs_ref, d_attended_ref, vectors_ref, vector_sums_ref, normed_ref, d_projected_ref, qkv_total_ref
):
    width = x_ref.shape[1]
    length = probs_ref.shape[2]
    per_step = probs_ref.shape[0]

    pairs = width // (2 * HEAD_DIM)
    first = pair_mask(length)
    scale = HEAD_DIM**-0.5

    def places(image, pair):
        low = pair * 2 * HEAD_DIM
        rows = slice(image * length, (image + 1) * length)
        return rows, [slice(part * width + low, part * width + low + 2 * HEAD_DIM) for part in range(3)]

    def entering(image):
        result = []
        for pair in range(pairs):
            rows, cols = places(image, pair)
            d_attended = stack_heads(d_attended_ref[rows, cols[0]], first)
            d_values = dot(probs_ref[image, pair], d_attended)
            d_projected_ref[rows, cols[2]] = d_values.astype(jnp.bfloat16)
            result.append(dot(qkv_ref[rows, cols[2]], d_attended, 1, 1))
        return result

    next_probs = entering(0)
    for image in range(per_step):
        all_d_probs = next_probs
        if image + 1 < per_step:
            next_probs = entering(image + 1)
        all_d_scores = []
        for pair in range(pairs):
            probs, d_probs = probs_ref[image, pair].astype(jnp.float32), all_d_probs[pair]
            along = jnp.sum(d_probs * probs, axis=0, keepdims=True)
            all_d_scores.append((probs * (d_probs - along)).astype(jnp.bfloat16))
        for pair in range(pairs):
            rows, cols = places(image, pair)
            d_scores = all_d_scores[pair]
            queries = stack_heads(qkv_ref[rows, cols[0]], first)
            d_queries = join_heads(dot(d_scores, qkv_ref[rows, cols[1]], 0, 0), first) * scale
            d_projected_ref[rows, cols[0]] = d_queries.astype(jnp.bfloat16)
            d_projected_ref[rows, cols[1]] = (dot(d_scores, queries) * scale).astype(jnp.bfloat16)

    vector_sums_ref[2:3] += column_sum(d_projected_ref[:, :width].astype(jnp.float32))
    vector_sums_ref[3:4] += column_sum(d_projected_ref[:, 2 * width :].astype(jnp.float32))
    for image in range(per_step):
        rows = slice(image * length, (image + 1) * length)
        unit, _ = normal_form(x_ref[rows, :].astype(jnp.float32))
        normed_ref[rows, :] = (unit * vectors_ref[0:1] + vectors_ref[1:2]).astype(jnp.bfloat16)
    qkv_total_ref[...] += dot(normed_ref[...], d_projected_ref[...], 0, 0)


def input_back_steps(
    put, length, x_ref, d_projected_ref, d_middle_ref, w_qkv_ref, vectors_ref, vector_sums_ref, back_ref
):
    step = pl.program_id(0)
    per_step = x_ref.shape[0] // length
    back_ref[...] = dot(d_projected_ref[...], w_qkv_ref[...], 1, 1)
    for image in range(per_step):
        rows = slice(image * length, (image + 1) * length)
        unit, scale = normal_form(x_ref[rows, :].astype(jnp.float32))
        grad = back_ref[rows, :]
        vector_sums_ref[0:1] += column_sum(grad * unit)
        vector_sums_ref[1:2] += column_sum(grad)
        d_input = d_middle_ref[rows, :] + norm_back(grad, unit, scale, vectors_ref[0:1])
        put(step * per_step + image, rows, d_input)


def whole_block(shape):
    return pl.BlockSpec(shape, lambda step: (0,) * len(shape))


def step_block(shape, first=0):
    return pl.BlockSpec(shape, lambda step: (first + step,) + (0,) * (len(shape) - 1))


def scratch(*shape, dtype=jnp.float32):
    return pltpu.VMEM(shape, dtype)


def call_kernel(kernel, statics, steps, ins, outs, scratches, operands, flops, transcendentals=0, first_step=0, aliases={}):
    in_specs = [
        pl.BlockSpec(memory_space=pltpu.SMEM)
        if block == "place"
        else pl.BlockSpec(memory_space=pl.ANY)
        if block == "await"
        else whole_block(op.shape) if block is None else step_block(block, first_step)
        for op, block in zip(operands, ins)
    ]
    out_specs = [
        whole_block(shape) if block is None else step_block(block, first_step) for shape, dtype, block in outs
    ]
    moved = sum(op.size * op.dtype.itemsize for op in operands) + sum(
        math.prod(shape) * jnp.dtype(dtype).itemsize for shape, dtype, block in outs
    )
    return pl.pallas_call(
        functools.partial(kernel, *statics),
        grid=(steps,),
        in_specs=in_specs,
        out_specs=out_specs,
        out_shape=[jax.ShapeDtypeStruct(shape, dtype) for shape, dtype, block in outs],
        scratch_shapes=scratches,
        input_output_aliases=aliases,
        compiler_params=pltpu.CompilerParams(vmem_limit_bytes=vmem_bytes),
        cost_estimate=pl.CostEstimate(
            flops=flops * 8, bytes_accessed=moved, transcendentals=transcendentals
        ),
    )(*operands)


def attention_forward(tokens, bias, w_qkv, w_proj, vectors):
    images, length, _ = bias.shape
    total, width = tokens.shape
    pairs = width // (2 * HEAD_DIM)
    rows = PER_STEP * length
    low, high = jnp.bfloat16, jnp.float32
    outs = [
        ((total, width), low, None),
        ((total, 3 * width), low, (rows, 3 * width)),
        ((images, pairs, length, 2 * length), low, (PER_STEP, pairs, length, 2 * length)),
        ((total, width), low, (rows, width)),
        ((total, width), high, (rows, width)),
    ]
    return call_kernel(
        attention_kernel, (images,), images // PER_STEP,
        [None, (PER_STEP, length, 1), None, None, None], outs,
        [scratch(width // 128, total, 128), scratch(rows, width, dtype=low)],
        (tokens, bias, w_qkv, w_proj, vectors),
        2 * total * width * 4 * width + 8 * total * length * width,
    )


def feed_forward(images, middle, cotangent, attended, w_up, w_down, w_proj, vectors):
    total, width = middle.shape
    hidden = w_up.shape[1]
    rows = total // images * PER_STEP
    low, high = jnp.bfloat16, jnp.float32
    block = (rows, width)
    outs = [
        ((total, width), low, None),
        ((total, width), high, block),
        ((total, width), low, block),
        ((width, hidden), low, None),
        ((hidden, width), low, None),
        ((width, width), low, None),
        ((8, width), high, None),
        ((1, hidden), high, None),
    ]
    scratches = [
        scratch(width // 128, total, 128),
        scratch(rows, width, dtype=low),
        scratch(width, rows, dtype=low),
        scratch(rows, width, dtype=low),
        scratch(width, rows, dtype=low),
        scratch(rows, width),
        scratch(rows, 128),
        scratch(rows, width),
        scratch(rows, width),
        scratch(hidden, width, dtype=low),
        scratch(width, hidden, dtype=low),
        scratch(width, hidden),
        scratch(width, hidden),
        scratch(width, width),
    ]
    return call_kernel(
        feed_forward_kernel, (images,), images // PER_STEP,
        [block, None, block, None, None, None, None, None], outs, scratches,
        (middle, cotangent, attended, w_up, w_down, w_proj, vectors, vectors[7:11].reshape(1, hidden)),
        12 * total * width * hidden + 4 * total * width * width, total * hidden,
    )


def attention_back(x, qkv, probs, d_attended, d_middle, w_qkv, vectors):
    images, pairs, length, _ = probs.shape
    total, width = x.shape
    rows = PER_STEP * length
    low, high = jnp.bfloat16, jnp.float32
    block = (rows, width)
    outs = [
        ((total, width), low, None),
        ((width, 3 * width), low, None),
        ((8, width), high, None),
    ]
    scratches = [
        scratch(width // 128, total, 128),
        scratch(rows, width, dtype=low),
        scratch(rows, 3 * width, dtype=low),
        scratch(rows, width),
        scratch(width, 3 * width),
    ]
    return call_kernel(
        attention_back_kernel, (images,), images // PER_STEP,
        [block, (rows, 3 * width), (PER_STEP, pairs, length, 2 * length), block, block, None, None],
        outs, scratches, (x, qkv, probs, d_attended, d_middle, w_qkv, vectors),
        4 * total * width * 3 * width + 16 * total * length * width,
    )

def linear_place():
    return lax.axis_index("dp") * lax.axis_size("group") + lax.axis_index("group")


def permute(array, mask):
    count = lax.axis_size("dp") * lax.axis_size("group")
    return lax.ppermute(array, ("dp", "group"), [(rank, rank ^ mask) for rank in range(count)])


def direct_masks(bits):
    masks = [0]
    for bit in bits:
        masks = masks + [mask | bit for mask in masks]
    return masks[1:]


def scatter_step(held, bits):
    masks = direct_masks(bits)
    size = held.shape[0] // (len(masks) + 1)
    parts = [
        permute(held[size * (at + 1) : size * (at + 2)].astype(jnp.bfloat16), mask)
        for at, mask in enumerate(masks)
    ]
    return held[:size], parts


def add_wide(first, *rest):
    total = first.astype(jnp.float32)
    for part in rest:
        total = total + part.astype(jnp.float32)
    return total


def packed_place(mask, spread, count):
    return ((mask >> 1) & (spread - 1)) * (count // (2 * spread)) + (mask >> (spread.bit_length()))


def scatter_step(held, bits):
    masks = direct_masks(bits)
    size = held.shape[0] // (len(masks) + 1)
    parts = [
        permute(held[size * (at + 1) : size * (at + 2)].astype(jnp.bfloat16), mask)
        for at, mask in enumerate(masks)
    ]
    return held[:size], parts


def add_wide(first, *rest):
    total = first.astype(jnp.float32)
    for part in rest:
        total = total + part.astype(jnp.float32)
    return total


def packed_place(mask, spread, count):
    return ((mask >> 1) & (spread - 1)) * (count // (2 * spread)) + (mask >> (spread.bit_length()))


def gather_step(held, bits):
    return held + [permute(part, mask) for mask in direct_masks(bits) for part in held]


def gathered_place(mask, count):
    return (mask & 1) * (count // 2) + ((mask >> 2) & 1) * (count // 4) + (mask >> 3) * 2 + ((mask >> 1) & 1)


def unpack(place_ref, block_refs, packed_ref, put, dp_size, spread):
    place = place_ref[0]
    size = block_refs[0].shape[0]
    for at, block_ref in enumerate(block_refs):
        packed_ref[at * size : (at + 1) * size] = block_ref[...]
    count = dp_size * spread
    for row in range(dp_size):
        for col in range(spread):
            put(row, col, packed_ref[gathered_place((row * spread + col) ^ place, count)])


def pack(place_ref, take, keep_ref, leave_ref, dp_size, spread):
    place = place_ref[0]
    odd = (place & 1) == 1
    for row in range(dp_size):
        for col in range(0, spread, 2):
            at = packed_place((row * spread + col) ^ place, spread, dp_size * spread)
            even_block, odd_block = take(row, col), take(row, col + 1)
            keep_ref[at] = jnp.where(odd, odd_block, even_block)
            leave_ref[at] = jnp.where(odd, even_block, odd_block)


def narrow_pieces(place_ref, wide_ref, piece_refs, spread):
    tiles, _, lanes = wide_ref.shape
    rows_of_piece = piece_refs[0].shape[0]
    step = 64
    group = place_ref[0] & (spread - 1)
    for relative, piece_ref in enumerate(piece_refs):
        base = (group ^ relative) * rows_of_piece

        @pl.loop(0, rows_of_piece // step)
        def _(part):
            target = pl.ds(pl.multiple_of(part * step, step), step)
            source = pl.ds(pl.multiple_of(base + part * step, step), step)
            for tile in range(tiles):
                cols = slice(tile * lanes, (tile + 1) * lanes)
                piece_ref[target, cols] = wide_ref[tile, source, :].astype(jnp.bfloat16)


def general_body(
    tokens,
    keep_mask,
    cotangent,
    qkv_weight,
    proj_weight,
    up_weight,
    down_weight,
    vectors,
    qkv_rows,
    qkv_cols,
    proj_rows,
    proj_cols,
    up_rows,
    up_cols,
    down_rows,
    down_cols,
    vector_moment,
):
    masters = (qkv_weight, proj_weight, up_weight, down_weight)
    lowered = tuple((master.astype(jnp.bfloat16) for master in masters))
    dp_bits, group_bits = axis_bits("dp"), axis_bits("group")
    gather_steps = dp_bits[1:] + group_bits[1:] + dp_bits[:1] + group_bits[:1]
    scatter_steps = gather_steps[::-1]
    w_qkv, w_proj, w_up, w_down = tuple(
        blocks_to_whole(gather_blocks(part, gather_steps), gather_steps) for part in lowered
    )
    spread = lax.axis_size("group")

    def slots_in(array):
        held, slots, width = array.shape
        parts = array.transpose(1, 0, 2).reshape(slots, spread, held // spread, width)
        parts = lax.all_to_all(
            parts.transpose(1, 0, 2, 3), "group", split_axis=0, concat_axis=0, tiled=True
        )
        return parts.reshape(spread * slots * (held // spread), width)

    def slots_out(array):
        held, slots, width = tokens.shape
        parts = array.reshape(spread, slots, held // spread, width)
        parts = lax.all_to_all(parts, "group", split_axis=0, concat_axis=0, tiled=True)
        return parts.transpose(1, 0, 2, 3).reshape(slots, held, width).transpose(1, 0, 2)

    images = keep_mask.shape[0]
    bias = jnp.where(keep_mask > 0, 0.0, -1e30)[:, :, None]
    x, qkv, probs, attended, middle = attention_forward(
        slots_in(tokens), bias, w_qkv, w_proj, vectors
    )
    output, d_middle, d_attended, up_grad, down_grad, proj_grad, ff_sums, up_sums = feed_forward(
        images, middle, slots_in(cotangent), attended, w_up, w_down, w_proj, vectors
    )
    block_output = slots_out(output)
    d_input, qkv_grad, att_sums = attention_back(
        x, qkv, probs, d_attended, d_middle, w_qkv, vectors
    )
    input_grad = slots_out(d_input)
    local_vectors = jnp.concatenate(
        [att_sums[:4], ff_sums[:3], up_sums.reshape(4, -1), ff_sums[3:4]], axis=0
    )
    vector_grad = sum_everywhere(local_vectors, group_bits + dp_bits)
    local_grads = (qkv_grad, proj_grad, up_grad, down_grad)
    owned = tuple(
        scatter_sum(whole_to_blocks(part, scatter_steps), scatter_steps) for part in local_grads
    )
    squares = tuple((gradient * gradient + tiny_square for gradient in owned))
    row_parts = tuple((jnp.sum(square, axis=1) for square in squares)) + tuple(
        (jnp.sum(master * master, axis=1) for master in masters)
    )
    row_sums = sum_parts(row_parts, group_bits)
    rows_old = (qkv_rows, proj_rows, up_rows, down_rows)
    cols_old = (qkv_cols, proj_cols, up_cols, down_cols)
    total_cols = tuple((gradient.shape[1] * lax.axis_size("group") for gradient in owned))
    total_rows = tuple((gradient.shape[0] * lax.axis_size("dp") for gradient in owned))
    rows_new = tuple(
        (
            decay_rate * rows_old[which] + (1.0 - decay_rate) * row_sums[which] / total_cols[which]
            for which in range(4)
        )
    )
    col_parts = (
        tuple((jnp.sum(square, axis=0) for square in squares))
        + tuple((jnp.sum(row_stat) for row_stat in rows_new))
        + tuple((jnp.sum(row_sums[4 + which]) for which in range(4)))
    )
    col_sums = sum_parts(col_parts, dp_bits)
    results = []
    for which in range(4):
        cols_new = (
            decay_rate * cols_old[which] + (1.0 - decay_rate) * col_sums[which] / total_rows[which]
        )
        mean_rows = col_sums[4 + which] / total_rows[which]
        spread = jnp.sqrt(col_sums[8 + which] / (total_rows[which] * total_cols[which]))
        second = rows_new[which][:, None] * cols_new[None, :] / mean_rows
        updated = masters[which] - step_rate * spread * owned[which] * lax.rsqrt(second)
        results.append((owned[which], rows_new[which], cols_new, updated))
    vector_moment_new = decay_rate * vector_moment + (1.0 - decay_rate) * (
        vector_grad * vector_grad + tiny_square
    )
    row_spread = jnp.sqrt(jnp.mean(vectors * vectors, axis=1, keepdims=True))
    vector_new = vectors - step_rate * row_spread * vector_grad * lax.rsqrt(vector_moment_new)
    return (
        block_output,
        input_grad,
        results[0][0],
        results[0][1],
        results[0][2],
        results[0][3],
        results[1][0],
        results[1][1],
        results[1][2],
        results[1][3],
        results[2][0],
        results[2][1],
        results[2][2],
        results[2][3],
        results[3][0],
        results[3][1],
        results[3][2],
        results[3][3],
        vector_grad,
        vector_moment_new,
        vector_new,
    )


def first_attention_kernel(images, dp_size, spread, place_ref, tokens_ref, *refs):
    blocks, refs = refs[:4], refs[4:]
    keep_ref, vectors_ref, *outs, x_ref, w_qkv_ref, w_proj_ref = refs[:-4]
    packed_ref, wide_ref, bias_ref, normed_ref = refs[-4:]
    rows = packed_ref.shape[1]
    qkv_cols, proj_cols = w_qkv_ref.shape[1] // spread, w_proj_ref.shape[1] // spread

    @pl.when(pl.program_id(0) == 0)
    def _():
        widen(tokens_ref, wide_ref, images)
        to_image_rows(wide_ref, x_ref, images)

        def put(row, col, block):
            down = slice(row * rows, (row + 1) * rows)
            w_qkv_ref[down, col * qkv_cols : (col + 1) * qkv_cols] = block[:, :qkv_cols]
            w_proj_ref[down, col * proj_cols : (col + 1) * proj_cols] = block[:, qkv_cols:]

        unpack(place_ref, blocks, packed_ref, put, dp_size, spread)

    attention_part(0, x_ref, keep_ref, w_qkv_ref, w_proj_ref, vectors_ref, *outs, bias_ref, normed_ref)


def next_attention_kernel(start, x_ref, keep_ref, w_qkv_ref, w_proj_ref, vectors_ref, *refs):
    attention_part(start, x_ref, keep_ref, w_qkv_ref, w_proj_ref, vectors_ref, *refs[-6:])


def attention_part(
    start, x_ref, keep_ref, w_qkv_ref, w_proj_ref, vectors_ref,
    qkv_ref, probs_ref, attended_ref, middle_ref, bias_ref, normed_ref,
):
    @pl.when(pl.program_id(0) == 0)
    def _():
        bias_ref[...] = jnp.where(keep_ref[...] > 0, 0.0, -1e30).T

    def bias_column(image):
        here = start + pl.program_id(0) * probs_ref.shape[0] + image
        lane = lax.broadcasted_iota(jnp.int32, bias_ref.shape, 1)
        return row_sum(jnp.where(lane == here, bias_ref[...], 0.0))

    attention_steps(
        x_ref, bias_column, w_qkv_ref, w_proj_ref, vectors_ref,
        qkv_ref, probs_ref, attended_ref, middle_ref, normed_ref,
    )


def feed_forward_packed_kernel(images, dp_size, spread, place_ref, *refs):
    cotangent_ref, blocks, refs = refs[0], refs[1:5], refs[5:]
    middle_ref, attended_ref, w_proj_ref, vectors_ref = refs[:4]
    outputs, refs = refs[4 : 4 + spread], refs[4 + spread :]
    d_middle_ref, d_attended_ref, keep_ref, leave_ref, proj_total_ref, vector_sums_ref, up_sums_ref = refs[:7]
    w_up_ref, w_down_ref, down_low_ref, packed_ref, bias_up_ref, wide_ref = refs[7:13]
    scratches = refs[13:]
    width = w_up_ref.shape[0]
    up_total_ref, down_total_ref = scratches[-2:]
    rows = packed_ref.shape[1]
    up_cols = w_up_ref.shape[1] // spread
    out_cols = w_down_ref.shape[1] // spread
    folds = w_down_ref.shape[0] // w_up_ref.shape[0]

    @pl.when(pl.program_id(0) == 0)
    def _():
        widen(cotangent_ref, wide_ref, images)
        for fold in range(bias_up_ref.shape[1] // width):
            bias_up_ref[:, fold * width : (fold + 1) * width] = vectors_ref[7 + fold : 8 + fold]

        def put(row, col, block):
            w_up_ref[row * rows : (row + 1) * rows, col * up_cols : (col + 1) * up_cols] = block[:, :up_cols]
            for fold in range(folds):
                down = (row * folds + fold) * rows
                start = up_cols + fold * out_cols
                w_down_ref[down : down + rows, col * out_cols : (col + 1) * out_cols] = block[
                    :, start : start + out_cols
                ]

        unpack(place_ref, blocks, packed_ref, put, dp_size, spread)

    feed_forward_steps(
        images, middle_ref, attended_ref, w_up_ref, w_down_ref, w_proj_ref, vectors_ref, bias_up_ref,
        d_middle_ref, d_attended_ref, vector_sums_ref, up_sums_ref, wide_ref, *scratches, proj_total_ref,
    )

    @pl.when(pl.program_id(0) == pl.num_programs(0) - 1)
    def _():
        narrow_pieces(place_ref, wide_ref, outputs, spread)
        down_low_ref[...] = down_total_ref[...].T.astype(jnp.bfloat16)

        def take(row, col):
            across = slice(row * rows, (row + 1) * rows)
            cols = slice(col * out_cols, (col + 1) * out_cols)
            parts = [up_total_ref[across, col * up_cols : (col + 1) * up_cols].astype(jnp.bfloat16)]
            for fold in range(folds):
                down = (row * folds + fold) * rows
                parts.append(down_low_ref[down : down + rows, cols])
            return jnp.concatenate(parts, axis=1)

        pack(place_ref, take, keep_ref, leave_ref, dp_size, spread)


def attention_back_packed_kernel(
    dp_size, spread, place_ref, x_ref, qkv_ref, probs_ref, d_attended_ref, vectors_ref, proj_total_ref, _,
    d_projected_ref, keep_ref, leave_ref, vector_sums_ref, normed_ref, total_ref,
):
    @pl.when(pl.program_id(0) == 0)
    def _():
        total_ref[...] = jnp.zeros_like(total_ref)
        vector_sums_ref[...] = jnp.zeros_like(vector_sums_ref)

    attention_back_steps(
        x_ref, qkv_ref, probs_ref, d_attended_ref, vectors_ref, vector_sums_ref, normed_ref, d_projected_ref, total_ref
    )

    @pl.when(pl.program_id(0) == pl.num_programs(0) - 1)
    def _():
        rows = keep_ref.shape[1]
        qkv_cols, proj_cols = total_ref.shape[1] // spread, proj_total_ref.shape[1] // spread

        def take(row, col):
            down = slice(row * rows, (row + 1) * rows)
            parts = [
                total_ref[down, col * qkv_cols : (col + 1) * qkv_cols],
                proj_total_ref[down, col * proj_cols : (col + 1) * proj_cols],
            ]
            return jnp.concatenate(parts, axis=1).astype(jnp.bfloat16)

        pack(place_ref, take, keep_ref, leave_ref, dp_size, spread)


def first_input_kernel(
    length, x_ref, d_projected_ref, d_middle_ref, w_qkv_ref, vectors_ref, before_ref,
    d_input_ref, vector_sums_ref, back_ref,
):
    @pl.when(pl.program_id(0) == 0)
    def _():
        vector_sums_ref[...] = before_ref[...]

    def put(image, rows, values):
        d_input_ref[rows, :] = values.astype(jnp.bfloat16)

    input_back_steps(
        put, length, x_ref, d_projected_ref, d_middle_ref, w_qkv_ref, vectors_ref, vector_sums_ref, back_ref
    )


def last_input_kernel(
    images, spread, length, first, place_ref, x_ref, d_projected_ref, d_middle_ref, w_qkv_ref, vectors_ref, before_ref,
    d_input_ref, *refs,
):
    pieces, (vector_sums_ref, wide_ref, back_ref) = refs[:spread], refs[spread:]

    @pl.when(pl.program_id(0) == 0)
    def _():
        vector_sums_ref[...] = before_ref[...]
        for image in range(first):
            rows = slice(image * length, (image + 1) * length)
            put_image(wide_ref, image, images, d_input_ref[rows, :].astype(jnp.float32))

    def put(image, rows, values):
        put_image(wide_ref, first + image, images, values)

    input_back_steps(
        put, length, x_ref, d_projected_ref, d_middle_ref, w_qkv_ref, vectors_ref, vector_sums_ref, back_ref
    )

    @pl.when(pl.program_id(0) == pl.num_programs(0) - 1)
    def _():
        narrow_pieces(place_ref, wide_ref, pieces, spread)


def cut(array_ref, parts_ref):
    count = parts_ref.shape[2]
    for member in range(parts_ref.shape[0]):
        parts_ref[member] = array_ref[:, member * count : (member + 1) * count, :]


def pack_kernel(qkv_ref, proj_ref, up_ref, down_ref, pack_ref):
    rows, start = pack_ref.shape[0], 0
    parts = [qkv_ref[...], proj_ref[...], up_ref[...]]
    parts += [down_ref[fold * rows : (fold + 1) * rows, :] for fold in range(down_ref.shape[0] // rows)]
    for part in parts:
        pack_ref[:, start : start + part.shape[1]] = part.astype(jnp.bfloat16)
        start += part.shape[1]


def token_kernel(array_ref, own_ref, arrived_ref, _, parts_ref, first_ref, second_ref):
    start = first_ref.shape[2]
    for at, pack_ref in enumerate((own_ref, arrived_ref)):
        first_ref[at] = pack_ref[:, :start]
        second_ref[at] = pack_ref[:, start:]
    cut(array_ref, parts_ref)


def join_kernel(count, *refs):
    size = refs[0].shape[0]
    for at, part_ref in enumerate(refs[:count]):
        refs[-1][at * size : (at + 1) * size] = part_ref[...]


def settle_kernel(spread, place_ref, *refs):
    lists, (output_ref, token_ref) = refs[:-2], refs[-2:]
    token_ref[...] = jnp.zeros_like(token_ref)
    group = place_ref[0] & (spread - 1)
    count = lists[0].shape[1]
    share = len(lists) // spread * count
    for at, piece_ref in enumerate(lists):
        relative, part = at % spread, at // spread
        start = pl.multiple_of((group ^ relative) * share + part * count, count)
        output_ref[:, pl.ds(start, count), :] = piece_ref[...]


def lane_table(rows, columns):
    lane = lax.broadcasted_iota(jnp.int32, (rows, 128), 1)
    table = jnp.zeros((rows, 128), jnp.float32)
    for at, column in enumerate(columns):
        table = jnp.where(lane == at, column, table)
    return table


def added(parts):
    while len(parts) > 1:
        parts = [sum(parts[at : at + 2][1:], parts[at]) for at in range(0, len(parts), 2)]
    return parts[0]


def row_sum(values):
    return jnp.sum(values, axis=1, keepdims=True)


def after_kernel(*refs):
    pass


def add_kernel(count, keep_ref, arrived_ref, *refs):
    parts = refs[-count:]
    size = parts[0].shape[0]
    for at, part_ref in enumerate(parts):
        rows = slice(at * size, (at + 1) * size)
        total = keep_ref[rows].astype(jnp.float32) + arrived_ref[rows].astype(jnp.float32)
        part_ref[...] = total.astype(part_ref.dtype)


def gradient_kernel(count, *refs):
    block_parts, sums, refs = refs[:count], refs[count : count + 3], refs[count + 3 :]
    masters, rows_old, refs = refs[:4], refs[4:8], refs[9:]
    grads, (row_ref, message_ref) = refs[:4], refs[4:]
    blocks = added([part[0].astype(jnp.float32) for part in block_parts])
    rows, up_cols = grads[2].shape
    qkv_cols, out_cols = grads[0].shape[1], grads[1].shape[1]
    folds = grads[3].shape[0] // rows
    up = blocks[:, :up_cols]
    downs = [blocks[:, up_cols + fold * out_cols :][:, :out_cols] for fold in range(folds)]
    start = up_cols + folds * out_cols
    qkv = blocks[:, start : start + qkv_cols]
    proj = blocks[:, start + qkv_cols :]
    grads[0][...] = qkv
    grads[1][...] = proj
    grads[2][...] = up
    for fold in range(folds):
        grads[3][fold * rows : (fold + 1) * rows, :] = downs[fold]
    squares = [part * part + tiny_square for part in (qkv, proj, up, *downs)]
    row_ref[...] = lane_table(rows, [row_sum(square) for square in squares]).T[: row_ref.shape[0], :]
    width = message_ref.shape[1]
    message_ref[...] = jnp.zeros_like(message_ref)
    for at, square in enumerate((*squares[:3], added(squares[3:]))):
        message_ref[at : at + 1, : square.shape[1]] = column_sum(square)
    scalars = [column_sum(row_sum(master[...] * master[...])) for master in masters]
    scalars += [row_sum(part[...].reshape(1, part.shape[0])) for part in rows_old]
    message_ref[4:5, :128] = lane_table(1, scalars)
    att_ref, ff_ref, up_ref = sums
    count = up_ref.shape[1] // width
    message_ref[8:12, :] = att_ref[:4]
    message_ref[12:15, :] = ff_ref[:3]
    for at in range(count):
        message_ref[15 + at : 16 + at, :] = up_ref[:, at * width : (at + 1) * width]
    message_ref[15 + count : 16 + count, :] = ff_ref[3:4]


def column_kernel(row_ref, *refs):
    parts, (cols_ref, message_ref) = refs[:-2], refs[-2:]
    total = added([part[...] for part in parts])
    cols_ref[...] = total[:8]
    width = total.shape[1]
    rows = row_ref.shape[1]
    message_ref[...] = jnp.zeros_like(message_ref)
    message_ref[:8, :rows] = row_ref[...]
    columns = [row_sum(total[which : which + 1]) for which in range(4)]
    squares = [total[4:5, which : which + 1] for which in range(4)]
    message_ref[8:9, :] = lane_table(1, columns + squares)
    for tile in range(width // 128):
        message_ref[16 * (tile + 1) : 16 * (tile + 2), :] = total[8:, tile * 128 : (tile + 1) * 128]


def update_kernel(count, heights, widths, *refs):
    messages, refs = refs[:count], refs[count:]
    cols_ref, vectors_ref, moment_ref, refs = refs[0], refs[1], refs[2], refs[3:]
    grads, masters, rows_old, cols_old, refs = refs[:4], refs[4:8], refs[8:12], refs[12:16], refs[17:]
    news, cols_new, rows_out, refs = refs[:4], refs[4:8], refs[8:12], refs[12:]
    vector_grad_ref, moment_new_ref, vector_new_ref = refs
    sums = added([message[...] for message in messages])
    height = grads[0].shape[0]
    folds = grads[3].shape[0] // height
    lanes = [[0], [1], [2], list(range(3, 3 + folds))]
    share = 1.0 - decay_rate
    for which in range(4):
        entries = heights[which] * widths[which]
        cols = cols_old[which].shape[0]
        new = decay_rate * cols_old[which][...].reshape(1, cols) + share / heights[which] * cols_ref[
            which : which + 1, :cols
        ]
        cols_new[which][...] = new[0]
        old_total = cols_ref[4:5, 4 + which : 5 + which]
        mean_rows = (decay_rate * old_total + share / widths[which] * sums[8:9, which : which + 1]) / heights[which]
        rate = step_rate * jnp.sqrt(sums[8:9, 4 + which : 5 + which] / entries)
        across = new / mean_rows
        old = rows_old[which][...].reshape(1, len(lanes[which]) * height)
        row_sums = jnp.concatenate([sums[lane : lane + 1, :height] for lane in lanes[which]], axis=1)
        row = decay_rate * old + share / widths[which] * row_sums
        rows_out[which][...] = row[0]
        for fold in range(len(lanes[which])):
            part = slice(fold * height, (fold + 1) * height)
            column = jnp.broadcast_to(row[:, part], (8, height)).T[:, :1]
            news[which][part, :] = masters[which][part, :] - rate * grads[which][part, :] * lax.rsqrt(column * across)
    vectors = vectors_ref[...]
    count = vectors.shape[0]
    gradient = jnp.concatenate(
        [sums[16 * (tile + 1) : 16 * (tile + 1) + count] for tile in range(vectors.shape[1] // 128)], axis=1
    )
    vector_grad_ref[...] = gradient
    moment = decay_rate * moment_ref[...] + share * (gradient * gradient + tiny_square)
    moment_new_ref[...] = moment
    spread = jnp.sqrt(jnp.mean(vectors * vectors, axis=1, keepdims=True))
    vector_new_ref[...] = vectors - step_rate * spread * gradient * lax.rsqrt(moment)


def packed_body(
    tokens, keep_mask, cotangent, qkv_weight, proj_weight, up_weight, down_weight, vectors,
    qkv_rows, qkv_cols, proj_rows, proj_cols, up_rows, up_cols, down_rows, down_cols, vector_moment,
):
    spread, dp_size = lax.axis_size("group"), lax.axis_size("dp")
    low, high = jnp.bfloat16, jnp.float32
    place = linear_place().astype(jnp.int32).reshape(1)
    group = lax.axis_index("group")
    held, slots, width = tokens.shape
    images, length = keep_mask.shape
    hidden = up_weight.shape[1] * spread
    total = images * length
    rows = qkv_weight.shape[0]
    folds = down_weight.shape[0] // rows
    core_bits = (1,)
    near_bits = tuple(1 << at for at in range(1, spread.bit_length()))
    far_bits = tuple(spread << at for at in range(1, dp_size.bit_length() - 1))
    half = spread * dp_size // 2

    anywhere = pl.BlockSpec(memory_space=pl.ANY)
    in_smem = pl.BlockSpec(memory_space=pltpu.SMEM)

    in_vmem = pl.BlockSpec(memory_space=pltpu.VMEM)
    small = functools.partial(
        pl.pallas_call, compiler_params=pltpu.CompilerParams(vmem_limit_bytes=vmem_bytes)
    )
    masters = (qkv_weight, proj_weight, up_weight, down_weight)
    parted = jax.ShapeDtypeStruct((spread, slots, images, width), low)

    def to_group(parts):
        return lax.all_to_all(parts, "group", split_axis=0, concat_axis=0, tiled=True)

    def to_images(parts):
        return to_group(parts).reshape(total, width)

    def exchange(parts):
        return [parts[0]] + [permute(part, relative) for relative, part in enumerate(parts) if relative]

    def settle(parts):
        parts = [part.reshape(slots, -1, width) for part in parts]
        whole, token = small(
            functools.partial(settle_kernel, spread),
            in_specs=[in_smem] + [in_vmem] * len(parts),
            out_specs=[in_vmem] * 2,
            out_shape=[
                jax.ShapeDtypeStruct((slots, held, width), low),
                jax.ShapeDtypeStruct((8, 128), high),
            ],
        )(place, *parts)
        return whole.transpose(1, 0, 2), token

    first_cols = qkv_weight.shape[1] + proj_weight.shape[1]
    second_cols = up_weight.shape[1] + folds * down_weight.shape[1]
    pack_own = small(pack_kernel, out_shape=jax.ShapeDtypeStruct((rows, first_cols + second_cols), low))(*masters)
    across_y, across_x = near_bits
    pack_arrived = permute(pack_own, across_y)
    cotangent_cut = small(cut, out_shape=parted)(cotangent.transpose(1, 0, 2))
    token_cut, first_pair, second_pair = small(
        token_kernel,
        in_specs=[in_vmem] * 3 + [anywhere],
        out_shape=[
            parted,
            jax.ShapeDtypeStruct((2, rows, first_cols), low),
            jax.ShapeDtypeStruct((2, rows, second_cols), low),
        ],
    )(tokens.transpose(1, 0, 2), pack_own, pack_arrived, cotangent_cut)
    inputs = to_images(token_cut)

    def gather_far(pair):
        return [pair] + [permute(pair, mask) for mask in direct_masks(far_bits)]

    def join(parts, awaited=()):
        count = len(parts) * parts[0].shape[0]
        return small(
            functools.partial(join_kernel, len(parts)),
            in_specs=[in_vmem] * len(parts) + [anywhere] * len(awaited),
            out_shape=jax.ShapeDtypeStruct((count, *parts[0].shape[1:]), low),
        )(*parts, *awaited)

    def gather_rest(held):
        arrived = permute(held, across_x)
        return [held, arrived, permute(held, core_bits[0]), permute(arrived, core_bits[0])]

    first_far = join(gather_far(first_pair))
    upstream = to_images(cotangent_cut)
    first_blocks = gather_rest(first_far)
    second_far = gather_far(second_pair)

    step_rows = PER_STEP * length
    block = (step_rows, width)
    pairs = width // (2 * HEAD_DIM)
    steps = images // PER_STEP
    statics = (images, dp_size, spread)
    wide = scratch(width // 128, total, 128)
    probs_block = (PER_STEP, pairs, length, 2 * length)
    attention_outs = [
        ((total, 3 * width), low, (step_rows, 3 * width)),
        ((images, *probs_block[1:]), low, probs_block),
        ((total, width), low, block),
        ((total, width), high, block),
    ]
    attention_flops = (2 * total * width * 4 * width + 8 * total * length * width) // steps
    attention_scratches = [scratch(length, images), scratch(step_rows, width, dtype=low)]
    *attention, x, w_qkv, w_proj = call_kernel(
        first_attention_kernel, statics, 1,
        ["place"] + [None] * 7,
        attention_outs
        + [
            ((total, width), low, None),
            ((width, 3 * width), low, None),
            ((width, width), low, None),
        ],
        [scratch(dp_size * spread, rows, first_cols, dtype=low), wide] + attention_scratches,
        (place, inputs, *first_blocks, keep_mask, vectors),
        attention_flops,
    )
    second_blocks = gather_rest(join(second_far, attention[:1]))
    for first_step, count in ((1, steps - 2), (steps - 1, 1)):
        attention = call_kernel(
            next_attention_kernel, (first_step * PER_STEP,), count,
            [block] + [None] * 4 + ["await"] * len(attention),
            attention_outs, attention_scratches,
            (x, keep_mask, w_qkv, w_proj, vectors, *attention),
            attention_flops * count, first_step=first_step,
            aliases={5 + at: at for at in range(len(attention))},
        )
    qkv, probs, attended, middle = attention
    piece = ((slots * images, width), low, None)
    results = call_kernel(
        feed_forward_packed_kernel, statics, steps,
        ["place"] + [None] * 5 + [block, block] + [None] * 2,
        [piece] * spread
        + [
            ((total, width), high, block),
            ((total, width), low, block),
            ((half, rows, second_cols), low, None),
            ((half, rows, second_cols), low, None),
            ((width, width), high, None),
            ((8, width), high, None),
            ((1, hidden), high, None),
        ],
        [
            scratch(width, hidden, dtype=low),
            scratch(hidden, width, dtype=low),
            scratch(hidden, width, dtype=low),
            scratch(dp_size * spread, rows, second_cols, dtype=low),
            scratch(1, hidden),
            wide,
            scratch(step_rows, width, dtype=low),
            scratch(width, step_rows, dtype=low),
            scratch(step_rows, width, dtype=low),
            scratch(width, step_rows, dtype=low),
            scratch(step_rows, width),
            scratch(step_rows, 128),
            scratch(step_rows, width),
            scratch(step_rows, width),
            scratch(hidden, width, dtype=low),
            scratch(width, hidden, dtype=low),
            scratch(width, hidden),
            scratch(width, hidden),
        ],
        (
            place, upstream, *second_blocks, middle, attended, w_proj, vectors,
        ),
        12 * total * width * hidden + 4 * total * width * width, total * hidden,
    )
    d_middle, d_attended, ff_keep, ff_leave, proj_total, ff_sums, up_sums = results[spread:]

    def after(array, awaited):
        return small(
            after_kernel,
            in_specs=[anywhere] * (1 + len(awaited)),
            out_specs=anywhere,
            out_shape=jax.ShapeDtypeStruct(array.shape, array.dtype),
            input_output_aliases={0: 0},
        )(array, *awaited)

    def add_parts(count, keep, arrived, awaited):
        part = (keep.shape[0] // count, *keep.shape[1:])
        return small(
            functools.partial(add_kernel, count),
            in_specs=[in_vmem] * 2 + [anywhere] * len(awaited),
            out_specs=[in_vmem] * count,
            out_shape=[jax.ShapeDtypeStruct(part, high)]
            + [jax.ShapeDtypeStruct(part, low)] * (count - 1),
        )(keep, arrived, *awaited)

    ff_first = permute(ff_leave, core_bits[0])
    ff_count = half // 2
    ff_next = add_wide(ff_keep[ff_count:], ff_first[ff_count:]).astype(low)
    ff_arrived = permute(ff_next, across_x)
    output_parts = exchange(results[:spread])
    pack_half = ((half, rows, first_cols), low, None)
    wide_rows = (step_rows, 3 * width)
    d_projected, qkv_keep, qkv_leave, att_sums = call_kernel(
        attention_back_packed_kernel, (dp_size, spread), steps,
        ["place", block, wide_rows, probs_block, block, None, None, "await"],
        [((total, 3 * width), low, wide_rows), pack_half, pack_half, ((8, width), high, None)],
        [scratch(step_rows, width, dtype=low), scratch(width, 3 * width)],
        (place, x, qkv, probs, d_attended, vectors, proj_total, ff_next),
        2 * total * width * 3 * width + 16 * total * length * width,
    )
    qkv_arrived = permute(after(qkv_leave, output_parts[1:]), core_bits[0])
    output_parts[0] = after(output_parts[0], [att_sums])
    input_flops = total * width * 3 * width
    d_input, att_sums = call_kernel(
        first_input_kernel, (length,), steps // 2,
        [block, wide_rows, block, None, None, None],
        [((total, width), low, block), ((8, width), high, None)],
        [scratch(step_rows, width)],
        (x, d_projected, d_middle, w_qkv, vectors, att_sums), input_flops,
    )
    results = call_kernel(
        last_input_kernel, (images, spread, length, images // 2), steps // 2,
        ["place", block, wide_rows, block, None, None, None, None],
        [piece] * spread + [((8, width), high, None)],
        [wide, scratch(step_rows, width)],
        (place, x, d_projected, d_middle, w_qkv, vectors, att_sums, d_input), input_flops,
        first_step=steps // 2,
    )
    att_sums = results[spread]
    input_pieces = list(results[:spread])
    ff_quarter = half // 4
    ff_last = add_wide(
        ff_keep[ff_quarter:ff_count], ff_first[ff_quarter:ff_count], ff_arrived[ff_quarter:]
    ).astype(low)
    ff_last_arrived = permute(ff_last, across_y)
    qkv_held, *leaving = add_parts(4, qkv_keep, qkv_arrived, [ff_last])
    qkv_parts = [permute(part, mask) for part, mask in zip(leaving, direct_masks(near_bits))]
    ff_held = add_wide(
        ff_keep[:ff_quarter], ff_first[:ff_quarter], ff_arrived[:ff_quarter], ff_last_arrived
    )
    qkv_held = add_wide(qkv_held, *qkv_parts)
    blocks, block_parts = scatter_step(jnp.concatenate([ff_held, qkv_held], axis=2), far_bits)
    block_parts = [blocks] + block_parts

    heights = [master.shape[0] * dp_size for master in masters]
    widths = [master.shape[1] * spread for master in masters]
    rows_old, cols_old = [qkv_rows, proj_rows, up_rows, down_rows], [qkv_cols, proj_cols, up_cols, down_cols]

    def like(*arrays):
        return [jax.ShapeDtypeStruct(array.shape, high) for array in arrays]

    block_output, settled = settle(output_parts)
    operands = (*block_parts, att_sums, ff_sums, up_sums, *masters, *rows_old)
    *grads, row_sums, message = small(
        functools.partial(gradient_kernel, len(block_parts)),
        in_specs=[in_vmem] * len(operands) + [anywhere],
        out_shape=like(*masters) + [jax.ShapeDtypeStruct((8, rows), high), jax.ShapeDtypeStruct((24, width), high)],
    )(*operands, settled)
    input_pieces[1] = after(input_pieces[1], [row_sums])
    input_grad, input_settled = settle(exchange(input_pieces))
    message = added([message] + [permute(message, mask) for mask in direct_masks((across_x, far_bits[0]))])
    for bit in far_bits[1:-1]:
        message = message + permute(message, bit)
    messages = [message, permute(message, far_bits[-1])]
    col_sums, message = small(
        column_kernel,
        out_shape=[
            jax.ShapeDtypeStruct((8, width), high),
            jax.ShapeDtypeStruct((16 + width // 8, 128), high),
        ],
    )(row_sums, *messages)
    messages = [message] + [permute(message, mask) for mask in range(1, spread)]
    operands = (*messages, col_sums, vectors, vector_moment, *grads, *masters, *rows_old, *cols_old)
    results = small(
        functools.partial(update_kernel, len(messages), heights, widths),
        in_specs=[in_vmem] * len(operands) + [anywhere],
        out_shape=like(*masters, *cols_old, *rows_old, vectors, vectors, vectors),
    )(*operands, input_settled)
    news, cols_new, rows_out = results[:4], results[4:8], results[8:12]
    vector_grad, vector_moment_new, vector_new = results[12:]
    factored = []
    for which in range(4):
        factored += [grads[which], rows_out[which], cols_new[which], news[which]]
    return (block_output, input_grad, *factored, vector_grad, vector_moment_new, vector_new)


def body(*arrays):
    spread, dp_size = lax.axis_size("group"), lax.axis_size("dp")
    rows, images = arrays[3].shape[0], arrays[1].shape[0]
    slots, width = arrays[0].shape[1:]
    folds = arrays[6].shape[0] // rows
    powers = all(size & (size - 1) == 0 for size in (spread, dp_size))
    fits = powers and spread == 4 and dp_size > 2
    fits = fits and arrays[5].shape[1] <= width and folds <= 5
    fits = fits and rows % 16 == 0 and images % PER_STEP == 0 and images > 2 * PER_STEP and images % 16 == 0 and slots % 4 == 0
    return packed_body(*arrays) if fits else general_body(*arrays)


def solution(mesh):
    in_specs = (
        P("dp", "group", None),
        P(("dp", "group"), None),
        P("dp", "group", None),
        P("dp", "group"),
        P("dp", "group"),
        P("dp", "group"),
        P("dp", "group"),
        P(),
        P("dp"),
        P("group"),
        P("dp"),
        P("group"),
        P("dp"),
        P("group"),
        P("dp"),
        P("group"),
        P(),
    )
    out_specs = (
        P("dp", "group", None),
        P("dp", "group", None),
        P("dp", "group"),
        P("dp"),
        P("group"),
        P("dp", "group"),
        P("dp", "group"),
        P("dp"),
        P("group"),
        P("dp", "group"),
        P("dp", "group"),
        P("dp"),
        P("group"),
        P("dp", "group"),
        P("dp", "group"),
        P("dp"),
        P("group"),
        P("dp", "group"),
        P(),
        P(),
        P(),
    )
    return jax.shard_map(body, mesh=mesh, in_specs=in_specs, out_specs=out_specs, check_vma=False)
```

```python
import functools
import math

import jax
import jax.numpy as jnp
from jax import lax
from jax.experimental import pallas as pl
from jax.experimental.pallas import tpu as pltpu
from jax.sharding import PartitionSpec as P

HEAD_DIM = 64
STEP_NUMBER = 10


step_rate = 0.3
norm_epsilon = 1e-06
tiny_square = 1e-30
decay_rate = 1.0 - STEP_NUMBER ** (-0.8)
LOG2_E = 1.4426950408889634


def axis_bits(name):
    count = lax.axis_size(name)
    return [(name, 1 << place) for place in range(count.bit_length() - 1)]


def swap_partner(array, step):
    name, bit = step
    count = lax.axis_size(name)
    return lax.ppermute(array, name, [(rank, rank ^ bit) for rank in range(count)])


def upper_side(step):
    name, bit = step
    return (lax.axis_index(name) & bit) != 0


def gather_blocks(array, steps):
    for step in steps:
        arrived = swap_partner(array, step)
        upper = upper_side(step)
        array = jnp.stack([jnp.where(upper, arrived, array), jnp.where(upper, array, arrived)])
    return array


def scatter_sum(array, steps):
    for step in steps:
        upper = upper_side(step)
        leaving = jnp.where(upper, array[0], array[1]).astype(jnp.bfloat16)
        arrived = swap_partner(leaving, step)
        array = jnp.where(upper, array[1], array[0]).astype(jnp.float32) + arrived.astype(jnp.float32)
    return array


def sum_everywhere(array, steps):
    for step in steps:
        array = array + swap_partner(array, step)
    return array


def sum_parts(parts, steps):
    flat = [part.reshape(-1) for part in parts]
    total = sum_everywhere(jnp.concatenate(flat), steps)
    result, start = [], 0
    for part in parts:
        result.append(total[start : start + part.size].reshape(part.shape))
        start += part.size
    return result


def block_order(steps):
    order = []
    for name in ("dp", "group"):
        bits = sorted((step for step in steps if step[0] == name), key=lambda step: -step[1])
        order.append([steps.index(step) for step in bits])
    return order


def blocks_to_whole(blocks, steps):
    count = len(steps)
    rows, cols = blocks.shape[count:]
    dp_axes, group_axes = block_order(steps)
    dp_axes = [count - 1 - axis for axis in dp_axes]
    group_axes = [count - 1 - axis for axis in group_axes]
    whole = blocks.transpose(dp_axes + [count] + group_axes + [count + 1])
    return whole.reshape(rows << len(dp_axes), cols << len(group_axes))


def whole_to_blocks(whole, steps):
    dp_axes, group_axes = block_order(steps)
    rows = whole.shape[0] >> len(dp_axes)
    cols = whole.shape[1] >> len(group_axes)
    split = whole.reshape([2] * len(dp_axes) + [rows] + [2] * len(group_axes) + [cols])
    places = dp_axes + [len(steps)] + group_axes + [len(steps) + 1]
    return split.transpose([places.index(axis) for axis in range(len(places))])


PER_STEP = 4
FF_PER_STEP = 8
FF_CHUNK = 256
vmem_bytes = 60 * 1024 * 1024


def dot(left, right, left_axis=1, right_axis=0):
    return lax.dot_general(
        left, right, (((left_axis,), (right_axis,)), ((), ())), preferred_element_type=jnp.float32
    )


def normal_form(values):
    center = jnp.mean(values, axis=-1, keepdims=True)
    centered = values - center
    spread = jnp.mean(centered * centered, axis=-1, keepdims=True)
    scale = lax.rsqrt(spread + norm_epsilon)
    return centered * scale, scale


def norm_back(grad, unit, scale, gain):
    weighted = grad * gain
    along = jnp.mean(weighted * unit, axis=-1, keepdims=True)
    level = jnp.mean(weighted, axis=-1, keepdims=True)
    return scale * (weighted - level - unit * along)


def column_sum(values):
    return jnp.sum(values, axis=0, keepdims=True)


def pair_mask(length):
    return lax.broadcasted_iota(jnp.int32, (length, 2 * HEAD_DIM), 1) < HEAD_DIM


def stack_heads(pair, first):
    none = jnp.zeros_like(pair)
    return jnp.concatenate([jnp.where(first, pair, none), jnp.where(first, none, pair)], axis=0)


def join_heads(rows, first):
    length = rows.shape[0] // 2
    return jnp.where(first, rows[:length], rows[length:])


def gelu_and_slope(pre):
    bell = jnp.exp2(pre * pre * (-0.5 * LOG2_E))
    base = 1.0 + (0.3275911 * 0.5**0.5) * jnp.abs(pre)
    inverse = pl.reciprocal(base, approx=True)
    inverse = inverse * (2.0 - base * inverse)
    poly = inverse * (
        0.5 * 0.254829592
        + inverse
        * (
            0.5 * -0.284496736
            + inverse
            * (0.5 * 1.421413741 + inverse * (0.5 * -1.453152027 + inverse * (0.5 * 1.061405429)))
        )
    )
    tail = poly * bell
    below = jnp.where(pre >= 0, 1.0 - tail, tail)
    return pre * below, below + pre * bell * 0.3989422804014327


def widen(source_ref, wide_ref, images):
    tiles, total, lanes = wide_ref.shape
    rows_at_once = 8 * images

    @pl.loop(0, total // rows_at_once)
    def _(part):
        rows = pl.ds(pl.multiple_of(part * rows_at_once, rows_at_once), rows_at_once)
        for tile in range(tiles):
            cols = slice(tile * lanes, (tile + 1) * lanes)
            wide_ref[tile, rows, :] = source_ref[rows, cols].astype(jnp.float32)


def narrow(wide_ref, target_ref, images):
    tiles, total, lanes = wide_ref.shape
    rows_at_once = 8 * images

    @pl.loop(0, total // rows_at_once)
    def _(part):
        rows = pl.ds(pl.multiple_of(part * rows_at_once, rows_at_once), rows_at_once)
        for tile in range(tiles):
            cols = slice(tile * lanes, (tile + 1) * lanes)
            target_ref[rows, cols] = wide_ref[tile, rows, :].astype(target_ref.dtype)


def take_image(wide_ref, image, images):
    tiles, total, _ = wide_ref.shape
    rows = pl.ds(image, total // images, images)
    return jnp.concatenate([wide_ref[tile, rows, :] for tile in range(tiles)], axis=1)


def put_image(wide_ref, image, images, values):
    tiles, total, lanes = wide_ref.shape
    rows = pl.ds(image, total // images, images)
    for tile in range(tiles):
        wide_ref[tile, rows, :] = values[:, tile * lanes : (tile + 1) * lanes]


def attention_kernel(
    images, tokens_ref, bias_ref, w_qkv_ref, w_proj_ref, vectors_ref,
    x_ref, qkv_ref, probs_ref, attended_ref, middle_ref, wide_ref, normed_ref,
):
    @pl.when(pl.program_id(0) == 0)
    def _():
        widen(tokens_ref, wide_ref, images)
        to_image_rows(wide_ref, x_ref, images)

    attention_steps(
        x_ref, lambda image: bias_ref[image], w_qkv_ref, w_proj_ref, vectors_ref,
        qkv_ref, probs_ref, attended_ref, middle_ref, normed_ref,
    )


def to_image_rows(wide_ref, x_ref, images):
    length = wide_ref.shape[1] // images

    @pl.loop(0, images)
    def _(image):
        rows = pl.ds(pl.multiple_of(image * length, length), length)
        x_ref[rows, :] = take_image(wide_ref, image, images).astype(jnp.bfloat16)


def attention_steps(
    x_ref, bias_column, w_qkv_ref, w_proj_ref, vectors_ref,
    qkv_ref, probs_ref, attended_ref, middle_ref, normed_ref,
):
    per_step, _, length, _ = probs_ref.shape
    step_rows, width = middle_ref.shape
    base = 0 if x_ref.shape[0] == step_rows else pl.program_id(0) * step_rows

    for image in range(per_step):
        rows = slice(image * length, (image + 1) * length)
        x = x_ref[pl.ds(pl.multiple_of(base + image * length, length), length), :].astype(jnp.float32)
        unit, _ = normal_form(x)
        normed_ref[rows, :] = (unit * vectors_ref[0:1] + vectors_ref[1:2]).astype(jnp.bfloat16)
    for part in range(3):
        cols = slice(part * width, (part + 1) * width)
        projected = dot(normed_ref[...], w_qkv_ref[:, cols])
        if part != 1:
            row = 2 if part == 0 else 3
            projected = projected + vectors_ref[row : row + 1]
        qkv_ref[:, cols] = projected.astype(jnp.bfloat16)

    pairs = width // (2 * HEAD_DIM)
    first = pair_mask(length)
    place = lax.broadcasted_iota(jnp.int32, (length, 2 * length), 0)
    asker = lax.broadcasted_iota(jnp.int32, (length, 2 * length), 1)
    own = place == jnp.where(asker >= length, asker - length, asker)

    def scores_of(image):
        rows = slice(image * length, (image + 1) * length)
        result = []
        for pair in range(pairs):
            low = pair * 2 * HEAD_DIM
            queries = stack_heads(qkv_ref[rows, low : low + 2 * HEAD_DIM], first)
            result.append(dot(qkv_ref[rows, width + low : width + low + 2 * HEAD_DIM], queries, 1, 1))
        return result

    next_scores = scores_of(0)
    for image in range(per_step):
        rows = slice(image * length, (image + 1) * length)
        all_scores = next_scores
        if image + 1 < per_step:
            next_scores = scores_of(image + 1)
        bias = jnp.where(own, 0.0, bias_column(image))
        for pair in range(pairs):
            scores = all_scores[pair] * (HEAD_DIM**-0.5 * LOG2_E) + bias
            weights = jnp.exp2(scores - jnp.max(scores, axis=0, keepdims=True))
            probs = weights * (1.0 / jnp.sum(weights, axis=0, keepdims=True))
            probs_ref[image, pair] = probs.astype(jnp.bfloat16)
        for pair in range(pairs):
            low = pair * 2 * HEAD_DIM
            values = qkv_ref[rows, 2 * width + low : 2 * width + low + 2 * HEAD_DIM]
            attended = join_heads(dot(probs_ref[image, pair], values, 0, 0), first)
            attended_ref[rows, low : low + 2 * HEAD_DIM] = attended.astype(jnp.bfloat16)

    middle_ref[...] = (
        x_ref[pl.ds(pl.multiple_of(base, length), step_rows), :].astype(jnp.float32)
        + dot(attended_ref[...], w_proj_ref[...])
        + vectors_ref[4:5]
    )


def feed_forward_kernel(
    images, middle_ref, cotangent_ref, attended_ref, w_up_ref, w_down_ref, proj_t_ref, vectors_ref, bias_up_ref,
    output_ref, d_middle_ref, d_attended_ref, up_grad_ref, down_grad_ref, proj_grad_ref, vector_sums_ref, up_sums_ref,
    wide_ref, *scratches,
):
    up_total_ref, down_total_ref, proj_total_ref = scratches[-3:]

    @pl.when(pl.program_id(0) == 0)
    def _():
        widen(cotangent_ref, wide_ref, images)

    feed_forward_steps(
        images, middle_ref, attended_ref, w_up_ref, w_down_ref, proj_t_ref, vectors_ref, bias_up_ref,
        d_middle_ref, d_attended_ref, vector_sums_ref, up_sums_ref, wide_ref, *scratches,
    )

    @pl.when(pl.program_id(0) == pl.num_programs(0) - 1)
    def _():
        narrow(wide_ref, output_ref, images)
        up_grad_ref[...] = up_total_ref[...].astype(jnp.bfloat16)
        down_grad_ref[...] = down_total_ref[...].T.astype(jnp.bfloat16)
        proj_grad_ref[...] = proj_total_ref[...].astype(jnp.bfloat16)


def feed_forward_steps(
    images, middle_ref, attended_ref, w_up_ref, w_down_ref, proj_t_ref, vectors_ref, bias_up_ref,
    d_middle_ref, d_attended_ref, vector_sums_ref, up_sums_ref,
    wide_ref, normed_ref, normed_t_ref, dy_ref, dy_t_ref, unit_ref, scale_ref, ahead_ref, back_ref,
    up_t_ref, down_t_ref, up_total_ref, down_total_ref, proj_total_ref,
):
    step = pl.program_id(0)
    length = wide_ref.shape[1] // images
    hidden = w_up_ref.shape[1]
    per_step = middle_ref.shape[0] // length

    @pl.when(step == 0)
    def _():
        for total in (up_total_ref, down_total_ref, proj_total_ref, vector_sums_ref, up_sums_ref):
            total[...] = jnp.zeros_like(total)
        up_t_ref[...] = w_up_ref[...].T
        down_t_ref[...] = w_down_ref[...].T

    for image in range(per_step):
        rows = slice(image * length, (image + 1) * length)
        dy = take_image(wide_ref, step * per_step + image, images)
        dy_ref[rows, :] = dy.astype(jnp.bfloat16)
        vector_sums_ref[3:4] += column_sum(dy)
        unit, scale = normal_form(middle_ref[rows, :])
        unit_ref[rows, :] = unit
        scale_ref[rows, :] = jnp.broadcast_to(scale, (length, scale_ref.shape[1]))
        normed_ref[rows, :] = (unit * vectors_ref[5:6] + vectors_ref[6:7]).astype(jnp.bfloat16)
    normed_t_ref[...] = normed_ref[...].T
    dy_t_ref[...] = dy_ref[...].T
    chunks = hidden // FF_CHUNK

    def cols_of(chunk):
        return slice(chunk * FF_CHUNK, (chunk + 1) * FF_CHUNK)

    def into(chunk):
        cols = cols_of(chunk)
        pre = dot(normed_ref[...], w_up_ref[:, cols])
        return pre + bias_up_ref[:, cols], dot(dy_ref[...], down_t_ref[:, cols])

    def across(pre, d_active):
        active, slope = gelu_and_slope(pre)
        return active.astype(jnp.bfloat16), (d_active * slope).astype(jnp.bfloat16)

    def out_of(chunk, active, d_hidden):
        cols = cols_of(chunk)
        ahead, back = dot(active, w_down_ref[cols, :]), dot(d_hidden, up_t_ref[cols, :])
        if chunk == 0:
            ahead_ref[...] = ahead
            back_ref[...] = back
        else:
            ahead_ref[...] += ahead
            back_ref[...] += back
        down_total_ref[:, cols] += dot(dy_t_ref[...], active)
        up_total_ref[:, cols] += dot(normed_t_ref[...], d_hidden)
        up_sums_ref[:, cols] += column_sum(d_hidden.astype(jnp.float32))

    entered, crossed = into(0), None
    for chunk in range(chunks + 1):
        next_entered = into(chunk + 1) if chunk + 1 < chunks else None
        next_crossed = across(*entered) if chunk < chunks else None
        if crossed is not None:
            out_of(chunk - 1, *crossed)
        entered, crossed = next_entered, next_crossed

    for image in range(per_step):
        rows = slice(image * length, (image + 1) * length)
        output = middle_ref[rows, :] + ahead_ref[rows, :] + vectors_ref[11:12]
        put_image(wide_ref, step * per_step + image, images, output)
        unit = unit_ref[rows, :]
        grad = back_ref[rows, :]
        vector_sums_ref[1:2] += column_sum(grad * unit)
        vector_sums_ref[2:3] += column_sum(grad)
        d_middle = dy_ref[rows, :].astype(jnp.float32) + norm_back(
            grad, unit, scale_ref[rows, 0:1], vectors_ref[5:6]
        )
        d_middle_ref[rows, :] = d_middle
        d_branch = d_middle.astype(jnp.bfloat16)
        dy_ref[rows, :] = d_branch
        vector_sums_ref[0:1] += column_sum(d_branch.astype(jnp.float32))
    proj_total_ref[...] += dot(attended_ref[...], dy_ref[...], 0, 0)
    d_attended_ref[...] = dot(dy_ref[...], proj_t_ref[...]).astype(jnp.bfloat16)


def attention_back_kernel(
    images, x_ref, qkv_ref, probs_ref, d_attended_ref, d_middle_ref, qkv_t_ref, vectors_ref,
    input_grad_ref, qkv_grad_ref, vector_sums_ref, wide_ref, normed_ref, d_projected_ref, back_ref, qkv_total_ref,
):
    @pl.when(pl.program_id(0) == 0)
    def _():
        qkv_total_ref[...] = jnp.zeros_like(qkv_total_ref)
        vector_sums_ref[...] = jnp.zeros_like(vector_sums_ref)

    def put(image, rows, values):
        put_image(wide_ref, image, images, values)

    attention_back_steps(
        x_ref, qkv_ref, probs_ref, d_attended_ref, vectors_ref, vector_sums_ref, normed_ref, d_projected_ref, qkv_total_ref
    )
    input_back_steps(
        put, probs_ref.shape[2], x_ref, d_projected_ref, d_middle_ref, qkv_t_ref, vectors_ref, vector_sums_ref, back_ref
    )

    @pl.when(pl.program_id(0) == pl.num_programs(0) - 1)
    def _():
        narrow(wide_ref, input_grad_ref, images)
        qkv_grad_ref[...] = qkv_total_ref[...].astype(jnp.bfloat16)


def attention_back_steps(
    x_ref, qkv_ref, probs_ref, d_attended_ref, vectors_ref, vector_sums_ref, normed_ref, d_projected_ref, qkv_total_ref
):
    width = x_ref.shape[1]
    length = probs_ref.shape[2]
    per_step = probs_ref.shape[0]

    pairs = width // (2 * HEAD_DIM)
    first = pair_mask(length)
    scale = HEAD_DIM**-0.5

    def places(image, pair):
        low = pair * 2 * HEAD_DIM
        rows = slice(image * length, (image + 1) * length)
        return rows, [slice(part * width + low, part * width + low + 2 * HEAD_DIM) for part in range(3)]

    def entering(image):
        result = []
        for pair in range(pairs):
            rows, cols = places(image, pair)
            d_attended = stack_heads(d_attended_ref[rows, cols[0]], first)
            d_values = dot(probs_ref[image, pair], d_attended)
            d_projected_ref[rows, cols[2]] = d_values.astype(jnp.bfloat16)
            result.append(dot(qkv_ref[rows, cols[2]], d_attended, 1, 1))
        return result

    next_probs = entering(0)
    for image in range(per_step):
        all_d_probs = next_probs
        if image + 1 < per_step:
            next_probs = entering(image + 1)
        all_d_scores = []
        for pair in range(pairs):
            probs, d_probs = probs_ref[image, pair].astype(jnp.float32), all_d_probs[pair]
            along = jnp.sum(d_probs * probs, axis=0, keepdims=True)
            all_d_scores.append((probs * (d_probs - along)).astype(jnp.bfloat16))
        for pair in range(pairs):
            rows, cols = places(image, pair)
            d_scores = all_d_scores[pair]
            queries = stack_heads(qkv_ref[rows, cols[0]], first)
            d_queries = join_heads(dot(d_scores, qkv_ref[rows, cols[1]], 0, 0), first) * scale
            d_projected_ref[rows, cols[0]] = d_queries.astype(jnp.bfloat16)
            d_projected_ref[rows, cols[1]] = (dot(d_scores, queries) * scale).astype(jnp.bfloat16)

    vector_sums_ref[2:3] += column_sum(d_projected_ref[:, :width].astype(jnp.float32))
    vector_sums_ref[3:4] += column_sum(d_projected_ref[:, 2 * width :].astype(jnp.float32))
    for image in range(per_step):
        rows = slice(image * length, (image + 1) * length)
        unit, _ = normal_form(x_ref[rows, :].astype(jnp.float32))
        normed_ref[rows, :] = (unit * vectors_ref[0:1] + vectors_ref[1:2]).astype(jnp.bfloat16)
    qkv_total_ref[...] += dot(normed_ref[...], d_projected_ref[...], 0, 0)


def input_back_steps(
    put, length, x_ref, d_projected_ref, d_middle_ref, qkv_t_ref, vectors_ref, vector_sums_ref, back_ref
):
    step = pl.program_id(0)
    per_step = x_ref.shape[0] // length
    back_ref[...] = dot(d_projected_ref[...], qkv_t_ref[...])
    for image in range(per_step):
        rows = slice(image * length, (image + 1) * length)
        unit, scale = normal_form(x_ref[rows, :].astype(jnp.float32))
        grad = back_ref[rows, :]
        vector_sums_ref[0:1] += column_sum(grad * unit)
        vector_sums_ref[1:2] += column_sum(grad)
        d_input = d_middle_ref[rows, :] + norm_back(grad, unit, scale, vectors_ref[0:1])
        put(step * per_step + image, rows, d_input)


def whole_block(shape):
    return pl.BlockSpec(shape, lambda step: (0,) * len(shape))


def step_block(shape, first=0):
    return pl.BlockSpec(shape, lambda step: (first + step,) + (0,) * (len(shape) - 1))


def scratch(*shape, dtype=jnp.float32):
    return pltpu.VMEM(shape, dtype)


def call_kernel(kernel, statics, steps, ins, outs, scratches, operands, flops, transcendentals=0, first_step=0, aliases={}):
    in_specs = [
        pl.BlockSpec(memory_space=pltpu.SMEM)
        if block == "place"
        else pl.BlockSpec(memory_space=pl.ANY)
        if block == "await"
        else whole_block(op.shape) if block is None else step_block(block, first_step)
        for op, block in zip(operands, ins)
    ]
    out_specs = [
        whole_block(shape) if block is None else step_block(block, first_step) for shape, dtype, block in outs
    ]
    moved = sum(op.size * op.dtype.itemsize for op in operands) + sum(
        math.prod(shape) * jnp.dtype(dtype).itemsize for shape, dtype, block in outs
    )
    return pl.pallas_call(
        functools.partial(kernel, *statics),
        grid=(steps,),
        in_specs=in_specs,
        out_specs=out_specs,
        out_shape=[jax.ShapeDtypeStruct(shape, dtype) for shape, dtype, block in outs],
        scratch_shapes=scratches,
        input_output_aliases=aliases,
        compiler_params=pltpu.CompilerParams(vmem_limit_bytes=vmem_bytes),
        cost_estimate=pl.CostEstimate(
            flops=flops * 8, bytes_accessed=moved, transcendentals=transcendentals
        ),
    )(*operands)


def attention_forward(tokens, bias, w_qkv, w_proj, vectors):
    images, length, _ = bias.shape
    total, width = tokens.shape
    pairs = width // (2 * HEAD_DIM)
    rows = PER_STEP * length
    low, high = jnp.bfloat16, jnp.float32
    outs = [
        ((total, width), low, None),
        ((total, 3 * width), low, (rows, 3 * width)),
        ((images, pairs, length, 2 * length), low, (PER_STEP, pairs, length, 2 * length)),
        ((total, width), low, (rows, width)),
        ((total, width), high, (rows, width)),
    ]
    return call_kernel(
        attention_kernel, (images,), images // PER_STEP,
        [None, (PER_STEP, length, 1), None, None, None], outs,
        [scratch(width // 128, total, 128), scratch(rows, width, dtype=low)],
        (tokens, bias, w_qkv, w_proj, vectors),
        2 * total * width * 4 * width + 8 * total * length * width,
    )


def feed_forward(images, middle, cotangent, attended, w_up, w_down, w_proj, vectors):
    total, width = middle.shape
    hidden = w_up.shape[1]
    rows = total // images * FF_PER_STEP
    low, high = jnp.bfloat16, jnp.float32
    block = (rows, width)
    outs = [
        ((total, width), low, None),
        ((total, width), high, block),
        ((total, width), low, block),
        ((width, hidden), low, None),
        ((hidden, width), low, None),
        ((width, width), low, None),
        ((8, width), high, None),
        ((1, hidden), high, None),
    ]
    scratches = [
        scratch(width // 128, total, 128),
        scratch(rows, width, dtype=low),
        scratch(width, rows, dtype=low),
        scratch(rows, width, dtype=low),
        scratch(width, rows, dtype=low),
        scratch(rows, width),
        scratch(rows, 128),
        scratch(rows, width),
        scratch(rows, width),
        scratch(hidden, width, dtype=low),
        scratch(width, hidden, dtype=low),
        scratch(width, hidden),
        scratch(width, hidden),
        scratch(width, width),
    ]
    return call_kernel(
        feed_forward_kernel, (images,), images // FF_PER_STEP,
        [block, None, block, None, None, None, None, None], outs, scratches,
        (middle, cotangent, attended, w_up, w_down, w_proj.T, vectors, vectors[7:11].reshape(1, hidden)),
        12 * total * width * hidden + 4 * total * width * width, total * hidden,
    )


def attention_back(x, qkv, probs, d_attended, d_middle, w_qkv, vectors):
    images, pairs, length, _ = probs.shape
    total, width = x.shape
    rows = PER_STEP * length
    low, high = jnp.bfloat16, jnp.float32
    block = (rows, width)
    outs = [
        ((total, width), low, None),
        ((width, 3 * width), low, None),
        ((8, width), high, None),
    ]
    scratches = [
        scratch(width // 128, total, 128),
        scratch(rows, width, dtype=low),
        scratch(rows, 3 * width, dtype=low),
        scratch(rows, width),
        scratch(width, 3 * width),
    ]
    return call_kernel(
        attention_back_kernel, (images,), images // PER_STEP,
        [block, (rows, 3 * width), (PER_STEP, pairs, length, 2 * length), block, block, None, None],
        outs, scratches, (x, qkv, probs, d_attended, d_middle, w_qkv.T, vectors),
        4 * total * width * 3 * width + 16 * total * length * width,
    )

def linear_place():
    return lax.axis_index("dp") * lax.axis_size("group") + lax.axis_index("group")


def permute(array, mask):
    count = lax.axis_size("dp") * lax.axis_size("group")
    return lax.ppermute(array, ("dp", "group"), [(rank, rank ^ mask) for rank in range(count)])


def direct_masks(bits):
    masks = [0]
    for bit in bits:
        masks = masks + [mask | bit for mask in masks]
    return masks[1:]


def add_wide(first, *rest):
    total = first.astype(jnp.float32)
    for part in rest:
        total = total + part.astype(jnp.float32)
    return total


def packed_place(mask, spread, count):
    return ((mask >> 1) & (spread - 1)) * (count // (2 * spread)) + (mask >> (spread.bit_length()))


def scatter_step(held, bits):
    masks = direct_masks(bits)
    size = held.shape[0] // (len(masks) + 1)
    parts = [
        permute(held[size * (at + 1) : size * (at + 2)].astype(jnp.bfloat16), mask)
        for at, mask in enumerate(masks)
    ]
    return held[:size], parts


def add_wide(first, *rest):
    total = first.astype(jnp.float32)
    for part in rest:
        total = total + part.astype(jnp.float32)
    return total


def packed_place(mask, spread, count):
    return ((mask >> 1) & (spread - 1)) * (count // (2 * spread)) + (mask >> (spread.bit_length()))


def gather_step(held, bits):
    return held + [permute(part, mask) for mask in direct_masks(bits) for part in held]


def gathered_place(mask, count):
    return (mask & 1) * (count // 2) + ((mask >> 2) & 1) * (count // 4) + (mask >> 3) * 2 + ((mask >> 1) & 1)


def unpack(place_ref, block_refs, packed_ref, put, dp_size, spread):
    place = place_ref[0]
    size = block_refs[0].shape[0]
    for at, block_ref in enumerate(block_refs):
        packed_ref[at * size : (at + 1) * size] = block_ref[...]
    count = dp_size * spread
    for row in range(dp_size):
        for col in range(spread):
            put(row, col, packed_ref[gathered_place((row * spread + col) ^ place, count)])


def pack(place_ref, take, keep_ref, leave_ref, dp_size, spread):
    place = place_ref[0]
    odd = (place & 1) == 1
    for row in range(dp_size):
        for col in range(0, spread, 2):
            at = packed_place((row * spread + col) ^ place, spread, dp_size * spread)
            even_block, odd_block = take(row, col), take(row, col + 1)
            keep_ref[at] = jnp.where(odd, odd_block, even_block)
            leave_ref[at] = jnp.where(odd, even_block, odd_block)


def narrow_pieces(place_ref, wide_ref, piece_refs, spread):
    tiles, _, lanes = wide_ref.shape
    rows_of_piece = piece_refs[0].shape[0]
    step = 64
    group = place_ref[0] & (spread - 1)
    for relative, piece_ref in enumerate(piece_refs):
        base = (group ^ relative) * rows_of_piece

        @pl.loop(0, rows_of_piece // step)
        def _(part):
            target = pl.ds(pl.multiple_of(part * step, step), step)
            source = pl.ds(pl.multiple_of(base + part * step, step), step)
            for tile in range(tiles):
                cols = slice(tile * lanes, (tile + 1) * lanes)
                piece_ref[target, cols] = wide_ref[tile, source, :].astype(jnp.bfloat16)


def general_body(
    tokens,
    keep_mask,
    cotangent,
    qkv_weight,
    proj_weight,
    up_weight,
    down_weight,
    vectors,
    qkv_rows,
    qkv_cols,
    proj_rows,
    proj_cols,
    up_rows,
    up_cols,
    down_rows,
    down_cols,
    vector_moment,
):
    masters = (qkv_weight, proj_weight, up_weight, down_weight)
    lowered = tuple((master.astype(jnp.bfloat16) for master in masters))
    dp_bits, group_bits = axis_bits("dp"), axis_bits("group")
    gather_steps = dp_bits[1:] + group_bits[1:] + dp_bits[:1] + group_bits[:1]
    scatter_steps = gather_steps[::-1]
    w_qkv, w_proj, w_up, w_down = tuple(
        blocks_to_whole(gather_blocks(part, gather_steps), gather_steps) for part in lowered
    )
    spread = lax.axis_size("group")

    def slots_in(array):
        held, slots, width = array.shape
        parts = array.transpose(1, 0, 2).reshape(slots, spread, held // spread, width)
        parts = lax.all_to_all(
            parts.transpose(1, 0, 2, 3), "group", split_axis=0, concat_axis=0, tiled=True
        )
        return parts.reshape(spread * slots * (held // spread), width)

    def slots_out(array):
        held, slots, width = tokens.shape
        parts = array.reshape(spread, slots, held // spread, width)
        parts = lax.all_to_all(parts, "group", split_axis=0, concat_axis=0, tiled=True)
        return parts.transpose(1, 0, 2, 3).reshape(slots, held, width).transpose(1, 0, 2)

    images = keep_mask.shape[0]
    bias = jnp.where(keep_mask > 0, 0.0, -1e30)[:, :, None]
    x, qkv, probs, attended, middle = attention_forward(
        slots_in(tokens), bias, w_qkv, w_proj, vectors
    )
    output, d_middle, d_attended, up_grad, down_grad, proj_grad, ff_sums, up_sums = feed_forward(
        images, middle, slots_in(cotangent), attended, w_up, w_down, w_proj, vectors
    )
    block_output = slots_out(output)
    d_input, qkv_grad, att_sums = attention_back(
        x, qkv, probs, d_attended, d_middle, w_qkv, vectors
    )
    input_grad = slots_out(d_input)
    local_vectors = jnp.concatenate(
        [att_sums[:4], ff_sums[:3], up_sums.reshape(4, -1), ff_sums[3:4]], axis=0
    )
    vector_grad = sum_everywhere(local_vectors, group_bits + dp_bits)
    local_grads = (qkv_grad, proj_grad, up_grad, down_grad)
    owned = tuple(
        scatter_sum(whole_to_blocks(part, scatter_steps), scatter_steps) for part in local_grads
    )
    squares = tuple((gradient * gradient + tiny_square for gradient in owned))
    row_parts = tuple((jnp.sum(square, axis=1) for square in squares)) + tuple(
        (jnp.sum(master * master, axis=1) for master in masters)
    )
    row_sums = sum_parts(row_parts, group_bits)
    rows_old = (qkv_rows, proj_rows, up_rows, down_rows)
    cols_old = (qkv_cols, proj_cols, up_cols, down_cols)
    total_cols = tuple((gradient.shape[1] * lax.axis_size("group") for gradient in owned))
    total_rows = tuple((gradient.shape[0] * lax.axis_size("dp") for gradient in owned))
    rows_new = tuple(
        (
            decay_rate * rows_old[which] + (1.0 - decay_rate) * row_sums[which] / total_cols[which]
            for which in range(4)
        )
    )
    col_parts = (
        tuple((jnp.sum(square, axis=0) for square in squares))
        + tuple((jnp.sum(row_stat) for row_stat in rows_new))
        + tuple((jnp.sum(row_sums[4 + which]) for which in range(4)))
    )
    col_sums = sum_parts(col_parts, dp_bits)
    results = []
    for which in range(4):
        cols_new = (
            decay_rate * cols_old[which] + (1.0 - decay_rate) * col_sums[which] / total_rows[which]
        )
        mean_rows = col_sums[4 + which] / total_rows[which]
        spread = jnp.sqrt(col_sums[8 + which] / (total_rows[which] * total_cols[which]))
        second = rows_new[which][:, None] * cols_new[None, :] / mean_rows
        updated = masters[which] - step_rate * spread * owned[which] * lax.rsqrt(second)
        results.append((owned[which], rows_new[which], cols_new, updated))
    vector_moment_new = decay_rate * vector_moment + (1.0 - decay_rate) * (
        vector_grad * vector_grad + tiny_square
    )
    row_spread = jnp.sqrt(jnp.mean(vectors * vectors, axis=1, keepdims=True))
    vector_new = vectors - step_rate * row_spread * vector_grad * lax.rsqrt(vector_moment_new)
    return (
        block_output,
        input_grad,
        results[0][0],
        results[0][1],
        results[0][2],
        results[0][3],
        results[1][0],
        results[1][1],
        results[1][2],
        results[1][3],
        results[2][0],
        results[2][1],
        results[2][2],
        results[2][3],
        results[3][0],
        results[3][1],
        results[3][2],
        results[3][3],
        vector_grad,
        vector_moment_new,
        vector_new,
    )


def first_attention_kernel(images, dp_size, spread, place_ref, tokens_ref, *refs):
    blocks, refs = refs[:4], refs[4:]
    keep_ref, vectors_ref, *outs, x_ref, w_qkv_ref, w_proj_ref, qkv_t_ref, proj_t_ref = refs[:-4]
    packed_ref, wide_ref, bias_ref, normed_ref = refs[-4:]
    rows = packed_ref.shape[1]
    qkv_cols, proj_cols = w_qkv_ref.shape[1] // spread, w_proj_ref.shape[1] // spread

    @pl.when(pl.program_id(0) == 0)
    def _():
        widen(tokens_ref, wide_ref, images)
        to_image_rows(wide_ref, x_ref, images)

        def put(row, col, block):
            down = slice(row * rows, (row + 1) * rows)
            w_qkv_ref[down, col * qkv_cols : (col + 1) * qkv_cols] = block[:, :qkv_cols]
            w_proj_ref[down, col * proj_cols : (col + 1) * proj_cols] = block[:, qkv_cols:]

        unpack(place_ref, blocks, packed_ref, put, dp_size, spread)
        qkv_t_ref[...] = w_qkv_ref[...].T
        proj_t_ref[...] = w_proj_ref[...].T

    attention_part(0, x_ref, keep_ref, w_qkv_ref, w_proj_ref, vectors_ref, *outs, bias_ref, normed_ref)


def next_attention_kernel(start, x_ref, keep_ref, w_qkv_ref, w_proj_ref, vectors_ref, *refs):
    attention_part(start, x_ref, keep_ref, w_qkv_ref, w_proj_ref, vectors_ref, *refs[-6:])


def attention_part(
    start, x_ref, keep_ref, w_qkv_ref, w_proj_ref, vectors_ref,
    qkv_ref, probs_ref, attended_ref, middle_ref, bias_ref, normed_ref,
):
    @pl.when(pl.program_id(0) == 0)
    def _():
        bias_ref[...] = jnp.where(keep_ref[...] > 0, 0.0, -1e30).T

    def bias_column(image):
        here = start + pl.program_id(0) * probs_ref.shape[0] + image
        lane = lax.broadcasted_iota(jnp.int32, bias_ref.shape, 1)
        return row_sum(jnp.where(lane == here, bias_ref[...], 0.0))

    attention_steps(
        x_ref, bias_column, w_qkv_ref, w_proj_ref, vectors_ref,
        qkv_ref, probs_ref, attended_ref, middle_ref, normed_ref,
    )


def feed_forward_packed_kernel(images, dp_size, spread, place_ref, *refs):
    cotangent_ref, blocks, refs = refs[0], refs[1:5], refs[5:]
    middle_ref, attended_ref, proj_t_ref, vectors_ref = refs[:4]
    outputs, refs = refs[4 : 4 + spread], refs[4 + spread :]
    d_middle_ref, d_attended_ref, keep_ref, leave_ref, proj_total_ref, vector_sums_ref, up_sums_ref = refs[:7]
    w_up_ref, w_down_ref, down_low_ref, packed_ref, bias_up_ref, wide_ref = refs[7:13]
    scratches = refs[13:]
    width = w_up_ref.shape[0]
    up_total_ref, down_total_ref = scratches[-2:]
    rows = packed_ref.shape[1]
    up_cols = w_up_ref.shape[1] // spread
    out_cols = w_down_ref.shape[1] // spread
    folds = w_down_ref.shape[0] // w_up_ref.shape[0]

    @pl.when(pl.program_id(0) == 0)
    def _():
        widen(cotangent_ref, wide_ref, images)
        for fold in range(bias_up_ref.shape[1] // width):
            bias_up_ref[:, fold * width : (fold + 1) * width] = vectors_ref[7 + fold : 8 + fold]

        def put(row, col, block):
            w_up_ref[row * rows : (row + 1) * rows, col * up_cols : (col + 1) * up_cols] = block[:, :up_cols]
            for fold in range(folds):
                down = (row * folds + fold) * rows
                start = up_cols + fold * out_cols
                w_down_ref[down : down + rows, col * out_cols : (col + 1) * out_cols] = block[
                    :, start : start + out_cols
                ]

        unpack(place_ref, blocks, packed_ref, put, dp_size, spread)

    feed_forward_steps(
        images, middle_ref, attended_ref, w_up_ref, w_down_ref, proj_t_ref, vectors_ref, bias_up_ref,
        d_middle_ref, d_attended_ref, vector_sums_ref, up_sums_ref, wide_ref, *scratches, proj_total_ref,
    )

    @pl.when(pl.program_id(0) == pl.num_programs(0) - 1)
    def _():
        narrow_pieces(place_ref, wide_ref, outputs, spread)
        down_low_ref[...] = down_total_ref[...].T.astype(jnp.bfloat16)

        def take(row, col):
            across = slice(row * rows, (row + 1) * rows)
            cols = slice(col * out_cols, (col + 1) * out_cols)
            parts = [up_total_ref[across, col * up_cols : (col + 1) * up_cols].astype(jnp.bfloat16)]
            for fold in range(folds):
                down = (row * folds + fold) * rows
                parts.append(down_low_ref[down : down + rows, cols])
            return jnp.concatenate(parts, axis=1)

        pack(place_ref, take, keep_ref, leave_ref, dp_size, spread)


def attention_back_packed_kernel(
    dp_size, spread, place_ref, x_ref, qkv_ref, probs_ref, d_attended_ref, vectors_ref, proj_total_ref, _,
    d_projected_ref, keep_ref, leave_ref, vector_sums_ref, normed_ref, total_ref,
):
    @pl.when(pl.program_id(0) == 0)
    def _():
        total_ref[...] = jnp.zeros_like(total_ref)
        vector_sums_ref[...] = jnp.zeros_like(vector_sums_ref)

    attention_back_steps(
        x_ref, qkv_ref, probs_ref, d_attended_ref, vectors_ref, vector_sums_ref, normed_ref, d_projected_ref, total_ref
    )

    @pl.when(pl.program_id(0) == pl.num_programs(0) - 1)
    def _():
        rows = keep_ref.shape[1]
        qkv_cols, proj_cols = total_ref.shape[1] // spread, proj_total_ref.shape[1] // spread

        def take(row, col):
            down = slice(row * rows, (row + 1) * rows)
            parts = [
                total_ref[down, col * qkv_cols : (col + 1) * qkv_cols],
                proj_total_ref[down, col * proj_cols : (col + 1) * proj_cols],
            ]
            return jnp.concatenate(parts, axis=1).astype(jnp.bfloat16)

        pack(place_ref, take, keep_ref, leave_ref, dp_size, spread)


def first_input_kernel(
    length, x_ref, d_projected_ref, d_middle_ref, qkv_t_ref, vectors_ref, before_ref, *refs
):
    d_input_ref, vector_sums_ref, back_ref = refs[-3:]

    @pl.when(pl.program_id(0) == 0)
    def _():
        vector_sums_ref[...] = before_ref[...]

    def put(image, rows, values):
        d_input_ref[rows, :] = values.astype(jnp.bfloat16)

    input_back_steps(
        put, length, x_ref, d_projected_ref, d_middle_ref, qkv_t_ref, vectors_ref, vector_sums_ref, back_ref
    )


def last_input_kernel(
    images, spread, length, first, place_ref, x_ref, d_projected_ref, d_middle_ref, qkv_t_ref, vectors_ref, before_ref,
    d_input_ref, _, *refs,
):
    pieces, (vector_sums_ref, wide_ref, back_ref) = refs[:spread], refs[spread:]

    @pl.when(pl.program_id(0) == 0)
    def _():
        vector_sums_ref[...] = before_ref[...]
        for image in range(first):
            rows = slice(image * length, (image + 1) * length)
            put_image(wide_ref, image, images, d_input_ref[rows, :].astype(jnp.float32))

    def put(image, rows, values):
        put_image(wide_ref, first + image, images, values)

    input_back_steps(
        put, length, x_ref, d_projected_ref, d_middle_ref, qkv_t_ref, vectors_ref, vector_sums_ref, back_ref
    )

    @pl.when(pl.program_id(0) == pl.num_programs(0) - 1)
    def _():
        narrow_pieces(place_ref, wide_ref, pieces, spread)


def cut(array_ref, parts_ref):
    count = parts_ref.shape[2]
    for member in range(parts_ref.shape[0]):
        parts_ref[member] = array_ref[:, member * count : (member + 1) * count, :]


def pack_kernel(qkv_ref, proj_ref, up_ref, down_ref, pack_ref):
    rows, start = pack_ref.shape[0], 0
    parts = [qkv_ref[...], proj_ref[...], up_ref[...]]
    parts += [down_ref[fold * rows : (fold + 1) * rows, :] for fold in range(down_ref.shape[0] // rows)]
    for part in parts:
        pack_ref[:, start : start + part.shape[1]] = part.astype(jnp.bfloat16)
        start += part.shape[1]


def pair_kernel(own_ref, arrived_ref, _, first_ref, second_ref):
    start = first_ref.shape[2]
    for at, pack_ref in enumerate((own_ref, arrived_ref)):
        first_ref[at] = pack_ref[:, :start]
        second_ref[at] = pack_ref[:, start:]


def join_kernel(count, *refs):
    size = refs[0].shape[0]
    for at, part_ref in enumerate(refs[:count]):
        refs[-1][at * size : (at + 1) * size] = part_ref[...]


def settle_kernel(spread, place_ref, *refs):
    lists, (output_ref, token_ref) = refs[:-2], refs[-2:]
    token_ref[...] = jnp.zeros_like(token_ref)
    group = place_ref[0] & (spread - 1)
    count = lists[0].shape[1]
    share = len(lists) // spread * count
    for at, piece_ref in enumerate(lists):
        relative, part = at % spread, at // spread
        start = pl.multiple_of((group ^ relative) * share + part * count, count)
        output_ref[:, pl.ds(start, count), :] = piece_ref[...]


def lane_table(rows, columns):
    lane = lax.broadcasted_iota(jnp.int32, (rows, 128), 1)
    table = jnp.zeros((rows, 128), jnp.float32)
    for at, column in enumerate(columns):
        table = jnp.where(lane == at, column, table)
    return table


def added(parts):
    while len(parts) > 1:
        parts = [sum(parts[at : at + 2][1:], parts[at]) for at in range(0, len(parts), 2)]
    return parts[0]


def row_sum(values):
    return jnp.sum(values, axis=1, keepdims=True)


def after_kernel(*refs):
    pass


def add_kernel(count, keep_ref, arrived_ref, *refs):
    parts = refs[-count:]
    size = parts[0].shape[0]
    for at, part_ref in enumerate(parts):
        rows = slice(at * size, (at + 1) * size)
        total = keep_ref[rows].astype(jnp.float32) + arrived_ref[rows].astype(jnp.float32)
        part_ref[...] = total.astype(part_ref.dtype)


def gradient_kernel(count, *refs):
    block_parts, sums, refs = refs[:count], refs[count : count + 3], refs[count + 3 :]
    masters, rows_old, refs = refs[:4], refs[4:8], refs[8:]
    grads, (row_ref, message_ref) = refs[:4], refs[4:]
    blocks = added([part[0].astype(jnp.float32) for part in block_parts])
    rows, up_cols = grads[2].shape
    qkv_cols, out_cols = grads[0].shape[1], grads[1].shape[1]
    folds = grads[3].shape[0] // rows
    up = blocks[:, :up_cols]
    downs = [blocks[:, up_cols + fold * out_cols :][:, :out_cols] for fold in range(folds)]
    start = up_cols + folds * out_cols
    qkv = blocks[:, start : start + qkv_cols]
    proj = blocks[:, start + qkv_cols :]
    grads[0][...] = qkv
    grads[1][...] = proj
    grads[2][...] = up
    for fold in range(folds):
        grads[3][fold * rows : (fold + 1) * rows, :] = downs[fold]
    squares = [part * part + tiny_square for part in (qkv, proj, up, *downs)]
    row_ref[...] = lane_table(rows, [row_sum(square) for square in squares]).T[: row_ref.shape[0], :]
    width = message_ref.shape[1]
    message_ref[...] = jnp.zeros_like(message_ref)
    for at, square in enumerate((*squares[:3], added(squares[3:]))):
        message_ref[at : at + 1, : square.shape[1]] = column_sum(square)
    scalars = [column_sum(row_sum(master[...] * master[...])) for master in masters]
    scalars += [row_sum(part[...].reshape(1, part.shape[0])) for part in rows_old]
    message_ref[4:5, :128] = lane_table(1, scalars)
    att_ref, ff_ref, up_ref = sums
    count = up_ref.shape[1] // width
    message_ref[8:12, :] = att_ref[:4]
    message_ref[12:15, :] = ff_ref[:3]
    for at in range(count):
        message_ref[15 + at : 16 + at, :] = up_ref[:, at * width : (at + 1) * width]
    message_ref[15 + count : 16 + count, :] = ff_ref[3:4]


def column_kernel(row_ref, *refs):
    parts, (cols_ref, message_ref) = refs[:-3], refs[-2:]
    total = added([part[...] for part in parts])
    cols_ref[...] = total[:8]
    width = total.shape[1]
    rows = row_ref.shape[1]
    message_ref[...] = jnp.zeros_like(message_ref)
    message_ref[:8, :rows] = row_ref[...]
    columns = [row_sum(total[which : which + 1]) for which in range(4)]
    squares = [total[4:5, which : which + 1] for which in range(4)]
    message_ref[8:9, :] = lane_table(1, columns + squares)
    for tile in range(width // 128):
        message_ref[16 * (tile + 1) : 16 * (tile + 2), :] = total[8:, tile * 128 : (tile + 1) * 128]


def update_kernel(count, heights, widths, *refs):
    messages, refs = refs[:count], refs[count:]
    cols_ref, vectors_ref, moment_ref, refs = refs[0], refs[1], refs[2], refs[3:]
    grads, masters, rows_old, cols_old, refs = refs[:4], refs[4:8], refs[8:12], refs[12:16], refs[17:]
    news, cols_new, rows_out, refs = refs[:4], refs[4:8], refs[8:12], refs[12:]
    vector_grad_ref, moment_new_ref, vector_new_ref = refs
    sums = added([message[...] for message in messages])
    height = grads[0].shape[0]
    folds = grads[3].shape[0] // height
    lanes = [[0], [1], [2], list(range(3, 3 + folds))]
    share = 1.0 - decay_rate
    for which in range(4):
        entries = heights[which] * widths[which]
        cols = cols_old[which].shape[0]
        new = decay_rate * cols_old[which][...].reshape(1, cols) + share / heights[which] * cols_ref[
            which : which + 1, :cols
        ]
        cols_new[which][...] = new[0]
        old_total = cols_ref[4:5, 4 + which : 5 + which]
        mean_rows = (decay_rate * old_total + share / widths[which] * sums[8:9, which : which + 1]) / heights[which]
        rate = step_rate * jnp.sqrt(sums[8:9, 4 + which : 5 + which] / entries)
        across = new / mean_rows
        old = rows_old[which][...].reshape(1, len(lanes[which]) * height)
        row_sums = jnp.concatenate([sums[lane : lane + 1, :height] for lane in lanes[which]], axis=1)
        row = decay_rate * old + share / widths[which] * row_sums
        rows_out[which][...] = row[0]
        for fold in range(len(lanes[which])):
            part = slice(fold * height, (fold + 1) * height)
            column = jnp.broadcast_to(row[:, part], (8, height)).T[:, :1]
            news[which][part, :] = masters[which][part, :] - rate * grads[which][part, :] * lax.rsqrt(column * across)
    vectors = vectors_ref[...]
    count = vectors.shape[0]
    gradient = jnp.concatenate(
        [sums[16 * (tile + 1) : 16 * (tile + 1) + count] for tile in range(vectors.shape[1] // 128)], axis=1
    )
    vector_grad_ref[...] = gradient
    moment = decay_rate * moment_ref[...] + share * (gradient * gradient + tiny_square)
    moment_new_ref[...] = moment
    spread = jnp.sqrt(jnp.mean(vectors * vectors, axis=1, keepdims=True))
    vector_new_ref[...] = vectors - step_rate * spread * gradient * lax.rsqrt(moment)


def packed_body(
    tokens, keep_mask, cotangent, qkv_weight, proj_weight, up_weight, down_weight, vectors,
    qkv_rows, qkv_cols, proj_rows, proj_cols, up_rows, up_cols, down_rows, down_cols, vector_moment,
):
    spread, dp_size = lax.axis_size("group"), lax.axis_size("dp")
    low, high = jnp.bfloat16, jnp.float32
    place = linear_place().astype(jnp.int32).reshape(1)
    group = lax.axis_index("group")
    held, slots, width = tokens.shape
    images, length = keep_mask.shape
    hidden = up_weight.shape[1] * spread
    total = images * length
    rows = qkv_weight.shape[0]
    folds = down_weight.shape[0] // rows
    core_bits = (1,)
    near_bits = tuple(1 << at for at in range(1, spread.bit_length()))
    far_bits = tuple(spread << at for at in range(1, dp_size.bit_length() - 1))
    half = spread * dp_size // 2

    anywhere = pl.BlockSpec(memory_space=pl.ANY)
    in_smem = pl.BlockSpec(memory_space=pltpu.SMEM)

    in_vmem = pl.BlockSpec(memory_space=pltpu.VMEM)
    small = functools.partial(
        pl.pallas_call, compiler_params=pltpu.CompilerParams(vmem_limit_bytes=vmem_bytes)
    )
    masters = (qkv_weight, proj_weight, up_weight, down_weight)
    parted = jax.ShapeDtypeStruct((spread, slots, images, width), low)

    def after(array, awaited):
        return small(
            after_kernel,
            in_specs=[anywhere] * (1 + len(awaited)),
            out_specs=anywhere,
            out_shape=jax.ShapeDtypeStruct(array.shape, array.dtype),
            input_output_aliases={0: 0},
        )(array, *awaited)

    def to_group(parts):
        return lax.all_to_all(parts, "group", split_axis=0, concat_axis=0, tiled=True)

    def to_images(parts):
        return to_group(parts).reshape(total, width)

    def exchange(parts):
        return [parts[0]] + [permute(part, relative) for relative, part in enumerate(parts) if relative]

    def settle(parts):
        parts = [part.reshape(slots, -1, width) for part in parts]
        whole, token = small(
            functools.partial(settle_kernel, spread),
            in_specs=[in_smem] + [in_vmem] * len(parts),
            out_specs=[in_vmem] * 2,
            out_shape=[
                jax.ShapeDtypeStruct((slots, held, width), low),
                jax.ShapeDtypeStruct((8, 128), high),
            ],
        )(place, *parts)
        return whole.transpose(1, 0, 2), token

    first_cols = qkv_weight.shape[1] + proj_weight.shape[1]
    second_cols = up_weight.shape[1] + folds * down_weight.shape[1]
    pack_own = small(pack_kernel, out_shape=jax.ShapeDtypeStruct((rows, first_cols + second_cols), low))(*masters)
    across_y, across_x = near_bits
    pack_arrived = permute(pack_own, across_y)
    token_cut = small(cut, out_shape=parted)(tokens.transpose(1, 0, 2))
    first_pair, second_pair = small(
        pair_kernel,
        in_specs=[in_vmem] * 2 + [anywhere],
        out_shape=[
            jax.ShapeDtypeStruct((2, rows, first_cols), low),
            jax.ShapeDtypeStruct((2, rows, second_cols), low),
        ],
    )(pack_own, pack_arrived, token_cut)
    cotangent_cut = small(cut, out_shape=parted)(cotangent.transpose(1, 0, 2))

    def gather_far(pair):
        return [pair] + [permute(pair, mask) for mask in direct_masks(far_bits)]

    def join(parts, awaited=()):
        count = len(parts) * parts[0].shape[0]
        return small(
            functools.partial(join_kernel, len(parts)),
            in_specs=[in_vmem] * len(parts) + [anywhere] * len(awaited),
            out_shape=jax.ShapeDtypeStruct((count, *parts[0].shape[1:]), low),
        )(*parts, *awaited)

    def gather_rest(held):
        arrived = permute(held, across_x)
        return [held, arrived, permute(held, core_bits[0]), permute(arrived, core_bits[0])]

    first_far = gather_far(first_pair)
    inputs = to_images(after(token_cut, first_far[1:2]))
    first_far = join(first_far, [cotangent_cut])
    upstream = to_images(cotangent_cut)
    first_blocks = gather_rest(first_far)
    second_far = gather_far(second_pair)

    step_rows = PER_STEP * length
    block = (step_rows, width)
    pairs = width // (2 * HEAD_DIM)
    steps = images // PER_STEP
    statics = (images, dp_size, spread)
    wide = scratch(width // 128, total, 128)
    probs_block = (PER_STEP, pairs, length, 2 * length)
    attention_outs = [
        ((total, 3 * width), low, (step_rows, 3 * width)),
        ((images, *probs_block[1:]), low, probs_block),
        ((total, width), low, block),
        ((total, width), high, block),
    ]
    attention_flops = (2 * total * width * 4 * width + 8 * total * length * width) // steps
    attention_scratches = [scratch(length, images), scratch(step_rows, width, dtype=low)]
    *attention, x, w_qkv, w_proj, qkv_t, proj_t = call_kernel(
        first_attention_kernel, statics, 1,
        ["place"] + [None] * 7,
        attention_outs
        + [
            ((total, width), low, None),
            ((width, 3 * width), low, None),
            ((width, width), low, None),
            ((3 * width, width), low, None),
            ((width, width), low, None),
        ],
        [scratch(dp_size * spread, rows, first_cols, dtype=low), wide] + attention_scratches,
        (place, inputs, *first_blocks, keep_mask, vectors),
        attention_flops,
    )
    second_blocks = gather_rest(join(second_far, attention[:1]))
    for first_step, count in ((1, steps - 2), (steps - 1, 1)):
        attention = call_kernel(
            next_attention_kernel, (first_step * PER_STEP,), count,
            [block] + [None] * 4 + ["await"] * len(attention),
            attention_outs, attention_scratches,
            (x, keep_mask, w_qkv, w_proj, vectors, *attention),
            attention_flops * count, first_step=first_step,
            aliases={5 + at: at for at in range(len(attention))},
        )
    qkv, probs, attended, middle = attention
    piece = ((slots * images, width), low, None)
    ff_rows = FF_PER_STEP * length
    ff_block = (ff_rows, width)
    results = call_kernel(
        feed_forward_packed_kernel, statics, images // FF_PER_STEP,
        ["place"] + [None] * 5 + [ff_block, ff_block] + [None] * 2,
        [piece] * spread
        + [
            ((total, width), high, ff_block),
            ((total, width), low, ff_block),
            ((half, rows, second_cols), low, None),
            ((half, rows, second_cols), low, None),
            ((width, width), high, None),
            ((8, width), high, None),
            ((1, hidden), high, None),
        ],
        [
            scratch(width, hidden, dtype=low),
            scratch(hidden, width, dtype=low),
            scratch(hidden, width, dtype=low),
            scratch(dp_size * spread, rows, second_cols, dtype=low),
            scratch(1, hidden),
            wide,
            scratch(ff_rows, width, dtype=low),
            scratch(width, ff_rows, dtype=low),
            scratch(ff_rows, width, dtype=low),
            scratch(width, ff_rows, dtype=low),
            scratch(ff_rows, width),
            scratch(ff_rows, 128),
            scratch(ff_rows, width),
            scratch(ff_rows, width),
            scratch(hidden, width, dtype=low),
            scratch(width, hidden, dtype=low),
            scratch(width, hidden),
            scratch(width, hidden),
        ],
        (
            place, upstream, *second_blocks, middle, attended, proj_t, vectors,
        ),
        12 * total * width * hidden + 4 * total * width * width, total * hidden,
    )
    d_middle, d_attended, ff_keep, ff_leave, proj_total, ff_sums, up_sums = results[spread:]

    def add_parts(count, keep, arrived, awaited):
        part = (keep.shape[0] // count, *keep.shape[1:])
        return small(
            functools.partial(add_kernel, count),
            in_specs=[in_vmem] * 2 + [anywhere] * len(awaited),
            out_specs=[in_vmem] * count,
            out_shape=[jax.ShapeDtypeStruct(part, high)]
            + [jax.ShapeDtypeStruct(part, low)] * (count - 1),
        )(keep, arrived, *awaited)

    ff_first = permute(ff_leave, core_bits[0])
    ff_count = half // 2
    ff_next = add_wide(ff_keep[ff_count:], ff_first[ff_count:]).astype(low)
    ff_arrived = permute(ff_next, across_x)
    output_parts = exchange(results[:spread])
    pack_half = ((half, rows, first_cols), low, None)
    wide_rows = (step_rows, 3 * width)
    d_projected, qkv_keep, qkv_leave, att_sums = call_kernel(
        attention_back_packed_kernel, (dp_size, spread), steps,
        ["place", block, wide_rows, probs_block, block, None, None, "await"],
        [((total, 3 * width), low, wide_rows), pack_half, pack_half, ((8, width), high, None)],
        [scratch(step_rows, width, dtype=low), scratch(width, 3 * width)],
        (place, x, qkv, probs, d_attended, vectors, proj_total, ff_next),
        2 * total * width * 3 * width + 16 * total * length * width,
    )
    qkv_arrived = permute(after(qkv_leave, output_parts[1:]), core_bits[0])
    input_flops = 2 * total * width * 3 * width
    input_ins = [block, wide_rows, block, None, None, None]
    input_outs = [((total, width), low, block), ((8, width), high, None)]
    d_input, att_sums = call_kernel(
        first_input_kernel, (length,), 1, input_ins, input_outs, [scratch(step_rows, width)],
        (x, d_projected, d_middle, qkv_t, vectors, att_sums), input_flops // steps,
    )
    ff_quarter = half // 4
    ff_last = add_wide(
        ff_keep[ff_quarter:ff_count], ff_first[ff_quarter:ff_count], ff_arrived[ff_quarter:]
    ).astype(low)
    ff_last_arrived = permute(ff_last, across_y)
    qkv_held, *leaving = add_parts(4, qkv_keep, qkv_arrived, [ff_last])
    qkv_parts = [permute(part, mask) for part, mask in zip(leaving, direct_masks(near_bits))]
    d_input, att_sums = call_kernel(
        first_input_kernel, (length,), 1, input_ins + ["await"] * 2, input_outs, [scratch(step_rows, width)],
        (x, d_projected, d_middle, qkv_t, vectors, att_sums, d_input, leaving[0]), input_flops // steps,
        first_step=1, aliases={6: 0},
    )
    ff_held = add_wide(
        ff_keep[:ff_quarter], ff_first[:ff_quarter], ff_arrived[:ff_quarter], ff_last_arrived
    )
    qkv_held = add_wide(qkv_held, *qkv_parts)
    blocks = jnp.concatenate([ff_held, qkv_held], axis=2)
    far_leaving = [blocks[at : at + 1].astype(low) for at in range(1, blocks.shape[0])]
    block_parts = [blocks[:1]] + [permute(part, mask) for part, mask in zip(far_leaving, direct_masks(far_bits))]
    results = call_kernel(
        last_input_kernel, (images, spread, length, 2 * PER_STEP), steps - 2,
        ["place"] + input_ins + [None, "await"],
        [piece] * spread + [((8, width), high, None)],
        [wide, scratch(step_rows, width)],
        (place, x, d_projected, d_middle, qkv_t, vectors, att_sums, d_input, far_leaving[0]), input_flops // steps * (steps - 2),
        first_step=2,
    )
    att_sums = results[spread]
    input_pieces = list(results[:spread])
    heights = [master.shape[0] * dp_size for master in masters]
    widths = [master.shape[1] * spread for master in masters]
    rows_old, cols_old = [qkv_rows, proj_rows, up_rows, down_rows], [qkv_cols, proj_cols, up_cols, down_cols]

    def like(*arrays):
        return [jax.ShapeDtypeStruct(array.shape, high) for array in arrays]

    operands = (*block_parts, att_sums, ff_sums, up_sums, *masters, *rows_old)
    *grads, row_sums, message = small(
        functools.partial(gradient_kernel, len(block_parts)),
        out_shape=like(*masters) + [jax.ShapeDtypeStruct((8, rows), high), jax.ShapeDtypeStruct((24, width), high)],
    )(*operands)
    input_pieces[1] = after(input_pieces[1], [row_sums])
    output_parts[0] = after(output_parts[0], [row_sums])
    block_output, settled = settle(output_parts)
    input_grad, input_settled = settle(exchange(input_pieces))
    message = added([message] + [permute(message, mask) for mask in direct_masks((across_x, far_bits[0]))])
    for bit in far_bits[1:-1]:
        message = message + permute(message, bit)
    messages = [message, permute(message, far_bits[-1])]
    col_sums, message = small(
        column_kernel,
        in_specs=[in_vmem] * (1 + len(messages)) + [anywhere],
        out_shape=[
            jax.ShapeDtypeStruct((8, width), high),
            jax.ShapeDtypeStruct((16 + width // 8, 128), high),
        ],
    )(row_sums, *messages, settled)
    messages = [message] + [permute(message, mask) for mask in range(1, spread)]
    operands = (*messages, col_sums, vectors, vector_moment, *grads, *masters, *rows_old, *cols_old)
    results = small(
        functools.partial(update_kernel, len(messages), heights, widths),
        in_specs=[in_vmem] * len(operands) + [anywhere],
        out_shape=like(*masters, *cols_old, *rows_old, vectors, vectors, vectors),
    )(*operands, input_settled)
    news, cols_new, rows_out = results[:4], results[4:8], results[8:12]
    vector_grad, vector_moment_new, vector_new = results[12:]
    factored = []
    for which in range(4):
        factored += [grads[which], rows_out[which], cols_new[which], news[which]]
    return (block_output, input_grad, *factored, vector_grad, vector_moment_new, vector_new)


def body(*arrays):
    spread, dp_size = lax.axis_size("group"), lax.axis_size("dp")
    rows, images = arrays[3].shape[0], arrays[1].shape[0]
    slots, width = arrays[0].shape[1:]
    folds = arrays[6].shape[0] // rows
    powers = all(size & (size - 1) == 0 for size in (spread, dp_size))
    fits = powers and spread == 4 and dp_size > 2
    fits = fits and arrays[5].shape[1] <= width and folds <= 5
    fits = fits and rows % 16 == 0 and images % FF_PER_STEP == 0 and images > 2 * PER_STEP and images % 16 == 0 and slots % 4 == 0
    return packed_body(*arrays) if fits else general_body(*arrays)


def solution(mesh):
    in_specs = (
        P("dp", "group", None),
        P(("dp", "group"), None),
        P("dp", "group", None),
        P("dp", "group"),
        P("dp", "group"),
        P("dp", "group"),
        P("dp", "group"),
        P(),
        P("dp"),
        P("group"),
        P("dp"),
        P("group"),
        P("dp"),
        P("group"),
        P("dp"),
        P("group"),
        P(),
    )
    out_specs = (
        P("dp", "group", None),
        P("dp", "group", None),
        P("dp", "group"),
        P("dp"),
        P("group"),
        P("dp", "group"),
        P("dp", "group"),
        P("dp"),
        P("group"),
        P("dp", "group"),
        P("dp", "group"),
        P("dp"),
        P("group"),
        P("dp", "group"),
        P("dp", "group"),
        P("dp"),
        P("group"),
        P("dp", "group"),
        P(),
        P(),
        P(),
    )
    return jax.shard_map(body, mesh=mesh, in_specs=in_specs, out_specs=out_specs, check_vma=False)
```

```python
import functools
import math

import jax
import jax.numpy as jnp
from jax import lax
from jax.experimental import pallas as pl
from jax.experimental.pallas import tpu as pltpu
from jax.sharding import PartitionSpec as P

HEAD_DIM = 64
STEP_NUMBER = 10


step_rate = 0.3
norm_epsilon = 1e-06
tiny_square = 1e-30
decay_rate = 1.0 - STEP_NUMBER ** (-0.8)
LOG2_E = 1.4426950408889634


def axis_bits(name):
    count = lax.axis_size(name)
    return [(name, 1 << place) for place in range(count.bit_length() - 1)]


def swap_partner(array, step):
    name, bit = step
    count = lax.axis_size(name)
    return lax.ppermute(array, name, [(rank, rank ^ bit) for rank in range(count)])


def upper_side(step):
    name, bit = step
    return (lax.axis_index(name) & bit) != 0


def gather_blocks(array, steps):
    for step in steps:
        arrived = swap_partner(array, step)
        upper = upper_side(step)
        array = jnp.stack([jnp.where(upper, arrived, array), jnp.where(upper, array, arrived)])
    return array


def scatter_sum(array, steps):
    for step in steps:
        upper = upper_side(step)
        leaving = jnp.where(upper, array[0], array[1]).astype(jnp.bfloat16)
        arrived = swap_partner(leaving, step)
        array = jnp.where(upper, array[1], array[0]).astype(jnp.float32) + arrived.astype(jnp.float32)
    return array


def sum_everywhere(array, steps):
    for step in steps:
        array = array + swap_partner(array, step)
    return array


def sum_parts(parts, steps):
    flat = [part.reshape(-1) for part in parts]
    total = sum_everywhere(jnp.concatenate(flat), steps)
    result, start = [], 0
    for part in parts:
        result.append(total[start : start + part.size].reshape(part.shape))
        start += part.size
    return result


def block_order(steps):
    order = []
    for name in ("dp", "group"):
        bits = sorted((step for step in steps if step[0] == name), key=lambda step: -step[1])
        order.append([steps.index(step) for step in bits])
    return order


def blocks_to_whole(blocks, steps):
    count = len(steps)
    rows, cols = blocks.shape[count:]
    dp_axes, group_axes = block_order(steps)
    dp_axes = [count - 1 - axis for axis in dp_axes]
    group_axes = [count - 1 - axis for axis in group_axes]
    whole = blocks.transpose(dp_axes + [count] + group_axes + [count + 1])
    return whole.reshape(rows << len(dp_axes), cols << len(group_axes))


def whole_to_blocks(whole, steps):
    dp_axes, group_axes = block_order(steps)
    rows = whole.shape[0] >> len(dp_axes)
    cols = whole.shape[1] >> len(group_axes)
    split = whole.reshape([2] * len(dp_axes) + [rows] + [2] * len(group_axes) + [cols])
    places = dp_axes + [len(steps)] + group_axes + [len(steps) + 1]
    return split.transpose([places.index(axis) for axis in range(len(places))])


PER_STEP = 4
FF_PER_STEP = 4
SLICE = 48
FF_CHUNK = 256
vmem_bytes = 60 * 1024 * 1024


def dot(left, right, left_axis=1, right_axis=0):
    return lax.dot_general(
        left, right, (((left_axis,), (right_axis,)), ((), ())), preferred_element_type=jnp.float32
    )


def normal_form(values):
    center = jnp.mean(values, axis=-1, keepdims=True)
    centered = values - center
    spread = jnp.mean(centered * centered, axis=-1, keepdims=True)
    scale = lax.rsqrt(spread + norm_epsilon)
    return centered * scale, scale


def norm_back(grad, unit, scale, gain):
    weighted = grad * gain
    along = jnp.mean(weighted * unit, axis=-1, keepdims=True)
    level = jnp.mean(weighted, axis=-1, keepdims=True)
    return scale * (weighted - level - unit * along)


def slices_of(count):
    return [slice(start, start + SLICE) for start in range(0, count, SLICE)]


def fold_rows(values):
    return jnp.sum(values.reshape(values.shape[0] // 8, 8, values.shape[1]), axis=0)


def column_sum(values):
    return jnp.sum(values, axis=0, keepdims=True)


def pair_mask(length):
    return lax.broadcasted_iota(jnp.int32, (length, 2 * HEAD_DIM), 1) < HEAD_DIM


def lane_tiles(count):
    return [slice(start, min(start + 128, count)) for start in range(0, count, 128)]


def stack_heads(pair, first):
    none = jnp.zeros_like(pair)
    return jnp.concatenate([jnp.where(first, pair, none), jnp.where(first, none, pair)], axis=0)


def join_heads(rows, first):
    length = rows.shape[0] // 2
    return jnp.where(first, rows[:length], rows[length:])


def gelu_and_slope(pre):
    bell = jnp.exp2(pre * pre * (-0.5 * LOG2_E))
    base = 1.0 + (0.3275911 * 0.5**0.5) * jnp.abs(pre)
    inverse = pl.reciprocal(base, approx=True)
    inverse = inverse * (2.0 - base * inverse)
    poly = inverse * (
        0.5 * 0.254829592
        + inverse
        * (
            0.5 * -0.284496736
            + inverse
            * (0.5 * 1.421413741 + inverse * (0.5 * -1.453152027 + inverse * (0.5 * 1.061405429)))
        )
    )
    tail = poly * bell
    below = jnp.where(pre >= 0, 1.0 - tail, tail)
    return pre * below, below + pre * bell * 0.3989422804014327


def widen(source_ref, wide_ref, images):
    tiles, total, lanes = wide_ref.shape
    rows_at_once = 8 * images

    @pl.loop(0, total // rows_at_once)
    def _(part):
        rows = pl.ds(pl.multiple_of(part * rows_at_once, rows_at_once), rows_at_once)
        for tile in range(tiles):
            cols = slice(tile * lanes, (tile + 1) * lanes)
            wide_ref[tile, rows, :] = source_ref[rows, cols].astype(jnp.float32)


def narrow(wide_ref, target_ref, images):
    tiles, total, lanes = wide_ref.shape
    rows_at_once = 8 * images

    @pl.loop(0, total // rows_at_once)
    def _(part):
        rows = pl.ds(pl.multiple_of(part * rows_at_once, rows_at_once), rows_at_once)
        for tile in range(tiles):
            cols = slice(tile * lanes, (tile + 1) * lanes)
            target_ref[rows, cols] = wide_ref[tile, rows, :].astype(target_ref.dtype)


def take_image(wide_ref, image, images):
    tiles, total, _ = wide_ref.shape
    rows = pl.ds(image, total // images, images)
    return jnp.concatenate([wide_ref[tile, rows, :] for tile in range(tiles)], axis=1)


def put_image(wide_ref, image, images, values):
    tiles, total, lanes = wide_ref.shape
    rows = pl.ds(image, total // images, images)
    for tile in range(tiles):
        wide_ref[tile, rows, :] = values[:, tile * lanes : (tile + 1) * lanes]


def attention_kernel(
    images, tokens_ref, bias_ref, w_qkv_ref, w_proj_ref, vectors_ref,
    x_ref, qkv_ref, probs_ref, attended_ref, middle_ref, wide_ref, normed_ref,
):
    @pl.when(pl.program_id(0) == 0)
    def _():
        widen(tokens_ref, wide_ref, images)
        to_image_rows(wide_ref, x_ref, images)

    attention_steps(
        x_ref, lambda image: bias_ref[image], w_qkv_ref, w_proj_ref, vectors_ref,
        qkv_ref, probs_ref, attended_ref, middle_ref, normed_ref,
    )


def to_image_rows(wide_ref, x_ref, images):
    length = wide_ref.shape[1] // images

    @pl.loop(0, images)
    def _(image):
        rows = pl.ds(pl.multiple_of(image * length, length), length)
        x_ref[rows, :] = take_image(wide_ref, image, images).astype(jnp.bfloat16)


def attention_steps(
    x_ref, bias_column, w_qkv_ref, w_proj_ref, vectors_ref,
    qkv_ref, probs_ref, attended_ref, middle_ref, normed_ref,
):
    per_step, _, length, _ = probs_ref.shape
    step_rows, width = middle_ref.shape
    base = 0 if x_ref.shape[0] == step_rows else pl.program_id(0) * step_rows

    for rows in slices_of(step_rows):
        x = x_ref[pl.ds(pl.multiple_of(base + rows.start, SLICE), SLICE), :].astype(jnp.float32)
        unit, _ = normal_form(x)
        normed_ref[rows, :] = (unit * vectors_ref[0:1] + vectors_ref[1:2]).astype(jnp.bfloat16)
    for part in range(3):
        cols = slice(part * width, (part + 1) * width)
        projected = dot(normed_ref[...], w_qkv_ref[:, cols])
        if part != 1:
            row = 2 if part == 0 else 3
            projected = projected + vectors_ref[row : row + 1]
        qkv_ref[:, cols] = projected.astype(jnp.bfloat16)

    pairs = width // (2 * HEAD_DIM)
    first = pair_mask(length)
    place = lax.broadcasted_iota(jnp.int32, (length, 2 * length), 0)
    asker = lax.broadcasted_iota(jnp.int32, (length, 2 * length), 1)
    own = place == jnp.where(asker >= length, asker - length, asker)

    def scores_of(image):
        rows = slice(image * length, (image + 1) * length)
        result = []
        for pair in range(pairs):
            low = pair * 2 * HEAD_DIM
            queries = stack_heads(qkv_ref[rows, low : low + 2 * HEAD_DIM], first)
            result.append(dot(qkv_ref[rows, width + low : width + low + 2 * HEAD_DIM], queries, 1, 1))
        return result

    next_scores = scores_of(0)
    for image in range(per_step):
        rows = slice(image * length, (image + 1) * length)
        all_scores = next_scores
        if image + 1 < per_step:
            next_scores = scores_of(image + 1)
        column = bias_column(image)
        for cols in lane_tiles(2 * length):
            bias = jnp.where(own[:, cols], 0.0, column)
            for pair in range(pairs):
                scores = all_scores[pair][:, cols] * (HEAD_DIM**-0.5 * LOG2_E) + bias
                weights = jnp.exp2(scores - jnp.max(scores, axis=0, keepdims=True))
                probs = weights * (1.0 / jnp.sum(weights, axis=0, keepdims=True))
                probs_ref[image, pair, :, cols] = probs.astype(jnp.bfloat16)
        for pair in range(pairs):
            low = pair * 2 * HEAD_DIM
            values = qkv_ref[rows, 2 * width + low : 2 * width + low + 2 * HEAD_DIM]
            attended = join_heads(dot(probs_ref[image, pair], values, 0, 0), first)
            attended_ref[rows, low : low + 2 * HEAD_DIM] = attended.astype(jnp.bfloat16)

    middle_ref[...] = (
        x_ref[pl.ds(pl.multiple_of(base, length), step_rows), :].astype(jnp.float32)
        + dot(attended_ref[...], w_proj_ref[...])
        + vectors_ref[4:5]
    )


def feed_forward_kernel(
    images, middle_ref, cotangent_ref, attended_ref, w_up_ref, w_down_ref, proj_t_ref, vectors_ref, bias_up_ref,
    output_ref, d_middle_ref, d_attended_ref, up_grad_ref, down_grad_ref, proj_grad_ref, vector_sums_ref, up_sums_ref,
    wide_ref, *scratches,
):
    up_total_ref, down_total_ref, proj_total_ref = scratches[-3:]

    @pl.when(pl.program_id(0) == 0)
    def _():
        widen(cotangent_ref, wide_ref, images)

    feed_forward_steps(
        images, middle_ref, attended_ref, w_up_ref, w_down_ref, proj_t_ref, vectors_ref, bias_up_ref,
        d_middle_ref, d_attended_ref, vector_sums_ref, up_sums_ref, wide_ref, *scratches,
    )

    @pl.when(pl.program_id(0) == pl.num_programs(0) - 1)
    def _():
        narrow(wide_ref, output_ref, images)
        up_grad_ref[...] = up_total_ref[...].astype(jnp.bfloat16)
        down_grad_ref[...] = down_total_ref[...].T.astype(jnp.bfloat16)
        proj_grad_ref[...] = proj_total_ref[...].astype(jnp.bfloat16)


def feed_forward_steps(
    images, middle_ref, attended_ref, w_up_ref, w_down_ref, proj_t_ref, vectors_ref, bias_up_ref,
    d_middle_ref, d_attended_ref, vector_sums_ref, up_sums_ref,
    wide_ref, normed_ref, normed_t_ref, dy_ref, dy_t_ref, unit_ref, scale_ref, ahead_ref, back_ref,
    pre_ref, d_active_ref, active_ref, d_hidden_ref, up_t_ref, down_t_ref, up_total_ref, down_total_ref, proj_total_ref,
):
    step = pl.program_id(0)
    length = wide_ref.shape[1] // images
    hidden = w_up_ref.shape[1]
    per_step = middle_ref.shape[0] // length

    @pl.when(step == 0)
    def _():
        for total in (up_total_ref, down_total_ref, proj_total_ref, vector_sums_ref, up_sums_ref):
            total[...] = jnp.zeros_like(total)
        up_t_ref[...] = w_up_ref[...].T
        down_t_ref[...] = w_down_ref[...].T

    step_rows, width = middle_ref.shape
    for image in range(per_step):
        rows = slice(image * length, (image + 1) * length)
        dy_ref[rows, :] = take_image(wide_ref, step * per_step + image, images).astype(jnp.bfloat16)
    dy_sums = jnp.zeros((8, width), jnp.float32)
    for rows in slices_of(step_rows):
        dy_sums += fold_rows(dy_ref[rows, :].astype(jnp.float32))
        unit, scale = normal_form(middle_ref[rows, :])
        unit_ref[rows, :] = unit
        scale_ref[rows, :] = jnp.broadcast_to(scale, (SLICE, scale_ref.shape[1]))
        normed_ref[rows, :] = (unit * vectors_ref[5:6] + vectors_ref[6:7]).astype(jnp.bfloat16)
    vector_sums_ref[3:4] += column_sum(dy_sums)
    normed_t_ref[...] = normed_ref[...].T
    dy_t_ref[...] = dy_ref[...].T
    chunks = hidden // FF_CHUNK

    def cols_of(chunk):
        return slice(chunk * FF_CHUNK, (chunk + 1) * FF_CHUNK)

    def enter(chunk):
        cols, slot = cols_of(chunk), chunk % 2
        pre_ref[slot] = dot(normed_ref[...], w_up_ref[:, cols])
        d_active_ref[slot] = dot(dy_ref[...], down_t_ref[:, cols])

    def cross(chunk):
        cols, slot = cols_of(chunk), chunk % 2
        sums = jnp.zeros((8, FF_CHUNK), jnp.float32)
        for rows in slices_of(step_rows):
            active, slope = gelu_and_slope(pre_ref[slot, rows, :] + bias_up_ref[:, cols])
            active_ref[rows, cols] = active.astype(jnp.bfloat16)
            d_hidden = (d_active_ref[slot, rows, :] * slope).astype(jnp.bfloat16)
            d_hidden_ref[rows, cols] = d_hidden
            sums += fold_rows(d_hidden.astype(jnp.float32))
        up_sums_ref[:, cols] += column_sum(sums)

    def leave(chunk):
        cols = cols_of(chunk)
        down_total_ref[:, cols] += dot(dy_t_ref[...], active_ref[:, cols])
        up_total_ref[:, cols] += dot(normed_t_ref[...], d_hidden_ref[:, cols])

    enter(0)
    for chunk in range(chunks):
        if chunk + 1 < chunks:
            enter(chunk + 1)
        cross(chunk)
        if chunk > 0:
            leave(chunk - 1)
    leave(chunks - 1)
    ahead_ref[...] = dot(active_ref[...], w_down_ref[...])
    back_ref[...] = dot(d_hidden_ref[...], up_t_ref[...])

    gain_sums = shift_sums = branch_sums = jnp.zeros((8, width), jnp.float32)
    for rows in slices_of(step_rows):
        ahead_ref[rows, :] = middle_ref[rows, :] + ahead_ref[rows, :] + vectors_ref[11:12]
        unit = unit_ref[rows, :]
        grad = back_ref[rows, :]
        gain_sums += fold_rows(grad * unit)
        shift_sums += fold_rows(grad)
        d_middle = dy_ref[rows, :].astype(jnp.float32) + norm_back(
            grad, unit, scale_ref[rows, 0:1], vectors_ref[5:6]
        )
        d_middle_ref[rows, :] = d_middle
        d_branch = d_middle.astype(jnp.bfloat16)
        dy_ref[rows, :] = d_branch
        branch_sums += fold_rows(d_branch.astype(jnp.float32))
    vector_sums_ref[0:1] += column_sum(branch_sums)
    vector_sums_ref[1:2] += column_sum(gain_sums)
    vector_sums_ref[2:3] += column_sum(shift_sums)
    for image in range(per_step):
        rows = slice(image * length, (image + 1) * length)
        put_image(wide_ref, step * per_step + image, images, ahead_ref[rows, :])
    proj_total_ref[...] += dot(attended_ref[...], dy_ref[...], 0, 0)
    d_attended_ref[...] = dot(dy_ref[...], proj_t_ref[...]).astype(jnp.bfloat16)


def attention_back_kernel(
    images, x_ref, qkv_ref, probs_ref, d_attended_ref, d_middle_ref, qkv_t_ref, vectors_ref,
    input_grad_ref, qkv_grad_ref, vector_sums_ref, wide_ref, normed_ref, d_projected_ref, back_ref, qkv_total_ref,
):
    @pl.when(pl.program_id(0) == 0)
    def _():
        qkv_total_ref[...] = jnp.zeros_like(qkv_total_ref)
        vector_sums_ref[...] = jnp.zeros_like(vector_sums_ref)

    def put(image, rows, values):
        put_image(wide_ref, image, images, values)

    attention_back_steps(
        x_ref, qkv_ref, probs_ref, d_attended_ref, vectors_ref, vector_sums_ref, normed_ref, d_projected_ref, qkv_total_ref
    )
    input_back_steps(
        put, probs_ref.shape[2], x_ref, d_projected_ref, d_middle_ref, qkv_t_ref, vectors_ref, vector_sums_ref, back_ref
    )

    @pl.when(pl.program_id(0) == pl.num_programs(0) - 1)
    def _():
        narrow(wide_ref, input_grad_ref, images)
        qkv_grad_ref[...] = qkv_total_ref[...].astype(jnp.bfloat16)


def attention_back_steps(
    x_ref, qkv_ref, probs_ref, d_attended_ref, vectors_ref, vector_sums_ref, normed_ref, d_projected_ref, qkv_total_ref
):
    width = x_ref.shape[1]
    length = probs_ref.shape[2]
    per_step = probs_ref.shape[0]

    pairs = width // (2 * HEAD_DIM)
    first = pair_mask(length)
    scale = HEAD_DIM**-0.5

    def places(image, pair):
        low = pair * 2 * HEAD_DIM
        rows = slice(image * length, (image + 1) * length)
        return rows, [slice(part * width + low, part * width + low + 2 * HEAD_DIM) for part in range(3)]

    def entering(image):
        result = []
        for pair in range(pairs):
            rows, cols = places(image, pair)
            d_attended = stack_heads(d_attended_ref[rows, cols[0]], first)
            d_values = dot(probs_ref[image, pair], d_attended)
            d_projected_ref[rows, cols[2]] = d_values.astype(jnp.bfloat16)
            result.append(dot(qkv_ref[rows, cols[2]], d_attended, 1, 1))
        return result

    next_probs = entering(0)
    for image in range(per_step):
        all_d_probs = next_probs
        if image + 1 < per_step:
            next_probs = entering(image + 1)
        all_d_scores = []
        for pair in range(pairs):
            parts = []
            for cols in lane_tiles(2 * length):
                probs, d_probs = probs_ref[image, pair, :, cols].astype(jnp.float32), all_d_probs[pair][:, cols]
                along = jnp.sum(d_probs * probs, axis=0, keepdims=True)
                parts.append((probs * (d_probs - along)).astype(jnp.bfloat16))
            all_d_scores.append(jnp.concatenate(parts, axis=1))
        for pair in range(pairs):
            rows, cols = places(image, pair)
            d_scores = all_d_scores[pair]
            queries = stack_heads(qkv_ref[rows, cols[0]], first)
            d_queries = join_heads(dot(d_scores, qkv_ref[rows, cols[1]], 0, 0), first) * scale
            d_projected_ref[rows, cols[0]] = d_queries.astype(jnp.bfloat16)
            d_projected_ref[rows, cols[1]] = (dot(d_scores, queries) * scale).astype(jnp.bfloat16)

    query_sums = value_sums = jnp.zeros((8, width), jnp.float32)
    for rows in slices_of(x_ref.shape[0]):
        query_sums += fold_rows(d_projected_ref[rows, :width].astype(jnp.float32))
        value_sums += fold_rows(d_projected_ref[rows, 2 * width :].astype(jnp.float32))
        unit, _ = normal_form(x_ref[rows, :].astype(jnp.float32))
        normed_ref[rows, :] = (unit * vectors_ref[0:1] + vectors_ref[1:2]).astype(jnp.bfloat16)
    vector_sums_ref[2:3] += column_sum(query_sums)
    vector_sums_ref[3:4] += column_sum(value_sums)
    qkv_total_ref[...] += dot(normed_ref[...], d_projected_ref[...], 0, 0)


def input_back_steps(
    put, length, x_ref, d_projected_ref, d_middle_ref, qkv_t_ref, vectors_ref, vector_sums_ref, back_ref
):
    step = pl.program_id(0)
    per_step = x_ref.shape[0] // length
    back_ref[...] = dot(d_projected_ref[...], qkv_t_ref[...])
    gain_sums = shift_sums = jnp.zeros((8, x_ref.shape[1]), jnp.float32)
    for rows in slices_of(x_ref.shape[0]):
        unit, scale = normal_form(x_ref[rows, :].astype(jnp.float32))
        grad = back_ref[rows, :]
        gain_sums += fold_rows(grad * unit)
        shift_sums += fold_rows(grad)
        back_ref[rows, :] = d_middle_ref[rows, :] + norm_back(grad, unit, scale, vectors_ref[0:1])
    vector_sums_ref[0:1] += column_sum(gain_sums)
    vector_sums_ref[1:2] += column_sum(shift_sums)
    for image in range(per_step):
        rows = slice(image * length, (image + 1) * length)
        put(step * per_step + image, rows, back_ref[rows, :])


def whole_block(shape):
    return pl.BlockSpec(shape, lambda step: (0,) * len(shape))


def step_block(shape, first=0):
    return pl.BlockSpec(shape, lambda step: (first + step,) + (0,) * (len(shape) - 1))


def scratch(*shape, dtype=jnp.float32):
    return pltpu.VMEM(shape, dtype)


def call_kernel(kernel, statics, steps, ins, outs, scratches, operands, flops, transcendentals=0, first_step=0, aliases={}):
    in_specs = [
        pl.BlockSpec(memory_space=pltpu.SMEM)
        if block == "place"
        else pl.BlockSpec(memory_space=pl.ANY)
        if block == "await"
        else whole_block(op.shape) if block is None else step_block(block, first_step)
        for op, block in zip(operands, ins)
    ]
    out_specs = [
        whole_block(shape) if block is None else step_block(block, first_step) for shape, dtype, block in outs
    ]
    moved = sum(op.size * op.dtype.itemsize for op in operands) + sum(
        math.prod(shape) * jnp.dtype(dtype).itemsize for shape, dtype, block in outs
    )
    return pl.pallas_call(
        functools.partial(kernel, *statics),
        grid=(steps,),
        in_specs=in_specs,
        out_specs=out_specs,
        out_shape=[jax.ShapeDtypeStruct(shape, dtype) for shape, dtype, block in outs],
        scratch_shapes=scratches,
        input_output_aliases=aliases,
        compiler_params=pltpu.CompilerParams(vmem_limit_bytes=vmem_bytes),
        cost_estimate=pl.CostEstimate(
            flops=flops * 8, bytes_accessed=moved, transcendentals=transcendentals
        ),
    )(*operands)


def attention_forward(tokens, bias, w_qkv, w_proj, vectors):
    images, length, _ = bias.shape
    total, width = tokens.shape
    pairs = width // (2 * HEAD_DIM)
    rows = PER_STEP * length
    low, high = jnp.bfloat16, jnp.float32
    outs = [
        ((total, width), low, None),
        ((total, 3 * width), low, (rows, 3 * width)),
        ((images, pairs, length, 2 * length), low, (PER_STEP, pairs, length, 2 * length)),
        ((total, width), low, (rows, width)),
        ((total, width), high, (rows, width)),
    ]
    return call_kernel(
        attention_kernel, (images,), images // PER_STEP,
        [None, (PER_STEP, length, 1), None, None, None], outs,
        [scratch(width // 128, total, 128), scratch(rows, width, dtype=low)],
        (tokens, bias, w_qkv, w_proj, vectors),
        2 * total * width * 4 * width + 8 * total * length * width,
    )


def feed_forward(images, middle, cotangent, attended, w_up, w_down, w_proj, vectors):
    total, width = middle.shape
    hidden = w_up.shape[1]
    rows = total // images * FF_PER_STEP
    low, high = jnp.bfloat16, jnp.float32
    block = (rows, width)
    outs = [
        ((total, width), low, None),
        ((total, width), high, block),
        ((total, width), low, block),
        ((width, hidden), low, None),
        ((hidden, width), low, None),
        ((width, width), low, None),
        ((8, width), high, None),
        ((1, hidden), high, None),
    ]
    scratches = [
        scratch(width // 128, total, 128),
        scratch(rows, width, dtype=low),
        scratch(width, rows, dtype=low),
        scratch(rows, width, dtype=low),
        scratch(width, rows, dtype=low),
        scratch(rows, width),
        scratch(rows, 128),
        scratch(rows, width),
        scratch(rows, width),
        scratch(2, rows, FF_CHUNK),
        scratch(2, rows, FF_CHUNK),
        scratch(rows, hidden, dtype=low),
        scratch(rows, hidden, dtype=low),
        scratch(hidden, width, dtype=low),
        scratch(width, hidden, dtype=low),
        scratch(width, hidden),
        scratch(width, hidden),
        scratch(width, width),
    ]
    return call_kernel(
        feed_forward_kernel, (images,), images // FF_PER_STEP,
        [block, None, block, None, None, None, None, None], outs, scratches,
        (middle, cotangent, attended, w_up, w_down, w_proj.T, vectors, vectors[7:11].reshape(1, hidden)),
        12 * total * width * hidden + 4 * total * width * width, total * hidden,
    )


def attention_back(x, qkv, probs, d_attended, d_middle, w_qkv, vectors):
    images, pairs, length, _ = probs.shape
    total, width = x.shape
    rows = PER_STEP * length
    low, high = jnp.bfloat16, jnp.float32
    block = (rows, width)
    outs = [
        ((total, width), low, None),
        ((width, 3 * width), low, None),
        ((8, width), high, None),
    ]
    scratches = [
        scratch(width // 128, total, 128),
        scratch(rows, width, dtype=low),
        scratch(rows, 3 * width, dtype=low),
        scratch(rows, width),
        scratch(width, 3 * width),
    ]
    return call_kernel(
        attention_back_kernel, (images,), images // PER_STEP,
        [block, (rows, 3 * width), (PER_STEP, pairs, length, 2 * length), block, block, None, None],
        outs, scratches, (x, qkv, probs, d_attended, d_middle, w_qkv.T, vectors),
        4 * total * width * 3 * width + 16 * total * length * width,
    )

def linear_place():
    return lax.axis_index("dp") * lax.axis_size("group") + lax.axis_index("group")


def permute(array, mask):
    count = lax.axis_size("dp") * lax.axis_size("group")
    return lax.ppermute(array, ("dp", "group"), [(rank, rank ^ mask) for rank in range(count)])


def direct_masks(bits):
    masks = [0]
    for bit in bits:
        masks = masks + [mask | bit for mask in masks]
    return masks[1:]


def add_wide(first, *rest):
    total = first.astype(jnp.float32)
    for part in rest:
        total = total + part.astype(jnp.float32)
    return total


def packed_place(mask, spread, count):
    return ((mask >> 1) & (spread - 1)) * (count // (2 * spread)) + (mask >> (spread.bit_length()))


def scatter_step(held, bits):
    masks = direct_masks(bits)
    size = held.shape[0] // (len(masks) + 1)
    parts = [
        permute(held[size * (at + 1) : size * (at + 2)].astype(jnp.bfloat16), mask)
        for at, mask in enumerate(masks)
    ]
    return held[:size], parts


def add_wide(first, *rest):
    total = first.astype(jnp.float32)
    for part in rest:
        total = total + part.astype(jnp.float32)
    return total


def packed_place(mask, spread, count):
    return ((mask >> 1) & (spread - 1)) * (count // (2 * spread)) + (mask >> (spread.bit_length()))


def gather_step(held, bits):
    return held + [permute(part, mask) for mask in direct_masks(bits) for part in held]


def gathered_place(mask, count):
    return (mask & 1) * (count // 2) + ((mask >> 2) & 1) * (count // 4) + (mask >> 3) * 2 + ((mask >> 1) & 1)


def unpack(place_ref, block_refs, packed_ref, put, dp_size, spread):
    place = place_ref[0]
    size = block_refs[0].shape[0]
    for at, block_ref in enumerate(block_refs):
        packed_ref[at * size : (at + 1) * size] = block_ref[...]
    count = dp_size * spread
    for row in range(dp_size):
        for col in range(spread):
            put(row, col, packed_ref[gathered_place((row * spread + col) ^ place, count)])


def pack(place_ref, take, keep_ref, leave_ref, dp_size, spread):
    place = place_ref[0]
    odd = (place & 1) == 1
    for row in range(dp_size):
        for col in range(0, spread, 2):
            at = packed_place((row * spread + col) ^ place, spread, dp_size * spread)
            even_block, odd_block = take(row, col), take(row, col + 1)
            keep_ref[at] = jnp.where(odd, odd_block, even_block)
            leave_ref[at] = jnp.where(odd, even_block, odd_block)


def narrow_pieces(place_ref, wide_ref, piece_refs, spread):
    tiles, _, lanes = wide_ref.shape
    rows_of_piece = piece_refs[0].shape[0]
    step = 64
    group = place_ref[0] & (spread - 1)
    for relative, piece_ref in enumerate(piece_refs):
        base = (group ^ relative) * rows_of_piece

        @pl.loop(0, rows_of_piece // step)
        def _(part):
            target = pl.ds(pl.multiple_of(part * step, step), step)
            source = pl.ds(pl.multiple_of(base + part * step, step), step)
            for tile in range(tiles):
                cols = slice(tile * lanes, (tile + 1) * lanes)
                piece_ref[target, cols] = wide_ref[tile, source, :].astype(jnp.bfloat16)


def general_body(
    tokens,
    keep_mask,
    cotangent,
    qkv_weight,
    proj_weight,
    up_weight,
    down_weight,
    vectors,
    qkv_rows,
    qkv_cols,
    proj_rows,
    proj_cols,
    up_rows,
    up_cols,
    down_rows,
    down_cols,
    vector_moment,
):
    masters = (qkv_weight, proj_weight, up_weight, down_weight)
    lowered = tuple((master.astype(jnp.bfloat16) for master in masters))
    dp_bits, group_bits = axis_bits("dp"), axis_bits("group")
    gather_steps = dp_bits[1:] + group_bits[1:] + dp_bits[:1] + group_bits[:1]
    scatter_steps = gather_steps[::-1]
    w_qkv, w_proj, w_up, w_down = tuple(
        blocks_to_whole(gather_blocks(part, gather_steps), gather_steps) for part in lowered
    )
    spread = lax.axis_size("group")

    def slots_in(array):
        held, slots, width = array.shape
        parts = array.transpose(1, 0, 2).reshape(slots, spread, held // spread, width)
        parts = lax.all_to_all(
            parts.transpose(1, 0, 2, 3), "group", split_axis=0, concat_axis=0, tiled=True
        )
        return parts.reshape(spread * slots * (held // spread), width)

    def slots_out(array):
        held, slots, width = tokens.shape
        parts = array.reshape(spread, slots, held // spread, width)
        parts = lax.all_to_all(parts, "group", split_axis=0, concat_axis=0, tiled=True)
        return parts.transpose(1, 0, 2, 3).reshape(slots, held, width).transpose(1, 0, 2)

    images = keep_mask.shape[0]
    bias = jnp.where(keep_mask > 0, 0.0, -1e30)[:, :, None]
    x, qkv, probs, attended, middle = attention_forward(
        slots_in(tokens), bias, w_qkv, w_proj, vectors
    )
    output, d_middle, d_attended, up_grad, down_grad, proj_grad, ff_sums, up_sums = feed_forward(
        images, middle, slots_in(cotangent), attended, w_up, w_down, w_proj, vectors
    )
    block_output = slots_out(output)
    d_input, qkv_grad, att_sums = attention_back(
        x, qkv, probs, d_attended, d_middle, w_qkv, vectors
    )
    input_grad = slots_out(d_input)
    local_vectors = jnp.concatenate(
        [att_sums[:4], ff_sums[:3], up_sums.reshape(4, -1), ff_sums[3:4]], axis=0
    )
    vector_grad = sum_everywhere(local_vectors, group_bits + dp_bits)
    local_grads = (qkv_grad, proj_grad, up_grad, down_grad)
    owned = tuple(
        scatter_sum(whole_to_blocks(part, scatter_steps), scatter_steps) for part in local_grads
    )
    squares = tuple((gradient * gradient + tiny_square for gradient in owned))
    row_parts = tuple((jnp.sum(square, axis=1) for square in squares)) + tuple(
        (jnp.sum(master * master, axis=1) for master in masters)
    )
    row_sums = sum_parts(row_parts, group_bits)
    rows_old = (qkv_rows, proj_rows, up_rows, down_rows)
    cols_old = (qkv_cols, proj_cols, up_cols, down_cols)
    total_cols = tuple((gradient.shape[1] * lax.axis_size("group") for gradient in owned))
    total_rows = tuple((gradient.shape[0] * lax.axis_size("dp") for gradient in owned))
    rows_new = tuple(
        (
            decay_rate * rows_old[which] + (1.0 - decay_rate) * row_sums[which] / total_cols[which]
            for which in range(4)
        )
    )
    col_parts = (
        tuple((jnp.sum(square, axis=0) for square in squares))
        + tuple((jnp.sum(row_stat) for row_stat in rows_new))
        + tuple((jnp.sum(row_sums[4 + which]) for which in range(4)))
    )
    col_sums = sum_parts(col_parts, dp_bits)
    results = []
    for which in range(4):
        cols_new = (
            decay_rate * cols_old[which] + (1.0 - decay_rate) * col_sums[which] / total_rows[which]
        )
        mean_rows = col_sums[4 + which] / total_rows[which]
        spread = jnp.sqrt(col_sums[8 + which] / (total_rows[which] * total_cols[which]))
        second = rows_new[which][:, None] * cols_new[None, :] / mean_rows
        updated = masters[which] - step_rate * spread * owned[which] * lax.rsqrt(second)
        results.append((owned[which], rows_new[which], cols_new, updated))
    vector_moment_new = decay_rate * vector_moment + (1.0 - decay_rate) * (
        vector_grad * vector_grad + tiny_square
    )
    row_spread = jnp.sqrt(jnp.mean(vectors * vectors, axis=1, keepdims=True))
    vector_new = vectors - step_rate * row_spread * vector_grad * lax.rsqrt(vector_moment_new)
    return (
        block_output,
        input_grad,
        results[0][0],
        results[0][1],
        results[0][2],
        results[0][3],
        results[1][0],
        results[1][1],
        results[1][2],
        results[1][3],
        results[2][0],
        results[2][1],
        results[2][2],
        results[2][3],
        results[3][0],
        results[3][1],
        results[3][2],
        results[3][3],
        vector_grad,
        vector_moment_new,
        vector_new,
    )


def first_attention_kernel(images, dp_size, spread, place_ref, tokens_ref, *refs):
    blocks, refs = refs[:4], refs[4:]
    keep_ref, vectors_ref, *outs, x_ref, w_qkv_ref, w_proj_ref, qkv_t_ref, proj_t_ref = refs[:-4]
    packed_ref, wide_ref, bias_ref, normed_ref = refs[-4:]
    rows = packed_ref.shape[1]
    qkv_cols, proj_cols = w_qkv_ref.shape[1] // spread, w_proj_ref.shape[1] // spread

    @pl.when(pl.program_id(0) == 0)
    def _():
        widen(tokens_ref, wide_ref, images)
        to_image_rows(wide_ref, x_ref, images)

        def put(row, col, block):
            down = slice(row * rows, (row + 1) * rows)
            w_qkv_ref[down, col * qkv_cols : (col + 1) * qkv_cols] = block[:, :qkv_cols]
            w_proj_ref[down, col * proj_cols : (col + 1) * proj_cols] = block[:, qkv_cols:]

        unpack(place_ref, blocks, packed_ref, put, dp_size, spread)
        qkv_t_ref[...] = w_qkv_ref[...].T
        proj_t_ref[...] = w_proj_ref[...].T

    attention_part(0, x_ref, keep_ref, w_qkv_ref, w_proj_ref, vectors_ref, *outs, bias_ref, normed_ref)


def next_attention_kernel(start, x_ref, keep_ref, w_qkv_ref, w_proj_ref, vectors_ref, *refs):
    attention_part(start, x_ref, keep_ref, w_qkv_ref, w_proj_ref, vectors_ref, *refs[-6:])


def attention_part(
    start, x_ref, keep_ref, w_qkv_ref, w_proj_ref, vectors_ref,
    qkv_ref, probs_ref, attended_ref, middle_ref, bias_ref, normed_ref,
):
    @pl.when(pl.program_id(0) == 0)
    def _():
        bias_ref[...] = jnp.where(keep_ref[...] > 0, 0.0, -1e30).T

    def bias_column(image):
        here = start + pl.program_id(0) * probs_ref.shape[0] + image
        lane = lax.broadcasted_iota(jnp.int32, bias_ref.shape, 1)
        return row_sum(jnp.where(lane == here, bias_ref[...], 0.0))

    attention_steps(
        x_ref, bias_column, w_qkv_ref, w_proj_ref, vectors_ref,
        qkv_ref, probs_ref, attended_ref, middle_ref, normed_ref,
    )


def feed_forward_packed_kernel(images, dp_size, spread, place_ref, *refs):
    cotangent_ref, blocks, refs = refs[0], refs[1:5], refs[5:]
    middle_ref, attended_ref, proj_t_ref, vectors_ref = refs[:4]
    outputs, refs = refs[4 : 4 + spread], refs[4 + spread :]
    d_middle_ref, d_attended_ref, keep_ref, leave_ref, proj_total_ref, vector_sums_ref, up_sums_ref = refs[:7]
    w_up_ref, w_down_ref, down_low_ref, packed_ref, bias_up_ref, wide_ref = refs[7:13]
    scratches = refs[13:]
    width = w_up_ref.shape[0]
    up_total_ref, down_total_ref = scratches[-2:]
    rows = packed_ref.shape[1]
    up_cols = w_up_ref.shape[1] // spread
    out_cols = w_down_ref.shape[1] // spread
    folds = w_down_ref.shape[0] // w_up_ref.shape[0]

    @pl.when(pl.program_id(0) == 0)
    def _():
        widen(cotangent_ref, wide_ref, images)
        for fold in range(bias_up_ref.shape[1] // width):
            bias_up_ref[:, fold * width : (fold + 1) * width] = vectors_ref[7 + fold : 8 + fold]

        def put(row, col, block):
            w_up_ref[row * rows : (row + 1) * rows, col * up_cols : (col + 1) * up_cols] = block[:, :up_cols]
            for fold in range(folds):
                down = (row * folds + fold) * rows
                start = up_cols + fold * out_cols
                w_down_ref[down : down + rows, col * out_cols : (col + 1) * out_cols] = block[
                    :, start : start + out_cols
                ]

        unpack(place_ref, blocks, packed_ref, put, dp_size, spread)

    feed_forward_steps(
        images, middle_ref, attended_ref, w_up_ref, w_down_ref, proj_t_ref, vectors_ref, bias_up_ref,
        d_middle_ref, d_attended_ref, vector_sums_ref, up_sums_ref, wide_ref, *scratches, proj_total_ref,
    )

    @pl.when(pl.program_id(0) == pl.num_programs(0) - 1)
    def _():
        narrow_pieces(place_ref, wide_ref, outputs, spread)
        down_low_ref[...] = down_total_ref[...].T.astype(jnp.bfloat16)

        def take(row, col):
            across = slice(row * rows, (row + 1) * rows)
            cols = slice(col * out_cols, (col + 1) * out_cols)
            parts = [up_total_ref[across, col * up_cols : (col + 1) * up_cols].astype(jnp.bfloat16)]
            for fold in range(folds):
                down = (row * folds + fold) * rows
                parts.append(down_low_ref[down : down + rows, cols])
            return jnp.concatenate(parts, axis=1)

        pack(place_ref, take, keep_ref, leave_ref, dp_size, spread)


def attention_back_packed_kernel(
    dp_size, spread, place_ref, x_ref, qkv_ref, probs_ref, d_attended_ref, vectors_ref, proj_total_ref, _,
    d_projected_ref, keep_ref, leave_ref, vector_sums_ref, normed_ref, total_ref,
):
    @pl.when(pl.program_id(0) == 0)
    def _():
        total_ref[...] = jnp.zeros_like(total_ref)
        vector_sums_ref[...] = jnp.zeros_like(vector_sums_ref)

    attention_back_steps(
        x_ref, qkv_ref, probs_ref, d_attended_ref, vectors_ref, vector_sums_ref, normed_ref, d_projected_ref, total_ref
    )

    @pl.when(pl.program_id(0) == pl.num_programs(0) - 1)
    def _():
        rows = keep_ref.shape[1]
        qkv_cols, proj_cols = total_ref.shape[1] // spread, proj_total_ref.shape[1] // spread

        def take(row, col):
            down = slice(row * rows, (row + 1) * rows)
            parts = [
                total_ref[down, col * qkv_cols : (col + 1) * qkv_cols],
                proj_total_ref[down, col * proj_cols : (col + 1) * proj_cols],
            ]
            return jnp.concatenate(parts, axis=1).astype(jnp.bfloat16)

        pack(place_ref, take, keep_ref, leave_ref, dp_size, spread)


def first_input_kernel(
    length, x_ref, d_projected_ref, d_middle_ref, qkv_t_ref, vectors_ref, before_ref, *refs
):
    d_input_ref, vector_sums_ref, back_ref = refs[-3:]

    @pl.when(pl.program_id(0) == 0)
    def _():
        vector_sums_ref[...] = before_ref[...]

    def put(image, rows, values):
        d_input_ref[rows, :] = values.astype(jnp.bfloat16)

    input_back_steps(
        put, length, x_ref, d_projected_ref, d_middle_ref, qkv_t_ref, vectors_ref, vector_sums_ref, back_ref
    )


def last_input_kernel(
    images, spread, length, first, place_ref, x_ref, d_projected_ref, d_middle_ref, qkv_t_ref, vectors_ref, before_ref,
    d_input_ref, _, *refs,
):
    pieces, (vector_sums_ref, wide_ref, back_ref) = refs[:spread], refs[spread:]

    @pl.when(pl.program_id(0) == 0)
    def _():
        vector_sums_ref[...] = before_ref[...]
        for image in range(first):
            rows = slice(image * length, (image + 1) * length)
            put_image(wide_ref, image, images, d_input_ref[rows, :].astype(jnp.float32))

    def put(image, rows, values):
        put_image(wide_ref, first + image, images, values)

    input_back_steps(
        put, length, x_ref, d_projected_ref, d_middle_ref, qkv_t_ref, vectors_ref, vector_sums_ref, back_ref
    )

    @pl.when(pl.program_id(0) == pl.num_programs(0) - 1)
    def _():
        narrow_pieces(place_ref, wide_ref, pieces, spread)


def cut(array_ref, parts_ref):
    count = parts_ref.shape[2]
    for member in range(parts_ref.shape[0]):
        parts_ref[member] = array_ref[:, member * count : (member + 1) * count, :]


def pack_kernel(qkv_ref, proj_ref, up_ref, down_ref, pack_ref):
    rows, start = pack_ref.shape[0], 0
    parts = [qkv_ref[...], proj_ref[...], up_ref[...]]
    parts += [down_ref[fold * rows : (fold + 1) * rows, :] for fold in range(down_ref.shape[0] // rows)]
    for part in parts:
        pack_ref[:, start : start + part.shape[1]] = part.astype(jnp.bfloat16)
        start += part.shape[1]


def pair_kernel(own_ref, arrived_ref, _, first_ref, second_ref):
    start = first_ref.shape[2]
    for at, pack_ref in enumerate((own_ref, arrived_ref)):
        first_ref[at] = pack_ref[:, :start]
        second_ref[at] = pack_ref[:, start:]


def cotangent_kernel(array_ref, _, parts_ref):
    cut(array_ref, parts_ref)


def join_kernel(count, *refs):
    size = refs[0].shape[0]
    for at, part_ref in enumerate(refs[:count]):
        refs[-1][at * size : (at + 1) * size] = part_ref[...]


def settle_kernel(spread, place_ref, *refs):
    lists, (output_ref, token_ref) = refs[:-2], refs[-2:]
    token_ref[...] = jnp.zeros_like(token_ref)
    group = place_ref[0] & (spread - 1)
    count = lists[0].shape[1]
    share = len(lists) // spread * count
    for at, piece_ref in enumerate(lists):
        relative, part = at % spread, at // spread
        start = pl.multiple_of((group ^ relative) * share + part * count, count)
        output_ref[:, pl.ds(start, count), :] = piece_ref[...]


def lane_table(rows, columns):
    lane = lax.broadcasted_iota(jnp.int32, (rows, 128), 1)
    table = jnp.zeros((rows, 128), jnp.float32)
    for at, column in enumerate(columns):
        table = jnp.where(lane == at, column, table)
    return table


def added(parts):
    while len(parts) > 1:
        parts = [sum(parts[at : at + 2][1:], parts[at]) for at in range(0, len(parts), 2)]
    return parts[0]


def row_sum(values):
    return jnp.sum(values, axis=1, keepdims=True)


def after_kernel(*refs):
    pass


def add_kernel(count, keep_ref, arrived_ref, *refs):
    parts = refs[-count:]
    size = parts[0].shape[0]
    for at, part_ref in enumerate(parts):
        rows = slice(at * size, (at + 1) * size)
        total = keep_ref[rows].astype(jnp.float32) + arrived_ref[rows].astype(jnp.float32)
        part_ref[...] = total.astype(part_ref.dtype)


def gradient_kernel(count, *refs):
    block_parts, sums, refs = refs[:count], refs[count : count + 3], refs[count + 3 :]
    masters, rows_old, refs = refs[:4], refs[4:8], refs[8:]
    grads, (row_ref, message_ref) = refs[:4], refs[4:]
    blocks = added([part[0].astype(jnp.float32) for part in block_parts])
    rows, up_cols = grads[2].shape
    qkv_cols, out_cols = grads[0].shape[1], grads[1].shape[1]
    folds = grads[3].shape[0] // rows
    up = blocks[:, :up_cols]
    downs = [blocks[:, up_cols + fold * out_cols :][:, :out_cols] for fold in range(folds)]
    start = up_cols + folds * out_cols
    qkv = blocks[:, start : start + qkv_cols]
    proj = blocks[:, start + qkv_cols :]
    grads[0][...] = qkv
    grads[1][...] = proj
    grads[2][...] = up
    for fold in range(folds):
        grads[3][fold * rows : (fold + 1) * rows, :] = downs[fold]
    squares = [part * part + tiny_square for part in (qkv, proj, up, *downs)]
    row_ref[...] = lane_table(rows, [row_sum(square) for square in squares]).T[: row_ref.shape[0], :]
    width = message_ref.shape[1]
    message_ref[...] = jnp.zeros_like(message_ref)
    for at, square in enumerate((*squares[:3], added(squares[3:]))):
        message_ref[at : at + 1, : square.shape[1]] = column_sum(square)
    scalars = [column_sum(row_sum(master[...] * master[...])) for master in masters]
    scalars += [row_sum(part[...].reshape(1, part.shape[0])) for part in rows_old]
    message_ref[4:5, :128] = lane_table(1, scalars)
    att_ref, ff_ref, up_ref = sums
    count = up_ref.shape[1] // width
    message_ref[8:12, :] = att_ref[:4]
    message_ref[12:15, :] = ff_ref[:3]
    for at in range(count):
        message_ref[15 + at : 16 + at, :] = up_ref[:, at * width : (at + 1) * width]
    message_ref[15 + count : 16 + count, :] = ff_ref[3:4]


def column_kernel(row_ref, *refs):
    parts, (cols_ref, message_ref) = refs[:-3], refs[-2:]
    total = added([part[...] for part in parts])
    cols_ref[...] = total[:8]
    width = total.shape[1]
    rows = row_ref.shape[1]
    message_ref[...] = jnp.zeros_like(message_ref)
    message_ref[:8, :rows] = row_ref[...]
    columns = [row_sum(total[which : which + 1]) for which in range(4)]
    squares = [total[4:5, which : which + 1] for which in range(4)]
    message_ref[8:9, :] = lane_table(1, columns + squares)
    for tile in range(width // 128):
        message_ref[16 * (tile + 1) : 16 * (tile + 2), :] = total[8:, tile * 128 : (tile + 1) * 128]


def update_kernel(count, heights, widths, *refs):
    messages, refs = refs[:count], refs[count:]
    cols_ref, vectors_ref, moment_ref, refs = refs[0], refs[1], refs[2], refs[3:]
    grads, masters, rows_old, cols_old, refs = refs[:4], refs[4:8], refs[8:12], refs[12:16], refs[17:]
    news, cols_new, rows_out, refs = refs[:4], refs[4:8], refs[8:12], refs[12:]
    vector_grad_ref, moment_new_ref, vector_new_ref = refs
    sums = added([message[...] for message in messages])
    height = grads[0].shape[0]
    folds = grads[3].shape[0] // height
    lanes = [[0], [1], [2], list(range(3, 3 + folds))]
    share = 1.0 - decay_rate
    for which in range(4):
        entries = heights[which] * widths[which]
        cols = cols_old[which].shape[0]
        new = decay_rate * cols_old[which][...].reshape(1, cols) + share / heights[which] * cols_ref[
            which : which + 1, :cols
        ]
        cols_new[which][...] = new[0]
        old_total = cols_ref[4:5, 4 + which : 5 + which]
        mean_rows = (decay_rate * old_total + share / widths[which] * sums[8:9, which : which + 1]) / heights[which]
        rate = step_rate * jnp.sqrt(sums[8:9, 4 + which : 5 + which] / entries)
        across = new / mean_rows
        old = rows_old[which][...].reshape(1, len(lanes[which]) * height)
        row_sums = jnp.concatenate([sums[lane : lane + 1, :height] for lane in lanes[which]], axis=1)
        row = decay_rate * old + share / widths[which] * row_sums
        rows_out[which][...] = row[0]
        for fold in range(len(lanes[which])):
            part = slice(fold * height, (fold + 1) * height)
            column = jnp.broadcast_to(row[:, part], (8, height)).T[:, :1]
            news[which][part, :] = masters[which][part, :] - rate * grads[which][part, :] * lax.rsqrt(column * across)
    vectors = vectors_ref[...]
    count = vectors.shape[0]
    gradient = jnp.concatenate(
        [sums[16 * (tile + 1) : 16 * (tile + 1) + count] for tile in range(vectors.shape[1] // 128)], axis=1
    )
    vector_grad_ref[...] = gradient
    moment = decay_rate * moment_ref[...] + share * (gradient * gradient + tiny_square)
    moment_new_ref[...] = moment
    spread = jnp.sqrt(jnp.mean(vectors * vectors, axis=1, keepdims=True))
    vector_new_ref[...] = vectors - step_rate * spread * gradient * lax.rsqrt(moment)


def packed_body(
    tokens, keep_mask, cotangent, qkv_weight, proj_weight, up_weight, down_weight, vectors,
    qkv_rows, qkv_cols, proj_rows, proj_cols, up_rows, up_cols, down_rows, down_cols, vector_moment,
):
    spread, dp_size = lax.axis_size("group"), lax.axis_size("dp")
    low, high = jnp.bfloat16, jnp.float32
    place = linear_place().astype(jnp.int32).reshape(1)
    group = lax.axis_index("group")
    held, slots, width = tokens.shape
    images, length = keep_mask.shape
    hidden = up_weight.shape[1] * spread
    total = images * length
    rows = qkv_weight.shape[0]
    folds = down_weight.shape[0] // rows
    core_bits = (1,)
    near_bits = tuple(1 << at for at in range(1, spread.bit_length()))
    far_bits = tuple(spread << at for at in range(1, dp_size.bit_length() - 1))
    half = spread * dp_size // 2

    anywhere = pl.BlockSpec(memory_space=pl.ANY)
    in_smem = pl.BlockSpec(memory_space=pltpu.SMEM)

    in_vmem = pl.BlockSpec(memory_space=pltpu.VMEM)
    small = functools.partial(
        pl.pallas_call, compiler_params=pltpu.CompilerParams(vmem_limit_bytes=vmem_bytes)
    )
    masters = (qkv_weight, proj_weight, up_weight, down_weight)
    parted = jax.ShapeDtypeStruct((spread, slots, images, width), low)

    def after(array, awaited):
        return small(
            after_kernel,
            in_specs=[anywhere] * (1 + len(awaited)),
            out_specs=anywhere,
            out_shape=jax.ShapeDtypeStruct(array.shape, array.dtype),
            input_output_aliases={0: 0},
        )(array, *awaited)

    def to_group(parts):
        return lax.all_to_all(parts, "group", split_axis=0, concat_axis=0, tiled=True)

    def to_images(parts):
        return to_group(parts).reshape(total, width)

    def exchange(parts):
        return [parts[0]] + [permute(part, relative) for relative, part in enumerate(parts) if relative]

    def settle(parts):
        parts = [part.reshape(slots, -1, width) for part in parts]
        whole, token = small(
            functools.partial(settle_kernel, spread),
            in_specs=[in_smem] + [in_vmem] * len(parts),
            out_specs=[in_vmem] * 2,
            out_shape=[
                jax.ShapeDtypeStruct((slots, held, width), low),
                jax.ShapeDtypeStruct((8, 128), high),
            ],
        )(place, *parts)
        return whole.transpose(1, 0, 2), token

    first_cols = qkv_weight.shape[1] + proj_weight.shape[1]
    second_cols = up_weight.shape[1] + folds * down_weight.shape[1]
    pack_own = small(pack_kernel, out_shape=jax.ShapeDtypeStruct((rows, first_cols + second_cols), low))(*masters)
    across_y, across_x = near_bits
    pack_arrived = permute(pack_own, across_y)
    token_cut = small(cut, out_shape=parted)(tokens.transpose(1, 0, 2))
    first_pair, second_pair = small(
        pair_kernel,
        in_specs=[in_vmem] * 2 + [anywhere],
        out_shape=[
            jax.ShapeDtypeStruct((2, rows, first_cols), low),
            jax.ShapeDtypeStruct((2, rows, second_cols), low),
        ],
    )(pack_own, pack_arrived, token_cut)
    cotangent_cut = small(
        cotangent_kernel, in_specs=[in_vmem, anywhere], out_shape=parted
    )(cotangent.transpose(1, 0, 2), first_pair)

    def gather_far(pair):
        return [pair] + [permute(pair, mask) for mask in direct_masks(far_bits)]

    def join(parts, awaited=()):
        count = len(parts) * parts[0].shape[0]
        return small(
            functools.partial(join_kernel, len(parts)),
            in_specs=[in_vmem] * len(parts) + [anywhere] * len(awaited),
            out_shape=jax.ShapeDtypeStruct((count, *parts[0].shape[1:]), low),
        )(*parts, *awaited)

    def gather_rest(held):
        arrived = permute(held, across_x)
        return [held, arrived, permute(held, core_bits[0]), permute(arrived, core_bits[0])]

    first_far = gather_far(first_pair)
    inputs = to_images(after(token_cut, [cotangent_cut]))
    first_far = join(first_far, [cotangent_cut])
    upstream = to_images(after(cotangent_cut, [inputs]))
    first_blocks = gather_rest(first_far)
    second_far = gather_far(second_pair)

    step_rows = PER_STEP * length
    block = (step_rows, width)
    pairs = width // (2 * HEAD_DIM)
    steps = images // PER_STEP
    statics = (images, dp_size, spread)
    wide = scratch(width // 128, total, 128)
    probs_block = (PER_STEP, pairs, length, 2 * length)
    attention_outs = [
        ((total, 3 * width), low, (step_rows, 3 * width)),
        ((images, *probs_block[1:]), low, probs_block),
        ((total, width), low, block),
        ((total, width), high, block),
    ]
    attention_flops = (2 * total * width * 4 * width + 8 * total * length * width) // steps
    attention_scratches = [scratch(length, images), scratch(step_rows, width, dtype=low)]
    *attention, x, w_qkv, w_proj, qkv_t, proj_t = call_kernel(
        first_attention_kernel, statics, 1,
        ["place"] + [None] * 7,
        attention_outs
        + [
            ((total, width), low, None),
            ((width, 3 * width), low, None),
            ((width, width), low, None),
            ((3 * width, width), low, None),
            ((width, width), low, None),
        ],
        [scratch(dp_size * spread, rows, first_cols, dtype=low), wide] + attention_scratches,
        (place, inputs, *first_blocks, keep_mask, vectors),
        attention_flops,
    )
    second_blocks = gather_rest(join(second_far, attention[:1]))
    for first_step, count in ((1, steps - 2), (steps - 1, 1)):
        attention = call_kernel(
            next_attention_kernel, (first_step * PER_STEP,), count,
            [block] + [None] * 4 + ["await"] * len(attention),
            attention_outs, attention_scratches,
            (x, keep_mask, w_qkv, w_proj, vectors, *attention),
            attention_flops * count, first_step=first_step,
            aliases={5 + at: at for at in range(len(attention))},
        )
    qkv, probs, attended, middle = attention
    piece = ((slots * images, width), low, None)
    ff_rows = FF_PER_STEP * length
    ff_block = (ff_rows, width)
    results = call_kernel(
        feed_forward_packed_kernel, statics, images // FF_PER_STEP,
        ["place"] + [None] * 5 + [ff_block, ff_block] + [None] * 2,
        [piece] * spread
        + [
            ((total, width), high, ff_block),
            ((total, width), low, ff_block),
            ((half, rows, second_cols), low, None),
            ((half, rows, second_cols), low, None),
            ((width, width), high, None),
            ((8, width), high, None),
            ((1, hidden), high, None),
        ],
        [
            scratch(width, hidden, dtype=low),
            scratch(hidden, width, dtype=low),
            scratch(hidden, width, dtype=low),
            scratch(dp_size * spread, rows, second_cols, dtype=low),
            scratch(1, hidden),
            wide,
            scratch(ff_rows, width, dtype=low),
            scratch(width, ff_rows, dtype=low),
            scratch(ff_rows, width, dtype=low),
            scratch(width, ff_rows, dtype=low),
            scratch(ff_rows, width),
            scratch(ff_rows, 128),
            scratch(ff_rows, width),
            scratch(ff_rows, width),
            scratch(2, ff_rows, FF_CHUNK),
            scratch(2, ff_rows, FF_CHUNK),
            scratch(ff_rows, hidden, dtype=low),
            scratch(ff_rows, hidden, dtype=low),
            scratch(hidden, width, dtype=low),
            scratch(width, hidden, dtype=low),
            scratch(width, hidden),
            scratch(width, hidden),
        ],
        (
            place, upstream, *second_blocks, middle, attended, proj_t, vectors,
        ),
        12 * total * width * hidden + 4 * total * width * width, total * hidden,
    )
    d_middle, d_attended, ff_keep, ff_leave, proj_total, ff_sums, up_sums = results[spread:]

    def add_parts(count, keep, arrived, awaited):
        part = (keep.shape[0] // count, *keep.shape[1:])
        return small(
            functools.partial(add_kernel, count),
            in_specs=[in_vmem] * 2 + [anywhere] * len(awaited),
            out_specs=[in_vmem] * count,
            out_shape=[jax.ShapeDtypeStruct(part, high)]
            + [jax.ShapeDtypeStruct(part, low)] * (count - 1),
        )(keep, arrived, *awaited)

    ff_first = permute(ff_leave, core_bits[0])
    ff_count = half // 2
    ff_next = add_wide(ff_keep[ff_count:], ff_first[ff_count:]).astype(low)
    ff_arrived = permute(ff_next, across_x)
    output_parts = exchange(results[:spread])
    pack_half = ((half, rows, first_cols), low, None)
    wide_rows = (step_rows, 3 * width)
    d_projected, qkv_keep, qkv_leave, att_sums = call_kernel(
        attention_back_packed_kernel, (dp_size, spread), steps,
        ["place", block, wide_rows, probs_block, block, None, None, "await"],
        [((total, 3 * width), low, wide_rows), pack_half, pack_half, ((8, width), high, None)],
        [scratch(step_rows, width, dtype=low), scratch(width, 3 * width)],
        (place, x, qkv, probs, d_attended, vectors, proj_total, ff_next),
        2 * total * width * 3 * width + 16 * total * length * width,
    )
    qkv_arrived = permute(after(qkv_leave, output_parts[1:]), core_bits[0])
    input_flops = 2 * total * width * 3 * width
    input_ins = [block, wide_rows, block, None, None, None]
    input_outs = [((total, width), low, block), ((8, width), high, None)]
    d_input, att_sums = call_kernel(
        first_input_kernel, (length,), 1, input_ins, input_outs, [scratch(step_rows, width)],
        (x, d_projected, d_middle, qkv_t, vectors, att_sums), input_flops // steps,
    )
    ff_quarter = half // 4
    ff_last = add_wide(
        ff_keep[ff_quarter:ff_count], ff_first[ff_quarter:ff_count], ff_arrived[ff_quarter:]
    ).astype(low)
    ff_last_arrived = permute(ff_last, across_y)
    qkv_held, *leaving = add_parts(4, qkv_keep, qkv_arrived, [ff_last])
    qkv_parts = [permute(part, mask) for part, mask in zip(leaving, direct_masks(near_bits))]
    d_input, att_sums = call_kernel(
        first_input_kernel, (length,), 1, input_ins + ["await"] * 2, input_outs, [scratch(step_rows, width)],
        (x, d_projected, d_middle, qkv_t, vectors, att_sums, d_input, leaving[0]), input_flops // steps,
        first_step=1, aliases={6: 0},
    )
    ff_held = add_wide(
        ff_keep[:ff_quarter], ff_first[:ff_quarter], ff_arrived[:ff_quarter], ff_last_arrived
    )
    qkv_held = add_wide(qkv_held, *qkv_parts)
    blocks = jnp.concatenate([ff_held, qkv_held], axis=2)
    far_leaving = [blocks[at : at + 1].astype(low) for at in range(1, blocks.shape[0])]
    block_parts = [blocks[:1]] + [permute(part, mask) for part, mask in zip(far_leaving, direct_masks(far_bits))]
    results = call_kernel(
        last_input_kernel, (images, spread, length, 2 * PER_STEP), steps - 2,
        ["place"] + input_ins + [None, "await"],
        [piece] * spread + [((8, width), high, None)],
        [wide, scratch(step_rows, width)],
        (place, x, d_projected, d_middle, qkv_t, vectors, att_sums, d_input, far_leaving[0]), input_flops // steps * (steps - 2),
        first_step=2,
    )
    att_sums = results[spread]
    input_pieces = list(results[:spread])
    heights = [master.shape[0] * dp_size for master in masters]
    widths = [master.shape[1] * spread for master in masters]
    rows_old, cols_old = [qkv_rows, proj_rows, up_rows, down_rows], [qkv_cols, proj_cols, up_cols, down_cols]

    def like(*arrays):
        return [jax.ShapeDtypeStruct(array.shape, high) for array in arrays]

    operands = (*block_parts, att_sums, ff_sums, up_sums, *masters, *rows_old)
    *grads, row_sums, message = small(
        functools.partial(gradient_kernel, len(block_parts)),
        out_shape=like(*masters) + [jax.ShapeDtypeStruct((8, rows), high), jax.ShapeDtypeStruct((24, width), high)],
    )(*operands)
    input_pieces[1] = after(input_pieces[1], [row_sums])
    output_parts[0] = after(output_parts[0], [row_sums])
    block_output, settled = settle(output_parts)
    input_grad, input_settled = settle(exchange(input_pieces))
    message = added([message] + [permute(message, mask) for mask in direct_masks((across_x, far_bits[0]))])
    for bit in far_bits[1:-1]:
        message = message + permute(message, bit)
    messages = [message, permute(message, far_bits[-1])]
    col_sums, message = small(
        column_kernel,
        in_specs=[in_vmem] * (1 + len(messages)) + [anywhere],
        out_shape=[
            jax.ShapeDtypeStruct((8, width), high),
            jax.ShapeDtypeStruct((16 + width // 8, 128), high),
        ],
    )(row_sums, *messages, settled)
    messages = [message] + [permute(message, mask) for mask in range(1, spread)]
    operands = (*messages, col_sums, vectors, vector_moment, *grads, *masters, *rows_old, *cols_old)
    results = small(
        functools.partial(update_kernel, len(messages), heights, widths),
        in_specs=[in_vmem] * len(operands) + [anywhere],
        out_shape=like(*masters, *cols_old, *rows_old, vectors, vectors, vectors),
    )(*operands, input_settled)
    news, cols_new, rows_out = results[:4], results[4:8], results[8:12]
    vector_grad, vector_moment_new, vector_new = results[12:]
    factored = []
    for which in range(4):
        factored += [grads[which], rows_out[which], cols_new[which], news[which]]
    return (block_output, input_grad, *factored, vector_grad, vector_moment_new, vector_new)


def body(*arrays):
    spread, dp_size = lax.axis_size("group"), lax.axis_size("dp")
    rows, images = arrays[3].shape[0], arrays[1].shape[0]
    slots, width = arrays[0].shape[1:]
    folds = arrays[6].shape[0] // rows
    powers = all(size & (size - 1) == 0 for size in (spread, dp_size))
    fits = powers and spread == 4 and dp_size > 2
    fits = fits and arrays[5].shape[1] <= width and folds <= 5
    fits = fits and rows % 16 == 0 and images % FF_PER_STEP == 0 and images > 2 * PER_STEP and images % 16 == 0 and slots % 4 == 0
    return packed_body(*arrays) if fits else general_body(*arrays)


def solution(mesh):
    in_specs = (
        P("dp", "group", None),
        P(("dp", "group"), None),
        P("dp", "group", None),
        P("dp", "group"),
        P("dp", "group"),
        P("dp", "group"),
        P("dp", "group"),
        P(),
        P("dp"),
        P("group"),
        P("dp"),
        P("group"),
        P("dp"),
        P("group"),
        P("dp"),
        P("group"),
        P(),
    )
    out_specs = (
        P("dp", "group", None),
        P("dp", "group", None),
        P("dp", "group"),
        P("dp"),
        P("group"),
        P("dp", "group"),
        P("dp", "group"),
        P("dp"),
        P("group"),
        P("dp", "group"),
        P("dp", "group"),
        P("dp"),
        P("group"),
        P("dp", "group"),
        P("dp", "group"),
        P("dp"),
        P("group"),
        P("dp", "group"),
        P(),
        P(),
        P(),
    )
    return jax.shard_map(body, mesh=mesh, in_specs=in_specs, out_specs=out_specs, check_vma=False)
```

```python
import functools
import math

import jax
import jax.numpy as jnp
from jax import lax
from jax.experimental import pallas as pl
from jax.experimental.pallas import tpu as pltpu
from jax.sharding import PartitionSpec as P

HEAD_DIM = 64
STEP_NUMBER = 10


step_rate = 0.3
norm_epsilon = 1e-06
tiny_square = 1e-30
decay_rate = 1.0 - STEP_NUMBER ** (-0.8)
LOG2_E = 1.4426950408889634


def axis_bits(name):
    count = lax.axis_size(name)
    return [(name, 1 << place) for place in range(count.bit_length() - 1)]


def swap_partner(array, step):
    name, bit = step
    count = lax.axis_size(name)
    return lax.ppermute(array, name, [(rank, rank ^ bit) for rank in range(count)])


def upper_side(step):
    name, bit = step
    return (lax.axis_index(name) & bit) != 0


def gather_blocks(array, steps):
    for step in steps:
        arrived = swap_partner(array, step)
        upper = upper_side(step)
        array = jnp.stack([jnp.where(upper, arrived, array), jnp.where(upper, array, arrived)])
    return array


def scatter_sum(array, steps):
    for step in steps:
        upper = upper_side(step)
        leaving = jnp.where(upper, array[0], array[1]).astype(jnp.bfloat16)
        arrived = swap_partner(leaving, step)
        array = jnp.where(upper, array[1], array[0]).astype(jnp.float32) + arrived.astype(jnp.float32)
    return array


def sum_everywhere(array, steps):
    for step in steps:
        array = array + swap_partner(array, step)
    return array


def sum_parts(parts, steps):
    flat = [part.reshape(-1) for part in parts]
    total = sum_everywhere(jnp.concatenate(flat), steps)
    result, start = [], 0
    for part in parts:
        result.append(total[start : start + part.size].reshape(part.shape))
        start += part.size
    return result


def block_order(steps):
    order = []
    for name in ("dp", "group"):
        bits = sorted((step for step in steps if step[0] == name), key=lambda step: -step[1])
        order.append([steps.index(step) for step in bits])
    return order


def blocks_to_whole(blocks, steps):
    count = len(steps)
    rows, cols = blocks.shape[count:]
    dp_axes, group_axes = block_order(steps)
    dp_axes = [count - 1 - axis for axis in dp_axes]
    group_axes = [count - 1 - axis for axis in group_axes]
    whole = blocks.transpose(dp_axes + [count] + group_axes + [count + 1])
    return whole.reshape(rows << len(dp_axes), cols << len(group_axes))


def whole_to_blocks(whole, steps):
    dp_axes, group_axes = block_order(steps)
    rows = whole.shape[0] >> len(dp_axes)
    cols = whole.shape[1] >> len(group_axes)
    split = whole.reshape([2] * len(dp_axes) + [rows] + [2] * len(group_axes) + [cols])
    places = dp_axes + [len(steps)] + group_axes + [len(steps) + 1]
    return split.transpose([places.index(axis) for axis in range(len(places))])


PER_STEP = 4
FF_PER_STEP = 4
SLICE = 48
FF_CHUNK = 256
vmem_bytes = 60 * 1024 * 1024


def dot(left, right, left_axis=1, right_axis=0):
    return lax.dot_general(
        left, right, (((left_axis,), (right_axis,)), ((), ())), preferred_element_type=jnp.float32
    )


def normal_form(values):
    center = jnp.mean(values, axis=-1, keepdims=True)
    centered = values - center
    spread = jnp.mean(centered * centered, axis=-1, keepdims=True)
    scale = lax.rsqrt(spread + norm_epsilon)
    return centered * scale, scale


def norm_back(grad, unit, scale, gain):
    weighted = grad * gain
    along = jnp.mean(weighted * unit, axis=-1, keepdims=True)
    level = jnp.mean(weighted, axis=-1, keepdims=True)
    return scale * (weighted - level - unit * along)


def slices_of(count):
    return [slice(start, start + SLICE) for start in range(0, count, SLICE)]


def fold_rows(values):
    return jnp.sum(values.reshape(values.shape[0] // 8, 8, values.shape[1]), axis=0)


def column_sum(values):
    return jnp.sum(values, axis=0, keepdims=True)


def pair_mask(length):
    return lax.broadcasted_iota(jnp.int32, (length, 2 * HEAD_DIM), 1) < HEAD_DIM


def lane_tiles(count):
    return [slice(start, min(start + 128, count)) for start in range(0, count, 128)]


def stack_heads(pair, first):
    none = jnp.zeros_like(pair)
    return jnp.concatenate([jnp.where(first, pair, none), jnp.where(first, none, pair)], axis=0)


def join_heads(rows, first):
    length = rows.shape[0] // 2
    return jnp.where(first, rows[:length], rows[length:])


def gelu_and_slope(pre):
    bell = jnp.exp2(pre * pre * (-0.5 * LOG2_E))
    base = 1.0 + (0.3275911 * 0.5**0.5) * jnp.abs(pre)
    inverse = pl.reciprocal(base, approx=True)
    inverse = inverse * (2.0 - base * inverse)
    poly = inverse * (
        0.5 * 0.254829592
        + inverse
        * (
            0.5 * -0.284496736
            + inverse
            * (0.5 * 1.421413741 + inverse * (0.5 * -1.453152027 + inverse * (0.5 * 1.061405429)))
        )
    )
    tail = poly * bell
    below = jnp.where(pre >= 0, 1.0 - tail, tail)
    return pre * below, below + pre * bell * 0.3989422804014327


def widen(source_ref, wide_ref, images):
    tiles, total, lanes = wide_ref.shape
    rows_at_once = 8 * images

    @pl.loop(0, total // rows_at_once)
    def _(part):
        rows = pl.ds(pl.multiple_of(part * rows_at_once, rows_at_once), rows_at_once)
        for tile in range(tiles):
            cols = slice(tile * lanes, (tile + 1) * lanes)
            wide_ref[tile, rows, :] = source_ref[rows, cols].astype(jnp.float32)


def narrow(wide_ref, target_ref, images):
    tiles, total, lanes = wide_ref.shape
    rows_at_once = 8 * images

    @pl.loop(0, total // rows_at_once)
    def _(part):
        rows = pl.ds(pl.multiple_of(part * rows_at_once, rows_at_once), rows_at_once)
        for tile in range(tiles):
            cols = slice(tile * lanes, (tile + 1) * lanes)
            target_ref[rows, cols] = wide_ref[tile, rows, :].astype(target_ref.dtype)


def take_image(wide_ref, image, images):
    tiles, total, _ = wide_ref.shape
    rows = pl.ds(image, total // images, images)
    return jnp.concatenate([wide_ref[tile, rows, :] for tile in range(tiles)], axis=1)


def put_image(wide_ref, image, images, values):
    tiles, total, lanes = wide_ref.shape
    rows = pl.ds(image, total // images, images)
    for tile in range(tiles):
        wide_ref[tile, rows, :] = values[:, tile * lanes : (tile + 1) * lanes]


def attention_kernel(
    images, tokens_ref, bias_ref, w_qkv_ref, w_proj_ref, vectors_ref,
    x_ref, qkv_ref, probs_ref, attended_ref, middle_ref, wide_ref, normed_ref,
):
    @pl.when(pl.program_id(0) == 0)
    def _():
        widen(tokens_ref, wide_ref, images)
        to_image_rows(wide_ref, x_ref, images)

    attention_steps(
        x_ref, lambda image: bias_ref[image], w_qkv_ref, w_proj_ref, vectors_ref,
        qkv_ref, probs_ref, attended_ref, middle_ref, normed_ref,
    )


def to_image_rows(wide_ref, x_ref, images):
    length = wide_ref.shape[1] // images

    @pl.loop(0, images)
    def _(image):
        rows = pl.ds(pl.multiple_of(image * length, length), length)
        x_ref[rows, :] = take_image(wide_ref, image, images).astype(jnp.bfloat16)


def attention_steps(
    x_ref, bias_column, w_qkv_ref, w_proj_ref, vectors_ref,
    qkv_ref, probs_ref, attended_ref, middle_ref, normed_ref,
):
    per_step, _, length, _ = probs_ref.shape
    step_rows, width = middle_ref.shape
    base = 0 if x_ref.shape[0] == step_rows else pl.program_id(0) * step_rows

    for rows in slices_of(step_rows):
        x = x_ref[pl.ds(pl.multiple_of(base + rows.start, SLICE), SLICE), :].astype(jnp.float32)
        unit, _ = normal_form(x)
        normed_ref[rows, :] = (unit * vectors_ref[0:1] + vectors_ref[1:2]).astype(jnp.bfloat16)
    for part in range(3):
        cols = slice(part * width, (part + 1) * width)
        projected = dot(normed_ref[...], w_qkv_ref[:, cols])
        if part != 1:
            row = 2 if part == 0 else 3
            projected = projected + vectors_ref[row : row + 1]
        qkv_ref[:, cols] = projected.astype(jnp.bfloat16)

    pairs = width // (2 * HEAD_DIM)
    first = pair_mask(length)
    place = lax.broadcasted_iota(jnp.int32, (length, 2 * length), 0)
    asker = lax.broadcasted_iota(jnp.int32, (length, 2 * length), 1)
    own = place == jnp.where(asker >= length, asker - length, asker)

    def scores_of(image):
        rows = slice(image * length, (image + 1) * length)
        result = []
        for pair in range(pairs):
            low = pair * 2 * HEAD_DIM
            queries = stack_heads(qkv_ref[rows, low : low + 2 * HEAD_DIM], first)
            result.append(dot(qkv_ref[rows, width + low : width + low + 2 * HEAD_DIM], queries, 1, 1))
        return result

    next_scores = scores_of(0)
    for image in range(per_step):
        rows = slice(image * length, (image + 1) * length)
        all_scores = next_scores
        if image + 1 < per_step:
            next_scores = scores_of(image + 1)
        column = bias_column(image)
        for cols in lane_tiles(2 * length):
            bias = jnp.where(own[:, cols], 0.0, column)
            for pair in range(pairs):
                scores = all_scores[pair][:, cols] * (HEAD_DIM**-0.5 * LOG2_E) + bias
                weights = jnp.exp2(scores - jnp.max(scores, axis=0, keepdims=True))
                probs = weights * (1.0 / jnp.sum(weights, axis=0, keepdims=True))
                probs_ref[image, pair, :, cols] = probs.astype(jnp.bfloat16)
        for pair in range(pairs):
            low = pair * 2 * HEAD_DIM
            values = qkv_ref[rows, 2 * width + low : 2 * width + low + 2 * HEAD_DIM]
            attended = join_heads(dot(probs_ref[image, pair], values, 0, 0), first)
            attended_ref[rows, low : low + 2 * HEAD_DIM] = attended.astype(jnp.bfloat16)

    middle_ref[...] = (
        x_ref[pl.ds(pl.multiple_of(base, length), step_rows), :].astype(jnp.float32)
        + dot(attended_ref[...], w_proj_ref[...])
        + vectors_ref[4:5]
    )


def feed_forward_kernel(
    images, middle_ref, cotangent_ref, attended_ref, w_up_ref, w_down_ref, proj_t_ref, vectors_ref, bias_up_ref,
    output_ref, d_middle_ref, d_attended_ref, up_grad_ref, down_grad_ref, proj_grad_ref, vector_sums_ref, up_sums_ref,
    wide_ref, *scratches,
):
    up_total_ref, down_total_ref, proj_total_ref = scratches[-3:]

    @pl.when(pl.program_id(0) == 0)
    def _():
        widen(cotangent_ref, wide_ref, images)

    feed_forward_steps(
        images, middle_ref, attended_ref, w_up_ref, w_down_ref, proj_t_ref, vectors_ref, bias_up_ref,
        d_middle_ref, d_attended_ref, vector_sums_ref, up_sums_ref, wide_ref, *scratches,
    )

    @pl.when(pl.program_id(0) == pl.num_programs(0) - 1)
    def _():
        narrow(wide_ref, output_ref, images)
        up_grad_ref[...] = up_total_ref[...].astype(jnp.bfloat16)
        down_grad_ref[...] = down_total_ref[...].T.astype(jnp.bfloat16)
        proj_grad_ref[...] = proj_total_ref[...].astype(jnp.bfloat16)


def feed_forward_steps(
    images, middle_ref, attended_ref, w_up_ref, w_down_ref, proj_t_ref, vectors_ref, bias_up_ref,
    d_middle_ref, d_attended_ref, vector_sums_ref, up_sums_ref,
    wide_ref, normed_ref, normed_t_ref, dy_ref, dy_t_ref, unit_ref, scale_ref, ahead_ref, back_ref,
    up_t_ref, down_t_ref, up_total_ref, down_total_ref, proj_total_ref,
):
    step = pl.program_id(0)
    length = wide_ref.shape[1] // images
    hidden = w_up_ref.shape[1]
    per_step = middle_ref.shape[0] // length

    @pl.when(step == 0)
    def _():
        for total in (up_total_ref, down_total_ref, proj_total_ref, vector_sums_ref, up_sums_ref):
            total[...] = jnp.zeros_like(total)
        up_t_ref[...] = w_up_ref[...].T
        down_t_ref[...] = w_down_ref[...].T

    for image in range(per_step):
        rows = slice(image * length, (image + 1) * length)
        dy = take_image(wide_ref, step * per_step + image, images)
        dy_ref[rows, :] = dy.astype(jnp.bfloat16)
        vector_sums_ref[3:4] += column_sum(dy)
        unit, scale = normal_form(middle_ref[rows, :])
        unit_ref[rows, :] = unit
        scale_ref[rows, :] = jnp.broadcast_to(scale, (length, scale_ref.shape[1]))
        normed_ref[rows, :] = (unit * vectors_ref[5:6] + vectors_ref[6:7]).astype(jnp.bfloat16)
    normed_t_ref[...] = normed_ref[...].T
    dy_t_ref[...] = dy_ref[...].T
    chunks = hidden // FF_CHUNK

    def cols_of(chunk):
        return slice(chunk * FF_CHUNK, (chunk + 1) * FF_CHUNK)

    def into(chunk):
        cols = cols_of(chunk)
        pre = dot(normed_ref[...], w_up_ref[:, cols])
        return pre + bias_up_ref[:, cols], dot(dy_ref[...], down_t_ref[:, cols])

    def across(pre, d_active):
        active, slope = gelu_and_slope(pre)
        return active.astype(jnp.bfloat16), (d_active * slope).astype(jnp.bfloat16)

    def out_of(chunk, active, d_hidden):
        cols = cols_of(chunk)
        ahead, back = dot(active, w_down_ref[cols, :]), dot(d_hidden, up_t_ref[cols, :])
        if chunk == 0:
            ahead_ref[...] = ahead
            back_ref[...] = back
        else:
            ahead_ref[...] += ahead
            back_ref[...] += back
        down_total_ref[:, cols] += dot(dy_t_ref[...], active)
        up_total_ref[:, cols] += dot(normed_t_ref[...], d_hidden)
        up_sums_ref[:, cols] += column_sum(d_hidden.astype(jnp.float32))

    entered, crossed = into(0), None
    for chunk in range(chunks + 1):
        next_entered = into(chunk + 1) if chunk + 1 < chunks else None
        next_crossed = across(*entered) if chunk < chunks else None
        if crossed is not None:
            out_of(chunk - 1, *crossed)
        entered, crossed = next_entered, next_crossed

    for image in range(per_step):
        rows = slice(image * length, (image + 1) * length)
        output = middle_ref[rows, :] + ahead_ref[rows, :] + vectors_ref[11:12]
        put_image(wide_ref, step * per_step + image, images, output)
        unit = unit_ref[rows, :]
        grad = back_ref[rows, :]
        vector_sums_ref[1:2] += column_sum(grad * unit)
        vector_sums_ref[2:3] += column_sum(grad)
        d_middle = dy_ref[rows, :].astype(jnp.float32) + norm_back(
            grad, unit, scale_ref[rows, 0:1], vectors_ref[5:6]
        )
        d_middle_ref[rows, :] = d_middle
        d_branch = d_middle.astype(jnp.bfloat16)
        dy_ref[rows, :] = d_branch
        vector_sums_ref[0:1] += column_sum(d_branch.astype(jnp.float32))
    proj_total_ref[...] += dot(attended_ref[...], dy_ref[...], 0, 0)
    d_attended_ref[...] = dot(dy_ref[...], proj_t_ref[...]).astype(jnp.bfloat16)


def attention_back_kernel(
    images, x_ref, qkv_ref, probs_ref, d_attended_ref, d_middle_ref, qkv_t_ref, vectors_ref,
    input_grad_ref, qkv_grad_ref, vector_sums_ref, wide_ref, normed_ref, d_projected_ref, back_ref, qkv_total_ref,
):
    @pl.when(pl.program_id(0) == 0)
    def _():
        qkv_total_ref[...] = jnp.zeros_like(qkv_total_ref)
        vector_sums_ref[...] = jnp.zeros_like(vector_sums_ref)

    def put(image, rows, values):
        put_image(wide_ref, image, images, values)

    attention_back_steps(
        x_ref, qkv_ref, probs_ref, d_attended_ref, vectors_ref, vector_sums_ref, normed_ref, d_projected_ref, qkv_total_ref
    )
    input_back_steps(
        put, probs_ref.shape[2], x_ref, d_projected_ref, d_middle_ref, qkv_t_ref, vectors_ref, vector_sums_ref, back_ref
    )

    @pl.when(pl.program_id(0) == pl.num_programs(0) - 1)
    def _():
        narrow(wide_ref, input_grad_ref, images)
        qkv_grad_ref[...] = qkv_total_ref[...].astype(jnp.bfloat16)


def attention_back_steps(
    x_ref, qkv_ref, probs_ref, d_attended_ref, vectors_ref, vector_sums_ref, normed_ref, d_projected_ref, qkv_total_ref
):
    width = x_ref.shape[1]
    length = probs_ref.shape[2]
    per_step = probs_ref.shape[0]

    pairs = width // (2 * HEAD_DIM)
    first = pair_mask(length)
    scale = HEAD_DIM**-0.5

    def places(image, pair):
        low = pair * 2 * HEAD_DIM
        rows = slice(image * length, (image + 1) * length)
        return rows, [slice(part * width + low, part * width + low + 2 * HEAD_DIM) for part in range(3)]

    def entering(image):
        result = []
        for pair in range(pairs):
            rows, cols = places(image, pair)
            d_attended = stack_heads(d_attended_ref[rows, cols[0]], first)
            d_values = dot(probs_ref[image, pair], d_attended)
            d_projected_ref[rows, cols[2]] = d_values.astype(jnp.bfloat16)
            result.append(dot(qkv_ref[rows, cols[2]], d_attended, 1, 1))
        return result

    next_probs = entering(0)
    for image in range(per_step):
        all_d_probs = next_probs
        if image + 1 < per_step:
            next_probs = entering(image + 1)
        all_d_scores = []
        for pair in range(pairs):
            parts = []
            for cols in lane_tiles(2 * length):
                probs, d_probs = probs_ref[image, pair, :, cols].astype(jnp.float32), all_d_probs[pair][:, cols]
                along = jnp.sum(d_probs * probs, axis=0, keepdims=True)
                parts.append((probs * (d_probs - along)).astype(jnp.bfloat16))
            all_d_scores.append(jnp.concatenate(parts, axis=1))
        for pair in range(pairs):
            rows, cols = places(image, pair)
            d_scores = all_d_scores[pair]
            queries = stack_heads(qkv_ref[rows, cols[0]], first)
            d_queries = join_heads(dot(d_scores, qkv_ref[rows, cols[1]], 0, 0), first) * scale
            d_projected_ref[rows, cols[0]] = d_queries.astype(jnp.bfloat16)
            d_projected_ref[rows, cols[1]] = (dot(d_scores, queries) * scale).astype(jnp.bfloat16)

    query_sums = value_sums = jnp.zeros((8, width), jnp.float32)
    for rows in slices_of(x_ref.shape[0]):
        query_sums += fold_rows(d_projected_ref[rows, :width].astype(jnp.float32))
        value_sums += fold_rows(d_projected_ref[rows, 2 * width :].astype(jnp.float32))
        unit, _ = normal_form(x_ref[rows, :].astype(jnp.float32))
        normed_ref[rows, :] = (unit * vectors_ref[0:1] + vectors_ref[1:2]).astype(jnp.bfloat16)
    vector_sums_ref[2:3] += column_sum(query_sums)
    vector_sums_ref[3:4] += column_sum(value_sums)
    qkv_total_ref[...] += dot(normed_ref[...], d_projected_ref[...], 0, 0)


def input_back_steps(
    put, length, x_ref, d_projected_ref, d_middle_ref, qkv_t_ref, vectors_ref, vector_sums_ref, back_ref
):
    step = pl.program_id(0)
    per_step = x_ref.shape[0] // length
    back_ref[...] = dot(d_projected_ref[...], qkv_t_ref[...])
    gain_sums = shift_sums = jnp.zeros((8, x_ref.shape[1]), jnp.float32)
    for rows in slices_of(x_ref.shape[0]):
        unit, scale = normal_form(x_ref[rows, :].astype(jnp.float32))
        grad = back_ref[rows, :]
        gain_sums += fold_rows(grad * unit)
        shift_sums += fold_rows(grad)
        back_ref[rows, :] = d_middle_ref[rows, :] + norm_back(grad, unit, scale, vectors_ref[0:1])
    vector_sums_ref[0:1] += column_sum(gain_sums)
    vector_sums_ref[1:2] += column_sum(shift_sums)
    for image in range(per_step):
        rows = slice(image * length, (image + 1) * length)
        put(step * per_step + image, rows, back_ref[rows, :])


def whole_block(shape):
    return pl.BlockSpec(shape, lambda step: (0,) * len(shape))


def step_block(shape, first=0):
    return pl.BlockSpec(shape, lambda step: (first + step,) + (0,) * (len(shape) - 1))


def scratch(*shape, dtype=jnp.float32):
    return pltpu.VMEM(shape, dtype)


def call_kernel(kernel, statics, steps, ins, outs, scratches, operands, flops, transcendentals=0, first_step=0, aliases={}):
    in_specs = [
        pl.BlockSpec(memory_space=pltpu.SMEM)
        if block == "place"
        else pl.BlockSpec(memory_space=pl.ANY)
        if block == "await"
        else whole_block(op.shape) if block is None else step_block(block, first_step)
        for op, block in zip(operands, ins)
    ]
    out_specs = [
        whole_block(shape) if block is None else step_block(block, first_step) for shape, dtype, block in outs
    ]
    moved = sum(op.size * op.dtype.itemsize for op in operands) + sum(
        math.prod(shape) * jnp.dtype(dtype).itemsize for shape, dtype, block in outs
    )
    return pl.pallas_call(
        functools.partial(kernel, *statics),
        grid=(steps,),
        in_specs=in_specs,
        out_specs=out_specs,
        out_shape=[jax.ShapeDtypeStruct(shape, dtype) for shape, dtype, block in outs],
        scratch_shapes=scratches,
        input_output_aliases=aliases,
        compiler_params=pltpu.CompilerParams(vmem_limit_bytes=vmem_bytes),
        cost_estimate=pl.CostEstimate(
            flops=flops * 8, bytes_accessed=moved, transcendentals=transcendentals
        ),
    )(*operands)


def attention_forward(tokens, bias, w_qkv, w_proj, vectors):
    images, length, _ = bias.shape
    total, width = tokens.shape
    pairs = width // (2 * HEAD_DIM)
    rows = PER_STEP * length
    low, high = jnp.bfloat16, jnp.float32
    outs = [
        ((total, width), low, None),
        ((total, 3 * width), low, (rows, 3 * width)),
        ((images, pairs, length, 2 * length), low, (PER_STEP, pairs, length, 2 * length)),
        ((total, width), low, (rows, width)),
        ((total, width), high, (rows, width)),
    ]
    return call_kernel(
        attention_kernel, (images,), images // PER_STEP,
        [None, (PER_STEP, length, 1), None, None, None], outs,
        [scratch(width // 128, total, 128), scratch(rows, width, dtype=low)],
        (tokens, bias, w_qkv, w_proj, vectors),
        2 * total * width * 4 * width + 8 * total * length * width,
    )


def feed_forward(images, middle, cotangent, attended, w_up, w_down, w_proj, vectors):
    total, width = middle.shape
    hidden = w_up.shape[1]
    rows = total // images * FF_PER_STEP
    low, high = jnp.bfloat16, jnp.float32
    block = (rows, width)
    outs = [
        ((total, width), low, None),
        ((total, width), high, block),
        ((total, width), low, block),
        ((width, hidden), low, None),
        ((hidden, width), low, None),
        ((width, width), low, None),
        ((8, width), high, None),
        ((1, hidden), high, None),
    ]
    scratches = [
        scratch(width // 128, total, 128),
        scratch(rows, width, dtype=low),
        scratch(width, rows, dtype=low),
        scratch(rows, width, dtype=low),
        scratch(width, rows, dtype=low),
        scratch(rows, width),
        scratch(rows, 128),
        scratch(rows, width),
        scratch(rows, width),
        scratch(hidden, width, dtype=low),
        scratch(width, hidden, dtype=low),
        scratch(width, hidden),
        scratch(width, hidden),
        scratch(width, width),
    ]
    return call_kernel(
        feed_forward_kernel, (images,), images // FF_PER_STEP,
        [block, None, block, None, None, None, None, None], outs, scratches,
        (middle, cotangent, attended, w_up, w_down, w_proj.T, vectors, vectors[7:11].reshape(1, hidden)),
        12 * total * width * hidden + 4 * total * width * width, total * hidden,
    )


def attention_back(x, qkv, probs, d_attended, d_middle, w_qkv, vectors):
    images, pairs, length, _ = probs.shape
    total, width = x.shape
    rows = PER_STEP * length
    low, high = jnp.bfloat16, jnp.float32
    block = (rows, width)
    outs = [
        ((total, width), low, None),
        ((width, 3 * width), low, None),
        ((8, width), high, None),
    ]
    scratches = [
        scratch(width // 128, total, 128),
        scratch(rows, width, dtype=low),
        scratch(rows, 3 * width, dtype=low),
        scratch(rows, width),
        scratch(width, 3 * width),
    ]
    return call_kernel(
        attention_back_kernel, (images,), images // PER_STEP,
        [block, (rows, 3 * width), (PER_STEP, pairs, length, 2 * length), block, block, None, None],
        outs, scratches, (x, qkv, probs, d_attended, d_middle, w_qkv.T, vectors),
        4 * total * width * 3 * width + 16 * total * length * width,
    )

def linear_place():
    return lax.axis_index("dp") * lax.axis_size("group") + lax.axis_index("group")


def permute(array, mask):
    count = lax.axis_size("dp") * lax.axis_size("group")
    return lax.ppermute(array, ("dp", "group"), [(rank, rank ^ mask) for rank in range(count)])


def direct_masks(bits):
    masks = [0]
    for bit in bits:
        masks = masks + [mask | bit for mask in masks]
    return masks[1:]


def add_wide(first, *rest):
    total = first.astype(jnp.float32)
    for part in rest:
        total = total + part.astype(jnp.float32)
    return total


def packed_place(mask, spread, count):
    return ((mask >> 1) & (spread - 1)) * (count // (2 * spread)) + (mask >> (spread.bit_length()))


def scatter_step(held, bits):
    masks = direct_masks(bits)
    size = held.shape[0] // (len(masks) + 1)
    parts = [
        permute(held[size * (at + 1) : size * (at + 2)].astype(jnp.bfloat16), mask)
        for at, mask in enumerate(masks)
    ]
    return held[:size], parts


def add_wide(first, *rest):
    total = first.astype(jnp.float32)
    for part in rest:
        total = total + part.astype(jnp.float32)
    return total


def packed_place(mask, spread, count):
    return ((mask >> 1) & (spread - 1)) * (count // (2 * spread)) + (mask >> (spread.bit_length()))


def gather_step(held, bits):
    return held + [permute(part, mask) for mask in direct_masks(bits) for part in held]


def gathered_place(mask, count):
    return (mask & 1) * (count // 2) + ((mask >> 2) & 1) * (count // 4) + (mask >> 3) * 2 + ((mask >> 1) & 1)


def unpack(place_ref, block_refs, packed_ref, put, dp_size, spread):
    place = place_ref[0]
    size = block_refs[0].shape[0]
    for at, block_ref in enumerate(block_refs):
        packed_ref[at * size : (at + 1) * size] = block_ref[...]
    count = dp_size * spread
    for row in range(dp_size):
        for col in range(spread):
            put(row, col, packed_ref[gathered_place((row * spread + col) ^ place, count)])


def pack(place_ref, take, keep_ref, leave_ref, dp_size, spread):
    place = place_ref[0]
    odd = (place & 1) == 1
    for row in range(dp_size):
        for col in range(0, spread, 2):
            at = packed_place((row * spread + col) ^ place, spread, dp_size * spread)
            even_block, odd_block = take(row, col), take(row, col + 1)
            keep_ref[at] = jnp.where(odd, odd_block, even_block)
            leave_ref[at] = jnp.where(odd, even_block, odd_block)


def narrow_pieces(place_ref, wide_ref, piece_refs, spread):
    tiles, _, lanes = wide_ref.shape
    rows_of_piece = piece_refs[0].shape[0]
    step = 64
    group = place_ref[0] & (spread - 1)
    for relative, piece_ref in enumerate(piece_refs):
        base = (group ^ relative) * rows_of_piece

        @pl.loop(0, rows_of_piece // step)
        def _(part):
            target = pl.ds(pl.multiple_of(part * step, step), step)
            source = pl.ds(pl.multiple_of(base + part * step, step), step)
            for tile in range(tiles):
                cols = slice(tile * lanes, (tile + 1) * lanes)
                piece_ref[target, cols] = wide_ref[tile, source, :].astype(jnp.bfloat16)


def general_body(
    tokens,
    keep_mask,
    cotangent,
    qkv_weight,
    proj_weight,
    up_weight,
    down_weight,
    vectors,
    qkv_rows,
    qkv_cols,
    proj_rows,
    proj_cols,
    up_rows,
    up_cols,
    down_rows,
    down_cols,
    vector_moment,
):
    masters = (qkv_weight, proj_weight, up_weight, down_weight)
    lowered = tuple((master.astype(jnp.bfloat16) for master in masters))
    dp_bits, group_bits = axis_bits("dp"), axis_bits("group")
    gather_steps = dp_bits[1:] + group_bits[1:] + dp_bits[:1] + group_bits[:1]
    scatter_steps = gather_steps[::-1]
    w_qkv, w_proj, w_up, w_down = tuple(
        blocks_to_whole(gather_blocks(part, gather_steps), gather_steps) for part in lowered
    )
    spread = lax.axis_size("group")

    def slots_in(array):
        held, slots, width = array.shape
        parts = array.transpose(1, 0, 2).reshape(slots, spread, held // spread, width)
        parts = lax.all_to_all(
            parts.transpose(1, 0, 2, 3), "group", split_axis=0, concat_axis=0, tiled=True
        )
        return parts.reshape(spread * slots * (held // spread), width)

    def slots_out(array):
        held, slots, width = tokens.shape
        parts = array.reshape(spread, slots, held // spread, width)
        parts = lax.all_to_all(parts, "group", split_axis=0, concat_axis=0, tiled=True)
        return parts.transpose(1, 0, 2, 3).reshape(slots, held, width).transpose(1, 0, 2)

    images = keep_mask.shape[0]
    bias = jnp.where(keep_mask > 0, 0.0, -1e30)[:, :, None]
    x, qkv, probs, attended, middle = attention_forward(
        slots_in(tokens), bias, w_qkv, w_proj, vectors
    )
    output, d_middle, d_attended, up_grad, down_grad, proj_grad, ff_sums, up_sums = feed_forward(
        images, middle, slots_in(cotangent), attended, w_up, w_down, w_proj, vectors
    )
    block_output = slots_out(output)
    d_input, qkv_grad, att_sums = attention_back(
        x, qkv, probs, d_attended, d_middle, w_qkv, vectors
    )
    input_grad = slots_out(d_input)
    local_vectors = jnp.concatenate(
        [att_sums[:4], ff_sums[:3], up_sums.reshape(4, -1), ff_sums[3:4]], axis=0
    )
    vector_grad = sum_everywhere(local_vectors, group_bits + dp_bits)
    local_grads = (qkv_grad, proj_grad, up_grad, down_grad)
    owned = tuple(
        scatter_sum(whole_to_blocks(part, scatter_steps), scatter_steps) for part in local_grads
    )
    squares = tuple((gradient * gradient + tiny_square for gradient in owned))
    row_parts = tuple((jnp.sum(square, axis=1) for square in squares)) + tuple(
        (jnp.sum(master * master, axis=1) for master in masters)
    )
    row_sums = sum_parts(row_parts, group_bits)
    rows_old = (qkv_rows, proj_rows, up_rows, down_rows)
    cols_old = (qkv_cols, proj_cols, up_cols, down_cols)
    total_cols = tuple((gradient.shape[1] * lax.axis_size("group") for gradient in owned))
    total_rows = tuple((gradient.shape[0] * lax.axis_size("dp") for gradient in owned))
    rows_new = tuple(
        (
            decay_rate * rows_old[which] + (1.0 - decay_rate) * row_sums[which] / total_cols[which]
            for which in range(4)
        )
    )
    col_parts = (
        tuple((jnp.sum(square, axis=0) for square in squares))
        + tuple((jnp.sum(row_stat) for row_stat in rows_new))
        + tuple((jnp.sum(row_sums[4 + which]) for which in range(4)))
    )
    col_sums = sum_parts(col_parts, dp_bits)
    results = []
    for which in range(4):
        cols_new = (
            decay_rate * cols_old[which] + (1.0 - decay_rate) * col_sums[which] / total_rows[which]
        )
        mean_rows = col_sums[4 + which] / total_rows[which]
        spread = jnp.sqrt(col_sums[8 + which] / (total_rows[which] * total_cols[which]))
        second = rows_new[which][:, None] * cols_new[None, :] / mean_rows
        updated = masters[which] - step_rate * spread * owned[which] * lax.rsqrt(second)
        results.append((owned[which], rows_new[which], cols_new, updated))
    vector_moment_new = decay_rate * vector_moment + (1.0 - decay_rate) * (
        vector_grad * vector_grad + tiny_square
    )
    row_spread = jnp.sqrt(jnp.mean(vectors * vectors, axis=1, keepdims=True))
    vector_new = vectors - step_rate * row_spread * vector_grad * lax.rsqrt(vector_moment_new)
    return (
        block_output,
        input_grad,
        results[0][0],
        results[0][1],
        results[0][2],
        results[0][3],
        results[1][0],
        results[1][1],
        results[1][2],
        results[1][3],
        results[2][0],
        results[2][1],
        results[2][2],
        results[2][3],
        results[3][0],
        results[3][1],
        results[3][2],
        results[3][3],
        vector_grad,
        vector_moment_new,
        vector_new,
    )


def first_attention_kernel(images, dp_size, spread, place_ref, tokens_ref, *refs):
    blocks, refs = refs[:4], refs[4:]
    keep_ref, vectors_ref, *outs, x_ref, w_qkv_ref, w_proj_ref, qkv_t_ref, proj_t_ref = refs[:-4]
    packed_ref, wide_ref, bias_ref, normed_ref = refs[-4:]
    rows = packed_ref.shape[1]
    qkv_cols, proj_cols = w_qkv_ref.shape[1] // spread, w_proj_ref.shape[1] // spread

    @pl.when(pl.program_id(0) == 0)
    def _():
        widen(tokens_ref, wide_ref, images)
        to_image_rows(wide_ref, x_ref, images)

        def put(row, col, block):
            down = slice(row * rows, (row + 1) * rows)
            w_qkv_ref[down, col * qkv_cols : (col + 1) * qkv_cols] = block[:, :qkv_cols]
            w_proj_ref[down, col * proj_cols : (col + 1) * proj_cols] = block[:, qkv_cols:]

        unpack(place_ref, blocks, packed_ref, put, dp_size, spread)
        qkv_t_ref[...] = w_qkv_ref[...].T
        proj_t_ref[...] = w_proj_ref[...].T

    attention_part(0, x_ref, keep_ref, w_qkv_ref, w_proj_ref, vectors_ref, *outs, bias_ref, normed_ref)


def next_attention_kernel(start, x_ref, keep_ref, w_qkv_ref, w_proj_ref, vectors_ref, *refs):
    attention_part(start, x_ref, keep_ref, w_qkv_ref, w_proj_ref, vectors_ref, *refs[-6:])


def attention_part(
    start, x_ref, keep_ref, w_qkv_ref, w_proj_ref, vectors_ref,
    qkv_ref, probs_ref, attended_ref, middle_ref, bias_ref, normed_ref,
):
    @pl.when(pl.program_id(0) == 0)
    def _():
        bias_ref[...] = jnp.where(keep_ref[...] > 0, 0.0, -1e30).T

    def bias_column(image):
        here = start + pl.program_id(0) * probs_ref.shape[0] + image
        lane = lax.broadcasted_iota(jnp.int32, bias_ref.shape, 1)
        return row_sum(jnp.where(lane == here, bias_ref[...], 0.0))

    attention_steps(
        x_ref, bias_column, w_qkv_ref, w_proj_ref, vectors_ref,
        qkv_ref, probs_ref, attended_ref, middle_ref, normed_ref,
    )


def feed_forward_packed_kernel(images, dp_size, spread, place_ref, *refs):
    cotangent_ref, blocks, refs = refs[0], refs[1:5], refs[5:]
    middle_ref, attended_ref, proj_t_ref, vectors_ref = refs[:4]
    outputs, refs = refs[4 : 4 + spread], refs[4 + spread :]
    d_middle_ref, d_attended_ref, keep_ref, leave_ref, proj_total_ref, vector_sums_ref, up_sums_ref = refs[:7]
    w_up_ref, w_down_ref, down_low_ref, packed_ref, bias_up_ref, wide_ref = refs[7:13]
    scratches = refs[13:]
    width = w_up_ref.shape[0]
    up_total_ref, down_total_ref = scratches[-2:]
    rows = packed_ref.shape[1]
    up_cols = w_up_ref.shape[1] // spread
    out_cols = w_down_ref.shape[1] // spread
    folds = w_down_ref.shape[0] // w_up_ref.shape[0]

    @pl.when(pl.program_id(0) == 0)
    def _():
        widen(cotangent_ref, wide_ref, images)
        for fold in range(bias_up_ref.shape[1] // width):
            bias_up_ref[:, fold * width : (fold + 1) * width] = vectors_ref[7 + fold : 8 + fold]

        def put(row, col, block):
            w_up_ref[row * rows : (row + 1) * rows, col * up_cols : (col + 1) * up_cols] = block[:, :up_cols]
            for fold in range(folds):
                down = (row * folds + fold) * rows
                start = up_cols + fold * out_cols
                w_down_ref[down : down + rows, col * out_cols : (col + 1) * out_cols] = block[
                    :, start : start + out_cols
                ]

        unpack(place_ref, blocks, packed_ref, put, dp_size, spread)

    feed_forward_steps(
        images, middle_ref, attended_ref, w_up_ref, w_down_ref, proj_t_ref, vectors_ref, bias_up_ref,
        d_middle_ref, d_attended_ref, vector_sums_ref, up_sums_ref, wide_ref, *scratches, proj_total_ref,
    )

    @pl.when(pl.program_id(0) == pl.num_programs(0) - 1)
    def _():
        narrow_pieces(place_ref, wide_ref, outputs, spread)
        down_low_ref[...] = down_total_ref[...].T.astype(jnp.bfloat16)

        def take(row, col):
            across = slice(row * rows, (row + 1) * rows)
            cols = slice(col * out_cols, (col + 1) * out_cols)
            parts = [up_total_ref[across, col * up_cols : (col + 1) * up_cols].astype(jnp.bfloat16)]
            for fold in range(folds):
                down = (row * folds + fold) * rows
                parts.append(down_low_ref[down : down + rows, cols])
            return jnp.concatenate(parts, axis=1)

        pack(place_ref, take, keep_ref, leave_ref, dp_size, spread)


def attention_back_packed_kernel(
    dp_size, spread, place_ref, x_ref, qkv_ref, probs_ref, d_attended_ref, vectors_ref, proj_total_ref, _,
    d_projected_ref, keep_ref, leave_ref, vector_sums_ref, normed_ref, total_ref,
):
    @pl.when(pl.program_id(0) == 0)
    def _():
        total_ref[...] = jnp.zeros_like(total_ref)
        vector_sums_ref[...] = jnp.zeros_like(vector_sums_ref)

    attention_back_steps(
        x_ref, qkv_ref, probs_ref, d_attended_ref, vectors_ref, vector_sums_ref, normed_ref, d_projected_ref, total_ref
    )

    @pl.when(pl.program_id(0) == pl.num_programs(0) - 1)
    def _():
        rows = keep_ref.shape[1]
        qkv_cols, proj_cols = total_ref.shape[1] // spread, proj_total_ref.shape[1] // spread

        def take(row, col):
            down = slice(row * rows, (row + 1) * rows)
            parts = [
                total_ref[down, col * qkv_cols : (col + 1) * qkv_cols],
                proj_total_ref[down, col * proj_cols : (col + 1) * proj_cols],
            ]
            return jnp.concatenate(parts, axis=1).astype(jnp.bfloat16)

        pack(place_ref, take, keep_ref, leave_ref, dp_size, spread)


def first_input_kernel(
    length, x_ref, d_projected_ref, d_middle_ref, qkv_t_ref, vectors_ref, before_ref, *refs
):
    d_input_ref, vector_sums_ref, back_ref = refs[-3:]

    @pl.when(pl.program_id(0) == 0)
    def _():
        vector_sums_ref[...] = before_ref[...]

    def put(image, rows, values):
        d_input_ref[rows, :] = values.astype(jnp.bfloat16)

    input_back_steps(
        put, length, x_ref, d_projected_ref, d_middle_ref, qkv_t_ref, vectors_ref, vector_sums_ref, back_ref
    )


def last_input_kernel(
    images, spread, length, first, place_ref, x_ref, d_projected_ref, d_middle_ref, qkv_t_ref, vectors_ref, before_ref,
    d_input_ref, _, *refs,
):
    pieces, (vector_sums_ref, wide_ref, back_ref) = refs[:spread], refs[spread:]

    @pl.when(pl.program_id(0) == 0)
    def _():
        vector_sums_ref[...] = before_ref[...]
        for image in range(first):
            rows = slice(image * length, (image + 1) * length)
            put_image(wide_ref, image, images, d_input_ref[rows, :].astype(jnp.float32))

    def put(image, rows, values):
        put_image(wide_ref, first + image, images, values)

    input_back_steps(
        put, length, x_ref, d_projected_ref, d_middle_ref, qkv_t_ref, vectors_ref, vector_sums_ref, back_ref
    )

    @pl.when(pl.program_id(0) == pl.num_programs(0) - 1)
    def _():
        narrow_pieces(place_ref, wide_ref, pieces, spread)


def cut(array_ref, parts_ref):
    count = parts_ref.shape[2]
    for member in range(parts_ref.shape[0]):
        parts_ref[member] = array_ref[:, member * count : (member + 1) * count, :]


def pack_kernel(qkv_ref, proj_ref, up_ref, down_ref, pack_ref):
    rows, start = pack_ref.shape[0], 0
    parts = [qkv_ref[...], proj_ref[...], up_ref[...]]
    parts += [down_ref[fold * rows : (fold + 1) * rows, :] for fold in range(down_ref.shape[0] // rows)]
    for part in parts:
        pack_ref[:, start : start + part.shape[1]] = part.astype(jnp.bfloat16)
        start += part.shape[1]


def pair_kernel(own_ref, arrived_ref, _, first_ref, second_ref):
    start = first_ref.shape[2]
    for at, pack_ref in enumerate((own_ref, arrived_ref)):
        first_ref[at] = pack_ref[:, :start]
        second_ref[at] = pack_ref[:, start:]


def cotangent_kernel(array_ref, _, parts_ref):
    cut(array_ref, parts_ref)


def join_kernel(count, *refs):
    size = refs[0].shape[0]
    for at, part_ref in enumerate(refs[:count]):
        refs[-1][at * size : (at + 1) * size] = part_ref[...]


def settle_kernel(spread, place_ref, *refs):
    lists, (output_ref, token_ref) = refs[:-2], refs[-2:]
    token_ref[...] = jnp.zeros_like(token_ref)
    group = place_ref[0] & (spread - 1)
    count = lists[0].shape[1]
    share = len(lists) // spread * count
    for at, piece_ref in enumerate(lists):
        relative, part = at % spread, at // spread
        start = pl.multiple_of((group ^ relative) * share + part * count, count)
        output_ref[:, pl.ds(start, count), :] = piece_ref[...]


def lane_table(rows, columns):
    lane = lax.broadcasted_iota(jnp.int32, (rows, 128), 1)
    table = jnp.zeros((rows, 128), jnp.float32)
    for at, column in enumerate(columns):
        table = jnp.where(lane == at, column, table)
    return table


def added(parts):
    while len(parts) > 1:
        parts = [sum(parts[at : at + 2][1:], parts[at]) for at in range(0, len(parts), 2)]
    return parts[0]


def row_sum(values):
    return jnp.sum(values, axis=1, keepdims=True)


def after_kernel(*refs):
    pass


def add_kernel(count, keep_ref, arrived_ref, *refs):
    parts = refs[-count:]
    size = parts[0].shape[0]
    for at, part_ref in enumerate(parts):
        rows = slice(at * size, (at + 1) * size)
        total = keep_ref[rows].astype(jnp.float32) + arrived_ref[rows].astype(jnp.float32)
        part_ref[...] = total.astype(part_ref.dtype)


def gradient_kernel(count, *refs):
    block_parts, sums, refs = refs[:count], refs[count : count + 3], refs[count + 3 :]
    masters, rows_old, refs = refs[:4], refs[4:8], refs[8:]
    grads, (row_ref, message_ref) = refs[:4], refs[4:]
    blocks = added([part[0].astype(jnp.float32) for part in block_parts])
    rows, up_cols = grads[2].shape
    qkv_cols, out_cols = grads[0].shape[1], grads[1].shape[1]
    folds = grads[3].shape[0] // rows
    up = blocks[:, :up_cols]
    downs = [blocks[:, up_cols + fold * out_cols :][:, :out_cols] for fold in range(folds)]
    start = up_cols + folds * out_cols
    qkv = blocks[:, start : start + qkv_cols]
    proj = blocks[:, start + qkv_cols :]
    grads[0][...] = qkv
    grads[1][...] = proj
    grads[2][...] = up
    for fold in range(folds):
        grads[3][fold * rows : (fold + 1) * rows, :] = downs[fold]
    squares = [part * part + tiny_square for part in (qkv, proj, up, *downs)]
    row_ref[...] = lane_table(rows, [row_sum(square) for square in squares]).T[: row_ref.shape[0], :]
    width = message_ref.shape[1]
    message_ref[...] = jnp.zeros_like(message_ref)
    for at, square in enumerate((*squares[:3], added(squares[3:]))):
        message_ref[at : at + 1, : square.shape[1]] = column_sum(square)
    scalars = [column_sum(row_sum(master[...] * master[...])) for master in masters]
    scalars += [row_sum(part[...].reshape(1, part.shape[0])) for part in rows_old]
    message_ref[4:5, :128] = lane_table(1, scalars)
    att_ref, ff_ref, up_ref = sums
    count = up_ref.shape[1] // width
    message_ref[8:12, :] = att_ref[:4]
    message_ref[12:15, :] = ff_ref[:3]
    for at in range(count):
        message_ref[15 + at : 16 + at, :] = up_ref[:, at * width : (at + 1) * width]
    message_ref[15 + count : 16 + count, :] = ff_ref[3:4]


def column_kernel(row_ref, *refs):
    parts, (cols_ref, message_ref) = refs[:-3], refs[-2:]
    total = added([part[...] for part in parts])
    cols_ref[...] = total[:8]
    width = total.shape[1]
    rows = row_ref.shape[1]
    message_ref[...] = jnp.zeros_like(message_ref)
    message_ref[:8, :rows] = row_ref[...]
    columns = [row_sum(total[which : which + 1]) for which in range(4)]
    squares = [total[4:5, which : which + 1] for which in range(4)]
    message_ref[8:9, :] = lane_table(1, columns + squares)
    for tile in range(width // 128):
        message_ref[16 * (tile + 1) : 16 * (tile + 2), :] = total[8:, tile * 128 : (tile + 1) * 128]


def update_kernel(count, heights, widths, *refs):
    messages, refs = refs[:count], refs[count:]
    cols_ref, vectors_ref, moment_ref, refs = refs[0], refs[1], refs[2], refs[3:]
    grads, masters, rows_old, cols_old, refs = refs[:4], refs[4:8], refs[8:12], refs[12:16], refs[17:]
    news, cols_new, rows_out, refs = refs[:4], refs[4:8], refs[8:12], refs[12:]
    vector_grad_ref, moment_new_ref, vector_new_ref = refs
    sums = added([message[...] for message in messages])
    height = grads[0].shape[0]
    folds = grads[3].shape[0] // height
    lanes = [[0], [1], [2], list(range(3, 3 + folds))]
    share = 1.0 - decay_rate
    for which in range(4):
        entries = heights[which] * widths[which]
        cols = cols_old[which].shape[0]
        new = decay_rate * cols_old[which][...].reshape(1, cols) + share / heights[which] * cols_ref[
            which : which + 1, :cols
        ]
        cols_new[which][...] = new[0]
        old_total = cols_ref[4:5, 4 + which : 5 + which]
        mean_rows = (decay_rate * old_total + share / widths[which] * sums[8:9, which : which + 1]) / heights[which]
        rate = step_rate * jnp.sqrt(sums[8:9, 4 + which : 5 + which] / entries)
        across = new / mean_rows
        old = rows_old[which][...].reshape(1, len(lanes[which]) * height)
        row_sums = jnp.concatenate([sums[lane : lane + 1, :height] for lane in lanes[which]], axis=1)
        row = decay_rate * old + share / widths[which] * row_sums
        rows_out[which][...] = row[0]
        for fold in range(len(lanes[which])):
            part = slice(fold * height, (fold + 1) * height)
            column = jnp.broadcast_to(row[:, part], (8, height)).T[:, :1]
            news[which][part, :] = masters[which][part, :] - rate * grads[which][part, :] * lax.rsqrt(column * across)
    vectors = vectors_ref[...]
    count = vectors.shape[0]
    gradient = jnp.concatenate(
        [sums[16 * (tile + 1) : 16 * (tile + 1) + count] for tile in range(vectors.shape[1] // 128)], axis=1
    )
    vector_grad_ref[...] = gradient
    moment = decay_rate * moment_ref[...] + share * (gradient * gradient + tiny_square)
    moment_new_ref[...] = moment
    spread = jnp.sqrt(jnp.mean(vectors * vectors, axis=1, keepdims=True))
    vector_new_ref[...] = vectors - step_rate * spread * gradient * lax.rsqrt(moment)


def packed_body(
    tokens, keep_mask, cotangent, qkv_weight, proj_weight, up_weight, down_weight, vectors,
    qkv_rows, qkv_cols, proj_rows, proj_cols, up_rows, up_cols, down_rows, down_cols, vector_moment,
):
    spread, dp_size = lax.axis_size("group"), lax.axis_size("dp")
    low, high = jnp.bfloat16, jnp.float32
    place = linear_place().astype(jnp.int32).reshape(1)
    group = lax.axis_index("group")
    held, slots, width = tokens.shape
    images, length = keep_mask.shape
    hidden = up_weight.shape[1] * spread
    total = images * length
    rows = qkv_weight.shape[0]
    folds = down_weight.shape[0] // rows
    core_bits = (1,)
    near_bits = tuple(1 << at for at in range(1, spread.bit_length()))
    far_bits = tuple(spread << at for at in range(1, dp_size.bit_length() - 1))
    half = spread * dp_size // 2

    anywhere = pl.BlockSpec(memory_space=pl.ANY)
    in_smem = pl.BlockSpec(memory_space=pltpu.SMEM)

    in_vmem = pl.BlockSpec(memory_space=pltpu.VMEM)
    small = functools.partial(
        pl.pallas_call, compiler_params=pltpu.CompilerParams(vmem_limit_bytes=vmem_bytes)
    )
    masters = (qkv_weight, proj_weight, up_weight, down_weight)
    parted = jax.ShapeDtypeStruct((spread, slots, images, width), low)

    def after(array, awaited):
        return small(
            after_kernel,
            in_specs=[anywhere] * (1 + len(awaited)),
            out_specs=anywhere,
            out_shape=jax.ShapeDtypeStruct(array.shape, array.dtype),
            input_output_aliases={0: 0},
        )(array, *awaited)

    def to_group(parts):
        return lax.all_to_all(parts, "group", split_axis=0, concat_axis=0, tiled=True)

    def to_images(parts):
        return to_group(parts).reshape(total, width)

    def exchange(parts):
        return [parts[0]] + [permute(part, relative) for relative, part in enumerate(parts) if relative]

    def settle(parts):
        parts = [part.reshape(slots, -1, width) for part in parts]
        whole, token = small(
            functools.partial(settle_kernel, spread),
            in_specs=[in_smem] + [in_vmem] * len(parts),
            out_specs=[in_vmem] * 2,
            out_shape=[
                jax.ShapeDtypeStruct((slots, held, width), low),
                jax.ShapeDtypeStruct((8, 128), high),
            ],
        )(place, *parts)
        return whole.transpose(1, 0, 2), token

    first_cols = qkv_weight.shape[1] + proj_weight.shape[1]
    second_cols = up_weight.shape[1] + folds * down_weight.shape[1]
    pack_own = small(pack_kernel, out_shape=jax.ShapeDtypeStruct((rows, first_cols + second_cols), low))(*masters)
    across_y, across_x = near_bits
    pack_arrived = permute(pack_own, across_y)
    token_cut = small(cut, out_shape=parted)(tokens.transpose(1, 0, 2))
    first_pair, second_pair = small(
        pair_kernel,
        in_specs=[in_vmem] * 2 + [anywhere],
        out_shape=[
            jax.ShapeDtypeStruct((2, rows, first_cols), low),
            jax.ShapeDtypeStruct((2, rows, second_cols), low),
        ],
    )(pack_own, pack_arrived, token_cut)
    cotangent_cut = small(
        cotangent_kernel, in_specs=[in_vmem, anywhere], out_shape=parted
    )(cotangent.transpose(1, 0, 2), first_pair)

    def gather_far(pair):
        return [pair] + [permute(pair, mask) for mask in direct_masks(far_bits)]

    def join(parts, awaited=()):
        count = len(parts) * parts[0].shape[0]
        return small(
            functools.partial(join_kernel, len(parts)),
            in_specs=[in_vmem] * len(parts) + [anywhere] * len(awaited),
            out_shape=jax.ShapeDtypeStruct((count, *parts[0].shape[1:]), low),
        )(*parts, *awaited)

    def gather_rest(held):
        arrived = permute(held, across_x)
        return [held, arrived, permute(held, core_bits[0]), permute(arrived, core_bits[0])]

    first_far = gather_far(first_pair)
    inputs = to_images(after(token_cut, first_far[1:]))
    first_far = join(first_far, [cotangent_cut])
    first_blocks = gather_rest(first_far)
    upstream = to_images(after(cotangent_cut, first_blocks[1:2]))
    second_far = gather_far(second_pair)

    step_rows = PER_STEP * length
    block = (step_rows, width)
    pairs = width // (2 * HEAD_DIM)
    steps = images // PER_STEP
    statics = (images, dp_size, spread)
    wide = scratch(width // 128, total, 128)
    probs_block = (PER_STEP, pairs, length, 2 * length)
    attention_outs = [
        ((total, 3 * width), low, (step_rows, 3 * width)),
        ((images, *probs_block[1:]), low, probs_block),
        ((total, width), low, block),
        ((total, width), high, block),
    ]
    attention_flops = (2 * total * width * 4 * width + 8 * total * length * width) // steps
    attention_scratches = [scratch(length, images), scratch(step_rows, width, dtype=low)]
    *attention, x, w_qkv, w_proj, qkv_t, proj_t = call_kernel(
        first_attention_kernel, statics, 1,
        ["place"] + [None] * 7,
        attention_outs
        + [
            ((total, width), low, None),
            ((width, 3 * width), low, None),
            ((width, width), low, None),
            ((3 * width, width), low, None),
            ((width, width), low, None),
        ],
        [scratch(dp_size * spread, rows, first_cols, dtype=low), wide] + attention_scratches,
        (place, inputs, *first_blocks, keep_mask, vectors),
        attention_flops,
    )
    second_blocks = gather_rest(join(second_far, attention[:1]))
    for first_step, count in ((1, steps - 2), (steps - 1, 1)):
        attention = call_kernel(
            next_attention_kernel, (first_step * PER_STEP,), count,
            [block] + [None] * 4 + ["await"] * len(attention),
            attention_outs, attention_scratches,
            (x, keep_mask, w_qkv, w_proj, vectors, *attention),
            attention_flops * count, first_step=first_step,
            aliases={5 + at: at for at in range(len(attention))},
        )
    qkv, probs, attended, middle = attention
    piece = ((slots * images, width), low, None)
    ff_rows = FF_PER_STEP * length
    ff_block = (ff_rows, width)
    results = call_kernel(
        feed_forward_packed_kernel, statics, images // FF_PER_STEP,
        ["place"] + [None] * 5 + [ff_block, ff_block] + [None] * 2,
        [piece] * spread
        + [
            ((total, width), high, ff_block),
            ((total, width), low, ff_block),
            ((half, rows, second_cols), low, None),
            ((half, rows, second_cols), low, None),
            ((width, width), high, None),
            ((8, width), high, None),
            ((1, hidden), high, None),
        ],
        [
            scratch(width, hidden, dtype=low),
            scratch(hidden, width, dtype=low),
            scratch(hidden, width, dtype=low),
            scratch(dp_size * spread, rows, second_cols, dtype=low),
            scratch(1, hidden),
            wide,
            scratch(ff_rows, width, dtype=low),
            scratch(width, ff_rows, dtype=low),
            scratch(ff_rows, width, dtype=low),
            scratch(width, ff_rows, dtype=low),
            scratch(ff_rows, width),
            scratch(ff_rows, 128),
            scratch(ff_rows, width),
            scratch(ff_rows, width),
            scratch(hidden, width, dtype=low),
            scratch(width, hidden, dtype=low),
            scratch(width, hidden),
            scratch(width, hidden),
        ],
        (
            place, upstream, *second_blocks, middle, attended, proj_t, vectors,
        ),
        12 * total * width * hidden + 4 * total * width * width, total * hidden,
    )
    d_middle, d_attended, ff_keep, ff_leave, proj_total, ff_sums, up_sums = results[spread:]

    def add_parts(count, keep, arrived, awaited):
        part = (keep.shape[0] // count, *keep.shape[1:])
        return small(
            functools.partial(add_kernel, count),
            in_specs=[in_vmem] * 2 + [anywhere] * len(awaited),
            out_specs=[in_vmem] * count,
            out_shape=[jax.ShapeDtypeStruct(part, high)]
            + [jax.ShapeDtypeStruct(part, low)] * (count - 1),
        )(keep, arrived, *awaited)

    ff_first = permute(ff_leave, core_bits[0])
    ff_count = half // 2
    ff_next = add_wide(ff_keep[ff_count:], ff_first[ff_count:]).astype(low)
    ff_arrived = permute(ff_next, across_x)
    output_parts = exchange(results[:spread])
    pack_half = ((half, rows, first_cols), low, None)
    wide_rows = (step_rows, 3 * width)
    d_projected, qkv_keep, qkv_leave, att_sums = call_kernel(
        attention_back_packed_kernel, (dp_size, spread), steps,
        ["place", block, wide_rows, probs_block, block, None, None, "await"],
        [((total, 3 * width), low, wide_rows), pack_half, pack_half, ((8, width), high, None)],
        [scratch(step_rows, width, dtype=low), scratch(width, 3 * width)],
        (place, x, qkv, probs, d_attended, vectors, proj_total, ff_next),
        2 * total * width * 3 * width + 16 * total * length * width,
    )
    qkv_arrived = permute(after(qkv_leave, output_parts[1:]), core_bits[0])
    input_flops = 2 * total * width * 3 * width
    input_ins = [block, wide_rows, block, None, None, None]
    input_outs = [((total, width), low, block), ((8, width), high, None)]
    d_input, att_sums = call_kernel(
        first_input_kernel, (length,), 1, input_ins, input_outs, [scratch(step_rows, width)],
        (x, d_projected, d_middle, qkv_t, vectors, att_sums), input_flops // steps,
    )
    ff_quarter = half // 4
    ff_last = add_wide(
        ff_keep[ff_quarter:ff_count], ff_first[ff_quarter:ff_count], ff_arrived[ff_quarter:]
    ).astype(low)
    ff_last_arrived = permute(ff_last, across_y)
    qkv_held, *leaving = add_parts(4, qkv_keep, qkv_arrived, [ff_last])
    qkv_parts = [permute(part, mask) for part, mask in zip(leaving, direct_masks(near_bits))]
    d_input, att_sums = call_kernel(
        first_input_kernel, (length,), 1, input_ins + ["await"] * 2, input_outs, [scratch(step_rows, width)],
        (x, d_projected, d_middle, qkv_t, vectors, att_sums, d_input, leaving[0]), input_flops // steps,
        first_step=1, aliases={6: 0},
    )
    ff_held = add_wide(
        ff_keep[:ff_quarter], ff_first[:ff_quarter], ff_arrived[:ff_quarter], ff_last_arrived
    )
    qkv_held = add_wide(qkv_held, *qkv_parts)
    blocks = jnp.concatenate([ff_held, qkv_held], axis=2)
    far_leaving = [blocks[at : at + 1].astype(low) for at in range(1, blocks.shape[0])]
    block_parts = [blocks[:1]] + [permute(part, mask) for part, mask in zip(far_leaving, direct_masks(far_bits))]
    results = call_kernel(
        last_input_kernel, (images, spread, length, 2 * PER_STEP), steps - 2,
        ["place"] + input_ins + [None, "await"],
        [piece] * spread + [((8, width), high, None)],
        [wide, scratch(step_rows, width)],
        (place, x, d_projected, d_middle, qkv_t, vectors, att_sums, d_input, far_leaving[0]), input_flops // steps * (steps - 2),
        first_step=2,
    )
    att_sums = results[spread]
    input_pieces = list(results[:spread])
    heights = [master.shape[0] * dp_size for master in masters]
    widths = [master.shape[1] * spread for master in masters]
    rows_old, cols_old = [qkv_rows, proj_rows, up_rows, down_rows], [qkv_cols, proj_cols, up_cols, down_cols]

    def like(*arrays):
        return [jax.ShapeDtypeStruct(array.shape, high) for array in arrays]

    operands = (*block_parts, att_sums, ff_sums, up_sums, *masters, *rows_old)
    *grads, row_sums, message = small(
        functools.partial(gradient_kernel, len(block_parts)),
        out_shape=like(*masters) + [jax.ShapeDtypeStruct((8, rows), high), jax.ShapeDtypeStruct((24, width), high)],
    )(*operands)
    input_pieces[1] = after(input_pieces[1], [row_sums])
    output_parts[0] = after(output_parts[0], [row_sums])
    block_output, settled = settle(output_parts)
    input_grad, input_settled = settle(exchange(input_pieces))
    message = added([message] + [permute(message, mask) for mask in direct_masks((across_x, far_bits[0]))])
    for bit in far_bits[1:-1]:
        message = message + permute(message, bit)
    messages = [message, permute(message, far_bits[-1])]
    col_sums, message = small(
        column_kernel,
        in_specs=[in_vmem] * (1 + len(messages)) + [anywhere],
        out_shape=[
            jax.ShapeDtypeStruct((8, width), high),
            jax.ShapeDtypeStruct((16 + width // 8, 128), high),
        ],
    )(row_sums, *messages, settled)
    messages = [message] + [permute(message, mask) for mask in range(1, spread)]
    operands = (*messages, col_sums, vectors, vector_moment, *grads, *masters, *rows_old, *cols_old)
    results = small(
        functools.partial(update_kernel, len(messages), heights, widths),
        in_specs=[in_vmem] * len(operands) + [anywhere],
        out_shape=like(*masters, *cols_old, *rows_old, vectors, vectors, vectors),
    )(*operands, input_settled)
    news, cols_new, rows_out = results[:4], results[4:8], results[8:12]
    vector_grad, vector_moment_new, vector_new = results[12:]
    factored = []
    for which in range(4):
        factored += [grads[which], rows_out[which], cols_new[which], news[which]]
    return (block_output, input_grad, *factored, vector_grad, vector_moment_new, vector_new)


def body(*arrays):
    spread, dp_size = lax.axis_size("group"), lax.axis_size("dp")
    rows, images = arrays[3].shape[0], arrays[1].shape[0]
    slots, width = arrays[0].shape[1:]
    folds = arrays[6].shape[0] // rows
    powers = all(size & (size - 1) == 0 for size in (spread, dp_size))
    fits = powers and spread == 4 and dp_size > 2
    fits = fits and arrays[5].shape[1] <= width and folds <= 5
    fits = fits and rows % 16 == 0 and images % FF_PER_STEP == 0 and images > 2 * PER_STEP and images % 16 == 0 and slots % 4 == 0
    return packed_body(*arrays) if fits else general_body(*arrays)


def solution(mesh):
    in_specs = (
        P("dp", "group", None),
        P(("dp", "group"), None),
        P("dp", "group", None),
        P("dp", "group"),
        P("dp", "group"),
        P("dp", "group"),
        P("dp", "group"),
        P(),
        P("dp"),
        P("group"),
        P("dp"),
        P("group"),
        P("dp"),
        P("group"),
        P("dp"),
        P("group"),
        P(),
    )
    out_specs = (
        P("dp", "group", None),
        P("dp", "group", None),
        P("dp", "group"),
        P("dp"),
        P("group"),
        P("dp", "group"),
        P("dp", "group"),
        P("dp"),
        P("group"),
        P("dp", "group"),
        P("dp", "group"),
        P("dp"),
        P("group"),
        P("dp", "group"),
        P("dp", "group"),
        P("dp"),
        P("group"),
        P("dp", "group"),
        P(),
        P(),
        P(),
    )
    return jax.shard_map(body, mesh=mesh, in_specs=in_specs, out_specs=out_specs, check_vma=False)
```

```python
import functools
import math

import jax
import jax.numpy as jnp
from jax import lax
from jax.experimental import pallas as pl
from jax.experimental.pallas import tpu as pltpu
from jax.sharding import PartitionSpec as P

HEAD_DIM = 64
STEP_NUMBER = 10


step_rate = 0.3
norm_epsilon = 1e-06
tiny_square = 1e-30
decay_rate = 1.0 - STEP_NUMBER ** (-0.8)
LOG2_E = 1.4426950408889634


def axis_bits(name):
    count = lax.axis_size(name)
    return [(name, 1 << place) for place in range(count.bit_length() - 1)]


def swap_partner(array, step):
    name, bit = step
    count = lax.axis_size(name)
    return lax.ppermute(array, name, [(rank, rank ^ bit) for rank in range(count)])


def upper_side(step):
    name, bit = step
    return (lax.axis_index(name) & bit) != 0


def gather_blocks(array, steps):
    for step in steps:
        arrived = swap_partner(array, step)
        upper = upper_side(step)
        array = jnp.stack([jnp.where(upper, arrived, array), jnp.where(upper, array, arrived)])
    return array


def scatter_sum(array, steps):
    for step in steps:
        upper = upper_side(step)
        leaving = jnp.where(upper, array[0], array[1]).astype(jnp.bfloat16)
        arrived = swap_partner(leaving, step)
        array = jnp.where(upper, array[1], array[0]).astype(jnp.float32) + arrived.astype(jnp.float32)
    return array


def sum_everywhere(array, steps):
    for step in steps:
        array = array + swap_partner(array, step)
    return array


def sum_parts(parts, steps):
    flat = [part.reshape(-1) for part in parts]
    total = sum_everywhere(jnp.concatenate(flat), steps)
    result, start = [], 0
    for part in parts:
        result.append(total[start : start + part.size].reshape(part.shape))
        start += part.size
    return result


def block_order(steps):
    order = []
    for name in ("dp", "group"):
        bits = sorted((step for step in steps if step[0] == name), key=lambda step: -step[1])
        order.append([steps.index(step) for step in bits])
    return order


def blocks_to_whole(blocks, steps):
    count = len(steps)
    rows, cols = blocks.shape[count:]
    dp_axes, group_axes = block_order(steps)
    dp_axes = [count - 1 - axis for axis in dp_axes]
    group_axes = [count - 1 - axis for axis in group_axes]
    whole = blocks.transpose(dp_axes + [count] + group_axes + [count + 1])
    return whole.reshape(rows << len(dp_axes), cols << len(group_axes))


def whole_to_blocks(whole, steps):
    dp_axes, group_axes = block_order(steps)
    rows = whole.shape[0] >> len(dp_axes)
    cols = whole.shape[1] >> len(group_axes)
    split = whole.reshape([2] * len(dp_axes) + [rows] + [2] * len(group_axes) + [cols])
    places = dp_axes + [len(steps)] + group_axes + [len(steps) + 1]
    return split.transpose([places.index(axis) for axis in range(len(places))])


PER_STEP = 4
FF_PER_STEP = 2
SLICE = 48
FF_CHUNK = 256
vmem_bytes = 60 * 1024 * 1024


def dot(left, right, left_axis=1, right_axis=0):
    return lax.dot_general(
        left, right, (((left_axis,), (right_axis,)), ((), ())), preferred_element_type=jnp.float32
    )


def normal_form(values):
    center = jnp.mean(values, axis=-1, keepdims=True)
    centered = values - center
    spread = jnp.mean(centered * centered, axis=-1, keepdims=True)
    scale = lax.rsqrt(spread + norm_epsilon)
    return centered * scale, scale


def norm_back(grad, unit, scale, gain):
    weighted = grad * gain
    along = jnp.mean(weighted * unit, axis=-1, keepdims=True)
    level = jnp.mean(weighted, axis=-1, keepdims=True)
    return scale * (weighted - level - unit * along)


def slices_of(count):
    return [slice(start, start + SLICE) for start in range(0, count, SLICE)]


def fold_rows(values):
    return jnp.sum(values.reshape(values.shape[0] // 8, 8, values.shape[1]), axis=0)


def column_sum(values):
    return jnp.sum(values, axis=0, keepdims=True)


def pair_mask(length):
    return lax.broadcasted_iota(jnp.int32, (length, 2 * HEAD_DIM), 1) < HEAD_DIM


def lane_tiles(count):
    return [slice(start, min(start + 128, count)) for start in range(0, count, 128)]


def stack_heads(pair, first):
    none = jnp.zeros_like(pair)
    return jnp.concatenate([jnp.where(first, pair, none), jnp.where(first, none, pair)], axis=0)


def join_heads(rows, first):
    length = rows.shape[0] // 2
    return jnp.where(first, rows[:length], rows[length:])


def gelu_and_slope(pre):
    bell = jnp.exp2(pre * pre * (-0.5 * LOG2_E))
    base = 1.0 + (0.3275911 * 0.5**0.5) * jnp.abs(pre)
    inverse = pl.reciprocal(base, approx=True)
    inverse = inverse * (2.0 - base * inverse)
    poly = inverse * (
        0.5 * 0.254829592
        + inverse
        * (
            0.5 * -0.284496736
            + inverse
            * (0.5 * 1.421413741 + inverse * (0.5 * -1.453152027 + inverse * (0.5 * 1.061405429)))
        )
    )
    tail = poly * bell
    below = jnp.where(pre >= 0, 1.0 - tail, tail)
    return pre * below, below + pre * bell * 0.3989422804014327


def widen(source_ref, wide_ref, images):
    tiles, total, lanes = wide_ref.shape
    rows_at_once = 8 * images

    @pl.loop(0, total // rows_at_once)
    def _(part):
        rows = pl.ds(pl.multiple_of(part * rows_at_once, rows_at_once), rows_at_once)
        for tile in range(tiles):
            cols = slice(tile * lanes, (tile + 1) * lanes)
            wide_ref[tile, rows, :] = source_ref[rows, cols].astype(jnp.float32)


def narrow(wide_ref, target_ref, images):
    tiles, total, lanes = wide_ref.shape
    rows_at_once = 8 * images

    @pl.loop(0, total // rows_at_once)
    def _(part):
        rows = pl.ds(pl.multiple_of(part * rows_at_once, rows_at_once), rows_at_once)
        for tile in range(tiles):
            cols = slice(tile * lanes, (tile + 1) * lanes)
            target_ref[rows, cols] = wide_ref[tile, rows, :].astype(target_ref.dtype)


def take_image(wide_ref, image, images):
    tiles, total, _ = wide_ref.shape
    rows = pl.ds(image, total // images, images)
    return jnp.concatenate([wide_ref[tile, rows, :] for tile in range(tiles)], axis=1)


def put_image(wide_ref, image, images, values):
    tiles, total, lanes = wide_ref.shape
    rows = pl.ds(image, total // images, images)
    for tile in range(tiles):
        wide_ref[tile, rows, :] = values[:, tile * lanes : (tile + 1) * lanes]


def attention_kernel(
    images, tokens_ref, bias_ref, w_qkv_ref, w_proj_ref, vectors_ref,
    x_ref, qkv_ref, probs_ref, attended_ref, middle_ref, wide_ref, normed_ref,
):
    @pl.when(pl.program_id(0) == 0)
    def _():
        widen(tokens_ref, wide_ref, images)
        to_image_rows(wide_ref, x_ref, images)

    attention_steps(
        x_ref, lambda image: bias_ref[image], w_qkv_ref, w_proj_ref, vectors_ref,
        qkv_ref, probs_ref, attended_ref, middle_ref, normed_ref,
    )


def to_image_rows(wide_ref, x_ref, images):
    length = wide_ref.shape[1] // images

    @pl.loop(0, images)
    def _(image):
        rows = pl.ds(pl.multiple_of(image * length, length), length)
        x_ref[rows, :] = take_image(wide_ref, image, images).astype(jnp.bfloat16)


def attention_steps(
    x_ref, bias_column, w_qkv_ref, w_proj_ref, vectors_ref,
    qkv_ref, probs_ref, attended_ref, middle_ref, normed_ref,
):
    per_step, _, length, _ = probs_ref.shape
    step_rows, width = middle_ref.shape
    base = 0 if x_ref.shape[0] == step_rows else pl.program_id(0) * step_rows

    for rows in slices_of(step_rows):
        x = x_ref[pl.ds(pl.multiple_of(base + rows.start, SLICE), SLICE), :].astype(jnp.float32)
        unit, _ = normal_form(x)
        normed_ref[rows, :] = (unit * vectors_ref[0:1] + vectors_ref[1:2]).astype(jnp.bfloat16)
    for part in range(3):
        cols = slice(part * width, (part + 1) * width)
        projected = dot(normed_ref[...], w_qkv_ref[:, cols])
        if part != 1:
            row = 2 if part == 0 else 3
            projected = projected + vectors_ref[row : row + 1]
        qkv_ref[:, cols] = projected.astype(jnp.bfloat16)

    pairs = width // (2 * HEAD_DIM)
    first = pair_mask(length)
    place = lax.broadcasted_iota(jnp.int32, (length, 2 * length), 0)
    asker = lax.broadcasted_iota(jnp.int32, (length, 2 * length), 1)
    own = place == jnp.where(asker >= length, asker - length, asker)

    def scores_of(image):
        rows = slice(image * length, (image + 1) * length)
        result = []
        for pair in range(pairs):
            low = pair * 2 * HEAD_DIM
            queries = stack_heads(qkv_ref[rows, low : low + 2 * HEAD_DIM], first)
            result.append(dot(qkv_ref[rows, width + low : width + low + 2 * HEAD_DIM], queries, 1, 1))
        return result

    next_scores = scores_of(0)
    for image in range(per_step):
        rows = slice(image * length, (image + 1) * length)
        all_scores = next_scores
        if image + 1 < per_step:
            next_scores = scores_of(image + 1)
        column = bias_column(image)
        for cols in lane_tiles(2 * length):
            bias = jnp.where(own[:, cols], 0.0, column)
            for pair in range(pairs):
                scores = all_scores[pair][:, cols] * (HEAD_DIM**-0.5 * LOG2_E) + bias
                weights = jnp.exp2(scores - jnp.max(scores, axis=0, keepdims=True))
                probs = weights * (1.0 / jnp.sum(weights, axis=0, keepdims=True))
                probs_ref[image, pair, :, cols] = probs.astype(jnp.bfloat16)
        for pair in range(pairs):
            low = pair * 2 * HEAD_DIM
            values = qkv_ref[rows, 2 * width + low : 2 * width + low + 2 * HEAD_DIM]
            attended = join_heads(dot(probs_ref[image, pair], values, 0, 0), first)
            attended_ref[rows, low : low + 2 * HEAD_DIM] = attended.astype(jnp.bfloat16)

    middle_ref[...] = (
        x_ref[pl.ds(pl.multiple_of(base, length), step_rows), :].astype(jnp.float32)
        + dot(attended_ref[...], w_proj_ref[...])
        + vectors_ref[4:5]
    )


def feed_forward_kernel(
    images, middle_ref, cotangent_ref, attended_ref, w_up_ref, w_down_ref, proj_t_ref, vectors_ref, bias_up_ref,
    output_ref, d_middle_ref, d_attended_ref, up_grad_ref, down_grad_ref, proj_grad_ref, vector_sums_ref, up_sums_ref,
    wide_ref, *scratches,
):
    up_total_ref, down_total_ref, proj_total_ref = scratches[-3:]

    @pl.when(pl.program_id(0) == 0)
    def _():
        widen(cotangent_ref, wide_ref, images)

    feed_forward_steps(
        images, middle_ref, attended_ref, w_up_ref, w_down_ref, proj_t_ref, vectors_ref, bias_up_ref,
        d_middle_ref, d_attended_ref, vector_sums_ref, up_sums_ref, wide_ref, *scratches,
    )

    @pl.when(pl.program_id(0) == pl.num_programs(0) - 1)
    def _():
        narrow(wide_ref, output_ref, images)
        up_grad_ref[...] = up_total_ref[...].astype(jnp.bfloat16)
        down_grad_ref[...] = down_total_ref[...].T.astype(jnp.bfloat16)
        proj_grad_ref[...] = proj_total_ref[...].astype(jnp.bfloat16)


def feed_forward_steps(
    images, middle_ref, attended_ref, w_up_ref, w_down_ref, proj_t_ref, vectors_ref, bias_up_ref,
    d_middle_ref, d_attended_ref, vector_sums_ref, up_sums_ref,
    wide_ref, normed_ref, normed_t_ref, dy_ref, dy_t_ref, unit_ref, scale_ref, ahead_ref, back_ref,
    up_t_ref, down_t_ref, up_total_ref, down_total_ref, proj_total_ref,
):
    step = pl.program_id(0)
    length = wide_ref.shape[1] // images
    hidden = w_up_ref.shape[1]
    per_step = middle_ref.shape[0] // length

    @pl.when(step == 0)
    def _():
        for total in (up_total_ref, down_total_ref, proj_total_ref, vector_sums_ref, up_sums_ref):
            total[...] = jnp.zeros_like(total)
        up_t_ref[...] = w_up_ref[...].T
        down_t_ref[...] = w_down_ref[...].T

    for image in range(per_step):
        rows = slice(image * length, (image + 1) * length)
        dy = take_image(wide_ref, step * per_step + image, images)
        dy_ref[rows, :] = dy.astype(jnp.bfloat16)
        vector_sums_ref[3:4] += column_sum(dy)
        unit, scale = normal_form(middle_ref[rows, :])
        unit_ref[rows, :] = unit
        scale_ref[rows, :] = jnp.broadcast_to(scale, (length, scale_ref.shape[1]))
        normed_ref[rows, :] = (unit * vectors_ref[5:6] + vectors_ref[6:7]).astype(jnp.bfloat16)
    normed_t_ref[...] = normed_ref[...].T
    dy_t_ref[...] = dy_ref[...].T
    chunks = hidden // FF_CHUNK

    def cols_of(chunk):
        return slice(chunk * FF_CHUNK, (chunk + 1) * FF_CHUNK)

    def into(chunk):
        cols = cols_of(chunk)
        pre = dot(normed_ref[...], w_up_ref[:, cols])
        return pre + bias_up_ref[:, cols], dot(dy_ref[...], down_t_ref[:, cols])

    def across(pre, d_active):
        active, slope = gelu_and_slope(pre)
        return active.astype(jnp.bfloat16), (d_active * slope).astype(jnp.bfloat16)

    def out_of(chunk, active, d_hidden):
        cols = cols_of(chunk)
        ahead, back = dot(active, w_down_ref[cols, :]), dot(d_hidden, up_t_ref[cols, :])
        if chunk == 0:
            ahead_ref[...] = ahead
            back_ref[...] = back
        else:
            ahead_ref[...] += ahead
            back_ref[...] += back
        down_total_ref[:, cols] += dot(dy_t_ref[...], active)
        up_total_ref[:, cols] += dot(normed_t_ref[...], d_hidden)
        up_sums_ref[:, cols] += column_sum(d_hidden.astype(jnp.float32))

    entered, crossed = into(0), None
    for chunk in range(chunks + 1):
        next_entered = into(chunk + 1) if chunk + 1 < chunks else None
        next_crossed = across(*entered) if chunk < chunks else None
        if crossed is not None:
            out_of(chunk - 1, *crossed)
        entered, crossed = next_entered, next_crossed

    for image in range(per_step):
        rows = slice(image * length, (image + 1) * length)
        output = middle_ref[rows, :] + ahead_ref[rows, :] + vectors_ref[11:12]
        put_image(wide_ref, step * per_step + image, images, output)
        unit = unit_ref[rows, :]
        grad = back_ref[rows, :]
        vector_sums_ref[1:2] += column_sum(grad * unit)
        vector_sums_ref[2:3] += column_sum(grad)
        d_middle = dy_ref[rows, :].astype(jnp.float32) + norm_back(
            grad, unit, scale_ref[rows, 0:1], vectors_ref[5:6]
        )
        d_middle_ref[rows, :] = d_middle
        d_branch = d_middle.astype(jnp.bfloat16)
        dy_ref[rows, :] = d_branch
        vector_sums_ref[0:1] += column_sum(d_branch.astype(jnp.float32))
    proj_total_ref[...] += dot(attended_ref[...], dy_ref[...], 0, 0)
    d_attended_ref[...] = dot(dy_ref[...], proj_t_ref[...]).astype(jnp.bfloat16)


def attention_back_kernel(
    images, x_ref, qkv_ref, probs_ref, d_attended_ref, d_middle_ref, qkv_t_ref, vectors_ref,
    input_grad_ref, qkv_grad_ref, vector_sums_ref, wide_ref, normed_ref, d_projected_ref, back_ref, qkv_total_ref,
):
    @pl.when(pl.program_id(0) == 0)
    def _():
        qkv_total_ref[...] = jnp.zeros_like(qkv_total_ref)
        vector_sums_ref[...] = jnp.zeros_like(vector_sums_ref)

    def put(image, rows, values):
        put_image(wide_ref, image, images, values)

    attention_back_steps(
        x_ref, qkv_ref, probs_ref, d_attended_ref, vectors_ref, vector_sums_ref, normed_ref, d_projected_ref, qkv_total_ref
    )
    input_back_steps(
        put, probs_ref.shape[2], x_ref, d_projected_ref, d_middle_ref, qkv_t_ref, vectors_ref, vector_sums_ref, back_ref
    )

    @pl.when(pl.program_id(0) == pl.num_programs(0) - 1)
    def _():
        narrow(wide_ref, input_grad_ref, images)
        qkv_grad_ref[...] = qkv_total_ref[...].astype(jnp.bfloat16)


def attention_back_steps(
    x_ref, qkv_ref, probs_ref, d_attended_ref, vectors_ref, vector_sums_ref, normed_ref, d_projected_ref, qkv_total_ref
):
    width = x_ref.shape[1]
    length = probs_ref.shape[2]
    per_step = probs_ref.shape[0]

    pairs = width // (2 * HEAD_DIM)
    first = pair_mask(length)
    scale = HEAD_DIM**-0.5

    def places(image, pair):
        low = pair * 2 * HEAD_DIM
        rows = slice(image * length, (image + 1) * length)
        return rows, [slice(part * width + low, part * width + low + 2 * HEAD_DIM) for part in range(3)]

    def entering(image):
        result = []
        for pair in range(pairs):
            rows, cols = places(image, pair)
            d_attended = stack_heads(d_attended_ref[rows, cols[0]], first)
            d_values = dot(probs_ref[image, pair], d_attended)
            d_projected_ref[rows, cols[2]] = d_values.astype(jnp.bfloat16)
            result.append(dot(qkv_ref[rows, cols[2]], d_attended, 1, 1))
        return result

    next_probs = entering(0)
    for image in range(per_step):
        all_d_probs = next_probs
        if image + 1 < per_step:
            next_probs = entering(image + 1)
        all_d_scores = []
        for pair in range(pairs):
            parts = []
            for cols in lane_tiles(2 * length):
                probs, d_probs = probs_ref[image, pair, :, cols].astype(jnp.float32), all_d_probs[pair][:, cols]
                along = jnp.sum(d_probs * probs, axis=0, keepdims=True)
                parts.append((probs * (d_probs - along)).astype(jnp.bfloat16))
            all_d_scores.append(jnp.concatenate(parts, axis=1))
        for pair in range(pairs):
            rows, cols = places(image, pair)
            d_scores = all_d_scores[pair]
            queries = stack_heads(qkv_ref[rows, cols[0]], first)
            d_queries = join_heads(dot(d_scores, qkv_ref[rows, cols[1]], 0, 0), first) * scale
            d_projected_ref[rows, cols[0]] = d_queries.astype(jnp.bfloat16)
            d_projected_ref[rows, cols[1]] = (dot(d_scores, queries) * scale).astype(jnp.bfloat16)

    query_sums = value_sums = jnp.zeros((8, width), jnp.float32)
    for rows in slices_of(x_ref.shape[0]):
        query_sums += fold_rows(d_projected_ref[rows, :width].astype(jnp.float32))
        value_sums += fold_rows(d_projected_ref[rows, 2 * width :].astype(jnp.float32))
        unit, _ = normal_form(x_ref[rows, :].astype(jnp.float32))
        normed_ref[rows, :] = (unit * vectors_ref[0:1] + vectors_ref[1:2]).astype(jnp.bfloat16)
    vector_sums_ref[2:3] += column_sum(query_sums)
    vector_sums_ref[3:4] += column_sum(value_sums)
    qkv_total_ref[...] += dot(normed_ref[...], d_projected_ref[...], 0, 0)


def input_back_steps(
    put, length, x_ref, d_projected_ref, d_middle_ref, qkv_t_ref, vectors_ref, vector_sums_ref, back_ref
):
    step = pl.program_id(0)
    per_step = x_ref.shape[0] // length
    back_ref[...] = dot(d_projected_ref[...], qkv_t_ref[...])
    gain_sums = shift_sums = jnp.zeros((8, x_ref.shape[1]), jnp.float32)
    for rows in slices_of(x_ref.shape[0]):
        unit, scale = normal_form(x_ref[rows, :].astype(jnp.float32))
        grad = back_ref[rows, :]
        gain_sums += fold_rows(grad * unit)
        shift_sums += fold_rows(grad)
        back_ref[rows, :] = d_middle_ref[rows, :] + norm_back(grad, unit, scale, vectors_ref[0:1])
    vector_sums_ref[0:1] += column_sum(gain_sums)
    vector_sums_ref[1:2] += column_sum(shift_sums)
    for image in range(per_step):
        rows = slice(image * length, (image + 1) * length)
        put(step * per_step + image, rows, back_ref[rows, :])


def whole_block(shape):
    return pl.BlockSpec(shape, lambda step: (0,) * len(shape))


def step_block(shape, first=0):
    return pl.BlockSpec(shape, lambda step: (first + step,) + (0,) * (len(shape) - 1))


def scratch(*shape, dtype=jnp.float32):
    return pltpu.VMEM(shape, dtype)


def call_kernel(kernel, statics, steps, ins, outs, scratches, operands, flops, transcendentals=0, first_step=0, aliases={}):
    in_specs = [
        pl.BlockSpec(memory_space=pltpu.SMEM)
        if block == "place"
        else pl.BlockSpec(memory_space=pl.ANY)
        if block == "await"
        else whole_block(op.shape) if block is None else step_block(block, first_step)
        for op, block in zip(operands, ins)
    ]
    out_specs = [
        whole_block(shape) if block is None else step_block(block, first_step) for shape, dtype, block in outs
    ]
    moved = sum(op.size * op.dtype.itemsize for op in operands) + sum(
        math.prod(shape) * jnp.dtype(dtype).itemsize for shape, dtype, block in outs
    )
    return pl.pallas_call(
        functools.partial(kernel, *statics),
        grid=(steps,),
        in_specs=in_specs,
        out_specs=out_specs,
        out_shape=[jax.ShapeDtypeStruct(shape, dtype) for shape, dtype, block in outs],
        scratch_shapes=scratches,
        input_output_aliases=aliases,
        compiler_params=pltpu.CompilerParams(vmem_limit_bytes=vmem_bytes),
        cost_estimate=pl.CostEstimate(
            flops=flops * 8, bytes_accessed=moved, transcendentals=transcendentals
        ),
    )(*operands)


def attention_forward(tokens, bias, w_qkv, w_proj, vectors):
    images, length, _ = bias.shape
    total, width = tokens.shape
    pairs = width // (2 * HEAD_DIM)
    rows = PER_STEP * length
    low, high = jnp.bfloat16, jnp.float32
    outs = [
        ((total, width), low, None),
        ((total, 3 * width), low, (rows, 3 * width)),
        ((images, pairs, length, 2 * length), low, (PER_STEP, pairs, length, 2 * length)),
        ((total, width), low, (rows, width)),
        ((total, width), high, (rows, width)),
    ]
    return call_kernel(
        attention_kernel, (images,), images // PER_STEP,
        [None, (PER_STEP, length, 1), None, None, None], outs,
        [scratch(width // 128, total, 128), scratch(rows, width, dtype=low)],
        (tokens, bias, w_qkv, w_proj, vectors),
        2 * total * width * 4 * width + 8 * total * length * width,
    )


def feed_forward(images, middle, cotangent, attended, w_up, w_down, w_proj, vectors):
    total, width = middle.shape
    hidden = w_up.shape[1]
    rows = total // images * FF_PER_STEP
    low, high = jnp.bfloat16, jnp.float32
    block = (rows, width)
    outs = [
        ((total, width), low, None),
        ((total, width), high, block),
        ((total, width), low, block),
        ((width, hidden), low, None),
        ((hidden, width), low, None),
        ((width, width), low, None),
        ((8, width), high, None),
        ((1, hidden), high, None),
    ]
    scratches = [
        scratch(width // 128, total, 128),
        scratch(rows, width, dtype=low),
        scratch(width, rows, dtype=low),
        scratch(rows, width, dtype=low),
        scratch(width, rows, dtype=low),
        scratch(rows, width),
        scratch(rows, 128),
        scratch(rows, width),
        scratch(rows, width),
        scratch(hidden, width, dtype=low),
        scratch(width, hidden, dtype=low),
        scratch(width, hidden),
        scratch(width, hidden),
        scratch(width, width),
    ]
    return call_kernel(
        feed_forward_kernel, (images,), images // FF_PER_STEP,
        [block, None, block, None, None, None, None, None], outs, scratches,
        (middle, cotangent, attended, w_up, w_down, w_proj.T, vectors, vectors[7:11].reshape(1, hidden)),
        12 * total * width * hidden + 4 * total * width * width, total * hidden,
    )


def attention_back(x, qkv, probs, d_attended, d_middle, w_qkv, vectors):
    images, pairs, length, _ = probs.shape
    total, width = x.shape
    rows = PER_STEP * length
    low, high = jnp.bfloat16, jnp.float32
    block = (rows, width)
    outs = [
        ((total, width), low, None),
        ((width, 3 * width), low, None),
        ((8, width), high, None),
    ]
    scratches = [
        scratch(width // 128, total, 128),
        scratch(rows, width, dtype=low),
        scratch(rows, 3 * width, dtype=low),
        scratch(rows, width),
        scratch(width, 3 * width),
    ]
    return call_kernel(
        attention_back_kernel, (images,), images // PER_STEP,
        [block, (rows, 3 * width), (PER_STEP, pairs, length, 2 * length), block, block, None, None],
        outs, scratches, (x, qkv, probs, d_attended, d_middle, w_qkv.T, vectors),
        4 * total * width * 3 * width + 16 * total * length * width,
    )

def linear_place():
    return lax.axis_index("dp") * lax.axis_size("group") + lax.axis_index("group")


def permute(array, mask):
    count = lax.axis_size("dp") * lax.axis_size("group")
    return lax.ppermute(array, ("dp", "group"), [(rank, rank ^ mask) for rank in range(count)])


def direct_masks(bits):
    masks = [0]
    for bit in bits:
        masks = masks + [mask | bit for mask in masks]
    return masks[1:]


def add_wide(first, *rest):
    total = first.astype(jnp.float32)
    for part in rest:
        total = total + part.astype(jnp.float32)
    return total


def packed_place(mask, spread, count):
    return ((mask >> 1) & (spread - 1)) * (count // (2 * spread)) + (mask >> (spread.bit_length()))


def scatter_step(held, bits):
    masks = direct_masks(bits)
    size = held.shape[0] // (len(masks) + 1)
    parts = [
        permute(held[size * (at + 1) : size * (at + 2)].astype(jnp.bfloat16), mask)
        for at, mask in enumerate(masks)
    ]
    return held[:size], parts


def add_wide(first, *rest):
    total = first.astype(jnp.float32)
    for part in rest:
        total = total + part.astype(jnp.float32)
    return total


def packed_place(mask, spread, count):
    return ((mask >> 1) & (spread - 1)) * (count // (2 * spread)) + (mask >> (spread.bit_length()))


def gather_step(held, bits):
    return held + [permute(part, mask) for mask in direct_masks(bits) for part in held]


def gathered_place(mask, count):
    return (mask & 1) * (count // 2) + ((mask >> 2) & 1) * (count // 4) + (mask >> 3) * 2 + ((mask >> 1) & 1)


def unpack(place_ref, block_refs, packed_ref, put, dp_size, spread):
    place = place_ref[0]
    size = block_refs[0].shape[0]
    for at, block_ref in enumerate(block_refs):
        packed_ref[at * size : (at + 1) * size] = block_ref[...]
    count = dp_size * spread
    for row in range(dp_size):
        for col in range(spread):
            put(row, col, packed_ref[gathered_place((row * spread + col) ^ place, count)])


def pack(place_ref, take, keep_ref, leave_ref, dp_size, spread):
    place = place_ref[0]
    odd = (place & 1) == 1
    for row in range(dp_size):
        for col in range(0, spread, 2):
            at = packed_place((row * spread + col) ^ place, spread, dp_size * spread)
            even_block, odd_block = take(row, col), take(row, col + 1)
            keep_ref[at] = jnp.where(odd, odd_block, even_block)
            leave_ref[at] = jnp.where(odd, even_block, odd_block)


def narrow_pieces(place_ref, wide_ref, piece_refs, spread):
    tiles, _, lanes = wide_ref.shape
    rows_of_piece = piece_refs[0].shape[0]
    step = 64
    group = place_ref[0] & (spread - 1)
    for relative, piece_ref in enumerate(piece_refs):
        base = (group ^ relative) * rows_of_piece

        @pl.loop(0, rows_of_piece // step)
        def _(part):
            target = pl.ds(pl.multiple_of(part * step, step), step)
            source = pl.ds(pl.multiple_of(base + part * step, step), step)
            for tile in range(tiles):
                cols = slice(tile * lanes, (tile + 1) * lanes)
                piece_ref[target, cols] = wide_ref[tile, source, :].astype(jnp.bfloat16)


def general_body(
    tokens,
    keep_mask,
    cotangent,
    qkv_weight,
    proj_weight,
    up_weight,
    down_weight,
    vectors,
    qkv_rows,
    qkv_cols,
    proj_rows,
    proj_cols,
    up_rows,
    up_cols,
    down_rows,
    down_cols,
    vector_moment,
):
    masters = (qkv_weight, proj_weight, up_weight, down_weight)
    lowered = tuple((master.astype(jnp.bfloat16) for master in masters))
    dp_bits, group_bits = axis_bits("dp"), axis_bits("group")
    gather_steps = dp_bits[1:] + group_bits[1:] + dp_bits[:1] + group_bits[:1]
    scatter_steps = gather_steps[::-1]
    w_qkv, w_proj, w_up, w_down = tuple(
        blocks_to_whole(gather_blocks(part, gather_steps), gather_steps) for part in lowered
    )
    spread = lax.axis_size("group")

    def slots_in(array):
        held, slots, width = array.shape
        parts = array.transpose(1, 0, 2).reshape(slots, spread, held // spread, width)
        parts = lax.all_to_all(
            parts.transpose(1, 0, 2, 3), "group", split_axis=0, concat_axis=0, tiled=True
        )
        return parts.reshape(spread * slots * (held // spread), width)

    def slots_out(array):
        held, slots, width = tokens.shape
        parts = array.reshape(spread, slots, held // spread, width)
        parts = lax.all_to_all(parts, "group", split_axis=0, concat_axis=0, tiled=True)
        return parts.transpose(1, 0, 2, 3).reshape(slots, held, width).transpose(1, 0, 2)

    images = keep_mask.shape[0]
    bias = jnp.where(keep_mask > 0, 0.0, -1e30)[:, :, None]
    x, qkv, probs, attended, middle = attention_forward(
        slots_in(tokens), bias, w_qkv, w_proj, vectors
    )
    output, d_middle, d_attended, up_grad, down_grad, proj_grad, ff_sums, up_sums = feed_forward(
        images, middle, slots_in(cotangent), attended, w_up, w_down, w_proj, vectors
    )
    block_output = slots_out(output)
    d_input, qkv_grad, att_sums = attention_back(
        x, qkv, probs, d_attended, d_middle, w_qkv, vectors
    )
    input_grad = slots_out(d_input)
    local_vectors = jnp.concatenate(
        [att_sums[:4], ff_sums[:3], up_sums.reshape(4, -1), ff_sums[3:4]], axis=0
    )
    vector_grad = sum_everywhere(local_vectors, group_bits + dp_bits)
    local_grads = (qkv_grad, proj_grad, up_grad, down_grad)
    owned = tuple(
        scatter_sum(whole_to_blocks(part, scatter_steps), scatter_steps) for part in local_grads
    )
    squares = tuple((gradient * gradient + tiny_square for gradient in owned))
    row_parts = tuple((jnp.sum(square, axis=1) for square in squares)) + tuple(
        (jnp.sum(master * master, axis=1) for master in masters)
    )
    row_sums = sum_parts(row_parts, group_bits)
    rows_old = (qkv_rows, proj_rows, up_rows, down_rows)
    cols_old = (qkv_cols, proj_cols, up_cols, down_cols)
    total_cols = tuple((gradient.shape[1] * lax.axis_size("group") for gradient in owned))
    total_rows = tuple((gradient.shape[0] * lax.axis_size("dp") for gradient in owned))
    rows_new = tuple(
        (
            decay_rate * rows_old[which] + (1.0 - decay_rate) * row_sums[which] / total_cols[which]
            for which in range(4)
        )
    )
    col_parts = (
        tuple((jnp.sum(square, axis=0) for square in squares))
        + tuple((jnp.sum(row_stat) for row_stat in rows_new))
        + tuple((jnp.sum(row_sums[4 + which]) for which in range(4)))
    )
    col_sums = sum_parts(col_parts, dp_bits)
    results = []
    for which in range(4):
        cols_new = (
            decay_rate * cols_old[which] + (1.0 - decay_rate) * col_sums[which] / total_rows[which]
        )
        mean_rows = col_sums[4 + which] / total_rows[which]
        spread = jnp.sqrt(col_sums[8 + which] / (total_rows[which] * total_cols[which]))
        second = rows_new[which][:, None] * cols_new[None, :] / mean_rows
        updated = masters[which] - step_rate * spread * owned[which] * lax.rsqrt(second)
        results.append((owned[which], rows_new[which], cols_new, updated))
    vector_moment_new = decay_rate * vector_moment + (1.0 - decay_rate) * (
        vector_grad * vector_grad + tiny_square
    )
    row_spread = jnp.sqrt(jnp.mean(vectors * vectors, axis=1, keepdims=True))
    vector_new = vectors - step_rate * row_spread * vector_grad * lax.rsqrt(vector_moment_new)
    return (
        block_output,
        input_grad,
        results[0][0],
        results[0][1],
        results[0][2],
        results[0][3],
        results[1][0],
        results[1][1],
        results[1][2],
        results[1][3],
        results[2][0],
        results[2][1],
        results[2][2],
        results[2][3],
        results[3][0],
        results[3][1],
        results[3][2],
        results[3][3],
        vector_grad,
        vector_moment_new,
        vector_new,
    )


def first_attention_kernel(images, dp_size, spread, place_ref, tokens_ref, *refs):
    blocks, refs = refs[:4], refs[4:]
    keep_ref, vectors_ref, *outs, x_ref, w_qkv_ref, w_proj_ref, qkv_t_ref, proj_t_ref = refs[:-4]
    packed_ref, wide_ref, bias_ref, normed_ref = refs[-4:]
    rows = packed_ref.shape[1]
    qkv_cols, proj_cols = w_qkv_ref.shape[1] // spread, w_proj_ref.shape[1] // spread

    @pl.when(pl.program_id(0) == 0)
    def _():
        widen(tokens_ref, wide_ref, images)
        to_image_rows(wide_ref, x_ref, images)

        def put(row, col, block):
            down = slice(row * rows, (row + 1) * rows)
            w_qkv_ref[down, col * qkv_cols : (col + 1) * qkv_cols] = block[:, :qkv_cols]
            w_proj_ref[down, col * proj_cols : (col + 1) * proj_cols] = block[:, qkv_cols:]

        unpack(place_ref, blocks, packed_ref, put, dp_size, spread)
        qkv_t_ref[...] = w_qkv_ref[...].T
        proj_t_ref[...] = w_proj_ref[...].T

    attention_part(0, x_ref, keep_ref, w_qkv_ref, w_proj_ref, vectors_ref, *outs, bias_ref, normed_ref)


def next_attention_kernel(start, x_ref, keep_ref, w_qkv_ref, w_proj_ref, vectors_ref, *refs):
    attention_part(start, x_ref, keep_ref, w_qkv_ref, w_proj_ref, vectors_ref, *refs[-6:])


def attention_part(
    start, x_ref, keep_ref, w_qkv_ref, w_proj_ref, vectors_ref,
    qkv_ref, probs_ref, attended_ref, middle_ref, bias_ref, normed_ref,
):
    @pl.when(pl.program_id(0) == 0)
    def _():
        bias_ref[...] = jnp.where(keep_ref[...] > 0, 0.0, -1e30).T

    def bias_column(image):
        here = start + pl.program_id(0) * probs_ref.shape[0] + image
        lane = lax.broadcasted_iota(jnp.int32, bias_ref.shape, 1)
        return row_sum(jnp.where(lane == here, bias_ref[...], 0.0))

    attention_steps(
        x_ref, bias_column, w_qkv_ref, w_proj_ref, vectors_ref,
        qkv_ref, probs_ref, attended_ref, middle_ref, normed_ref,
    )


def feed_forward_packed_kernel(images, dp_size, spread, place_ref, *refs):
    cotangent_ref, blocks, refs = refs[0], refs[1:5], refs[5:]
    middle_ref, attended_ref, proj_t_ref, vectors_ref = refs[:4]
    outputs, refs = refs[4 : 4 + spread], refs[4 + spread :]
    d_middle_ref, d_attended_ref, keep_ref, leave_ref, proj_total_ref, vector_sums_ref, up_sums_ref = refs[:7]
    w_up_ref, w_down_ref, down_low_ref, packed_ref, bias_up_ref, wide_ref = refs[7:13]
    scratches = refs[13:]
    width = w_up_ref.shape[0]
    up_total_ref, down_total_ref = scratches[-2:]
    rows = packed_ref.shape[1]
    up_cols = w_up_ref.shape[1] // spread
    out_cols = w_down_ref.shape[1] // spread
    folds = w_down_ref.shape[0] // w_up_ref.shape[0]

    @pl.when(pl.program_id(0) == 0)
    def _():
        widen(cotangent_ref, wide_ref, images)
        for fold in range(bias_up_ref.shape[1] // width):
            bias_up_ref[:, fold * width : (fold + 1) * width] = vectors_ref[7 + fold : 8 + fold]

        def put(row, col, block):
            w_up_ref[row * rows : (row + 1) * rows, col * up_cols : (col + 1) * up_cols] = block[:, :up_cols]
            for fold in range(folds):
                down = (row * folds + fold) * rows
                start = up_cols + fold * out_cols
                w_down_ref[down : down + rows, col * out_cols : (col + 1) * out_cols] = block[
                    :, start : start + out_cols
                ]

        unpack(place_ref, blocks, packed_ref, put, dp_size, spread)

    feed_forward_steps(
        images, middle_ref, attended_ref, w_up_ref, w_down_ref, proj_t_ref, vectors_ref, bias_up_ref,
        d_middle_ref, d_attended_ref, vector_sums_ref, up_sums_ref, wide_ref, *scratches, proj_total_ref,
    )

    @pl.when(pl.program_id(0) == pl.num_programs(0) - 1)
    def _():
        narrow_pieces(place_ref, wide_ref, outputs, spread)
        down_low_ref[...] = down_total_ref[...].T.astype(jnp.bfloat16)

        def take(row, col):
            across = slice(row * rows, (row + 1) * rows)
            cols = slice(col * out_cols, (col + 1) * out_cols)
            parts = [up_total_ref[across, col * up_cols : (col + 1) * up_cols].astype(jnp.bfloat16)]
            for fold in range(folds):
                down = (row * folds + fold) * rows
                parts.append(down_low_ref[down : down + rows, cols])
            return jnp.concatenate(parts, axis=1)

        pack(place_ref, take, keep_ref, leave_ref, dp_size, spread)


def attention_back_packed_kernel(
    dp_size, spread, place_ref, x_ref, qkv_ref, probs_ref, d_attended_ref, vectors_ref, proj_total_ref, _,
    d_projected_ref, keep_ref, leave_ref, vector_sums_ref, normed_ref, total_ref,
):
    @pl.when(pl.program_id(0) == 0)
    def _():
        total_ref[...] = jnp.zeros_like(total_ref)
        vector_sums_ref[...] = jnp.zeros_like(vector_sums_ref)

    attention_back_steps(
        x_ref, qkv_ref, probs_ref, d_attended_ref, vectors_ref, vector_sums_ref, normed_ref, d_projected_ref, total_ref
    )

    @pl.when(pl.program_id(0) == pl.num_programs(0) - 1)
    def _():
        rows = keep_ref.shape[1]
        qkv_cols, proj_cols = total_ref.shape[1] // spread, proj_total_ref.shape[1] // spread

        def take(row, col):
            down = slice(row * rows, (row + 1) * rows)
            parts = [
                total_ref[down, col * qkv_cols : (col + 1) * qkv_cols],
                proj_total_ref[down, col * proj_cols : (col + 1) * proj_cols],
            ]
            return jnp.concatenate(parts, axis=1).astype(jnp.bfloat16)

        pack(place_ref, take, keep_ref, leave_ref, dp_size, spread)


def first_input_kernel(
    length, x_ref, d_projected_ref, d_middle_ref, qkv_t_ref, vectors_ref, before_ref, *refs
):
    d_input_ref, vector_sums_ref, back_ref = refs[-3:]

    @pl.when(pl.program_id(0) == 0)
    def _():
        vector_sums_ref[...] = before_ref[...]

    def put(image, rows, values):
        d_input_ref[rows, :] = values.astype(jnp.bfloat16)

    input_back_steps(
        put, length, x_ref, d_projected_ref, d_middle_ref, qkv_t_ref, vectors_ref, vector_sums_ref, back_ref
    )


def last_input_kernel(
    images, spread, length, first, place_ref, x_ref, d_projected_ref, d_middle_ref, qkv_t_ref, vectors_ref, before_ref,
    d_input_ref, _, *refs,
):
    pieces, (vector_sums_ref, wide_ref, back_ref) = refs[:spread], refs[spread:]

    @pl.when(pl.program_id(0) == 0)
    def _():
        vector_sums_ref[...] = before_ref[...]
        for image in range(first):
            rows = slice(image * length, (image + 1) * length)
            put_image(wide_ref, image, images, d_input_ref[rows, :].astype(jnp.float32))

    def put(image, rows, values):
        put_image(wide_ref, first + image, images, values)

    input_back_steps(
        put, length, x_ref, d_projected_ref, d_middle_ref, qkv_t_ref, vectors_ref, vector_sums_ref, back_ref
    )

    @pl.when(pl.program_id(0) == pl.num_programs(0) - 1)
    def _():
        narrow_pieces(place_ref, wide_ref, pieces, spread)


def cut(array_ref, parts_ref):
    count = parts_ref.shape[2]
    for member in range(parts_ref.shape[0]):
        parts_ref[member] = array_ref[:, member * count : (member + 1) * count, :]


def pack_kernel(qkv_ref, proj_ref, up_ref, down_ref, pack_ref):
    rows, start = pack_ref.shape[0], 0
    parts = [qkv_ref[...], proj_ref[...], up_ref[...]]
    parts += [down_ref[fold * rows : (fold + 1) * rows, :] for fold in range(down_ref.shape[0] // rows)]
    for part in parts:
        pack_ref[:, start : start + part.shape[1]] = part.astype(jnp.bfloat16)
        start += part.shape[1]


def token_kernel(array_ref, own_ref, arrived_ref, _, parts_ref, first_ref, second_ref):
    start = first_ref.shape[2]
    for at, pack_ref in enumerate((own_ref, arrived_ref)):
        first_ref[at] = pack_ref[:, :start]
        second_ref[at] = pack_ref[:, start:]
    cut(array_ref, parts_ref)


def join_kernel(count, *refs):
    size = refs[0].shape[0]
    for at, part_ref in enumerate(refs[:count]):
        refs[-1][at * size : (at + 1) * size] = part_ref[...]


def settle_kernel(spread, place_ref, *refs):
    lists, (output_ref, token_ref) = refs[:-2], refs[-2:]
    token_ref[...] = jnp.zeros_like(token_ref)
    group = place_ref[0] & (spread - 1)
    count = lists[0].shape[1]
    share = len(lists) // spread * count
    for at, piece_ref in enumerate(lists):
        relative, part = at % spread, at // spread
        start = pl.multiple_of((group ^ relative) * share + part * count, count)
        output_ref[:, pl.ds(start, count), :] = piece_ref[...]


def lane_table(rows, columns):
    lane = lax.broadcasted_iota(jnp.int32, (rows, 128), 1)
    table = jnp.zeros((rows, 128), jnp.float32)
    for at, column in enumerate(columns):
        table = jnp.where(lane == at, column, table)
    return table


def added(parts):
    while len(parts) > 1:
        parts = [sum(parts[at : at + 2][1:], parts[at]) for at in range(0, len(parts), 2)]
    return parts[0]


def row_sum(values):
    return jnp.sum(values, axis=1, keepdims=True)


def after_kernel(*refs):
    pass


def add_kernel(count, keep_ref, arrived_ref, *refs):
    parts = refs[-count:]
    size = parts[0].shape[0]
    for at, part_ref in enumerate(parts):
        rows = slice(at * size, (at + 1) * size)
        total = keep_ref[rows].astype(jnp.float32) + arrived_ref[rows].astype(jnp.float32)
        part_ref[...] = total.astype(part_ref.dtype)


def gradient_kernel(count, *refs):
    block_parts, sums, refs = refs[:count], refs[count : count + 3], refs[count + 3 :]
    masters, rows_old, refs = refs[:4], refs[4:8], refs[8:]
    grads, (row_ref, message_ref) = refs[:4], refs[4:]
    blocks = added([part[0].astype(jnp.float32) for part in block_parts])
    rows, up_cols = grads[2].shape
    qkv_cols, out_cols = grads[0].shape[1], grads[1].shape[1]
    folds = grads[3].shape[0] // rows
    up = blocks[:, :up_cols]
    downs = [blocks[:, up_cols + fold * out_cols :][:, :out_cols] for fold in range(folds)]
    start = up_cols + folds * out_cols
    qkv = blocks[:, start : start + qkv_cols]
    proj = blocks[:, start + qkv_cols :]
    grads[0][...] = qkv
    grads[1][...] = proj
    grads[2][...] = up
    for fold in range(folds):
        grads[3][fold * rows : (fold + 1) * rows, :] = downs[fold]
    squares = [part * part + tiny_square for part in (qkv, proj, up, *downs)]
    row_ref[...] = lane_table(rows, [row_sum(square) for square in squares]).T[: row_ref.shape[0], :]
    width = message_ref.shape[1]
    message_ref[...] = jnp.zeros_like(message_ref)
    for at, square in enumerate((*squares[:3], added(squares[3:]))):
        message_ref[at : at + 1, : square.shape[1]] = column_sum(square)
    scalars = [column_sum(row_sum(master[...] * master[...])) for master in masters]
    scalars += [row_sum(part[...].reshape(1, part.shape[0])) for part in rows_old]
    message_ref[4:5, :128] = lane_table(1, scalars)
    att_ref, ff_ref, up_ref = sums
    count = up_ref.shape[1] // width
    message_ref[8:12, :] = att_ref[:4]
    message_ref[12:15, :] = ff_ref[:3]
    for at in range(count):
        message_ref[15 + at : 16 + at, :] = up_ref[:, at * width : (at + 1) * width]
    message_ref[15 + count : 16 + count, :] = ff_ref[3:4]


def column_kernel(row_ref, *refs):
    parts, (cols_ref, message_ref) = refs[:-3], refs[-2:]
    total = added([part[...] for part in parts])
    cols_ref[...] = total[:8]
    width = total.shape[1]
    rows = row_ref.shape[1]
    message_ref[...] = jnp.zeros_like(message_ref)
    message_ref[:8, :rows] = row_ref[...]
    columns = [row_sum(total[which : which + 1]) for which in range(4)]
    squares = [total[4:5, which : which + 1] for which in range(4)]
    message_ref[8:9, :] = lane_table(1, columns + squares)
    for tile in range(width // 128):
        message_ref[16 * (tile + 1) : 16 * (tile + 2), :] = total[8:, tile * 128 : (tile + 1) * 128]


def update_kernel(count, heights, widths, *refs):
    messages, refs = refs[:count], refs[count:]
    cols_ref, vectors_ref, moment_ref, refs = refs[0], refs[1], refs[2], refs[3:]
    grads, masters, rows_old, cols_old, refs = refs[:4], refs[4:8], refs[8:12], refs[12:16], refs[17:]
    news, cols_new, rows_out, refs = refs[:4], refs[4:8], refs[8:12], refs[12:]
    vector_grad_ref, moment_new_ref, vector_new_ref = refs
    sums = added([message[...] for message in messages])
    height = grads[0].shape[0]
    folds = grads[3].shape[0] // height
    lanes = [[0], [1], [2], list(range(3, 3 + folds))]
    share = 1.0 - decay_rate
    for which in range(4):
        entries = heights[which] * widths[which]
        cols = cols_old[which].shape[0]
        new = decay_rate * cols_old[which][...].reshape(1, cols) + share / heights[which] * cols_ref[
            which : which + 1, :cols
        ]
        cols_new[which][...] = new[0]
        old_total = cols_ref[4:5, 4 + which : 5 + which]
        mean_rows = (decay_rate * old_total + share / widths[which] * sums[8:9, which : which + 1]) / heights[which]
        rate = step_rate * jnp.sqrt(sums[8:9, 4 + which : 5 + which] / entries)
        across = new / mean_rows
        old = rows_old[which][...].reshape(1, len(lanes[which]) * height)
        row_sums = jnp.concatenate([sums[lane : lane + 1, :height] for lane in lanes[which]], axis=1)
        row = decay_rate * old + share / widths[which] * row_sums
        rows_out[which][...] = row[0]
        for fold in range(len(lanes[which])):
            part = slice(fold * height, (fold + 1) * height)
            column = jnp.broadcast_to(row[:, part], (8, height)).T[:, :1]
            news[which][part, :] = masters[which][part, :] - rate * grads[which][part, :] * lax.rsqrt(column * across)
    vectors = vectors_ref[...]
    count = vectors.shape[0]
    gradient = jnp.concatenate(
        [sums[16 * (tile + 1) : 16 * (tile + 1) + count] for tile in range(vectors.shape[1] // 128)], axis=1
    )
    vector_grad_ref[...] = gradient
    moment = decay_rate * moment_ref[...] + share * (gradient * gradient + tiny_square)
    moment_new_ref[...] = moment
    spread = jnp.sqrt(jnp.mean(vectors * vectors, axis=1, keepdims=True))
    vector_new_ref[...] = vectors - step_rate * spread * gradient * lax.rsqrt(moment)


def packed_body(
    tokens, keep_mask, cotangent, qkv_weight, proj_weight, up_weight, down_weight, vectors,
    qkv_rows, qkv_cols, proj_rows, proj_cols, up_rows, up_cols, down_rows, down_cols, vector_moment,
):
    spread, dp_size = lax.axis_size("group"), lax.axis_size("dp")
    low, high = jnp.bfloat16, jnp.float32
    place = linear_place().astype(jnp.int32).reshape(1)
    group = lax.axis_index("group")
    held, slots, width = tokens.shape
    images, length = keep_mask.shape
    hidden = up_weight.shape[1] * spread
    total = images * length
    rows = qkv_weight.shape[0]
    folds = down_weight.shape[0] // rows
    core_bits = (1,)
    near_bits = tuple(1 << at for at in range(1, spread.bit_length()))
    far_bits = tuple(spread << at for at in range(1, dp_size.bit_length() - 1))
    half = spread * dp_size // 2

    anywhere = pl.BlockSpec(memory_space=pl.ANY)
    in_smem = pl.BlockSpec(memory_space=pltpu.SMEM)

    in_vmem = pl.BlockSpec(memory_space=pltpu.VMEM)
    small = functools.partial(
        pl.pallas_call, compiler_params=pltpu.CompilerParams(vmem_limit_bytes=vmem_bytes)
    )
    masters = (qkv_weight, proj_weight, up_weight, down_weight)
    parted = jax.ShapeDtypeStruct((spread, slots, images, width), low)

    def after(array, awaited):
        return small(
            after_kernel,
            in_specs=[anywhere] * (1 + len(awaited)),
            out_specs=anywhere,
            out_shape=jax.ShapeDtypeStruct(array.shape, array.dtype),
            input_output_aliases={0: 0},
        )(array, *awaited)

    def to_group(parts):
        return lax.all_to_all(parts, "group", split_axis=0, concat_axis=0, tiled=True)

    def to_images(parts):
        return to_group(parts).reshape(total, width)

    def exchange(parts):
        return [parts[0]] + [permute(part, relative) for relative, part in enumerate(parts) if relative]

    def settle(parts):
        parts = [part.reshape(slots, -1, width) for part in parts]
        whole, token = small(
            functools.partial(settle_kernel, spread),
            in_specs=[in_smem] + [in_vmem] * len(parts),
            out_specs=[in_vmem] * 2,
            out_shape=[
                jax.ShapeDtypeStruct((slots, held, width), low),
                jax.ShapeDtypeStruct((8, 128), high),
            ],
        )(place, *parts)
        return whole.transpose(1, 0, 2), token

    first_cols = qkv_weight.shape[1] + proj_weight.shape[1]
    second_cols = up_weight.shape[1] + folds * down_weight.shape[1]
    pack_own = small(pack_kernel, out_shape=jax.ShapeDtypeStruct((rows, first_cols + second_cols), low))(*masters)
    across_y, across_x = near_bits
    pack_arrived = permute(pack_own, across_y)
    cotangent_cut = small(cut, out_shape=parted)(cotangent.transpose(1, 0, 2))
    token_cut, first_pair, second_pair = small(
        token_kernel,
        in_specs=[in_vmem] * 3 + [anywhere],
        out_shape=[
            parted,
            jax.ShapeDtypeStruct((2, rows, first_cols), low),
            jax.ShapeDtypeStruct((2, rows, second_cols), low),
        ],
    )(tokens.transpose(1, 0, 2), pack_own, pack_arrived, cotangent_cut)
    inputs = to_images(token_cut)

    def gather_far(pair):
        return [pair] + [permute(pair, mask) for mask in direct_masks(far_bits)]

    def join(parts, awaited=()):
        count = len(parts) * parts[0].shape[0]
        return small(
            functools.partial(join_kernel, len(parts)),
            in_specs=[in_vmem] * len(parts) + [anywhere] * len(awaited),
            out_shape=jax.ShapeDtypeStruct((count, *parts[0].shape[1:]), low),
        )(*parts, *awaited)

    def gather_rest(held):
        arrived = permute(held, across_x)
        return [held, arrived, permute(held, core_bits[0]), permute(arrived, core_bits[0])]

    first_far = join(gather_far(first_pair))
    upstream = to_images(cotangent_cut)
    first_blocks = gather_rest(first_far)
    second_far = gather_far(second_pair)

    step_rows = PER_STEP * length
    block = (step_rows, width)
    pairs = width // (2 * HEAD_DIM)
    steps = images // PER_STEP
    statics = (images, dp_size, spread)
    wide = scratch(width // 128, total, 128)
    probs_block = (PER_STEP, pairs, length, 2 * length)
    attention_outs = [
        ((total, 3 * width), low, (step_rows, 3 * width)),
        ((images, *probs_block[1:]), low, probs_block),
        ((total, width), low, block),
        ((total, width), high, block),
    ]
    attention_flops = (2 * total * width * 4 * width + 8 * total * length * width) // steps
    attention_scratches = [scratch(length, images), scratch(step_rows, width, dtype=low)]
    *attention, x, w_qkv, w_proj, qkv_t, proj_t = call_kernel(
        first_attention_kernel, statics, 1,
        ["place"] + [None] * 7,
        attention_outs
        + [
            ((total, width), low, None),
            ((width, 3 * width), low, None),
            ((width, width), low, None),
            ((3 * width, width), low, None),
            ((width, width), low, None),
        ],
        [scratch(dp_size * spread, rows, first_cols, dtype=low), wide] + attention_scratches,
        (place, inputs, *first_blocks, keep_mask, vectors),
        attention_flops,
    )
    second_blocks = gather_rest(join(second_far, attention[:1]))
    for first_step, count in ((1, steps - 2), (steps - 1, 1)):
        attention = call_kernel(
            next_attention_kernel, (first_step * PER_STEP,), count,
            [block] + [None] * 4 + ["await"] * len(attention),
            attention_outs, attention_scratches,
            (x, keep_mask, w_qkv, w_proj, vectors, *attention),
            attention_flops * count, first_step=first_step,
            aliases={5 + at: at for at in range(len(attention))},
        )
    qkv, probs, attended, middle = attention
    piece = ((slots * images, width), low, None)
    ff_rows = FF_PER_STEP * length
    ff_block = (ff_rows, width)
    results = call_kernel(
        feed_forward_packed_kernel, statics, images // FF_PER_STEP,
        ["place"] + [None] * 5 + [ff_block, ff_block] + [None] * 2,
        [piece] * spread
        + [
            ((total, width), high, ff_block),
            ((total, width), low, ff_block),
            ((half, rows, second_cols), low, None),
            ((half, rows, second_cols), low, None),
            ((width, width), high, None),
            ((8, width), high, None),
            ((1, hidden), high, None),
        ],
        [
            scratch(width, hidden, dtype=low),
            scratch(hidden, width, dtype=low),
            scratch(hidden, width, dtype=low),
            scratch(dp_size * spread, rows, second_cols, dtype=low),
            scratch(1, hidden),
            wide,
            scratch(ff_rows, width, dtype=low),
            scratch(width, ff_rows, dtype=low),
            scratch(ff_rows, width, dtype=low),
            scratch(width, ff_rows, dtype=low),
            scratch(ff_rows, width),
            scratch(ff_rows, 128),
            scratch(ff_rows, width),
            scratch(ff_rows, width),
            scratch(hidden, width, dtype=low),
            scratch(width, hidden, dtype=low),
            scratch(width, hidden),
            scratch(width, hidden),
        ],
        (
            place, upstream, *second_blocks, middle, attended, proj_t, vectors,
        ),
        12 * total * width * hidden + 4 * total * width * width, total * hidden,
    )
    d_middle, d_attended, ff_keep, ff_leave, proj_total, ff_sums, up_sums = results[spread:]

    def add_parts(count, keep, arrived, awaited):
        part = (keep.shape[0] // count, *keep.shape[1:])
        return small(
            functools.partial(add_kernel, count),
            in_specs=[in_vmem] * 2 + [anywhere] * len(awaited),
            out_specs=[in_vmem] * count,
            out_shape=[jax.ShapeDtypeStruct(part, high)]
            + [jax.ShapeDtypeStruct(part, low)] * (count - 1),
        )(keep, arrived, *awaited)

    ff_first = permute(ff_leave, core_bits[0])
    ff_count = half // 2
    ff_next = add_wide(ff_keep[ff_count:], ff_first[ff_count:]).astype(low)
    ff_arrived = permute(ff_next, across_x)
    output_parts = exchange(results[:spread])
    pack_half = ((half, rows, first_cols), low, None)
    wide_rows = (step_rows, 3 * width)
    d_projected, qkv_keep, qkv_leave, att_sums = call_kernel(
        attention_back_packed_kernel, (dp_size, spread), steps,
        ["place", block, wide_rows, probs_block, block, None, None, "await"],
        [((total, 3 * width), low, wide_rows), pack_half, pack_half, ((8, width), high, None)],
        [scratch(step_rows, width, dtype=low), scratch(width, 3 * width)],
        (place, x, qkv, probs, d_attended, vectors, proj_total, ff_next),
        2 * total * width * 3 * width + 16 * total * length * width,
    )
    qkv_arrived = permute(after(qkv_leave, output_parts[1:]), core_bits[0])
    input_flops = 2 * total * width * 3 * width
    input_ins = [block, wide_rows, block, None, None, None]
    input_outs = [((total, width), low, block), ((8, width), high, None)]
    d_input, att_sums = call_kernel(
        first_input_kernel, (length,), 1, input_ins, input_outs, [scratch(step_rows, width)],
        (x, d_projected, d_middle, qkv_t, vectors, att_sums), input_flops // steps,
    )
    ff_quarter = half // 4
    ff_last = add_wide(
        ff_keep[ff_quarter:ff_count], ff_first[ff_quarter:ff_count], ff_arrived[ff_quarter:]
    ).astype(low)
    ff_last_arrived = permute(ff_last, across_y)
    qkv_held, *leaving = add_parts(4, qkv_keep, qkv_arrived, [ff_last])
    qkv_parts = [permute(part, mask) for part, mask in zip(leaving, direct_masks(near_bits))]
    d_input, att_sums = call_kernel(
        first_input_kernel, (length,), 1, input_ins + ["await"] * 2, input_outs, [scratch(step_rows, width)],
        (x, d_projected, d_middle, qkv_t, vectors, att_sums, d_input, leaving[0]), input_flops // steps,
        first_step=1, aliases={6: 0},
    )
    ff_held = add_wide(
        ff_keep[:ff_quarter], ff_first[:ff_quarter], ff_arrived[:ff_quarter], ff_last_arrived
    )
    qkv_held = add_wide(qkv_held, *qkv_parts)
    blocks = jnp.concatenate([ff_held, qkv_held], axis=2)
    far_leaving = [blocks[at : at + 1].astype(low) for at in range(1, blocks.shape[0])]
    block_parts = [blocks[:1]] + [permute(part, mask) for part, mask in zip(far_leaving, direct_masks(far_bits))]
    results = call_kernel(
        last_input_kernel, (images, spread, length, 2 * PER_STEP), steps - 2,
        ["place"] + input_ins + [None, "await"],
        [piece] * spread + [((8, width), high, None)],
        [wide, scratch(step_rows, width)],
        (place, x, d_projected, d_middle, qkv_t, vectors, att_sums, d_input, far_leaving[0]), input_flops // steps * (steps - 2),
        first_step=2,
    )
    att_sums = results[spread]
    input_pieces = list(results[:spread])
    heights = [master.shape[0] * dp_size for master in masters]
    widths = [master.shape[1] * spread for master in masters]
    rows_old, cols_old = [qkv_rows, proj_rows, up_rows, down_rows], [qkv_cols, proj_cols, up_cols, down_cols]

    def like(*arrays):
        return [jax.ShapeDtypeStruct(array.shape, high) for array in arrays]

    operands = (*block_parts, att_sums, ff_sums, up_sums, *masters, *rows_old)
    *grads, row_sums, message = small(
        functools.partial(gradient_kernel, len(block_parts)),
        out_shape=like(*masters) + [jax.ShapeDtypeStruct((8, rows), high), jax.ShapeDtypeStruct((24, width), high)],
    )(*operands)
    input_pieces[1] = after(input_pieces[1], [row_sums])
    output_parts[0] = after(output_parts[0], [row_sums])
    block_output, settled = settle(output_parts)
    input_grad, input_settled = settle(exchange(input_pieces))
    message = added([message] + [permute(message, mask) for mask in direct_masks((across_x, far_bits[0]))])
    for bit in far_bits[1:-1]:
        message = message + permute(message, bit)
    messages = [message, permute(message, far_bits[-1])]
    col_sums, message = small(
        column_kernel,
        in_specs=[in_vmem] * (1 + len(messages)) + [anywhere],
        out_shape=[
            jax.ShapeDtypeStruct((8, width), high),
            jax.ShapeDtypeStruct((16 + width // 8, 128), high),
        ],
    )(row_sums, *messages, settled)
    messages = [message] + [permute(message, mask) for mask in range(1, spread)]
    operands = (*messages, col_sums, vectors, vector_moment, *grads, *masters, *rows_old, *cols_old)
    results = small(
        functools.partial(update_kernel, len(messages), heights, widths),
        in_specs=[in_vmem] * len(operands) + [anywhere],
        out_shape=like(*masters, *cols_old, *rows_old, vectors, vectors, vectors),
    )(*operands, input_settled)
    news, cols_new, rows_out = results[:4], results[4:8], results[8:12]
    vector_grad, vector_moment_new, vector_new = results[12:]
    factored = []
    for which in range(4):
        factored += [grads[which], rows_out[which], cols_new[which], news[which]]
    return (block_output, input_grad, *factored, vector_grad, vector_moment_new, vector_new)


def body(*arrays):
    spread, dp_size = lax.axis_size("group"), lax.axis_size("dp")
    rows, images = arrays[3].shape[0], arrays[1].shape[0]
    slots, width = arrays[0].shape[1:]
    folds = arrays[6].shape[0] // rows
    powers = all(size & (size - 1) == 0 for size in (spread, dp_size))
    fits = powers and spread == 4 and dp_size > 2
    fits = fits and arrays[5].shape[1] <= width and folds <= 5
    fits = fits and rows % 16 == 0 and images % FF_PER_STEP == 0 and images > 2 * PER_STEP and images % 16 == 0 and slots % 4 == 0
    return packed_body(*arrays) if fits else general_body(*arrays)


def solution(mesh):
    in_specs = (
        P("dp", "group", None),
        P(("dp", "group"), None),
        P("dp", "group", None),
        P("dp", "group"),
        P("dp", "group"),
        P("dp", "group"),
        P("dp", "group"),
        P(),
        P("dp"),
        P("group"),
        P("dp"),
        P("group"),
        P("dp"),
        P("group"),
        P("dp"),
        P("group"),
        P(),
    )
    out_specs = (
        P("dp", "group", None),
        P("dp", "group", None),
        P("dp", "group"),
        P("dp"),
        P("group"),
        P("dp", "group"),
        P("dp", "group"),
        P("dp"),
        P("group"),
        P("dp", "group"),
        P("dp", "group"),
        P("dp"),
        P("group"),
        P("dp", "group"),
        P("dp", "group"),
        P("dp"),
        P("group"),
        P("dp", "group"),
        P(),
        P(),
        P(),
    )
    return jax.shard_map(body, mesh=mesh, in_specs=in_specs, out_specs=out_specs, check_vma=False)
```

```python
import functools
import math

import jax
import jax.numpy as jnp
from jax import lax
from jax.experimental import pallas as pl
from jax.experimental.pallas import tpu as pltpu
from jax.sharding import PartitionSpec as P

HEAD_DIM = 64
STEP_NUMBER = 10


step_rate = 0.3
norm_epsilon = 1e-06
tiny_square = 1e-30
decay_rate = 1.0 - STEP_NUMBER ** (-0.8)
LOG2_E = 1.4426950408889634


def axis_bits(name):
    count = lax.axis_size(name)
    return [(name, 1 << place) for place in range(count.bit_length() - 1)]


def swap_partner(array, step):
    name, bit = step
    count = lax.axis_size(name)
    return lax.ppermute(array, name, [(rank, rank ^ bit) for rank in range(count)])


def upper_side(step):
    name, bit = step
    return (lax.axis_index(name) & bit) != 0


def gather_blocks(array, steps):
    for step in steps:
        arrived = swap_partner(array, step)
        upper = upper_side(step)
        array = jnp.stack([jnp.where(upper, arrived, array), jnp.where(upper, array, arrived)])
    return array


def scatter_sum(array, steps):
    for step in steps:
        upper = upper_side(step)
        leaving = jnp.where(upper, array[0], array[1]).astype(jnp.bfloat16)
        arrived = swap_partner(leaving, step)
        array = jnp.where(upper, array[1], array[0]).astype(jnp.float32) + arrived.astype(jnp.float32)
    return array


def sum_everywhere(array, steps):
    for step in steps:
        array = array + swap_partner(array, step)
    return array


def sum_parts(parts, steps):
    flat = [part.reshape(-1) for part in parts]
    total = sum_everywhere(jnp.concatenate(flat), steps)
    result, start = [], 0
    for part in parts:
        result.append(total[start : start + part.size].reshape(part.shape))
        start += part.size
    return result


def block_order(steps):
    order = []
    for name in ("dp", "group"):
        bits = sorted((step for step in steps if step[0] == name), key=lambda step: -step[1])
        order.append([steps.index(step) for step in bits])
    return order


def blocks_to_whole(blocks, steps):
    count = len(steps)
    rows, cols = blocks.shape[count:]
    dp_axes, group_axes = block_order(steps)
    dp_axes = [count - 1 - axis for axis in dp_axes]
    group_axes = [count - 1 - axis for axis in group_axes]
    whole = blocks.transpose(dp_axes + [count] + group_axes + [count + 1])
    return whole.reshape(rows << len(dp_axes), cols << len(group_axes))


def whole_to_blocks(whole, steps):
    dp_axes, group_axes = block_order(steps)
    rows = whole.shape[0] >> len(dp_axes)
    cols = whole.shape[1] >> len(group_axes)
    split = whole.reshape([2] * len(dp_axes) + [rows] + [2] * len(group_axes) + [cols])
    places = dp_axes + [len(steps)] + group_axes + [len(steps) + 1]
    return split.transpose([places.index(axis) for axis in range(len(places))])


PER_STEP = 4
FF_PER_STEP = 4
SLICE = 48
FF_CHUNK = 256
vmem_bytes = 60 * 1024 * 1024


def dot(left, right, left_axis=1, right_axis=0):
    return lax.dot_general(
        left, right, (((left_axis,), (right_axis,)), ((), ())), preferred_element_type=jnp.float32
    )


def normal_form(values):
    center = jnp.mean(values, axis=-1, keepdims=True)
    centered = values - center
    spread = jnp.mean(centered * centered, axis=-1, keepdims=True)
    scale = lax.rsqrt(spread + norm_epsilon)
    return centered * scale, scale


def norm_back(grad, unit, scale, gain):
    weighted = grad * gain
    along = jnp.mean(weighted * unit, axis=-1, keepdims=True)
    level = jnp.mean(weighted, axis=-1, keepdims=True)
    return scale * (weighted - level - unit * along)


def slices_of(count):
    return [slice(start, start + SLICE) for start in range(0, count, SLICE)]


def fold_rows(values):
    return jnp.sum(values.reshape(values.shape[0] // 8, 8, values.shape[1]), axis=0)


def column_sum(values):
    return jnp.sum(values, axis=0, keepdims=True)


def pair_mask(length):
    return lax.broadcasted_iota(jnp.int32, (length, 2 * HEAD_DIM), 1) < HEAD_DIM


def lane_tiles(count):
    return [slice(start, min(start + 128, count)) for start in range(0, count, 128)]


def stack_heads(pair, first):
    none = jnp.zeros_like(pair)
    return jnp.concatenate([jnp.where(first, pair, none), jnp.where(first, none, pair)], axis=0)


def join_heads(rows, first):
    length = rows.shape[0] // 2
    return jnp.where(first, rows[:length], rows[length:])


def gelu_and_slope(pre):
    bell = jnp.exp2(pre * pre * (-0.5 * LOG2_E))
    base = 1.0 + (0.3275911 * 0.5**0.5) * jnp.abs(pre)
    inverse = pl.reciprocal(base, approx=True)
    inverse = inverse * (2.0 - base * inverse)
    poly = inverse * (
        0.5 * 0.254829592
        + inverse
        * (
            0.5 * -0.284496736
            + inverse
            * (0.5 * 1.421413741 + inverse * (0.5 * -1.453152027 + inverse * (0.5 * 1.061405429)))
        )
    )
    tail = poly * bell
    below = jnp.where(pre >= 0, 1.0 - tail, tail)
    return pre * below, below + pre * bell * 0.3989422804014327


def widen(source_ref, wide_ref, images):
    tiles, total, lanes = wide_ref.shape
    rows_at_once = 8 * images

    @pl.loop(0, total // rows_at_once)
    def _(part):
        rows = pl.ds(pl.multiple_of(part * rows_at_once, rows_at_once), rows_at_once)
        for tile in range(tiles):
            cols = slice(tile * lanes, (tile + 1) * lanes)
            wide_ref[tile, rows, :] = source_ref[rows, cols].astype(jnp.float32)


def narrow(wide_ref, target_ref, images):
    tiles, total, lanes = wide_ref.shape
    rows_at_once = 8 * images

    @pl.loop(0, total // rows_at_once)
    def _(part):
        rows = pl.ds(pl.multiple_of(part * rows_at_once, rows_at_once), rows_at_once)
        for tile in range(tiles):
            cols = slice(tile * lanes, (tile + 1) * lanes)
            target_ref[rows, cols] = wide_ref[tile, rows, :].astype(target_ref.dtype)


def take_image(wide_ref, image, images):
    tiles, total, _ = wide_ref.shape
    rows = pl.ds(image, total // images, images)
    return jnp.concatenate([wide_ref[tile, rows, :] for tile in range(tiles)], axis=1)


def put_image(wide_ref, image, images, values):
    tiles, total, lanes = wide_ref.shape
    rows = pl.ds(image, total // images, images)
    for tile in range(tiles):
        wide_ref[tile, rows, :] = values[:, tile * lanes : (tile + 1) * lanes]


def attention_kernel(
    images, tokens_ref, bias_ref, w_qkv_ref, w_proj_ref, vectors_ref,
    x_ref, qkv_ref, probs_ref, attended_ref, middle_ref, wide_ref, normed_ref,
):
    @pl.when(pl.program_id(0) == 0)
    def _():
        widen(tokens_ref, wide_ref, images)
        to_image_rows(wide_ref, x_ref, images)

    attention_steps(
        x_ref, lambda image: bias_ref[image], w_qkv_ref, w_proj_ref, vectors_ref,
        qkv_ref, probs_ref, attended_ref, middle_ref, normed_ref,
    )


def to_image_rows(wide_ref, x_ref, images):
    length = wide_ref.shape[1] // images

    @pl.loop(0, images)
    def _(image):
        rows = pl.ds(pl.multiple_of(image * length, length), length)
        x_ref[rows, :] = take_image(wide_ref, image, images).astype(jnp.bfloat16)


def attention_steps(
    x_ref, bias_column, w_qkv_ref, w_proj_ref, vectors_ref,
    qkv_ref, probs_ref, attended_ref, middle_ref, normed_ref,
):
    per_step, _, length, _ = probs_ref.shape
    step_rows, width = middle_ref.shape
    base = 0 if x_ref.shape[0] == step_rows else pl.program_id(0) * step_rows

    for rows in slices_of(step_rows):
        x = x_ref[pl.ds(pl.multiple_of(base + rows.start, SLICE), SLICE), :].astype(jnp.float32)
        unit, _ = normal_form(x)
        normed_ref[rows, :] = (unit * vectors_ref[0:1] + vectors_ref[1:2]).astype(jnp.bfloat16)
    shift = jnp.concatenate(
        [vectors_ref[2:3], jnp.zeros((1, width), jnp.float32), vectors_ref[3:4]], axis=1
    )
    for start in range(0, 3 * width, 512):
        cols = slice(start, min(start + 512, 3 * width))
        projected = dot(normed_ref[...], w_qkv_ref[:, cols]) + shift[:, cols]
        qkv_ref[:, cols] = projected.astype(jnp.bfloat16)

    pairs = width // (2 * HEAD_DIM)
    first = pair_mask(length)
    place = lax.broadcasted_iota(jnp.int32, (length, 2 * length), 0)
    asker = lax.broadcasted_iota(jnp.int32, (length, 2 * length), 1)
    own = place == jnp.where(asker >= length, asker - length, asker)

    def scores_of(image):
        rows = slice(image * length, (image + 1) * length)
        result = []
        for pair in range(pairs):
            low = pair * 2 * HEAD_DIM
            queries = stack_heads(qkv_ref[rows, low : low + 2 * HEAD_DIM], first)
            result.append(dot(qkv_ref[rows, width + low : width + low + 2 * HEAD_DIM], queries, 1, 1))
        return result

    next_scores = scores_of(0)
    for image in range(per_step):
        rows = slice(image * length, (image + 1) * length)
        all_scores = next_scores
        if image + 1 < per_step:
            next_scores = scores_of(image + 1)
        column = bias_column(image)
        for cols in lane_tiles(2 * length):
            bias = jnp.where(own[:, cols], 0.0, column)
            for pair in range(pairs):
                scores = all_scores[pair][:, cols] * (HEAD_DIM**-0.5 * LOG2_E) + bias
                weights = jnp.exp2(scores - jnp.max(scores, axis=0, keepdims=True))
                probs = weights * (1.0 / jnp.sum(weights, axis=0, keepdims=True))
                probs_ref[image, pair, :, cols] = probs.astype(jnp.bfloat16)
        for pair in range(pairs):
            low = pair * 2 * HEAD_DIM
            values = qkv_ref[rows, 2 * width + low : 2 * width + low + 2 * HEAD_DIM]
            attended = join_heads(dot(probs_ref[image, pair], values, 0, 0), first)
            attended_ref[rows, low : low + 2 * HEAD_DIM] = attended.astype(jnp.bfloat16)

    middle_ref[...] = (
        x_ref[pl.ds(pl.multiple_of(base, length), step_rows), :].astype(jnp.float32)
        + dot(attended_ref[...], w_proj_ref[...])
        + vectors_ref[4:5]
    )


def feed_forward_kernel(
    images, middle_ref, cotangent_ref, attended_ref, w_up_ref, w_down_ref, proj_t_ref, vectors_ref, bias_up_ref,
    output_ref, d_middle_ref, d_attended_ref, up_grad_ref, down_grad_ref, proj_grad_ref, vector_sums_ref, up_sums_ref,
    wide_ref, *scratches,
):
    up_total_ref, down_total_ref, proj_total_ref = scratches[-3:]

    @pl.when(pl.program_id(0) == 0)
    def _():
        widen(cotangent_ref, wide_ref, images)

    feed_forward_steps(
        images, middle_ref, attended_ref, w_up_ref, w_down_ref, proj_t_ref, vectors_ref, bias_up_ref,
        d_middle_ref, d_attended_ref, vector_sums_ref, up_sums_ref, wide_ref, *scratches,
    )

    @pl.when(pl.program_id(0) == pl.num_programs(0) - 1)
    def _():
        narrow(wide_ref, output_ref, images)
        up_grad_ref[...] = up_total_ref[...].astype(jnp.bfloat16)
        down_grad_ref[...] = down_total_ref[...].T.astype(jnp.bfloat16)
        proj_grad_ref[...] = proj_total_ref[...].astype(jnp.bfloat16)


def feed_forward_steps(
    images, middle_ref, attended_ref, w_up_ref, w_down_ref, proj_t_ref, vectors_ref, bias_up_ref,
    d_middle_ref, d_attended_ref, vector_sums_ref, up_sums_ref,
    wide_ref, normed_ref, normed_t_ref, dy_ref, dy_t_ref, unit_ref, scale_ref, ahead_ref, back_ref,
    up_t_ref, down_t_ref, up_total_ref, down_total_ref, proj_total_ref,
):
    step = pl.program_id(0)
    length = wide_ref.shape[1] // images
    hidden = w_up_ref.shape[1]
    per_step = middle_ref.shape[0] // length

    @pl.when(step == 0)
    def _():
        for total in (up_total_ref, down_total_ref, proj_total_ref, vector_sums_ref, up_sums_ref):
            total[...] = jnp.zeros_like(total)
        up_t_ref[...] = w_up_ref[...].T
        down_t_ref[...] = w_down_ref[...].T

    for image in range(per_step):
        rows = slice(image * length, (image + 1) * length)
        dy = take_image(wide_ref, step * per_step + image, images)
        dy_ref[rows, :] = dy.astype(jnp.bfloat16)
        vector_sums_ref[3:4] += column_sum(dy)
        unit, scale = normal_form(middle_ref[rows, :])
        unit_ref[rows, :] = unit
        scale_ref[rows, :] = jnp.broadcast_to(scale, (length, scale_ref.shape[1]))
        normed_ref[rows, :] = (unit * vectors_ref[5:6] + vectors_ref[6:7]).astype(jnp.bfloat16)
    normed_t_ref[...] = normed_ref[...].T
    dy_t_ref[...] = dy_ref[...].T
    chunks = hidden // FF_CHUNK

    def cols_of(chunk):
        return slice(chunk * FF_CHUNK, (chunk + 1) * FF_CHUNK)

    def into(chunk):
        cols = cols_of(chunk)
        pre = dot(normed_ref[...], w_up_ref[:, cols])
        return pre + bias_up_ref[:, cols], dot(dy_ref[...], down_t_ref[:, cols])

    def across(pre, d_active):
        active, slope = gelu_and_slope(pre)
        return active.astype(jnp.bfloat16), (d_active * slope).astype(jnp.bfloat16)

    def out_of(chunk, active, d_hidden):
        cols = cols_of(chunk)
        ahead, back = dot(active, w_down_ref[cols, :]), dot(d_hidden, up_t_ref[cols, :])
        if chunk == 0:
            ahead_ref[...] = ahead
            back_ref[...] = back
        else:
            ahead_ref[...] += ahead
            back_ref[...] += back
        down_total_ref[:, cols] += dot(dy_t_ref[...], active)
        up_total_ref[:, cols] += dot(normed_t_ref[...], d_hidden)
        up_sums_ref[:, cols] += column_sum(d_hidden.astype(jnp.float32))

    entered, crossed = into(0), None
    for chunk in range(chunks + 1):
        next_entered = into(chunk + 1) if chunk + 1 < chunks else None
        next_crossed = across(*entered) if chunk < chunks else None
        if crossed is not None:
            out_of(chunk - 1, *crossed)
        entered, crossed = next_entered, next_crossed

    for image in range(per_step):
        rows = slice(image * length, (image + 1) * length)
        output = middle_ref[rows, :] + ahead_ref[rows, :] + vectors_ref[11:12]
        put_image(wide_ref, step * per_step + image, images, output)
        unit = unit_ref[rows, :]
        grad = back_ref[rows, :]
        vector_sums_ref[1:2] += column_sum(grad * unit)
        vector_sums_ref[2:3] += column_sum(grad)
        d_middle = dy_ref[rows, :].astype(jnp.float32) + norm_back(
            grad, unit, scale_ref[rows, 0:1], vectors_ref[5:6]
        )
        d_middle_ref[rows, :] = d_middle
        d_branch = d_middle.astype(jnp.bfloat16)
        dy_ref[rows, :] = d_branch
        vector_sums_ref[0:1] += column_sum(d_branch.astype(jnp.float32))
    proj_total_ref[...] += dot(attended_ref[...], dy_ref[...], 0, 0)
    d_attended_ref[...] = dot(dy_ref[...], proj_t_ref[...]).astype(jnp.bfloat16)


def attention_back_kernel(
    images, x_ref, qkv_ref, probs_ref, d_attended_ref, d_middle_ref, qkv_t_ref, vectors_ref,
    input_grad_ref, qkv_grad_ref, vector_sums_ref, wide_ref, normed_ref, d_projected_ref, back_ref, qkv_total_ref,
):
    @pl.when(pl.program_id(0) == 0)
    def _():
        qkv_total_ref[...] = jnp.zeros_like(qkv_total_ref)
        vector_sums_ref[...] = jnp.zeros_like(vector_sums_ref)

    def put(image, rows, values):
        put_image(wide_ref, image, images, values)

    attention_back_steps(
        x_ref, qkv_ref, probs_ref, d_attended_ref, vectors_ref, vector_sums_ref, normed_ref, d_projected_ref, qkv_total_ref
    )
    input_back_steps(
        put, probs_ref.shape[2], x_ref, d_projected_ref, d_middle_ref, qkv_t_ref, vectors_ref, vector_sums_ref, back_ref
    )

    @pl.when(pl.program_id(0) == pl.num_programs(0) - 1)
    def _():
        narrow(wide_ref, input_grad_ref, images)
        qkv_grad_ref[...] = qkv_total_ref[...].astype(jnp.bfloat16)


def attention_back_steps(
    x_ref, qkv_ref, probs_ref, d_attended_ref, vectors_ref, vector_sums_ref, normed_ref, d_projected_ref, qkv_total_ref
):
    width = x_ref.shape[1]
    length = probs_ref.shape[2]
    per_step = probs_ref.shape[0]

    pairs = width // (2 * HEAD_DIM)
    first = pair_mask(length)
    scale = HEAD_DIM**-0.5

    def places(image, pair):
        low = pair * 2 * HEAD_DIM
        rows = slice(image * length, (image + 1) * length)
        return rows, [slice(part * width + low, part * width + low + 2 * HEAD_DIM) for part in range(3)]

    def entering(image):
        result = []
        for pair in range(pairs):
            rows, cols = places(image, pair)
            d_attended = stack_heads(d_attended_ref[rows, cols[0]], first)
            d_values = dot(probs_ref[image, pair], d_attended)
            d_projected_ref[rows, cols[2]] = d_values.astype(jnp.bfloat16)
            result.append(dot(qkv_ref[rows, cols[2]], d_attended, 1, 1))
        return result

    next_probs = entering(0)
    for image in range(per_step):
        all_d_probs = next_probs
        if image + 1 < per_step:
            next_probs = entering(image + 1)
        all_d_scores = []
        for pair in range(pairs):
            parts = []
            for cols in lane_tiles(2 * length):
                probs, d_probs = probs_ref[image, pair, :, cols].astype(jnp.float32), all_d_probs[pair][:, cols]
                along = jnp.sum(d_probs * probs, axis=0, keepdims=True)
                parts.append((probs * (d_probs - along)).astype(jnp.bfloat16))
            all_d_scores.append(jnp.concatenate(parts, axis=1))
        for pair in range(pairs):
            rows, cols = places(image, pair)
            d_scores = all_d_scores[pair]
            queries = stack_heads(qkv_ref[rows, cols[0]], first)
            d_queries = join_heads(dot(d_scores, qkv_ref[rows, cols[1]], 0, 0), first) * scale
            d_projected_ref[rows, cols[0]] = d_queries.astype(jnp.bfloat16)
            d_projected_ref[rows, cols[1]] = (dot(d_scores, queries) * scale).astype(jnp.bfloat16)

    query_sums = value_sums = jnp.zeros((8, width), jnp.float32)
    for rows in slices_of(x_ref.shape[0]):
        query_sums += fold_rows(d_projected_ref[rows, :width].astype(jnp.float32))
        value_sums += fold_rows(d_projected_ref[rows, 2 * width :].astype(jnp.float32))
        unit, _ = normal_form(x_ref[rows, :].astype(jnp.float32))
        normed_ref[rows, :] = (unit * vectors_ref[0:1] + vectors_ref[1:2]).astype(jnp.bfloat16)
    vector_sums_ref[2:3] += column_sum(query_sums)
    vector_sums_ref[3:4] += column_sum(value_sums)
    qkv_total_ref[...] += dot(normed_ref[...], d_projected_ref[...], 0, 0)


def input_back_steps(
    put, length, x_ref, d_projected_ref, d_middle_ref, qkv_t_ref, vectors_ref, vector_sums_ref, back_ref
):
    step = pl.program_id(0)
    per_step = x_ref.shape[0] // length
    back_ref[...] = dot(d_projected_ref[...], qkv_t_ref[...])
    gain_sums = shift_sums = jnp.zeros((8, x_ref.shape[1]), jnp.float32)
    for rows in slices_of(x_ref.shape[0]):
        unit, scale = normal_form(x_ref[rows, :].astype(jnp.float32))
        grad = back_ref[rows, :]
        gain_sums += fold_rows(grad * unit)
        shift_sums += fold_rows(grad)
        back_ref[rows, :] = d_middle_ref[rows, :] + norm_back(grad, unit, scale, vectors_ref[0:1])
    vector_sums_ref[0:1] += column_sum(gain_sums)
    vector_sums_ref[1:2] += column_sum(shift_sums)
    for image in range(per_step):
        rows = slice(image * length, (image + 1) * length)
        put(step * per_step + image, rows, back_ref[rows, :])


def whole_block(shape):
    return pl.BlockSpec(shape, lambda step: (0,) * len(shape))


def step_block(shape, first=0):
    return pl.BlockSpec(shape, lambda step: (first + step,) + (0,) * (len(shape) - 1))


def scratch(*shape, dtype=jnp.float32):
    return pltpu.VMEM(shape, dtype)


def call_kernel(kernel, statics, steps, ins, outs, scratches, operands, flops, transcendentals=0, first_step=0, aliases={}):
    in_specs = [
        pl.BlockSpec(memory_space=pltpu.SMEM)
        if block == "place"
        else pl.BlockSpec(memory_space=pl.ANY)
        if block == "await"
        else whole_block(op.shape) if block is None else step_block(block, first_step)
        for op, block in zip(operands, ins)
    ]
    out_specs = [
        whole_block(shape) if block is None else step_block(block, first_step) for shape, dtype, block in outs
    ]
    moved = sum(op.size * op.dtype.itemsize for op in operands) + sum(
        math.prod(shape) * jnp.dtype(dtype).itemsize for shape, dtype, block in outs
    )
    return pl.pallas_call(
        functools.partial(kernel, *statics),
        grid=(steps,),
        in_specs=in_specs,
        out_specs=out_specs,
        out_shape=[jax.ShapeDtypeStruct(shape, dtype) for shape, dtype, block in outs],
        scratch_shapes=scratches,
        input_output_aliases=aliases,
        compiler_params=pltpu.CompilerParams(vmem_limit_bytes=vmem_bytes),
        cost_estimate=pl.CostEstimate(
            flops=flops * 8, bytes_accessed=moved, transcendentals=transcendentals
        ),
    )(*operands)


def attention_forward(tokens, bias, w_qkv, w_proj, vectors):
    images, length, _ = bias.shape
    total, width = tokens.shape
    pairs = width // (2 * HEAD_DIM)
    rows = PER_STEP * length
    low, high = jnp.bfloat16, jnp.float32
    outs = [
        ((total, width), low, None),
        ((total, 3 * width), low, (rows, 3 * width)),
        ((images, pairs, length, 2 * length), low, (PER_STEP, pairs, length, 2 * length)),
        ((total, width), low, (rows, width)),
        ((total, width), high, (rows, width)),
    ]
    return call_kernel(
        attention_kernel, (images,), images // PER_STEP,
        [None, (PER_STEP, length, 1), None, None, None], outs,
        [scratch(width // 128, total, 128), scratch(rows, width, dtype=low)],
        (tokens, bias, w_qkv, w_proj, vectors),
        2 * total * width * 4 * width + 8 * total * length * width,
    )


def feed_forward(images, middle, cotangent, attended, w_up, w_down, w_proj, vectors):
    total, width = middle.shape
    hidden = w_up.shape[1]
    rows = total // images * FF_PER_STEP
    low, high = jnp.bfloat16, jnp.float32
    block = (rows, width)
    outs = [
        ((total, width), low, None),
        ((total, width), high, block),
        ((total, width), low, block),
        ((width, hidden), low, None),
        ((hidden, width), low, None),
        ((width, width), low, None),
        ((8, width), high, None),
        ((1, hidden), high, None),
    ]
    scratches = [
        scratch(width // 128, total, 128),
        scratch(rows, width, dtype=low),
        scratch(width, rows, dtype=low),
        scratch(rows, width, dtype=low),
        scratch(width, rows, dtype=low),
        scratch(rows, width),
        scratch(rows, 128),
        scratch(rows, width),
        scratch(rows, width),
        scratch(hidden, width, dtype=low),
        scratch(width, hidden, dtype=low),
        scratch(width, hidden),
        scratch(width, hidden),
        scratch(width, width),
    ]
    return call_kernel(
        feed_forward_kernel, (images,), images // FF_PER_STEP,
        [block, None, block, None, None, None, None, None], outs, scratches,
        (middle, cotangent, attended, w_up, w_down, w_proj.T, vectors, vectors[7:11].reshape(1, hidden)),
        12 * total * width * hidden + 4 * total * width * width, total * hidden,
    )


def attention_back(x, qkv, probs, d_attended, d_middle, w_qkv, vectors):
    images, pairs, length, _ = probs.shape
    total, width = x.shape
    rows = PER_STEP * length
    low, high = jnp.bfloat16, jnp.float32
    block = (rows, width)
    outs = [
        ((total, width), low, None),
        ((width, 3 * width), low, None),
        ((8, width), high, None),
    ]
    scratches = [
        scratch(width // 128, total, 128),
        scratch(rows, width, dtype=low),
        scratch(rows, 3 * width, dtype=low),
        scratch(rows, width),
        scratch(width, 3 * width),
    ]
    return call_kernel(
        attention_back_kernel, (images,), images // PER_STEP,
        [block, (rows, 3 * width), (PER_STEP, pairs, length, 2 * length), block, block, None, None],
        outs, scratches, (x, qkv, probs, d_attended, d_middle, w_qkv.T, vectors),
        4 * total * width * 3 * width + 16 * total * length * width,
    )

def linear_place():
    return lax.axis_index("dp") * lax.axis_size("group") + lax.axis_index("group")


def permute(array, mask):
    count = lax.axis_size("dp") * lax.axis_size("group")
    return lax.ppermute(array, ("dp", "group"), [(rank, rank ^ mask) for rank in range(count)])


def direct_masks(bits):
    masks = [0]
    for bit in bits:
        masks = masks + [mask | bit for mask in masks]
    return masks[1:]


def add_wide(first, *rest):
    total = first.astype(jnp.float32)
    for part in rest:
        total = total + part.astype(jnp.float32)
    return total


def packed_place(mask, spread, count):
    return ((mask >> 1) & (spread - 1)) * (count // (2 * spread)) + (mask >> (spread.bit_length()))


def scatter_step(held, bits):
    masks = direct_masks(bits)
    size = held.shape[0] // (len(masks) + 1)
    parts = [
        permute(held[size * (at + 1) : size * (at + 2)].astype(jnp.bfloat16), mask)
        for at, mask in enumerate(masks)
    ]
    return held[:size], parts


def add_wide(first, *rest):
    total = first.astype(jnp.float32)
    for part in rest:
        total = total + part.astype(jnp.float32)
    return total


def packed_place(mask, spread, count):
    return ((mask >> 1) & (spread - 1)) * (count // (2 * spread)) + (mask >> (spread.bit_length()))


def gather_step(held, bits):
    return held + [permute(part, mask) for mask in direct_masks(bits) for part in held]


def gathered_place(mask, count):
    return (mask & 1) * (count // 2) + ((mask >> 2) & 1) * (count // 4) + (mask >> 3) * 2 + ((mask >> 1) & 1)


def unpack(place_ref, block_refs, packed_ref, put, dp_size, spread):
    place = place_ref[0]
    size = block_refs[0].shape[0]
    for at, block_ref in enumerate(block_refs):
        packed_ref[at * size : (at + 1) * size] = block_ref[...]
    count = dp_size * spread
    for row in range(dp_size):
        for col in range(spread):
            put(row, col, packed_ref[gathered_place((row * spread + col) ^ place, count)])


def unpack_in_order(blocks_ref, put, dp_size, spread):
    for row in range(dp_size):
        for col in range(spread):
            put(row, col, blocks_ref[row * spread + col])


def pack(place_ref, take, keep_ref, leave_ref, dp_size, spread):
    place = place_ref[0]
    odd = (place & 1) == 1
    for row in range(dp_size):
        for col in range(0, spread, 2):
            at = packed_place((row * spread + col) ^ place, spread, dp_size * spread)
            even_block, odd_block = take(row, col), take(row, col + 1)
            keep_ref[at] = jnp.where(odd, odd_block, even_block)
            leave_ref[at] = jnp.where(odd, even_block, odd_block)


def narrow_pieces(place_ref, wide_ref, piece_refs, spread):
    tiles, _, lanes = wide_ref.shape
    rows_of_piece = piece_refs[0].shape[0]
    step = 64
    group = place_ref[0] & (spread - 1)
    for relative, piece_ref in enumerate(piece_refs):
        base = (group ^ relative) * rows_of_piece

        @pl.loop(0, rows_of_piece // step)
        def _(part):
            target = pl.ds(pl.multiple_of(part * step, step), step)
            source = pl.ds(pl.multiple_of(base + part * step, step), step)
            for tile in range(tiles):
                cols = slice(tile * lanes, (tile + 1) * lanes)
                piece_ref[target, cols] = wide_ref[tile, source, :].astype(jnp.bfloat16)


def general_body(
    tokens,
    keep_mask,
    cotangent,
    qkv_weight,
    proj_weight,
    up_weight,
    down_weight,
    vectors,
    qkv_rows,
    qkv_cols,
    proj_rows,
    proj_cols,
    up_rows,
    up_cols,
    down_rows,
    down_cols,
    vector_moment,
):
    masters = (qkv_weight, proj_weight, up_weight, down_weight)
    lowered = tuple((master.astype(jnp.bfloat16) for master in masters))
    dp_bits, group_bits = axis_bits("dp"), axis_bits("group")
    gather_steps = dp_bits[1:] + group_bits[1:] + dp_bits[:1] + group_bits[:1]
    scatter_steps = gather_steps[::-1]
    w_qkv, w_proj, w_up, w_down = tuple(
        blocks_to_whole(gather_blocks(part, gather_steps), gather_steps) for part in lowered
    )
    spread = lax.axis_size("group")

    def slots_in(array):
        held, slots, width = array.shape
        parts = array.transpose(1, 0, 2).reshape(slots, spread, held // spread, width)
        parts = lax.all_to_all(
            parts.transpose(1, 0, 2, 3), "group", split_axis=0, concat_axis=0, tiled=True
        )
        return parts.reshape(spread * slots * (held // spread), width)

    def slots_out(array):
        held, slots, width = tokens.shape
        parts = array.reshape(spread, slots, held // spread, width)
        parts = lax.all_to_all(parts, "group", split_axis=0, concat_axis=0, tiled=True)
        return parts.transpose(1, 0, 2, 3).reshape(slots, held, width).transpose(1, 0, 2)

    images = keep_mask.shape[0]
    bias = jnp.where(keep_mask > 0, 0.0, -1e30)[:, :, None]
    x, qkv, probs, attended, middle = attention_forward(
        slots_in(tokens), bias, w_qkv, w_proj, vectors
    )
    output, d_middle, d_attended, up_grad, down_grad, proj_grad, ff_sums, up_sums = feed_forward(
        images, middle, slots_in(cotangent), attended, w_up, w_down, w_proj, vectors
    )
    block_output = slots_out(output)
    d_input, qkv_grad, att_sums = attention_back(
        x, qkv, probs, d_attended, d_middle, w_qkv, vectors
    )
    input_grad = slots_out(d_input)
    local_vectors = jnp.concatenate(
        [att_sums[:4], ff_sums[:3], up_sums.reshape(4, -1), ff_sums[3:4]], axis=0
    )
    vector_grad = sum_everywhere(local_vectors, group_bits + dp_bits)
    local_grads = (qkv_grad, proj_grad, up_grad, down_grad)
    owned = tuple(
        scatter_sum(whole_to_blocks(part, scatter_steps), scatter_steps) for part in local_grads
    )
    squares = tuple((gradient * gradient + tiny_square for gradient in owned))
    row_parts = tuple((jnp.sum(square, axis=1) for square in squares)) + tuple(
        (jnp.sum(master * master, axis=1) for master in masters)
    )
    row_sums = sum_parts(row_parts, group_bits)
    rows_old = (qkv_rows, proj_rows, up_rows, down_rows)
    cols_old = (qkv_cols, proj_cols, up_cols, down_cols)
    total_cols = tuple((gradient.shape[1] * lax.axis_size("group") for gradient in owned))
    total_rows = tuple((gradient.shape[0] * lax.axis_size("dp") for gradient in owned))
    rows_new = tuple(
        (
            decay_rate * rows_old[which] + (1.0 - decay_rate) * row_sums[which] / total_cols[which]
            for which in range(4)
        )
    )
    col_parts = (
        tuple((jnp.sum(square, axis=0) for square in squares))
        + tuple((jnp.sum(row_stat) for row_stat in rows_new))
        + tuple((jnp.sum(row_sums[4 + which]) for which in range(4)))
    )
    col_sums = sum_parts(col_parts, dp_bits)
    results = []
    for which in range(4):
        cols_new = (
            decay_rate * cols_old[which] + (1.0 - decay_rate) * col_sums[which] / total_rows[which]
        )
        mean_rows = col_sums[4 + which] / total_rows[which]
        spread = jnp.sqrt(col_sums[8 + which] / (total_rows[which] * total_cols[which]))
        second = rows_new[which][:, None] * cols_new[None, :] / mean_rows
        updated = masters[which] - step_rate * spread * owned[which] * lax.rsqrt(second)
        results.append((owned[which], rows_new[which], cols_new, updated))
    vector_moment_new = decay_rate * vector_moment + (1.0 - decay_rate) * (
        vector_grad * vector_grad + tiny_square
    )
    row_spread = jnp.sqrt(jnp.mean(vectors * vectors, axis=1, keepdims=True))
    vector_new = vectors - step_rate * row_spread * vector_grad * lax.rsqrt(vector_moment_new)
    return (
        block_output,
        input_grad,
        results[0][0],
        results[0][1],
        results[0][2],
        results[0][3],
        results[1][0],
        results[1][1],
        results[1][2],
        results[1][3],
        results[2][0],
        results[2][1],
        results[2][2],
        results[2][3],
        results[3][0],
        results[3][1],
        results[3][2],
        results[3][3],
        vector_grad,
        vector_moment_new,
        vector_new,
    )


def first_attention_kernel(images, dp_size, spread, place_ref, tokens_ref, *refs):
    blocks, refs = refs[:4], refs[4:]
    keep_ref, vectors_ref, *outs, x_ref, w_qkv_ref, w_proj_ref, qkv_t_ref, proj_t_ref = refs[:-4]
    packed_ref, wide_ref, bias_ref, normed_ref = refs[-4:]
    rows = packed_ref.shape[1]
    qkv_cols, proj_cols = w_qkv_ref.shape[1] // spread, w_proj_ref.shape[1] // spread

    @pl.when(pl.program_id(0) == 0)
    def _():
        widen(tokens_ref, wide_ref, images)
        to_image_rows(wide_ref, x_ref, images)

        def put(row, col, block):
            down = slice(row * rows, (row + 1) * rows)
            w_qkv_ref[down, col * qkv_cols : (col + 1) * qkv_cols] = block[:, :qkv_cols]
            w_proj_ref[down, col * proj_cols : (col + 1) * proj_cols] = block[:, qkv_cols:]

        unpack(place_ref, blocks, packed_ref, put, dp_size, spread)
        qkv_t_ref[...] = w_qkv_ref[...].T
        proj_t_ref[...] = w_proj_ref[...].T

    attention_part(0, x_ref, keep_ref, w_qkv_ref, w_proj_ref, vectors_ref, *outs, bias_ref, normed_ref)


def attention_part(
    start, x_ref, keep_ref, w_qkv_ref, w_proj_ref, vectors_ref,
    qkv_ref, probs_ref, attended_ref, middle_ref, bias_ref, normed_ref,
):
    @pl.when(pl.program_id(0) == 0)
    def _():
        bias_ref[...] = jnp.where(keep_ref[...] > 0, 0.0, -1e30).T

    def bias_column(image):
        here = start + pl.program_id(0) * probs_ref.shape[0] + image
        lane = lax.broadcasted_iota(jnp.int32, bias_ref.shape, 1)
        return row_sum(jnp.where(lane == here, bias_ref[...], 0.0))

    attention_steps(
        x_ref, bias_column, w_qkv_ref, w_proj_ref, vectors_ref,
        qkv_ref, probs_ref, attended_ref, middle_ref, normed_ref,
    )


def feed_forward_packed_kernel(images, dp_size, spread, place_ref, *refs):
    cotangent_ref, blocks_ref, refs = refs[0], refs[1], refs[2:]
    middle_ref, attended_ref, proj_t_ref, vectors_ref = refs[:4]
    outputs, refs = refs[4 : 4 + spread], refs[4 + spread :]
    d_middle_ref, d_attended_ref, keep_ref, leave_ref, proj_total_ref, vector_sums_ref, up_sums_ref = refs[:7]
    w_up_ref, w_down_ref, down_low_ref, bias_up_ref, wide_ref = refs[7:12]
    scratches = refs[12:]
    width = w_up_ref.shape[0]
    up_total_ref, down_total_ref = scratches[-2:]
    rows = blocks_ref.shape[1]
    up_cols = w_up_ref.shape[1] // spread
    out_cols = w_down_ref.shape[1] // spread
    folds = w_down_ref.shape[0] // w_up_ref.shape[0]

    @pl.when(pl.program_id(0) == 0)
    def _():
        widen(cotangent_ref, wide_ref, images)
        for fold in range(bias_up_ref.shape[1] // width):
            bias_up_ref[:, fold * width : (fold + 1) * width] = vectors_ref[7 + fold : 8 + fold]

        def put(row, col, block):
            w_up_ref[row * rows : (row + 1) * rows, col * up_cols : (col + 1) * up_cols] = block[:, :up_cols]
            for fold in range(folds):
                down = (row * folds + fold) * rows
                start = up_cols + fold * out_cols
                w_down_ref[down : down + rows, col * out_cols : (col + 1) * out_cols] = block[
                    :, start : start + out_cols
                ]

        unpack_in_order(blocks_ref, put, dp_size, spread)

    feed_forward_steps(
        images, middle_ref, attended_ref, w_up_ref, w_down_ref, proj_t_ref, vectors_ref, bias_up_ref,
        d_middle_ref, d_attended_ref, vector_sums_ref, up_sums_ref, wide_ref, *scratches, proj_total_ref,
    )

    @pl.when(pl.program_id(0) == pl.num_programs(0) - 1)
    def _():
        narrow_pieces(place_ref, wide_ref, outputs, spread)
        down_low_ref[...] = down_total_ref[...].T.astype(jnp.bfloat16)

        def take(row, col):
            across = slice(row * rows, (row + 1) * rows)
            cols = slice(col * out_cols, (col + 1) * out_cols)
            parts = [up_total_ref[across, col * up_cols : (col + 1) * up_cols].astype(jnp.bfloat16)]
            for fold in range(folds):
                down = (row * folds + fold) * rows
                parts.append(down_low_ref[down : down + rows, cols])
            return jnp.concatenate(parts, axis=1)

        pack(place_ref, take, keep_ref, leave_ref, dp_size, spread)


def attention_back_packed_kernel(
    dp_size, spread, place_ref, x_ref, qkv_ref, probs_ref, d_attended_ref, vectors_ref, proj_total_ref, _,
    d_projected_ref, keep_ref, leave_ref, vector_sums_ref, normed_ref, total_ref,
):
    @pl.when(pl.program_id(0) == 0)
    def _():
        total_ref[...] = jnp.zeros_like(total_ref)
        vector_sums_ref[...] = jnp.zeros_like(vector_sums_ref)

    attention_back_steps(
        x_ref, qkv_ref, probs_ref, d_attended_ref, vectors_ref, vector_sums_ref, normed_ref, d_projected_ref, total_ref
    )

    @pl.when(pl.program_id(0) == pl.num_programs(0) - 1)
    def _():
        rows = keep_ref.shape[1]
        qkv_cols, proj_cols = total_ref.shape[1] // spread, proj_total_ref.shape[1] // spread

        def take(row, col):
            down = slice(row * rows, (row + 1) * rows)
            parts = [
                total_ref[down, col * qkv_cols : (col + 1) * qkv_cols],
                proj_total_ref[down, col * proj_cols : (col + 1) * proj_cols],
            ]
            return jnp.concatenate(parts, axis=1).astype(jnp.bfloat16)

        pack(place_ref, take, keep_ref, leave_ref, dp_size, spread)


def first_input_kernel(
    length, x_ref, d_projected_ref, d_middle_ref, qkv_t_ref, vectors_ref, before_ref, *refs
):
    d_input_ref, vector_sums_ref, back_ref = refs[-3:]

    @pl.when(pl.program_id(0) == 0)
    def _():
        vector_sums_ref[...] = before_ref[...]

    def put(image, rows, values):
        d_input_ref[rows, :] = values.astype(jnp.bfloat16)

    input_back_steps(
        put, length, x_ref, d_projected_ref, d_middle_ref, qkv_t_ref, vectors_ref, vector_sums_ref, back_ref
    )


def last_input_kernel(
    images, spread, length, first, place_ref, x_ref, d_projected_ref, d_middle_ref, qkv_t_ref, vectors_ref, before_ref,
    d_input_ref, _, *refs,
):
    pieces, (vector_sums_ref, wide_ref, back_ref) = refs[:spread], refs[spread:]

    @pl.when(pl.program_id(0) == 0)
    def _():
        vector_sums_ref[...] = before_ref[...]
        for image in range(first):
            rows = slice(image * length, (image + 1) * length)
            put_image(wide_ref, image, images, d_input_ref[rows, :].astype(jnp.float32))

    def put(image, rows, values):
        put_image(wide_ref, first + image, images, values)

    input_back_steps(
        put, length, x_ref, d_projected_ref, d_middle_ref, qkv_t_ref, vectors_ref, vector_sums_ref, back_ref
    )

    @pl.when(pl.program_id(0) == pl.num_programs(0) - 1)
    def _():
        narrow_pieces(place_ref, wide_ref, pieces, spread)


def cut(array_ref, parts_ref):
    count = parts_ref.shape[2]
    for member in range(parts_ref.shape[0]):
        parts_ref[member] = array_ref[:, member * count : (member + 1) * count, :]


def pack_kernel(qkv_ref, proj_ref, up_ref, down_ref, first_ref, second_ref):
    rows = first_ref.shape[0]
    folds = [down_ref[fold * rows : (fold + 1) * rows, :] for fold in range(down_ref.shape[0] // rows)]
    for pack_ref, parts in ((first_ref, [qkv_ref[...], proj_ref[...]]), (second_ref, [up_ref[...], *folds])):
        start = 0
        for part in parts:
            pack_ref[:, start : start + part.shape[1]] = part.astype(jnp.bfloat16)
            start += part.shape[1]


def token_kernel(array_ref, own_ref, arrived_ref, _, parts_ref, pair_ref):
    pair_ref[0] = own_ref[...]
    pair_ref[1] = arrived_ref[...]
    cut(array_ref, parts_ref)


def join_kernel(count, *refs):
    size = refs[0].shape[0]
    for at, part_ref in enumerate(refs[:count]):
        refs[-1][at * size : (at + 1) * size] = part_ref[...]


def settle_kernel(spread, place_ref, *refs):
    lists, (output_ref, token_ref) = refs[:-2], refs[-2:]
    token_ref[...] = jnp.zeros_like(token_ref)
    group = place_ref[0] & (spread - 1)
    count = lists[0].shape[1]
    share = len(lists) // spread * count
    for at, piece_ref in enumerate(lists):
        relative, part = at % spread, at // spread
        start = pl.multiple_of((group ^ relative) * share + part * count, count)
        output_ref[:, pl.ds(start, count), :] = piece_ref[...]


def lane_table(rows, columns):
    lane = lax.broadcasted_iota(jnp.int32, (rows, 128), 1)
    table = jnp.zeros((rows, 128), jnp.float32)
    for at, column in enumerate(columns):
        table = jnp.where(lane == at, column, table)
    return table


def added(parts):
    while len(parts) > 1:
        parts = [sum(parts[at : at + 2][1:], parts[at]) for at in range(0, len(parts), 2)]
    return parts[0]


def row_sum(values):
    return jnp.sum(values, axis=1, keepdims=True)


def after_kernel(*refs):
    pass


def gradient_kernel(count, *refs):
    block_parts, sums, refs = refs[:count], refs[count : count + 3], refs[count + 3 :]
    masters, rows_old, refs = refs[:4], refs[4:8], refs[8:]
    grads, (row_ref, message_ref) = refs[:4], refs[4:]
    blocks = added([part[0].astype(jnp.float32) for part in block_parts])
    rows, up_cols = grads[2].shape
    qkv_cols, out_cols = grads[0].shape[1], grads[1].shape[1]
    folds = grads[3].shape[0] // rows
    up = blocks[:, :up_cols]
    downs = [blocks[:, up_cols + fold * out_cols :][:, :out_cols] for fold in range(folds)]
    start = up_cols + folds * out_cols
    qkv = blocks[:, start : start + qkv_cols]
    proj = blocks[:, start + qkv_cols :]
    grads[0][...] = qkv
    grads[1][...] = proj
    grads[2][...] = up
    for fold in range(folds):
        grads[3][fold * rows : (fold + 1) * rows, :] = downs[fold]
    squares = [part * part + tiny_square for part in (qkv, proj, up, *downs)]
    row_ref[...] = lane_table(rows, [row_sum(square) for square in squares]).T[: row_ref.shape[0], :]
    width = message_ref.shape[1]
    message_ref[...] = jnp.zeros_like(message_ref)
    for at, square in enumerate((*squares[:3], added(squares[3:]))):
        message_ref[at : at + 1, : square.shape[1]] = column_sum(square)
    scalars = [column_sum(row_sum(master[...] * master[...])) for master in masters]
    scalars += [row_sum(part[...].reshape(1, part.shape[0])) for part in rows_old]
    message_ref[4:5, :128] = lane_table(1, scalars)
    att_ref, ff_ref, up_ref = sums
    count = up_ref.shape[1] // width
    message_ref[8:12, :] = att_ref[:4]
    message_ref[12:15, :] = ff_ref[:3]
    for at in range(count):
        message_ref[15 + at : 16 + at, :] = up_ref[:, at * width : (at + 1) * width]
    message_ref[15 + count : 16 + count, :] = ff_ref[3:4]


def column_kernel(row_ref, *refs):
    parts, (cols_ref, message_ref) = refs[:-3], refs[-2:]
    total = added([part[...] for part in parts])
    cols_ref[...] = total[:8]
    width = total.shape[1]
    rows = row_ref.shape[1]
    message_ref[...] = jnp.zeros_like(message_ref)
    message_ref[:8, :rows] = row_ref[...]
    columns = [row_sum(total[which : which + 1]) for which in range(4)]
    squares = [total[4:5, which : which + 1] for which in range(4)]
    message_ref[8:9, :] = lane_table(1, columns + squares)
    for tile in range(width // 128):
        message_ref[16 * (tile + 1) : 16 * (tile + 2), :] = total[8:, tile * 128 : (tile + 1) * 128]


def update_kernel(count, heights, widths, *refs):
    messages, refs = refs[:count], refs[count:]
    cols_ref, vectors_ref, moment_ref, refs = refs[0], refs[1], refs[2], refs[3:]
    grads, masters, rows_old, cols_old, refs = refs[:4], refs[4:8], refs[8:12], refs[12:16], refs[17:]
    news, cols_new, rows_out, refs = refs[:4], refs[4:8], refs[8:12], refs[12:]
    vector_grad_ref, moment_new_ref, vector_new_ref = refs
    sums = added([message[...] for message in messages])
    height = grads[0].shape[0]
    folds = grads[3].shape[0] // height
    lanes = [[0], [1], [2], list(range(3, 3 + folds))]
    share = 1.0 - decay_rate
    for which in range(4):
        entries = heights[which] * widths[which]
        cols = cols_old[which].shape[0]
        new = decay_rate * cols_old[which][...].reshape(1, cols) + share / heights[which] * cols_ref[
            which : which + 1, :cols
        ]
        cols_new[which][...] = new[0]
        old_total = cols_ref[4:5, 4 + which : 5 + which]
        mean_rows = (decay_rate * old_total + share / widths[which] * sums[8:9, which : which + 1]) / heights[which]
        rate = step_rate * jnp.sqrt(sums[8:9, 4 + which : 5 + which] / entries)
        across = new / mean_rows
        old = rows_old[which][...].reshape(1, len(lanes[which]) * height)
        row_sums = jnp.concatenate([sums[lane : lane + 1, :height] for lane in lanes[which]], axis=1)
        row = decay_rate * old + share / widths[which] * row_sums
        rows_out[which][...] = row[0]
        for fold in range(len(lanes[which])):
            part = slice(fold * height, (fold + 1) * height)
            column = jnp.broadcast_to(row[:, part], (8, height)).T[:, :1]
            news[which][part, :] = masters[which][part, :] - rate * grads[which][part, :] * lax.rsqrt(column * across)
    vectors = vectors_ref[...]
    count = vectors.shape[0]
    gradient = jnp.concatenate(
        [sums[16 * (tile + 1) : 16 * (tile + 1) + count] for tile in range(vectors.shape[1] // 128)], axis=1
    )
    vector_grad_ref[...] = gradient
    moment = decay_rate * moment_ref[...] + share * (gradient * gradient + tiny_square)
    moment_new_ref[...] = moment
    spread = jnp.sqrt(jnp.mean(vectors * vectors, axis=1, keepdims=True))
    vector_new_ref[...] = vectors - step_rate * spread * gradient * lax.rsqrt(moment)


def packed_body(
    tokens, keep_mask, cotangent, qkv_weight, proj_weight, up_weight, down_weight, vectors,
    qkv_rows, qkv_cols, proj_rows, proj_cols, up_rows, up_cols, down_rows, down_cols, vector_moment,
):
    spread, dp_size = lax.axis_size("group"), lax.axis_size("dp")
    low, high = jnp.bfloat16, jnp.float32
    place = linear_place().astype(jnp.int32).reshape(1)
    group = lax.axis_index("group")
    held, slots, width = tokens.shape
    images, length = keep_mask.shape
    hidden = up_weight.shape[1] * spread
    total = images * length
    rows = qkv_weight.shape[0]
    folds = down_weight.shape[0] // rows
    core_bits = (1,)
    near_bits = tuple(1 << at for at in range(1, spread.bit_length()))
    far_bits = tuple(spread << at for at in range(1, dp_size.bit_length() - 1))
    half = spread * dp_size // 2

    anywhere = pl.BlockSpec(memory_space=pl.ANY)
    in_smem = pl.BlockSpec(memory_space=pltpu.SMEM)

    in_vmem = pl.BlockSpec(memory_space=pltpu.VMEM)
    small = functools.partial(
        pl.pallas_call, compiler_params=pltpu.CompilerParams(vmem_limit_bytes=vmem_bytes)
    )
    masters = (qkv_weight, proj_weight, up_weight, down_weight)
    parted = jax.ShapeDtypeStruct((spread, slots, images, width), low)

    def after(array, awaited):
        return small(
            after_kernel,
            in_specs=[anywhere] * (1 + len(awaited)),
            out_specs=anywhere,
            out_shape=jax.ShapeDtypeStruct(array.shape, array.dtype),
            input_output_aliases={0: 0},
        )(array, *awaited)

    def to_group(parts):
        return lax.all_to_all(parts, "group", split_axis=0, concat_axis=0, tiled=True)

    def to_images(parts):
        return to_group(parts).reshape(total, width)

    def exchange(parts):
        return [parts[0]] + [permute(part, relative) for relative, part in enumerate(parts) if relative]

    def settle(parts):
        parts = [part.reshape(slots, -1, width) for part in parts]
        whole, token = small(
            functools.partial(settle_kernel, spread),
            in_specs=[in_smem] + [in_vmem] * len(parts),
            out_specs=[in_vmem] * 2,
            out_shape=[
                jax.ShapeDtypeStruct((slots, held, width), low),
                jax.ShapeDtypeStruct((8, 128), high),
            ],
        )(place, *parts)
        return whole.transpose(1, 0, 2), token

    first_cols = qkv_weight.shape[1] + proj_weight.shape[1]
    second_cols = up_weight.shape[1] + folds * down_weight.shape[1]
    pack_own, second_pack = small(
        pack_kernel,
        out_shape=[jax.ShapeDtypeStruct((rows, first_cols), low), jax.ShapeDtypeStruct((rows, second_cols), low)],
    )(*masters)
    second_blocks = lax.all_gather(second_pack, ("dp", "group"), axis=0)
    across_y, across_x = near_bits
    pack_arrived = permute(pack_own, across_y)
    cotangent_cut = small(cut, out_shape=parted)(cotangent.transpose(1, 0, 2))
    token_cut, first_pair = small(
        token_kernel,
        in_specs=[in_vmem] * 3 + [anywhere],
        out_shape=[
            parted,
            jax.ShapeDtypeStruct((2, rows, first_cols), low),
        ],
    )(tokens.transpose(1, 0, 2), pack_own, pack_arrived, cotangent_cut)
    inputs = to_images(token_cut)

    def gather_far(pair):
        return [pair] + [permute(pair, mask) for mask in direct_masks(far_bits)]

    def join(parts, awaited=()):
        count = len(parts) * parts[0].shape[0]
        return small(
            functools.partial(join_kernel, len(parts)),
            in_specs=[in_vmem] * len(parts) + [anywhere] * len(awaited),
            out_shape=jax.ShapeDtypeStruct((count, *parts[0].shape[1:]), low),
        )(*parts, *awaited)

    def gather_rest(held):
        arrived = permute(held, across_x)
        return [held, arrived, permute(held, core_bits[0]), permute(arrived, core_bits[0])]

    first_far = join(gather_far(first_pair))
    upstream = to_images(cotangent_cut)
    first_blocks = gather_rest(first_far)

    step_rows = PER_STEP * length
    block = (step_rows, width)
    pairs = width // (2 * HEAD_DIM)
    steps = images // PER_STEP
    statics = (images, dp_size, spread)
    wide = scratch(width // 128, total, 128)
    probs_block = (PER_STEP, pairs, length, 2 * length)
    attention_outs = [
        ((total, 3 * width), low, (step_rows, 3 * width)),
        ((images, *probs_block[1:]), low, probs_block),
        ((total, width), low, block),
        ((total, width), high, block),
    ]
    attention_flops = (2 * total * width * 4 * width + 8 * total * length * width) // steps
    attention_scratches = [scratch(length, images), scratch(step_rows, width, dtype=low)]
    *attention, x, w_qkv, w_proj, qkv_t, proj_t = call_kernel(
        first_attention_kernel, statics, steps,
        ["place"] + [None] * 7,
        attention_outs
        + [
            ((total, width), low, None),
            ((width, 3 * width), low, None),
            ((width, width), low, None),
            ((3 * width, width), low, None),
            ((width, width), low, None),
        ],
        [scratch(dp_size * spread, rows, first_cols, dtype=low), wide] + attention_scratches,
        (place, inputs, *first_blocks, keep_mask, vectors),
        attention_flops * steps // 16,
    )
    qkv, probs, attended, middle = attention
    piece = ((slots * images, width), low, None)
    ff_rows = FF_PER_STEP * length
    ff_block = (ff_rows, width)
    results = call_kernel(
        feed_forward_packed_kernel, statics, images // FF_PER_STEP,
        ["place"] + [None] * 2 + [ff_block, ff_block] + [None] * 2,
        [piece] * spread
        + [
            ((total, width), high, ff_block),
            ((total, width), low, ff_block),
            ((half, rows, second_cols), low, None),
            ((half, rows, second_cols), low, None),
            ((width, width), high, None),
            ((8, width), high, None),
            ((1, hidden), high, None),
        ],
        [
            scratch(width, hidden, dtype=low),
            scratch(hidden, width, dtype=low),
            scratch(hidden, width, dtype=low),
            scratch(1, hidden),
            wide,
            scratch(ff_rows, width, dtype=low),
            scratch(width, ff_rows, dtype=low),
            scratch(ff_rows, width, dtype=low),
            scratch(width, ff_rows, dtype=low),
            scratch(ff_rows, width),
            scratch(ff_rows, 128),
            scratch(ff_rows, width),
            scratch(ff_rows, width),
            scratch(hidden, width, dtype=low),
            scratch(width, hidden, dtype=low),
            scratch(width, hidden),
            scratch(width, hidden),
        ],
        (
            place, upstream, second_blocks, middle, attended, proj_t, vectors,
        ),
        12 * total * width * hidden + 4 * total * width * width, total * hidden,
    )
    d_middle, d_attended, ff_keep, ff_leave, proj_total, ff_sums, up_sums = results[spread:]

    ff_first = permute(ff_leave, core_bits[0])
    ff_count = half // 2
    ff_next = add_wide(ff_keep[ff_count:], ff_first[ff_count:]).astype(low)
    ff_arrived = permute(ff_next, across_x)
    output_parts = exchange(results[:spread])
    pack_half = ((half, rows, first_cols), low, None)
    wide_rows = (step_rows, 3 * width)
    d_projected, qkv_keep, qkv_leave, att_sums = call_kernel(
        attention_back_packed_kernel, (dp_size, spread), steps,
        ["place", block, wide_rows, probs_block, block, None, None, "await"],
        [((total, 3 * width), low, wide_rows), pack_half, pack_half, ((8, width), high, None)],
        [scratch(step_rows, width, dtype=low), scratch(width, 3 * width)],
        (place, x, qkv, probs, d_attended, vectors, proj_total, ff_next),
        2 * total * width * 3 * width + 16 * total * length * width,
    )
    qkv_arrived = permute(after(qkv_leave, output_parts[1:] + [ff_arrived]), core_bits[0])
    input_flops = 2 * total * width * 3 * width
    input_ins = [block, wide_rows, block, None, None, None]
    input_outs = [((total, width), low, block), ((8, width), high, None)]
    d_input, att_sums = call_kernel(
        first_input_kernel, (length,), 1, input_ins, input_outs, [scratch(step_rows, width)],
        (x, d_projected, d_middle, qkv_t, vectors, att_sums), input_flops // steps,
    )
    ff_quarter = half // 4
    ff_last = add_wide(
        ff_keep[ff_quarter:ff_count], ff_first[ff_quarter:ff_count], ff_arrived[ff_quarter:]
    ).astype(low)
    ff_last_arrived = permute(ff_last, across_y)
    qkv_held = add_wide(qkv_keep, qkv_arrived)
    leaving = [
        qkv_held[at : at + ff_quarter].astype(low) for at in range(ff_quarter, half, ff_quarter)
    ]
    qkv_held = qkv_held[:ff_quarter]
    qkv_parts = [permute(part, mask) for part, mask in zip(leaving, direct_masks(near_bits))]
    d_input, att_sums = call_kernel(
        first_input_kernel, (length,), 1, input_ins + ["await"] * 2, input_outs, [scratch(step_rows, width)],
        (x, d_projected, d_middle, qkv_t, vectors, att_sums, d_input, leaving[0]), input_flops // steps,
        first_step=1, aliases={6: 0},
    )
    ff_held = add_wide(
        ff_keep[:ff_quarter], ff_first[:ff_quarter], ff_arrived[:ff_quarter], ff_last_arrived
    )
    qkv_held = add_wide(qkv_held, *qkv_parts)
    blocks = jnp.concatenate([ff_held, qkv_held], axis=2)
    far_leaving = [blocks[at : at + 1].astype(low) for at in range(1, blocks.shape[0])]
    block_parts = [blocks[:1]] + [permute(part, mask) for part, mask in zip(far_leaving, direct_masks(far_bits))]
    results = call_kernel(
        last_input_kernel, (images, spread, length, 2 * PER_STEP), steps - 2,
        ["place"] + input_ins + [None, "await"],
        [piece] * spread + [((8, width), high, None)],
        [wide, scratch(step_rows, width)],
        (place, x, d_projected, d_middle, qkv_t, vectors, att_sums, d_input, far_leaving[0]), input_flops // steps * (steps - 2),
        first_step=2,
    )
    att_sums = results[spread]
    input_pieces = list(results[:spread])
    heights = [master.shape[0] * dp_size for master in masters]
    widths = [master.shape[1] * spread for master in masters]
    rows_old, cols_old = [qkv_rows, proj_rows, up_rows, down_rows], [qkv_cols, proj_cols, up_cols, down_cols]

    def like(*arrays):
        return [jax.ShapeDtypeStruct(array.shape, high) for array in arrays]

    operands = (*block_parts, att_sums, ff_sums, up_sums, *masters, *rows_old)
    *grads, row_sums, message = small(
        functools.partial(gradient_kernel, len(block_parts)),
        out_shape=like(*masters) + [jax.ShapeDtypeStruct((8, rows), high), jax.ShapeDtypeStruct((24, width), high)],
    )(*operands)
    input_pieces[1] = after(input_pieces[1], [row_sums])
    output_parts[0] = after(output_parts[0], [row_sums])
    block_output, settled = settle(output_parts)
    input_grad, input_settled = settle(exchange(input_pieces))
    message = added([message] + [permute(message, mask) for mask in direct_masks((across_x, far_bits[0]))])
    for bit in far_bits[1:-1]:
        message = message + permute(message, bit)
    messages = [message, permute(message, far_bits[-1])]
    col_sums, message = small(
        column_kernel,
        in_specs=[in_vmem] * (1 + len(messages)) + [anywhere],
        out_shape=[
            jax.ShapeDtypeStruct((8, width), high),
            jax.ShapeDtypeStruct((16 + width // 8, 128), high),
        ],
    )(row_sums, *messages, settled)
    messages = [message] + [permute(message, mask) for mask in range(1, spread)]
    operands = (*messages, col_sums, vectors, vector_moment, *grads, *masters, *rows_old, *cols_old)
    results = small(
        functools.partial(update_kernel, len(messages), heights, widths),
        in_specs=[in_vmem] * len(operands) + [anywhere],
        out_shape=like(*masters, *cols_old, *rows_old, vectors, vectors, vectors),
    )(*operands, input_settled)
    news, cols_new, rows_out = results[:4], results[4:8], results[8:12]
    vector_grad, vector_moment_new, vector_new = results[12:]
    factored = []
    for which in range(4):
        factored += [grads[which], rows_out[which], cols_new[which], news[which]]
    return (block_output, input_grad, *factored, vector_grad, vector_moment_new, vector_new)


def body(*arrays):
    spread, dp_size = lax.axis_size("group"), lax.axis_size("dp")
    rows, images = arrays[3].shape[0], arrays[1].shape[0]
    slots, width = arrays[0].shape[1:]
    folds = arrays[6].shape[0] // rows
    powers = all(size & (size - 1) == 0 for size in (spread, dp_size))
    fits = powers and spread == 4 and dp_size > 2
    fits = fits and arrays[5].shape[1] <= width and folds <= 5
    fits = fits and rows % 16 == 0 and images % FF_PER_STEP == 0 and images > 2 * PER_STEP and images % 16 == 0 and slots % 4 == 0
    return packed_body(*arrays) if fits else general_body(*arrays)


def solution(mesh):
    in_specs = (
        P("dp", "group", None),
        P(("dp", "group"), None),
        P("dp", "group", None),
        P("dp", "group"),
        P("dp", "group"),
        P("dp", "group"),
        P("dp", "group"),
        P(),
        P("dp"),
        P("group"),
        P("dp"),
        P("group"),
        P("dp"),
        P("group"),
        P("dp"),
        P("group"),
        P(),
    )
    out_specs = (
        P("dp", "group", None),
        P("dp", "group", None),
        P("dp", "group"),
        P("dp"),
        P("group"),
        P("dp", "group"),
        P("dp", "group"),
        P("dp"),
        P("group"),
        P("dp", "group"),
        P("dp", "group"),
        P("dp"),
        P("group"),
        P("dp", "group"),
        P("dp", "group"),
        P("dp"),
        P("group"),
        P("dp", "group"),
        P(),
        P(),
        P(),
    )
    return jax.shard_map(body, mesh=mesh, in_specs=in_specs, out_specs=out_specs, check_vma=False)
```

```python
import functools
import math

import jax
import jax.numpy as jnp
from jax import lax
from jax.experimental import pallas as pl
from jax.experimental.pallas import tpu as pltpu
from jax.sharding import PartitionSpec as P

HEAD_DIM = 64
STEP_NUMBER = 10


step_rate = 0.3
norm_epsilon = 1e-06
tiny_square = 1e-30
decay_rate = 1.0 - STEP_NUMBER ** (-0.8)
LOG2_E = 1.4426950408889634


def axis_bits(name):
    count = lax.axis_size(name)
    return [(name, 1 << place) for place in range(count.bit_length() - 1)]


def swap_partner(array, step):
    name, bit = step
    count = lax.axis_size(name)
    return lax.ppermute(array, name, [(rank, rank ^ bit) for rank in range(count)])


def upper_side(step):
    name, bit = step
    return (lax.axis_index(name) & bit) != 0


def gather_blocks(array, steps):
    for step in steps:
        arrived = swap_partner(array, step)
        upper = upper_side(step)
        array = jnp.stack([jnp.where(upper, arrived, array), jnp.where(upper, array, arrived)])
    return array


def scatter_sum(array, steps):
    for step in steps:
        upper = upper_side(step)
        leaving = jnp.where(upper, array[0], array[1]).astype(jnp.bfloat16)
        arrived = swap_partner(leaving, step)
        array = jnp.where(upper, array[1], array[0]).astype(jnp.float32) + arrived.astype(jnp.float32)
    return array


def sum_everywhere(array, steps):
    for step in steps:
        array = array + swap_partner(array, step)
    return array


def sum_parts(parts, steps):
    flat = [part.reshape(-1) for part in parts]
    total = sum_everywhere(jnp.concatenate(flat), steps)
    result, start = [], 0
    for part in parts:
        result.append(total[start : start + part.size].reshape(part.shape))
        start += part.size
    return result


def block_order(steps):
    order = []
    for name in ("dp", "group"):
        bits = sorted((step for step in steps if step[0] == name), key=lambda step: -step[1])
        order.append([steps.index(step) for step in bits])
    return order


def blocks_to_whole(blocks, steps):
    count = len(steps)
    rows, cols = blocks.shape[count:]
    dp_axes, group_axes = block_order(steps)
    dp_axes = [count - 1 - axis for axis in dp_axes]
    group_axes = [count - 1 - axis for axis in group_axes]
    whole = blocks.transpose(dp_axes + [count] + group_axes + [count + 1])
    return whole.reshape(rows << len(dp_axes), cols << len(group_axes))


def whole_to_blocks(whole, steps):
    dp_axes, group_axes = block_order(steps)
    rows = whole.shape[0] >> len(dp_axes)
    cols = whole.shape[1] >> len(group_axes)
    split = whole.reshape([2] * len(dp_axes) + [rows] + [2] * len(group_axes) + [cols])
    places = dp_axes + [len(steps)] + group_axes + [len(steps) + 1]
    return split.transpose([places.index(axis) for axis in range(len(places))])


PER_STEP = 4
FF_PER_STEP = 4
SLICE = 48
FF_CHUNK = 256
vmem_bytes = 60 * 1024 * 1024


def dot(left, right, left_axis=1, right_axis=0):
    return lax.dot_general(
        left, right, (((left_axis,), (right_axis,)), ((), ())), preferred_element_type=jnp.float32
    )


def normal_form(values):
    center = jnp.mean(values, axis=-1, keepdims=True)
    centered = values - center
    spread = jnp.mean(centered * centered, axis=-1, keepdims=True)
    scale = lax.rsqrt(spread + norm_epsilon)
    return centered * scale, scale


def norm_back(grad, unit, scale, gain):
    weighted = grad * gain
    along = jnp.mean(weighted * unit, axis=-1, keepdims=True)
    level = jnp.mean(weighted, axis=-1, keepdims=True)
    return scale * (weighted - level - unit * along)


def slices_of(count):
    return [slice(start, start + SLICE) for start in range(0, count, SLICE)]


def fold_rows(values):
    return jnp.sum(values.reshape(values.shape[0] // 8, 8, values.shape[1]), axis=0)


def column_sum(values):
    return jnp.sum(values, axis=0, keepdims=True)


def pair_mask(length):
    return lax.broadcasted_iota(jnp.int32, (length, 2 * HEAD_DIM), 1) < HEAD_DIM


def lane_tiles(count):
    return [slice(start, min(start + 128, count)) for start in range(0, count, 128)]


def stack_heads(pair, first):
    none = jnp.zeros_like(pair)
    return jnp.concatenate([jnp.where(first, pair, none), jnp.where(first, none, pair)], axis=0)


def join_heads(rows, first):
    length = rows.shape[0] // 2
    return jnp.where(first, rows[:length], rows[length:])


def gelu_and_slope(pre):
    bell = jnp.exp2(pre * pre * (-0.5 * LOG2_E))
    base = 1.0 + (0.3275911 * 0.5**0.5) * jnp.abs(pre)
    inverse = pl.reciprocal(base, approx=True)
    inverse = inverse * (2.0 - base * inverse)
    poly = inverse * (
        0.5 * 0.254829592
        + inverse
        * (
            0.5 * -0.284496736
            + inverse
            * (0.5 * 1.421413741 + inverse * (0.5 * -1.453152027 + inverse * (0.5 * 1.061405429)))
        )
    )
    tail = poly * bell
    below = jnp.where(pre >= 0, 1.0 - tail, tail)
    return pre * below, below + pre * bell * 0.3989422804014327


def widen(source_ref, wide_ref, images):
    tiles, total, lanes = wide_ref.shape
    rows_at_once = 8 * images

    @pl.loop(0, total // rows_at_once)
    def _(part):
        rows = pl.ds(pl.multiple_of(part * rows_at_once, rows_at_once), rows_at_once)
        for tile in range(tiles):
            cols = slice(tile * lanes, (tile + 1) * lanes)
            wide_ref[tile, rows, :] = source_ref[rows, cols].astype(jnp.float32)


def narrow(wide_ref, target_ref, images):
    tiles, total, lanes = wide_ref.shape
    rows_at_once = 8 * images

    @pl.loop(0, total // rows_at_once)
    def _(part):
        rows = pl.ds(pl.multiple_of(part * rows_at_once, rows_at_once), rows_at_once)
        for tile in range(tiles):
            cols = slice(tile * lanes, (tile + 1) * lanes)
            target_ref[rows, cols] = wide_ref[tile, rows, :].astype(target_ref.dtype)


def take_image(wide_ref, image, images):
    tiles, total, _ = wide_ref.shape
    rows = pl.ds(image, total // images, images)
    return jnp.concatenate([wide_ref[tile, rows, :] for tile in range(tiles)], axis=1)


def put_image(wide_ref, image, images, values):
    tiles, total, lanes = wide_ref.shape
    rows = pl.ds(image, total // images, images)
    for tile in range(tiles):
        wide_ref[tile, rows, :] = values[:, tile * lanes : (tile + 1) * lanes]


def attention_kernel(
    images, tokens_ref, bias_ref, w_qkv_ref, w_proj_ref, vectors_ref,
    x_ref, qkv_ref, probs_ref, attended_ref, middle_ref, wide_ref, normed_ref,
):
    @pl.when(pl.program_id(0) == 0)
    def _():
        widen(tokens_ref, wide_ref, images)
        to_image_rows(wide_ref, x_ref, images)

    attention_steps(
        x_ref, lambda image: bias_ref[image], w_qkv_ref, w_proj_ref, vectors_ref,
        qkv_ref, probs_ref, attended_ref, middle_ref, normed_ref,
    )


def to_image_rows(wide_ref, x_ref, images):
    length = wide_ref.shape[1] // images

    @pl.loop(0, images)
    def _(image):
        rows = pl.ds(pl.multiple_of(image * length, length), length)
        x_ref[rows, :] = take_image(wide_ref, image, images).astype(jnp.bfloat16)


def attention_steps(
    x_ref, bias_column, w_qkv_ref, w_proj_ref, vectors_ref,
    qkv_ref, probs_ref, attended_ref, middle_ref, normed_ref,
):
    per_step, _, length, _ = probs_ref.shape
    step_rows, width = middle_ref.shape
    base = 0 if x_ref.shape[0] == step_rows else pl.program_id(0) * step_rows

    for rows in slices_of(step_rows):
        x = x_ref[pl.ds(pl.multiple_of(base + rows.start, SLICE), SLICE), :].astype(jnp.float32)
        unit, _ = normal_form(x)
        normed_ref[rows, :] = (unit * vectors_ref[0:1] + vectors_ref[1:2]).astype(jnp.bfloat16)
    shift = jnp.concatenate(
        [vectors_ref[2:3], jnp.zeros((1, width), jnp.float32), vectors_ref[3:4]], axis=1
    )
    for start in range(0, 3 * width, 512):
        cols = slice(start, min(start + 512, 3 * width))
        projected = dot(normed_ref[...], w_qkv_ref[:, cols]) + shift[:, cols]
        qkv_ref[:, cols] = projected.astype(jnp.bfloat16)

    pairs = width // (2 * HEAD_DIM)
    first = pair_mask(length)
    place = lax.broadcasted_iota(jnp.int32, (length, 2 * length), 0)
    asker = lax.broadcasted_iota(jnp.int32, (length, 2 * length), 1)
    own = place == jnp.where(asker >= length, asker - length, asker)

    def scores_of(image):
        rows = slice(image * length, (image + 1) * length)
        result = []
        for pair in range(pairs):
            low = pair * 2 * HEAD_DIM
            queries = stack_heads(qkv_ref[rows, low : low + 2 * HEAD_DIM], first)
            result.append(dot(qkv_ref[rows, width + low : width + low + 2 * HEAD_DIM], queries, 1, 1))
        return result

    next_scores = scores_of(0)
    for image in range(per_step):
        rows = slice(image * length, (image + 1) * length)
        all_scores = next_scores
        if image + 1 < per_step:
            next_scores = scores_of(image + 1)
        column = bias_column(image)
        for cols in lane_tiles(2 * length):
            bias = jnp.where(own[:, cols], 0.0, column)
            for pair in range(pairs):
                scores = all_scores[pair][:, cols] * (HEAD_DIM**-0.5 * LOG2_E) + bias
                weights = jnp.exp2(scores - jnp.max(scores, axis=0, keepdims=True))
                probs = weights * (1.0 / jnp.sum(weights, axis=0, keepdims=True))
                probs_ref[image, pair, :, cols] = probs.astype(jnp.bfloat16)
        for pair in range(pairs):
            low = pair * 2 * HEAD_DIM
            values = qkv_ref[rows, 2 * width + low : 2 * width + low + 2 * HEAD_DIM]
            attended = join_heads(dot(probs_ref[image, pair], values, 0, 0), first)
            attended_ref[rows, low : low + 2 * HEAD_DIM] = attended.astype(jnp.bfloat16)

    middle_ref[...] = (
        x_ref[pl.ds(pl.multiple_of(base, length), step_rows), :].astype(jnp.float32)
        + dot(attended_ref[...], w_proj_ref[...])
        + vectors_ref[4:5]
    )


def feed_forward_kernel(
    images, middle_ref, cotangent_ref, attended_ref, w_up_ref, w_down_ref, proj_t_ref, vectors_ref, bias_up_ref,
    output_ref, d_middle_ref, d_attended_ref, up_grad_ref, down_grad_ref, proj_grad_ref, vector_sums_ref, up_sums_ref,
    wide_ref, *scratches,
):
    up_total_ref, down_total_ref, proj_total_ref = scratches[-3:]

    @pl.when(pl.program_id(0) == 0)
    def _():
        widen(cotangent_ref, wide_ref, images)

    feed_forward_steps(
        images, middle_ref, attended_ref, w_up_ref, w_down_ref, proj_t_ref, vectors_ref, bias_up_ref,
        d_middle_ref, d_attended_ref, vector_sums_ref, up_sums_ref, wide_ref, *scratches,
    )

    @pl.when(pl.program_id(0) == pl.num_programs(0) - 1)
    def _():
        narrow(wide_ref, output_ref, images)
        up_grad_ref[...] = up_total_ref[...].astype(jnp.bfloat16)
        down_grad_ref[...] = down_total_ref[...].T.astype(jnp.bfloat16)
        proj_grad_ref[...] = proj_total_ref[...].astype(jnp.bfloat16)


def feed_forward_steps(
    images, middle_ref, attended_ref, w_up_ref, w_down_ref, proj_t_ref, vectors_ref, bias_up_ref,
    d_middle_ref, d_attended_ref, vector_sums_ref, up_sums_ref,
    wide_ref, normed_ref, normed_t_ref, dy_ref, dy_t_ref, unit_ref, scale_ref, ahead_ref, back_ref,
    up_t_ref, down_t_ref, up_total_ref, down_total_ref, proj_total_ref,
):
    step = pl.program_id(0)
    length = wide_ref.shape[1] // images
    hidden = w_up_ref.shape[1]
    per_step = middle_ref.shape[0] // length

    @pl.when(step == 0)
    def _():
        for total in (up_total_ref, down_total_ref, proj_total_ref, vector_sums_ref, up_sums_ref):
            total[...] = jnp.zeros_like(total)
        up_t_ref[...] = w_up_ref[...].T
        down_t_ref[...] = w_down_ref[...].T

    for image in range(per_step):
        rows = slice(image * length, (image + 1) * length)
        dy = take_image(wide_ref, step * per_step + image, images)
        dy_ref[rows, :] = dy.astype(jnp.bfloat16)
        vector_sums_ref[3:4] += column_sum(dy)
        unit, scale = normal_form(middle_ref[rows, :])
        unit_ref[rows, :] = unit
        scale_ref[rows, :] = jnp.broadcast_to(scale, (length, scale_ref.shape[1]))
        normed_ref[rows, :] = (unit * vectors_ref[5:6] + vectors_ref[6:7]).astype(jnp.bfloat16)
    normed_t_ref[...] = normed_ref[...].T
    dy_t_ref[...] = dy_ref[...].T
    chunks = hidden // FF_CHUNK

    def cols_of(chunk):
        return slice(chunk * FF_CHUNK, (chunk + 1) * FF_CHUNK)

    def into(chunk):
        cols = cols_of(chunk)
        pre = dot(normed_ref[...], w_up_ref[:, cols])
        return pre + bias_up_ref[:, cols], dot(dy_ref[...], down_t_ref[:, cols])

    def across(pre, d_active):
        active, slope = gelu_and_slope(pre)
        return active.astype(jnp.bfloat16), (d_active * slope).astype(jnp.bfloat16)

    def out_of(chunk, active, d_hidden):
        cols = cols_of(chunk)
        ahead, back = dot(active, w_down_ref[cols, :]), dot(d_hidden, up_t_ref[cols, :])
        if chunk == 0:
            ahead_ref[...] = ahead
            back_ref[...] = back
        else:
            ahead_ref[...] += ahead
            back_ref[...] += back
        down_total_ref[:, cols] += dot(dy_t_ref[...], active)
        up_total_ref[:, cols] += dot(normed_t_ref[...], d_hidden)
        up_sums_ref[:, cols] += column_sum(d_hidden.astype(jnp.float32))

    entered, crossed = into(0), None
    for chunk in range(chunks + 1):
        next_entered = into(chunk + 1) if chunk + 1 < chunks else None
        next_crossed = across(*entered) if chunk < chunks else None
        if crossed is not None:
            out_of(chunk - 1, *crossed)
        entered, crossed = next_entered, next_crossed

    for image in range(per_step):
        rows = slice(image * length, (image + 1) * length)
        output = middle_ref[rows, :] + ahead_ref[rows, :] + vectors_ref[11:12]
        put_image(wide_ref, step * per_step + image, images, output)
        unit = unit_ref[rows, :]
        grad = back_ref[rows, :]
        vector_sums_ref[1:2] += column_sum(grad * unit)
        vector_sums_ref[2:3] += column_sum(grad)
        d_middle = dy_ref[rows, :].astype(jnp.float32) + norm_back(
            grad, unit, scale_ref[rows, 0:1], vectors_ref[5:6]
        )
        d_middle_ref[rows, :] = d_middle
        d_branch = d_middle.astype(jnp.bfloat16)
        dy_ref[rows, :] = d_branch
        vector_sums_ref[0:1] += column_sum(d_branch.astype(jnp.float32))
    proj_total_ref[...] += dot(attended_ref[...], dy_ref[...], 0, 0)
    d_attended_ref[...] = dot(dy_ref[...], proj_t_ref[...]).astype(jnp.bfloat16)


def attention_back_kernel(
    images, x_ref, qkv_ref, probs_ref, d_attended_ref, d_middle_ref, qkv_t_ref, vectors_ref,
    input_grad_ref, qkv_grad_ref, vector_sums_ref, wide_ref, normed_ref, d_projected_ref, back_ref, qkv_total_ref,
):
    @pl.when(pl.program_id(0) == 0)
    def _():
        qkv_total_ref[...] = jnp.zeros_like(qkv_total_ref)
        vector_sums_ref[...] = jnp.zeros_like(vector_sums_ref)

    def put(image, rows, values):
        put_image(wide_ref, image, images, values)

    attention_back_steps(
        x_ref, qkv_ref, probs_ref, d_attended_ref, vectors_ref, vector_sums_ref, normed_ref, d_projected_ref, qkv_total_ref
    )
    input_back_steps(
        put, probs_ref.shape[2], x_ref, d_projected_ref, d_middle_ref, qkv_t_ref, vectors_ref, vector_sums_ref, back_ref
    )

    @pl.when(pl.program_id(0) == pl.num_programs(0) - 1)
    def _():
        narrow(wide_ref, input_grad_ref, images)
        qkv_grad_ref[...] = qkv_total_ref[...].astype(jnp.bfloat16)


def attention_back_steps(
    x_ref, qkv_ref, probs_ref, d_attended_ref, vectors_ref, vector_sums_ref, normed_ref, d_projected_ref, qkv_total_ref
):
    width = x_ref.shape[1]
    length = probs_ref.shape[2]
    per_step = probs_ref.shape[0]

    pairs = width // (2 * HEAD_DIM)
    first = pair_mask(length)
    scale = HEAD_DIM**-0.5

    def places(image, pair):
        low = pair * 2 * HEAD_DIM
        rows = slice(image * length, (image + 1) * length)
        return rows, [slice(part * width + low, part * width + low + 2 * HEAD_DIM) for part in range(3)]

    def entering(image):
        result = []
        for pair in range(pairs):
            rows, cols = places(image, pair)
            d_attended = stack_heads(d_attended_ref[rows, cols[0]], first)
            d_values = dot(probs_ref[image, pair], d_attended)
            d_projected_ref[rows, cols[2]] = d_values.astype(jnp.bfloat16)
            result.append(dot(qkv_ref[rows, cols[2]], d_attended, 1, 1))
        return result

    next_probs = entering(0)
    for image in range(per_step):
        all_d_probs = next_probs
        if image + 1 < per_step:
            next_probs = entering(image + 1)
        all_d_scores = []
        for pair in range(pairs):
            parts = []
            for cols in lane_tiles(2 * length):
                probs, d_probs = probs_ref[image, pair, :, cols].astype(jnp.float32), all_d_probs[pair][:, cols]
                along = jnp.sum(d_probs * probs, axis=0, keepdims=True)
                parts.append((probs * (d_probs - along)).astype(jnp.bfloat16))
            all_d_scores.append(jnp.concatenate(parts, axis=1))
        for pair in range(pairs):
            rows, cols = places(image, pair)
            d_scores = all_d_scores[pair]
            queries = stack_heads(qkv_ref[rows, cols[0]], first)
            d_queries = join_heads(dot(d_scores, qkv_ref[rows, cols[1]], 0, 0), first) * scale
            d_projected_ref[rows, cols[0]] = d_queries.astype(jnp.bfloat16)
            d_projected_ref[rows, cols[1]] = (dot(d_scores, queries) * scale).astype(jnp.bfloat16)

    query_sums = value_sums = jnp.zeros((8, width), jnp.float32)
    for rows in slices_of(x_ref.shape[0]):
        query_sums += fold_rows(d_projected_ref[rows, :width].astype(jnp.float32))
        value_sums += fold_rows(d_projected_ref[rows, 2 * width :].astype(jnp.float32))
        unit, _ = normal_form(x_ref[rows, :].astype(jnp.float32))
        normed_ref[rows, :] = (unit * vectors_ref[0:1] + vectors_ref[1:2]).astype(jnp.bfloat16)
    vector_sums_ref[2:3] += column_sum(query_sums)
    vector_sums_ref[3:4] += column_sum(value_sums)
    qkv_total_ref[...] += dot(normed_ref[...], d_projected_ref[...], 0, 0)


def input_back_steps(
    put, length, x_ref, d_projected_ref, d_middle_ref, qkv_t_ref, vectors_ref, vector_sums_ref, back_ref
):
    step = pl.program_id(0)
    per_step = x_ref.shape[0] // length
    back_ref[...] = dot(d_projected_ref[...], qkv_t_ref[...])
    gain_sums = shift_sums = jnp.zeros((8, x_ref.shape[1]), jnp.float32)
    for rows in slices_of(x_ref.shape[0]):
        unit, scale = normal_form(x_ref[rows, :].astype(jnp.float32))
        grad = back_ref[rows, :]
        gain_sums += fold_rows(grad * unit)
        shift_sums += fold_rows(grad)
        back_ref[rows, :] = d_middle_ref[rows, :] + norm_back(grad, unit, scale, vectors_ref[0:1])
    vector_sums_ref[0:1] += column_sum(gain_sums)
    vector_sums_ref[1:2] += column_sum(shift_sums)
    for image in range(per_step):
        rows = slice(image * length, (image + 1) * length)
        put(step * per_step + image, rows, back_ref[rows, :])


def whole_block(shape):
    return pl.BlockSpec(shape, lambda step: (0,) * len(shape))


def step_block(shape, first=0):
    return pl.BlockSpec(shape, lambda step: (first + step,) + (0,) * (len(shape) - 1))


def scratch(*shape, dtype=jnp.float32):
    return pltpu.VMEM(shape, dtype)


def call_kernel(kernel, statics, steps, ins, outs, scratches, operands, flops, transcendentals=0, first_step=0, aliases={}):
    in_specs = [
        pl.BlockSpec(memory_space=pltpu.SMEM)
        if block == "place"
        else pl.BlockSpec(memory_space=pl.ANY)
        if block == "await"
        else whole_block(op.shape) if block is None else step_block(block, first_step)
        for op, block in zip(operands, ins)
    ]
    out_specs = [
        whole_block(shape) if block is None else step_block(block, first_step) for shape, dtype, block in outs
    ]
    moved = sum(op.size * op.dtype.itemsize for op in operands) + sum(
        math.prod(shape) * jnp.dtype(dtype).itemsize for shape, dtype, block in outs
    )
    return pl.pallas_call(
        functools.partial(kernel, *statics),
        grid=(steps,),
        in_specs=in_specs,
        out_specs=out_specs,
        out_shape=[jax.ShapeDtypeStruct(shape, dtype) for shape, dtype, block in outs],
        scratch_shapes=scratches,
        input_output_aliases=aliases,
        compiler_params=pltpu.CompilerParams(vmem_limit_bytes=vmem_bytes),
        cost_estimate=pl.CostEstimate(
            flops=flops * 8, bytes_accessed=moved, transcendentals=transcendentals
        ),
    )(*operands)


def attention_forward(tokens, bias, w_qkv, w_proj, vectors):
    images, length, _ = bias.shape
    total, width = tokens.shape
    pairs = width // (2 * HEAD_DIM)
    rows = PER_STEP * length
    low, high = jnp.bfloat16, jnp.float32
    outs = [
        ((total, width), low, None),
        ((total, 3 * width), low, (rows, 3 * width)),
        ((images, pairs, length, 2 * length), low, (PER_STEP, pairs, length, 2 * length)),
        ((total, width), low, (rows, width)),
        ((total, width), high, (rows, width)),
    ]
    return call_kernel(
        attention_kernel, (images,), images // PER_STEP,
        [None, (PER_STEP, length, 1), None, None, None], outs,
        [scratch(width // 128, total, 128), scratch(rows, width, dtype=low)],
        (tokens, bias, w_qkv, w_proj, vectors),
        2 * total * width * 4 * width + 8 * total * length * width,
    )


def feed_forward(images, middle, cotangent, attended, w_up, w_down, w_proj, vectors):
    total, width = middle.shape
    hidden = w_up.shape[1]
    rows = total // images * FF_PER_STEP
    low, high = jnp.bfloat16, jnp.float32
    block = (rows, width)
    outs = [
        ((total, width), low, None),
        ((total, width), high, block),
        ((total, width), low, block),
        ((width, hidden), low, None),
        ((hidden, width), low, None),
        ((width, width), low, None),
        ((8, width), high, None),
        ((1, hidden), high, None),
    ]
    scratches = [
        scratch(width // 128, total, 128),
        scratch(rows, width, dtype=low),
        scratch(width, rows, dtype=low),
        scratch(rows, width, dtype=low),
        scratch(width, rows, dtype=low),
        scratch(rows, width),
        scratch(rows, 128),
        scratch(rows, width),
        scratch(rows, width),
        scratch(hidden, width, dtype=low),
        scratch(width, hidden, dtype=low),
        scratch(width, hidden),
        scratch(width, hidden),
        scratch(width, width),
    ]
    return call_kernel(
        feed_forward_kernel, (images,), images // FF_PER_STEP,
        [block, None, block, None, None, None, None, None], outs, scratches,
        (middle, cotangent, attended, w_up, w_down, w_proj.T, vectors, vectors[7:11].reshape(1, hidden)),
        12 * total * width * hidden + 4 * total * width * width, total * hidden,
    )


def attention_back(x, qkv, probs, d_attended, d_middle, w_qkv, vectors):
    images, pairs, length, _ = probs.shape
    total, width = x.shape
    rows = PER_STEP * length
    low, high = jnp.bfloat16, jnp.float32
    block = (rows, width)
    outs = [
        ((total, width), low, None),
        ((width, 3 * width), low, None),
        ((8, width), high, None),
    ]
    scratches = [
        scratch(width // 128, total, 128),
        scratch(rows, width, dtype=low),
        scratch(rows, 3 * width, dtype=low),
        scratch(rows, width),
        scratch(width, 3 * width),
    ]
    return call_kernel(
        attention_back_kernel, (images,), images // PER_STEP,
        [block, (rows, 3 * width), (PER_STEP, pairs, length, 2 * length), block, block, None, None],
        outs, scratches, (x, qkv, probs, d_attended, d_middle, w_qkv.T, vectors),
        4 * total * width * 3 * width + 16 * total * length * width,
    )

def linear_place():
    return lax.axis_index("dp") * lax.axis_size("group") + lax.axis_index("group")


def permute(array, mask):
    count = lax.axis_size("dp") * lax.axis_size("group")
    return lax.ppermute(array, ("dp", "group"), [(rank, rank ^ mask) for rank in range(count)])


def direct_masks(bits):
    masks = [0]
    for bit in bits:
        masks = masks + [mask | bit for mask in masks]
    return masks[1:]


def add_wide(first, *rest):
    total = first.astype(jnp.float32)
    for part in rest:
        total = total + part.astype(jnp.float32)
    return total


def packed_place(mask, spread, count):
    return ((mask >> 1) & (spread - 1)) * (count // (2 * spread)) + (mask >> (spread.bit_length()))


def scatter_step(held, bits):
    masks = direct_masks(bits)
    size = held.shape[0] // (len(masks) + 1)
    parts = [
        permute(held[size * (at + 1) : size * (at + 2)].astype(jnp.bfloat16), mask)
        for at, mask in enumerate(masks)
    ]
    return held[:size], parts


def add_wide(first, *rest):
    total = first.astype(jnp.float32)
    for part in rest:
        total = total + part.astype(jnp.float32)
    return total


def packed_place(mask, spread, count):
    return ((mask >> 1) & (spread - 1)) * (count // (2 * spread)) + (mask >> (spread.bit_length()))


def gather_step(held, bits):
    return held + [permute(part, mask) for mask in direct_masks(bits) for part in held]


def gathered_place(mask, count):
    return (mask & 1) * (count // 2) + ((mask >> 2) & 1) * (count // 4) + (mask >> 3) * 2 + ((mask >> 1) & 1)


def unpack(place_ref, block_refs, packed_ref, put, dp_size, spread):
    place = place_ref[0]
    size = block_refs[0].shape[0]
    for at, block_ref in enumerate(block_refs):
        packed_ref[at * size : (at + 1) * size] = block_ref[...]
    count = dp_size * spread
    for row in range(dp_size):
        for col in range(spread):
            put(row, col, packed_ref[gathered_place((row * spread + col) ^ place, count)])


def unpack_in_order(blocks_ref, put, dp_size, spread):
    for row in range(dp_size):
        for col in range(spread):
            put(row, col, blocks_ref[row * spread + col])


def pack(place_ref, take, keep_ref, leave_ref, dp_size, spread):
    place = place_ref[0]
    odd = (place & 1) == 1
    for row in range(dp_size):
        for col in range(0, spread, 2):
            at = packed_place((row * spread + col) ^ place, spread, dp_size * spread)
            even_block, odd_block = take(row, col), take(row, col + 1)
            keep_ref[at] = jnp.where(odd, odd_block, even_block)
            leave_ref[at] = jnp.where(odd, even_block, odd_block)


def narrow_pieces(place_ref, wide_ref, piece_refs, spread):
    tiles, _, lanes = wide_ref.shape
    rows_of_piece = piece_refs[0].shape[0]
    step = 64
    group = place_ref[0] & (spread - 1)
    for relative, piece_ref in enumerate(piece_refs):
        base = (group ^ relative) * rows_of_piece

        @pl.loop(0, rows_of_piece // step)
        def _(part):
            target = pl.ds(pl.multiple_of(part * step, step), step)
            source = pl.ds(pl.multiple_of(base + part * step, step), step)
            for tile in range(tiles):
                cols = slice(tile * lanes, (tile + 1) * lanes)
                piece_ref[target, cols] = wide_ref[tile, source, :].astype(jnp.bfloat16)


def general_body(
    tokens,
    keep_mask,
    cotangent,
    qkv_weight,
    proj_weight,
    up_weight,
    down_weight,
    vectors,
    qkv_rows,
    qkv_cols,
    proj_rows,
    proj_cols,
    up_rows,
    up_cols,
    down_rows,
    down_cols,
    vector_moment,
):
    masters = (qkv_weight, proj_weight, up_weight, down_weight)
    lowered = tuple((master.astype(jnp.bfloat16) for master in masters))
    dp_bits, group_bits = axis_bits("dp"), axis_bits("group")
    gather_steps = dp_bits[1:] + group_bits[1:] + dp_bits[:1] + group_bits[:1]
    scatter_steps = gather_steps[::-1]
    w_qkv, w_proj, w_up, w_down = tuple(
        blocks_to_whole(gather_blocks(part, gather_steps), gather_steps) for part in lowered
    )
    spread = lax.axis_size("group")

    def slots_in(array):
        held, slots, width = array.shape
        parts = array.transpose(1, 0, 2).reshape(slots, spread, held // spread, width)
        parts = lax.all_to_all(
            parts.transpose(1, 0, 2, 3), "group", split_axis=0, concat_axis=0, tiled=True
        )
        return parts.reshape(spread * slots * (held // spread), width)

    def slots_out(array):
        held, slots, width = tokens.shape
        parts = array.reshape(spread, slots, held // spread, width)
        parts = lax.all_to_all(parts, "group", split_axis=0, concat_axis=0, tiled=True)
        return parts.transpose(1, 0, 2, 3).reshape(slots, held, width).transpose(1, 0, 2)

    images = keep_mask.shape[0]
    bias = jnp.where(keep_mask > 0, 0.0, -1e30)[:, :, None]
    x, qkv, probs, attended, middle = attention_forward(
        slots_in(tokens), bias, w_qkv, w_proj, vectors
    )
    output, d_middle, d_attended, up_grad, down_grad, proj_grad, ff_sums, up_sums = feed_forward(
        images, middle, slots_in(cotangent), attended, w_up, w_down, w_proj, vectors
    )
    block_output = slots_out(output)
    d_input, qkv_grad, att_sums = attention_back(
        x, qkv, probs, d_attended, d_middle, w_qkv, vectors
    )
    input_grad = slots_out(d_input)
    local_vectors = jnp.concatenate(
        [att_sums[:4], ff_sums[:3], up_sums.reshape(4, -1), ff_sums[3:4]], axis=0
    )
    vector_grad = sum_everywhere(local_vectors, group_bits + dp_bits)
    local_grads = (qkv_grad, proj_grad, up_grad, down_grad)
    owned = tuple(
        scatter_sum(whole_to_blocks(part, scatter_steps), scatter_steps) for part in local_grads
    )
    squares = tuple((gradient * gradient + tiny_square for gradient in owned))
    row_parts = tuple((jnp.sum(square, axis=1) for square in squares)) + tuple(
        (jnp.sum(master * master, axis=1) for master in masters)
    )
    row_sums = sum_parts(row_parts, group_bits)
    rows_old = (qkv_rows, proj_rows, up_rows, down_rows)
    cols_old = (qkv_cols, proj_cols, up_cols, down_cols)
    total_cols = tuple((gradient.shape[1] * lax.axis_size("group") for gradient in owned))
    total_rows = tuple((gradient.shape[0] * lax.axis_size("dp") for gradient in owned))
    rows_new = tuple(
        (
            decay_rate * rows_old[which] + (1.0 - decay_rate) * row_sums[which] / total_cols[which]
            for which in range(4)
        )
    )
    col_parts = (
        tuple((jnp.sum(square, axis=0) for square in squares))
        + tuple((jnp.sum(row_stat) for row_stat in rows_new))
        + tuple((jnp.sum(row_sums[4 + which]) for which in range(4)))
    )
    col_sums = sum_parts(col_parts, dp_bits)
    results = []
    for which in range(4):
        cols_new = (
            decay_rate * cols_old[which] + (1.0 - decay_rate) * col_sums[which] / total_rows[which]
        )
        mean_rows = col_sums[4 + which] / total_rows[which]
        spread = jnp.sqrt(col_sums[8 + which] / (total_rows[which] * total_cols[which]))
        second = rows_new[which][:, None] * cols_new[None, :] / mean_rows
        updated = masters[which] - step_rate * spread * owned[which] * lax.rsqrt(second)
        results.append((owned[which], rows_new[which], cols_new, updated))
    vector_moment_new = decay_rate * vector_moment + (1.0 - decay_rate) * (
        vector_grad * vector_grad + tiny_square
    )
    row_spread = jnp.sqrt(jnp.mean(vectors * vectors, axis=1, keepdims=True))
    vector_new = vectors - step_rate * row_spread * vector_grad * lax.rsqrt(vector_moment_new)
    return (
        block_output,
        input_grad,
        results[0][0],
        results[0][1],
        results[0][2],
        results[0][3],
        results[1][0],
        results[1][1],
        results[1][2],
        results[1][3],
        results[2][0],
        results[2][1],
        results[2][2],
        results[2][3],
        results[3][0],
        results[3][1],
        results[3][2],
        results[3][3],
        vector_grad,
        vector_moment_new,
        vector_new,
    )


def first_attention_kernel(images, dp_size, spread, place_ref, tokens_ref, *refs):
    blocks, refs = refs[:4], refs[4:]
    keep_ref, vectors_ref, *outs, x_ref, w_qkv_ref, w_proj_ref, qkv_t_ref, proj_t_ref = refs[:-4]
    packed_ref, wide_ref, bias_ref, normed_ref = refs[-4:]
    rows = packed_ref.shape[1]
    qkv_cols, proj_cols = w_qkv_ref.shape[1] // spread, w_proj_ref.shape[1] // spread

    @pl.when(pl.program_id(0) == 0)
    def _():
        widen(tokens_ref, wide_ref, images)
        to_image_rows(wide_ref, x_ref, images)

        def put(row, col, block):
            down = slice(row * rows, (row + 1) * rows)
            w_qkv_ref[down, col * qkv_cols : (col + 1) * qkv_cols] = block[:, :qkv_cols]
            w_proj_ref[down, col * proj_cols : (col + 1) * proj_cols] = block[:, qkv_cols:]

        unpack(place_ref, blocks, packed_ref, put, dp_size, spread)
        qkv_t_ref[...] = w_qkv_ref[...].T
        proj_t_ref[...] = w_proj_ref[...].T

    attention_part(0, x_ref, keep_ref, w_qkv_ref, w_proj_ref, vectors_ref, *outs, bias_ref, normed_ref)


def next_attention_kernel(start, x_ref, keep_ref, w_qkv_ref, w_proj_ref, vectors_ref, *refs):
    attention_part(start, x_ref, keep_ref, w_qkv_ref, w_proj_ref, vectors_ref, *refs[-6:])


def attention_part(
    start, x_ref, keep_ref, w_qkv_ref, w_proj_ref, vectors_ref,
    qkv_ref, probs_ref, attended_ref, middle_ref, bias_ref, normed_ref,
):
    @pl.when(pl.program_id(0) == 0)
    def _():
        bias_ref[...] = jnp.where(keep_ref[...] > 0, 0.0, -1e30).T

    def bias_column(image):
        here = start + pl.program_id(0) * probs_ref.shape[0] + image
        lane = lax.broadcasted_iota(jnp.int32, bias_ref.shape, 1)
        return row_sum(jnp.where(lane == here, bias_ref[...], 0.0))

    attention_steps(
        x_ref, bias_column, w_qkv_ref, w_proj_ref, vectors_ref,
        qkv_ref, probs_ref, attended_ref, middle_ref, normed_ref,
    )


def feed_forward_packed_kernel(images, dp_size, spread, place_ref, *refs):
    cotangent_ref, blocks, refs = refs[0], refs[1:5], refs[5:]
    middle_ref, attended_ref, proj_t_ref, vectors_ref = refs[:4]
    outputs, refs = refs[4 : 4 + spread], refs[4 + spread :]
    d_middle_ref, d_attended_ref, keep_ref, leave_ref, proj_total_ref, vector_sums_ref, up_sums_ref = refs[:7]
    w_up_ref, w_down_ref, down_low_ref, packed_ref, bias_up_ref, wide_ref = refs[7:13]
    scratches = refs[13:]
    width = w_up_ref.shape[0]
    up_total_ref, down_total_ref = scratches[-2:]
    rows = packed_ref.shape[1]
    up_cols = w_up_ref.shape[1] // spread
    out_cols = w_down_ref.shape[1] // spread
    folds = w_down_ref.shape[0] // w_up_ref.shape[0]

    @pl.when(pl.program_id(0) == 0)
    def _():
        widen(cotangent_ref, wide_ref, images)
        for fold in range(bias_up_ref.shape[1] // width):
            bias_up_ref[:, fold * width : (fold + 1) * width] = vectors_ref[7 + fold : 8 + fold]

        def put(row, col, block):
            w_up_ref[row * rows : (row + 1) * rows, col * up_cols : (col + 1) * up_cols] = block[:, :up_cols]
            for fold in range(folds):
                down = (row * folds + fold) * rows
                start = up_cols + fold * out_cols
                w_down_ref[down : down + rows, col * out_cols : (col + 1) * out_cols] = block[
                    :, start : start + out_cols
                ]

        unpack(place_ref, blocks, packed_ref, put, dp_size, spread)

    feed_forward_steps(
        images, middle_ref, attended_ref, w_up_ref, w_down_ref, proj_t_ref, vectors_ref, bias_up_ref,
        d_middle_ref, d_attended_ref, vector_sums_ref, up_sums_ref, wide_ref, *scratches, proj_total_ref,
    )

    @pl.when(pl.program_id(0) == pl.num_programs(0) - 1)
    def _():
        narrow_pieces(place_ref, wide_ref, outputs, spread)
        down_low_ref[...] = down_total_ref[...].T.astype(jnp.bfloat16)

        def take(row, col):
            across = slice(row * rows, (row + 1) * rows)
            cols = slice(col * out_cols, (col + 1) * out_cols)
            parts = [up_total_ref[across, col * up_cols : (col + 1) * up_cols].astype(jnp.bfloat16)]
            for fold in range(folds):
                down = (row * folds + fold) * rows
                parts.append(down_low_ref[down : down + rows, cols])
            return jnp.concatenate(parts, axis=1)

        pack(place_ref, take, keep_ref, leave_ref, dp_size, spread)


def attention_back_packed_kernel(
    dp_size, spread, place_ref, x_ref, qkv_ref, probs_ref, d_attended_ref, vectors_ref, proj_total_ref, _,
    d_projected_ref, keep_ref, leave_ref, vector_sums_ref, normed_ref, total_ref,
):
    @pl.when(pl.program_id(0) == 0)
    def _():
        total_ref[...] = jnp.zeros_like(total_ref)
        vector_sums_ref[...] = jnp.zeros_like(vector_sums_ref)

    attention_back_steps(
        x_ref, qkv_ref, probs_ref, d_attended_ref, vectors_ref, vector_sums_ref, normed_ref, d_projected_ref, total_ref
    )

    @pl.when(pl.program_id(0) == pl.num_programs(0) - 1)
    def _():
        rows = keep_ref.shape[1]
        qkv_cols, proj_cols = total_ref.shape[1] // spread, proj_total_ref.shape[1] // spread

        def take(row, col):
            down = slice(row * rows, (row + 1) * rows)
            parts = [
                total_ref[down, col * qkv_cols : (col + 1) * qkv_cols],
                proj_total_ref[down, col * proj_cols : (col + 1) * proj_cols],
            ]
            return jnp.concatenate(parts, axis=1).astype(jnp.bfloat16)

        pack(place_ref, take, keep_ref, leave_ref, dp_size, spread)


def first_input_kernel(
    length, x_ref, d_projected_ref, d_middle_ref, qkv_t_ref, vectors_ref, before_ref, *refs
):
    d_input_ref, vector_sums_ref, back_ref = refs[-3:]

    @pl.when(pl.program_id(0) == 0)
    def _():
        vector_sums_ref[...] = before_ref[...]

    def put(image, rows, values):
        d_input_ref[rows, :] = values.astype(jnp.bfloat16)

    input_back_steps(
        put, length, x_ref, d_projected_ref, d_middle_ref, qkv_t_ref, vectors_ref, vector_sums_ref, back_ref
    )


def last_input_kernel(
    images, spread, length, first, place_ref, x_ref, d_projected_ref, d_middle_ref, qkv_t_ref, vectors_ref, before_ref,
    d_input_ref, _, *refs,
):
    pieces, (vector_sums_ref, wide_ref, back_ref) = refs[:spread], refs[spread:]

    @pl.when(pl.program_id(0) == 0)
    def _():
        vector_sums_ref[...] = before_ref[...]
        for image in range(first):
            rows = slice(image * length, (image + 1) * length)
            put_image(wide_ref, image, images, d_input_ref[rows, :].astype(jnp.float32))

    def put(image, rows, values):
        put_image(wide_ref, first + image, images, values)

    input_back_steps(
        put, length, x_ref, d_projected_ref, d_middle_ref, qkv_t_ref, vectors_ref, vector_sums_ref, back_ref
    )

    @pl.when(pl.program_id(0) == pl.num_programs(0) - 1)
    def _():
        narrow_pieces(place_ref, wide_ref, pieces, spread)


def cut(array_ref, parts_ref):
    count = parts_ref.shape[2]
    for member in range(parts_ref.shape[0]):
        parts_ref[member] = array_ref[:, member * count : (member + 1) * count, :]


def pack_kernel(qkv_ref, proj_ref, up_ref, down_ref, pack_ref):
    rows, start = pack_ref.shape[0], 0
    parts = [qkv_ref[...], proj_ref[...], up_ref[...]]
    parts += [down_ref[fold * rows : (fold + 1) * rows, :] for fold in range(down_ref.shape[0] // rows)]
    for part in parts:
        pack_ref[:, start : start + part.shape[1]] = part.astype(jnp.bfloat16)
        start += part.shape[1]


def token_kernel(array_ref, own_ref, arrived_ref, _, parts_ref, first_ref, second_ref):
    start = first_ref.shape[2]
    for at, pack_ref in enumerate((own_ref, arrived_ref)):
        first_ref[at] = pack_ref[:, :start]
        second_ref[at] = pack_ref[:, start:]
    cut(array_ref, parts_ref)


def join_kernel(count, *refs):
    size = refs[0].shape[0]
    for at, part_ref in enumerate(refs[:count]):
        refs[-1][at * size : (at + 1) * size] = part_ref[...]


def settle_kernel(spread, place_ref, *refs):
    lists, (output_ref, token_ref) = refs[:-2], refs[-2:]
    token_ref[...] = jnp.zeros_like(token_ref)
    group = place_ref[0] & (spread - 1)
    count = lists[0].shape[1]
    share = len(lists) // spread * count
    for at, piece_ref in enumerate(lists):
        relative, part = at % spread, at // spread
        start = pl.multiple_of((group ^ relative) * share + part * count, count)
        output_ref[:, pl.ds(start, count), :] = piece_ref[...]


def lane_table(rows, columns):
    lane = lax.broadcasted_iota(jnp.int32, (rows, 128), 1)
    table = jnp.zeros((rows, 128), jnp.float32)
    for at, column in enumerate(columns):
        table = jnp.where(lane == at, column, table)
    return table


def added(parts):
    while len(parts) > 1:
        parts = [sum(parts[at : at + 2][1:], parts[at]) for at in range(0, len(parts), 2)]
    return parts[0]


def row_sum(values):
    return jnp.sum(values, axis=1, keepdims=True)


def after_kernel(*refs):
    pass


def gradient_kernel(count, *refs):
    block_parts, sums, refs = refs[:count], refs[count : count + 3], refs[count + 3 :]
    masters, rows_old, refs = refs[:4], refs[4:8], refs[8:]
    grads, (row_ref, message_ref) = refs[:4], refs[4:]
    blocks = added([part[0].astype(jnp.float32) for part in block_parts])
    rows, up_cols = grads[2].shape
    qkv_cols, out_cols = grads[0].shape[1], grads[1].shape[1]
    folds = grads[3].shape[0] // rows
    up = blocks[:, :up_cols]
    downs = [blocks[:, up_cols + fold * out_cols :][:, :out_cols] for fold in range(folds)]
    start = up_cols + folds * out_cols
    qkv = blocks[:, start : start + qkv_cols]
    proj = blocks[:, start + qkv_cols :]
    grads[0][...] = qkv
    grads[1][...] = proj
    grads[2][...] = up
    for fold in range(folds):
        grads[3][fold * rows : (fold + 1) * rows, :] = downs[fold]
    squares = [part * part + tiny_square for part in (qkv, proj, up, *downs)]
    row_ref[...] = lane_table(rows, [row_sum(square) for square in squares]).T[: row_ref.shape[0], :]
    width = message_ref.shape[1]
    message_ref[...] = jnp.zeros_like(message_ref)
    for at, square in enumerate((*squares[:3], added(squares[3:]))):
        message_ref[at : at + 1, : square.shape[1]] = column_sum(square)
    scalars = [column_sum(row_sum(master[...] * master[...])) for master in masters]
    scalars += [row_sum(part[...].reshape(1, part.shape[0])) for part in rows_old]
    message_ref[4:5, :128] = lane_table(1, scalars)
    att_ref, ff_ref, up_ref = sums
    count = up_ref.shape[1] // width
    message_ref[8:12, :] = att_ref[:4]
    message_ref[12:15, :] = ff_ref[:3]
    for at in range(count):
        message_ref[15 + at : 16 + at, :] = up_ref[:, at * width : (at + 1) * width]
    message_ref[15 + count : 16 + count, :] = ff_ref[3:4]


def column_kernel(row_ref, *refs):
    parts, (cols_ref, message_ref) = refs[:-3], refs[-2:]
    total = added([part[...] for part in parts])
    cols_ref[...] = total[:8]
    width = total.shape[1]
    rows = row_ref.shape[1]
    message_ref[...] = jnp.zeros_like(message_ref)
    message_ref[:8, :rows] = row_ref[...]
    columns = [row_sum(total[which : which + 1]) for which in range(4)]
    squares = [total[4:5, which : which + 1] for which in range(4)]
    message_ref[8:9, :] = lane_table(1, columns + squares)
    for tile in range(width // 128):
        message_ref[16 * (tile + 1) : 16 * (tile + 2), :] = total[8:, tile * 128 : (tile + 1) * 128]


def update_kernel(count, heights, widths, *refs):
    messages, refs = refs[:count], refs[count:]
    cols_ref, vectors_ref, moment_ref, refs = refs[0], refs[1], refs[2], refs[3:]
    grads, masters, rows_old, cols_old, refs = refs[:4], refs[4:8], refs[8:12], refs[12:16], refs[17:]
    news, cols_new, rows_out, refs = refs[:4], refs[4:8], refs[8:12], refs[12:]
    vector_grad_ref, moment_new_ref, vector_new_ref = refs
    sums = added([message[...] for message in messages])
    height = grads[0].shape[0]
    folds = grads[3].shape[0] // height
    lanes = [[0], [1], [2], list(range(3, 3 + folds))]
    share = 1.0 - decay_rate
    for which in range(4):
        entries = heights[which] * widths[which]
        cols = cols_old[which].shape[0]
        new = decay_rate * cols_old[which][...].reshape(1, cols) + share / heights[which] * cols_ref[
            which : which + 1, :cols
        ]
        cols_new[which][...] = new[0]
        old_total = cols_ref[4:5, 4 + which : 5 + which]
        mean_rows = (decay_rate * old_total + share / widths[which] * sums[8:9, which : which + 1]) / heights[which]
        rate = step_rate * jnp.sqrt(sums[8:9, 4 + which : 5 + which] / entries)
        across = new / mean_rows
        old = rows_old[which][...].reshape(1, len(lanes[which]) * height)
        row_sums = jnp.concatenate([sums[lane : lane + 1, :height] for lane in lanes[which]], axis=1)
        row = decay_rate * old + share / widths[which] * row_sums
        rows_out[which][...] = row[0]
        for fold in range(len(lanes[which])):
            part = slice(fold * height, (fold + 1) * height)
            column = jnp.broadcast_to(row[:, part], (8, height)).T[:, :1]
            news[which][part, :] = masters[which][part, :] - rate * grads[which][part, :] * lax.rsqrt(column * across)
    vectors = vectors_ref[...]
    count = vectors.shape[0]
    gradient = jnp.concatenate(
        [sums[16 * (tile + 1) : 16 * (tile + 1) + count] for tile in range(vectors.shape[1] // 128)], axis=1
    )
    vector_grad_ref[...] = gradient
    moment = decay_rate * moment_ref[...] + share * (gradient * gradient + tiny_square)
    moment_new_ref[...] = moment
    spread = jnp.sqrt(jnp.mean(vectors * vectors, axis=1, keepdims=True))
    vector_new_ref[...] = vectors - step_rate * spread * gradient * lax.rsqrt(moment)


def packed_body(
    tokens, keep_mask, cotangent, qkv_weight, proj_weight, up_weight, down_weight, vectors,
    qkv_rows, qkv_cols, proj_rows, proj_cols, up_rows, up_cols, down_rows, down_cols, vector_moment,
):
    spread, dp_size = lax.axis_size("group"), lax.axis_size("dp")
    low, high = jnp.bfloat16, jnp.float32
    place = linear_place().astype(jnp.int32).reshape(1)
    group = lax.axis_index("group")
    held, slots, width = tokens.shape
    images, length = keep_mask.shape
    hidden = up_weight.shape[1] * spread
    total = images * length
    rows = qkv_weight.shape[0]
    folds = down_weight.shape[0] // rows
    core_bits = (1,)
    near_bits = tuple(1 << at for at in range(1, spread.bit_length()))
    far_bits = tuple(spread << at for at in range(1, dp_size.bit_length() - 1))
    half = spread * dp_size // 2

    anywhere = pl.BlockSpec(memory_space=pl.ANY)
    in_smem = pl.BlockSpec(memory_space=pltpu.SMEM)

    in_vmem = pl.BlockSpec(memory_space=pltpu.VMEM)
    small = functools.partial(
        pl.pallas_call, compiler_params=pltpu.CompilerParams(vmem_limit_bytes=vmem_bytes)
    )
    masters = (qkv_weight, proj_weight, up_weight, down_weight)
    parted = jax.ShapeDtypeStruct((spread, slots, images, width), low)

    def after(array, awaited):
        return small(
            after_kernel,
            in_specs=[anywhere] * (1 + len(awaited)),
            out_specs=anywhere,
            out_shape=jax.ShapeDtypeStruct(array.shape, array.dtype),
            input_output_aliases={0: 0},
        )(array, *awaited)

    def to_group(parts):
        return lax.all_to_all(parts, "group", split_axis=0, concat_axis=0, tiled=True)

    def to_images(parts):
        return to_group(parts).reshape(total, width)

    def exchange(parts):
        return [parts[0]] + [permute(part, relative) for relative, part in enumerate(parts) if relative]

    def settle(parts):
        parts = [part.reshape(slots, -1, width) for part in parts]
        whole, token = small(
            functools.partial(settle_kernel, spread),
            in_specs=[in_smem] + [in_vmem] * len(parts),
            out_specs=[in_vmem] * 2,
            out_shape=[
                jax.ShapeDtypeStruct((slots, held, width), low),
                jax.ShapeDtypeStruct((8, 128), high),
            ],
        )(place, *parts)
        return whole.transpose(1, 0, 2), token

    first_cols = qkv_weight.shape[1] + proj_weight.shape[1]
    second_cols = up_weight.shape[1] + folds * down_weight.shape[1]
    pack_own = small(pack_kernel, out_shape=jax.ShapeDtypeStruct((rows, first_cols + second_cols), low))(*masters)
    across_y, across_x = near_bits
    pack_arrived = permute(pack_own, across_y)
    cotangent_cut = small(cut, out_shape=parted)(cotangent.transpose(1, 0, 2))
    token_cut, first_pair, second_pair = small(
        token_kernel,
        in_specs=[in_vmem] * 3 + [anywhere],
        out_shape=[
            parted,
            jax.ShapeDtypeStruct((2, rows, first_cols), low),
            jax.ShapeDtypeStruct((2, rows, second_cols), low),
        ],
    )(tokens.transpose(1, 0, 2), pack_own, pack_arrived, cotangent_cut)
    inputs = to_images(token_cut)

    def gather_far(pair):
        return [pair] + [permute(pair, mask) for mask in direct_masks(far_bits)]

    def join(parts, awaited=()):
        count = len(parts) * parts[0].shape[0]
        return small(
            functools.partial(join_kernel, len(parts)),
            in_specs=[in_vmem] * len(parts) + [anywhere] * len(awaited),
            out_shape=jax.ShapeDtypeStruct((count, *parts[0].shape[1:]), low),
        )(*parts, *awaited)

    def gather_rest(held, awaited=None):
        arrived = permute(held, across_x)
        leaving = [held, arrived]
        if awaited is not None:
            leaving = [after(part, [awaited]) for part in leaving]
        return leaving + [permute(part, core_bits[0]) for part in leaving]

    first_far = join(gather_far(first_pair))
    upstream = to_images(cotangent_cut)
    first_blocks = gather_rest(first_far)
    second_far = gather_far(second_pair)

    step_rows = PER_STEP * length
    block = (step_rows, width)
    pairs = width // (2 * HEAD_DIM)
    steps = images // PER_STEP
    statics = (images, dp_size, spread)
    wide = scratch(width // 128, total, 128)
    probs_block = (PER_STEP, pairs, length, 2 * length)
    attention_outs = [
        ((total, 3 * width), low, (step_rows, 3 * width)),
        ((images, *probs_block[1:]), low, probs_block),
        ((total, width), low, block),
        ((total, width), high, block),
    ]
    attention_flops = (2 * total * width * 4 * width + 8 * total * length * width) // steps
    attention_scratches = [scratch(length, images), scratch(step_rows, width, dtype=low)]
    *attention, x, w_qkv, w_proj, qkv_t, proj_t = call_kernel(
        first_attention_kernel, statics, 1,
        ["place"] + [None] * 7,
        attention_outs
        + [
            ((total, width), low, None),
            ((width, 3 * width), low, None),
            ((width, width), low, None),
            ((3 * width, width), low, None),
            ((width, width), low, None),
        ],
        [scratch(dp_size * spread, rows, first_cols, dtype=low), wide] + attention_scratches,
        (place, inputs, *first_blocks, keep_mask, vectors),
        attention_flops,
    )
    second_joined = join(second_far, attention[:1])
    attention = call_kernel(
        next_attention_kernel, (PER_STEP,), steps - 1,
        [block] + [None] * 4 + ["await"] * len(attention),
        attention_outs, attention_scratches,
        (x, keep_mask, w_qkv, w_proj, vectors, *attention),
        attention_flops * (steps - 1), first_step=1,
        aliases={5 + at: at for at in range(len(attention))},
    )
    qkv, probs, attended, middle = attention
    second_blocks = gather_rest(second_joined, middle)
    piece = ((slots * images, width), low, None)
    ff_rows = FF_PER_STEP * length
    ff_block = (ff_rows, width)
    results = call_kernel(
        feed_forward_packed_kernel, statics, images // FF_PER_STEP,
        ["place"] + [None] * 5 + [ff_block, ff_block] + [None] * 2,
        [piece] * spread
        + [
            ((total, width), high, ff_block),
            ((total, width), low, ff_block),
            ((half, rows, second_cols), low, None),
            ((half, rows, second_cols), low, None),
            ((width, width), high, None),
            ((8, width), high, None),
            ((1, hidden), high, None),
        ],
        [
            scratch(width, hidden, dtype=low),
            scratch(hidden, width, dtype=low),
            scratch(hidden, width, dtype=low),
            scratch(dp_size * spread, rows, second_cols, dtype=low),
            scratch(1, hidden),
            wide,
            scratch(ff_rows, width, dtype=low),
            scratch(width, ff_rows, dtype=low),
            scratch(ff_rows, width, dtype=low),
            scratch(width, ff_rows, dtype=low),
            scratch(ff_rows, width),
            scratch(ff_rows, 128),
            scratch(ff_rows, width),
            scratch(ff_rows, width),
            scratch(hidden, width, dtype=low),
            scratch(width, hidden, dtype=low),
            scratch(width, hidden),
            scratch(width, hidden),
        ],
        (
            place, upstream, *second_blocks, middle, attended, proj_t, vectors,
        ),
        12 * total * width * hidden + 4 * total * width * width, total * hidden,
    )
    d_middle, d_attended, ff_keep, ff_leave, proj_total, ff_sums, up_sums = results[spread:]

    ff_first = permute(ff_leave, core_bits[0])
    ff_count = half // 2
    ff_next = add_wide(ff_keep[ff_count:], ff_first[ff_count:]).astype(low)
    ff_arrived = permute(ff_next, across_x)
    output_parts = exchange(results[:spread])
    pack_half = ((half, rows, first_cols), low, None)
    wide_rows = (step_rows, 3 * width)
    d_projected, qkv_keep, qkv_leave, att_sums = call_kernel(
        attention_back_packed_kernel, (dp_size, spread), steps,
        ["place", block, wide_rows, probs_block, block, None, None, "await"],
        [((total, 3 * width), low, wide_rows), pack_half, pack_half, ((8, width), high, None)],
        [scratch(step_rows, width, dtype=low), scratch(width, 3 * width)],
        (place, x, qkv, probs, d_attended, vectors, proj_total, ff_next),
        2 * total * width * 3 * width + 16 * total * length * width,
    )
    qkv_arrived = permute(after(qkv_leave, output_parts[1:] + [ff_arrived]), core_bits[0])
    input_flops = 2 * total * width * 3 * width
    input_ins = [block, wide_rows, block, None, None, None]
    input_outs = [((total, width), low, block), ((8, width), high, None)]
    d_input, att_sums = call_kernel(
        first_input_kernel, (length,), 1, input_ins, input_outs, [scratch(step_rows, width)],
        (x, d_projected, d_middle, qkv_t, vectors, att_sums), input_flops // steps,
    )
    ff_quarter = half // 4
    ff_last = add_wide(
        ff_keep[ff_quarter:ff_count], ff_first[ff_quarter:ff_count], ff_arrived[ff_quarter:]
    ).astype(low)
    ff_last_arrived = permute(ff_last, across_y)
    qkv_held = add_wide(qkv_keep, qkv_arrived)
    leaving = [
        qkv_held[at : at + ff_quarter].astype(low) for at in range(ff_quarter, half, ff_quarter)
    ]
    qkv_held = qkv_held[:ff_quarter]
    qkv_parts = [permute(part, mask) for part, mask in zip(leaving, direct_masks(near_bits))]
    d_input, att_sums = call_kernel(
        first_input_kernel, (length,), 1, input_ins + ["await"] * 2, input_outs, [scratch(step_rows, width)],
        (x, d_projected, d_middle, qkv_t, vectors, att_sums, d_input, leaving[0]), input_flops // steps,
        first_step=1, aliases={6: 0},
    )
    ff_held = add_wide(
        ff_keep[:ff_quarter], ff_first[:ff_quarter], ff_arrived[:ff_quarter], ff_last_arrived
    )
    qkv_held = add_wide(qkv_held, *qkv_parts)
    blocks = jnp.concatenate([ff_held, qkv_held], axis=2)
    far_leaving = [blocks[at : at + 1].astype(low) for at in range(1, blocks.shape[0])]
    block_parts = [blocks[:1]] + [permute(part, mask) for part, mask in zip(far_leaving, direct_masks(far_bits))]
    results = call_kernel(
        last_input_kernel, (images, spread, length, 2 * PER_STEP), steps - 2,
        ["place"] + input_ins + [None, "await"],
        [piece] * spread + [((8, width), high, None)],
        [wide, scratch(step_rows, width)],
        (place, x, d_projected, d_middle, qkv_t, vectors, att_sums, d_input, far_leaving[0]), input_flops // steps * (steps - 2),
        first_step=2,
    )
    att_sums = results[spread]
    input_pieces = list(results[:spread])
    heights = [master.shape[0] * dp_size for master in masters]
    widths = [master.shape[1] * spread for master in masters]
    rows_old, cols_old = [qkv_rows, proj_rows, up_rows, down_rows], [qkv_cols, proj_cols, up_cols, down_cols]

    def like(*arrays):
        return [jax.ShapeDtypeStruct(array.shape, high) for array in arrays]

    operands = (*block_parts, att_sums, ff_sums, up_sums, *masters, *rows_old)
    *grads, row_sums, message = small(
        functools.partial(gradient_kernel, len(block_parts)),
        out_shape=like(*masters) + [jax.ShapeDtypeStruct((8, rows), high), jax.ShapeDtypeStruct((24, width), high)],
    )(*operands)
    input_pieces[1] = after(input_pieces[1], [row_sums])
    output_parts[0] = after(output_parts[0], [row_sums])
    block_output, settled = settle(output_parts)
    input_grad, input_settled = settle(exchange(input_pieces))
    message = added([message] + [permute(message, mask) for mask in direct_masks((across_x, far_bits[0]))])
    for bit in far_bits[1:-1]:
        message = message + permute(message, bit)
    messages = [message, permute(message, far_bits[-1])]
    col_sums, message = small(
        column_kernel,
        in_specs=[in_vmem] * (1 + len(messages)) + [anywhere],
        out_shape=[
            jax.ShapeDtypeStruct((8, width), high),
            jax.ShapeDtypeStruct((16 + width // 8, 128), high),
        ],
    )(row_sums, *messages, settled)
    messages = [message] + [permute(message, mask) for mask in range(1, spread)]
    operands = (*messages, col_sums, vectors, vector_moment, *grads, *masters, *rows_old, *cols_old)
    results = small(
        functools.partial(update_kernel, len(messages), heights, widths),
        in_specs=[in_vmem] * len(operands) + [anywhere],
        out_shape=like(*masters, *cols_old, *rows_old, vectors, vectors, vectors),
    )(*operands, input_settled)
    news, cols_new, rows_out = results[:4], results[4:8], results[8:12]
    vector_grad, vector_moment_new, vector_new = results[12:]
    factored = []
    for which in range(4):
        factored += [grads[which], rows_out[which], cols_new[which], news[which]]
    return (block_output, input_grad, *factored, vector_grad, vector_moment_new, vector_new)


def body(*arrays):
    spread, dp_size = lax.axis_size("group"), lax.axis_size("dp")
    rows, images = arrays[3].shape[0], arrays[1].shape[0]
    slots, width = arrays[0].shape[1:]
    folds = arrays[6].shape[0] // rows
    powers = all(size & (size - 1) == 0 for size in (spread, dp_size))
    fits = powers and spread == 4 and dp_size > 2
    fits = fits and arrays[5].shape[1] <= width and folds <= 5
    fits = fits and rows % 16 == 0 and images % FF_PER_STEP == 0 and images > 2 * PER_STEP and images % 16 == 0 and slots % 4 == 0
    return packed_body(*arrays) if fits else general_body(*arrays)


def solution(mesh):
    in_specs = (
        P("dp", "group", None),
        P(("dp", "group"), None),
        P("dp", "group", None),
        P("dp", "group"),
        P("dp", "group"),
        P("dp", "group"),
        P("dp", "group"),
        P(),
        P("dp"),
        P("group"),
        P("dp"),
        P("group"),
        P("dp"),
        P("group"),
        P("dp"),
        P("group"),
        P(),
    )
    out_specs = (
        P("dp", "group", None),
        P("dp", "group", None),
        P("dp", "group"),
        P("dp"),
        P("group"),
        P("dp", "group"),
        P("dp", "group"),
        P("dp"),
        P("group"),
        P("dp", "group"),
        P("dp", "group"),
        P("dp"),
        P("group"),
        P("dp", "group"),
        P("dp", "group"),
        P("dp"),
        P("group"),
        P("dp", "group"),
        P(),
        P(),
        P(),
    )
    return jax.shard_map(body, mesh=mesh, in_specs=in_specs, out_specs=out_specs, check_vma=False)
```

```python
import functools
import math

import jax
import jax.numpy as jnp
from jax import lax
from jax.experimental import pallas as pl
from jax.experimental.pallas import tpu as pltpu
from jax.sharding import PartitionSpec as P

HEAD_DIM = 64
STEP_NUMBER = 10


step_rate = 0.3
norm_epsilon = 1e-06
tiny_square = 1e-30
decay_rate = 1.0 - STEP_NUMBER ** (-0.8)
LOG2_E = 1.4426950408889634


def axis_bits(name):
    count = lax.axis_size(name)
    return [(name, 1 << place) for place in range(count.bit_length() - 1)]


def swap_partner(array, step):
    name, bit = step
    count = lax.axis_size(name)
    return lax.ppermute(array, name, [(rank, rank ^ bit) for rank in range(count)])


def upper_side(step):
    name, bit = step
    return (lax.axis_index(name) & bit) != 0


def gather_blocks(array, steps):
    for step in steps:
        arrived = swap_partner(array, step)
        upper = upper_side(step)
        array = jnp.stack([jnp.where(upper, arrived, array), jnp.where(upper, array, arrived)])
    return array


def scatter_sum(array, steps):
    for step in steps:
        upper = upper_side(step)
        leaving = jnp.where(upper, array[0], array[1]).astype(jnp.bfloat16)
        arrived = swap_partner(leaving, step)
        array = jnp.where(upper, array[1], array[0]).astype(jnp.float32) + arrived.astype(jnp.float32)
    return array


def sum_everywhere(array, steps):
    for step in steps:
        array = array + swap_partner(array, step)
    return array


def sum_parts(parts, steps):
    flat = [part.reshape(-1) for part in parts]
    total = sum_everywhere(jnp.concatenate(flat), steps)
    result, start = [], 0
    for part in parts:
        result.append(total[start : start + part.size].reshape(part.shape))
        start += part.size
    return result


def block_order(steps):
    order = []
    for name in ("dp", "group"):
        bits = sorted((step for step in steps if step[0] == name), key=lambda step: -step[1])
        order.append([steps.index(step) for step in bits])
    return order


def blocks_to_whole(blocks, steps):
    count = len(steps)
    rows, cols = blocks.shape[count:]
    dp_axes, group_axes = block_order(steps)
    dp_axes = [count - 1 - axis for axis in dp_axes]
    group_axes = [count - 1 - axis for axis in group_axes]
    whole = blocks.transpose(dp_axes + [count] + group_axes + [count + 1])
    return whole.reshape(rows << len(dp_axes), cols << len(group_axes))


def whole_to_blocks(whole, steps):
    dp_axes, group_axes = block_order(steps)
    rows = whole.shape[0] >> len(dp_axes)
    cols = whole.shape[1] >> len(group_axes)
    split = whole.reshape([2] * len(dp_axes) + [rows] + [2] * len(group_axes) + [cols])
    places = dp_axes + [len(steps)] + group_axes + [len(steps) + 1]
    return split.transpose([places.index(axis) for axis in range(len(places))])


PER_STEP = 4
FF_PER_STEP = 4
SLICE = 48
FF_CHUNK = 256
vmem_bytes = 64 * 1024 * 1024


def dot(left, right, left_axis=1, right_axis=0):
    return lax.dot_general(
        left, right, (((left_axis,), (right_axis,)), ((), ())), preferred_element_type=jnp.float32
    )


def normal_form(values):
    center = jnp.mean(values, axis=-1, keepdims=True)
    centered = values - center
    spread = jnp.mean(centered * centered, axis=-1, keepdims=True)
    scale = lax.rsqrt(spread + norm_epsilon)
    return centered * scale, scale


def norm_back(grad, unit, scale, gain):
    weighted = grad * gain
    along = jnp.mean(weighted * unit, axis=-1, keepdims=True)
    level = jnp.mean(weighted, axis=-1, keepdims=True)
    return scale * (weighted - level - unit * along)


def slices_of(count):
    return [slice(start, start + SLICE) for start in range(0, count, SLICE)]


def fold_rows(values):
    return jnp.sum(values.reshape(values.shape[0] // 8, 8, values.shape[1]), axis=0)


def column_sum(values):
    return jnp.sum(values, axis=0, keepdims=True)


def pair_mask(length):
    return lax.broadcasted_iota(jnp.int32, (length, 2 * HEAD_DIM), 1) < HEAD_DIM


def lane_tiles(count):
    return [slice(start, min(start + 128, count)) for start in range(0, count, 128)]


def stack_heads(pair, first):
    none = jnp.zeros_like(pair)
    return jnp.concatenate([jnp.where(first, pair, none), jnp.where(first, none, pair)], axis=0)


def join_heads(rows, first):
    length = rows.shape[0] // 2
    return jnp.where(first, rows[:length], rows[length:])


def gelu_and_slope(pre):
    bell = jnp.exp2(pre * pre * (-0.5 * LOG2_E))
    base = 1.0 + (0.3275911 * 0.5**0.5) * jnp.abs(pre)
    inverse = pl.reciprocal(base, approx=True)
    inverse = inverse * (2.0 - base * inverse)
    poly = inverse * (
        0.5 * 0.254829592
        + inverse
        * (
            0.5 * -0.284496736
            + inverse
            * (0.5 * 1.421413741 + inverse * (0.5 * -1.453152027 + inverse * (0.5 * 1.061405429)))
        )
    )
    tail = poly * bell
    below = jnp.where(pre >= 0, 1.0 - tail, tail)
    return pre * below, below + pre * bell * 0.3989422804014327


def widen(source_ref, wide_ref, images):
    tiles, total, lanes = wide_ref.shape
    rows_at_once = 8 * images

    @pl.loop(0, total // rows_at_once)
    def _(part):
        rows = pl.ds(pl.multiple_of(part * rows_at_once, rows_at_once), rows_at_once)
        for tile in range(tiles):
            cols = slice(tile * lanes, (tile + 1) * lanes)
            wide_ref[tile, rows, :] = source_ref[rows, cols].astype(jnp.float32)


def narrow(wide_ref, target_ref, images):
    tiles, total, lanes = wide_ref.shape
    rows_at_once = 8 * images

    @pl.loop(0, total // rows_at_once)
    def _(part):
        rows = pl.ds(pl.multiple_of(part * rows_at_once, rows_at_once), rows_at_once)
        for tile in range(tiles):
            cols = slice(tile * lanes, (tile + 1) * lanes)
            target_ref[rows, cols] = wide_ref[tile, rows, :].astype(target_ref.dtype)


def take_image(wide_ref, image, images):
    tiles, total, _ = wide_ref.shape
    rows = pl.ds(image, total // images, images)
    return jnp.concatenate([wide_ref[tile, rows, :] for tile in range(tiles)], axis=1)


def put_image(wide_ref, image, images, values):
    tiles, total, lanes = wide_ref.shape
    rows = pl.ds(image, total // images, images)
    for tile in range(tiles):
        wide_ref[tile, rows, :] = values[:, tile * lanes : (tile + 1) * lanes]


def attention_kernel(
    images, tokens_ref, bias_ref, w_qkv_ref, w_proj_ref, vectors_ref,
    x_ref, qkv_ref, probs_ref, attended_ref, middle_ref, wide_ref, normed_ref,
):
    @pl.when(pl.program_id(0) == 0)
    def _():
        widen(tokens_ref, wide_ref, images)
        to_image_rows(wide_ref, x_ref, images)

    attention_steps(
        x_ref, lambda image: bias_ref[image], w_qkv_ref, w_proj_ref, vectors_ref,
        qkv_ref, probs_ref, attended_ref, middle_ref, normed_ref,
    )


def to_image_rows(wide_ref, x_ref, images):
    length = wide_ref.shape[1] // images

    @pl.loop(0, images)
    def _(image):
        rows = pl.ds(pl.multiple_of(image * length, length), length)
        x_ref[rows, :] = take_image(wide_ref, image, images).astype(jnp.bfloat16)


def attention_steps(
    x_ref, bias_column, w_qkv_ref, w_proj_ref, vectors_ref,
    qkv_ref, probs_ref, attended_ref, middle_ref, normed_ref,
):
    per_step, _, length, _ = probs_ref.shape
    step_rows, width = middle_ref.shape
    base = 0 if x_ref.shape[0] == step_rows else pl.program_id(0) * step_rows

    for rows in slices_of(step_rows):
        x = x_ref[pl.ds(pl.multiple_of(base + rows.start, SLICE), SLICE), :].astype(jnp.float32)
        unit, _ = normal_form(x)
        normed_ref[rows, :] = (unit * vectors_ref[0:1] + vectors_ref[1:2]).astype(jnp.bfloat16)
    shift = jnp.concatenate(
        [vectors_ref[2:3], jnp.zeros((1, width), jnp.float32), vectors_ref[3:4]], axis=1
    )
    for start in range(0, 3 * width, 512):
        cols = slice(start, min(start + 512, 3 * width))
        projected = dot(normed_ref[...], w_qkv_ref[:, cols]) + shift[:, cols]
        qkv_ref[:, cols] = projected.astype(jnp.bfloat16)

    pairs = width // (2 * HEAD_DIM)
    first = pair_mask(length)
    place = lax.broadcasted_iota(jnp.int32, (length, 2 * length), 0)
    asker = lax.broadcasted_iota(jnp.int32, (length, 2 * length), 1)
    own = place == jnp.where(asker >= length, asker - length, asker)

    def scores_of(image):
        rows = slice(image * length, (image + 1) * length)
        result = []
        for pair in range(pairs):
            low = pair * 2 * HEAD_DIM
            queries = stack_heads(qkv_ref[rows, low : low + 2 * HEAD_DIM], first)
            result.append(dot(qkv_ref[rows, width + low : width + low + 2 * HEAD_DIM], queries, 1, 1))
        return result

    next_scores = scores_of(0)
    for image in range(per_step):
        rows = slice(image * length, (image + 1) * length)
        all_scores = next_scores
        if image + 1 < per_step:
            next_scores = scores_of(image + 1)
        column = bias_column(image)
        for cols in lane_tiles(2 * length):
            bias = jnp.where(own[:, cols], 0.0, column)
            for pair in range(pairs):
                scores = all_scores[pair][:, cols] * (HEAD_DIM**-0.5 * LOG2_E) + bias
                weights = jnp.exp2(scores - jnp.max(scores, axis=0, keepdims=True))
                probs = weights * (1.0 / jnp.sum(weights, axis=0, keepdims=True))
                probs_ref[image, pair, :, cols] = probs.astype(jnp.bfloat16)
        for pair in range(pairs):
            low = pair * 2 * HEAD_DIM
            values = qkv_ref[rows, 2 * width + low : 2 * width + low + 2 * HEAD_DIM]
            attended = join_heads(dot(probs_ref[image, pair], values, 0, 0), first)
            attended_ref[rows, low : low + 2 * HEAD_DIM] = attended.astype(jnp.bfloat16)

    middle_ref[...] = (
        x_ref[pl.ds(pl.multiple_of(base, length), step_rows), :].astype(jnp.float32)
        + dot(attended_ref[...], w_proj_ref[...])
        + vectors_ref[4:5]
    )


def feed_forward_kernel(
    images, middle_ref, cotangent_ref, attended_ref, w_up_ref, w_down_ref, proj_t_ref, vectors_ref, bias_up_ref,
    output_ref, d_middle_ref, d_attended_ref, up_grad_ref, down_grad_ref, proj_grad_ref, vector_sums_ref, up_sums_ref,
    wide_ref, *scratches,
):
    up_total_ref, down_total_ref, proj_total_ref = scratches[-3:]

    @pl.when(pl.program_id(0) == 0)
    def _():
        widen(cotangent_ref, wide_ref, images)

    feed_forward_steps(
        images, middle_ref, attended_ref, w_up_ref, w_down_ref, proj_t_ref, vectors_ref, bias_up_ref,
        d_middle_ref, d_attended_ref, vector_sums_ref, up_sums_ref, wide_ref, *scratches,
    )

    @pl.when(pl.program_id(0) == pl.num_programs(0) - 1)
    def _():
        narrow(wide_ref, output_ref, images)
        up_grad_ref[...] = up_total_ref[...].astype(jnp.bfloat16)
        down_grad_ref[...] = down_total_ref[...].T.astype(jnp.bfloat16)
        proj_grad_ref[...] = proj_total_ref[...].astype(jnp.bfloat16)


def feed_forward_steps(
    images, middle_ref, attended_ref, w_up_ref, w_down_ref, proj_t_ref, vectors_ref, bias_up_ref,
    d_middle_ref, d_attended_ref, vector_sums_ref, up_sums_ref,
    wide_ref, normed_ref, normed_t_ref, dy_ref, dy_t_ref, unit_ref, scale_ref, ahead_ref, back_ref,
    up_t_ref, down_t_ref, up_total_ref, down_total_ref, proj_total_ref,
):
    step = pl.program_id(0)
    length = wide_ref.shape[1] // images
    hidden = w_up_ref.shape[1]
    per_step = middle_ref.shape[0] // length

    @pl.when(step == 0)
    def _():
        for total in (up_total_ref, down_total_ref, proj_total_ref, vector_sums_ref, up_sums_ref):
            total[...] = jnp.zeros_like(total)
        up_t_ref[...] = w_up_ref[...].T
        down_t_ref[...] = w_down_ref[...].T

    for image in range(per_step):
        rows = slice(image * length, (image + 1) * length)
        dy = take_image(wide_ref, step * per_step + image, images)
        dy_ref[rows, :] = dy.astype(jnp.bfloat16)
        vector_sums_ref[3:4] += column_sum(dy)
        unit, scale = normal_form(middle_ref[rows, :])
        unit_ref[rows, :] = unit
        scale_ref[rows, :] = jnp.broadcast_to(scale, (length, scale_ref.shape[1]))
        normed_ref[rows, :] = (unit * vectors_ref[5:6] + vectors_ref[6:7]).astype(jnp.bfloat16)
    normed_t_ref[...] = normed_ref[...].T
    dy_t_ref[...] = dy_ref[...].T
    chunks = hidden // FF_CHUNK

    def cols_of(chunk):
        return slice(chunk * FF_CHUNK, (chunk + 1) * FF_CHUNK)

    def into(chunk):
        cols = cols_of(chunk)
        pre = dot(normed_ref[...], w_up_ref[:, cols])
        return pre + bias_up_ref[:, cols], dot(dy_ref[...], down_t_ref[:, cols])

    def across(pre, d_active):
        active, slope = gelu_and_slope(pre)
        return active.astype(jnp.bfloat16), (d_active * slope).astype(jnp.bfloat16)

    def out_of(chunk, active, d_hidden):
        cols = cols_of(chunk)
        ahead, back = dot(active, w_down_ref[cols, :]), dot(d_hidden, up_t_ref[cols, :])
        if chunk == 0:
            ahead_ref[...] = ahead
            back_ref[...] = back
        else:
            ahead_ref[...] += ahead
            back_ref[...] += back
        down_total_ref[:, cols] += dot(dy_t_ref[...], active)
        up_total_ref[:, cols] += dot(normed_t_ref[...], d_hidden)
        up_sums_ref[:, cols] += column_sum(d_hidden.astype(jnp.float32))

    entered, crossed = into(0), None
    for chunk in range(chunks + 1):
        next_entered = into(chunk + 1) if chunk + 1 < chunks else None
        next_crossed = across(*entered) if chunk < chunks else None
        if crossed is not None:
            out_of(chunk - 1, *crossed)
        entered, crossed = next_entered, next_crossed

    for image in range(per_step):
        rows = slice(image * length, (image + 1) * length)
        output = middle_ref[rows, :] + ahead_ref[rows, :] + vectors_ref[11:12]
        put_image(wide_ref, step * per_step + image, images, output)
        unit = unit_ref[rows, :]
        grad = back_ref[rows, :]
        vector_sums_ref[1:2] += column_sum(grad * unit)
        vector_sums_ref[2:3] += column_sum(grad)
        d_middle = dy_ref[rows, :].astype(jnp.float32) + norm_back(
            grad, unit, scale_ref[rows, 0:1], vectors_ref[5:6]
        )
        d_middle_ref[rows, :] = d_middle
        d_branch = d_middle.astype(jnp.bfloat16)
        dy_ref[rows, :] = d_branch
        vector_sums_ref[0:1] += column_sum(d_branch.astype(jnp.float32))
    proj_total_ref[...] += dot(attended_ref[...], dy_ref[...], 0, 0)
    d_attended_ref[...] = dot(dy_ref[...], proj_t_ref[...]).astype(jnp.bfloat16)


def attention_back_kernel(
    images, x_ref, qkv_ref, probs_ref, d_attended_ref, d_middle_ref, qkv_t_ref, vectors_ref,
    input_grad_ref, qkv_grad_ref, vector_sums_ref, wide_ref, normed_ref, d_projected_ref, back_ref, qkv_total_ref,
):
    @pl.when(pl.program_id(0) == 0)
    def _():
        qkv_total_ref[...] = jnp.zeros_like(qkv_total_ref)
        vector_sums_ref[...] = jnp.zeros_like(vector_sums_ref)

    def put(image, rows, values):
        put_image(wide_ref, image, images, values)

    attention_back_steps(
        x_ref, qkv_ref, probs_ref, d_attended_ref, vectors_ref, vector_sums_ref, normed_ref, d_projected_ref, qkv_total_ref
    )
    input_back_steps(
        put, probs_ref.shape[2], x_ref, d_projected_ref, d_middle_ref, qkv_t_ref, vectors_ref, vector_sums_ref, back_ref
    )

    @pl.when(pl.program_id(0) == pl.num_programs(0) - 1)
    def _():
        narrow(wide_ref, input_grad_ref, images)
        qkv_grad_ref[...] = qkv_total_ref[...].astype(jnp.bfloat16)


def attention_back_steps(
    x_ref, qkv_ref, probs_ref, d_attended_ref, vectors_ref, vector_sums_ref, normed_ref, d_projected_ref, qkv_total_ref
):
    width = d_attended_ref.shape[1]
    length = probs_ref.shape[2]
    per_step = probs_ref.shape[0]

    pairs = width // (2 * HEAD_DIM)
    first = pair_mask(length)
    scale = HEAD_DIM**-0.5

    def places(image, pair):
        low = pair * 2 * HEAD_DIM
        rows = slice(image * length, (image + 1) * length)
        return rows, [slice(part * width + low, part * width + low + 2 * HEAD_DIM) for part in range(3)]

    def entering(image):
        result = []
        for pair in range(pairs):
            rows, cols = places(image, pair)
            d_attended = stack_heads(d_attended_ref[rows, cols[0]], first)
            d_values = dot(probs_ref[image, pair], d_attended)
            d_projected_ref[rows, cols[2]] = d_values.astype(jnp.bfloat16)
            result.append(dot(qkv_ref[rows, cols[2]], d_attended, 1, 1))
        return result

    next_probs = entering(0)
    for image in range(per_step):
        all_d_probs = next_probs
        if image + 1 < per_step:
            next_probs = entering(image + 1)
        all_d_scores = []
        for pair in range(pairs):
            parts = []
            for cols in lane_tiles(2 * length):
                probs, d_probs = probs_ref[image, pair, :, cols].astype(jnp.float32), all_d_probs[pair][:, cols]
                along = jnp.sum(d_probs * probs, axis=0, keepdims=True)
                parts.append((probs * (d_probs - along)).astype(jnp.bfloat16))
            all_d_scores.append(jnp.concatenate(parts, axis=1))
        for pair in range(pairs):
            rows, cols = places(image, pair)
            d_scores = all_d_scores[pair]
            queries = stack_heads(qkv_ref[rows, cols[0]], first)
            d_queries = join_heads(dot(d_scores, qkv_ref[rows, cols[1]], 0, 0), first) * scale
            d_projected_ref[rows, cols[0]] = d_queries.astype(jnp.bfloat16)
            d_projected_ref[rows, cols[1]] = (dot(d_scores, queries) * scale).astype(jnp.bfloat16)

    query_sums = value_sums = jnp.zeros((8, width), jnp.float32)
    for rows in slices_of(d_attended_ref.shape[0]):
        query_sums += fold_rows(d_projected_ref[rows, :width].astype(jnp.float32))
        value_sums += fold_rows(d_projected_ref[rows, 2 * width :].astype(jnp.float32))
        if x_ref is not None:
            unit, _ = normal_form(x_ref[rows, :].astype(jnp.float32))
            normed_ref[rows, :] = (unit * vectors_ref[0:1] + vectors_ref[1:2]).astype(jnp.bfloat16)
    vector_sums_ref[2:3] += column_sum(query_sums)
    vector_sums_ref[3:4] += column_sum(value_sums)
    qkv_total_ref[...] += dot(normed_ref[...], d_projected_ref[...], 0, 0)


def input_back_steps(
    put, length, x_ref, d_projected_ref, d_middle_ref, qkv_t_ref, vectors_ref, vector_sums_ref, back_ref
):
    step = pl.program_id(0)
    per_step = x_ref.shape[0] // length
    back_ref[...] = dot(d_projected_ref[...], qkv_t_ref[...])
    gain_sums = shift_sums = jnp.zeros((8, x_ref.shape[1]), jnp.float32)
    for rows in slices_of(x_ref.shape[0]):
        unit, scale = normal_form(x_ref[rows, :].astype(jnp.float32))
        grad = back_ref[rows, :]
        gain_sums += fold_rows(grad * unit)
        shift_sums += fold_rows(grad)
        back_ref[rows, :] = d_middle_ref[rows, :] + norm_back(grad, unit, scale, vectors_ref[0:1])
    vector_sums_ref[0:1] += column_sum(gain_sums)
    vector_sums_ref[1:2] += column_sum(shift_sums)
    for image in range(per_step):
        rows = slice(image * length, (image + 1) * length)
        put(step * per_step + image, rows, back_ref[rows, :])


def whole_block(shape):
    return pl.BlockSpec(shape, lambda step: (0,) * len(shape))


def step_block(shape, first=0):
    return pl.BlockSpec(shape, lambda step: (first + step,) + (0,) * (len(shape) - 1))


def scratch(*shape, dtype=jnp.float32):
    return pltpu.VMEM(shape, dtype)


def call_kernel(kernel, statics, steps, ins, outs, scratches, operands, flops, transcendentals=0, first_step=0, aliases={}):
    in_specs = [
        pl.BlockSpec(memory_space=pltpu.SMEM)
        if block == "place"
        else pl.BlockSpec(memory_space=pl.ANY)
        if block == "await"
        else whole_block(op.shape) if block is None else step_block(block, first_step)
        for op, block in zip(operands, ins)
    ]
    out_specs = [
        whole_block(shape) if block is None else step_block(block, first_step) for shape, dtype, block in outs
    ]
    moved = sum(op.size * op.dtype.itemsize for op in operands) + sum(
        math.prod(shape) * jnp.dtype(dtype).itemsize for shape, dtype, block in outs
    )
    return pl.pallas_call(
        functools.partial(kernel, *statics),
        grid=(steps,),
        in_specs=in_specs,
        out_specs=out_specs,
        out_shape=[jax.ShapeDtypeStruct(shape, dtype) for shape, dtype, block in outs],
        scratch_shapes=scratches,
        input_output_aliases=aliases,
        compiler_params=pltpu.CompilerParams(vmem_limit_bytes=vmem_bytes),
        cost_estimate=pl.CostEstimate(
            flops=flops * 8, bytes_accessed=moved, transcendentals=transcendentals
        ),
    )(*operands)


def attention_forward(tokens, bias, w_qkv, w_proj, vectors):
    images, length, _ = bias.shape
    total, width = tokens.shape
    pairs = width // (2 * HEAD_DIM)
    rows = PER_STEP * length
    low, high = jnp.bfloat16, jnp.float32
    outs = [
        ((total, width), low, None),
        ((total, 3 * width), low, (rows, 3 * width)),
        ((images, pairs, length, 2 * length), low, (PER_STEP, pairs, length, 2 * length)),
        ((total, width), low, (rows, width)),
        ((total, width), high, (rows, width)),
    ]
    return call_kernel(
        attention_kernel, (images,), images // PER_STEP,
        [None, (PER_STEP, length, 1), None, None, None], outs,
        [scratch(width // 128, total, 128), scratch(rows, width, dtype=low)],
        (tokens, bias, w_qkv, w_proj, vectors),
        2 * total * width * 4 * width + 8 * total * length * width,
    )


def feed_forward(images, middle, cotangent, attended, w_up, w_down, w_proj, vectors):
    total, width = middle.shape
    hidden = w_up.shape[1]
    rows = total // images * FF_PER_STEP
    low, high = jnp.bfloat16, jnp.float32
    block = (rows, width)
    outs = [
        ((total, width), low, None),
        ((total, width), high, block),
        ((total, width), low, block),
        ((width, hidden), low, None),
        ((hidden, width), low, None),
        ((width, width), low, None),
        ((8, width), high, None),
        ((1, hidden), high, None),
    ]
    scratches = [
        scratch(width // 128, total, 128),
        scratch(rows, width, dtype=low),
        scratch(width, rows, dtype=low),
        scratch(rows, width, dtype=low),
        scratch(width, rows, dtype=low),
        scratch(rows, width),
        scratch(rows, 128),
        scratch(rows, width),
        scratch(rows, width),
        scratch(hidden, width, dtype=low),
        scratch(width, hidden, dtype=low),
        scratch(width, hidden),
        scratch(width, hidden),
        scratch(width, width),
    ]
    return call_kernel(
        feed_forward_kernel, (images,), images // FF_PER_STEP,
        [block, None, block, None, None, None, None, None], outs, scratches,
        (middle, cotangent, attended, w_up, w_down, w_proj.T, vectors, vectors[7:11].reshape(1, hidden)),
        12 * total * width * hidden + 4 * total * width * width, total * hidden,
    )


def attention_back(x, qkv, probs, d_attended, d_middle, w_qkv, vectors):
    images, pairs, length, _ = probs.shape
    total, width = x.shape
    rows = PER_STEP * length
    low, high = jnp.bfloat16, jnp.float32
    block = (rows, width)
    outs = [
        ((total, width), low, None),
        ((width, 3 * width), low, None),
        ((8, width), high, None),
    ]
    scratches = [
        scratch(width // 128, total, 128),
        scratch(rows, width, dtype=low),
        scratch(rows, 3 * width, dtype=low),
        scratch(rows, width),
        scratch(width, 3 * width),
    ]
    return call_kernel(
        attention_back_kernel, (images,), images // PER_STEP,
        [block, (rows, 3 * width), (PER_STEP, pairs, length, 2 * length), block, block, None, None],
        outs, scratches, (x, qkv, probs, d_attended, d_middle, w_qkv.T, vectors),
        4 * total * width * 3 * width + 16 * total * length * width,
    )

def linear_place():
    return lax.axis_index("dp") * lax.axis_size("group") + lax.axis_index("group")


def permute(array, mask):
    count = lax.axis_size("dp") * lax.axis_size("group")
    return lax.ppermute(array, ("dp", "group"), [(rank, rank ^ mask) for rank in range(count)])


def direct_masks(bits):
    masks = [0]
    for bit in bits:
        masks = masks + [mask | bit for mask in masks]
    return masks[1:]


def add_wide(first, *rest):
    total = first.astype(jnp.float32)
    for part in rest:
        total = total + part.astype(jnp.float32)
    return total


def packed_place(mask, spread, count):
    return ((mask >> 1) & (spread - 1)) * (count // (2 * spread)) + (mask >> (spread.bit_length()))


def scatter_step(held, bits):
    masks = direct_masks(bits)
    size = held.shape[0] // (len(masks) + 1)
    parts = [
        permute(held[size * (at + 1) : size * (at + 2)].astype(jnp.bfloat16), mask)
        for at, mask in enumerate(masks)
    ]
    return held[:size], parts


def add_wide(first, *rest):
    total = first.astype(jnp.float32)
    for part in rest:
        total = total + part.astype(jnp.float32)
    return total


def packed_place(mask, spread, count):
    return ((mask >> 1) & (spread - 1)) * (count // (2 * spread)) + (mask >> (spread.bit_length()))


def gather_step(held, bits):
    return held + [permute(part, mask) for mask in direct_masks(bits) for part in held]


def gathered_place(mask, count):
    return (mask & 1) * (count // 2) + ((mask >> 2) & 1) * (count // 4) + (mask >> 3) * 2 + ((mask >> 1) & 1)


def unpack(place_ref, block_refs, packed_ref, put, dp_size, spread):
    place = place_ref[0]
    size = block_refs[0].shape[0]
    for at, block_ref in enumerate(block_refs):
        packed_ref[at * size : (at + 1) * size] = block_ref[...]
    count = dp_size * spread
    for row in range(dp_size):
        for col in range(spread):
            put(row, col, packed_ref[gathered_place((row * spread + col) ^ place, count)])


def unpack_in_order(blocks_ref, put, dp_size, spread):
    for row in range(dp_size):
        for col in range(spread):
            put(row, col, blocks_ref[row * spread + col])


def pack(place_ref, take, keep_ref, leave_ref, dp_size, spread):
    place = place_ref[0]
    odd = (place & 1) == 1
    for row in range(dp_size):
        for col in range(0, spread, 2):
            at = packed_place((row * spread + col) ^ place, spread, dp_size * spread)
            even_block, odd_block = take(row, col), take(row, col + 1)
            keep_ref[at] = jnp.where(odd, odd_block, even_block)
            leave_ref[at] = jnp.where(odd, even_block, odd_block)


def narrow_pieces(place_ref, wide_ref, piece_refs, spread):
    tiles, _, lanes = wide_ref.shape
    rows_of_piece = piece_refs[0].shape[0]
    step = 64
    group = place_ref[0] & (spread - 1)
    for relative, piece_ref in enumerate(piece_refs):
        base = (group ^ relative) * rows_of_piece

        @pl.loop(0, rows_of_piece // step)
        def _(part):
            target = pl.ds(pl.multiple_of(part * step, step), step)
            source = pl.ds(pl.multiple_of(base + part * step, step), step)
            for tile in range(tiles):
                cols = slice(tile * lanes, (tile + 1) * lanes)
                piece_ref[target, cols] = wide_ref[tile, source, :].astype(jnp.bfloat16)


def general_body(
    tokens,
    keep_mask,
    cotangent,
    qkv_weight,
    proj_weight,
    up_weight,
    down_weight,
    vectors,
    qkv_rows,
    qkv_cols,
    proj_rows,
    proj_cols,
    up_rows,
    up_cols,
    down_rows,
    down_cols,
    vector_moment,
):
    masters = (qkv_weight, proj_weight, up_weight, down_weight)
    lowered = tuple((master.astype(jnp.bfloat16) for master in masters))
    dp_bits, group_bits = axis_bits("dp"), axis_bits("group")
    gather_steps = dp_bits[1:] + group_bits[1:] + dp_bits[:1] + group_bits[:1]
    scatter_steps = gather_steps[::-1]
    w_qkv, w_proj, w_up, w_down = tuple(
        blocks_to_whole(gather_blocks(part, gather_steps), gather_steps) for part in lowered
    )
    spread = lax.axis_size("group")

    def slots_in(array):
        held, slots, width = array.shape
        parts = array.transpose(1, 0, 2).reshape(slots, spread, held // spread, width)
        parts = lax.all_to_all(
            parts.transpose(1, 0, 2, 3), "group", split_axis=0, concat_axis=0, tiled=True
        )
        return parts.reshape(spread * slots * (held // spread), width)

    def slots_out(array):
        held, slots, width = tokens.shape
        parts = array.reshape(spread, slots, held // spread, width)
        parts = lax.all_to_all(parts, "group", split_axis=0, concat_axis=0, tiled=True)
        return parts.transpose(1, 0, 2, 3).reshape(slots, held, width).transpose(1, 0, 2)

    images = keep_mask.shape[0]
    bias = jnp.where(keep_mask > 0, 0.0, -1e30)[:, :, None]
    x, qkv, probs, attended, middle = attention_forward(
        slots_in(tokens), bias, w_qkv, w_proj, vectors
    )
    output, d_middle, d_attended, up_grad, down_grad, proj_grad, ff_sums, up_sums = feed_forward(
        images, middle, slots_in(cotangent), attended, w_up, w_down, w_proj, vectors
    )
    block_output = slots_out(output)
    d_input, qkv_grad, att_sums = attention_back(
        x, qkv, probs, d_attended, d_middle, w_qkv, vectors
    )
    input_grad = slots_out(d_input)
    local_vectors = jnp.concatenate(
        [att_sums[:4], ff_sums[:3], up_sums.reshape(4, -1), ff_sums[3:4]], axis=0
    )
    vector_grad = sum_everywhere(local_vectors, group_bits + dp_bits)
    local_grads = (qkv_grad, proj_grad, up_grad, down_grad)
    owned = tuple(
        scatter_sum(whole_to_blocks(part, scatter_steps), scatter_steps) for part in local_grads
    )
    squares = tuple((gradient * gradient + tiny_square for gradient in owned))
    row_parts = tuple((jnp.sum(square, axis=1) for square in squares)) + tuple(
        (jnp.sum(master * master, axis=1) for master in masters)
    )
    row_sums = sum_parts(row_parts, group_bits)
    rows_old = (qkv_rows, proj_rows, up_rows, down_rows)
    cols_old = (qkv_cols, proj_cols, up_cols, down_cols)
    total_cols = tuple((gradient.shape[1] * lax.axis_size("group") for gradient in owned))
    total_rows = tuple((gradient.shape[0] * lax.axis_size("dp") for gradient in owned))
    rows_new = tuple(
        (
            decay_rate * rows_old[which] + (1.0 - decay_rate) * row_sums[which] / total_cols[which]
            for which in range(4)
        )
    )
    col_parts = (
        tuple((jnp.sum(square, axis=0) for square in squares))
        + tuple((jnp.sum(row_stat) for row_stat in rows_new))
        + tuple((jnp.sum(row_sums[4 + which]) for which in range(4)))
    )
    col_sums = sum_parts(col_parts, dp_bits)
    results = []
    for which in range(4):
        cols_new = (
            decay_rate * cols_old[which] + (1.0 - decay_rate) * col_sums[which] / total_rows[which]
        )
        mean_rows = col_sums[4 + which] / total_rows[which]
        spread = jnp.sqrt(col_sums[8 + which] / (total_rows[which] * total_cols[which]))
        second = rows_new[which][:, None] * cols_new[None, :] / mean_rows
        updated = masters[which] - step_rate * spread * owned[which] * lax.rsqrt(second)
        results.append((owned[which], rows_new[which], cols_new, updated))
    vector_moment_new = decay_rate * vector_moment + (1.0 - decay_rate) * (
        vector_grad * vector_grad + tiny_square
    )
    row_spread = jnp.sqrt(jnp.mean(vectors * vectors, axis=1, keepdims=True))
    vector_new = vectors - step_rate * row_spread * vector_grad * lax.rsqrt(vector_moment_new)
    return (
        block_output,
        input_grad,
        results[0][0],
        results[0][1],
        results[0][2],
        results[0][3],
        results[1][0],
        results[1][1],
        results[1][2],
        results[1][3],
        results[2][0],
        results[2][1],
        results[2][2],
        results[2][3],
        results[3][0],
        results[3][1],
        results[3][2],
        results[3][3],
        vector_grad,
        vector_moment_new,
        vector_new,
    )


def first_attention_kernel(images, dp_size, spread, place_ref, tokens_ref, *refs):
    blocks, refs = refs[:4], refs[4:]
    keep_ref, vectors_ref, *outs, x_ref, w_qkv_ref, w_proj_ref, qkv_t_ref, proj_t_ref = refs[:-3]
    packed_ref, wide_ref, bias_ref = refs[-3:]
    rows = packed_ref.shape[1]
    qkv_cols, proj_cols = w_qkv_ref.shape[1] // spread, w_proj_ref.shape[1] // spread

    @pl.when(pl.program_id(0) == 0)
    def _():
        widen(tokens_ref, wide_ref, images)
        to_image_rows(wide_ref, x_ref, images)

        def put(row, col, block):
            down = slice(row * rows, (row + 1) * rows)
            w_qkv_ref[down, col * qkv_cols : (col + 1) * qkv_cols] = block[:, :qkv_cols]
            w_proj_ref[down, col * proj_cols : (col + 1) * proj_cols] = block[:, qkv_cols:]

        unpack(place_ref, blocks, packed_ref, put, dp_size, spread)
        qkv_t_ref[...] = w_qkv_ref[...].T
        proj_t_ref[...] = w_proj_ref[...].T

    attention_part(0, x_ref, keep_ref, w_qkv_ref, w_proj_ref, vectors_ref, *outs, bias_ref)


def next_attention_kernel(start, x_ref, keep_ref, w_qkv_ref, w_proj_ref, vectors_ref, *refs):
    attention_part(start, x_ref, keep_ref, w_qkv_ref, w_proj_ref, vectors_ref, *refs[-6:])


def attention_part(
    start, x_ref, keep_ref, w_qkv_ref, w_proj_ref, vectors_ref,
    qkv_ref, probs_ref, attended_ref, middle_ref, normed_ref, bias_ref,
):
    @pl.when(pl.program_id(0) == 0)
    def _():
        bias_ref[...] = jnp.where(keep_ref[...] > 0, 0.0, -1e30).T

    def bias_column(image):
        here = start + pl.program_id(0) * probs_ref.shape[0] + image
        lane = lax.broadcasted_iota(jnp.int32, bias_ref.shape, 1)
        return row_sum(jnp.where(lane == here, bias_ref[...], 0.0))

    attention_steps(
        x_ref, bias_column, w_qkv_ref, w_proj_ref, vectors_ref,
        qkv_ref, probs_ref, attended_ref, middle_ref, normed_ref,
    )


def feed_forward_packed_kernel(images, dp_size, spread, place_ref, *refs):
    cotangent_ref, blocks, refs = refs[0], refs[1:5], refs[5:]
    middle_ref, attended_ref, proj_t_ref, vectors_ref = refs[:4]
    outputs, refs = refs[4 : 4 + spread], refs[4 + spread :]
    d_middle_ref, d_attended_ref, keep_ref, leave_ref, proj_total_ref, vector_sums_ref, up_sums_ref = refs[:7]
    w_up_ref, w_down_ref, down_low_ref, packed_ref, bias_up_ref, wide_ref = refs[7:13]
    scratches = refs[13:]
    width = w_up_ref.shape[0]
    up_total_ref, down_total_ref = scratches[-2:]
    rows = packed_ref.shape[1]
    up_cols = w_up_ref.shape[1] // spread
    out_cols = w_down_ref.shape[1] // spread
    folds = w_down_ref.shape[0] // w_up_ref.shape[0]

    @pl.when(pl.program_id(0) == 0)
    def _():
        widen(cotangent_ref, wide_ref, images)
        for fold in range(bias_up_ref.shape[1] // width):
            bias_up_ref[:, fold * width : (fold + 1) * width] = vectors_ref[7 + fold : 8 + fold]

        def put(row, col, block):
            w_up_ref[row * rows : (row + 1) * rows, col * up_cols : (col + 1) * up_cols] = block[:, :up_cols]
            for fold in range(folds):
                down = (row * folds + fold) * rows
                start = up_cols + fold * out_cols
                w_down_ref[down : down + rows, col * out_cols : (col + 1) * out_cols] = block[
                    :, start : start + out_cols
                ]

        unpack(place_ref, blocks, packed_ref, put, dp_size, spread)

    feed_forward_steps(
        images, middle_ref, attended_ref, w_up_ref, w_down_ref, proj_t_ref, vectors_ref, bias_up_ref,
        d_middle_ref, d_attended_ref, vector_sums_ref, up_sums_ref, wide_ref, *scratches, proj_total_ref,
    )

    @pl.when(pl.program_id(0) == pl.num_programs(0) - 1)
    def _():
        narrow_pieces(place_ref, wide_ref, outputs, spread)
        down_low_ref[...] = down_total_ref[...].T.astype(jnp.bfloat16)

        def take(row, col):
            across = slice(row * rows, (row + 1) * rows)
            cols = slice(col * out_cols, (col + 1) * out_cols)
            parts = [up_total_ref[across, col * up_cols : (col + 1) * up_cols].astype(jnp.bfloat16)]
            for fold in range(folds):
                down = (row * folds + fold) * rows
                parts.append(down_low_ref[down : down + rows, cols])
            return jnp.concatenate(parts, axis=1)

        pack(place_ref, take, keep_ref, leave_ref, dp_size, spread)


def attention_back_packed_kernel(
    dp_size, spread, place_ref, normed_ref, qkv_ref, probs_ref, d_attended_ref, vectors_ref, proj_total_ref, _,
    d_projected_ref, keep_ref, leave_ref, vector_sums_ref, total_ref,
):
    @pl.when(pl.program_id(0) == 0)
    def _():
        total_ref[...] = jnp.zeros_like(total_ref)
        vector_sums_ref[...] = jnp.zeros_like(vector_sums_ref)

    attention_back_steps(
        None, qkv_ref, probs_ref, d_attended_ref, vectors_ref, vector_sums_ref, normed_ref, d_projected_ref, total_ref
    )

    @pl.when(pl.program_id(0) == pl.num_programs(0) - 1)
    def _():
        rows = keep_ref.shape[1]
        qkv_cols, proj_cols = total_ref.shape[1] // spread, proj_total_ref.shape[1] // spread

        def take(row, col):
            down = slice(row * rows, (row + 1) * rows)
            parts = [
                total_ref[down, col * qkv_cols : (col + 1) * qkv_cols],
                proj_total_ref[down, col * proj_cols : (col + 1) * proj_cols],
            ]
            return jnp.concatenate(parts, axis=1).astype(jnp.bfloat16)

        pack(place_ref, take, keep_ref, leave_ref, dp_size, spread)


def first_input_kernel(
    length, x_ref, d_projected_ref, d_middle_ref, qkv_t_ref, vectors_ref, before_ref, *refs
):
    d_input_ref, vector_sums_ref, back_ref = refs[-3:]

    @pl.when(pl.program_id(0) == 0)
    def _():
        vector_sums_ref[...] = before_ref[...]

    def put(image, rows, values):
        d_input_ref[rows, :] = values.astype(jnp.bfloat16)

    input_back_steps(
        put, length, x_ref, d_projected_ref, d_middle_ref, qkv_t_ref, vectors_ref, vector_sums_ref, back_ref
    )


def last_input_kernel(
    images, spread, length, first, place_ref, x_ref, d_projected_ref, d_middle_ref, qkv_t_ref, vectors_ref, before_ref,
    d_input_ref, _, *refs,
):
    pieces, (vector_sums_ref, wide_ref, back_ref) = refs[:spread], refs[spread:]

    @pl.when(pl.program_id(0) == 0)
    def _():
        vector_sums_ref[...] = before_ref[...]
        for image in range(first):
            rows = slice(image * length, (image + 1) * length)
            put_image(wide_ref, image, images, d_input_ref[rows, :].astype(jnp.float32))

    def put(image, rows, values):
        put_image(wide_ref, first + image, images, values)

    input_back_steps(
        put, length, x_ref, d_projected_ref, d_middle_ref, qkv_t_ref, vectors_ref, vector_sums_ref, back_ref
    )

    @pl.when(pl.program_id(0) == pl.num_programs(0) - 1)
    def _():
        narrow_pieces(place_ref, wide_ref, pieces, spread)


def cut(array_ref, parts_ref):
    count = parts_ref.shape[2]
    for member in range(parts_ref.shape[0]):
        parts_ref[member] = array_ref[:, member * count : (member + 1) * count, :]


def pack_kernel(qkv_ref, proj_ref, up_ref, down_ref, pack_ref):
    rows, start = pack_ref.shape[0], 0
    parts = [qkv_ref[...], proj_ref[...], up_ref[...]]
    parts += [down_ref[fold * rows : (fold + 1) * rows, :] for fold in range(down_ref.shape[0] // rows)]
    for part in parts:
        pack_ref[:, start : start + part.shape[1]] = part.astype(jnp.bfloat16)
        start += part.shape[1]


def token_kernel(array_ref, own_ref, arrived_ref, _, parts_ref, first_ref, second_ref):
    start = first_ref.shape[2]
    for at, pack_ref in enumerate((own_ref, arrived_ref)):
        first_ref[at] = pack_ref[:, :start]
        second_ref[at] = pack_ref[:, start:]
    cut(array_ref, parts_ref)


def join_kernel(count, *refs):
    size = refs[0].shape[0]
    for at, part_ref in enumerate(refs[:count]):
        refs[-1][at * size : (at + 1) * size] = part_ref[...]


def settle_kernel(spread, place_ref, *refs):
    lists, (output_ref, token_ref) = refs[:-2], refs[-2:]
    token_ref[...] = jnp.zeros_like(token_ref)
    group = place_ref[0] & (spread - 1)
    count = lists[0].shape[1]
    share = len(lists) // spread * count
    for at, piece_ref in enumerate(lists):
        relative, part = at % spread, at // spread
        start = pl.multiple_of((group ^ relative) * share + part * count, count)
        output_ref[:, pl.ds(start, count), :] = piece_ref[...]


def lane_table(rows, columns):
    lane = lax.broadcasted_iota(jnp.int32, (rows, 128), 1)
    table = jnp.zeros((rows, 128), jnp.float32)
    for at, column in enumerate(columns):
        table = jnp.where(lane == at, column, table)
    return table


def added(parts):
    while len(parts) > 1:
        parts = [sum(parts[at : at + 2][1:], parts[at]) for at in range(0, len(parts), 2)]
    return parts[0]


def row_sum(values):
    return jnp.sum(values, axis=1, keepdims=True)


def after_kernel(*refs):
    pass


def gradient_kernel(count, *refs):
    block_parts, sums, refs = refs[:count], refs[count : count + 3], refs[count + 3 :]
    masters, rows_old, refs = refs[:4], refs[4:8], refs[8:]
    grads, (row_ref, message_ref) = refs[:4], refs[4:]
    blocks = added([part[0].astype(jnp.float32) for part in block_parts])
    rows, up_cols = grads[2].shape
    qkv_cols, out_cols = grads[0].shape[1], grads[1].shape[1]
    folds = grads[3].shape[0] // rows
    up = blocks[:, :up_cols]
    downs = [blocks[:, up_cols + fold * out_cols :][:, :out_cols] for fold in range(folds)]
    start = up_cols + folds * out_cols
    qkv = blocks[:, start : start + qkv_cols]
    proj = blocks[:, start + qkv_cols :]
    grads[0][...] = qkv
    grads[1][...] = proj
    grads[2][...] = up
    for fold in range(folds):
        grads[3][fold * rows : (fold + 1) * rows, :] = downs[fold]
    squares = [part * part + tiny_square for part in (qkv, proj, up, *downs)]
    row_ref[...] = lane_table(rows, [row_sum(square) for square in squares]).T[: row_ref.shape[0], :]
    width = message_ref.shape[1]
    message_ref[...] = jnp.zeros_like(message_ref)
    for at, square in enumerate((*squares[:3], added(squares[3:]))):
        message_ref[at : at + 1, : square.shape[1]] = column_sum(square)
    scalars = [column_sum(row_sum(master[...] * master[...])) for master in masters]
    scalars += [row_sum(part[...].reshape(1, part.shape[0])) for part in rows_old]
    message_ref[4:5, :128] = lane_table(1, scalars)
    att_ref, ff_ref, up_ref = sums
    count = up_ref.shape[1] // width
    message_ref[8:12, :] = att_ref[:4]
    message_ref[12:15, :] = ff_ref[:3]
    for at in range(count):
        message_ref[15 + at : 16 + at, :] = up_ref[:, at * width : (at + 1) * width]
    message_ref[15 + count : 16 + count, :] = ff_ref[3:4]


def column_kernel(row_ref, *refs):
    parts, (cols_ref, message_ref) = refs[:-3], refs[-2:]
    total = added([part[...] for part in parts])
    cols_ref[...] = total[:8]
    width = total.shape[1]
    rows = row_ref.shape[1]
    message_ref[...] = jnp.zeros_like(message_ref)
    message_ref[:8, :rows] = row_ref[...]
    columns = [row_sum(total[which : which + 1]) for which in range(4)]
    squares = [total[4:5, which : which + 1] for which in range(4)]
    message_ref[8:9, :] = lane_table(1, columns + squares)
    for tile in range(width // 128):
        message_ref[16 * (tile + 1) : 16 * (tile + 2), :] = total[8:, tile * 128 : (tile + 1) * 128]


def update_kernel(count, heights, widths, *refs):
    messages, refs = refs[:count], refs[count:]
    cols_ref, vectors_ref, moment_ref, refs = refs[0], refs[1], refs[2], refs[3:]
    grads, masters, rows_old, cols_old, refs = refs[:4], refs[4:8], refs[8:12], refs[12:16], refs[17:]
    news, cols_new, rows_out, refs = refs[:4], refs[4:8], refs[8:12], refs[12:]
    vector_grad_ref, moment_new_ref, vector_new_ref = refs
    sums = added([message[...] for message in messages])
    height = grads[0].shape[0]
    folds = grads[3].shape[0] // height
    lanes = [[0], [1], [2], list(range(3, 3 + folds))]
    share = 1.0 - decay_rate
    for which in range(4):
        entries = heights[which] * widths[which]
        cols = cols_old[which].shape[0]
        new = decay_rate * cols_old[which][...].reshape(1, cols) + share / heights[which] * cols_ref[
            which : which + 1, :cols
        ]
        cols_new[which][...] = new[0]
        old_total = cols_ref[4:5, 4 + which : 5 + which]
        mean_rows = (decay_rate * old_total + share / widths[which] * sums[8:9, which : which + 1]) / heights[which]
        rate = step_rate * jnp.sqrt(sums[8:9, 4 + which : 5 + which] / entries)
        across = new / mean_rows
        old = rows_old[which][...].reshape(1, len(lanes[which]) * height)
        row_sums = jnp.concatenate([sums[lane : lane + 1, :height] for lane in lanes[which]], axis=1)
        row = decay_rate * old + share / widths[which] * row_sums
        rows_out[which][...] = row[0]
        for fold in range(len(lanes[which])):
            part = slice(fold * height, (fold + 1) * height)
            column = jnp.broadcast_to(row[:, part], (8, height)).T[:, :1]
            news[which][part, :] = masters[which][part, :] - rate * grads[which][part, :] * lax.rsqrt(column * across)
    vectors = vectors_ref[...]
    count = vectors.shape[0]
    gradient = jnp.concatenate(
        [sums[16 * (tile + 1) : 16 * (tile + 1) + count] for tile in range(vectors.shape[1] // 128)], axis=1
    )
    vector_grad_ref[...] = gradient
    moment = decay_rate * moment_ref[...] + share * (gradient * gradient + tiny_square)
    moment_new_ref[...] = moment
    spread = jnp.sqrt(jnp.mean(vectors * vectors, axis=1, keepdims=True))
    vector_new_ref[...] = vectors - step_rate * spread * gradient * lax.rsqrt(moment)


def packed_body(
    tokens, keep_mask, cotangent, qkv_weight, proj_weight, up_weight, down_weight, vectors,
    qkv_rows, qkv_cols, proj_rows, proj_cols, up_rows, up_cols, down_rows, down_cols, vector_moment,
):
    spread, dp_size = lax.axis_size("group"), lax.axis_size("dp")
    low, high = jnp.bfloat16, jnp.float32
    place = linear_place().astype(jnp.int32).reshape(1)
    group = lax.axis_index("group")
    held, slots, width = tokens.shape
    images, length = keep_mask.shape
    hidden = up_weight.shape[1] * spread
    total = images * length
    rows = qkv_weight.shape[0]
    folds = down_weight.shape[0] // rows
    core_bits = (1,)
    near_bits = tuple(1 << at for at in range(1, spread.bit_length()))
    far_bits = tuple(spread << at for at in range(1, dp_size.bit_length() - 1))
    half = spread * dp_size // 2

    anywhere = pl.BlockSpec(memory_space=pl.ANY)
    in_smem = pl.BlockSpec(memory_space=pltpu.SMEM)

    in_vmem = pl.BlockSpec(memory_space=pltpu.VMEM)
    small = functools.partial(
        pl.pallas_call, compiler_params=pltpu.CompilerParams(vmem_limit_bytes=vmem_bytes)
    )
    masters = (qkv_weight, proj_weight, up_weight, down_weight)
    parted = jax.ShapeDtypeStruct((spread, slots, images, width), low)

    def after(array, awaited):
        return small(
            after_kernel,
            in_specs=[anywhere] * (1 + len(awaited)),
            out_specs=anywhere,
            out_shape=jax.ShapeDtypeStruct(array.shape, array.dtype),
            input_output_aliases={0: 0},
        )(array, *awaited)

    def to_group(parts):
        return lax.all_to_all(parts, "group", split_axis=0, concat_axis=0, tiled=True)

    def to_images(parts):
        return to_group(parts).reshape(total, width)

    def exchange(parts):
        return [parts[0]] + [permute(part, relative) for relative, part in enumerate(parts) if relative]

    def settle(parts):
        parts = [part.reshape(slots, -1, width) for part in parts]
        whole, token = small(
            functools.partial(settle_kernel, spread),
            in_specs=[in_smem] + [in_vmem] * len(parts),
            out_specs=[in_vmem] * 2,
            out_shape=[
                jax.ShapeDtypeStruct((slots, held, width), low),
                jax.ShapeDtypeStruct((8, 128), high),
            ],
        )(place, *parts)
        return whole.transpose(1, 0, 2), token

    first_cols = qkv_weight.shape[1] + proj_weight.shape[1]
    second_cols = up_weight.shape[1] + folds * down_weight.shape[1]
    pack_own = small(pack_kernel, out_shape=jax.ShapeDtypeStruct((rows, first_cols + second_cols), low))(*masters)
    across_y, across_x = near_bits
    pack_arrived = permute(pack_own, across_y)
    cotangent_cut = small(cut, out_shape=parted)(cotangent.transpose(1, 0, 2))
    token_cut, first_pair, second_pair = small(
        token_kernel,
        in_specs=[in_vmem] * 3 + [anywhere],
        out_shape=[
            parted,
            jax.ShapeDtypeStruct((2, rows, first_cols), low),
            jax.ShapeDtypeStruct((2, rows, second_cols), low),
        ],
    )(tokens.transpose(1, 0, 2), pack_own, pack_arrived, cotangent_cut)
    inputs = to_images(token_cut)

    def gather_far(pair):
        return [pair] + [permute(pair, mask) for mask in direct_masks(far_bits)]

    def join(parts, awaited=()):
        count = len(parts) * parts[0].shape[0]
        return small(
            functools.partial(join_kernel, len(parts)),
            in_specs=[in_vmem] * len(parts) + [anywhere] * len(awaited),
            out_shape=jax.ShapeDtypeStruct((count, *parts[0].shape[1:]), low),
        )(*parts, *awaited)

    def gather_rest(held, awaited=None):
        arrived = permute(held, across_x)
        leaving = [held, arrived]
        if awaited is not None:
            leaving = [after(part, [awaited]) for part in leaving]
        return leaving + [permute(part, core_bits[0]) for part in leaving]

    first_far = join(gather_far(first_pair))
    upstream = to_images(cotangent_cut)
    first_blocks = gather_rest(first_far)
    second_far = gather_far(second_pair)

    step_rows = PER_STEP * length
    block = (step_rows, width)
    pairs = width // (2 * HEAD_DIM)
    steps = images // PER_STEP
    statics = (images, dp_size, spread)
    wide = scratch(width // 128, total, 128)
    probs_block = (PER_STEP, pairs, length, 2 * length)
    attention_outs = [
        ((total, 3 * width), low, (step_rows, 3 * width)),
        ((images, *probs_block[1:]), low, probs_block),
        ((total, width), low, block),
        ((total, width), high, block),
        ((total, width), low, block),
    ]
    attention_flops = (2 * total * width * 4 * width + 8 * total * length * width) // steps
    attention_scratches = [scratch(length, images)]
    *attention, x, w_qkv, w_proj, qkv_t, proj_t = call_kernel(
        first_attention_kernel, statics, 1,
        ["place"] + [None] * 7,
        attention_outs
        + [
            ((total, width), low, None),
            ((width, 3 * width), low, None),
            ((width, width), low, None),
            ((3 * width, width), low, None),
            ((width, width), low, None),
        ],
        [scratch(dp_size * spread, rows, first_cols, dtype=low), wide] + attention_scratches,
        (place, inputs, *first_blocks, keep_mask, vectors),
        attention_flops,
    )
    second_joined = join(second_far, attention[:1])
    attention = call_kernel(
        next_attention_kernel, (PER_STEP,), steps - 1,
        [block] + [None] * 4 + ["await"] * len(attention),
        attention_outs, attention_scratches,
        (x, keep_mask, w_qkv, w_proj, vectors, *attention),
        attention_flops * (steps - 1), first_step=1,
        aliases={5 + at: at for at in range(len(attention))},
    )
    qkv, probs, attended, middle, normed = attention
    second_blocks = gather_rest(second_joined, middle)
    piece = ((slots * images, width), low, None)
    ff_rows = FF_PER_STEP * length
    ff_block = (ff_rows, width)
    results = call_kernel(
        feed_forward_packed_kernel, statics, images // FF_PER_STEP,
        ["place"] + [None] * 5 + [ff_block, ff_block] + [None] * 2,
        [piece] * spread
        + [
            ((total, width), high, ff_block),
            ((total, width), low, ff_block),
            ((half, rows, second_cols), low, None),
            ((half, rows, second_cols), low, None),
            ((width, width), high, None),
            ((8, width), high, None),
            ((1, hidden), high, None),
        ],
        [
            scratch(width, hidden, dtype=low),
            scratch(hidden, width, dtype=low),
            scratch(hidden, width, dtype=low),
            scratch(dp_size * spread, rows, second_cols, dtype=low),
            scratch(1, hidden),
            wide,
            scratch(ff_rows, width, dtype=low),
            scratch(width, ff_rows, dtype=low),
            scratch(ff_rows, width, dtype=low),
            scratch(width, ff_rows, dtype=low),
            scratch(ff_rows, width),
            scratch(ff_rows, 128),
            scratch(ff_rows, width),
            scratch(ff_rows, width),
            scratch(hidden, width, dtype=low),
            scratch(width, hidden, dtype=low),
            scratch(width, hidden),
            scratch(width, hidden),
        ],
        (
            place, upstream, *second_blocks, middle, attended, proj_t, vectors,
        ),
        12 * total * width * hidden + 4 * total * width * width, total * hidden,
    )
    d_middle, d_attended, ff_keep, ff_leave, proj_total, ff_sums, up_sums = results[spread:]

    ff_first = permute(ff_leave, core_bits[0])
    ff_count = half // 2
    ff_next = add_wide(ff_keep[ff_count:], ff_first[ff_count:]).astype(low)
    ff_arrived = permute(ff_next, across_x)
    output_parts = exchange(results[:spread])
    pack_half = ((half, rows, first_cols), low, None)
    wide_rows = (step_rows, 3 * width)
    d_projected, qkv_keep, qkv_leave, att_sums = call_kernel(
        attention_back_packed_kernel, (dp_size, spread), steps,
        ["place", block, wide_rows, probs_block, block, None, None, "await"],
        [((total, 3 * width), low, wide_rows), pack_half, pack_half, ((8, width), high, None)],
        [scratch(width, 3 * width)],
        (place, normed, qkv, probs, d_attended, vectors, proj_total, ff_next),
        2 * total * width * 3 * width + 16 * total * length * width,
    )
    qkv_arrived = permute(after(qkv_leave, output_parts[1:] + [ff_arrived]), core_bits[0])
    input_flops = 2 * total * width * 3 * width
    input_ins = [block, wide_rows, block, None, None, None]
    input_outs = [((total, width), low, block), ((8, width), high, None)]
    d_input, att_sums = call_kernel(
        first_input_kernel, (length,), 1, input_ins, input_outs, [scratch(step_rows, width)],
        (x, d_projected, d_middle, qkv_t, vectors, att_sums), input_flops // steps,
    )
    ff_quarter = half // 4
    ff_last = add_wide(
        ff_keep[ff_quarter:ff_count], ff_first[ff_quarter:ff_count], ff_arrived[ff_quarter:]
    ).astype(low)
    ff_last_arrived = permute(ff_last, across_y)
    qkv_held = add_wide(qkv_keep, qkv_arrived)
    leaving = [
        qkv_held[at : at + ff_quarter].astype(low) for at in range(ff_quarter, half, ff_quarter)
    ]
    qkv_held = qkv_held[:ff_quarter]
    qkv_parts = [permute(part, mask) for part, mask in zip(leaving, direct_masks(near_bits))]
    d_input, att_sums = call_kernel(
        first_input_kernel, (length,), 1, input_ins + ["await"] * 2, input_outs, [scratch(step_rows, width)],
        (x, d_projected, d_middle, qkv_t, vectors, att_sums, d_input, leaving[0]), input_flops // steps,
        first_step=1, aliases={6: 0},
    )
    ff_held = add_wide(
        ff_keep[:ff_quarter], ff_first[:ff_quarter], ff_arrived[:ff_quarter], ff_last_arrived
    )
    qkv_held = add_wide(qkv_held, *qkv_parts)
    blocks = jnp.concatenate([ff_held, qkv_held], axis=2)
    far_leaving = [blocks[at : at + 1].astype(low) for at in range(1, blocks.shape[0])]
    block_parts = [blocks[:1]] + [permute(part, mask) for part, mask in zip(far_leaving, direct_masks(far_bits))]
    results = call_kernel(
        last_input_kernel, (images, spread, length, 2 * PER_STEP), steps - 2,
        ["place"] + input_ins + [None, "await"],
        [piece] * spread + [((8, width), high, None)],
        [wide, scratch(step_rows, width)],
        (place, x, d_projected, d_middle, qkv_t, vectors, att_sums, d_input, far_leaving[0]), input_flops // steps * (steps - 2),
        first_step=2,
    )
    att_sums = results[spread]
    input_pieces = list(results[:spread])
    heights = [master.shape[0] * dp_size for master in masters]
    widths = [master.shape[1] * spread for master in masters]
    rows_old, cols_old = [qkv_rows, proj_rows, up_rows, down_rows], [qkv_cols, proj_cols, up_cols, down_cols]

    def like(*arrays):
        return [jax.ShapeDtypeStruct(array.shape, high) for array in arrays]

    operands = (*block_parts, att_sums, ff_sums, up_sums, *masters, *rows_old)
    *grads, row_sums, message = small(
        functools.partial(gradient_kernel, len(block_parts)),
        out_shape=like(*masters) + [jax.ShapeDtypeStruct((8, rows), high), jax.ShapeDtypeStruct((24, width), high)],
    )(*operands)
    input_pieces[1] = after(input_pieces[1], [row_sums])
    output_parts[0] = after(output_parts[0], [row_sums])
    block_output, settled = settle(output_parts)
    input_grad, input_settled = settle(exchange(input_pieces))
    message = added([message] + [permute(message, mask) for mask in direct_masks((across_x, far_bits[0]))])
    for bit in far_bits[1:-1]:
        message = message + permute(message, bit)
    messages = [message, permute(message, far_bits[-1])]
    col_sums, message = small(
        column_kernel,
        in_specs=[in_vmem] * (1 + len(messages)) + [anywhere],
        out_shape=[
            jax.ShapeDtypeStruct((8, width), high),
            jax.ShapeDtypeStruct((16 + width // 8, 128), high),
        ],
    )(row_sums, *messages, settled)
    messages = [message] + [permute(message, mask) for mask in range(1, spread)]
    operands = (*messages, col_sums, vectors, vector_moment, *grads, *masters, *rows_old, *cols_old)
    results = small(
        functools.partial(update_kernel, len(messages), heights, widths),
        in_specs=[in_vmem] * len(operands) + [anywhere],
        out_shape=like(*masters, *cols_old, *rows_old, vectors, vectors, vectors),
    )(*operands, input_settled)
    news, cols_new, rows_out = results[:4], results[4:8], results[8:12]
    vector_grad, vector_moment_new, vector_new = results[12:]
    factored = []
    for which in range(4):
        factored += [grads[which], rows_out[which], cols_new[which], news[which]]
    return (block_output, input_grad, *factored, vector_grad, vector_moment_new, vector_new)


def body(*arrays):
    spread, dp_size = lax.axis_size("group"), lax.axis_size("dp")
    rows, images = arrays[3].shape[0], arrays[1].shape[0]
    slots, width = arrays[0].shape[1:]
    folds = arrays[6].shape[0] // rows
    powers = all(size & (size - 1) == 0 for size in (spread, dp_size))
    fits = powers and spread == 4 and dp_size > 2
    fits = fits and arrays[5].shape[1] <= width and folds <= 5
    fits = fits and rows % 16 == 0 and images % FF_PER_STEP == 0 and images > 2 * PER_STEP and images % 16 == 0 and slots % 4 == 0
    return packed_body(*arrays) if fits else general_body(*arrays)


def solution(mesh):
    in_specs = (
        P("dp", "group", None),
        P(("dp", "group"), None),
        P("dp", "group", None),
        P("dp", "group"),
        P("dp", "group"),
        P("dp", "group"),
        P("dp", "group"),
        P(),
        P("dp"),
        P("group"),
        P("dp"),
        P("group"),
        P("dp"),
        P("group"),
        P("dp"),
        P("group"),
        P(),
    )
    out_specs = (
        P("dp", "group", None),
        P("dp", "group", None),
        P("dp", "group"),
        P("dp"),
        P("group"),
        P("dp", "group"),
        P("dp", "group"),
        P("dp"),
        P("group"),
        P("dp", "group"),
        P("dp", "group"),
        P("dp"),
        P("group"),
        P("dp", "group"),
        P("dp", "group"),
        P("dp"),
        P("group"),
        P("dp", "group"),
        P(),
        P(),
        P(),
    )
    return jax.shard_map(body, mesh=mesh, in_specs=in_specs, out_specs=out_specs, check_vma=False)
```

```python
import functools
import math

import jax
import jax.numpy as jnp
from jax import lax
from jax.experimental import pallas as pl
from jax.experimental.pallas import tpu as pltpu
from jax.sharding import PartitionSpec as P

HEAD_DIM = 64
STEP_NUMBER = 10


step_rate = 0.3
norm_epsilon = 1e-06
tiny_square = 1e-30
decay_rate = 1.0 - STEP_NUMBER ** (-0.8)
LOG2_E = 1.4426950408889634


def axis_bits(name):
    count = lax.axis_size(name)
    return [(name, 1 << place) for place in range(count.bit_length() - 1)]


def swap_partner(array, step):
    name, bit = step
    count = lax.axis_size(name)
    return lax.ppermute(array, name, [(rank, rank ^ bit) for rank in range(count)])


def upper_side(step):
    name, bit = step
    return (lax.axis_index(name) & bit) != 0


def gather_blocks(array, steps):
    for step in steps:
        arrived = swap_partner(array, step)
        upper = upper_side(step)
        array = jnp.stack([jnp.where(upper, arrived, array), jnp.where(upper, array, arrived)])
    return array


def scatter_sum(array, steps):
    for step in steps:
        upper = upper_side(step)
        leaving = jnp.where(upper, array[0], array[1]).astype(jnp.bfloat16)
        arrived = swap_partner(leaving, step)
        array = jnp.where(upper, array[1], array[0]).astype(jnp.float32) + arrived.astype(jnp.float32)
    return array


def sum_everywhere(array, steps):
    for step in steps:
        array = array + swap_partner(array, step)
    return array


def sum_parts(parts, steps):
    flat = [part.reshape(-1) for part in parts]
    total = sum_everywhere(jnp.concatenate(flat), steps)
    result, start = [], 0
    for part in parts:
        result.append(total[start : start + part.size].reshape(part.shape))
        start += part.size
    return result


def block_order(steps):
    order = []
    for name in ("dp", "group"):
        bits = sorted((step for step in steps if step[0] == name), key=lambda step: -step[1])
        order.append([steps.index(step) for step in bits])
    return order


def blocks_to_whole(blocks, steps):
    count = len(steps)
    rows, cols = blocks.shape[count:]
    dp_axes, group_axes = block_order(steps)
    dp_axes = [count - 1 - axis for axis in dp_axes]
    group_axes = [count - 1 - axis for axis in group_axes]
    whole = blocks.transpose(dp_axes + [count] + group_axes + [count + 1])
    return whole.reshape(rows << len(dp_axes), cols << len(group_axes))


def whole_to_blocks(whole, steps):
    dp_axes, group_axes = block_order(steps)
    rows = whole.shape[0] >> len(dp_axes)
    cols = whole.shape[1] >> len(group_axes)
    split = whole.reshape([2] * len(dp_axes) + [rows] + [2] * len(group_axes) + [cols])
    places = dp_axes + [len(steps)] + group_axes + [len(steps) + 1]
    return split.transpose([places.index(axis) for axis in range(len(places))])


PER_STEP = 4
FF_PER_STEP = 4
SLICE = 48
FF_CHUNK = 256
vmem_bytes = 60 * 1024 * 1024
all_vmem_bytes = 64 * 1024 * 1024


def dot(left, right, left_axis=1, right_axis=0):
    return lax.dot_general(
        left, right, (((left_axis,), (right_axis,)), ((), ())), preferred_element_type=jnp.float32
    )


def normal_form(values):
    center = jnp.mean(values, axis=-1, keepdims=True)
    centered = values - center
    spread = jnp.mean(centered * centered, axis=-1, keepdims=True)
    scale = lax.rsqrt(spread + norm_epsilon)
    return centered * scale, scale


def norm_back(grad, unit, scale, gain):
    weighted = grad * gain
    along = jnp.mean(weighted * unit, axis=-1, keepdims=True)
    level = jnp.mean(weighted, axis=-1, keepdims=True)
    return scale * (weighted - level - unit * along)


def slices_of(count):
    return [slice(start, start + SLICE) for start in range(0, count, SLICE)]


def fold_rows(values):
    return jnp.sum(values.reshape(values.shape[0] // 8, 8, values.shape[1]), axis=0)


def column_sum(values):
    return jnp.sum(values, axis=0, keepdims=True)


def pair_mask(length):
    return lax.broadcasted_iota(jnp.int32, (length, 2 * HEAD_DIM), 1) < HEAD_DIM


def lane_tiles(count):
    return [slice(start, min(start + 128, count)) for start in range(0, count, 128)]


def stack_heads(pair, first):
    none = jnp.zeros_like(pair)
    return jnp.concatenate([jnp.where(first, pair, none), jnp.where(first, none, pair)], axis=0)


def join_heads(rows, first):
    length = rows.shape[0] // 2
    return jnp.where(first, rows[:length], rows[length:])


def gelu_and_slope(pre):
    bell = jnp.exp2(pre * pre * (-0.5 * LOG2_E))
    base = 1.0 + (0.3275911 * 0.5**0.5) * jnp.abs(pre)
    inverse = pl.reciprocal(base, approx=True)
    inverse = inverse * (2.0 - base * inverse)
    poly = inverse * (
        0.5 * 0.254829592
        + inverse
        * (
            0.5 * -0.284496736
            + inverse
            * (0.5 * 1.421413741 + inverse * (0.5 * -1.453152027 + inverse * (0.5 * 1.061405429)))
        )
    )
    tail = poly * bell
    below = jnp.where(pre >= 0, 1.0 - tail, tail)
    return pre * below, below + pre * bell * 0.3989422804014327


def widen(source_ref, wide_ref, images):
    tiles, total, lanes = wide_ref.shape
    rows_at_once = 8 * images

    @pl.loop(0, total // rows_at_once)
    def _(part):
        rows = pl.ds(pl.multiple_of(part * rows_at_once, rows_at_once), rows_at_once)
        for tile in range(tiles):
            cols = slice(tile * lanes, (tile + 1) * lanes)
            wide_ref[tile, rows, :] = source_ref[rows, cols].astype(jnp.float32)


def narrow(wide_ref, target_ref, images):
    tiles, total, lanes = wide_ref.shape
    rows_at_once = 8 * images

    @pl.loop(0, total // rows_at_once)
    def _(part):
        rows = pl.ds(pl.multiple_of(part * rows_at_once, rows_at_once), rows_at_once)
        for tile in range(tiles):
            cols = slice(tile * lanes, (tile + 1) * lanes)
            target_ref[rows, cols] = wide_ref[tile, rows, :].astype(target_ref.dtype)


def take_image(wide_ref, image, images):
    tiles, total, _ = wide_ref.shape
    rows = pl.ds(image, total // images, images)
    return jnp.concatenate([wide_ref[tile, rows, :] for tile in range(tiles)], axis=1)


def put_image(wide_ref, image, images, values):
    tiles, total, lanes = wide_ref.shape
    rows = pl.ds(image, total // images, images)
    for tile in range(tiles):
        wide_ref[tile, rows, :] = values[:, tile * lanes : (tile + 1) * lanes]


def attention_kernel(
    images, tokens_ref, bias_ref, w_qkv_ref, w_proj_ref, vectors_ref,
    x_ref, qkv_ref, probs_ref, attended_ref, middle_ref, wide_ref, normed_ref,
):
    @pl.when(pl.program_id(0) == 0)
    def _():
        widen(tokens_ref, wide_ref, images)
        to_image_rows(wide_ref, x_ref, images)

    attention_steps(
        x_ref, lambda image: bias_ref[image], w_qkv_ref, w_proj_ref, vectors_ref,
        qkv_ref, probs_ref, attended_ref, middle_ref, normed_ref,
    )


def to_image_rows(wide_ref, x_ref, images):
    length = wide_ref.shape[1] // images

    @pl.loop(0, images)
    def _(image):
        rows = pl.ds(pl.multiple_of(image * length, length), length)
        x_ref[rows, :] = take_image(wide_ref, image, images).astype(jnp.bfloat16)


def attention_steps(
    x_ref, bias_column, w_qkv_ref, w_proj_ref, vectors_ref,
    qkv_ref, probs_ref, attended_ref, middle_ref, normed_ref,
):
    per_step, _, length, _ = probs_ref.shape
    step_rows, width = middle_ref.shape
    base = 0 if x_ref.shape[0] == step_rows else pl.program_id(0) * step_rows

    for rows in slices_of(step_rows):
        x = x_ref[pl.ds(pl.multiple_of(base + rows.start, SLICE), SLICE), :].astype(jnp.float32)
        unit, _ = normal_form(x)
        normed_ref[rows, :] = (unit * vectors_ref[0:1] + vectors_ref[1:2]).astype(jnp.bfloat16)
    shift = jnp.concatenate(
        [vectors_ref[2:3], jnp.zeros((1, width), jnp.float32), vectors_ref[3:4]], axis=1
    )
    for start in range(0, 3 * width, 512):
        cols = slice(start, min(start + 512, 3 * width))
        projected = dot(normed_ref[...], w_qkv_ref[:, cols]) + shift[:, cols]
        qkv_ref[:, cols] = projected.astype(jnp.bfloat16)

    pairs = width // (2 * HEAD_DIM)
    first = pair_mask(length)
    place = lax.broadcasted_iota(jnp.int32, (length, 2 * length), 0)
    asker = lax.broadcasted_iota(jnp.int32, (length, 2 * length), 1)
    own = place == jnp.where(asker >= length, asker - length, asker)

    def scores_of(image):
        rows = slice(image * length, (image + 1) * length)
        result = []
        for pair in range(pairs):
            low = pair * 2 * HEAD_DIM
            queries = stack_heads(qkv_ref[rows, low : low + 2 * HEAD_DIM], first)
            result.append(dot(qkv_ref[rows, width + low : width + low + 2 * HEAD_DIM], queries, 1, 1))
        return result

    next_scores = scores_of(0)
    for image in range(per_step):
        rows = slice(image * length, (image + 1) * length)
        all_scores = next_scores
        if image + 1 < per_step:
            next_scores = scores_of(image + 1)
        column = bias_column(image)
        for cols in lane_tiles(2 * length):
            bias = jnp.where(own[:, cols], 0.0, column)
            for pair in range(pairs):
                scores = all_scores[pair][:, cols] * (HEAD_DIM**-0.5 * LOG2_E) + bias
                weights = jnp.exp2(scores - jnp.max(scores, axis=0, keepdims=True))
                probs = weights * (1.0 / jnp.sum(weights, axis=0, keepdims=True))
                probs_ref[image, pair, :, cols] = probs.astype(jnp.bfloat16)
        for pair in range(pairs):
            low = pair * 2 * HEAD_DIM
            values = qkv_ref[rows, 2 * width + low : 2 * width + low + 2 * HEAD_DIM]
            attended = join_heads(dot(probs_ref[image, pair], values, 0, 0), first)
            attended_ref[rows, low : low + 2 * HEAD_DIM] = attended.astype(jnp.bfloat16)

    middle_ref[...] = (
        x_ref[pl.ds(pl.multiple_of(base, length), step_rows), :].astype(jnp.float32)
        + dot(attended_ref[...], w_proj_ref[...])
        + vectors_ref[4:5]
    )


def feed_forward_kernel(
    images, middle_ref, cotangent_ref, attended_ref, w_up_ref, w_down_ref, proj_t_ref, vectors_ref, bias_up_ref,
    output_ref, d_middle_ref, d_attended_ref, up_grad_ref, down_grad_ref, proj_grad_ref, vector_sums_ref, up_sums_ref,
    wide_ref, *scratches,
):
    up_total_ref, down_total_ref, proj_total_ref = scratches[-3:]

    @pl.when(pl.program_id(0) == 0)
    def _():
        widen(cotangent_ref, wide_ref, images)

    feed_forward_steps(
        images, middle_ref, attended_ref, w_up_ref, w_down_ref, proj_t_ref, vectors_ref, bias_up_ref,
        d_middle_ref, d_attended_ref, vector_sums_ref, up_sums_ref, wide_ref, *scratches,
    )

    @pl.when(pl.program_id(0) == pl.num_programs(0) - 1)
    def _():
        narrow(wide_ref, output_ref, images)
        up_grad_ref[...] = up_total_ref[...].astype(jnp.bfloat16)
        down_grad_ref[...] = down_total_ref[...].T.astype(jnp.bfloat16)
        proj_grad_ref[...] = proj_total_ref[...].astype(jnp.bfloat16)


def feed_forward_steps(
    images, middle_ref, attended_ref, w_up_ref, w_down_ref, proj_t_ref, vectors_ref, bias_up_ref,
    d_middle_ref, d_attended_ref, vector_sums_ref, up_sums_ref,
    wide_ref, normed_ref, normed_t_ref, dy_ref, dy_t_ref, unit_ref, scale_ref, ahead_ref, back_ref,
    up_t_ref, down_t_ref, up_total_ref, down_total_ref, proj_total_ref,
):
    step = pl.program_id(0)
    length = wide_ref.shape[1] // images
    hidden = w_up_ref.shape[1]
    per_step = middle_ref.shape[0] // length

    @pl.when(step == 0)
    def _():
        for total in (up_total_ref, down_total_ref, proj_total_ref, vector_sums_ref, up_sums_ref):
            total[...] = jnp.zeros_like(total)
        up_t_ref[...] = w_up_ref[...].T
        down_t_ref[...] = w_down_ref[...].T

    for image in range(per_step):
        rows = slice(image * length, (image + 1) * length)
        dy = take_image(wide_ref, step * per_step + image, images)
        dy_ref[rows, :] = dy.astype(jnp.bfloat16)
        vector_sums_ref[3:4] += column_sum(dy)
        unit, scale = normal_form(middle_ref[rows, :])
        unit_ref[rows, :] = unit
        scale_ref[rows, :] = jnp.broadcast_to(scale, (length, scale_ref.shape[1]))
        normed_ref[rows, :] = (unit * vectors_ref[5:6] + vectors_ref[6:7]).astype(jnp.bfloat16)
    normed_t_ref[...] = normed_ref[...].T
    dy_t_ref[...] = dy_ref[...].T
    chunks = hidden // FF_CHUNK

    def cols_of(chunk):
        return slice(chunk * FF_CHUNK, (chunk + 1) * FF_CHUNK)

    def into(chunk):
        cols = cols_of(chunk)
        pre = dot(normed_ref[...], w_up_ref[:, cols])
        return pre + bias_up_ref[:, cols], dot(dy_ref[...], down_t_ref[:, cols])

    def across(pre, d_active):
        active, slope = gelu_and_slope(pre)
        return active.astype(jnp.bfloat16), (d_active * slope).astype(jnp.bfloat16)

    def out_of(chunk, active, d_hidden):
        cols = cols_of(chunk)
        ahead, back = dot(active, w_down_ref[cols, :]), dot(d_hidden, up_t_ref[cols, :])
        if chunk == 0:
            ahead_ref[...] = ahead
            back_ref[...] = back
        else:
            ahead_ref[...] += ahead
            back_ref[...] += back
        down_total_ref[:, cols] += dot(dy_t_ref[...], active)
        up_total_ref[:, cols] += dot(normed_t_ref[...], d_hidden)
        up_sums_ref[:, cols] += column_sum(d_hidden.astype(jnp.float32))

    entered, crossed = into(0), None
    for chunk in range(chunks + 1):
        next_entered = into(chunk + 1) if chunk + 1 < chunks else None
        next_crossed = across(*entered) if chunk < chunks else None
        if crossed is not None:
            out_of(chunk - 1, *crossed)
        entered, crossed = next_entered, next_crossed

    for image in range(per_step):
        rows = slice(image * length, (image + 1) * length)
        output = middle_ref[rows, :] + ahead_ref[rows, :] + vectors_ref[11:12]
        put_image(wide_ref, step * per_step + image, images, output)
        unit = unit_ref[rows, :]
        grad = back_ref[rows, :]
        vector_sums_ref[1:2] += column_sum(grad * unit)
        vector_sums_ref[2:3] += column_sum(grad)
        d_middle = dy_ref[rows, :].astype(jnp.float32) + norm_back(
            grad, unit, scale_ref[rows, 0:1], vectors_ref[5:6]
        )
        d_middle_ref[rows, :] = d_middle
        d_branch = d_middle.astype(jnp.bfloat16)
        dy_ref[rows, :] = d_branch
        vector_sums_ref[0:1] += column_sum(d_branch.astype(jnp.float32))
    proj_total_ref[...] += dot(attended_ref[...], dy_ref[...], 0, 0)
    d_attended_ref[...] = dot(dy_ref[...], proj_t_ref[...]).astype(jnp.bfloat16)


def attention_back_kernel(
    images, x_ref, qkv_ref, probs_ref, d_attended_ref, d_middle_ref, qkv_t_ref, vectors_ref,
    input_grad_ref, qkv_grad_ref, vector_sums_ref, wide_ref, normed_ref, d_projected_ref, back_ref, qkv_total_ref,
):
    @pl.when(pl.program_id(0) == 0)
    def _():
        qkv_total_ref[...] = jnp.zeros_like(qkv_total_ref)
        vector_sums_ref[...] = jnp.zeros_like(vector_sums_ref)

    def put(image, rows, values):
        put_image(wide_ref, image, images, values)

    attention_back_steps(
        x_ref, qkv_ref, probs_ref, d_attended_ref, vectors_ref, vector_sums_ref, normed_ref, d_projected_ref, qkv_total_ref
    )
    input_back_steps(
        put, probs_ref.shape[2], x_ref, d_projected_ref, d_middle_ref, qkv_t_ref, vectors_ref, vector_sums_ref, back_ref
    )

    @pl.when(pl.program_id(0) == pl.num_programs(0) - 1)
    def _():
        narrow(wide_ref, input_grad_ref, images)
        qkv_grad_ref[...] = qkv_total_ref[...].astype(jnp.bfloat16)


def attention_back_steps(
    x_ref, qkv_ref, probs_ref, d_attended_ref, vectors_ref, vector_sums_ref, normed_ref, d_projected_ref, qkv_total_ref
):
    width = d_attended_ref.shape[1]
    length = probs_ref.shape[2]
    per_step = probs_ref.shape[0]

    pairs = width // (2 * HEAD_DIM)
    first = pair_mask(length)
    scale = HEAD_DIM**-0.5

    def places(image, pair):
        low = pair * 2 * HEAD_DIM
        rows = slice(image * length, (image + 1) * length)
        return rows, [slice(part * width + low, part * width + low + 2 * HEAD_DIM) for part in range(3)]

    def entering(image):
        result = []
        for pair in range(pairs):
            rows, cols = places(image, pair)
            d_attended = stack_heads(d_attended_ref[rows, cols[0]], first)
            d_values = dot(probs_ref[image, pair], d_attended)
            d_projected_ref[rows, cols[2]] = d_values.astype(jnp.bfloat16)
            result.append(dot(qkv_ref[rows, cols[2]], d_attended, 1, 1))
        return result

    next_probs = entering(0)
    for image in range(per_step):
        all_d_probs = next_probs
        if image + 1 < per_step:
            next_probs = entering(image + 1)
        all_d_scores = []
        for pair in range(pairs):
            parts = []
            for cols in lane_tiles(2 * length):
                probs, d_probs = probs_ref[image, pair, :, cols].astype(jnp.float32), all_d_probs[pair][:, cols]
                along = jnp.sum(d_probs * probs, axis=0, keepdims=True)
                parts.append((probs * (d_probs - along)).astype(jnp.bfloat16))
            all_d_scores.append(jnp.concatenate(parts, axis=1))
        for pair in range(pairs):
            rows, cols = places(image, pair)
            d_scores = all_d_scores[pair]
            queries = stack_heads(qkv_ref[rows, cols[0]], first)
            d_queries = join_heads(dot(d_scores, qkv_ref[rows, cols[1]], 0, 0), first) * scale
            d_projected_ref[rows, cols[0]] = d_queries.astype(jnp.bfloat16)
            d_projected_ref[rows, cols[1]] = (dot(d_scores, queries) * scale).astype(jnp.bfloat16)

    query_sums = value_sums = jnp.zeros((8, width), jnp.float32)
    for rows in slices_of(d_attended_ref.shape[0]):
        query_sums += fold_rows(d_projected_ref[rows, :width].astype(jnp.float32))
        value_sums += fold_rows(d_projected_ref[rows, 2 * width :].astype(jnp.float32))
        if x_ref is not None:
            unit, _ = normal_form(x_ref[rows, :].astype(jnp.float32))
            normed_ref[rows, :] = (unit * vectors_ref[0:1] + vectors_ref[1:2]).astype(jnp.bfloat16)
    vector_sums_ref[2:3] += column_sum(query_sums)
    vector_sums_ref[3:4] += column_sum(value_sums)
    qkv_total_ref[...] += dot(normed_ref[...], d_projected_ref[...], 0, 0)


def input_back_steps(
    put, length, x_ref, d_projected_ref, d_middle_ref, qkv_t_ref, vectors_ref, vector_sums_ref, back_ref
):
    step = pl.program_id(0)
    per_step = x_ref.shape[0] // length
    back_ref[...] = dot(d_projected_ref[...], qkv_t_ref[...])
    gain_sums = shift_sums = jnp.zeros((8, x_ref.shape[1]), jnp.float32)
    for rows in slices_of(x_ref.shape[0]):
        unit, scale = normal_form(x_ref[rows, :].astype(jnp.float32))
        grad = back_ref[rows, :]
        gain_sums += fold_rows(grad * unit)
        shift_sums += fold_rows(grad)
        back_ref[rows, :] = d_middle_ref[rows, :] + norm_back(grad, unit, scale, vectors_ref[0:1])
    vector_sums_ref[0:1] += column_sum(gain_sums)
    vector_sums_ref[1:2] += column_sum(shift_sums)
    for image in range(per_step):
        rows = slice(image * length, (image + 1) * length)
        put(step * per_step + image, rows, back_ref[rows, :])


def whole_block(shape):
    return pl.BlockSpec(shape, lambda step: (0,) * len(shape))


def step_block(shape, first=0):
    return pl.BlockSpec(shape, lambda step: (first + step,) + (0,) * (len(shape) - 1))


def scratch(*shape, dtype=jnp.float32):
    return pltpu.VMEM(shape, dtype)


def call_kernel(kernel, statics, steps, ins, outs, scratches, operands, flops, transcendentals=0, first_step=0, aliases={}, vmem=vmem_bytes):
    in_specs = [
        pl.BlockSpec(memory_space=pltpu.SMEM)
        if block == "place"
        else pl.BlockSpec(memory_space=pl.ANY)
        if block == "await"
        else whole_block(op.shape) if block is None else step_block(block, first_step)
        for op, block in zip(operands, ins)
    ]
    out_specs = [
        whole_block(shape) if block is None else step_block(block, first_step) for shape, dtype, block in outs
    ]
    moved = sum(op.size * op.dtype.itemsize for op in operands) + sum(
        math.prod(shape) * jnp.dtype(dtype).itemsize for shape, dtype, block in outs
    )
    return pl.pallas_call(
        functools.partial(kernel, *statics),
        grid=(steps,),
        in_specs=in_specs,
        out_specs=out_specs,
        out_shape=[jax.ShapeDtypeStruct(shape, dtype) for shape, dtype, block in outs],
        scratch_shapes=scratches,
        input_output_aliases=aliases,
        compiler_params=pltpu.CompilerParams(vmem_limit_bytes=vmem),
        cost_estimate=pl.CostEstimate(
            flops=flops * 8, bytes_accessed=moved, transcendentals=transcendentals
        ),
    )(*operands)


def attention_forward(tokens, bias, w_qkv, w_proj, vectors):
    images, length, _ = bias.shape
    total, width = tokens.shape
    pairs = width // (2 * HEAD_DIM)
    rows = PER_STEP * length
    low, high = jnp.bfloat16, jnp.float32
    outs = [
        ((total, width), low, None),
        ((total, 3 * width), low, (rows, 3 * width)),
        ((images, pairs, length, 2 * length), low, (PER_STEP, pairs, length, 2 * length)),
        ((total, width), low, (rows, width)),
        ((total, width), high, (rows, width)),
    ]
    return call_kernel(
        attention_kernel, (images,), images // PER_STEP,
        [None, (PER_STEP, length, 1), None, None, None], outs,
        [scratch(width // 128, total, 128), scratch(rows, width, dtype=low)],
        (tokens, bias, w_qkv, w_proj, vectors),
        2 * total * width * 4 * width + 8 * total * length * width,
    )


def feed_forward(images, middle, cotangent, attended, w_up, w_down, w_proj, vectors):
    total, width = middle.shape
    hidden = w_up.shape[1]
    rows = total // images * FF_PER_STEP
    low, high = jnp.bfloat16, jnp.float32
    block = (rows, width)
    outs = [
        ((total, width), low, None),
        ((total, width), high, block),
        ((total, width), low, block),
        ((width, hidden), low, None),
        ((hidden, width), low, None),
        ((width, width), low, None),
        ((8, width), high, None),
        ((1, hidden), high, None),
    ]
    scratches = [
        scratch(width // 128, total, 128),
        scratch(rows, width, dtype=low),
        scratch(width, rows, dtype=low),
        scratch(rows, width, dtype=low),
        scratch(width, rows, dtype=low),
        scratch(rows, width),
        scratch(rows, 128),
        scratch(rows, width),
        scratch(rows, width),
        scratch(hidden, width, dtype=low),
        scratch(width, hidden, dtype=low),
        scratch(width, hidden),
        scratch(width, hidden),
        scratch(width, width),
    ]
    return call_kernel(
        feed_forward_kernel, (images,), images // FF_PER_STEP,
        [block, None, block, None, None, None, None, None], outs, scratches,
        (middle, cotangent, attended, w_up, w_down, w_proj.T, vectors, vectors[7:11].reshape(1, hidden)),
        12 * total * width * hidden + 4 * total * width * width, total * hidden,
    )


def attention_back(x, qkv, probs, d_attended, d_middle, w_qkv, vectors):
    images, pairs, length, _ = probs.shape
    total, width = x.shape
    rows = PER_STEP * length
    low, high = jnp.bfloat16, jnp.float32
    block = (rows, width)
    outs = [
        ((total, width), low, None),
        ((width, 3 * width), low, None),
        ((8, width), high, None),
    ]
    scratches = [
        scratch(width // 128, total, 128),
        scratch(rows, width, dtype=low),
        scratch(rows, 3 * width, dtype=low),
        scratch(rows, width),
        scratch(width, 3 * width),
    ]
    return call_kernel(
        attention_back_kernel, (images,), images // PER_STEP,
        [block, (rows, 3 * width), (PER_STEP, pairs, length, 2 * length), block, block, None, None],
        outs, scratches, (x, qkv, probs, d_attended, d_middle, w_qkv.T, vectors),
        4 * total * width * 3 * width + 16 * total * length * width,
    )

def linear_place():
    return lax.axis_index("dp") * lax.axis_size("group") + lax.axis_index("group")


def permute(array, mask):
    count = lax.axis_size("dp") * lax.axis_size("group")
    return lax.ppermute(array, ("dp", "group"), [(rank, rank ^ mask) for rank in range(count)])


def direct_masks(bits):
    masks = [0]
    for bit in bits:
        masks = masks + [mask | bit for mask in masks]
    return masks[1:]


def add_wide(first, *rest):
    total = first.astype(jnp.float32)
    for part in rest:
        total = total + part.astype(jnp.float32)
    return total


def packed_place(mask, spread, count):
    return ((mask >> 1) & (spread - 1)) * (count // (2 * spread)) + (mask >> (spread.bit_length()))


def scatter_step(held, bits):
    masks = direct_masks(bits)
    size = held.shape[0] // (len(masks) + 1)
    parts = [
        permute(held[size * (at + 1) : size * (at + 2)].astype(jnp.bfloat16), mask)
        for at, mask in enumerate(masks)
    ]
    return held[:size], parts


def add_wide(first, *rest):
    total = first.astype(jnp.float32)
    for part in rest:
        total = total + part.astype(jnp.float32)
    return total


def packed_place(mask, spread, count):
    return ((mask >> 1) & (spread - 1)) * (count // (2 * spread)) + (mask >> (spread.bit_length()))


def gather_step(held, bits):
    return held + [permute(part, mask) for mask in direct_masks(bits) for part in held]


def gathered_place(mask, count):
    return (mask & 1) * (count // 2) + ((mask >> 2) & 1) * (count // 4) + (mask >> 3) * 2 + ((mask >> 1) & 1)


def unpack(place_ref, block_refs, packed_ref, put, dp_size, spread):
    place = place_ref[0]
    size = block_refs[0].shape[0]
    for at, block_ref in enumerate(block_refs):
        packed_ref[at * size : (at + 1) * size] = block_ref[...]
    count = dp_size * spread
    for row in range(dp_size):
        for col in range(spread):
            put(row, col, packed_ref[gathered_place((row * spread + col) ^ place, count)])


def unpack_in_order(blocks_ref, put, dp_size, spread):
    for row in range(dp_size):
        for col in range(spread):
            put(row, col, blocks_ref[row * spread + col])


def pack(place_ref, take, keep_ref, leave_ref, dp_size, spread):
    place = place_ref[0]
    odd = (place & 1) == 1
    for row in range(dp_size):
        for col in range(0, spread, 2):
            at = packed_place((row * spread + col) ^ place, spread, dp_size * spread)
            even_block, odd_block = take(row, col), take(row, col + 1)
            keep_ref[at] = jnp.where(odd, odd_block, even_block)
            leave_ref[at] = jnp.where(odd, even_block, odd_block)


def narrow_pieces(place_ref, wide_ref, piece_refs, spread):
    tiles, _, lanes = wide_ref.shape
    rows_of_piece = piece_refs[0].shape[0]
    step = 64
    group = place_ref[0] & (spread - 1)
    for relative, piece_ref in enumerate(piece_refs):
        base = (group ^ relative) * rows_of_piece

        @pl.loop(0, rows_of_piece // step)
        def _(part):
            target = pl.ds(pl.multiple_of(part * step, step), step)
            source = pl.ds(pl.multiple_of(base + part * step, step), step)
            for tile in range(tiles):
                cols = slice(tile * lanes, (tile + 1) * lanes)
                piece_ref[target, cols] = wide_ref[tile, source, :].astype(jnp.bfloat16)


def general_body(
    tokens,
    keep_mask,
    cotangent,
    qkv_weight,
    proj_weight,
    up_weight,
    down_weight,
    vectors,
    qkv_rows,
    qkv_cols,
    proj_rows,
    proj_cols,
    up_rows,
    up_cols,
    down_rows,
    down_cols,
    vector_moment,
):
    masters = (qkv_weight, proj_weight, up_weight, down_weight)
    lowered = tuple((master.astype(jnp.bfloat16) for master in masters))
    dp_bits, group_bits = axis_bits("dp"), axis_bits("group")
    gather_steps = dp_bits[1:] + group_bits[1:] + dp_bits[:1] + group_bits[:1]
    scatter_steps = gather_steps[::-1]
    w_qkv, w_proj, w_up, w_down = tuple(
        blocks_to_whole(gather_blocks(part, gather_steps), gather_steps) for part in lowered
    )
    spread = lax.axis_size("group")

    def slots_in(array):
        held, slots, width = array.shape
        parts = array.transpose(1, 0, 2).reshape(slots, spread, held // spread, width)
        parts = lax.all_to_all(
            parts.transpose(1, 0, 2, 3), "group", split_axis=0, concat_axis=0, tiled=True
        )
        return parts.reshape(spread * slots * (held // spread), width)

    def slots_out(array):
        held, slots, width = tokens.shape
        parts = array.reshape(spread, slots, held // spread, width)
        parts = lax.all_to_all(parts, "group", split_axis=0, concat_axis=0, tiled=True)
        return parts.transpose(1, 0, 2, 3).reshape(slots, held, width).transpose(1, 0, 2)

    images = keep_mask.shape[0]
    bias = jnp.where(keep_mask > 0, 0.0, -1e30)[:, :, None]
    x, qkv, probs, attended, middle = attention_forward(
        slots_in(tokens), bias, w_qkv, w_proj, vectors
    )
    output, d_middle, d_attended, up_grad, down_grad, proj_grad, ff_sums, up_sums = feed_forward(
        images, middle, slots_in(cotangent), attended, w_up, w_down, w_proj, vectors
    )
    block_output = slots_out(output)
    d_input, qkv_grad, att_sums = attention_back(
        x, qkv, probs, d_attended, d_middle, w_qkv, vectors
    )
    input_grad = slots_out(d_input)
    local_vectors = jnp.concatenate(
        [att_sums[:4], ff_sums[:3], up_sums.reshape(4, -1), ff_sums[3:4]], axis=0
    )
    vector_grad = sum_everywhere(local_vectors, group_bits + dp_bits)
    local_grads = (qkv_grad, proj_grad, up_grad, down_grad)
    owned = tuple(
        scatter_sum(whole_to_blocks(part, scatter_steps), scatter_steps) for part in local_grads
    )
    squares = tuple((gradient * gradient + tiny_square for gradient in owned))
    row_parts = tuple((jnp.sum(square, axis=1) for square in squares)) + tuple(
        (jnp.sum(master * master, axis=1) for master in masters)
    )
    row_sums = sum_parts(row_parts, group_bits)
    rows_old = (qkv_rows, proj_rows, up_rows, down_rows)
    cols_old = (qkv_cols, proj_cols, up_cols, down_cols)
    total_cols = tuple((gradient.shape[1] * lax.axis_size("group") for gradient in owned))
    total_rows = tuple((gradient.shape[0] * lax.axis_size("dp") for gradient in owned))
    rows_new = tuple(
        (
            decay_rate * rows_old[which] + (1.0 - decay_rate) * row_sums[which] / total_cols[which]
            for which in range(4)
        )
    )
    col_parts = (
        tuple((jnp.sum(square, axis=0) for square in squares))
        + tuple((jnp.sum(row_stat) for row_stat in rows_new))
        + tuple((jnp.sum(row_sums[4 + which]) for which in range(4)))
    )
    col_sums = sum_parts(col_parts, dp_bits)
    results = []
    for which in range(4):
        cols_new = (
            decay_rate * cols_old[which] + (1.0 - decay_rate) * col_sums[which] / total_rows[which]
        )
        mean_rows = col_sums[4 + which] / total_rows[which]
        spread = jnp.sqrt(col_sums[8 + which] / (total_rows[which] * total_cols[which]))
        second = rows_new[which][:, None] * cols_new[None, :] / mean_rows
        updated = masters[which] - step_rate * spread * owned[which] * lax.rsqrt(second)
        results.append((owned[which], rows_new[which], cols_new, updated))
    vector_moment_new = decay_rate * vector_moment + (1.0 - decay_rate) * (
        vector_grad * vector_grad + tiny_square
    )
    row_spread = jnp.sqrt(jnp.mean(vectors * vectors, axis=1, keepdims=True))
    vector_new = vectors - step_rate * row_spread * vector_grad * lax.rsqrt(vector_moment_new)
    return (
        block_output,
        input_grad,
        results[0][0],
        results[0][1],
        results[0][2],
        results[0][3],
        results[1][0],
        results[1][1],
        results[1][2],
        results[1][3],
        results[2][0],
        results[2][1],
        results[2][2],
        results[2][3],
        results[3][0],
        results[3][1],
        results[3][2],
        results[3][3],
        vector_grad,
        vector_moment_new,
        vector_new,
    )


def first_attention_kernel(images, dp_size, spread, place_ref, tokens_ref, *refs):
    blocks, refs = refs[:4], refs[4:]
    keep_ref, vectors_ref, *outs, x_ref, w_qkv_ref, w_proj_ref, qkv_t_ref, proj_t_ref = refs[:-3]
    packed_ref, wide_ref, bias_ref = refs[-3:]
    rows = packed_ref.shape[1]
    qkv_cols, proj_cols = w_qkv_ref.shape[1] // spread, w_proj_ref.shape[1] // spread

    @pl.when(pl.program_id(0) == 0)
    def _():
        widen(tokens_ref, wide_ref, images)
        to_image_rows(wide_ref, x_ref, images)

        def put(row, col, block):
            down = slice(row * rows, (row + 1) * rows)
            w_qkv_ref[down, col * qkv_cols : (col + 1) * qkv_cols] = block[:, :qkv_cols]
            w_proj_ref[down, col * proj_cols : (col + 1) * proj_cols] = block[:, qkv_cols:]

        unpack(place_ref, blocks, packed_ref, put, dp_size, spread)
        qkv_t_ref[...] = w_qkv_ref[...].T
        proj_t_ref[...] = w_proj_ref[...].T

    attention_part(0, x_ref, keep_ref, w_qkv_ref, w_proj_ref, vectors_ref, *outs, bias_ref)


def next_attention_kernel(start, x_ref, keep_ref, w_qkv_ref, w_proj_ref, vectors_ref, *refs):
    attention_part(start, x_ref, keep_ref, w_qkv_ref, w_proj_ref, vectors_ref, *refs[-6:])


def attention_part(
    start, x_ref, keep_ref, w_qkv_ref, w_proj_ref, vectors_ref,
    qkv_ref, probs_ref, attended_ref, middle_ref, normed_ref, bias_ref,
):
    @pl.when(pl.program_id(0) == 0)
    def _():
        bias_ref[...] = jnp.where(keep_ref[...] > 0, 0.0, -1e30).T

    def bias_column(image):
        here = start + pl.program_id(0) * probs_ref.shape[0] + image
        lane = lax.broadcasted_iota(jnp.int32, bias_ref.shape, 1)
        return row_sum(jnp.where(lane == here, bias_ref[...], 0.0))

    attention_steps(
        x_ref, bias_column, w_qkv_ref, w_proj_ref, vectors_ref,
        qkv_ref, probs_ref, attended_ref, middle_ref, normed_ref,
    )


def feed_forward_packed_kernel(images, dp_size, spread, place_ref, *refs):
    cotangent_ref, blocks, refs = refs[0], refs[1:5], refs[5:]
    middle_ref, attended_ref, proj_t_ref, vectors_ref = refs[:4]
    outputs, refs = refs[4 : 4 + spread], refs[4 + spread :]
    d_middle_ref, d_attended_ref, keep_ref, leave_ref, proj_total_ref, vector_sums_ref, up_sums_ref = refs[:7]
    w_up_ref, w_down_ref, down_low_ref, packed_ref, bias_up_ref, wide_ref = refs[7:13]
    scratches = refs[13:]
    width = w_up_ref.shape[0]
    up_total_ref, down_total_ref = scratches[-2:]
    rows = packed_ref.shape[1]
    up_cols = w_up_ref.shape[1] // spread
    out_cols = w_down_ref.shape[1] // spread
    folds = w_down_ref.shape[0] // w_up_ref.shape[0]

    @pl.when(pl.program_id(0) == 0)
    def _():
        widen(cotangent_ref, wide_ref, images)
        for fold in range(bias_up_ref.shape[1] // width):
            bias_up_ref[:, fold * width : (fold + 1) * width] = vectors_ref[7 + fold : 8 + fold]

        def put(row, col, block):
            w_up_ref[row * rows : (row + 1) * rows, col * up_cols : (col + 1) * up_cols] = block[:, :up_cols]
            for fold in range(folds):
                down = (row * folds + fold) * rows
                start = up_cols + fold * out_cols
                w_down_ref[down : down + rows, col * out_cols : (col + 1) * out_cols] = block[
                    :, start : start + out_cols
                ]

        unpack(place_ref, blocks, packed_ref, put, dp_size, spread)

    feed_forward_steps(
        images, middle_ref, attended_ref, w_up_ref, w_down_ref, proj_t_ref, vectors_ref, bias_up_ref,
        d_middle_ref, d_attended_ref, vector_sums_ref, up_sums_ref, wide_ref, *scratches, proj_total_ref,
    )

    @pl.when(pl.program_id(0) == pl.num_programs(0) - 1)
    def _():
        narrow_pieces(place_ref, wide_ref, outputs, spread)
        down_low_ref[...] = down_total_ref[...].T.astype(jnp.bfloat16)

        def take(row, col):
            across = slice(row * rows, (row + 1) * rows)
            cols = slice(col * out_cols, (col + 1) * out_cols)
            parts = [up_total_ref[across, col * up_cols : (col + 1) * up_cols].astype(jnp.bfloat16)]
            for fold in range(folds):
                down = (row * folds + fold) * rows
                parts.append(down_low_ref[down : down + rows, cols])
            return jnp.concatenate(parts, axis=1)

        pack(place_ref, take, keep_ref, leave_ref, dp_size, spread)


def attention_back_packed_kernel(
    dp_size, spread, place_ref, normed_ref, qkv_ref, probs_ref, d_attended_ref, vectors_ref, proj_total_ref, _,
    d_projected_ref, keep_ref, leave_ref, vector_sums_ref, total_ref,
):
    @pl.when(pl.program_id(0) == 0)
    def _():
        total_ref[...] = jnp.zeros_like(total_ref)
        vector_sums_ref[...] = jnp.zeros_like(vector_sums_ref)

    attention_back_steps(
        None, qkv_ref, probs_ref, d_attended_ref, vectors_ref, vector_sums_ref, normed_ref, d_projected_ref, total_ref
    )

    @pl.when(pl.program_id(0) == pl.num_programs(0) - 1)
    def _():
        rows = keep_ref.shape[1]
        qkv_cols, proj_cols = total_ref.shape[1] // spread, proj_total_ref.shape[1] // spread

        def take(row, col):
            down = slice(row * rows, (row + 1) * rows)
            parts = [
                total_ref[down, col * qkv_cols : (col + 1) * qkv_cols],
                proj_total_ref[down, col * proj_cols : (col + 1) * proj_cols],
            ]
            return jnp.concatenate(parts, axis=1).astype(jnp.bfloat16)

        pack(place_ref, take, keep_ref, leave_ref, dp_size, spread)


def first_input_kernel(
    length, x_ref, d_projected_ref, d_middle_ref, qkv_t_ref, vectors_ref, before_ref, *refs
):
    d_input_ref, vector_sums_ref, back_ref = refs[-3:]

    @pl.when(pl.program_id(0) == 0)
    def _():
        vector_sums_ref[...] = before_ref[...]

    def put(image, rows, values):
        d_input_ref[rows, :] = values.astype(jnp.bfloat16)

    input_back_steps(
        put, length, x_ref, d_projected_ref, d_middle_ref, qkv_t_ref, vectors_ref, vector_sums_ref, back_ref
    )


def last_input_kernel(
    images, spread, length, first, place_ref, x_ref, d_projected_ref, d_middle_ref, qkv_t_ref, vectors_ref, before_ref,
    d_input_ref, _, *refs,
):
    pieces, (vector_sums_ref, wide_ref, back_ref) = refs[:spread], refs[spread:]

    @pl.when(pl.program_id(0) == 0)
    def _():
        vector_sums_ref[...] = before_ref[...]
        for image in range(first):
            rows = slice(image * length, (image + 1) * length)
            put_image(wide_ref, image, images, d_input_ref[rows, :].astype(jnp.float32))

    def put(image, rows, values):
        put_image(wide_ref, first + image, images, values)

    input_back_steps(
        put, length, x_ref, d_projected_ref, d_middle_ref, qkv_t_ref, vectors_ref, vector_sums_ref, back_ref
    )

    @pl.when(pl.program_id(0) == pl.num_programs(0) - 1)
    def _():
        narrow_pieces(place_ref, wide_ref, pieces, spread)


def cut(array_ref, parts_ref):
    count = parts_ref.shape[2]
    for member in range(parts_ref.shape[0]):
        parts_ref[member] = array_ref[:, member * count : (member + 1) * count, :]


def pack_kernel(qkv_ref, proj_ref, up_ref, down_ref, pack_ref):
    rows, start = pack_ref.shape[0], 0
    parts = [qkv_ref[...], proj_ref[...], up_ref[...]]
    parts += [down_ref[fold * rows : (fold + 1) * rows, :] for fold in range(down_ref.shape[0] // rows)]
    for part in parts:
        pack_ref[:, start : start + part.shape[1]] = part.astype(jnp.bfloat16)
        start += part.shape[1]


def token_kernel(array_ref, own_ref, arrived_ref, _, parts_ref, first_ref, second_ref):
    start = first_ref.shape[2]
    for at, pack_ref in enumerate((own_ref, arrived_ref)):
        first_ref[at] = pack_ref[:, :start]
        second_ref[at] = pack_ref[:, start:]
    cut(array_ref, parts_ref)


def join_kernel(count, *refs):
    size = refs[0].shape[0]
    for at, part_ref in enumerate(refs[:count]):
        refs[-1][at * size : (at + 1) * size] = part_ref[...]


def settle_kernel(spread, place_ref, *refs):
    lists, (output_ref, token_ref) = refs[:-2], refs[-2:]
    token_ref[...] = jnp.zeros_like(token_ref)
    group = place_ref[0] & (spread - 1)
    count = lists[0].shape[1]
    share = len(lists) // spread * count
    for at, piece_ref in enumerate(lists):
        relative, part = at % spread, at // spread
        start = pl.multiple_of((group ^ relative) * share + part * count, count)
        output_ref[:, pl.ds(start, count), :] = piece_ref[...]


def lane_table(rows, columns):
    lane = lax.broadcasted_iota(jnp.int32, (rows, 128), 1)
    table = jnp.zeros((rows, 128), jnp.float32)
    for at, column in enumerate(columns):
        table = jnp.where(lane == at, column, table)
    return table


def added(parts):
    while len(parts) > 1:
        parts = [sum(parts[at : at + 2][1:], parts[at]) for at in range(0, len(parts), 2)]
    return parts[0]


def row_sum(values):
    return jnp.sum(values, axis=1, keepdims=True)


def after_kernel(*refs):
    pass


def gradient_kernel(count, *refs):
    block_parts, sums, refs = refs[:count], refs[count : count + 3], refs[count + 3 :]
    masters, rows_old, refs = refs[:4], refs[4:8], refs[8:]
    grads, (row_ref, message_ref) = refs[:4], refs[4:]
    blocks = added([part[0].astype(jnp.float32) for part in block_parts])
    rows, up_cols = grads[2].shape
    qkv_cols, out_cols = grads[0].shape[1], grads[1].shape[1]
    folds = grads[3].shape[0] // rows
    up = blocks[:, :up_cols]
    downs = [blocks[:, up_cols + fold * out_cols :][:, :out_cols] for fold in range(folds)]
    start = up_cols + folds * out_cols
    qkv = blocks[:, start : start + qkv_cols]
    proj = blocks[:, start + qkv_cols :]
    grads[0][...] = qkv
    grads[1][...] = proj
    grads[2][...] = up
    for fold in range(folds):
        grads[3][fold * rows : (fold + 1) * rows, :] = downs[fold]
    squares = [part * part + tiny_square for part in (qkv, proj, up, *downs)]
    row_ref[...] = lane_table(rows, [row_sum(square) for square in squares]).T[: row_ref.shape[0], :]
    width = message_ref.shape[1]
    message_ref[...] = jnp.zeros_like(message_ref)
    for at, square in enumerate((*squares[:3], added(squares[3:]))):
        message_ref[at : at + 1, : square.shape[1]] = column_sum(square)
    scalars = [column_sum(row_sum(master[...] * master[...])) for master in masters]
    scalars += [row_sum(part[...].reshape(1, part.shape[0])) for part in rows_old]
    message_ref[4:5, :128] = lane_table(1, scalars)
    att_ref, ff_ref, up_ref = sums
    count = up_ref.shape[1] // width
    message_ref[8:12, :] = att_ref[:4]
    message_ref[12:15, :] = ff_ref[:3]
    for at in range(count):
        message_ref[15 + at : 16 + at, :] = up_ref[:, at * width : (at + 1) * width]
    message_ref[15 + count : 16 + count, :] = ff_ref[3:4]


def column_kernel(row_ref, *refs):
    parts, (cols_ref, message_ref) = refs[:-3], refs[-2:]
    total = added([part[...] for part in parts])
    cols_ref[...] = total[:8]
    width = total.shape[1]
    rows = row_ref.shape[1]
    message_ref[...] = jnp.zeros_like(message_ref)
    message_ref[:8, :rows] = row_ref[...]
    columns = [row_sum(total[which : which + 1]) for which in range(4)]
    squares = [total[4:5, which : which + 1] for which in range(4)]
    message_ref[8:9, :] = lane_table(1, columns + squares)
    for tile in range(width // 128):
        message_ref[16 * (tile + 1) : 16 * (tile + 2), :] = total[8:, tile * 128 : (tile + 1) * 128]


def update_kernel(count, heights, widths, *refs):
    messages, refs = refs[:count], refs[count:]
    cols_ref, vectors_ref, moment_ref, refs = refs[0], refs[1], refs[2], refs[3:]
    grads, masters, rows_old, cols_old, refs = refs[:4], refs[4:8], refs[8:12], refs[12:16], refs[17:]
    news, cols_new, rows_out, refs = refs[:4], refs[4:8], refs[8:12], refs[12:]
    vector_grad_ref, moment_new_ref, vector_new_ref = refs
    sums = added([message[...] for message in messages])
    height = grads[0].shape[0]
    folds = grads[3].shape[0] // height
    lanes = [[0], [1], [2], list(range(3, 3 + folds))]
    share = 1.0 - decay_rate
    for which in range(4):
        entries = heights[which] * widths[which]
        cols = cols_old[which].shape[0]
        new = decay_rate * cols_old[which][...].reshape(1, cols) + share / heights[which] * cols_ref[
            which : which + 1, :cols
        ]
        cols_new[which][...] = new[0]
        old_total = cols_ref[4:5, 4 + which : 5 + which]
        mean_rows = (decay_rate * old_total + share / widths[which] * sums[8:9, which : which + 1]) / heights[which]
        rate = step_rate * jnp.sqrt(sums[8:9, 4 + which : 5 + which] / entries)
        across = new / mean_rows
        old = rows_old[which][...].reshape(1, len(lanes[which]) * height)
        row_sums = jnp.concatenate([sums[lane : lane + 1, :height] for lane in lanes[which]], axis=1)
        row = decay_rate * old + share / widths[which] * row_sums
        rows_out[which][...] = row[0]
        for fold in range(len(lanes[which])):
            part = slice(fold * height, (fold + 1) * height)
            column = jnp.broadcast_to(row[:, part], (8, height)).T[:, :1]
            news[which][part, :] = masters[which][part, :] - rate * grads[which][part, :] * lax.rsqrt(column * across)
    vectors = vectors_ref[...]
    count = vectors.shape[0]
    gradient = jnp.concatenate(
        [sums[16 * (tile + 1) : 16 * (tile + 1) + count] for tile in range(vectors.shape[1] // 128)], axis=1
    )
    vector_grad_ref[...] = gradient
    moment = decay_rate * moment_ref[...] + share * (gradient * gradient + tiny_square)
    moment_new_ref[...] = moment
    spread = jnp.sqrt(jnp.mean(vectors * vectors, axis=1, keepdims=True))
    vector_new_ref[...] = vectors - step_rate * spread * gradient * lax.rsqrt(moment)


def packed_body(
    tokens, keep_mask, cotangent, qkv_weight, proj_weight, up_weight, down_weight, vectors,
    qkv_rows, qkv_cols, proj_rows, proj_cols, up_rows, up_cols, down_rows, down_cols, vector_moment,
):
    spread, dp_size = lax.axis_size("group"), lax.axis_size("dp")
    low, high = jnp.bfloat16, jnp.float32
    place = linear_place().astype(jnp.int32).reshape(1)
    group = lax.axis_index("group")
    held, slots, width = tokens.shape
    images, length = keep_mask.shape
    hidden = up_weight.shape[1] * spread
    total = images * length
    rows = qkv_weight.shape[0]
    folds = down_weight.shape[0] // rows
    core_bits = (1,)
    near_bits = tuple(1 << at for at in range(1, spread.bit_length()))
    far_bits = tuple(spread << at for at in range(1, dp_size.bit_length() - 1))
    half = spread * dp_size // 2

    anywhere = pl.BlockSpec(memory_space=pl.ANY)
    in_smem = pl.BlockSpec(memory_space=pltpu.SMEM)

    in_vmem = pl.BlockSpec(memory_space=pltpu.VMEM)
    small = functools.partial(
        pl.pallas_call, compiler_params=pltpu.CompilerParams(vmem_limit_bytes=vmem_bytes)
    )
    masters = (qkv_weight, proj_weight, up_weight, down_weight)
    parted = jax.ShapeDtypeStruct((spread, slots, images, width), low)

    def after(array, awaited):
        return small(
            after_kernel,
            in_specs=[anywhere] * (1 + len(awaited)),
            out_specs=anywhere,
            out_shape=jax.ShapeDtypeStruct(array.shape, array.dtype),
            input_output_aliases={0: 0},
        )(array, *awaited)

    def to_group(parts):
        return lax.all_to_all(parts, "group", split_axis=0, concat_axis=0, tiled=True)

    def to_images(parts):
        return to_group(parts).reshape(total, width)

    def exchange(parts):
        return [parts[0]] + [permute(part, relative) for relative, part in enumerate(parts) if relative]

    def settle(parts):
        parts = [part.reshape(slots, -1, width) for part in parts]
        whole, token = small(
            functools.partial(settle_kernel, spread),
            in_specs=[in_smem] + [in_vmem] * len(parts),
            out_specs=[in_vmem] * 2,
            out_shape=[
                jax.ShapeDtypeStruct((slots, held, width), low),
                jax.ShapeDtypeStruct((8, 128), high),
            ],
        )(place, *parts)
        return whole.transpose(1, 0, 2), token

    first_cols = qkv_weight.shape[1] + proj_weight.shape[1]
    second_cols = up_weight.shape[1] + folds * down_weight.shape[1]
    pack_own = small(pack_kernel, out_shape=jax.ShapeDtypeStruct((rows, first_cols + second_cols), low))(*masters)
    across_y, across_x = near_bits
    pack_arrived = permute(pack_own, across_y)
    cotangent_cut = small(cut, out_shape=parted)(cotangent.transpose(1, 0, 2))
    token_cut, first_pair, second_pair = small(
        token_kernel,
        in_specs=[in_vmem] * 3 + [anywhere],
        out_shape=[
            parted,
            jax.ShapeDtypeStruct((2, rows, first_cols), low),
            jax.ShapeDtypeStruct((2, rows, second_cols), low),
        ],
    )(tokens.transpose(1, 0, 2), pack_own, pack_arrived, cotangent_cut)
    inputs = to_images(token_cut)

    def gather_far(pair):
        return [pair] + [permute(pair, mask) for mask in direct_masks(far_bits)]

    def join(parts, awaited=()):
        count = len(parts) * parts[0].shape[0]
        return small(
            functools.partial(join_kernel, len(parts)),
            in_specs=[in_vmem] * len(parts) + [anywhere] * len(awaited),
            out_shape=jax.ShapeDtypeStruct((count, *parts[0].shape[1:]), low),
        )(*parts, *awaited)

    def gather_rest(held, awaited=None):
        arrived = permute(held, across_x)
        leaving = [held, arrived]
        if awaited is not None:
            leaving = [after(part, [awaited]) for part in leaving]
        return leaving + [permute(part, core_bits[0]) for part in leaving]

    first_far = join(gather_far(first_pair))
    upstream = to_images(cotangent_cut)
    first_blocks = gather_rest(first_far)
    second_far = gather_far(second_pair)

    step_rows = PER_STEP * length
    block = (step_rows, width)
    pairs = width // (2 * HEAD_DIM)
    steps = images // PER_STEP
    statics = (images, dp_size, spread)
    wide = scratch(width // 128, total, 128)
    probs_block = (PER_STEP, pairs, length, 2 * length)
    attention_outs = [
        ((total, 3 * width), low, (step_rows, 3 * width)),
        ((images, *probs_block[1:]), low, probs_block),
        ((total, width), low, block),
        ((total, width), high, block),
        ((total, width), low, block),
    ]
    attention_flops = (2 * total * width * 4 * width + 8 * total * length * width) // steps
    attention_scratches = [scratch(length, images)]
    *attention, x, w_qkv, w_proj, qkv_t, proj_t = call_kernel(
        first_attention_kernel, statics, 1,
        ["place"] + [None] * 7,
        attention_outs
        + [
            ((total, width), low, None),
            ((width, 3 * width), low, None),
            ((width, width), low, None),
            ((3 * width, width), low, None),
            ((width, width), low, None),
        ],
        [scratch(dp_size * spread, rows, first_cols, dtype=low), wide] + attention_scratches,
        (place, inputs, *first_blocks, keep_mask, vectors),
        attention_flops, vmem=all_vmem_bytes,
    )
    second_joined = join(second_far, attention[:1])
    attention = call_kernel(
        next_attention_kernel, (PER_STEP,), steps - 1,
        [block] + [None] * 4 + ["await"] * len(attention),
        attention_outs, attention_scratches,
        (x, keep_mask, w_qkv, w_proj, vectors, *attention),
        attention_flops * (steps - 1), first_step=1,
        aliases={5 + at: at for at in range(len(attention))}, vmem=all_vmem_bytes,
    )
    qkv, probs, attended, middle, normed = attention
    second_blocks = gather_rest(second_joined, middle)
    piece = ((slots * images, width), low, None)
    ff_rows = FF_PER_STEP * length
    ff_block = (ff_rows, width)
    results = call_kernel(
        feed_forward_packed_kernel, statics, images // FF_PER_STEP,
        ["place"] + [None] * 5 + [ff_block, ff_block] + [None] * 2,
        [piece] * spread
        + [
            ((total, width), high, ff_block),
            ((total, width), low, ff_block),
            ((half, rows, second_cols), low, None),
            ((half, rows, second_cols), low, None),
            ((width, width), high, None),
            ((8, width), high, None),
            ((1, hidden), high, None),
        ],
        [
            scratch(width, hidden, dtype=low),
            scratch(hidden, width, dtype=low),
            scratch(hidden, width, dtype=low),
            scratch(dp_size * spread, rows, second_cols, dtype=low),
            scratch(1, hidden),
            wide,
            scratch(ff_rows, width, dtype=low),
            scratch(width, ff_rows, dtype=low),
            scratch(ff_rows, width, dtype=low),
            scratch(width, ff_rows, dtype=low),
            scratch(ff_rows, width),
            scratch(ff_rows, 128),
            scratch(ff_rows, width),
            scratch(ff_rows, width),
            scratch(hidden, width, dtype=low),
            scratch(width, hidden, dtype=low),
            scratch(width, hidden),
            scratch(width, hidden),
        ],
        (
            place, upstream, *second_blocks, middle, attended, proj_t, vectors,
        ),
        12 * total * width * hidden + 4 * total * width * width, total * hidden, vmem=all_vmem_bytes,
    )
    d_middle, d_attended, ff_keep, ff_leave, proj_total, ff_sums, up_sums = results[spread:]

    ff_first = permute(ff_leave, core_bits[0])
    ff_count = half // 2
    ff_next = add_wide(ff_keep[ff_count:], ff_first[ff_count:]).astype(low)
    ff_arrived = permute(ff_next, across_x)
    output_parts = exchange(results[:spread])
    pack_half = ((half, rows, first_cols), low, None)
    wide_rows = (step_rows, 3 * width)
    d_projected, qkv_keep, qkv_leave, att_sums = call_kernel(
        attention_back_packed_kernel, (dp_size, spread), steps,
        ["place", block, wide_rows, probs_block, block, None, None, "await"],
        [((total, 3 * width), low, wide_rows), pack_half, pack_half, ((8, width), high, None)],
        [scratch(width, 3 * width)],
        (place, normed, qkv, probs, d_attended, vectors, proj_total, ff_next),
        2 * total * width * 3 * width + 16 * total * length * width,
    )
    qkv_arrived = permute(after(qkv_leave, output_parts[1:] + [ff_arrived]), core_bits[0])
    input_flops = 2 * total * width * 3 * width
    input_ins = [block, wide_rows, block, None, None, None]
    input_outs = [((total, width), low, block), ((8, width), high, None)]
    d_input, att_sums = call_kernel(
        first_input_kernel, (length,), 1, input_ins, input_outs, [scratch(step_rows, width)],
        (x, d_projected, d_middle, qkv_t, vectors, att_sums), input_flops // steps,
    )
    ff_quarter = half // 4
    ff_last = add_wide(
        ff_keep[ff_quarter:ff_count], ff_first[ff_quarter:ff_count], ff_arrived[ff_quarter:]
    ).astype(low)
    ff_last_arrived = permute(ff_last, across_y)
    qkv_held = add_wide(qkv_keep, qkv_arrived)
    leaving = [
        qkv_held[at : at + ff_quarter].astype(low) for at in range(ff_quarter, half, ff_quarter)
    ]
    qkv_held = qkv_held[:ff_quarter]
    qkv_parts = [permute(part, mask) for part, mask in zip(leaving, direct_masks(near_bits))]
    d_input, att_sums = call_kernel(
        first_input_kernel, (length,), 1, input_ins + ["await"] * 2, input_outs, [scratch(step_rows, width)],
        (x, d_projected, d_middle, qkv_t, vectors, att_sums, d_input, leaving[0]), input_flops // steps,
        first_step=1, aliases={6: 0},
    )
    ff_held = add_wide(
        ff_keep[:ff_quarter], ff_first[:ff_quarter], ff_arrived[:ff_quarter], ff_last_arrived
    )
    qkv_held = add_wide(qkv_held, *qkv_parts)
    blocks = jnp.concatenate([ff_held, qkv_held], axis=2)
    far_leaving = [blocks[at : at + 1].astype(low) for at in range(1, blocks.shape[0])]
    block_parts = [blocks[:1]] + [permute(part, mask) for part, mask in zip(far_leaving, direct_masks(far_bits))]
    results = call_kernel(
        last_input_kernel, (images, spread, length, 2 * PER_STEP), steps - 2,
        ["place"] + input_ins + [None, "await"],
        [piece] * spread + [((8, width), high, None)],
        [wide, scratch(step_rows, width)],
        (place, x, d_projected, d_middle, qkv_t, vectors, att_sums, d_input, far_leaving[0]), input_flops // steps * (steps - 2),
        first_step=2,
    )
    att_sums = results[spread]
    input_pieces = list(results[:spread])
    heights = [master.shape[0] * dp_size for master in masters]
    widths = [master.shape[1] * spread for master in masters]
    rows_old, cols_old = [qkv_rows, proj_rows, up_rows, down_rows], [qkv_cols, proj_cols, up_cols, down_cols]

    def like(*arrays):
        return [jax.ShapeDtypeStruct(array.shape, high) for array in arrays]

    operands = (*block_parts, att_sums, ff_sums, up_sums, *masters, *rows_old)
    *grads, row_sums, message = small(
        functools.partial(gradient_kernel, len(block_parts)),
        out_shape=like(*masters) + [jax.ShapeDtypeStruct((8, rows), high), jax.ShapeDtypeStruct((24, width), high)],
    )(*operands)
    input_pieces[1] = after(input_pieces[1], [row_sums])
    output_parts[0] = after(output_parts[0], [row_sums])
    block_output, settled = settle(output_parts)
    input_grad, input_settled = settle(exchange(input_pieces))
    message = added([message] + [permute(message, mask) for mask in direct_masks((across_x, far_bits[0]))])
    for bit in far_bits[1:-1]:
        message = message + permute(message, bit)
    messages = [message, permute(message, far_bits[-1])]
    col_sums, message = small(
        column_kernel,
        in_specs=[in_vmem] * (1 + len(messages)) + [anywhere],
        out_shape=[
            jax.ShapeDtypeStruct((8, width), high),
            jax.ShapeDtypeStruct((16 + width // 8, 128), high),
        ],
    )(row_sums, *messages, settled)
    messages = [message] + [permute(message, mask) for mask in range(1, spread)]
    operands = (*messages, col_sums, vectors, vector_moment, *grads, *masters, *rows_old, *cols_old)
    results = small(
        functools.partial(update_kernel, len(messages), heights, widths),
        in_specs=[in_vmem] * len(operands) + [anywhere],
        out_shape=like(*masters, *cols_old, *rows_old, vectors, vectors, vectors),
    )(*operands, input_settled)
    news, cols_new, rows_out = results[:4], results[4:8], results[8:12]
    vector_grad, vector_moment_new, vector_new = results[12:]
    factored = []
    for which in range(4):
        factored += [grads[which], rows_out[which], cols_new[which], news[which]]
    return (block_output, input_grad, *factored, vector_grad, vector_moment_new, vector_new)


def body(*arrays):
    spread, dp_size = lax.axis_size("group"), lax.axis_size("dp")
    rows, images = arrays[3].shape[0], arrays[1].shape[0]
    slots, width = arrays[0].shape[1:]
    folds = arrays[6].shape[0] // rows
    powers = all(size & (size - 1) == 0 for size in (spread, dp_size))
    fits = powers and spread == 4 and dp_size > 2
    fits = fits and arrays[5].shape[1] <= width and folds <= 5
    fits = fits and rows % 16 == 0 and images % FF_PER_STEP == 0 and images > 2 * PER_STEP and images % 16 == 0 and slots % 4 == 0
    return packed_body(*arrays) if fits else general_body(*arrays)


def solution(mesh):
    in_specs = (
        P("dp", "group", None),
        P(("dp", "group"), None),
        P("dp", "group", None),
        P("dp", "group"),
        P("dp", "group"),
        P("dp", "group"),
        P("dp", "group"),
        P(),
        P("dp"),
        P("group"),
        P("dp"),
        P("group"),
        P("dp"),
        P("group"),
        P("dp"),
        P("group"),
        P(),
    )
    out_specs = (
        P("dp", "group", None),
        P("dp", "group", None),
        P("dp", "group"),
        P("dp"),
        P("group"),
        P("dp", "group"),
        P("dp", "group"),
        P("dp"),
        P("group"),
        P("dp", "group"),
        P("dp", "group"),
        P("dp"),
        P("group"),
        P("dp", "group"),
        P("dp", "group"),
        P("dp"),
        P("group"),
        P("dp", "group"),
        P(),
        P(),
        P(),
    )
    return jax.shard_map(body, mesh=mesh, in_specs=in_specs, out_specs=out_specs, check_vma=False)
```

```python
import functools
import math

import jax
import jax.numpy as jnp
from jax import lax
from jax.experimental import pallas as pl
from jax.experimental.pallas import tpu as pltpu
from jax.sharding import PartitionSpec as P

HEAD_DIM = 64
STEP_NUMBER = 10


step_rate = 0.3
norm_epsilon = 1e-06
tiny_square = 1e-30
decay_rate = 1.0 - STEP_NUMBER ** (-0.8)
LOG2_E = 1.4426950408889634


def axis_bits(name):
    count = lax.axis_size(name)
    return [(name, 1 << place) for place in range(count.bit_length() - 1)]


def swap_partner(array, step):
    name, bit = step
    count = lax.axis_size(name)
    return lax.ppermute(array, name, [(rank, rank ^ bit) for rank in range(count)])


def upper_side(step):
    name, bit = step
    return (lax.axis_index(name) & bit) != 0


def gather_blocks(array, steps):
    for step in steps:
        arrived = swap_partner(array, step)
        upper = upper_side(step)
        array = jnp.stack([jnp.where(upper, arrived, array), jnp.where(upper, array, arrived)])
    return array


def scatter_sum(array, steps):
    for step in steps:
        upper = upper_side(step)
        leaving = jnp.where(upper, array[0], array[1]).astype(jnp.bfloat16)
        arrived = swap_partner(leaving, step)
        array = jnp.where(upper, array[1], array[0]).astype(jnp.float32) + arrived.astype(jnp.float32)
    return array


def sum_everywhere(array, steps):
    for step in steps:
        array = array + swap_partner(array, step)
    return array


def sum_parts(parts, steps):
    flat = [part.reshape(-1) for part in parts]
    total = sum_everywhere(jnp.concatenate(flat), steps)
    result, start = [], 0
    for part in parts:
        result.append(total[start : start + part.size].reshape(part.shape))
        start += part.size
    return result


def block_order(steps):
    order = []
    for name in ("dp", "group"):
        bits = sorted((step for step in steps if step[0] == name), key=lambda step: -step[1])
        order.append([steps.index(step) for step in bits])
    return order


def blocks_to_whole(blocks, steps):
    count = len(steps)
    rows, cols = blocks.shape[count:]
    dp_axes, group_axes = block_order(steps)
    dp_axes = [count - 1 - axis for axis in dp_axes]
    group_axes = [count - 1 - axis for axis in group_axes]
    whole = blocks.transpose(dp_axes + [count] + group_axes + [count + 1])
    return whole.reshape(rows << len(dp_axes), cols << len(group_axes))


def whole_to_blocks(whole, steps):
    dp_axes, group_axes = block_order(steps)
    rows = whole.shape[0] >> len(dp_axes)
    cols = whole.shape[1] >> len(group_axes)
    split = whole.reshape([2] * len(dp_axes) + [rows] + [2] * len(group_axes) + [cols])
    places = dp_axes + [len(steps)] + group_axes + [len(steps) + 1]
    return split.transpose([places.index(axis) for axis in range(len(places))])


PER_STEP = 4
FF_PER_STEP = 4
SLICE = 48
FF_CHUNK = 256
vmem_bytes = 60 * 1024 * 1024


def dot(left, right, left_axis=1, right_axis=0):
    return lax.dot_general(
        left, right, (((left_axis,), (right_axis,)), ((), ())), preferred_element_type=jnp.float32
    )


def normal_form(values):
    center = jnp.mean(values, axis=-1, keepdims=True)
    centered = values - center
    spread = jnp.mean(centered * centered, axis=-1, keepdims=True)
    scale = lax.rsqrt(spread + norm_epsilon)
    return centered * scale, scale


def norm_back(grad, unit, scale, gain):
    weighted = grad * gain
    along = jnp.mean(weighted * unit, axis=-1, keepdims=True)
    level = jnp.mean(weighted, axis=-1, keepdims=True)
    return scale * (weighted - level - unit * along)


def slices_of(count):
    return [slice(start, start + SLICE) for start in range(0, count, SLICE)]


def fold_rows(values):
    return jnp.sum(values.reshape(values.shape[0] // 8, 8, values.shape[1]), axis=0)


def column_sum(values):
    return jnp.sum(values, axis=0, keepdims=True)


def pair_mask(length):
    return lax.broadcasted_iota(jnp.int32, (length, 2 * HEAD_DIM), 1) < HEAD_DIM


def lane_tiles(count):
    return [slice(start, min(start + 128, count)) for start in range(0, count, 128)]


def stack_heads(pair, first):
    none = jnp.zeros_like(pair)
    return jnp.concatenate([jnp.where(first, pair, none), jnp.where(first, none, pair)], axis=0)


def join_heads(rows, first):
    length = rows.shape[0] // 2
    return jnp.where(first, rows[:length], rows[length:])


def gelu_and_slope(pre):
    bell = jnp.exp2(pre * pre * (-0.5 * LOG2_E))
    base = 1.0 + (0.3275911 * 0.5**0.5) * jnp.abs(pre)
    inverse = pl.reciprocal(base, approx=True)
    inverse = inverse * (2.0 - base * inverse)
    poly = inverse * (
        0.5 * 0.254829592
        + inverse
        * (
            0.5 * -0.284496736
            + inverse
            * (0.5 * 1.421413741 + inverse * (0.5 * -1.453152027 + inverse * (0.5 * 1.061405429)))
        )
    )
    tail = poly * bell
    below = jnp.where(pre >= 0, 1.0 - tail, tail)
    return pre * below, below + pre * bell * 0.3989422804014327


def widen(source_ref, wide_ref, images):
    tiles, total, lanes = wide_ref.shape
    rows_at_once = 8 * images

    @pl.loop(0, total // rows_at_once)
    def _(part):
        rows = pl.ds(pl.multiple_of(part * rows_at_once, rows_at_once), rows_at_once)
        for tile in range(tiles):
            cols = slice(tile * lanes, (tile + 1) * lanes)
            wide_ref[tile, rows, :] = source_ref[rows, cols].astype(jnp.float32)


def narrow(wide_ref, target_ref, images):
    tiles, total, lanes = wide_ref.shape
    rows_at_once = 8 * images

    @pl.loop(0, total // rows_at_once)
    def _(part):
        rows = pl.ds(pl.multiple_of(part * rows_at_once, rows_at_once), rows_at_once)
        for tile in range(tiles):
            cols = slice(tile * lanes, (tile + 1) * lanes)
            target_ref[rows, cols] = wide_ref[tile, rows, :].astype(target_ref.dtype)


def take_image(wide_ref, image, images):
    tiles, total, _ = wide_ref.shape
    rows = pl.ds(image, total // images, images)
    return jnp.concatenate([wide_ref[tile, rows, :] for tile in range(tiles)], axis=1)


def put_image(wide_ref, image, images, values):
    tiles, total, lanes = wide_ref.shape
    rows = pl.ds(image, total // images, images)
    for tile in range(tiles):
        wide_ref[tile, rows, :] = values[:, tile * lanes : (tile + 1) * lanes]


def attention_kernel(
    images, tokens_ref, bias_ref, w_qkv_ref, w_proj_ref, vectors_ref,
    x_ref, qkv_ref, probs_ref, attended_ref, middle_ref, wide_ref, normed_ref,
):
    @pl.when(pl.program_id(0) == 0)
    def _():
        widen(tokens_ref, wide_ref, images)
        to_image_rows(wide_ref, x_ref, images)

    attention_steps(
        x_ref, lambda image: bias_ref[image], w_qkv_ref, w_proj_ref, vectors_ref,
        qkv_ref, probs_ref, attended_ref, middle_ref, normed_ref,
    )


def to_image_rows(wide_ref, x_ref, images):
    length = wide_ref.shape[1] // images

    @pl.loop(0, images)
    def _(image):
        rows = pl.ds(pl.multiple_of(image * length, length), length)
        x_ref[rows, :] = take_image(wide_ref, image, images).astype(jnp.bfloat16)


def attention_steps(
    x_ref, bias_column, w_qkv_ref, w_proj_ref, vectors_ref,
    qkv_ref, probs_ref, attended_ref, middle_ref, normed_ref,
):
    per_step, _, length, _ = probs_ref.shape
    step_rows, width = middle_ref.shape
    base = 0 if x_ref.shape[0] == step_rows else pl.program_id(0) * step_rows

    for rows in slices_of(step_rows):
        x = x_ref[pl.ds(pl.multiple_of(base + rows.start, SLICE), SLICE), :].astype(jnp.float32)
        unit, _ = normal_form(x)
        normed_ref[rows, :] = (unit * vectors_ref[0:1] + vectors_ref[1:2]).astype(jnp.bfloat16)
    shift = jnp.concatenate(
        [vectors_ref[2:3], jnp.zeros((1, width), jnp.float32), vectors_ref[3:4]], axis=1
    )
    for start in range(0, 3 * width, 512):
        cols = slice(start, min(start + 512, 3 * width))
        projected = dot(normed_ref[...], w_qkv_ref[:, cols]) + shift[:, cols]
        qkv_ref[:, cols] = projected.astype(jnp.bfloat16)

    pairs = width // (2 * HEAD_DIM)
    first = pair_mask(length)
    place = lax.broadcasted_iota(jnp.int32, (length, 2 * length), 0)
    asker = lax.broadcasted_iota(jnp.int32, (length, 2 * length), 1)
    own = place == jnp.where(asker >= length, asker - length, asker)

    def scores_of(image):
        rows = slice(image * length, (image + 1) * length)
        result = []
        for pair in range(pairs):
            low = pair * 2 * HEAD_DIM
            queries = stack_heads(qkv_ref[rows, low : low + 2 * HEAD_DIM], first)
            result.append(dot(qkv_ref[rows, width + low : width + low + 2 * HEAD_DIM], queries, 1, 1))
        return result

    next_scores = scores_of(0)
    for image in range(per_step):
        rows = slice(image * length, (image + 1) * length)
        all_scores = next_scores
        if image + 1 < per_step:
            next_scores = scores_of(image + 1)
        column = bias_column(image)
        for cols in lane_tiles(2 * length):
            bias = jnp.where(own[:, cols], 0.0, column)
            for pair in range(pairs):
                scores = all_scores[pair][:, cols] * (HEAD_DIM**-0.5 * LOG2_E) + bias
                weights = jnp.exp2(scores - jnp.max(scores, axis=0, keepdims=True))
                probs = weights * (1.0 / jnp.sum(weights, axis=0, keepdims=True))
                probs_ref[image, pair, :, cols] = probs.astype(jnp.bfloat16)
        for pair in range(pairs):
            low = pair * 2 * HEAD_DIM
            values = qkv_ref[rows, 2 * width + low : 2 * width + low + 2 * HEAD_DIM]
            attended = join_heads(dot(probs_ref[image, pair], values, 0, 0), first)
            attended_ref[rows, low : low + 2 * HEAD_DIM] = attended.astype(jnp.bfloat16)

    middle_ref[...] = (
        x_ref[pl.ds(pl.multiple_of(base, length), step_rows), :].astype(jnp.float32)
        + dot(attended_ref[...], w_proj_ref[...])
        + vectors_ref[4:5]
    )


def feed_forward_kernel(
    images, middle_ref, cotangent_ref, attended_ref, w_up_ref, w_down_ref, proj_t_ref, vectors_ref, bias_up_ref,
    output_ref, d_middle_ref, d_attended_ref, up_grad_ref, down_grad_ref, proj_grad_ref, vector_sums_ref, up_sums_ref,
    wide_ref, *scratches,
):
    up_total_ref, down_total_ref, proj_total_ref = scratches[-3:]

    @pl.when(pl.program_id(0) == 0)
    def _():
        widen(cotangent_ref, wide_ref, images)

    feed_forward_steps(
        images, middle_ref, attended_ref, w_up_ref, w_down_ref, proj_t_ref, vectors_ref, bias_up_ref,
        d_middle_ref, d_attended_ref, vector_sums_ref, up_sums_ref, wide_ref, *scratches,
    )

    @pl.when(pl.program_id(0) == pl.num_programs(0) - 1)
    def _():
        narrow(wide_ref, output_ref, images)
        up_grad_ref[...] = up_total_ref[...].astype(jnp.bfloat16)
        down_grad_ref[...] = down_total_ref[...].T.astype(jnp.bfloat16)
        proj_grad_ref[...] = proj_total_ref[...].astype(jnp.bfloat16)


def feed_forward_steps(
    images, middle_ref, attended_ref, w_up_ref, w_down_ref, proj_t_ref, vectors_ref, bias_up_ref,
    d_middle_ref, d_attended_ref, vector_sums_ref, up_sums_ref,
    wide_ref, normed_ref, normed_t_ref, dy_ref, dy_t_ref, unit_ref, scale_ref, ahead_ref, back_ref,
    up_t_ref, down_t_ref, up_total_ref, down_total_ref, proj_total_ref,
):
    step = pl.program_id(0)
    length = wide_ref.shape[1] // images
    hidden = w_up_ref.shape[1]
    per_step = middle_ref.shape[0] // length

    @pl.when(step == 0)
    def _():
        for total in (up_total_ref, down_total_ref, proj_total_ref, vector_sums_ref, up_sums_ref):
            total[...] = jnp.zeros_like(total)
        up_t_ref[...] = w_up_ref[...].T
        down_t_ref[...] = w_down_ref[...].T

    for image in range(per_step):
        rows = slice(image * length, (image + 1) * length)
        dy = take_image(wide_ref, step * per_step + image, images)
        dy_ref[rows, :] = dy.astype(jnp.bfloat16)
        vector_sums_ref[3:4] += column_sum(dy)
        unit, scale = normal_form(middle_ref[rows, :])
        unit_ref[rows, :] = unit
        scale_ref[rows, :] = jnp.broadcast_to(scale, (length, scale_ref.shape[1]))
        normed_ref[rows, :] = (unit * vectors_ref[5:6] + vectors_ref[6:7]).astype(jnp.bfloat16)
    normed_t_ref[...] = normed_ref[...].T
    dy_t_ref[...] = dy_ref[...].T
    chunks = hidden // FF_CHUNK

    def cols_of(chunk):
        return slice(chunk * FF_CHUNK, (chunk + 1) * FF_CHUNK)

    def into(chunk):
        cols = cols_of(chunk)
        pre = dot(normed_ref[...], w_up_ref[:, cols])
        return pre + bias_up_ref[:, cols], dot(dy_ref[...], down_t_ref[:, cols])

    def across(pre, d_active):
        active, slope = gelu_and_slope(pre)
        return active.astype(jnp.bfloat16), (d_active * slope).astype(jnp.bfloat16)

    def out_of(chunk, active, d_hidden):
        cols = cols_of(chunk)
        ahead, back = dot(active, w_down_ref[cols, :]), dot(d_hidden, up_t_ref[cols, :])
        if chunk == 0:
            ahead_ref[...] = ahead
            back_ref[...] = back
        else:
            ahead_ref[...] += ahead
            back_ref[...] += back
        down_total_ref[:, cols] += dot(dy_t_ref[...], active)
        up_total_ref[:, cols] += dot(normed_t_ref[...], d_hidden)
        up_sums_ref[:, cols] += column_sum(d_hidden.astype(jnp.float32))

    entered, crossed = into(0), None
    for chunk in range(chunks + 1):
        next_entered = into(chunk + 1) if chunk + 1 < chunks else None
        next_crossed = across(*entered) if chunk < chunks else None
        if crossed is not None:
            out_of(chunk - 1, *crossed)
        entered, crossed = next_entered, next_crossed

    for image in range(per_step):
        rows = slice(image * length, (image + 1) * length)
        output = middle_ref[rows, :] + ahead_ref[rows, :] + vectors_ref[11:12]
        put_image(wide_ref, step * per_step + image, images, output)
        unit = unit_ref[rows, :]
        grad = back_ref[rows, :]
        vector_sums_ref[1:2] += column_sum(grad * unit)
        vector_sums_ref[2:3] += column_sum(grad)
        d_middle = dy_ref[rows, :].astype(jnp.float32) + norm_back(
            grad, unit, scale_ref[rows, 0:1], vectors_ref[5:6]
        )
        d_middle_ref[rows, :] = d_middle
        d_branch = d_middle.astype(jnp.bfloat16)
        dy_ref[rows, :] = d_branch
        vector_sums_ref[0:1] += column_sum(d_branch.astype(jnp.float32))
    proj_total_ref[...] += dot(attended_ref[...], dy_ref[...], 0, 0)
    d_attended_ref[...] = dot(dy_ref[...], proj_t_ref[...]).astype(jnp.bfloat16)


def attention_back_kernel(
    images, x_ref, qkv_ref, probs_ref, d_attended_ref, d_middle_ref, qkv_t_ref, vectors_ref,
    input_grad_ref, qkv_grad_ref, vector_sums_ref, wide_ref, normed_ref, d_projected_ref, back_ref, qkv_total_ref,
):
    @pl.when(pl.program_id(0) == 0)
    def _():
        qkv_total_ref[...] = jnp.zeros_like(qkv_total_ref)
        vector_sums_ref[...] = jnp.zeros_like(vector_sums_ref)

    def put(image, rows, values):
        put_image(wide_ref, image, images, values)

    attention_back_steps(
        x_ref, qkv_ref, probs_ref, d_attended_ref, vectors_ref, vector_sums_ref, normed_ref, d_projected_ref, qkv_total_ref
    )
    input_back_steps(
        put, probs_ref.shape[2], x_ref, d_projected_ref, d_middle_ref, qkv_t_ref, vectors_ref, vector_sums_ref, back_ref
    )

    @pl.when(pl.program_id(0) == pl.num_programs(0) - 1)
    def _():
        narrow(wide_ref, input_grad_ref, images)
        qkv_grad_ref[...] = qkv_total_ref[...].astype(jnp.bfloat16)


def attention_back_steps(
    x_ref, qkv_ref, probs_ref, d_attended_ref, vectors_ref, vector_sums_ref, normed_ref, d_projected_ref, qkv_total_ref
):
    width = d_attended_ref.shape[1]
    length = probs_ref.shape[2]
    per_step = probs_ref.shape[0]

    pairs = width // (2 * HEAD_DIM)
    first = pair_mask(length)
    scale = HEAD_DIM**-0.5

    def places(image, pair):
        low = pair * 2 * HEAD_DIM
        rows = slice(image * length, (image + 1) * length)
        return rows, [slice(part * width + low, part * width + low + 2 * HEAD_DIM) for part in range(3)]

    def entering(image):
        result = []
        for pair in range(pairs):
            rows, cols = places(image, pair)
            d_attended = stack_heads(d_attended_ref[rows, cols[0]], first)
            d_values = dot(probs_ref[image, pair], d_attended)
            d_projected_ref[rows, cols[2]] = d_values.astype(jnp.bfloat16)
            result.append(dot(qkv_ref[rows, cols[2]], d_attended, 1, 1))
        return result

    next_probs = entering(0)
    for image in range(per_step):
        all_d_probs = next_probs
        if image + 1 < per_step:
            next_probs = entering(image + 1)
        all_d_scores = []
        for pair in range(pairs):
            parts = []
            for cols in lane_tiles(2 * length):
                probs, d_probs = probs_ref[image, pair, :, cols].astype(jnp.float32), all_d_probs[pair][:, cols]
                along = jnp.sum(d_probs * probs, axis=0, keepdims=True)
                parts.append((probs * (d_probs - along)).astype(jnp.bfloat16))
            all_d_scores.append(jnp.concatenate(parts, axis=1))
        for pair in range(pairs):
            rows, cols = places(image, pair)
            d_scores = all_d_scores[pair]
            queries = stack_heads(qkv_ref[rows, cols[0]], first)
            d_queries = join_heads(dot(d_scores, qkv_ref[rows, cols[1]], 0, 0), first) * scale
            d_projected_ref[rows, cols[0]] = d_queries.astype(jnp.bfloat16)
            d_projected_ref[rows, cols[1]] = (dot(d_scores, queries) * scale).astype(jnp.bfloat16)

    query_sums = value_sums = jnp.zeros((8, width), jnp.float32)
    for rows in slices_of(d_attended_ref.shape[0]):
        query_sums += fold_rows(d_projected_ref[rows, :width].astype(jnp.float32))
        value_sums += fold_rows(d_projected_ref[rows, 2 * width :].astype(jnp.float32))
        if x_ref is not None:
            unit, _ = normal_form(x_ref[rows, :].astype(jnp.float32))
            normed_ref[rows, :] = (unit * vectors_ref[0:1] + vectors_ref[1:2]).astype(jnp.bfloat16)
    vector_sums_ref[2:3] += column_sum(query_sums)
    vector_sums_ref[3:4] += column_sum(value_sums)
    qkv_total_ref[...] += dot(normed_ref[...], d_projected_ref[...], 0, 0)


def input_back_steps(
    put, length, x_ref, d_projected_ref, d_middle_ref, qkv_t_ref, vectors_ref, vector_sums_ref, back_ref
):
    step = pl.program_id(0)
    per_step = x_ref.shape[0] // length
    back_ref[...] = dot(d_projected_ref[...], qkv_t_ref[...])
    gain_sums = shift_sums = jnp.zeros((8, x_ref.shape[1]), jnp.float32)
    for rows in slices_of(x_ref.shape[0]):
        unit, scale = normal_form(x_ref[rows, :].astype(jnp.float32))
        grad = back_ref[rows, :]
        gain_sums += fold_rows(grad * unit)
        shift_sums += fold_rows(grad)
        back_ref[rows, :] = d_middle_ref[rows, :] + norm_back(grad, unit, scale, vectors_ref[0:1])
    vector_sums_ref[0:1] += column_sum(gain_sums)
    vector_sums_ref[1:2] += column_sum(shift_sums)
    for image in range(per_step):
        rows = slice(image * length, (image + 1) * length)
        put(step * per_step + image, rows, back_ref[rows, :])


def whole_block(shape):
    return pl.BlockSpec(shape, lambda step: (0,) * len(shape))


def step_block(shape, first=0):
    return pl.BlockSpec(shape, lambda step: (first + step,) + (0,) * (len(shape) - 1))


def scratch(*shape, dtype=jnp.float32):
    return pltpu.VMEM(shape, dtype)


def call_kernel(kernel, statics, steps, ins, outs, scratches, operands, flops, transcendentals=0, first_step=0, aliases={}):
    in_specs = [
        pl.BlockSpec(memory_space=pltpu.SMEM)
        if block == "place"
        else pl.BlockSpec(memory_space=pl.ANY)
        if block == "await"
        else whole_block(op.shape) if block is None else step_block(block, first_step)
        for op, block in zip(operands, ins)
    ]
    out_specs = [
        whole_block(shape) if block is None else step_block(block, first_step) for shape, dtype, block in outs
    ]
    moved = sum(op.size * op.dtype.itemsize for op in operands) + sum(
        math.prod(shape) * jnp.dtype(dtype).itemsize for shape, dtype, block in outs
    )
    return pl.pallas_call(
        functools.partial(kernel, *statics),
        grid=(steps,),
        in_specs=in_specs,
        out_specs=out_specs,
        out_shape=[jax.ShapeDtypeStruct(shape, dtype) for shape, dtype, block in outs],
        scratch_shapes=scratches,
        input_output_aliases=aliases,
        compiler_params=pltpu.CompilerParams(vmem_limit_bytes=vmem_bytes),
        cost_estimate=pl.CostEstimate(
            flops=flops * 8, bytes_accessed=moved, transcendentals=transcendentals
        ),
    )(*operands)


def attention_forward(tokens, bias, w_qkv, w_proj, vectors):
    images, length, _ = bias.shape
    total, width = tokens.shape
    pairs = width // (2 * HEAD_DIM)
    rows = PER_STEP * length
    low, high = jnp.bfloat16, jnp.float32
    outs = [
        ((total, width), low, None),
        ((total, 3 * width), low, (rows, 3 * width)),
        ((images, pairs, length, 2 * length), low, (PER_STEP, pairs, length, 2 * length)),
        ((total, width), low, (rows, width)),
        ((total, width), high, (rows, width)),
    ]
    return call_kernel(
        attention_kernel, (images,), images // PER_STEP,
        [None, (PER_STEP, length, 1), None, None, None], outs,
        [scratch(width // 128, total, 128), scratch(rows, width, dtype=low)],
        (tokens, bias, w_qkv, w_proj, vectors),
        2 * total * width * 4 * width + 8 * total * length * width,
    )


def feed_forward(images, middle, cotangent, attended, w_up, w_down, w_proj, vectors):
    total, width = middle.shape
    hidden = w_up.shape[1]
    rows = total // images * FF_PER_STEP
    low, high = jnp.bfloat16, jnp.float32
    block = (rows, width)
    outs = [
        ((total, width), low, None),
        ((total, width), high, block),
        ((total, width), low, block),
        ((width, hidden), low, None),
        ((hidden, width), low, None),
        ((width, width), low, None),
        ((8, width), high, None),
        ((1, hidden), high, None),
    ]
    scratches = [
        scratch(width // 128, total, 128),
        scratch(rows, width, dtype=low),
        scratch(width, rows, dtype=low),
        scratch(rows, width, dtype=low),
        scratch(width, rows, dtype=low),
        scratch(rows, width),
        scratch(rows, 128),
        scratch(rows, width),
        scratch(rows, width),
        scratch(hidden, width, dtype=low),
        scratch(width, hidden, dtype=low),
        scratch(width, hidden),
        scratch(width, hidden),
        scratch(width, width),
    ]
    return call_kernel(
        feed_forward_kernel, (images,), images // FF_PER_STEP,
        [block, None, block, None, None, None, None, None], outs, scratches,
        (middle, cotangent, attended, w_up, w_down, w_proj.T, vectors, vectors[7:11].reshape(1, hidden)),
        12 * total * width * hidden + 4 * total * width * width, total * hidden,
    )


def attention_back(x, qkv, probs, d_attended, d_middle, w_qkv, vectors):
    images, pairs, length, _ = probs.shape
    total, width = x.shape
    rows = PER_STEP * length
    low, high = jnp.bfloat16, jnp.float32
    block = (rows, width)
    outs = [
        ((total, width), low, None),
        ((width, 3 * width), low, None),
        ((8, width), high, None),
    ]
    scratches = [
        scratch(width // 128, total, 128),
        scratch(rows, width, dtype=low),
        scratch(rows, 3 * width, dtype=low),
        scratch(rows, width),
        scratch(width, 3 * width),
    ]
    return call_kernel(
        attention_back_kernel, (images,), images // PER_STEP,
        [block, (rows, 3 * width), (PER_STEP, pairs, length, 2 * length), block, block, None, None],
        outs, scratches, (x, qkv, probs, d_attended, d_middle, w_qkv.T, vectors),
        4 * total * width * 3 * width + 16 * total * length * width,
    )

def linear_place():
    return lax.axis_index("dp") * lax.axis_size("group") + lax.axis_index("group")


def permute(array, mask):
    count = lax.axis_size("dp") * lax.axis_size("group")
    return lax.ppermute(array, ("dp", "group"), [(rank, rank ^ mask) for rank in range(count)])


def direct_masks(bits):
    masks = [0]
    for bit in bits:
        masks = masks + [mask | bit for mask in masks]
    return masks[1:]


def add_wide(first, *rest):
    total = first.astype(jnp.float32)
    for part in rest:
        total = total + part.astype(jnp.float32)
    return total


def packed_place(mask, spread, count):
    return ((mask >> 1) & (spread - 1)) * (count // (2 * spread)) + (mask >> (spread.bit_length()))


def scatter_step(held, bits):
    masks = direct_masks(bits)
    size = held.shape[0] // (len(masks) + 1)
    parts = [
        permute(held[size * (at + 1) : size * (at + 2)].astype(jnp.bfloat16), mask)
        for at, mask in enumerate(masks)
    ]
    return held[:size], parts


def add_wide(first, *rest):
    total = first.astype(jnp.float32)
    for part in rest:
        total = total + part.astype(jnp.float32)
    return total


def packed_place(mask, spread, count):
    return ((mask >> 1) & (spread - 1)) * (count // (2 * spread)) + (mask >> (spread.bit_length()))


def gather_step(held, bits):
    return held + [permute(part, mask) for mask in direct_masks(bits) for part in held]


def gathered_place(mask, count):
    return (mask & 1) * (count // 2) + ((mask >> 2) & 1) * (count // 4) + (mask >> 3) * 2 + ((mask >> 1) & 1)


def unpack(place_ref, block_refs, packed_ref, put, dp_size, spread):
    place = place_ref[0]
    size = block_refs[0].shape[0]
    for at, block_ref in enumerate(block_refs):
        packed_ref[at * size : (at + 1) * size] = block_ref[...]
    count = dp_size * spread
    for row in range(dp_size):
        for col in range(spread):
            put(row, col, packed_ref[gathered_place((row * spread + col) ^ place, count)])


def unpack_in_order(blocks_ref, put, dp_size, spread):
    for row in range(dp_size):
        for col in range(spread):
            put(row, col, blocks_ref[row * spread + col])


def pack(place_ref, take, keep_ref, leave_ref, dp_size, spread):
    place = place_ref[0]
    odd = (place & 1) == 1
    for row in range(dp_size):
        for col in range(0, spread, 2):
            at = packed_place((row * spread + col) ^ place, spread, dp_size * spread)
            even_block, odd_block = take(row, col), take(row, col + 1)
            keep_ref[at] = jnp.where(odd, odd_block, even_block)
            leave_ref[at] = jnp.where(odd, even_block, odd_block)


def narrow_pieces(place_ref, wide_ref, piece_refs, spread):
    tiles, _, lanes = wide_ref.shape
    rows_of_piece = piece_refs[0].shape[0]
    step = 64
    group = place_ref[0] & (spread - 1)
    for relative, piece_ref in enumerate(piece_refs):
        base = (group ^ relative) * rows_of_piece

        @pl.loop(0, rows_of_piece // step)
        def _(part):
            target = pl.ds(pl.multiple_of(part * step, step), step)
            source = pl.ds(pl.multiple_of(base + part * step, step), step)
            for tile in range(tiles):
                cols = slice(tile * lanes, (tile + 1) * lanes)
                piece_ref[target, cols] = wide_ref[tile, source, :].astype(jnp.bfloat16)


def general_body(
    tokens,
    keep_mask,
    cotangent,
    qkv_weight,
    proj_weight,
    up_weight,
    down_weight,
    vectors,
    qkv_rows,
    qkv_cols,
    proj_rows,
    proj_cols,
    up_rows,
    up_cols,
    down_rows,
    down_cols,
    vector_moment,
):
    masters = (qkv_weight, proj_weight, up_weight, down_weight)
    lowered = tuple((master.astype(jnp.bfloat16) for master in masters))
    dp_bits, group_bits = axis_bits("dp"), axis_bits("group")
    gather_steps = dp_bits[1:] + group_bits[1:] + dp_bits[:1] + group_bits[:1]
    scatter_steps = gather_steps[::-1]
    w_qkv, w_proj, w_up, w_down = tuple(
        blocks_to_whole(gather_blocks(part, gather_steps), gather_steps) for part in lowered
    )
    spread = lax.axis_size("group")

    def slots_in(array):
        held, slots, width = array.shape
        parts = array.transpose(1, 0, 2).reshape(slots, spread, held // spread, width)
        parts = lax.all_to_all(
            parts.transpose(1, 0, 2, 3), "group", split_axis=0, concat_axis=0, tiled=True
        )
        return parts.reshape(spread * slots * (held // spread), width)

    def slots_out(array):
        held, slots, width = tokens.shape
        parts = array.reshape(spread, slots, held // spread, width)
        parts = lax.all_to_all(parts, "group", split_axis=0, concat_axis=0, tiled=True)
        return parts.transpose(1, 0, 2, 3).reshape(slots, held, width).transpose(1, 0, 2)

    images = keep_mask.shape[0]
    bias = jnp.where(keep_mask > 0, 0.0, -1e30)[:, :, None]
    x, qkv, probs, attended, middle = attention_forward(
        slots_in(tokens), bias, w_qkv, w_proj, vectors
    )
    output, d_middle, d_attended, up_grad, down_grad, proj_grad, ff_sums, up_sums = feed_forward(
        images, middle, slots_in(cotangent), attended, w_up, w_down, w_proj, vectors
    )
    block_output = slots_out(output)
    d_input, qkv_grad, att_sums = attention_back(
        x, qkv, probs, d_attended, d_middle, w_qkv, vectors
    )
    input_grad = slots_out(d_input)
    local_vectors = jnp.concatenate(
        [att_sums[:4], ff_sums[:3], up_sums.reshape(4, -1), ff_sums[3:4]], axis=0
    )
    vector_grad = sum_everywhere(local_vectors, group_bits + dp_bits)
    local_grads = (qkv_grad, proj_grad, up_grad, down_grad)
    owned = tuple(
        scatter_sum(whole_to_blocks(part, scatter_steps), scatter_steps) for part in local_grads
    )
    squares = tuple((gradient * gradient + tiny_square for gradient in owned))
    row_parts = tuple((jnp.sum(square, axis=1) for square in squares)) + tuple(
        (jnp.sum(master * master, axis=1) for master in masters)
    )
    row_sums = sum_parts(row_parts, group_bits)
    rows_old = (qkv_rows, proj_rows, up_rows, down_rows)
    cols_old = (qkv_cols, proj_cols, up_cols, down_cols)
    total_cols = tuple((gradient.shape[1] * lax.axis_size("group") for gradient in owned))
    total_rows = tuple((gradient.shape[0] * lax.axis_size("dp") for gradient in owned))
    rows_new = tuple(
        (
            decay_rate * rows_old[which] + (1.0 - decay_rate) * row_sums[which] / total_cols[which]
            for which in range(4)
        )
    )
    col_parts = (
        tuple((jnp.sum(square, axis=0) for square in squares))
        + tuple((jnp.sum(row_stat) for row_stat in rows_new))
        + tuple((jnp.sum(row_sums[4 + which]) for which in range(4)))
    )
    col_sums = sum_parts(col_parts, dp_bits)
    results = []
    for which in range(4):
        cols_new = (
            decay_rate * cols_old[which] + (1.0 - decay_rate) * col_sums[which] / total_rows[which]
        )
        mean_rows = col_sums[4 + which] / total_rows[which]
        spread = jnp.sqrt(col_sums[8 + which] / (total_rows[which] * total_cols[which]))
        second = rows_new[which][:, None] * cols_new[None, :] / mean_rows
        updated = masters[which] - step_rate * spread * owned[which] * lax.rsqrt(second)
        results.append((owned[which], rows_new[which], cols_new, updated))
    vector_moment_new = decay_rate * vector_moment + (1.0 - decay_rate) * (
        vector_grad * vector_grad + tiny_square
    )
    row_spread = jnp.sqrt(jnp.mean(vectors * vectors, axis=1, keepdims=True))
    vector_new = vectors - step_rate * row_spread * vector_grad * lax.rsqrt(vector_moment_new)
    return (
        block_output,
        input_grad,
        results[0][0],
        results[0][1],
        results[0][2],
        results[0][3],
        results[1][0],
        results[1][1],
        results[1][2],
        results[1][3],
        results[2][0],
        results[2][1],
        results[2][2],
        results[2][3],
        results[3][0],
        results[3][1],
        results[3][2],
        results[3][3],
        vector_grad,
        vector_moment_new,
        vector_new,
    )


def first_attention_kernel(images, dp_size, spread, place_ref, tokens_ref, *refs):
    blocks, refs = refs[:4], refs[4:]
    keep_ref, vectors_ref, *outs, x_ref, w_qkv_ref, w_proj_ref, qkv_t_ref, proj_t_ref = refs[:-3]
    packed_ref, wide_ref, bias_ref = refs[-3:]
    rows = packed_ref.shape[1]
    qkv_cols, proj_cols = w_qkv_ref.shape[1] // spread, w_proj_ref.shape[1] // spread

    @pl.when(pl.program_id(0) == 0)
    def _():
        widen(tokens_ref, wide_ref, images)
        to_image_rows(wide_ref, x_ref, images)

        def put(row, col, block):
            down = slice(row * rows, (row + 1) * rows)
            w_qkv_ref[down, col * qkv_cols : (col + 1) * qkv_cols] = block[:, :qkv_cols]
            w_proj_ref[down, col * proj_cols : (col + 1) * proj_cols] = block[:, qkv_cols:]

        unpack(place_ref, blocks, packed_ref, put, dp_size, spread)
        qkv_t_ref[...] = w_qkv_ref[...].T
        proj_t_ref[...] = w_proj_ref[...].T

    attention_part(0, x_ref, keep_ref, w_qkv_ref, w_proj_ref, vectors_ref, *outs, bias_ref)


def next_attention_kernel(start, x_ref, keep_ref, w_qkv_ref, w_proj_ref, vectors_ref, *refs):
    attention_part(start, x_ref, keep_ref, w_qkv_ref, w_proj_ref, vectors_ref, *refs[-6:])


def attention_part(
    start, x_ref, keep_ref, w_qkv_ref, w_proj_ref, vectors_ref,
    qkv_ref, probs_ref, attended_ref, middle_ref, normed_ref, bias_ref,
):
    @pl.when(pl.program_id(0) == 0)
    def _():
        bias_ref[...] = jnp.where(keep_ref[...] > 0, 0.0, -1e30).T

    def bias_column(image):
        here = start + pl.program_id(0) * probs_ref.shape[0] + image
        lane = lax.broadcasted_iota(jnp.int32, bias_ref.shape, 1)
        return row_sum(jnp.where(lane == here, bias_ref[...], 0.0))

    attention_steps(
        x_ref, bias_column, w_qkv_ref, w_proj_ref, vectors_ref,
        qkv_ref, probs_ref, attended_ref, middle_ref, normed_ref,
    )


def feed_forward_packed_kernel(images, dp_size, spread, place_ref, *refs):
    cotangent_ref, blocks, refs = refs[0], refs[1:5], refs[5:]
    middle_ref, attended_ref, proj_t_ref, vectors_ref = refs[:4]
    outputs, refs = refs[4 : 4 + spread], refs[4 + spread :]
    d_middle_ref, d_attended_ref, keep_ref, leave_ref, proj_total_ref, vector_sums_ref, up_sums_ref = refs[:7]
    w_up_ref, w_down_ref, packed_ref, bias_up_ref, wide_ref = refs[7:12]
    scratches = refs[12:]
    width = w_up_ref.shape[0]
    up_total_ref, down_total_ref = scratches[-2:]
    rows = packed_ref.shape[1]
    up_cols = w_up_ref.shape[1] // spread
    out_cols = w_down_ref.shape[1] // spread
    folds = w_down_ref.shape[0] // w_up_ref.shape[0]

    @pl.when(pl.program_id(0) == 0)
    def _():
        widen(cotangent_ref, wide_ref, images)
        for fold in range(bias_up_ref.shape[1] // width):
            bias_up_ref[:, fold * width : (fold + 1) * width] = vectors_ref[7 + fold : 8 + fold]

        def put(row, col, block):
            w_up_ref[row * rows : (row + 1) * rows, col * up_cols : (col + 1) * up_cols] = block[:, :up_cols]
            for fold in range(folds):
                down = (row * folds + fold) * rows
                start = up_cols + fold * out_cols
                w_down_ref[down : down + rows, col * out_cols : (col + 1) * out_cols] = block[
                    :, start : start + out_cols
                ]

        unpack(place_ref, blocks, packed_ref, put, dp_size, spread)

    feed_forward_steps(
        images, middle_ref, attended_ref, w_up_ref, w_down_ref, proj_t_ref, vectors_ref, bias_up_ref,
        d_middle_ref, d_attended_ref, vector_sums_ref, up_sums_ref, wide_ref, *scratches, proj_total_ref,
    )

    @pl.when(pl.program_id(0) == pl.num_programs(0) - 1)
    def _():
        narrow_pieces(place_ref, wide_ref, outputs, spread)

        def take(row, col):
            across = slice(row * rows, (row + 1) * rows)
            parts = [up_total_ref[across, col * up_cols : (col + 1) * up_cols].astype(jnp.bfloat16)]
            lanes = slice(row * folds * rows, (row + 1) * folds * rows)
            for start in range(col * out_cols, (col + 1) * out_cols, rows):
                parts.append(down_total_ref[start : start + rows, lanes].astype(jnp.bfloat16))
            return jnp.concatenate(parts, axis=1)

        pack(place_ref, take, keep_ref, leave_ref, dp_size, spread)


def attention_back_packed_kernel(
    dp_size, spread, place_ref, normed_ref, qkv_ref, probs_ref, d_attended_ref, vectors_ref, proj_total_ref, _,
    d_projected_ref, keep_ref, leave_ref, vector_sums_ref, total_ref,
):
    @pl.when(pl.program_id(0) == 0)
    def _():
        total_ref[...] = jnp.zeros_like(total_ref)
        vector_sums_ref[...] = jnp.zeros_like(vector_sums_ref)

    attention_back_steps(
        None, qkv_ref, probs_ref, d_attended_ref, vectors_ref, vector_sums_ref, normed_ref, d_projected_ref, total_ref
    )

    @pl.when(pl.program_id(0) == pl.num_programs(0) - 1)
    def _():
        rows = keep_ref.shape[1]
        qkv_cols, proj_cols = total_ref.shape[1] // spread, proj_total_ref.shape[1] // spread

        def take(row, col):
            down = slice(row * rows, (row + 1) * rows)
            parts = [
                total_ref[down, col * qkv_cols : (col + 1) * qkv_cols],
                proj_total_ref[down, col * proj_cols : (col + 1) * proj_cols],
            ]
            return jnp.concatenate(parts, axis=1).astype(jnp.bfloat16)

        pack(place_ref, take, keep_ref, leave_ref, dp_size, spread)


def first_input_kernel(
    length, x_ref, d_projected_ref, d_middle_ref, qkv_t_ref, vectors_ref, before_ref, *refs
):
    d_input_ref, vector_sums_ref, back_ref = refs[-3:]

    @pl.when(pl.program_id(0) == 0)
    def _():
        vector_sums_ref[...] = before_ref[...]

    def put(image, rows, values):
        d_input_ref[rows, :] = values.astype(jnp.bfloat16)

    input_back_steps(
        put, length, x_ref, d_projected_ref, d_middle_ref, qkv_t_ref, vectors_ref, vector_sums_ref, back_ref
    )


def last_input_kernel(
    images, spread, length, first, place_ref, x_ref, d_projected_ref, d_middle_ref, qkv_t_ref, vectors_ref, before_ref,
    d_input_ref, _, *refs,
):
    pieces, (vector_sums_ref, wide_ref, back_ref) = refs[:spread], refs[spread:]

    @pl.when(pl.program_id(0) == 0)
    def _():
        vector_sums_ref[...] = before_ref[...]
        for image in range(first):
            rows = slice(image * length, (image + 1) * length)
            put_image(wide_ref, image, images, d_input_ref[rows, :].astype(jnp.float32))

    def put(image, rows, values):
        put_image(wide_ref, first + image, images, values)

    input_back_steps(
        put, length, x_ref, d_projected_ref, d_middle_ref, qkv_t_ref, vectors_ref, vector_sums_ref, back_ref
    )

    @pl.when(pl.program_id(0) == pl.num_programs(0) - 1)
    def _():
        narrow_pieces(place_ref, wide_ref, pieces, spread)


def cut(array_ref, parts_ref):
    count = parts_ref.shape[2]
    for member in range(parts_ref.shape[0]):
        parts_ref[member] = array_ref[:, member * count : (member + 1) * count, :]


def pack_kernel(qkv_ref, proj_ref, up_ref, down_ref, pack_ref):
    rows, start = pack_ref.shape[0], 0
    parts = [qkv_ref[...], proj_ref[...], up_ref[...]]
    parts += [down_ref[fold * rows : (fold + 1) * rows, :] for fold in range(down_ref.shape[0] // rows)]
    for part in parts:
        pack_ref[:, start : start + part.shape[1]] = part.astype(jnp.bfloat16)
        start += part.shape[1]


def token_kernel(array_ref, own_ref, arrived_ref, _, parts_ref, first_ref, second_ref):
    start = first_ref.shape[2]
    for at, pack_ref in enumerate((own_ref, arrived_ref)):
        first_ref[at] = pack_ref[:, :start]
        second_ref[at] = pack_ref[:, start:]
    cut(array_ref, parts_ref)


def join_kernel(count, *refs):
    size = refs[0].shape[0]
    for at, part_ref in enumerate(refs[:count]):
        refs[-1][at * size : (at + 1) * size] = part_ref[...]


def settle_kernel(spread, place_ref, *refs):
    lists, (output_ref, token_ref) = refs[:-2], refs[-2:]
    token_ref[...] = jnp.zeros_like(token_ref)
    group = place_ref[0] & (spread - 1)
    count = lists[0].shape[1]
    share = len(lists) // spread * count
    for at, piece_ref in enumerate(lists):
        relative, part = at % spread, at // spread
        start = pl.multiple_of((group ^ relative) * share + part * count, count)
        output_ref[:, pl.ds(start, count), :] = piece_ref[...]


def lane_table(rows, columns):
    lane = lax.broadcasted_iota(jnp.int32, (rows, 128), 1)
    table = jnp.zeros((rows, 128), jnp.float32)
    for at, column in enumerate(columns):
        table = jnp.where(lane == at, column, table)
    return table


def added(parts):
    while len(parts) > 1:
        parts = [sum(parts[at : at + 2][1:], parts[at]) for at in range(0, len(parts), 2)]
    return parts[0]


def row_sum(values):
    return jnp.sum(values, axis=1, keepdims=True)


def after_kernel(*refs):
    pass


def gradient_kernel(count, *refs):
    block_parts, sums, refs = refs[:count], refs[count : count + 3], refs[count + 3 :]
    masters, rows_old, refs = refs[:4], refs[4:8], refs[8:]
    grads, (row_ref, message_ref) = refs[:4], refs[4:]
    blocks = added([part[0].astype(jnp.float32) for part in block_parts])
    rows, up_cols = grads[2].shape
    qkv_cols, out_cols = grads[0].shape[1], grads[1].shape[1]
    folds = grads[3].shape[0] // rows
    up = blocks[:, :up_cols]
    turned = [
        blocks[:, up_cols + part * folds * rows : up_cols + (part + 1) * folds * rows]
        for part in range(out_cols // rows)
    ]
    down = jnp.concatenate(turned, axis=0).T
    downs = [down[fold * rows : (fold + 1) * rows] for fold in range(folds)]
    start = up_cols + folds * out_cols
    qkv = blocks[:, start : start + qkv_cols]
    proj = blocks[:, start + qkv_cols :]
    grads[0][...] = qkv
    grads[1][...] = proj
    grads[2][...] = up
    for fold in range(folds):
        grads[3][fold * rows : (fold + 1) * rows, :] = downs[fold]
    squares = [part * part + tiny_square for part in (qkv, proj, up, *downs)]
    row_ref[...] = lane_table(rows, [row_sum(square) for square in squares]).T[: row_ref.shape[0], :]
    width = message_ref.shape[1]
    message_ref[...] = jnp.zeros_like(message_ref)
    for at, square in enumerate((*squares[:3], added(squares[3:]))):
        message_ref[at : at + 1, : square.shape[1]] = column_sum(square)
    scalars = [column_sum(row_sum(master[...] * master[...])) for master in masters]
    scalars += [row_sum(part[...].reshape(1, part.shape[0])) for part in rows_old]
    message_ref[4:5, :128] = lane_table(1, scalars)
    att_ref, ff_ref, up_ref = sums
    count = up_ref.shape[1] // width
    message_ref[8:12, :] = att_ref[:4]
    message_ref[12:15, :] = ff_ref[:3]
    for at in range(count):
        message_ref[15 + at : 16 + at, :] = up_ref[:, at * width : (at + 1) * width]
    message_ref[15 + count : 16 + count, :] = ff_ref[3:4]


def column_kernel(row_ref, *refs):
    parts, (cols_ref, message_ref) = refs[:-3], refs[-2:]
    total = added([part[...] for part in parts])
    cols_ref[...] = total[:8]
    width = total.shape[1]
    rows = row_ref.shape[1]
    message_ref[...] = jnp.zeros_like(message_ref)
    message_ref[:8, :rows] = row_ref[...]
    columns = [row_sum(total[which : which + 1]) for which in range(4)]
    squares = [total[4:5, which : which + 1] for which in range(4)]
    message_ref[8:9, :] = lane_table(1, columns + squares)
    for tile in range(width // 128):
        message_ref[16 * (tile + 1) : 16 * (tile + 2), :] = total[8:, tile * 128 : (tile + 1) * 128]


def update_kernel(count, heights, widths, *refs):
    messages, refs = refs[:count], refs[count:]
    cols_ref, vectors_ref, moment_ref, refs = refs[0], refs[1], refs[2], refs[3:]
    grads, masters, rows_old, cols_old, refs = refs[:4], refs[4:8], refs[8:12], refs[12:16], refs[17:]
    news, cols_new, rows_out, refs = refs[:4], refs[4:8], refs[8:12], refs[12:]
    vector_grad_ref, moment_new_ref, vector_new_ref = refs
    sums = added([message[...] for message in messages])
    height = grads[0].shape[0]
    folds = grads[3].shape[0] // height
    lanes = [[0], [1], [2], list(range(3, 3 + folds))]
    share = 1.0 - decay_rate
    for which in range(4):
        entries = heights[which] * widths[which]
        cols = cols_old[which].shape[0]
        new = decay_rate * cols_old[which][...].reshape(1, cols) + share / heights[which] * cols_ref[
            which : which + 1, :cols
        ]
        cols_new[which][...] = new[0]
        old_total = cols_ref[4:5, 4 + which : 5 + which]
        mean_rows = (decay_rate * old_total + share / widths[which] * sums[8:9, which : which + 1]) / heights[which]
        rate = step_rate * jnp.sqrt(sums[8:9, 4 + which : 5 + which] / entries)
        across = new / mean_rows
        old = rows_old[which][...].reshape(1, len(lanes[which]) * height)
        row_sums = jnp.concatenate([sums[lane : lane + 1, :height] for lane in lanes[which]], axis=1)
        row = decay_rate * old + share / widths[which] * row_sums
        rows_out[which][...] = row[0]
        for fold in range(len(lanes[which])):
            part = slice(fold * height, (fold + 1) * height)
            column = jnp.broadcast_to(row[:, part], (8, height)).T[:, :1]
            news[which][part, :] = masters[which][part, :] - rate * grads[which][part, :] * lax.rsqrt(column * across)
    vectors = vectors_ref[...]
    count = vectors.shape[0]
    gradient = jnp.concatenate(
        [sums[16 * (tile + 1) : 16 * (tile + 1) + count] for tile in range(vectors.shape[1] // 128)], axis=1
    )
    vector_grad_ref[...] = gradient
    moment = decay_rate * moment_ref[...] + share * (gradient * gradient + tiny_square)
    moment_new_ref[...] = moment
    spread = jnp.sqrt(jnp.mean(vectors * vectors, axis=1, keepdims=True))
    vector_new_ref[...] = vectors - step_rate * spread * gradient * lax.rsqrt(moment)


def packed_body(
    tokens, keep_mask, cotangent, qkv_weight, proj_weight, up_weight, down_weight, vectors,
    qkv_rows, qkv_cols, proj_rows, proj_cols, up_rows, up_cols, down_rows, down_cols, vector_moment,
):
    spread, dp_size = lax.axis_size("group"), lax.axis_size("dp")
    low, high = jnp.bfloat16, jnp.float32
    place = linear_place().astype(jnp.int32).reshape(1)
    group = lax.axis_index("group")
    held, slots, width = tokens.shape
    images, length = keep_mask.shape
    hidden = up_weight.shape[1] * spread
    total = images * length
    rows = qkv_weight.shape[0]
    folds = down_weight.shape[0] // rows
    core_bits = (1,)
    near_bits = tuple(1 << at for at in range(1, spread.bit_length()))
    far_bits = tuple(spread << at for at in range(1, dp_size.bit_length() - 1))
    half = spread * dp_size // 2

    anywhere = pl.BlockSpec(memory_space=pl.ANY)
    in_smem = pl.BlockSpec(memory_space=pltpu.SMEM)

    in_vmem = pl.BlockSpec(memory_space=pltpu.VMEM)
    small = functools.partial(
        pl.pallas_call, compiler_params=pltpu.CompilerParams(vmem_limit_bytes=vmem_bytes)
    )
    masters = (qkv_weight, proj_weight, up_weight, down_weight)
    parted = jax.ShapeDtypeStruct((spread, slots, images, width), low)

    def after(array, awaited):
        return small(
            after_kernel,
            in_specs=[anywhere] * (1 + len(awaited)),
            out_specs=anywhere,
            out_shape=jax.ShapeDtypeStruct(array.shape, array.dtype),
            input_output_aliases={0: 0},
        )(array, *awaited)

    def to_group(parts):
        return lax.all_to_all(parts, "group", split_axis=0, concat_axis=0, tiled=True)

    def to_images(parts):
        return to_group(parts).reshape(total, width)

    def exchange(parts):
        return [parts[0]] + [permute(part, relative) for relative, part in enumerate(parts) if relative]

    def settle(parts):
        parts = [part.reshape(slots, -1, width) for part in parts]
        whole, token = small(
            functools.partial(settle_kernel, spread),
            in_specs=[in_smem] + [in_vmem] * len(parts),
            out_specs=[in_vmem] * 2,
            out_shape=[
                jax.ShapeDtypeStruct((slots, held, width), low),
                jax.ShapeDtypeStruct((8, 128), high),
            ],
        )(place, *parts)
        return whole.transpose(1, 0, 2), token

    first_cols = qkv_weight.shape[1] + proj_weight.shape[1]
    second_cols = up_weight.shape[1] + folds * down_weight.shape[1]
    pack_own = small(pack_kernel, out_shape=jax.ShapeDtypeStruct((rows, first_cols + second_cols), low))(*masters)
    across_y, across_x = near_bits
    pack_arrived = permute(pack_own, across_y)
    cotangent_cut = small(cut, out_shape=parted)(cotangent.transpose(1, 0, 2))
    token_cut, first_pair, second_pair = small(
        token_kernel,
        in_specs=[in_vmem] * 3 + [anywhere],
        out_shape=[
            parted,
            jax.ShapeDtypeStruct((2, rows, first_cols), low),
            jax.ShapeDtypeStruct((2, rows, second_cols), low),
        ],
    )(tokens.transpose(1, 0, 2), pack_own, pack_arrived, cotangent_cut)
    inputs = to_images(token_cut)

    def gather_far(pair):
        return [pair] + [permute(pair, mask) for mask in direct_masks(far_bits)]

    def join(parts, awaited=()):
        count = len(parts) * parts[0].shape[0]
        return small(
            functools.partial(join_kernel, len(parts)),
            in_specs=[in_vmem] * len(parts) + [anywhere] * len(awaited),
            out_shape=jax.ShapeDtypeStruct((count, *parts[0].shape[1:]), low),
        )(*parts, *awaited)

    def gather_rest(held, awaited=None):
        arrived = permute(held, across_x)
        leaving = [held, arrived]
        if awaited is not None:
            leaving = [after(part, [awaited]) for part in leaving]
        return leaving + [permute(part, core_bits[0]) for part in leaving]

    first_far = join(gather_far(first_pair))
    upstream = to_images(cotangent_cut)
    first_blocks = gather_rest(first_far)
    second_far = gather_far(second_pair)

    step_rows = PER_STEP * length
    block = (step_rows, width)
    pairs = width // (2 * HEAD_DIM)
    steps = images // PER_STEP
    statics = (images, dp_size, spread)
    wide = scratch(width // 128, total, 128)
    probs_block = (PER_STEP, pairs, length, 2 * length)
    attention_outs = [
        ((total, 3 * width), low, (step_rows, 3 * width)),
        ((images, *probs_block[1:]), low, probs_block),
        ((total, width), low, block),
        ((total, width), high, block),
        ((total, width), low, block),
    ]
    attention_flops = (2 * total * width * 4 * width + 8 * total * length * width) // steps
    attention_scratches = [scratch(length, images)]
    *attention, x, w_qkv, w_proj, qkv_t, proj_t = call_kernel(
        first_attention_kernel, statics, 1,
        ["place"] + [None] * 7,
        attention_outs
        + [
            ((total, width), low, None),
            ((width, 3 * width), low, None),
            ((width, width), low, None),
            ((3 * width, width), low, None),
            ((width, width), low, None),
        ],
        [scratch(dp_size * spread, rows, first_cols, dtype=low), wide] + attention_scratches,
        (place, inputs, *first_blocks, keep_mask, vectors),
        attention_flops,
    )
    second_joined = join(second_far, attention[:1])
    attention = call_kernel(
        next_attention_kernel, (PER_STEP,), steps - 1,
        [block] + [None] * 4 + ["await"] * len(attention),
        attention_outs, attention_scratches,
        (x, keep_mask, w_qkv, w_proj, vectors, *attention),
        attention_flops * (steps - 1), first_step=1,
        aliases={5 + at: at for at in range(len(attention))},
    )
    qkv, probs, attended, middle, normed = attention
    second_blocks = gather_rest(second_joined, middle)
    piece = ((slots * images, width), low, None)
    ff_rows = FF_PER_STEP * length
    ff_block = (ff_rows, width)
    results = call_kernel(
        feed_forward_packed_kernel, statics, images // FF_PER_STEP,
        ["place"] + [None] * 5 + [ff_block, ff_block] + [None] * 2,
        [piece] * spread
        + [
            ((total, width), high, ff_block),
            ((total, width), low, ff_block),
            ((half, rows, second_cols), low, None),
            ((half, rows, second_cols), low, None),
            ((width, width), high, None),
            ((8, width), high, None),
            ((1, hidden), high, None),
        ],
        [
            scratch(width, hidden, dtype=low),
            scratch(hidden, width, dtype=low),
            scratch(dp_size * spread, rows, second_cols, dtype=low),
            scratch(1, hidden),
            wide,
            scratch(ff_rows, width, dtype=low),
            scratch(width, ff_rows, dtype=low),
            scratch(ff_rows, width, dtype=low),
            scratch(width, ff_rows, dtype=low),
            scratch(ff_rows, width),
            scratch(ff_rows, 128),
            scratch(ff_rows, width),
            scratch(ff_rows, width),
            scratch(hidden, width, dtype=low),
            scratch(width, hidden, dtype=low),
            scratch(width, hidden),
            scratch(width, hidden),
        ],
        (
            place, upstream, *second_blocks, middle, attended, proj_t, vectors,
        ),
        12 * total * width * hidden + 4 * total * width * width, total * hidden,
    )
    d_middle, d_attended, ff_keep, ff_leave, proj_total, ff_sums, up_sums = results[spread:]

    ff_first = permute(ff_leave, core_bits[0])
    ff_count = half // 2
    ff_next = add_wide(ff_keep[ff_count:], ff_first[ff_count:]).astype(low)
    ff_arrived = permute(ff_next, across_x)
    output_parts = exchange(results[:spread])
    pack_half = ((half, rows, first_cols), low, None)
    wide_rows = (step_rows, 3 * width)
    d_projected, qkv_keep, qkv_leave, att_sums = call_kernel(
        attention_back_packed_kernel, (dp_size, spread), steps,
        ["place", block, wide_rows, probs_block, block, None, None, "await"],
        [((total, 3 * width), low, wide_rows), pack_half, pack_half, ((8, width), high, None)],
        [scratch(width, 3 * width)],
        (place, normed, qkv, probs, d_attended, vectors, proj_total, ff_next),
        2 * total * width * 3 * width + 16 * total * length * width,
    )
    qkv_arrived = permute(after(qkv_leave, output_parts[1:] + [ff_arrived]), core_bits[0])
    input_flops = 2 * total * width * 3 * width
    input_ins = [block, wide_rows, block, None, None, None]
    input_outs = [((total, width), low, block), ((8, width), high, None)]
    d_input, att_sums = call_kernel(
        first_input_kernel, (length,), 1, input_ins, input_outs, [scratch(step_rows, width)],
        (x, d_projected, d_middle, qkv_t, vectors, att_sums), input_flops // steps,
    )
    ff_quarter = half // 4
    ff_last = add_wide(
        ff_keep[ff_quarter:ff_count], ff_first[ff_quarter:ff_count], ff_arrived[ff_quarter:]
    ).astype(low)
    ff_last_arrived = permute(ff_last, across_y)
    qkv_held = add_wide(qkv_keep, qkv_arrived)
    leaving = [
        qkv_held[at : at + ff_quarter].astype(low) for at in range(ff_quarter, half, ff_quarter)
    ]
    qkv_held = qkv_held[:ff_quarter]
    qkv_parts = [permute(part, mask) for part, mask in zip(leaving, direct_masks(near_bits))]
    d_input, att_sums = call_kernel(
        first_input_kernel, (length,), 1, input_ins + ["await"] * 2, input_outs, [scratch(step_rows, width)],
        (x, d_projected, d_middle, qkv_t, vectors, att_sums, d_input, leaving[0]), input_flops // steps,
        first_step=1, aliases={6: 0},
    )
    ff_held = add_wide(
        ff_keep[:ff_quarter], ff_first[:ff_quarter], ff_arrived[:ff_quarter], ff_last_arrived
    )
    qkv_held = add_wide(qkv_held, *qkv_parts)
    blocks = jnp.concatenate([ff_held, qkv_held], axis=2)
    far_leaving = [blocks[at : at + 1].astype(low) for at in range(1, blocks.shape[0])]
    block_parts = [blocks[:1]] + [permute(part, mask) for part, mask in zip(far_leaving, direct_masks(far_bits))]
    results = call_kernel(
        last_input_kernel, (images, spread, length, 2 * PER_STEP), steps - 2,
        ["place"] + input_ins + [None, "await"],
        [piece] * spread + [((8, width), high, None)],
        [wide, scratch(step_rows, width)],
        (place, x, d_projected, d_middle, qkv_t, vectors, att_sums, d_input, far_leaving[0]), input_flops // steps * (steps - 2),
        first_step=2,
    )
    att_sums = results[spread]
    input_pieces = list(results[:spread])
    heights = [master.shape[0] * dp_size for master in masters]
    widths = [master.shape[1] * spread for master in masters]
    rows_old, cols_old = [qkv_rows, proj_rows, up_rows, down_rows], [qkv_cols, proj_cols, up_cols, down_cols]

    def like(*arrays):
        return [jax.ShapeDtypeStruct(array.shape, high) for array in arrays]

    operands = (*block_parts, att_sums, ff_sums, up_sums, *masters, *rows_old)
    *grads, row_sums, message = small(
        functools.partial(gradient_kernel, len(block_parts)),
        out_shape=like(*masters) + [jax.ShapeDtypeStruct((8, rows), high), jax.ShapeDtypeStruct((24, width), high)],
    )(*operands)
    input_pieces[1] = after(input_pieces[1], [row_sums])
    output_parts[0] = after(output_parts[0], [row_sums])
    block_output, settled = settle(output_parts)
    input_grad, input_settled = settle(exchange(input_pieces))
    message = added([message] + [permute(message, mask) for mask in direct_masks((across_x, far_bits[0]))])
    for bit in far_bits[1:-1]:
        message = message + permute(message, bit)
    messages = [message, permute(message, far_bits[-1])]
    col_sums, message = small(
        column_kernel,
        in_specs=[in_vmem] * (1 + len(messages)) + [anywhere],
        out_shape=[
            jax.ShapeDtypeStruct((8, width), high),
            jax.ShapeDtypeStruct((16 + width // 8, 128), high),
        ],
    )(row_sums, *messages, settled)
    messages = [message] + [permute(message, mask) for mask in range(1, spread)]
    operands = (*messages, col_sums, vectors, vector_moment, *grads, *masters, *rows_old, *cols_old)
    results = small(
        functools.partial(update_kernel, len(messages), heights, widths),
        in_specs=[in_vmem] * len(operands) + [anywhere],
        out_shape=like(*masters, *cols_old, *rows_old, vectors, vectors, vectors),
    )(*operands, input_settled)
    news, cols_new, rows_out = results[:4], results[4:8], results[8:12]
    vector_grad, vector_moment_new, vector_new = results[12:]
    factored = []
    for which in range(4):
        factored += [grads[which], rows_out[which], cols_new[which], news[which]]
    return (block_output, input_grad, *factored, vector_grad, vector_moment_new, vector_new)


def body(*arrays):
    spread, dp_size = lax.axis_size("group"), lax.axis_size("dp")
    rows, images = arrays[3].shape[0], arrays[1].shape[0]
    slots, width = arrays[0].shape[1:]
    folds = arrays[6].shape[0] // rows
    powers = all(size & (size - 1) == 0 for size in (spread, dp_size))
    fits = powers and spread == 4 and dp_size > 2
    fits = fits and arrays[5].shape[1] <= width and folds <= 5
    fits = fits and arrays[6].shape[1] % rows == 0 and rows % 16 == 0 and images % FF_PER_STEP == 0 and images > 2 * PER_STEP and images % 16 == 0 and slots % 4 == 0
    return packed_body(*arrays) if fits else general_body(*arrays)


def solution(mesh):
    in_specs = (
        P("dp", "group", None),
        P(("dp", "group"), None),
        P("dp", "group", None),
        P("dp", "group"),
        P("dp", "group"),
        P("dp", "group"),
        P("dp", "group"),
        P(),
        P("dp"),
        P("group"),
        P("dp"),
        P("group"),
        P("dp"),
        P("group"),
        P("dp"),
        P("group"),
        P(),
    )
    out_specs = (
        P("dp", "group", None),
        P("dp", "group", None),
        P("dp", "group"),
        P("dp"),
        P("group"),
        P("dp", "group"),
        P("dp", "group"),
        P("dp"),
        P("group"),
        P("dp", "group"),
        P("dp", "group"),
        P("dp"),
        P("group"),
        P("dp", "group"),
        P("dp", "group"),
        P("dp"),
        P("group"),
        P("dp", "group"),
        P(),
        P(),
        P(),
    )
    return jax.shard_map(body, mesh=mesh, in_specs=in_specs, out_specs=out_specs, check_vma=False)
```

```python
import functools
import math

import jax
import jax.numpy as jnp
from jax import lax
from jax.experimental import pallas as pl
from jax.experimental.pallas import tpu as pltpu
from jax.sharding import PartitionSpec as P

HEAD_DIM = 64
STEP_NUMBER = 10


step_rate = 0.3
norm_epsilon = 1e-06
tiny_square = 1e-30
decay_rate = 1.0 - STEP_NUMBER ** (-0.8)
LOG2_E = 1.4426950408889634


def axis_bits(name):
    count = lax.axis_size(name)
    return [(name, 1 << place) for place in range(count.bit_length() - 1)]


def swap_partner(array, step):
    name, bit = step
    count = lax.axis_size(name)
    return lax.ppermute(array, name, [(rank, rank ^ bit) for rank in range(count)])


def upper_side(step):
    name, bit = step
    return (lax.axis_index(name) & bit) != 0


def gather_blocks(array, steps):
    for step in steps:
        arrived = swap_partner(array, step)
        upper = upper_side(step)
        array = jnp.stack([jnp.where(upper, arrived, array), jnp.where(upper, array, arrived)])
    return array


def scatter_sum(array, steps):
    for step in steps:
        upper = upper_side(step)
        leaving = jnp.where(upper, array[0], array[1]).astype(jnp.bfloat16)
        arrived = swap_partner(leaving, step)
        array = jnp.where(upper, array[1], array[0]).astype(jnp.float32) + arrived.astype(jnp.float32)
    return array


def sum_everywhere(array, steps):
    for step in steps:
        array = array + swap_partner(array, step)
    return array


def sum_parts(parts, steps):
    flat = [part.reshape(-1) for part in parts]
    total = sum_everywhere(jnp.concatenate(flat), steps)
    result, start = [], 0
    for part in parts:
        result.append(total[start : start + part.size].reshape(part.shape))
        start += part.size
    return result


def block_order(steps):
    order = []
    for name in ("dp", "group"):
        bits = sorted((step for step in steps if step[0] == name), key=lambda step: -step[1])
        order.append([steps.index(step) for step in bits])
    return order


def blocks_to_whole(blocks, steps):
    count = len(steps)
    rows, cols = blocks.shape[count:]
    dp_axes, group_axes = block_order(steps)
    dp_axes = [count - 1 - axis for axis in dp_axes]
    group_axes = [count - 1 - axis for axis in group_axes]
    whole = blocks.transpose(dp_axes + [count] + group_axes + [count + 1])
    return whole.reshape(rows << len(dp_axes), cols << len(group_axes))


def whole_to_blocks(whole, steps):
    dp_axes, group_axes = block_order(steps)
    rows = whole.shape[0] >> len(dp_axes)
    cols = whole.shape[1] >> len(group_axes)
    split = whole.reshape([2] * len(dp_axes) + [rows] + [2] * len(group_axes) + [cols])
    places = dp_axes + [len(steps)] + group_axes + [len(steps) + 1]
    return split.transpose([places.index(axis) for axis in range(len(places))])


PER_STEP = 4
FF_PER_STEP = 4
SLICE = 48
FF_CHUNK = 256
vmem_bytes = 60 * 1024 * 1024
all_vmem_bytes = 64 * 1024 * 1024


def dot(left, right, left_axis=1, right_axis=0):
    return lax.dot_general(
        left, right, (((left_axis,), (right_axis,)), ((), ())), preferred_element_type=jnp.float32
    )


def normal_form(values):
    center = jnp.mean(values, axis=-1, keepdims=True)
    centered = values - center
    spread = jnp.mean(centered * centered, axis=-1, keepdims=True)
    scale = lax.rsqrt(spread + norm_epsilon)
    return centered * scale, scale


def norm_back(grad, unit, scale, gain):
    weighted = grad * gain
    along = jnp.mean(weighted * unit, axis=-1, keepdims=True)
    level = jnp.mean(weighted, axis=-1, keepdims=True)
    return scale * (weighted - level - unit * along)


def slices_of(count):
    return [slice(start, start + SLICE) for start in range(0, count, SLICE)]


def fold_rows(values):
    return jnp.sum(values.reshape(values.shape[0] // 8, 8, values.shape[1]), axis=0)


def column_sum(values):
    return jnp.sum(values, axis=0, keepdims=True)


def pair_mask(length):
    return lax.broadcasted_iota(jnp.int32, (length, 2 * HEAD_DIM), 1) < HEAD_DIM


def lane_tiles(count):
    return [slice(start, min(start + 128, count)) for start in range(0, count, 128)]


def stack_heads(pair, first):
    none = jnp.zeros_like(pair)
    return jnp.concatenate([jnp.where(first, pair, none), jnp.where(first, none, pair)], axis=0)


def join_heads(rows, first):
    length = rows.shape[0] // 2
    return jnp.where(first, rows[:length], rows[length:])


def gelu_and_slope(pre):
    bell = jnp.exp2(pre * pre * (-0.5 * LOG2_E))
    base = 1.0 + (0.3275911 * 0.5**0.5) * jnp.abs(pre)
    inverse = pl.reciprocal(base, approx=True)
    inverse = inverse * (2.0 - base * inverse)
    poly = inverse * (
        0.5 * 0.254829592
        + inverse
        * (
            0.5 * -0.284496736
            + inverse
            * (0.5 * 1.421413741 + inverse * (0.5 * -1.453152027 + inverse * (0.5 * 1.061405429)))
        )
    )
    tail = poly * bell
    below = jnp.where(pre >= 0, 1.0 - tail, tail)
    return pre * below, below + pre * bell * 0.3989422804014327


def widen(source_ref, wide_ref, images):
    tiles, total, lanes = wide_ref.shape
    rows_at_once = 8 * images

    @pl.loop(0, total // rows_at_once)
    def _(part):
        rows = pl.ds(pl.multiple_of(part * rows_at_once, rows_at_once), rows_at_once)
        for tile in range(tiles):
            cols = slice(tile * lanes, (tile + 1) * lanes)
            wide_ref[tile, rows, :] = source_ref[rows, cols].astype(jnp.float32)


def narrow(wide_ref, target_ref, images):
    tiles, total, lanes = wide_ref.shape
    rows_at_once = 8 * images

    @pl.loop(0, total // rows_at_once)
    def _(part):
        rows = pl.ds(pl.multiple_of(part * rows_at_once, rows_at_once), rows_at_once)
        for tile in range(tiles):
            cols = slice(tile * lanes, (tile + 1) * lanes)
            target_ref[rows, cols] = wide_ref[tile, rows, :].astype(target_ref.dtype)


def take_image(wide_ref, image, images):
    tiles, total, _ = wide_ref.shape
    rows = pl.ds(image, total // images, images)
    return jnp.concatenate([wide_ref[tile, rows, :] for tile in range(tiles)], axis=1)


def put_image(wide_ref, image, images, values):
    tiles, total, lanes = wide_ref.shape
    rows = pl.ds(image, total // images, images)
    for tile in range(tiles):
        wide_ref[tile, rows, :] = values[:, tile * lanes : (tile + 1) * lanes]


def attention_kernel(
    images, tokens_ref, bias_ref, w_qkv_ref, w_proj_ref, vectors_ref,
    x_ref, qkv_ref, probs_ref, attended_ref, middle_ref, wide_ref, normed_ref,
):
    @pl.when(pl.program_id(0) == 0)
    def _():
        widen(tokens_ref, wide_ref, images)
        to_image_rows(wide_ref, x_ref, images)

    attention_steps(
        x_ref, lambda image: bias_ref[image], w_qkv_ref, w_proj_ref, vectors_ref,
        qkv_ref, probs_ref, attended_ref, middle_ref, normed_ref,
    )


def to_image_rows(wide_ref, x_ref, images):
    length = wide_ref.shape[1] // images

    @pl.loop(0, images)
    def _(image):
        rows = pl.ds(pl.multiple_of(image * length, length), length)
        x_ref[rows, :] = take_image(wide_ref, image, images).astype(jnp.bfloat16)


def attention_steps(
    x_ref, bias_column, w_qkv_ref, w_proj_ref, vectors_ref,
    qkv_ref, probs_ref, attended_ref, middle_ref, normed_ref,
):
    per_step, _, length, _ = probs_ref.shape
    step_rows, width = middle_ref.shape
    base = 0 if x_ref.shape[0] == step_rows else pl.program_id(0) * step_rows

    for rows in slices_of(step_rows):
        x = x_ref[pl.ds(pl.multiple_of(base + rows.start, SLICE), SLICE), :].astype(jnp.float32)
        unit, _ = normal_form(x)
        normed_ref[rows, :] = (unit * vectors_ref[0:1] + vectors_ref[1:2]).astype(jnp.bfloat16)
    shift = jnp.concatenate(
        [vectors_ref[2:3], jnp.zeros((1, width), jnp.float32), vectors_ref[3:4]], axis=1
    )
    for start in range(0, 3 * width, 512):
        cols = slice(start, min(start + 512, 3 * width))
        projected = dot(normed_ref[...], w_qkv_ref[:, cols]) + shift[:, cols]
        qkv_ref[:, cols] = projected.astype(jnp.bfloat16)

    pairs = width // (2 * HEAD_DIM)
    first = pair_mask(length)
    place = lax.broadcasted_iota(jnp.int32, (length, 2 * length), 0)
    asker = lax.broadcasted_iota(jnp.int32, (length, 2 * length), 1)
    own = place == jnp.where(asker >= length, asker - length, asker)

    def scores_of(image):
        rows = slice(image * length, (image + 1) * length)
        result = []
        for pair in range(pairs):
            low = pair * 2 * HEAD_DIM
            queries = stack_heads(qkv_ref[rows, low : low + 2 * HEAD_DIM], first)
            result.append(dot(qkv_ref[rows, width + low : width + low + 2 * HEAD_DIM], queries, 1, 1))
        return result

    next_scores = scores_of(0)
    for image in range(per_step):
        rows = slice(image * length, (image + 1) * length)
        all_scores = next_scores
        if image + 1 < per_step:
            next_scores = scores_of(image + 1)
        column = bias_column(image)
        for cols in lane_tiles(2 * length):
            bias = jnp.where(own[:, cols], 0.0, column)
            for pair in range(pairs):
                scores = all_scores[pair][:, cols] * (HEAD_DIM**-0.5 * LOG2_E) + bias
                weights = jnp.exp2(scores - jnp.max(scores, axis=0, keepdims=True))
                probs = weights * (1.0 / jnp.sum(weights, axis=0, keepdims=True))
                probs_ref[image, pair, :, cols] = probs.astype(jnp.bfloat16)
        for pair in range(pairs):
            low = pair * 2 * HEAD_DIM
            values = qkv_ref[rows, 2 * width + low : 2 * width + low + 2 * HEAD_DIM]
            attended = join_heads(dot(probs_ref[image, pair], values, 0, 0), first)
            attended_ref[rows, low : low + 2 * HEAD_DIM] = attended.astype(jnp.bfloat16)

    middle_ref[...] = (
        x_ref[pl.ds(pl.multiple_of(base, length), step_rows), :].astype(jnp.float32)
        + dot(attended_ref[...], w_proj_ref[...])
        + vectors_ref[4:5]
    )


def feed_forward_kernel(
    images, middle_ref, cotangent_ref, attended_ref, w_up_ref, w_down_ref, proj_t_ref, vectors_ref, bias_up_ref,
    output_ref, d_middle_ref, d_attended_ref, up_grad_ref, down_grad_ref, proj_grad_ref, vector_sums_ref, up_sums_ref,
    wide_ref, *scratches,
):
    up_total_ref, down_total_ref, proj_total_ref = scratches[-3:]

    @pl.when(pl.program_id(0) == 0)
    def _():
        widen(cotangent_ref, wide_ref, images)

    feed_forward_steps(
        images, middle_ref, attended_ref, w_up_ref, w_down_ref, proj_t_ref, vectors_ref, bias_up_ref,
        d_middle_ref, d_attended_ref, vector_sums_ref, up_sums_ref, wide_ref, *scratches,
    )

    @pl.when(pl.program_id(0) == pl.num_programs(0) - 1)
    def _():
        narrow(wide_ref, output_ref, images)
        up_grad_ref[...] = up_total_ref[...].astype(jnp.bfloat16)
        down_grad_ref[...] = down_total_ref[...].T.astype(jnp.bfloat16)
        proj_grad_ref[...] = proj_total_ref[...].astype(jnp.bfloat16)


def feed_forward_steps(
    images, middle_ref, attended_ref, w_up_ref, w_down_ref, proj_t_ref, vectors_ref, bias_up_ref,
    d_middle_ref, d_attended_ref, vector_sums_ref, up_sums_ref,
    wide_ref, normed_ref, normed_t_ref, dy_ref, dy_t_ref, unit_ref, scale_ref, ahead_ref, back_ref,
    up_t_ref, down_t_ref, up_total_ref, down_total_ref, proj_total_ref,
):
    step = pl.program_id(0)
    length = wide_ref.shape[1] // images
    hidden = w_up_ref.shape[1]
    per_step = middle_ref.shape[0] // length

    @pl.when(step == 0)
    def _():
        for total in (up_total_ref, down_total_ref, proj_total_ref, vector_sums_ref, up_sums_ref):
            total[...] = jnp.zeros_like(total)
        up_t_ref[...] = w_up_ref[...].T
        down_t_ref[...] = w_down_ref[...].T

    for image in range(per_step):
        rows = slice(image * length, (image + 1) * length)
        dy = take_image(wide_ref, step * per_step + image, images)
        dy_ref[rows, :] = dy.astype(jnp.bfloat16)
        vector_sums_ref[3:4] += column_sum(dy)
        unit, scale = normal_form(middle_ref[rows, :])
        unit_ref[rows, :] = unit
        scale_ref[rows, :] = jnp.broadcast_to(scale, (length, scale_ref.shape[1]))
        normed_ref[rows, :] = (unit * vectors_ref[5:6] + vectors_ref[6:7]).astype(jnp.bfloat16)
    normed_t_ref[...] = normed_ref[...].T
    dy_t_ref[...] = dy_ref[...].T
    chunks = hidden // FF_CHUNK

    def cols_of(chunk):
        return slice(chunk * FF_CHUNK, (chunk + 1) * FF_CHUNK)

    def into(chunk):
        cols = cols_of(chunk)
        pre = dot(normed_ref[...], w_up_ref[:, cols])
        return pre + bias_up_ref[:, cols], dot(dy_ref[...], down_t_ref[:, cols])

    def across(pre, d_active):
        active, slope = gelu_and_slope(pre)
        return active.astype(jnp.bfloat16), (d_active * slope).astype(jnp.bfloat16)

    def out_of(chunk, active, d_hidden):
        cols = cols_of(chunk)
        ahead, back = dot(active, w_down_ref[cols, :]), dot(d_hidden, up_t_ref[cols, :])
        if chunk == 0:
            ahead_ref[...] = ahead
            back_ref[...] = back
        else:
            ahead_ref[...] += ahead
            back_ref[...] += back
        down_total_ref[:, cols] += dot(dy_t_ref[...], active)
        up_total_ref[:, cols] += dot(normed_t_ref[...], d_hidden)
        up_sums_ref[:, cols] += column_sum(d_hidden.astype(jnp.float32))

    entered, crossed = into(0), None
    for chunk in range(chunks + 1):
        next_entered = into(chunk + 1) if chunk + 1 < chunks else None
        next_crossed = across(*entered) if chunk < chunks else None
        if crossed is not None:
            out_of(chunk - 1, *crossed)
        entered, crossed = next_entered, next_crossed

    for image in range(per_step):
        rows = slice(image * length, (image + 1) * length)
        output = middle_ref[rows, :] + ahead_ref[rows, :] + vectors_ref[11:12]
        put_image(wide_ref, step * per_step + image, images, output)
        unit = unit_ref[rows, :]
        grad = back_ref[rows, :]
        vector_sums_ref[1:2] += column_sum(grad * unit)
        vector_sums_ref[2:3] += column_sum(grad)
        d_middle = dy_ref[rows, :].astype(jnp.float32) + norm_back(
            grad, unit, scale_ref[rows, 0:1], vectors_ref[5:6]
        )
        d_middle_ref[rows, :] = d_middle
        d_branch = d_middle.astype(jnp.bfloat16)
        dy_ref[rows, :] = d_branch
        vector_sums_ref[0:1] += column_sum(d_branch.astype(jnp.float32))
    proj_total_ref[...] += dot(attended_ref[...], dy_ref[...], 0, 0)
    d_attended_ref[...] = dot(dy_ref[...], proj_t_ref[...]).astype(jnp.bfloat16)


def attention_back_kernel(
    images, x_ref, qkv_ref, probs_ref, d_attended_ref, d_middle_ref, qkv_t_ref, vectors_ref,
    input_grad_ref, qkv_grad_ref, vector_sums_ref, wide_ref, normed_ref, d_projected_ref, back_ref, qkv_total_ref,
):
    @pl.when(pl.program_id(0) == 0)
    def _():
        qkv_total_ref[...] = jnp.zeros_like(qkv_total_ref)
        vector_sums_ref[...] = jnp.zeros_like(vector_sums_ref)

    def put(image, rows, values):
        put_image(wide_ref, image, images, values)

    attention_back_steps(
        x_ref, qkv_ref, probs_ref, d_attended_ref, vectors_ref, vector_sums_ref, normed_ref, d_projected_ref, qkv_total_ref
    )
    input_back_steps(
        put, probs_ref.shape[2], x_ref, d_projected_ref, d_middle_ref, qkv_t_ref, vectors_ref, vector_sums_ref, back_ref
    )

    @pl.when(pl.program_id(0) == pl.num_programs(0) - 1)
    def _():
        narrow(wide_ref, input_grad_ref, images)
        qkv_grad_ref[...] = qkv_total_ref[...].astype(jnp.bfloat16)


def attention_back_steps(
    x_ref, qkv_ref, probs_ref, d_attended_ref, vectors_ref, vector_sums_ref, normed_ref, d_projected_ref, qkv_total_ref
):
    width = d_attended_ref.shape[1]
    length = probs_ref.shape[2]
    per_step = probs_ref.shape[0]

    pairs = width // (2 * HEAD_DIM)
    first = pair_mask(length)
    scale = HEAD_DIM**-0.5

    def places(image, pair):
        low = pair * 2 * HEAD_DIM
        rows = slice(image * length, (image + 1) * length)
        return rows, [slice(part * width + low, part * width + low + 2 * HEAD_DIM) for part in range(3)]

    def entering(image):
        result = []
        for pair in range(pairs):
            rows, cols = places(image, pair)
            d_attended = stack_heads(d_attended_ref[rows, cols[0]], first)
            d_values = dot(probs_ref[image, pair], d_attended)
            d_projected_ref[rows, cols[2]] = d_values.astype(jnp.bfloat16)
            result.append(dot(qkv_ref[rows, cols[2]], d_attended, 1, 1))
        return result

    next_probs = entering(0)
    for image in range(per_step):
        all_d_probs = next_probs
        if image + 1 < per_step:
            next_probs = entering(image + 1)
        all_d_scores = []
        for pair in range(pairs):
            parts = []
            for cols in lane_tiles(2 * length):
                probs, d_probs = probs_ref[image, pair, :, cols].astype(jnp.float32), all_d_probs[pair][:, cols]
                along = jnp.sum(d_probs * probs, axis=0, keepdims=True)
                parts.append((probs * (d_probs - along)).astype(jnp.bfloat16))
            all_d_scores.append(jnp.concatenate(parts, axis=1))
        for pair in range(pairs):
            rows, cols = places(image, pair)
            d_scores = all_d_scores[pair]
            queries = stack_heads(qkv_ref[rows, cols[0]], first)
            d_queries = join_heads(dot(d_scores, qkv_ref[rows, cols[1]], 0, 0), first) * scale
            d_projected_ref[rows, cols[0]] = d_queries.astype(jnp.bfloat16)
            d_projected_ref[rows, cols[1]] = (dot(d_scores, queries) * scale).astype(jnp.bfloat16)

    query_sums = value_sums = jnp.zeros((8, width), jnp.float32)
    for rows in slices_of(d_attended_ref.shape[0]):
        query_sums += fold_rows(d_projected_ref[rows, :width].astype(jnp.float32))
        value_sums += fold_rows(d_projected_ref[rows, 2 * width :].astype(jnp.float32))
        if x_ref is not None:
            unit, _ = normal_form(x_ref[rows, :].astype(jnp.float32))
            normed_ref[rows, :] = (unit * vectors_ref[0:1] + vectors_ref[1:2]).astype(jnp.bfloat16)
    vector_sums_ref[2:3] += column_sum(query_sums)
    vector_sums_ref[3:4] += column_sum(value_sums)
    qkv_total_ref[...] += dot(normed_ref[...], d_projected_ref[...], 0, 0)


def input_back_steps(
    put, length, x_ref, d_projected_ref, d_middle_ref, qkv_t_ref, vectors_ref, vector_sums_ref, back_ref
):
    step = pl.program_id(0)
    per_step = x_ref.shape[0] // length
    back_ref[...] = dot(d_projected_ref[...], qkv_t_ref[...])
    gain_sums = shift_sums = jnp.zeros((8, x_ref.shape[1]), jnp.float32)
    for rows in slices_of(x_ref.shape[0]):
        unit, scale = normal_form(x_ref[rows, :].astype(jnp.float32))
        grad = back_ref[rows, :]
        gain_sums += fold_rows(grad * unit)
        shift_sums += fold_rows(grad)
        back_ref[rows, :] = d_middle_ref[rows, :] + norm_back(grad, unit, scale, vectors_ref[0:1])
    vector_sums_ref[0:1] += column_sum(gain_sums)
    vector_sums_ref[1:2] += column_sum(shift_sums)
    for image in range(per_step):
        rows = slice(image * length, (image + 1) * length)
        put(step * per_step + image, rows, back_ref[rows, :])


def whole_block(shape):
    return pl.BlockSpec(shape, lambda step: (0,) * len(shape))


def step_block(shape, first=0):
    return pl.BlockSpec(shape, lambda step: (first + step,) + (0,) * (len(shape) - 1))


def scratch(*shape, dtype=jnp.float32):
    return pltpu.VMEM(shape, dtype)


def call_kernel(kernel, statics, steps, ins, outs, scratches, operands, flops, transcendentals=0, first_step=0, aliases={}):
    in_specs = [
        pl.BlockSpec(memory_space=pltpu.SMEM)
        if block == "place"
        else pl.BlockSpec(memory_space=pl.ANY)
        if block == "await"
        else whole_block(op.shape) if block is None else step_block(block, first_step)
        for op, block in zip(operands, ins)
    ]
    out_specs = [
        whole_block(shape) if block is None else step_block(block, first_step) for shape, dtype, block in outs
    ]
    moved = sum(op.size * op.dtype.itemsize for op in operands) + sum(
        math.prod(shape) * jnp.dtype(dtype).itemsize for shape, dtype, block in outs
    )
    return pl.pallas_call(
        functools.partial(kernel, *statics),
        grid=(steps,),
        in_specs=in_specs,
        out_specs=out_specs,
        out_shape=[jax.ShapeDtypeStruct(shape, dtype) for shape, dtype, block in outs],
        scratch_shapes=scratches,
        input_output_aliases=aliases,
        compiler_params=pltpu.CompilerParams(vmem_limit_bytes=vmem_bytes),
        cost_estimate=pl.CostEstimate(
            flops=flops * 8, bytes_accessed=moved, transcendentals=transcendentals
        ),
    )(*operands)


def attention_forward(tokens, bias, w_qkv, w_proj, vectors):
    images, length, _ = bias.shape
    total, width = tokens.shape
    pairs = width // (2 * HEAD_DIM)
    rows = PER_STEP * length
    low, high = jnp.bfloat16, jnp.float32
    outs = [
        ((total, width), low, None),
        ((total, 3 * width), low, (rows, 3 * width)),
        ((images, pairs, length, 2 * length), low, (PER_STEP, pairs, length, 2 * length)),
        ((total, width), low, (rows, width)),
        ((total, width), high, (rows, width)),
    ]
    return call_kernel(
        attention_kernel, (images,), images // PER_STEP,
        [None, (PER_STEP, length, 1), None, None, None], outs,
        [scratch(width // 128, total, 128), scratch(rows, width, dtype=low)],
        (tokens, bias, w_qkv, w_proj, vectors),
        2 * total * width * 4 * width + 8 * total * length * width,
    )


def feed_forward(images, middle, cotangent, attended, w_up, w_down, w_proj, vectors):
    total, width = middle.shape
    hidden = w_up.shape[1]
    rows = total // images * FF_PER_STEP
    low, high = jnp.bfloat16, jnp.float32
    block = (rows, width)
    outs = [
        ((total, width), low, None),
        ((total, width), high, block),
        ((total, width), low, block),
        ((width, hidden), low, None),
        ((hidden, width), low, None),
        ((width, width), low, None),
        ((8, width), high, None),
        ((1, hidden), high, None),
    ]
    scratches = [
        scratch(width // 128, total, 128),
        scratch(rows, width, dtype=low),
        scratch(width, rows, dtype=low),
        scratch(rows, width, dtype=low),
        scratch(width, rows, dtype=low),
        scratch(rows, width),
        scratch(rows, 128),
        scratch(rows, width),
        scratch(rows, width),
        scratch(hidden, width, dtype=low),
        scratch(width, hidden, dtype=low),
        scratch(width, hidden),
        scratch(width, hidden),
        scratch(width, width),
    ]
    return call_kernel(
        feed_forward_kernel, (images,), images // FF_PER_STEP,
        [block, None, block, None, None, None, None, None], outs, scratches,
        (middle, cotangent, attended, w_up, w_down, w_proj.T, vectors, vectors[7:11].reshape(1, hidden)),
        12 * total * width * hidden + 4 * total * width * width, total * hidden,
    )


def attention_back(x, qkv, probs, d_attended, d_middle, w_qkv, vectors):
    images, pairs, length, _ = probs.shape
    total, width = x.shape
    rows = PER_STEP * length
    low, high = jnp.bfloat16, jnp.float32
    block = (rows, width)
    outs = [
        ((total, width), low, None),
        ((width, 3 * width), low, None),
        ((8, width), high, None),
    ]
    scratches = [
        scratch(width // 128, total, 128),
        scratch(rows, width, dtype=low),
        scratch(rows, 3 * width, dtype=low),
        scratch(rows, width),
        scratch(width, 3 * width),
    ]
    return call_kernel(
        attention_back_kernel, (images,), images // PER_STEP,
        [block, (rows, 3 * width), (PER_STEP, pairs, length, 2 * length), block, block, None, None],
        outs, scratches, (x, qkv, probs, d_attended, d_middle, w_qkv.T, vectors),
        4 * total * width * 3 * width + 16 * total * length * width,
    )

def linear_place():
    return lax.axis_index("dp") * lax.axis_size("group") + lax.axis_index("group")


def permute(array, mask):
    count = lax.axis_size("dp") * lax.axis_size("group")
    return lax.ppermute(array, ("dp", "group"), [(rank, rank ^ mask) for rank in range(count)])


def direct_masks(bits):
    masks = [0]
    for bit in bits:
        masks = masks + [mask | bit for mask in masks]
    return masks[1:]


def add_wide(first, *rest):
    total = first.astype(jnp.float32)
    for part in rest:
        total = total + part.astype(jnp.float32)
    return total


def packed_place(mask, spread, count):
    return ((mask >> 1) & (spread - 1)) * (count // (2 * spread)) + (mask >> (spread.bit_length()))


def scatter_step(held, bits):
    masks = direct_masks(bits)
    size = held.shape[0] // (len(masks) + 1)
    parts = [
        permute(held[size * (at + 1) : size * (at + 2)].astype(jnp.bfloat16), mask)
        for at, mask in enumerate(masks)
    ]
    return held[:size], parts


def add_wide(first, *rest):
    total = first.astype(jnp.float32)
    for part in rest:
        total = total + part.astype(jnp.float32)
    return total


def packed_place(mask, spread, count):
    return ((mask >> 1) & (spread - 1)) * (count // (2 * spread)) + (mask >> (spread.bit_length()))


def gather_step(held, bits):
    return held + [permute(part, mask) for mask in direct_masks(bits) for part in held]


def gathered_place(mask, count):
    return (mask & 1) * (count // 2) + ((mask >> 2) & 1) * (count // 4) + (mask >> 3) * 2 + ((mask >> 1) & 1)


def unpack(place_ref, block_refs, packed_ref, put, dp_size, spread):
    place = place_ref[0]
    size = block_refs[0].shape[0]
    for at, block_ref in enumerate(block_refs):
        packed_ref[at * size : (at + 1) * size] = block_ref[...]
    count = dp_size * spread
    for row in range(dp_size):
        for col in range(spread):
            put(row, col, packed_ref[gathered_place((row * spread + col) ^ place, count)])


def unpack_in_order(blocks_ref, put, dp_size, spread):
    for row in range(dp_size):
        for col in range(spread):
            put(row, col, blocks_ref[row * spread + col])


def pack(place_ref, take, keep_ref, leave_ref, dp_size, spread):
    place = place_ref[0]
    odd = (place & 1) == 1
    for row in range(dp_size):
        for col in range(0, spread, 2):
            at = packed_place((row * spread + col) ^ place, spread, dp_size * spread)
            even_block, odd_block = take(row, col), take(row, col + 1)
            keep_ref[at] = jnp.where(odd, odd_block, even_block)
            leave_ref[at] = jnp.where(odd, even_block, odd_block)


def narrow_pieces(place_ref, wide_ref, piece_refs, spread):
    tiles, _, lanes = wide_ref.shape
    rows_of_piece = piece_refs[0].shape[0]
    step = 64
    group = place_ref[0] & (spread - 1)
    for relative, piece_ref in enumerate(piece_refs):
        base = (group ^ relative) * rows_of_piece

        @pl.loop(0, rows_of_piece // step)
        def _(part):
            target = pl.ds(pl.multiple_of(part * step, step), step)
            source = pl.ds(pl.multiple_of(base + part * step, step), step)
            for tile in range(tiles):
                cols = slice(tile * lanes, (tile + 1) * lanes)
                piece_ref[target, cols] = wide_ref[tile, source, :].astype(jnp.bfloat16)


def general_body(
    tokens,
    keep_mask,
    cotangent,
    qkv_weight,
    proj_weight,
    up_weight,
    down_weight,
    vectors,
    qkv_rows,
    qkv_cols,
    proj_rows,
    proj_cols,
    up_rows,
    up_cols,
    down_rows,
    down_cols,
    vector_moment,
):
    masters = (qkv_weight, proj_weight, up_weight, down_weight)
    lowered = tuple((master.astype(jnp.bfloat16) for master in masters))
    dp_bits, group_bits = axis_bits("dp"), axis_bits("group")
    gather_steps = dp_bits[1:] + group_bits[1:] + dp_bits[:1] + group_bits[:1]
    scatter_steps = gather_steps[::-1]
    w_qkv, w_proj, w_up, w_down = tuple(
        blocks_to_whole(gather_blocks(part, gather_steps), gather_steps) for part in lowered
    )
    spread = lax.axis_size("group")

    def slots_in(array):
        held, slots, width = array.shape
        parts = array.transpose(1, 0, 2).reshape(slots, spread, held // spread, width)
        parts = lax.all_to_all(
            parts.transpose(1, 0, 2, 3), "group", split_axis=0, concat_axis=0, tiled=True
        )
        return parts.reshape(spread * slots * (held // spread), width)

    def slots_out(array):
        held, slots, width = tokens.shape
        parts = array.reshape(spread, slots, held // spread, width)
        parts = lax.all_to_all(parts, "group", split_axis=0, concat_axis=0, tiled=True)
        return parts.transpose(1, 0, 2, 3).reshape(slots, held, width).transpose(1, 0, 2)

    images = keep_mask.shape[0]
    bias = jnp.where(keep_mask > 0, 0.0, -1e30)[:, :, None]
    x, qkv, probs, attended, middle = attention_forward(
        slots_in(tokens), bias, w_qkv, w_proj, vectors
    )
    output, d_middle, d_attended, up_grad, down_grad, proj_grad, ff_sums, up_sums = feed_forward(
        images, middle, slots_in(cotangent), attended, w_up, w_down, w_proj, vectors
    )
    block_output = slots_out(output)
    d_input, qkv_grad, att_sums = attention_back(
        x, qkv, probs, d_attended, d_middle, w_qkv, vectors
    )
    input_grad = slots_out(d_input)
    local_vectors = jnp.concatenate(
        [att_sums[:4], ff_sums[:3], up_sums.reshape(4, -1), ff_sums[3:4]], axis=0
    )
    vector_grad = sum_everywhere(local_vectors, group_bits + dp_bits)
    local_grads = (qkv_grad, proj_grad, up_grad, down_grad)
    owned = tuple(
        scatter_sum(whole_to_blocks(part, scatter_steps), scatter_steps) for part in local_grads
    )
    squares = tuple((gradient * gradient + tiny_square for gradient in owned))
    row_parts = tuple((jnp.sum(square, axis=1) for square in squares)) + tuple(
        (jnp.sum(master * master, axis=1) for master in masters)
    )
    row_sums = sum_parts(row_parts, group_bits)
    rows_old = (qkv_rows, proj_rows, up_rows, down_rows)
    cols_old = (qkv_cols, proj_cols, up_cols, down_cols)
    total_cols = tuple((gradient.shape[1] * lax.axis_size("group") for gradient in owned))
    total_rows = tuple((gradient.shape[0] * lax.axis_size("dp") for gradient in owned))
    rows_new = tuple(
        (
            decay_rate * rows_old[which] + (1.0 - decay_rate) * row_sums[which] / total_cols[which]
            for which in range(4)
        )
    )
    col_parts = (
        tuple((jnp.sum(square, axis=0) for square in squares))
        + tuple((jnp.sum(row_stat) for row_stat in rows_new))
        + tuple((jnp.sum(row_sums[4 + which]) for which in range(4)))
    )
    col_sums = sum_parts(col_parts, dp_bits)
    results = []
    for which in range(4):
        cols_new = (
            decay_rate * cols_old[which] + (1.0 - decay_rate) * col_sums[which] / total_rows[which]
        )
        mean_rows = col_sums[4 + which] / total_rows[which]
        spread = jnp.sqrt(col_sums[8 + which] / (total_rows[which] * total_cols[which]))
        second = rows_new[which][:, None] * cols_new[None, :] / mean_rows
        updated = masters[which] - step_rate * spread * owned[which] * lax.rsqrt(second)
        results.append((owned[which], rows_new[which], cols_new, updated))
    vector_moment_new = decay_rate * vector_moment + (1.0 - decay_rate) * (
        vector_grad * vector_grad + tiny_square
    )
    row_spread = jnp.sqrt(jnp.mean(vectors * vectors, axis=1, keepdims=True))
    vector_new = vectors - step_rate * row_spread * vector_grad * lax.rsqrt(vector_moment_new)
    return (
        block_output,
        input_grad,
        results[0][0],
        results[0][1],
        results[0][2],
        results[0][3],
        results[1][0],
        results[1][1],
        results[1][2],
        results[1][3],
        results[2][0],
        results[2][1],
        results[2][2],
        results[2][3],
        results[3][0],
        results[3][1],
        results[3][2],
        results[3][3],
        vector_grad,
        vector_moment_new,
        vector_new,
    )


def first_attention_kernel(images, dp_size, spread, place_ref, tokens_ref, *refs):
    blocks, refs = refs[:4], refs[4:]
    keep_ref, vectors_ref, *outs, x_ref, w_qkv_ref, w_proj_ref, qkv_t_ref, proj_t_ref = refs[:-3]
    packed_ref, wide_ref, bias_ref = refs[-3:]
    rows = packed_ref.shape[1]
    qkv_cols, proj_cols = w_qkv_ref.shape[1] // spread, w_proj_ref.shape[1] // spread

    @pl.when(pl.program_id(0) == 0)
    def _():
        widen(tokens_ref, wide_ref, images)
        to_image_rows(wide_ref, x_ref, images)

        def put(row, col, block):
            down = slice(row * rows, (row + 1) * rows)
            w_qkv_ref[down, col * qkv_cols : (col + 1) * qkv_cols] = block[:, :qkv_cols]
            w_proj_ref[down, col * proj_cols : (col + 1) * proj_cols] = block[:, qkv_cols:]

        unpack(place_ref, blocks, packed_ref, put, dp_size, spread)
        qkv_t_ref[...] = w_qkv_ref[...].T
        proj_t_ref[...] = w_proj_ref[...].T

    attention_part(0, x_ref, keep_ref, w_qkv_ref, w_proj_ref, vectors_ref, *outs, bias_ref)


def next_attention_kernel(start, x_ref, keep_ref, w_qkv_ref, w_proj_ref, vectors_ref, *refs):
    attention_part(start, x_ref, keep_ref, w_qkv_ref, w_proj_ref, vectors_ref, *refs[-6:])


def attention_part(
    start, x_ref, keep_ref, w_qkv_ref, w_proj_ref, vectors_ref,
    qkv_ref, probs_ref, attended_ref, middle_ref, normed_ref, bias_ref,
):
    @pl.when(pl.program_id(0) == 0)
    def _():
        bias_ref[...] = jnp.where(keep_ref[...] > 0, 0.0, -1e30).T

    def bias_column(image):
        here = start + pl.program_id(0) * probs_ref.shape[0] + image
        lane = lax.broadcasted_iota(jnp.int32, bias_ref.shape, 1)
        return row_sum(jnp.where(lane == here, bias_ref[...], 0.0))

    attention_steps(
        x_ref, bias_column, w_qkv_ref, w_proj_ref, vectors_ref,
        qkv_ref, probs_ref, attended_ref, middle_ref, normed_ref,
    )


def feed_forward_packed_kernel(images, dp_size, spread, place_ref, *refs):
    cotangent_ref, blocks, refs = refs[0], refs[1:5], refs[5:]
    middle_ref, attended_ref, proj_t_ref, vectors_ref = refs[:4]
    outputs, refs = refs[4 : 4 + spread], refs[4 + spread :]
    d_middle_ref, d_attended_ref, keep_ref, leave_ref, proj_total_ref, vector_sums_ref, up_sums_ref = refs[:7]
    w_up_ref, w_down_ref, packed_ref, bias_up_ref, wide_ref = refs[7:12]
    scratches = refs[12:]
    width = w_up_ref.shape[0]
    up_total_ref, down_total_ref = scratches[-2:]
    rows = packed_ref.shape[1]
    up_cols = w_up_ref.shape[1] // spread
    out_cols = w_down_ref.shape[1] // spread
    folds = w_down_ref.shape[0] // w_up_ref.shape[0]

    @pl.when(pl.program_id(0) == 0)
    def _():
        widen(cotangent_ref, wide_ref, images)
        for fold in range(bias_up_ref.shape[1] // width):
            bias_up_ref[:, fold * width : (fold + 1) * width] = vectors_ref[7 + fold : 8 + fold]

        def put(row, col, block):
            w_up_ref[row * rows : (row + 1) * rows, col * up_cols : (col + 1) * up_cols] = block[:, :up_cols]
            for fold in range(folds):
                down = (row * folds + fold) * rows
                start = up_cols + fold * out_cols
                w_down_ref[down : down + rows, col * out_cols : (col + 1) * out_cols] = block[
                    :, start : start + out_cols
                ]

        unpack(place_ref, blocks, packed_ref, put, dp_size, spread)

    feed_forward_steps(
        images, middle_ref, attended_ref, w_up_ref, w_down_ref, proj_t_ref, vectors_ref, bias_up_ref,
        d_middle_ref, d_attended_ref, vector_sums_ref, up_sums_ref, wide_ref, *scratches, proj_total_ref,
    )

    @pl.when(pl.program_id(0) == pl.num_programs(0) - 1)
    def _():
        narrow_pieces(place_ref, wide_ref, outputs, spread)

        def take(row, col):
            across = slice(row * rows, (row + 1) * rows)
            parts = [up_total_ref[across, col * up_cols : (col + 1) * up_cols].astype(jnp.bfloat16)]
            lanes = slice(row * folds * rows, (row + 1) * folds * rows)
            for start in range(col * out_cols, (col + 1) * out_cols, rows):
                parts.append(down_total_ref[start : start + rows, lanes].astype(jnp.bfloat16))
            return jnp.concatenate(parts, axis=1)

        pack(place_ref, take, keep_ref, leave_ref, dp_size, spread)


def attention_back_packed_kernel(
    dp_size, spread, place_ref, normed_ref, qkv_ref, probs_ref, d_attended_ref, vectors_ref, proj_total_ref, _,
    d_projected_ref, keep_ref, leave_ref, vector_sums_ref, total_ref,
):
    @pl.when(pl.program_id(0) == 0)
    def _():
        total_ref[...] = jnp.zeros_like(total_ref)
        vector_sums_ref[...] = jnp.zeros_like(vector_sums_ref)

    attention_back_steps(
        None, qkv_ref, probs_ref, d_attended_ref, vectors_ref, vector_sums_ref, normed_ref, d_projected_ref, total_ref
    )

    @pl.when(pl.program_id(0) == pl.num_programs(0) - 1)
    def _():
        rows = keep_ref.shape[1]
        qkv_cols, proj_cols = total_ref.shape[1] // spread, proj_total_ref.shape[1] // spread

        def take(row, col):
            down = slice(row * rows, (row + 1) * rows)
            parts = [
                total_ref[down, col * qkv_cols : (col + 1) * qkv_cols],
                proj_total_ref[down, col * proj_cols : (col + 1) * proj_cols],
            ]
            return jnp.concatenate(parts, axis=1).astype(jnp.bfloat16)

        pack(place_ref, take, keep_ref, leave_ref, dp_size, spread)


def first_input_kernel(
    length, x_ref, d_projected_ref, d_middle_ref, qkv_t_ref, vectors_ref, before_ref, *refs
):
    d_input_ref, vector_sums_ref, back_ref = refs[-3:]

    @pl.when(pl.program_id(0) == 0)
    def _():
        vector_sums_ref[...] = before_ref[...]

    def put(image, rows, values):
        d_input_ref[rows, :] = values.astype(jnp.bfloat16)

    input_back_steps(
        put, length, x_ref, d_projected_ref, d_middle_ref, qkv_t_ref, vectors_ref, vector_sums_ref, back_ref
    )


def last_input_kernel(
    images, spread, length, first, place_ref, x_ref, d_projected_ref, d_middle_ref, qkv_t_ref, vectors_ref, before_ref,
    d_input_ref, _, *refs,
):
    pieces, (vector_sums_ref, wide_ref, back_ref) = refs[:spread], refs[spread:]

    @pl.when(pl.program_id(0) == 0)
    def _():
        vector_sums_ref[...] = before_ref[...]
        for image in range(first):
            rows = slice(image * length, (image + 1) * length)
            put_image(wide_ref, image, images, d_input_ref[rows, :].astype(jnp.float32))

    def put(image, rows, values):
        put_image(wide_ref, first + image, images, values)

    input_back_steps(
        put, length, x_ref, d_projected_ref, d_middle_ref, qkv_t_ref, vectors_ref, vector_sums_ref, back_ref
    )

    @pl.when(pl.program_id(0) == pl.num_programs(0) - 1)
    def _():
        narrow_pieces(place_ref, wide_ref, pieces, spread)


def cut(array_ref, parts_ref):
    count = parts_ref.shape[2]
    for member in range(parts_ref.shape[0]):
        parts_ref[member] = array_ref[:, member * count : (member + 1) * count, :]


def pack_kernel(qkv_ref, proj_ref, up_ref, down_ref, pack_ref):
    rows, start = pack_ref.shape[0], 0
    parts = [qkv_ref[...], proj_ref[...], up_ref[...]]
    parts += [down_ref[fold * rows : (fold + 1) * rows, :] for fold in range(down_ref.shape[0] // rows)]
    for part in parts:
        pack_ref[:, start : start + part.shape[1]] = part.astype(jnp.bfloat16)
        start += part.shape[1]


def token_kernel(array_ref, own_ref, arrived_ref, _, parts_ref, first_ref, second_ref):
    start = first_ref.shape[2]
    for at, pack_ref in enumerate((own_ref, arrived_ref)):
        first_ref[at] = pack_ref[:, :start]
        second_ref[at] = pack_ref[:, start:]
    cut(array_ref, parts_ref)


def join_kernel(count, *refs):
    size = refs[0].shape[0]
    for at, part_ref in enumerate(refs[:count]):
        refs[-1][at * size : (at + 1) * size] = part_ref[...]


def settle_kernel(spread, place_ref, *refs):
    lists, (output_ref, token_ref) = refs[:-2], refs[-2:]
    token_ref[...] = jnp.zeros_like(token_ref)
    group = place_ref[0] & (spread - 1)
    count = lists[0].shape[1]
    share = len(lists) // spread * count
    for at, piece_ref in enumerate(lists):
        relative, part = at % spread, at // spread
        start = pl.multiple_of((group ^ relative) * share + part * count, count)
        output_ref[:, pl.ds(start, count), :] = piece_ref[...]


def lane_table(rows, columns):
    lane = lax.broadcasted_iota(jnp.int32, (rows, 128), 1)
    table = jnp.zeros((rows, 128), jnp.float32)
    for at, column in enumerate(columns):
        table = jnp.where(lane == at, column, table)
    return table


def added(parts):
    while len(parts) > 1:
        parts = [sum(parts[at : at + 2][1:], parts[at]) for at in range(0, len(parts), 2)]
    return parts[0]


def row_sum(values):
    return jnp.sum(values, axis=1, keepdims=True)


def after_kernel(*refs):
    pass


def gradient_kernel(count, *refs):
    block_parts, sums, refs = refs[:count], refs[count : count + 3], refs[count + 3 :]
    masters, rows_old, refs = refs[:4], refs[4:8], refs[8:]
    grads, (row_ref, message_ref) = refs[:4], refs[4:]
    blocks = added([part[0].astype(jnp.float32) for part in block_parts])
    rows, up_cols = grads[2].shape
    qkv_cols, out_cols = grads[0].shape[1], grads[1].shape[1]
    folds = grads[3].shape[0] // rows
    up = blocks[:, :up_cols]
    turned = [
        blocks[:, up_cols + part * folds * rows : up_cols + (part + 1) * folds * rows]
        for part in range(out_cols // rows)
    ]
    down = jnp.concatenate(turned, axis=0).T
    downs = [down[fold * rows : (fold + 1) * rows] for fold in range(folds)]
    start = up_cols + folds * out_cols
    qkv = blocks[:, start : start + qkv_cols]
    proj = blocks[:, start + qkv_cols :]
    grads[0][...] = qkv
    grads[1][...] = proj
    grads[2][...] = up
    for fold in range(folds):
        grads[3][fold * rows : (fold + 1) * rows, :] = downs[fold]
    squares = [part * part + tiny_square for part in (qkv, proj, up, *downs)]
    row_ref[...] = lane_table(rows, [row_sum(square) for square in squares]).T[: row_ref.shape[0], :]
    width = message_ref.shape[1]
    message_ref[...] = jnp.zeros_like(message_ref)
    for at, square in enumerate((*squares[:3], added(squares[3:]))):
        message_ref[at : at + 1, : square.shape[1]] = column_sum(square)
    scalars = [column_sum(row_sum(master[...] * master[...])) for master in masters]
    scalars += [row_sum(part[...].reshape(1, part.shape[0])) for part in rows_old]
    message_ref[4:5, :128] = lane_table(1, scalars)
    att_ref, ff_ref, up_ref = sums
    count = up_ref.shape[1] // width
    message_ref[8:12, :] = att_ref[:4]
    message_ref[12:15, :] = ff_ref[:3]
    for at in range(count):
        message_ref[15 + at : 16 + at, :] = up_ref[:, at * width : (at + 1) * width]
    message_ref[15 + count : 16 + count, :] = ff_ref[3:4]


def column_kernel(row_ref, *refs):
    parts, (cols_ref, message_ref) = refs[:-3], refs[-2:]
    total = added([part[...] for part in parts])
    cols_ref[...] = total[:8]
    width = total.shape[1]
    rows = row_ref.shape[1]
    message_ref[...] = jnp.zeros_like(message_ref)
    message_ref[:8, :rows] = row_ref[...]
    columns = [row_sum(total[which : which + 1]) for which in range(4)]
    squares = [total[4:5, which : which + 1] for which in range(4)]
    message_ref[8:9, :] = lane_table(1, columns + squares)
    for tile in range(width // 128):
        message_ref[16 * (tile + 1) : 16 * (tile + 2), :] = total[8:, tile * 128 : (tile + 1) * 128]


def update_kernel(count, heights, widths, *refs):
    messages, refs = refs[:count], refs[count:]
    cols_ref, vectors_ref, moment_ref, refs = refs[0], refs[1], refs[2], refs[3:]
    grads, masters, rows_old, cols_old, refs = refs[:4], refs[4:8], refs[8:12], refs[12:16], refs[17:]
    news, cols_new, rows_out, refs = refs[:4], refs[4:8], refs[8:12], refs[12:]
    vector_grad_ref, moment_new_ref, vector_new_ref = refs
    sums = added([message[...] for message in messages])
    height = grads[0].shape[0]
    folds = grads[3].shape[0] // height
    lanes = [[0], [1], [2], list(range(3, 3 + folds))]
    share = 1.0 - decay_rate
    for which in range(4):
        entries = heights[which] * widths[which]
        cols = cols_old[which].shape[0]
        new = decay_rate * cols_old[which][...].reshape(1, cols) + share / heights[which] * cols_ref[
            which : which + 1, :cols
        ]
        cols_new[which][...] = new[0]
        old_total = cols_ref[4:5, 4 + which : 5 + which]
        mean_rows = (decay_rate * old_total + share / widths[which] * sums[8:9, which : which + 1]) / heights[which]
        rate = step_rate * jnp.sqrt(sums[8:9, 4 + which : 5 + which] / entries)
        across = new / mean_rows
        old = rows_old[which][...].reshape(1, len(lanes[which]) * height)
        row_sums = jnp.concatenate([sums[lane : lane + 1, :height] for lane in lanes[which]], axis=1)
        row = decay_rate * old + share / widths[which] * row_sums
        rows_out[which][...] = row[0]
        for fold in range(len(lanes[which])):
            part = slice(fold * height, (fold + 1) * height)
            column = jnp.broadcast_to(row[:, part], (8, height)).T[:, :1]
            news[which][part, :] = masters[which][part, :] - rate * grads[which][part, :] * lax.rsqrt(column * across)
    vectors = vectors_ref[...]
    count = vectors.shape[0]
    gradient = jnp.concatenate(
        [sums[16 * (tile + 1) : 16 * (tile + 1) + count] for tile in range(vectors.shape[1] // 128)], axis=1
    )
    vector_grad_ref[...] = gradient
    moment = decay_rate * moment_ref[...] + share * (gradient * gradient + tiny_square)
    moment_new_ref[...] = moment
    spread = jnp.sqrt(jnp.mean(vectors * vectors, axis=1, keepdims=True))
    vector_new_ref[...] = vectors - step_rate * spread * gradient * lax.rsqrt(moment)


def packed_body(
    tokens, keep_mask, cotangent, qkv_weight, proj_weight, up_weight, down_weight, vectors,
    qkv_rows, qkv_cols, proj_rows, proj_cols, up_rows, up_cols, down_rows, down_cols, vector_moment,
):
    spread, dp_size = lax.axis_size("group"), lax.axis_size("dp")
    low, high = jnp.bfloat16, jnp.float32
    place = linear_place().astype(jnp.int32).reshape(1)
    group = lax.axis_index("group")
    held, slots, width = tokens.shape
    images, length = keep_mask.shape
    hidden = up_weight.shape[1] * spread
    total = images * length
    rows = qkv_weight.shape[0]
    folds = down_weight.shape[0] // rows
    core_bits = (1,)
    near_bits = tuple(1 << at for at in range(1, spread.bit_length()))
    far_bits = tuple(spread << at for at in range(1, dp_size.bit_length() - 1))
    half = spread * dp_size // 2

    anywhere = pl.BlockSpec(memory_space=pl.ANY)
    in_smem = pl.BlockSpec(memory_space=pltpu.SMEM)

    in_vmem = pl.BlockSpec(memory_space=pltpu.VMEM)
    small = functools.partial(
        pl.pallas_call, compiler_params=pltpu.CompilerParams(vmem_limit_bytes=vmem_bytes)
    )
    masters = (qkv_weight, proj_weight, up_weight, down_weight)
    parted = jax.ShapeDtypeStruct((spread, slots, images, width), low)

    def after(array, awaited):
        return small(
            after_kernel,
            in_specs=[anywhere] * (1 + len(awaited)),
            out_specs=anywhere,
            out_shape=jax.ShapeDtypeStruct(array.shape, array.dtype),
            input_output_aliases={0: 0},
        )(array, *awaited)

    def to_group(parts):
        return lax.all_to_all(parts, "group", split_axis=0, concat_axis=0, tiled=True)

    def to_images(parts):
        return to_group(parts).reshape(total, width)

    def exchange(parts):
        return [parts[0]] + [permute(part, relative) for relative, part in enumerate(parts) if relative]

    def settle(parts):
        parts = [part.reshape(slots, -1, width) for part in parts]
        whole, token = small(
            functools.partial(settle_kernel, spread),
            in_specs=[in_smem] + [in_vmem] * len(parts),
            out_specs=[in_vmem] * 2,
            out_shape=[
                jax.ShapeDtypeStruct((slots, held, width), low),
                jax.ShapeDtypeStruct((8, 128), high),
            ],
        )(place, *parts)
        return whole.transpose(1, 0, 2), token

    first_cols = qkv_weight.shape[1] + proj_weight.shape[1]
    second_cols = up_weight.shape[1] + folds * down_weight.shape[1]
    pack_own = small(pack_kernel, out_shape=jax.ShapeDtypeStruct((rows, first_cols + second_cols), low))(*masters)
    across_y, across_x = near_bits
    pack_arrived = permute(pack_own, across_y)
    cotangent_cut = small(cut, out_shape=parted)(cotangent.transpose(1, 0, 2))
    roomy = functools.partial(
        pl.pallas_call, compiler_params=pltpu.CompilerParams(vmem_limit_bytes=all_vmem_bytes)
    )
    token_cut, first_pair, second_pair = roomy(
        token_kernel,
        in_specs=[in_vmem] * 3 + [anywhere],
        out_shape=[
            parted,
            jax.ShapeDtypeStruct((2, rows, first_cols), low),
            jax.ShapeDtypeStruct((2, rows, second_cols), low),
        ],
    )(tokens.transpose(1, 0, 2), pack_own, pack_arrived, cotangent_cut)
    inputs = to_images(token_cut)

    def gather_far(pair):
        return [pair] + [permute(pair, mask) for mask in direct_masks(far_bits)]

    def join(parts, awaited=()):
        count = len(parts) * parts[0].shape[0]
        return roomy(
            functools.partial(join_kernel, len(parts)),
            in_specs=[in_vmem] * len(parts) + [anywhere] * len(awaited),
            out_shape=jax.ShapeDtypeStruct((count, *parts[0].shape[1:]), low),
        )(*parts, *awaited)

    def gather_rest(held, awaited=None):
        arrived = permute(held, across_x)
        leaving = [held, arrived]
        if awaited is not None:
            leaving = [after(part, [awaited]) for part in leaving]
        return leaving + [permute(part, core_bits[0]) for part in leaving]

    first_far = join(gather_far(first_pair))
    upstream = to_images(cotangent_cut)
    first_blocks = gather_rest(first_far)
    second_far = gather_far(second_pair)

    step_rows = PER_STEP * length
    block = (step_rows, width)
    pairs = width // (2 * HEAD_DIM)
    steps = images // PER_STEP
    statics = (images, dp_size, spread)
    wide = scratch(width // 128, total, 128)
    probs_block = (PER_STEP, pairs, length, 2 * length)
    attention_outs = [
        ((total, 3 * width), low, (step_rows, 3 * width)),
        ((images, *probs_block[1:]), low, probs_block),
        ((total, width), low, block),
        ((total, width), high, block),
        ((total, width), low, block),
    ]
    attention_flops = (2 * total * width * 4 * width + 8 * total * length * width) // steps
    attention_scratches = [scratch(length, images)]
    *attention, x, w_qkv, w_proj, qkv_t, proj_t = call_kernel(
        first_attention_kernel, statics, 1,
        ["place"] + [None] * 7,
        attention_outs
        + [
            ((total, width), low, None),
            ((width, 3 * width), low, None),
            ((width, width), low, None),
            ((3 * width, width), low, None),
            ((width, width), low, None),
        ],
        [scratch(dp_size * spread, rows, first_cols, dtype=low), wide] + attention_scratches,
        (place, inputs, *first_blocks, keep_mask, vectors),
        attention_flops,
    )
    second_joined = join(second_far, attention[:1])
    attention = call_kernel(
        next_attention_kernel, (PER_STEP,), steps - 1,
        [block] + [None] * 4 + ["await"] * len(attention),
        attention_outs, attention_scratches,
        (x, keep_mask, w_qkv, w_proj, vectors, *attention),
        attention_flops * (steps - 1), first_step=1,
        aliases={5 + at: at for at in range(len(attention))},
    )
    qkv, probs, attended, middle, normed = attention
    second_blocks = gather_rest(second_joined, middle)
    piece = ((slots * images, width), low, None)
    ff_rows = FF_PER_STEP * length
    ff_block = (ff_rows, width)
    results = call_kernel(
        feed_forward_packed_kernel, statics, images // FF_PER_STEP,
        ["place"] + [None] * 5 + [ff_block, ff_block] + [None] * 2,
        [piece] * spread
        + [
            ((total, width), high, ff_block),
            ((total, width), low, ff_block),
            ((half, rows, second_cols), low, None),
            ((half, rows, second_cols), low, None),
            ((width, width), high, None),
            ((8, width), high, None),
            ((1, hidden), high, None),
        ],
        [
            scratch(width, hidden, dtype=low),
            scratch(hidden, width, dtype=low),
            scratch(dp_size * spread, rows, second_cols, dtype=low),
            scratch(1, hidden),
            wide,
            scratch(ff_rows, width, dtype=low),
            scratch(width, ff_rows, dtype=low),
            scratch(ff_rows, width, dtype=low),
            scratch(width, ff_rows, dtype=low),
            scratch(ff_rows, width),
            scratch(ff_rows, 128),
            scratch(ff_rows, width),
            scratch(ff_rows, width),
            scratch(hidden, width, dtype=low),
            scratch(width, hidden, dtype=low),
            scratch(width, hidden),
            scratch(width, hidden),
        ],
        (
            place, upstream, *second_blocks, middle, attended, proj_t, vectors,
        ),
        12 * total * width * hidden + 4 * total * width * width, total * hidden,
    )
    d_middle, d_attended, ff_keep, ff_leave, proj_total, ff_sums, up_sums = results[spread:]

    ff_first = permute(ff_leave, core_bits[0])
    ff_count = half // 2
    ff_next = add_wide(ff_keep[ff_count:], ff_first[ff_count:]).astype(low)
    ff_arrived = permute(ff_next, across_x)
    output_parts = exchange(results[:spread])
    pack_half = ((half, rows, first_cols), low, None)
    wide_rows = (step_rows, 3 * width)
    d_projected, qkv_keep, qkv_leave, att_sums = call_kernel(
        attention_back_packed_kernel, (dp_size, spread), steps,
        ["place", block, wide_rows, probs_block, block, None, None, "await"],
        [((total, 3 * width), low, wide_rows), pack_half, pack_half, ((8, width), high, None)],
        [scratch(width, 3 * width)],
        (place, normed, qkv, probs, d_attended, vectors, proj_total, ff_next),
        2 * total * width * 3 * width + 16 * total * length * width,
    )
    qkv_arrived = permute(after(qkv_leave, output_parts[1:] + [ff_arrived]), core_bits[0])
    input_flops = 2 * total * width * 3 * width
    input_ins = [block, wide_rows, block, None, None, None]
    input_outs = [((total, width), low, block), ((8, width), high, None)]
    d_input, att_sums = call_kernel(
        first_input_kernel, (length,), 1, input_ins, input_outs, [scratch(step_rows, width)],
        (x, d_projected, d_middle, qkv_t, vectors, att_sums), input_flops // steps,
    )
    ff_quarter = half // 4
    ff_last = add_wide(
        ff_keep[ff_quarter:ff_count], ff_first[ff_quarter:ff_count], ff_arrived[ff_quarter:]
    ).astype(low)
    ff_last_arrived = permute(ff_last, across_y)
    qkv_held = add_wide(qkv_keep, qkv_arrived)
    leaving = [
        qkv_held[at : at + ff_quarter].astype(low) for at in range(ff_quarter, half, ff_quarter)
    ]
    qkv_held = qkv_held[:ff_quarter]
    qkv_parts = [permute(part, mask) for part, mask in zip(leaving, direct_masks(near_bits))]
    d_input, att_sums = call_kernel(
        first_input_kernel, (length,), 1, input_ins + ["await"] * 2, input_outs, [scratch(step_rows, width)],
        (x, d_projected, d_middle, qkv_t, vectors, att_sums, d_input, leaving[0]), input_flops // steps,
        first_step=1, aliases={6: 0},
    )
    ff_held = add_wide(
        ff_keep[:ff_quarter], ff_first[:ff_quarter], ff_arrived[:ff_quarter], ff_last_arrived
    )
    qkv_held = add_wide(qkv_held, *qkv_parts)
    blocks = jnp.concatenate([ff_held, qkv_held], axis=2)
    far_leaving = [blocks[at : at + 1].astype(low) for at in range(1, blocks.shape[0])]
    block_parts = [blocks[:1]] + [permute(part, mask) for part, mask in zip(far_leaving, direct_masks(far_bits))]
    results = call_kernel(
        last_input_kernel, (images, spread, length, 2 * PER_STEP), steps - 2,
        ["place"] + input_ins + [None, "await"],
        [piece] * spread + [((8, width), high, None)],
        [wide, scratch(step_rows, width)],
        (place, x, d_projected, d_middle, qkv_t, vectors, att_sums, d_input, far_leaving[0]), input_flops // steps * (steps - 2),
        first_step=2,
    )
    att_sums = results[spread]
    input_pieces = list(results[:spread])
    heights = [master.shape[0] * dp_size for master in masters]
    widths = [master.shape[1] * spread for master in masters]
    rows_old, cols_old = [qkv_rows, proj_rows, up_rows, down_rows], [qkv_cols, proj_cols, up_cols, down_cols]

    def like(*arrays):
        return [jax.ShapeDtypeStruct(array.shape, high) for array in arrays]

    operands = (*block_parts, att_sums, ff_sums, up_sums, *masters, *rows_old)
    *grads, row_sums, message = small(
        functools.partial(gradient_kernel, len(block_parts)),
        out_shape=like(*masters) + [jax.ShapeDtypeStruct((8, rows), high), jax.ShapeDtypeStruct((24, width), high)],
    )(*operands)
    input_pieces[1] = after(input_pieces[1], [row_sums])
    output_parts[0] = after(output_parts[0], [row_sums])
    block_output, settled = settle(output_parts)
    input_grad, input_settled = settle(exchange(input_pieces))
    message = added([message] + [permute(message, mask) for mask in direct_masks((across_x, far_bits[0]))])
    for bit in far_bits[1:-1]:
        message = message + permute(message, bit)
    messages = [message, permute(message, far_bits[-1])]
    col_sums, message = small(
        column_kernel,
        in_specs=[in_vmem] * (1 + len(messages)) + [anywhere],
        out_shape=[
            jax.ShapeDtypeStruct((8, width), high),
            jax.ShapeDtypeStruct((16 + width // 8, 128), high),
        ],
    )(row_sums, *messages, settled)
    messages = [message] + [permute(message, mask) for mask in range(1, spread)]
    operands = (*messages, col_sums, vectors, vector_moment, *grads, *masters, *rows_old, *cols_old)
    results = small(
        functools.partial(update_kernel, len(messages), heights, widths),
        in_specs=[in_vmem] * len(operands) + [anywhere],
        out_shape=like(*masters, *cols_old, *rows_old, vectors, vectors, vectors),
    )(*operands, input_settled)
    news, cols_new, rows_out = results[:4], results[4:8], results[8:12]
    vector_grad, vector_moment_new, vector_new = results[12:]
    factored = []
    for which in range(4):
        factored += [grads[which], rows_out[which], cols_new[which], news[which]]
    return (block_output, input_grad, *factored, vector_grad, vector_moment_new, vector_new)


def body(*arrays):
    spread, dp_size = lax.axis_size("group"), lax.axis_size("dp")
    rows, images = arrays[3].shape[0], arrays[1].shape[0]
    slots, width = arrays[0].shape[1:]
    folds = arrays[6].shape[0] // rows
    powers = all(size & (size - 1) == 0 for size in (spread, dp_size))
    fits = powers and spread == 4 and dp_size > 2
    fits = fits and arrays[5].shape[1] <= width and folds <= 5
    fits = fits and arrays[6].shape[1] % rows == 0 and rows % 16 == 0 and images % FF_PER_STEP == 0 and images > 2 * PER_STEP and images % 16 == 0 and slots % 4 == 0
    return packed_body(*arrays) if fits else general_body(*arrays)


def solution(mesh):
    in_specs = (
        P("dp", "group", None),
        P(("dp", "group"), None),
        P("dp", "group", None),
        P("dp", "group"),
        P("dp", "group"),
        P("dp", "group"),
        P("dp", "group"),
        P(),
        P("dp"),
        P("group"),
        P("dp"),
        P("group"),
        P("dp"),
        P("group"),
        P("dp"),
        P("group"),
        P(),
    )
    out_specs = (
        P("dp", "group", None),
        P("dp", "group", None),
        P("dp", "group"),
        P("dp"),
        P("group"),
        P("dp", "group"),
        P("dp", "group"),
        P("dp"),
        P("group"),
        P("dp", "group"),
        P("dp", "group"),
        P("dp"),
        P("group"),
        P("dp", "group"),
        P("dp", "group"),
        P("dp"),
        P("group"),
        P("dp", "group"),
        P(),
        P(),
        P(),
    )
    return jax.shard_map(body, mesh=mesh, in_specs=in_specs, out_specs=out_specs, check_vma=False)
```
